32 devices in a mesh: dp: 8 (over z, core), fsdp: 4 (over y, x).
Axes of the slice: x: 2, y: 2, z: 4, core: 2. Of those that a mesh axis runs over, the one named last changes fastest.
Arguments:
- tokens: bfloat16 [32768, 768], P(('dp', 'fsdp')), may hold values from -6 to 6
- cotangent: bfloat16 [32768, 768], P(('dp', 'fsdp')), may hold values from -6 to 6
- perms: int32 [16, 2, 2048], P('dp'), may hold values from 0 to 2047, as said below
- unit_kind: int32 [16], P('dp'), may hold values from 0 to 1
- w_qkv: bfloat16 [768, 2304], P('fsdp'), may hold values from -0.21875 to 0.21875
- bias_qv: bfloat16 [2, 768], P(None, 'fsdp'), may hold values from -3 to 3
- w_out: bfloat16 [768, 768], P('fsdp'), may hold values from -1.75 to 1.75
- bias_out: bfloat16 [768], P('fsdp'), may hold values from -3 to 3
- ln_gain: bfloat16 [2, 768], P(None, 'fsdp'), may hold values from 0.099609375 to 1.8984375
- ln_bias: bfloat16 [2, 768], P(None, 'fsdp'), may hold values from -3 to 3
- w_up: bfloat16 [768, 3072], P('fsdp'), may hold values from -0.21875 to 0.21875
- bias_up: bfloat16 [3072], P('fsdp'), may hold values from -3 to 3
- w_down: bfloat16 [3072, 768], P('fsdp'), may hold values from -0.109375 to 0.109375
- bias_down: bfloat16 [768], P('fsdp'), may hold values from -3 to 3
Outputs:
- block_out: bfloat16 [32768, 768], P(('dp', 'fsdp'))
- d_tokens: float32 [32768, 768], P(('dp', 'fsdp'))
- grad_w_qkv: float32 [768, 2304], P('fsdp')
- grad_bias_qv: float32 [2, 768], P(None, 'fsdp')
- grad_w_out: float32 [768, 768], P('fsdp')
- grad_bias_out: float32 [768], P('fsdp')
- grad_ln_gain: float32 [2, 768], P(None, 'fsdp')
- grad_ln_bias: float32 [2, 768], P(None, 'fsdp')
- grad_w_up: float32 [768, 3072], P('fsdp')
- grad_bias_up: float32 [3072], P('fsdp')
- grad_w_down: float32 [3072, 768], P('fsdp')
- grad_bias_down: float32 [768], P('fsdp')
The draws below stay inside these ranges and needn't reach their ends.
Inputs may be any that keep to these rules, and one draw needn't show every extreme that they name: Each perms[u, r] lists the 2048 tokens of unit u once each. Cut positions and tokens alike into blocks of 512: at most 192 tokens of one token block stand in one position block, and some pair of blocks reaches 192 in every unit and round. Where unit_kind is 0, the four sequences of a unit are the tokens with (t mod 512) // 128 equal to 0, 1, 2, 3, and each cluster of 64 holds one sequence's tokens.
All inputs are finite; a program needn't handle non-finite values.
Results may differ from the reference program's by a relative error of at most 0.015.
Values may be sent and summed in bfloat16 or wider, within the bound.
No kernel may reach another device: no remote copies, remote signals or barrier semaphores. Data moves between devices by JAX's collectives and lax.ppermute only.
A program may use at most 256 MiB of HBM per device.

```python
import jax
import jax.numpy as jnp
from jax import lax

D = 768
HEAD_DIM = 64
FF = 3072
UNITS = 2
UNIT_TOK = 2048
ROUNDS = 2
UNIT_DEV = 512
UNIT_ALL = 16
TOKENS = 32768
N_DP = 8
N_FSDP = 4


def unit_types(key):
    return jax.random.randint(jax.random.fold_in(key, 101), (UNIT_ALL,), 0, 2).astype(jnp.int32)


def one_perm(key, seg_count):
    shard_count = UNIT_TOK // UNIT_DEV
    per_device = UNIT_DEV
    seg_width = per_device // seg_count
    base_count = seg_width // shard_count
    extra_count = base_count // 2
    sigma_perm = jax.random.permutation(jax.random.fold_in(key, 1), shard_count)
    next_perm = jnp.roll(sigma_perm, -1)
    column_ids = jnp.arange(shard_count)
    counts = base_count + extra_count * (column_ids[None, :] == sigma_perm[:, None]).astype(jnp.int32) - extra_count * (column_ids[None, :] == next_perm[:, None]).astype(jnp.int32)
    bounds = jnp.cumsum(counts, axis=1)
    token_ids = jnp.arange(UNIT_TOK)
    source = token_ids // per_device
    segment = token_ids % per_device // seg_width
    group_ids = source * seg_count + segment
    noise_rank = jax.random.permutation(jax.random.fold_in(key, 2), UNIT_TOK)
    ordering = jnp.argsort(group_ids * UNIT_TOK + noise_rank, stable=True)
    sorted_at = jnp.argsort(ordering, stable=True)
    rank_within = sorted_at - group_ids * seg_width
    destination = jnp.sum((rank_within[:, None] >= bounds[source]).astype(jnp.int32), axis=1)
    place_noise = jax.random.permutation(jax.random.fold_in(key, 3), UNIT_TOK)
    sort_score = (destination * seg_count + segment) * UNIT_TOK + place_noise
    return jnp.argsort(sort_score, stable=True).astype(jnp.int32)


def draw_perms(key, part):
    type_list = unit_types(key)
    key = jax.random.fold_in(key, 7)

    def per_unit(unit_index):
        unit_key = jax.random.fold_in(key, unit_index)
        round_perms = []
        for round_index in range(ROUNDS):
            round_key = jax.random.fold_in(unit_key, round_index)
            short_perm = one_perm(jax.random.fold_in(round_key, 11), 4)
            long_perm = one_perm(jax.random.fold_in(round_key, 13), 1)
            round_perms.append(jnp.where(type_list[unit_index] == 1, long_perm, short_perm))
        return jnp.stack(round_perms)
    return jax.vmap(per_unit)(jnp.arange(UNIT_ALL))


def draw_unit_kind(key, part):
    return unit_types(key)


def block_scale(stream_key, extent, cuts, least, largest):
    def one(axis_at, parts):
        draws = jax.random.uniform(jax.random.fold_in(jax.random.fold_in(stream_key, 6), axis_at), (parts,), jnp.float32, least / len(cuts), largest / len(cuts))
        return jnp.repeat(jnp.exp(draws), extent[axis_at] // parts).reshape((-1,) + (1,) * (len(extent) - axis_at - 1))

    level = one(*cuts[0])
    for cut in cuts[1:]:
        level = level * one(*cut)
    return level


def noise(key, extent, scale, reach, split=(), dtype=jnp.bfloat16):
    result = scale * jax.random.normal(key, extent, jnp.float32)
    if split:
        result = result * block_scale(key, extent, split, -0.22, 0.18)
    return jnp.clip(result, -reach, reach).astype(dtype)


def setup_inputs(seed: int = 0) -> dict:
    seeds = jax.random.split(jax.random.key(seed), 15)
    tokens = noise(seeds[0], (TOKENS, D), 1.0, 6.0, ((0, 32),))
    cotangent = noise(seeds[1], (TOKENS, D), 1.0, 6.0, ((0, 32),))
    perms = draw_perms(jax.random.fold_in(seeds[14], 71), 0)
    unit_kind = draw_unit_kind(jax.random.fold_in(seeds[14], 71), 0)
    w_qkv = noise(seeds[4], (D, 3 * D), D ** -0.5, 0.21875, ((0, 4),))
    bias_qv = noise(seeds[5], (2, D), 0.5, 3.0, ((1, 4),))
    w_out = noise(seeds[6], (D, D), (D // 64) ** -0.5, 1.75, ((0, 4),))
    bias_out = noise(seeds[7], (D,), 0.5, 3.0, ((0, 4),))
    ln_gain = jnp.clip(1.0 + 0.18 * jax.random.normal(seeds[8], (2, D), jnp.float32), 0.099609375, 1.8984375).astype(jnp.bfloat16)
    ln_bias = noise(seeds[9], (2, D), 0.5, 3.0, ((1, 4),))
    w_up = noise(seeds[10], (D, FF), D ** -0.5, 0.21875, ((0, 4),))
    bias_up = noise(seeds[11], (FF,), 0.5, 3.0, ((0, 4),))
    w_down = noise(seeds[12], (FF, D), FF ** -0.5, 0.109375, ((0, 4),))
    bias_down = noise(seeds[13], (D,), 0.5, 3.0, ((0, 4),))
    return dict(tokens=tokens, cotangent=cotangent, perms=perms, unit_kind=unit_kind, w_qkv=w_qkv, bias_qv=bias_qv, w_out=w_out, bias_out=bias_out, ln_gain=ln_gain, ln_bias=ln_bias, w_up=w_up, bias_up=bias_up, w_down=w_down, bias_down=bias_down)


@jax.custom_vjp
def low(v):
    return lax.optimization_barrier(v.astype(jnp.bfloat16)).astype(jnp.float32)

@jax.custom_vjp
def low_back(v):
    return v

def low_keep(v):
    return (low(v), None)

def low_pass(kept, grad):
    return (grad,)

def back_keep(v):
    return (v, None)

def back_low(kept, grad):
    return (low(grad),)
low.defvjp(low_keep, low_pass)
low_back.defvjp(back_keep, back_low)
HIGHEST_MODE = lax.Precision.HIGHEST
NEG_FILL = -1000000000.0
EPSILON = 1e-05
CLUSTER_ROWS = 128
HALF_ROWS = 64

def layer_norm(summed, gain_row, shift_row):
    average = lax.optimization_barrier(jnp.mean(summed, axis=-1, keepdims=True))
    centred = summed - average
    spread = lax.optimization_barrier(jnp.mean(centred * centred, axis=-1, keepdims=True))
    return centred * lax.rsqrt(spread + EPSILON) * gain_row + shift_row

def unit_forward(unit_input, ordering, unit_type, w_qkv, bias_qv, w_out, bias_out, ln_gain, ln_bias, w_up, bias_up, w_down, bias_down):
    model_width = unit_input.shape[1]
    head_count = model_width // HEAD_DIM
    scale = HEAD_DIM ** (-0.5)
    joined_bias = jnp.concatenate([bias_qv[0], jnp.zeros((model_width,), jnp.float32), bias_qv[1]])
    projected = low_back(low(jnp.dot(unit_input, w_qkv, precision=HIGHEST_MODE) + joined_bias))
    position = jnp.arange(CLUSTER_ROWS)
    same_half = position[:, None] // HALF_ROWS == position[None, :] // HALF_ROWS
    allowed = jnp.logical_or(same_half, unit_type == 1)
    attended = jnp.zeros_like(unit_input)
    for round_index in range(ROUNDS):
        order_now = ordering[round_index]
        arranged = low_back(projected[order_now])
        pieces = arranged.reshape(UNIT_TOK // CLUSTER_ROWS, CLUSTER_ROWS, 3, head_count, HEAD_DIM)
        scores = low_back(jnp.einsum('nqhd,nkhd->nhqk', pieces[:, :, 0], pieces[:, :, 1], precision=HIGHEST_MODE)) * scale
        weights = low(jax.nn.softmax(jnp.where(allowed, scores, NEG_FILL), axis=-1))
        mixture = jnp.einsum('nhqk,nkhd->nqhd', weights, pieces[:, :, 2], precision=HIGHEST_MODE).reshape(UNIT_TOK, model_width)
        mixture = low_back(low(mixture))
        attended = attended + jnp.zeros_like(mixture).at[order_now].set(mixture)
    attended = 0.5 * attended
    branch = low_back(jnp.dot(low(attended), w_out, precision=HIGHEST_MODE) + bias_out)
    first_norm = layer_norm(unit_input + branch, ln_gain[0], ln_bias[0])
    pre_act = low_back(jnp.dot(low(first_norm), w_up, precision=HIGHEST_MODE) + bias_up)
    hidden = low(jax.nn.gelu(pre_act, approximate=False))
    ffn_out = low_back(jnp.dot(hidden, w_down, precision=HIGHEST_MODE) + bias_down)
    return layer_norm(first_norm + ffn_out, ln_gain[1], ln_bias[1])

def reference(tokens, cotangent, perms, unit_kind, w_qkv, bias_qv, w_out, bias_out, ln_gain, ln_bias, w_up, bias_up, w_down, bias_down):
    per_device = UNIT_TOK // N_FSDP

    def to_units(array):
        return array.reshape(N_DP, N_FSDP, UNITS, per_device, D).transpose(0, 2, 1, 3, 4).reshape(N_DP * UNITS, UNIT_TOK, D)

    def from_units(array):
        return array.reshape(N_DP, UNITS, N_FSDP, per_device, D).transpose(0, 2, 1, 3, 4).reshape(N_DP * N_FSDP * UNITS * per_device, D)
    params = (w_qkv.astype(jnp.float32), bias_qv.astype(jnp.float32), w_out.astype(jnp.float32), bias_out.astype(jnp.float32), ln_gain.astype(jnp.float32), ln_bias.astype(jnp.float32), w_up.astype(jnp.float32), bias_up.astype(jnp.float32), w_down.astype(jnp.float32), bias_down.astype(jnp.float32))

    def scan_step(state_sum, unit_data):
        unit_input, unit_cot, ordering, unit_type = unit_data

        def forward_only(input_rows, *weights_now):
            return unit_forward(input_rows, ordering, unit_type, *weights_now)
        unit_out, pullback = jax.vjp(forward_only, unit_input, *params)
        gradients = pullback(unit_cot)
        new_sum = tuple((old + new for old, new in zip(state_sum, gradients[1:])))
        return (new_sum, (unit_out.astype(jnp.bfloat16), gradients[0]))
    zero_grads = tuple((jnp.zeros_like(weight) for weight in params))
    unit_inputs = to_units(tokens.astype(jnp.float32))
    unit_cots = to_units(cotangent.astype(jnp.float32))
    sums, (outputs, input_grads) = lax.scan(scan_step, zero_grads, (unit_inputs, unit_cots, perms, unit_kind))
    return (from_units(outputs), from_units(input_grads), sums[0], sums[1], sums[2], sums[3], sums[4], sums[5], sums[6], sums[7], sums[8], sums[9])
```

```python
from functools import partial

import jax
import jax.numpy as jnp
from jax import lax
from jax.experimental import pallas as pl
from jax.experimental.pallas import tpu as pltpu
from jax.sharding import PartitionSpec as P

HEAD_DIM = 64
CORES = 2
NEG_FILL = -1000000000.0
EPSILON = 1e-05
CLUSTER_ROWS = 128
HALF_ROWS = 64
POS_BLOCK = 256
ROW_BLOCK = 256
FF_BLOCK = 512
VMEM_BYTES = 60 * 1024 * 1024
NT = (((1,), (1,)), ((), ()))
TN = (((0,), (0,)), ((), ()))
F32 = jnp.float32
BF16 = jnp.bfloat16
ANYWHERE = pl.BlockSpec(memory_space=pl.ANY)
IN_SMEM = pl.BlockSpec(memory_space=pltpu.SMEM)


def whole(shape):
    return pl.BlockSpec(shape, lambda i: (0,) * len(shape))


def rows_of(shape):
    return pl.BlockSpec(shape, lambda i: (i,) + (0,) * (len(shape) - 1))


def dot(a, b, dims=(((1,), (0,)), ((), ()))):
    return lax.dot_general(a, b, dims, preferred_element_type=F32)


def params(flops=0, moved=0):
    return dict(
        compiler_params=pltpu.CompilerParams(
            dimension_semantics=("arbitrary",), vmem_limit_bytes=VMEM_BYTES
        ),
        cost_estimate=pl.CostEstimate(flops=flops, bytes_accessed=moved, transcendentals=0),
    )


def lane_masks():
    lane = lax.broadcasted_iota(jnp.int32, (CLUSTER_ROWS, CLUSTER_ROWS), 1)
    low = (lane < HEAD_DIM).astype(F32)
    return low.astype(BF16), (1.0 - low).astype(BF16), lane < HEAD_DIM


def both_heads(rows_now, low, high):
    return jnp.concatenate([rows_now * low, rows_now * high], axis=0)


def pick_rows(order_ref, first_row, unit_len):
    parts = []
    for part in range(POS_BLOCK // CLUSTER_ROWS):
        row = order_ref[pl.ds(first_row + part, 1), :]
        column = jnp.transpose(jnp.broadcast_to(row, (CLUSTER_ROWS, CLUSTER_ROWS)))
        lane = lax.broadcasted_iota(jnp.int32, (CLUSTER_ROWS, CLUSTER_ROWS), 1)
        pieces = [
            (column == lane + base).astype(F32).astype(BF16)
            for base in range(0, unit_len, CLUSTER_ROWS)
        ]
        parts.append(jnp.concatenate(pieces, axis=1))
    return jnp.concatenate(parts, axis=0)


def place_rows(order_row_ref, first_token):
    row = order_row_ref[...]
    shape = (POS_BLOCK, row.shape[1])
    token = lax.broadcasted_iota(jnp.int32, shape, 0) + first_token
    return (jnp.broadcast_to(row, shape) == token).astype(F32).astype(BF16)


def attend_kernel(sizes, meta, order_ref, order_row_ref, bias_ref, *refs):
    members, shards, unit_len, row_shard = sizes
    x_refs, refs = refs[:members], refs[members:]
    w_refs, refs = refs[:shards], refs[shards:]
    arranged_ref, probs_ref, refs = refs[0], refs[1], refs[2:]
    out_refs, refs = refs[:members], refs[members:]
    x_all, w_all, mixed, sems = refs
    member_rows = unit_len // members
    width = w_all.shape[1] // 3
    step = pl.program_id(0)

    @pl.when(step == 0)
    def _():
        copies = []
        for index, ref in enumerate(x_refs):
            copies.append(
                pltpu.make_async_copy(
                    ref, x_all.at[pl.ds(index * member_rows, member_rows), :], sems.at[index]
                )
            )
        for index, ref in enumerate(w_refs):
            start = pl.multiple_of(lax.bitwise_xor(meta[1], index) * row_shard, 16)
            copies.append(
                pltpu.make_async_copy(
                    ref.at[pl.ds(0, row_shard), :],
                    w_all.at[pl.ds(start, row_shard), :],
                    sems.at[members + index],
                )
            )
        for copy in copies:
            copy.start()
        for copy in copies:
            copy.wait()

    picks = pick_rows(order_ref, step * (POS_BLOCK // CLUSTER_ROWS), unit_len)
    x_now = dot(picks, x_all[...]).astype(BF16)
    arranged = (dot(x_now, w_all[...]) + bias_ref[...]).astype(BF16)
    arranged_ref[...] = arranged
    low, high, lane_low = lane_masks()
    position = lax.broadcasted_iota(jnp.int32, (CLUSTER_ROWS, CLUSTER_ROWS), 0)
    other = lax.broadcasted_iota(jnp.int32, (CLUSTER_ROWS, CLUSTER_ROWS), 1)
    same_half = (position < HALF_ROWS) == (other < HALF_ROWS)
    shift = jnp.where(
        jnp.logical_or(same_half, meta[0] == 1), jnp.zeros_like(position, F32), NEG_FILL
    )
    scale = HEAD_DIM ** (-0.5)
    for part in range(POS_BLOCK // CLUSTER_ROWS):
        rows_now = slice(part * CLUSTER_ROWS, (part + 1) * CLUSTER_ROWS)
        for pair in range(width // CLUSTER_ROWS):
            base = pair * CLUSTER_ROWS
            queries = arranged[rows_now, base : base + CLUSTER_ROWS]
            keys = arranged[rows_now, width + base : width + base + CLUSTER_ROWS]
            values = arranged[rows_now, 2 * width + base : 2 * width + base + CLUSTER_ROWS]
            scores = dot(queries, both_heads(keys, low, high), NT) * scale
            halves = []
            for head in range(2):
                one = scores[:, head * CLUSTER_ROWS : (head + 1) * CLUSTER_ROWS]
                one = jnp.where(shift < 0, NEG_FILL, one)
                top = jnp.max(one, axis=-1, keepdims=True)
                grown = jnp.exp(one - top)
                halves.append(grown * (1.0 / jnp.sum(grown, axis=-1, keepdims=True)))
            probs = jnp.concatenate(halves, axis=1).astype(BF16)
            probs_ref[rows_now, 2 * base : 2 * base + 2 * CLUSTER_ROWS] = probs
            mixture = dot(probs, both_heads(values, low, high)).astype(BF16)
            at = pl.multiple_of(step * POS_BLOCK + part * CLUSTER_ROWS, CLUSTER_ROWS)
            mixed[pl.ds(at, CLUSTER_ROWS), base : base + CLUSTER_ROWS] = mixture

    @pl.when(step == pl.num_programs(0) - 1)
    def _():
        for member in range(members):

            @pl.loop(0, member_rows // POS_BLOCK)
            def _(block):
                start = pl.multiple_of(block * POS_BLOCK, POS_BLOCK)
                places = place_rows(order_row_ref, member * member_rows + start)
                summed = dot(places, mixed[...])
                out_refs[member][pl.ds(start, POS_BLOCK), :] = (0.5 * summed).astype(BF16)


def attend(meta, order, order_row, bias, x_pieces, w_pieces, row_shard):
    members, shards = len(x_pieces), len(w_pieces)
    member_rows, model_width = x_pieces[0].shape
    unit_len = members * member_rows
    position_count = order_row.shape[1]
    cols = w_pieces[0].shape[1]
    width = cols // 3
    grid = position_count // POS_BLOCK
    return pl.pallas_call(
        partial(attend_kernel, (members, shards, unit_len, row_shard)),
        grid=(grid,),
        in_specs=[IN_SMEM, whole(order.shape), whole(order_row.shape), whole(bias.shape)]
        + [ANYWHERE] * (members + shards),
        out_specs=[rows_of((POS_BLOCK, cols)), rows_of((POS_BLOCK, 2 * width))]
        + [whole((member_rows, width))] * members,
        out_shape=[
            jax.ShapeDtypeStruct((position_count, cols), BF16),
            jax.ShapeDtypeStruct((position_count, 2 * width), BF16),
        ]
        + [jax.ShapeDtypeStruct((member_rows, width), BF16)] * members,
        scratch_shapes=[
            pltpu.VMEM((unit_len, model_width), BF16),
            pltpu.VMEM((model_width, cols), BF16),
            pltpu.VMEM((position_count, width), BF16),
            pltpu.SemaphoreType.DMA((members + shards,)),
        ],
        name="attend",
        **params(
            2 * position_count * (unit_len * (model_width + width) + model_width * cols),
            30_000_000,
        ),
    )(meta, order, order_row, bias, *x_pieces, *w_pieces)


def attend_back_kernel(sizes, meta, order_ref, order_row_ref, arranged_ref, probs_ref, *refs):
    members, shards, unit_len, row_shard = sizes
    g_refs, refs = refs[:members], refs[members:]
    w_refs, refs = refs[:shards], refs[shards:]
    dx_refs, refs = refs[:members], refs[members:]
    dq_refs, refs = refs[:members], refs[members:]
    sums_ref, g_all, w_all, grads, sems = refs
    member_rows = unit_len // members
    width = w_all.shape[1] // 3
    step = pl.program_id(0)

    @pl.when(step == 0)
    def _():
        copies = []
        for index, ref in enumerate(g_refs):
            copies.append(
                pltpu.make_async_copy(
                    ref, g_all.at[pl.ds(index * member_rows, member_rows), :], sems.at[index]
                )
            )
        for index, ref in enumerate(w_refs):
            start = pl.multiple_of(lax.bitwise_xor(meta[1], index) * row_shard, 16)
            copies.append(
                pltpu.make_async_copy(
                    ref.at[pl.ds(0, row_shard), :],
                    w_all.at[pl.ds(start, row_shard), :],
                    sems.at[members + index],
                )
            )
        for copy in copies:
            copy.start()
        for copy in copies:
            copy.wait()

    picks = pick_rows(order_ref, step * (POS_BLOCK // CLUSTER_ROWS), unit_len)
    d_mixture = dot(picks, g_all[...]).astype(BF16)
    low, high, lane_low = lane_masks()
    scale = HEAD_DIM ** (-0.5)
    for part in range(POS_BLOCK // CLUSTER_ROWS):
        rows_now = slice(part * CLUSTER_ROWS, (part + 1) * CLUSTER_ROWS)
        at = pl.multiple_of(step * POS_BLOCK + part * CLUSTER_ROWS, CLUSTER_ROWS)
        for pair in range(width // CLUSTER_ROWS):
            base = pair * CLUSTER_ROWS
            queries = arranged_ref[rows_now, base : base + CLUSTER_ROWS]
            keys = arranged_ref[rows_now, width + base : width + base + CLUSTER_ROWS]
            values = arranged_ref[rows_now, 2 * width + base : 2 * width + base + CLUSTER_ROWS]
            probs = probs_ref[rows_now, 2 * base : 2 * base + 2 * CLUSTER_ROWS]
            d_now = d_mixture[rows_now, base : base + CLUSTER_ROWS]
            d_probs = dot(d_now, both_heads(values, low, high), NT)
            pieces = []
            for head in range(2):
                lanes = slice(head * CLUSTER_ROWS, (head + 1) * CLUSTER_ROWS)
                weight = probs[:, lanes].astype(F32)
                d_one = d_probs[:, lanes]
                inner = jnp.sum(weight * d_one, axis=-1, keepdims=True)
                pieces.append(weight * (d_one - inner) * scale)
            d_scores = jnp.concatenate(pieces, axis=1).astype(BF16)
            d_query = dot(d_scores, both_heads(keys, low, high))
            d_keys = dot(d_scores, queries, TN)
            d_values = dot(probs, d_now, TN)
            grads[pl.ds(at, CLUSTER_ROWS), base : base + CLUSTER_ROWS] = d_query.astype(BF16)
            grads[pl.ds(at, CLUSTER_ROWS), width + base : width + base + CLUSTER_ROWS] = jnp.where(
                lane_low, d_keys[:CLUSTER_ROWS], d_keys[CLUSTER_ROWS:]
            ).astype(BF16)
            grads[
                pl.ds(at, CLUSTER_ROWS), 2 * width + base : 2 * width + base + CLUSTER_ROWS
            ] = jnp.where(lane_low, d_values[:CLUSTER_ROWS], d_values[CLUSTER_ROWS:]).astype(BF16)

    @pl.when(step == pl.num_programs(0) - 1)
    def _():
        sums_ref[...] = jnp.zeros_like(sums_ref)
        for member in range(members):

            @pl.loop(0, member_rows // POS_BLOCK)
            def _(block):
                start = pl.multiple_of(block * POS_BLOCK, POS_BLOCK)
                places = place_rows(order_row_ref, member * member_rows + start)
                summed = dot(places, grads[...]).astype(BF16)
                dq_refs[member][pl.ds(start, POS_BLOCK), :] = summed
                sums_ref[...] += jnp.sum(summed.astype(F32), axis=0, keepdims=True)
                d_x = dot(summed, w_all[...], NT)
                dx_refs[member][pl.ds(start, POS_BLOCK), :] = d_x.astype(dx_refs[member].dtype)


def attend_back(meta, order, order_row, arranged, probs, g_pieces, w_pieces, row_shard):
    members, shards = len(g_pieces), len(w_pieces)
    member_rows, width = g_pieces[0].shape
    unit_len = members * member_rows
    position_count = order_row.shape[1]
    cols = w_pieces[0].shape[1]
    model_width = row_shard * shards
    grid = position_count // POS_BLOCK
    return pl.pallas_call(
        partial(attend_back_kernel, (members, shards, unit_len, row_shard)),
        grid=(grid,),
        in_specs=[
            IN_SMEM,
            whole(order.shape),
            whole(order_row.shape),
            rows_of((POS_BLOCK, cols)),
            rows_of((POS_BLOCK, 2 * width)),
        ]
        + [ANYWHERE] * (members + shards),
        out_specs=[whole((member_rows, model_width))] * members
        + [whole((member_rows, cols))] * members
        + [whole((1, cols))],
        out_shape=[
            jax.ShapeDtypeStruct((member_rows, model_width), F32 if member == 0 else BF16)
            for member in range(members)
        ]
        + [jax.ShapeDtypeStruct((member_rows, cols), BF16)] * members
        + [jax.ShapeDtypeStruct((1, cols), F32)],
        scratch_shapes=[
            pltpu.VMEM((unit_len, width), BF16),
            pltpu.VMEM((model_width, cols), BF16),
            pltpu.VMEM((position_count, cols), BF16),
            pltpu.SemaphoreType.DMA((members + shards,)),
        ],
        name="attend_back",
        **params(2 * position_count * unit_len * (width + cols), 40_000_000),
    )(meta, order, order_row, arranged, probs, *g_pieces, *w_pieces)


def normalise(summed):
    average = jnp.mean(summed, axis=-1, keepdims=True)
    centred = summed - average
    spread = jnp.mean(centred * centred, axis=-1, keepdims=True)
    scale_inv = lax.rsqrt(spread + EPSILON)
    return centred * scale_inv, scale_inv


def normalise_back(grad_out, normed, scale_inv, gain_row):
    scaled = grad_out * gain_row
    return scale_inv * (
        scaled
        - jnp.mean(scaled, axis=-1, keepdims=True)
        - normed * jnp.mean(scaled * normed, axis=-1, keepdims=True)
    )


def column_sum(rows_now):
    return jnp.sum(rows_now, axis=0, keepdims=True)


def gelu_parts(value):
    bell = jnp.exp(-0.5 * value * value)
    inverse = 1.0 / (1.0 + (0.3275911 * 0.7071067811865476) * jnp.abs(value))
    tail = 1.061405429 * inverse - 1.453152027
    tail = tail * inverse + 1.421413741
    tail = tail * inverse - 0.284496736
    tail = tail * inverse + 0.254829592
    tail = 0.5 * tail * inverse * bell
    below = jnp.where(value >= 0, 1.0 - tail, tail)
    return value * below, below + value * bell * 0.3989422804014327


def feed_kernel(sizes, meta, x_ref, cot_ref, vec_ref, up_bias_ref, *refs):
    members, shards, row_shard, out_group = sizes
    att_count = sizes[0]
    att_refs, refs = refs[:att_count], refs[att_count:]
    piece_count = 1 + 2 * (shards - 1)
    out_w, refs = refs[:piece_count], refs[piece_count:]
    up_w, refs = refs[:piece_count], refs[piece_count:]
    down_w, refs = refs[:piece_count], refs[piece_count:]
    out_ref, d_first_low_ref, d_branch_ref, d_ffn_ref, hidden_ref, d_pre_ref, d_h1_ref = refs[:7]
    refs = refs[7:]
    d_att_refs, refs = refs[:att_count], refs[att_count:]
    sums_ref, up_sums_ref, w_out, w_up, w_down, slope, sems = refs
    step = pl.program_id(0)
    here, core, group = meta[1], meta[2], meta[3]
    model_width, feed_width = w_up.shape
    feed_shard = feed_width // shards

    def loads(kind):
        pieces, target, rows = (
            (out_w, w_out, row_shard),
            (up_w, w_up, row_shard),
            (down_w, w_down, feed_shard),
        )[kind]
        half = rows // 2
        copies = []
        for index, ref in enumerate(pieces):
            if index == 0:
                peer, offset, length = here, 0, rows
            elif index < shards:
                peer, offset, length = lax.bitwise_xor(here, index), core * half, half
            else:
                peer = lax.bitwise_xor(here, index - shards + 1)
                offset, length = (1 - core) * half, half
            if kind == 0:
                unit_shards = out_group // row_shard
                start = (
                    lax.bitwise_xor(peer // unit_shards, group) * out_group
                    + (peer % unit_shards) * row_shard
                )
            else:
                start = peer * rows
            start = pl.multiple_of(start + offset, 16)
            copies.append(
                pltpu.make_async_copy(
                    ref, target.at[pl.ds(start, length), :], sems.at[kind * piece_count + index]
                )
            )
        return copies

    @pl.when(step == 0)
    def _():
        for kind in range(3):
            for copy in loads(kind):
                copy.start()
        sums_ref[...] = jnp.zeros_like(sums_ref)
        up_sums_ref[...] = jnp.zeros_like(up_sums_ref)
        for copy in loads(0):
            copy.wait()

    bias_out, gain_one, gain_two = vec_ref[0:1, :], vec_ref[1:2, :], vec_ref[2:3, :]
    shift_one, shift_two, bias_down = vec_ref[3:4, :], vec_ref[4:5, :], vec_ref[5:6, :]
    att_width = att_refs[0].shape[1]
    summed = x_ref[...].astype(F32) + bias_out
    for index, ref in enumerate(att_refs):
        summed += dot(ref[...], w_out[index * att_width : (index + 1) * att_width, :])
    normed_one, inv_one = normalise(summed)
    first = normed_one * gain_one + shift_one
    first_low = first.astype(BF16)
    d_first_low_ref[...] = first_low

    @pl.when(step == 0)
    def _():
        for kind in (1, 2):
            for copy in loads(kind):
                copy.wait()

    second = first + bias_down
    for base in range(0, feed_width, FF_BLOCK):
        lanes = slice(base, base + FF_BLOCK)
        pre = dot(first_low, w_up[:, lanes]) + up_bias_ref[:, lanes]
        hidden, slope_now = gelu_parts(pre)
        hidden = hidden.astype(BF16)
        hidden_ref[:, lanes] = hidden
        slope[:, lanes] = slope_now
        second += dot(hidden, w_down[lanes, :])
    normed_two, inv_two = normalise(second)
    out_ref[...] = (normed_two * gain_two + shift_two).astype(BF16)
    top = cot_ref[...].astype(F32)
    d_second = normalise_back(top, normed_two, inv_two, gain_two)
    d_ffn = d_second.astype(BF16)
    d_ffn_ref[...] = d_ffn
    d_first = d_second
    for base in range(0, feed_width, FF_BLOCK):
        lanes = slice(base, base + FF_BLOCK)
        d_pre = (dot(d_ffn, w_down[lanes, :], NT) * slope[:, lanes]).astype(BF16)
        d_pre_ref[:, lanes] = d_pre
        up_sums_ref[:, lanes] += column_sum(d_pre.astype(F32))
        d_first += dot(d_pre, w_up[:, lanes], NT)
    d_lower = normalise_back(d_first, normed_one, inv_one, gain_one)
    d_h1_ref[...] = d_lower
    d_branch = d_lower.astype(BF16)
    d_branch_ref[...] = d_branch
    for index, ref in enumerate(d_att_refs):
        back = dot(d_branch, w_out[index * att_width : (index + 1) * att_width, :], NT)
        ref[...] = (0.5 * back).astype(BF16)
    sums_ref[0:1, :] += column_sum(d_branch.astype(F32))
    sums_ref[1:2, :] += column_sum(d_first * normed_one)
    sums_ref[2:3, :] += column_sum(top * normed_two)
    sums_ref[3:4, :] += column_sum(d_first)
    sums_ref[4:5, :] += column_sum(top)
    sums_ref[5:6, :] += column_sum(d_ffn.astype(F32))


def feed(meta, x_own, cot_own, vectors, up_bias, att, out_w, up_w, down_w, row_shard, out_group):
    row_count, model_width = x_own.shape
    feed_width = up_bias.shape[1]
    shards = model_width // row_shard
    att_width = att[0].shape[1]
    grid = row_count // ROW_BLOCK
    one = rows_of((ROW_BLOCK, model_width))
    wide = rows_of((ROW_BLOCK, feed_width))
    narrow = rows_of((ROW_BLOCK, att_width))

    def like(width, dtype=BF16):
        return jax.ShapeDtypeStruct((row_count, width), dtype)

    return pl.pallas_call(
        partial(feed_kernel, (len(att), shards, row_shard, out_group)),
        grid=(grid,),
        in_specs=[IN_SMEM, one, one, whole(vectors.shape), whole(up_bias.shape)]
        + [narrow] * len(att)
        + [ANYWHERE] * (len(out_w) + len(up_w) + len(down_w)),
        out_specs=[one, one, one, one, wide, wide, one]
        + [narrow] * len(att)
        + [whole((8, model_width)), whole((1, feed_width))],
        out_shape=[
            like(model_width),
            like(model_width),
            like(model_width),
            like(model_width),
            like(feed_width),
            like(feed_width),
            like(model_width, F32),
        ]
        + [like(att_width)] * len(att)
        + [
            jax.ShapeDtypeStruct((8, model_width), F32),
            jax.ShapeDtypeStruct((1, feed_width), F32),
        ],
        scratch_shapes=[
            pltpu.VMEM((model_width, model_width), BF16),
            pltpu.VMEM((model_width, feed_width), BF16),
            pltpu.VMEM((feed_width, model_width), BF16),
            pltpu.VMEM((ROW_BLOCK, feed_width), F32),
            pltpu.SemaphoreType.DMA((3 * len(up_w),)),
        ],
        name="feed",
        **params(
            2 * row_count * model_width * (2 * model_width + 4 * feed_width), 40_000_000
        ),
    )(meta, x_own, cot_own, vectors, up_bias, *att, *out_w, *up_w, *down_w)


def chain(value, *after):
    return lax.optimization_barrier((value,) + after)[0]


def body(
    tokens,
    cotangent,
    perms,
    unit_kind,
    w_qkv,
    bias_qv,
    w_out,
    bias_out,
    ln_gain,
    ln_bias,
    w_up,
    bias_up,
    w_down,
    bias_down,
):
    shards = lax.axis_size("fsdp")
    groups = lax.axis_size("dp")
    here = lax.axis_index("fsdp")
    dp_index = lax.axis_index("dp")
    core = dp_index % CORES
    depth = groups // CORES
    units, rounds, unit_len = perms.shape
    per_device = unit_len // shards
    model_width = tokens.shape[1]
    feed_width = w_up.shape[1]
    row_shard = model_width // shards
    members = shards // units
    member_rows = unit_len // members
    head_cols = model_width // members
    padded = -(-head_cols // CLUSTER_ROWS) * CLUSTER_ROWS
    place = here * CORES + core
    home_core = place // shards
    unit = (place // members) % units
    member = place % members
    meta_core = core

    def plane_pairs(target):
        pairs = []
        for level in range(depth):
            for f_index in range(shards):
                for c_index in range(CORES):
                    f_new, c_new = target(f_index, c_index)
                    pairs.append(
                        (
                            (level * CORES + c_index) * shards + f_index,
                            (level * CORES + c_new) * shards + f_new,
                        )
                    )
        return pairs

    def send(value, pairs):
        return lax.ppermute(value, ("dp", "fsdp"), pairs)

    def cross(value, mask):
        return send(
            value, plane_pairs(lambda f, c: divmod((f * CORES + c) ^ mask, CORES))
        )

    def climb(value, mask):
        pairs = []
        for level in range(depth):
            for rest in range(CORES * shards):
                pairs.append((level * CORES * shards + rest, (level ^ mask) * CORES * shards + rest))
        return send(value, pairs)

    def outward(step):
        def target(f, c):
            spot = (c * units + (f % units + step) % units) * members + f // units
            return divmod(spot, CORES)

        return plane_pairs(target)

    def homeward(step):
        return [(b, a) for a, b in outward(step)]

    def bring(value):
        blocks = value.reshape(units, per_device, model_width)
        return jnp.concatenate(
            [
                send(
                    lax.dynamic_index_in_dim(
                        blocks, (here % units + step) % units, axis=0, keepdims=False
                    ),
                    outward(step),
                )
                for step in range(units)
            ],
            axis=0,
        )

    def take_home(value):
        blocks = value.reshape(units, per_device, model_width)
        landed = jnp.stack([send(blocks[step], homeward(step)) for step in range(units)])
        wanted = [
            lax.dynamic_index_in_dim(landed, (index - here % units) % units, 0, keepdims=False)
            for index in range(units)
        ]
        return jnp.concatenate(wanted, axis=0)

    x_own = bring(tokens)
    order_pack = jnp.concatenate(
        [perms.reshape(-1), jnp.broadcast_to(unit_kind[:, None], (units, 128)).reshape(-1)]
    )
    order_other = cross(order_pack, 1)
    order_pack = jnp.where(home_core == core, order_pack, order_other)
    unit_perm = lax.dynamic_index_in_dim(
        order_pack[: units * rounds * unit_len].reshape(units, rounds * unit_len),
        unit,
        0,
        keepdims=False,
    )
    kind_now = lax.dynamic_index_in_dim(
        order_pack[units * rounds * unit_len :].reshape(units, 128), unit, 0, keepdims=False
    )[0]
    owner = unit_perm // per_device
    order = (
        (lax.bitwise_xor(owner // units, member) * units + (unit - owner % units) % units)
        * per_device
        + unit_perm % per_device
    )
    order_row = order.reshape(1, rounds * unit_len)
    order = order.reshape(-1, CLUSTER_ROWS)
    meta = jnp.stack([kind_now, here, meta_core, member]).astype(jnp.int32)

    small = jnp.concatenate(
        [
            bias_qv.reshape(-1),
            bias_out,
            ln_gain.reshape(-1),
            ln_bias.reshape(-1),
            bias_up,
            bias_down,
        ]
    )
    columns = w_qkv.reshape(row_shard, 3, members, head_cols)
    small_rows = small.shape[0] // (3 * padded)
    if small.shape[0] % (3 * padded):
        small_rows += 1
    small_flat = jnp.pad(small, (0, small_rows * 3 * padded - small.shape[0]))
    small_block = jnp.pad(
        small_flat.reshape(small_rows, 3 * padded), ((0, 16 - small_rows), (0, 0))
    )

    def columns_for(offset):
        chosen = lax.dynamic_index_in_dim(
            columns, lax.bitwise_xor(member, offset), axis=2, keepdims=False
        )
        chosen = jnp.pad(chosen, ((0, 0), (0, 0), (0, padded - head_cols)))
        return jnp.concatenate([chosen.reshape(row_shard, 3 * padded), small_block], axis=0)

    piece_kinds = {offset: columns_for(offset) for offset in {(CORES * m) % members for m in range(shards)}}
    qkv_pieces = [piece_kinds[0]] + [
        cross(piece_kinds[(CORES * m) % members], CORES * m) for m in range(1, shards)
    ]
    x_pieces = [x_own] + [cross(x_own, mask) for mask in range(1, members)]

    smalls = jnp.stack(
        [
            piece[row_shard : row_shard + small_rows].reshape(-1)[: small.shape[0]]
            for piece in qkv_pieces
        ]
    )
    smalls = jnp.take(smalls, lax.bitwise_xor(here, jnp.arange(shards)), axis=0).astype(F32)

    def vectors_at(start, count, length):
        part = smalls[:, start * row_shard : start * row_shard + count * length]
        return (
            part.reshape(shards, count, length).transpose(1, 0, 2).reshape(count, shards * length)
        )

    full_bias_qv = vectors_at(0, 2, row_shard)
    norm_vectors = vectors_at(2, 5, row_shard)
    up_bias = vectors_at(7, 1, feed_width // shards)
    last = small.shape[0] - row_shard
    down_bias = smalls[:, last:].reshape(1, model_width)
    vectors = jnp.concatenate(
        [norm_vectors, down_bias, jnp.zeros((2, model_width), F32)], axis=0
    )
    my_bias = lax.dynamic_index_in_dim(
        full_bias_qv.reshape(2, members, head_cols), member, 1, keepdims=False
    )
    my_bias = jnp.pad(my_bias, ((0, 0), (0, padded - head_cols)))
    my_bias = jnp.stack([my_bias[0], jnp.zeros_like(my_bias[0]), my_bias[1]]).reshape(1, -1)

    def gather_halves(shard, after):
        half = shard.shape[0] // CORES
        mine = lax.dynamic_slice_in_dim(shard, core * half, half, axis=0)
        mine = chain(mine, after)
        direct = [cross(mine, CORES * m) for m in range(1, shards)]
        return [shard] + direct + [cross(piece, 1) for piece in direct]

    out_pieces = gather_halves(w_out, x_pieces[-1])
    up_pieces = gather_halves(w_up, x_pieces[-1])
    down_pieces = gather_halves(w_down, x_pieces[-1])
    cot_own = bring(chain(cotangent, x_pieces[-1]))

    arranged, probs, *att = attend(
        meta, order, order_row, my_bias, x_pieces, qkv_pieces, row_shard
    )

    def trim(value):
        return value[:, :head_cols]

    att_raw = [trim(att[0])] + [cross(trim(att[mask]), mask) for mask in range(1, members)]
    if head_cols % CLUSTER_ROWS:
        att_raw = [jnp.concatenate(att_raw, axis=1)]
    (
        block_out,
        first_low,
        d_branch,
        d_ffn,
        hidden,
        d_pre,
        d_lower,
        *rest,
    ) = feed(
        meta,
        x_own,
        cot_own,
        vectors,
        up_bias,
        att_raw,
        out_pieces,
        up_pieces,
        down_pieces,
        row_shard,
        head_cols,
    )
    d_att, (row_sums, up_sums) = rest[: len(att_raw)], rest[len(att_raw) :]
    if head_cols % CLUSTER_ROWS:
        d_att = [
            d_att[0][:, mask * head_cols : (mask + 1) * head_cols] for mask in range(members)
        ]
    d_att = [d_att[0]] + [cross(d_att[mask], mask) for mask in range(1, members)]
    d_att = [jnp.pad(piece, ((0, 0), (0, padded - head_cols))) for piece in d_att]
    output = take_home(block_out)

    back = attend_back(
        meta, order, order_row, arranged, probs, d_att, qkv_pieces, row_shard
    )
    dx, dq, (bias_sums,) = back[:members], back[members : 2 * members], back[2 * members :]
    d_inputs = dx[0] + d_lower
    for mask in range(1, members):
        d_inputs = d_inputs + cross(dx[mask], mask).astype(F32)
    d_inputs = take_home(d_inputs.astype(BF16)).astype(F32)

    def grad_of(left, right):
        return lax.dot_general(left, right, TN, preferred_element_type=F32)

    def level_sum(block):
        rows = block.shape[0]
        if depth == 1:
            return block.astype(BF16)
        level = dp_index // CORES
        cut = block.reshape((depth, rows // depth) + block.shape[1:])
        total = lax.dynamic_index_in_dim(cut, level, 0, keepdims=False).astype(F32)
        for mask in range(1, depth):
            piece = lax.dynamic_index_in_dim(cut, lax.bitwise_xor(level, mask), 0, keepdims=False)
            total = total + climb(piece, mask).astype(F32)
        total = total.astype(BF16)
        landed = jnp.stack([total] + [climb(total, mask) for mask in range(1, depth)])
        landed = jnp.take(landed, lax.bitwise_xor(level, jnp.arange(depth)), axis=0)
        return landed.reshape(block.shape)

    def shard_sum(gradient):
        rows = gradient.shape[1]
        half = rows // CORES
        cut = gradient.reshape(shards, CORES, half, gradient.shape[2])
        mine = lax.dynamic_index_in_dim(cut, core, 1, keepdims=False)
        theirs = lax.dynamic_index_in_dim(cut, 1 - core, 1, keepdims=False)
        pair = (mine.astype(F32) + cross(theirs, 1).astype(F32)).astype(BF16)
        total = lax.dynamic_index_in_dim(pair, here, 0, keepdims=False).astype(F32)
        for m in range(1, shards):
            piece = lax.dynamic_index_in_dim(
                pair, lax.bitwise_xor(here, m), 0, keepdims=False
            )
            total = total + cross(piece, CORES * m).astype(F32)
        total = level_sum(total.astype(BF16))
        other = cross(total, 1)
        return jnp.where(
            core == 0,
            jnp.concatenate([total, other], axis=0),
            jnp.concatenate([other, total], axis=0),
        ).astype(F32)

    grad_down = shard_sum(
        grad_of(hidden, d_ffn).astype(BF16).reshape(shards, feed_width // shards, model_width)
    )
    grad_up = shard_sum(
        grad_of(first_low, d_pre).astype(BF16).reshape(shards, row_shard, feed_width)
    )
    out_raw = [grad_of(piece, d_branch).astype(BF16) for piece in att_raw]
    out_raw = jnp.concatenate(out_raw, axis=0).reshape(members, head_cols, model_width)
    out_raw = jnp.take(out_raw, lax.bitwise_xor(member, jnp.arange(members)), axis=0)
    grad_out = shard_sum(out_raw.reshape(shards, row_shard, model_width))

    qkv_grad = sum(grad_of(x_pieces[i], dq[i]) for i in range(members)).astype(BF16)
    qkv_grad = qkv_grad.reshape(shards, row_shard, 3, padded)[..., :head_cols]
    qkv_grad = qkv_grad.reshape(shards, row_shard, 3 * head_cols)
    bias_sums = bias_sums.reshape(3, padded)[:, :head_cols]
    mine_now = (jnp.arange(members) == member)[None, :, None]
    bias_parts = jnp.where(mine_now, bias_sums[::2][:, None, :], 0.0).reshape(2, model_width)

    def by_shard(value):
        count, length = value.shape
        return (
            value.reshape(count, shards, length // shards)
            .transpose(1, 0, 2)
            .reshape(shards, count * length // shards)
        )

    small_grad = jnp.concatenate(
        [
            by_shard(bias_parts),
            by_shard(row_sums[:5]),
            by_shard(up_sums),
            by_shard(row_sums[5:6]),
        ],
        axis=1,
    ).astype(BF16)
    small_length = small_grad.shape[1]
    extra = -(-small_length // (3 * head_cols))
    extra_rows = -(-extra // 16) * 16
    small_grad = jnp.pad(
        small_grad, ((0, 0), (0, extra_rows * 3 * head_cols - small_length))
    ).reshape(shards, extra_rows, 3 * head_cols)
    packed = jnp.concatenate([qkv_grad, small_grad], axis=1)
    classes = max(1, members // CORES)
    totals = [None] * classes
    for m in range(shards):
        offset = ((CORES * m) % members) // CORES
        piece = lax.dynamic_index_in_dim(packed, lax.bitwise_xor(here, m), 0, keepdims=False)
        piece = (piece if m == 0 else cross(piece, CORES * m)).astype(F32)
        totals[offset] = piece if totals[offset] is None else totals[offset] + piece
    stacked = jnp.concatenate(totals, axis=0).astype(BF16)
    stacked = level_sum(stacked)
    stacked_other = cross(stacked, 1)
    rows_each = row_shard + extra_rows
    landed = jnp.stack([stacked, stacked_other], axis=0).reshape(
        CORES, classes, rows_each, 3 * head_cols
    )
    smalls_out = jnp.sum(
        landed[:, :, row_shard:].astype(F32), axis=(0, 1)
    ).reshape(-1)[:small_length]
    landed = landed[:, :, :row_shard].transpose(1, 0, 2, 3).reshape(
        members, row_shard, 3, head_cols
    )
    landed = jnp.take(landed, lax.bitwise_xor(member, jnp.arange(members)), axis=0)
    grad_qkv = landed.transpose(1, 2, 0, 3).reshape(row_shard, 3 * model_width).astype(F32)

    feed_shard = feed_width // shards
    spots = [2 * row_shard, 3 * row_shard, 5 * row_shard, 7 * row_shard]
    return (
        output,
        d_inputs,
        grad_qkv,
        smalls_out[: spots[0]].reshape(2, row_shard),
        grad_out,
        smalls_out[spots[0] : spots[1]],
        smalls_out[spots[1] : spots[2]].reshape(2, row_shard),
        smalls_out[spots[2] : spots[3]].reshape(2, row_shard),
        grad_up,
        smalls_out[spots[3] : spots[3] + feed_shard],
        grad_down,
        smalls_out[spots[3] + feed_shard :],
    )


def solution(mesh):
    placed = (
        P(("dp", "fsdp"), None),
        P(("dp", "fsdp"), None),
        P("dp", None, None),
        P("dp"),
        P("fsdp", None),
        P(None, "fsdp"),
        P("fsdp", None),
        P("fsdp"),
        P(None, "fsdp"),
        P(None, "fsdp"),
        P("fsdp", None),
        P("fsdp"),
        P("fsdp", None),
        P("fsdp"),
    )
    return jax.shard_map(
        body,
        mesh=mesh,
        in_specs=placed,
        out_specs=(
            P(("dp", "fsdp"), None),
            P(("dp", "fsdp"), None),
            P("fsdp", None),
            P(None, "fsdp"),
            P("fsdp", None),
            P("fsdp"),
            P(None, "fsdp"),
            P(None, "fsdp"),
            P("fsdp", None),
            P("fsdp"),
            P("fsdp", None),
            P("fsdp"),
        ),
        check_vma=False,
    )
```

```python
from functools import partial

import jax
import jax.numpy as jnp
from jax import lax
from jax.experimental import pallas as pl
from jax.experimental.pallas import tpu as pltpu
from jax.sharding import PartitionSpec as P

HEAD_DIM = 64
CORES = 2
NEG_FILL = -1000000000.0
EPSILON = 1e-05
CLUSTER_ROWS = 128
HALF_ROWS = 64
POS_BLOCK = 512
TOKEN_BLOCK = 512
ROW_BLOCK = 256
FF_BLOCK = 512
VMEM_BYTES = 60 * 1024 * 1024
NT = (((1,), (1,)), ((), ()))
TN = (((0,), (0,)), ((), ()))
F32 = jnp.float32
BF16 = jnp.bfloat16
ANYWHERE = pl.BlockSpec(memory_space=pl.ANY)
IN_SMEM = pl.BlockSpec(memory_space=pltpu.SMEM)


def whole(shape):
    return pl.BlockSpec(shape, lambda i: (0,) * len(shape))


def rows_of(shape):
    return pl.BlockSpec(shape, lambda i: (i,) + (0,) * (len(shape) - 1))


def dot(a, b, dims=(((1,), (0,)), ((), ()))):
    return lax.dot_general(a, b, dims, preferred_element_type=F32)


def params(flops=0, moved=0):
    return dict(
        compiler_params=pltpu.CompilerParams(
            dimension_semantics=("arbitrary",), vmem_limit_bytes=VMEM_BYTES
        ),
        cost_estimate=pl.CostEstimate(flops=flops, bytes_accessed=moved, transcendentals=0),
    )


def lane_masks():
    lane = lax.broadcasted_iota(jnp.int32, (CLUSTER_ROWS, CLUSTER_ROWS), 1)
    low = (lane < HEAD_DIM).astype(F32)
    return low.astype(BF16), (1.0 - low).astype(BF16), lane < HEAD_DIM


def both_heads(rows_now, low, high):
    return jnp.concatenate([rows_now * low, rows_now * high], axis=0)


def pick_rows(order_ref, first_row, unit_len):
    parts = []
    for part in range(POS_BLOCK // CLUSTER_ROWS):
        row = order_ref[pl.ds(first_row + part, 1), :]
        column = jnp.transpose(jnp.broadcast_to(row, (CLUSTER_ROWS, CLUSTER_ROWS)))
        lane = lax.broadcasted_iota(jnp.int32, (CLUSTER_ROWS, CLUSTER_ROWS), 1)
        pieces = [
            (column == lane + base).astype(F32).astype(BF16)
            for base in range(0, unit_len, CLUSTER_ROWS)
        ]
        parts.append(jnp.concatenate(pieces, axis=1))
    return jnp.concatenate(parts, axis=0)


def load_pieces(meta, x_refs, w_refs, x_all, w_all, sems, row_shard):
    member_rows = x_all.shape[0] // len(x_refs)
    copies = []
    for index, ref in enumerate(x_refs):
        copies.append(
            pltpu.make_async_copy(
                ref, x_all.at[pl.ds(index * member_rows, member_rows), :], sems.at[index]
            )
        )
    for index, ref in enumerate(w_refs):
        start = pl.multiple_of(lax.bitwise_xor(meta[1], index) * row_shard, 16)
        copies.append(
            pltpu.make_async_copy(
                ref.at[pl.ds(0, row_shard), :],
                w_all.at[pl.ds(start, row_shard), :],
                sems.at[len(x_refs) + index],
            )
        )
    for copy in copies:
        copy.start()
    for copy in copies:
        copy.wait()


def attend_kernel(sizes, meta, order_ref, bias_ref, *refs):
    members, shards, unit_len, row_shard, first_row = sizes
    x_refs, refs = refs[:members], refs[members:]
    w_refs, refs = refs[:shards], refs[shards:]
    x_now_ref, arranged_ref, probs_ref, mixture_ref, x_all, w_all, sems = refs
    width = w_all.shape[1] // 3
    step = pl.program_id(0)

    @pl.when(step == 0)
    def _():
        load_pieces(meta, x_refs, w_refs, x_all, w_all, sems, row_shard)

    picks = pick_rows(order_ref, first_row + step * (POS_BLOCK // CLUSTER_ROWS), unit_len)
    x_now = dot(picks, x_all[...]).astype(BF16)
    x_now_ref[...] = x_now
    arranged = (dot(x_now, w_all[...]) + bias_ref[...]).astype(BF16)
    arranged_ref[...] = arranged
    low, high, lane_low = lane_masks()
    position = lax.broadcasted_iota(jnp.int32, (CLUSTER_ROWS, CLUSTER_ROWS), 0)
    other = lax.broadcasted_iota(jnp.int32, (CLUSTER_ROWS, CLUSTER_ROWS), 1)
    same_half = (position < HALF_ROWS) == (other < HALF_ROWS)
    allowed = jnp.logical_or(same_half, meta[0] == 1)
    scale = HEAD_DIM ** (-0.5)
    for part in range(POS_BLOCK // CLUSTER_ROWS):
        rows_now = slice(part * CLUSTER_ROWS, (part + 1) * CLUSTER_ROWS)
        for pair in range(width // CLUSTER_ROWS):
            base = pair * CLUSTER_ROWS
            queries = arranged[rows_now, base : base + CLUSTER_ROWS]
            keys = arranged[rows_now, width + base : width + base + CLUSTER_ROWS]
            values = arranged[rows_now, 2 * width + base : 2 * width + base + CLUSTER_ROWS]
            scores = dot(queries, both_heads(keys, low, high), NT) * scale
            halves = []
            for head in range(2):
                one = scores[:, head * CLUSTER_ROWS : (head + 1) * CLUSTER_ROWS]
                one = jnp.where(allowed, one, NEG_FILL)
                top = jnp.max(one, axis=-1, keepdims=True)
                grown = jnp.exp(one - top)
                halves.append(grown * (1.0 / jnp.sum(grown, axis=-1, keepdims=True)))
            probs = jnp.concatenate(halves, axis=1).astype(BF16)
            probs_ref[rows_now, 2 * base : 2 * base + 2 * CLUSTER_ROWS] = probs
            mixture = dot(probs, both_heads(values, low, high)).astype(BF16)
            mixture_ref[rows_now, base : base + CLUSTER_ROWS] = mixture


def attend(meta, order, bias, x_pieces, w_pieces, row_shard, position_count, first_row):
    members, shards = len(x_pieces), len(w_pieces)
    member_rows, model_width = x_pieces[0].shape
    unit_len = members * member_rows
    cols = w_pieces[0].shape[1]
    width = cols // 3
    outs = (model_width, cols, 2 * width, width)
    return pl.pallas_call(
        partial(attend_kernel, (members, shards, unit_len, row_shard, first_row)),
        grid=(position_count // POS_BLOCK,),
        in_specs=[IN_SMEM, whole(order.shape), whole(bias.shape)] + [ANYWHERE] * (members + shards),
        out_specs=[rows_of((POS_BLOCK, length)) for length in outs],
        out_shape=[jax.ShapeDtypeStruct((position_count, length), BF16) for length in outs],
        scratch_shapes=[
            pltpu.VMEM((unit_len, model_width), BF16),
            pltpu.VMEM((model_width, cols), BF16),
            pltpu.SemaphoreType.DMA((members + shards,)),
        ],
        name="attend",
        **params(
            2 * position_count * (unit_len * model_width + model_width * cols), 20_000_000
        ),
    )(meta, order, bias, *x_pieces, *w_pieces)


def place_kernel(sizes, scale, has_base, order_row_ref, *refs):
    unit_len, first_token = sizes
    base_ref = refs[0] if has_base else None
    source_refs, out_ref = refs[1 if has_base else 0 : -1], refs[-1]
    block_rows = out_ref.shape[0]
    token = (
        lax.broadcasted_iota(jnp.int32, (block_rows, unit_len), 0)
        + first_token
        + pl.program_id(0) * block_rows
    )
    total = None
    for index, ref in enumerate(source_refs):
        row = order_row_ref[:, index * unit_len : (index + 1) * unit_len]
        places = (jnp.broadcast_to(row, token.shape) == token).astype(F32).astype(BF16)
        term = dot(places, ref[...])
        total = term if total is None else total + term
    if scale != 1.0:
        total = total * scale
    if has_base:
        total = total + base_ref[...]
    out_ref[...] = total.astype(out_ref.dtype)


def place(order_row, sources, first_token, row_count, scale=1.0, dtype=BF16, base=None):
    unit_len, width = sources[0].shape
    block_rows = min(TOKEN_BLOCK, row_count)
    extra = [] if base is None else [base]
    return pl.pallas_call(
        partial(place_kernel, (unit_len, first_token), scale, base is not None),
        grid=(row_count // block_rows,),
        in_specs=[whole(order_row.shape)]
        + [rows_of((block_rows, width))] * len(extra)
        + [whole(source.shape) for source in sources],
        out_specs=rows_of((block_rows, width)),
        out_shape=jax.ShapeDtypeStruct((row_count, width), dtype),
        name="place",
        **params(2 * row_count * unit_len * len(sources) * width, 10_000_000),
    )(order_row, *extra, *sources)


def attend_back_kernel(sizes, meta, order_ref, arranged_ref, probs_ref, *refs):
    members, shards, unit_len, row_shard, first_row = sizes
    g_refs, refs = refs[:members], refs[members:]
    w_refs, refs = refs[:shards], refs[shards:]
    grads_ref, d_x_ref, sums_ref, g_all, w_all, sems = refs
    width = w_all.shape[1] // 3
    step = pl.program_id(0)

    @pl.when(step == 0)
    def _():
        load_pieces(meta, g_refs, w_refs, g_all, w_all, sems, row_shard)
        sums_ref[...] = jnp.zeros_like(sums_ref)

    picks = pick_rows(order_ref, first_row + step * (POS_BLOCK // CLUSTER_ROWS), unit_len)
    d_mixture = dot(picks, g_all[...]).astype(BF16)
    low, high, lane_low = lane_masks()
    scale = HEAD_DIM ** (-0.5)
    for part in range(POS_BLOCK // CLUSTER_ROWS):
        rows_now = slice(part * CLUSTER_ROWS, (part + 1) * CLUSTER_ROWS)
        for pair in range(width // CLUSTER_ROWS):
            base = pair * CLUSTER_ROWS
            q_lanes = slice(base, base + CLUSTER_ROWS)
            k_lanes = slice(width + base, width + base + CLUSTER_ROWS)
            v_lanes = slice(2 * width + base, 2 * width + base + CLUSTER_ROWS)
            queries = arranged_ref[rows_now, q_lanes]
            keys = arranged_ref[rows_now, k_lanes]
            values = arranged_ref[rows_now, v_lanes]
            probs = probs_ref[rows_now, 2 * base : 2 * base + 2 * CLUSTER_ROWS]
            d_now = d_mixture[rows_now, base : base + CLUSTER_ROWS]
            d_probs = dot(d_now, both_heads(values, low, high), NT)
            pieces = []
            for head in range(2):
                lanes = slice(head * CLUSTER_ROWS, (head + 1) * CLUSTER_ROWS)
                weight = probs[:, lanes].astype(F32)
                d_one = d_probs[:, lanes]
                inner = jnp.sum(weight * d_one, axis=-1, keepdims=True)
                pieces.append(weight * (d_one - inner) * scale)
            d_scores = jnp.concatenate(pieces, axis=1).astype(BF16)
            d_query = dot(d_scores, both_heads(keys, low, high))
            d_keys = dot(d_scores, queries, TN)
            d_values = dot(probs, d_now, TN)
            grads_ref[rows_now, q_lanes] = d_query.astype(BF16)
            grads_ref[rows_now, k_lanes] = jnp.where(
                lane_low, d_keys[:CLUSTER_ROWS], d_keys[CLUSTER_ROWS:]
            ).astype(BF16)
            grads_ref[rows_now, v_lanes] = jnp.where(
                lane_low, d_values[:CLUSTER_ROWS], d_values[CLUSTER_ROWS:]
            ).astype(BF16)
    grads = grads_ref[...]
    sums_ref[...] += jnp.sum(grads.astype(F32), axis=0, keepdims=True)
    d_x_ref[...] = dot(grads, w_all[...], NT).astype(BF16)


def attend_back(meta, order, arranged, probs, g_pieces, w_pieces, row_shard, first_row):
    members, shards = len(g_pieces), len(w_pieces)
    member_rows, width = g_pieces[0].shape
    unit_len = members * member_rows
    position_count, cols = arranged.shape
    model_width = row_shard * shards
    return pl.pallas_call(
        partial(attend_back_kernel, (members, shards, unit_len, row_shard, first_row)),
        grid=(position_count // POS_BLOCK,),
        in_specs=[
            IN_SMEM,
            whole(order.shape),
            rows_of((POS_BLOCK, cols)),
            rows_of((POS_BLOCK, 2 * width)),
        ]
        + [ANYWHERE] * (members + shards),
        out_specs=[
            rows_of((POS_BLOCK, cols)),
            rows_of((POS_BLOCK, model_width)),
            whole((1, cols)),
        ],
        out_shape=[
            jax.ShapeDtypeStruct((position_count, cols), BF16),
            jax.ShapeDtypeStruct((position_count, model_width), BF16),
            jax.ShapeDtypeStruct((1, cols), F32),
        ],
        scratch_shapes=[
            pltpu.VMEM((unit_len, width), BF16),
            pltpu.VMEM((model_width, cols), BF16),
            pltpu.SemaphoreType.DMA((members + shards,)),
        ],
        name="attend_back",
        **params(2 * position_count * (unit_len * width + model_width * cols), 20_000_000),
    )(meta, order, arranged, probs, *g_pieces, *w_pieces)


def normalise(summed):
    average = jnp.mean(summed, axis=-1, keepdims=True)
    centred = summed - average
    spread = jnp.mean(centred * centred, axis=-1, keepdims=True)
    scale_inv = lax.rsqrt(spread + EPSILON)
    return centred * scale_inv, scale_inv


def normalise_back(grad_out, normed, scale_inv, gain_row):
    scaled = grad_out * gain_row
    return scale_inv * (
        scaled
        - jnp.mean(scaled, axis=-1, keepdims=True)
        - normed * jnp.mean(scaled * normed, axis=-1, keepdims=True)
    )


def column_sum(rows_now):
    return jnp.sum(rows_now, axis=0, keepdims=True)


def gelu_parts(value):
    bell = jnp.exp(-0.5 * value * value)
    inverse = 1.0 / (1.0 + (0.3275911 * 0.7071067811865476) * jnp.abs(value))
    tail = 1.061405429 * inverse - 1.453152027
    tail = tail * inverse + 1.421413741
    tail = tail * inverse - 0.284496736
    tail = tail * inverse + 0.254829592
    tail = 0.5 * tail * inverse * bell
    below = jnp.where(value >= 0, 1.0 - tail, tail)
    return value * below, below + value * bell * 0.3989422804014327


class Pack:
    def __init__(self, model_width, feed_width, shards, units, depth):
        self.model_width, self.feed_width, self.shards = model_width, feed_width, shards
        self.row_shard = model_width // shards
        self.feed_shard = feed_width // shards
        self.down_rows = self.feed_shard // CORES
        self.blocks = feed_width // CORES // model_width
        self.up_at = self.down_rows
        self.out_at = self.up_at + self.blocks * self.row_shard
        self.out_rows = self.row_shard // CORES
        self.used = self.out_at + self.out_rows
        unit = 16 * depth
        self.rows = -(-self.used // unit) * unit
        self.units = units
        self.group = units * self.row_shard

    def out_start(self, shard, member):
        return (
            lax.bitwise_xor(jnp.int32(shard) // self.units, member) * self.group
            + (shard % self.units) * self.row_shard
        )


def feed_kernel(pack, att_count, meta, x_ref, cot_ref, vec_ref, up_bias_ref, *refs):
    shards = pack.shards
    att_refs, refs = refs[:att_count], refs[att_count:]
    own_out, own_up, own_down = refs[:3]
    refs = refs[3:]
    pieces, refs = refs[: 2 * (shards - 1)], refs[2 * (shards - 1) :]
    out_ref, first_low_ref, d_branch_ref, d_ffn_ref, hidden_ref, d_pre_ref, d_h1_ref = refs[:7]
    refs = refs[7:]
    d_att_refs, refs = refs[:att_count], refs[att_count:]
    sums_ref, up_sums_ref, w_out, w_up, w_down, slope, sems = refs
    step = pl.program_id(0)
    here, core, member = meta[1], meta[2], meta[3]
    feed_width = pack.feed_width

    def loads(kind):
        copies = []

        def add(source, target):
            copies.append(pltpu.make_async_copy(source, target, sems.at[kind, len(copies)]))

        if kind == 0:
            start = pl.multiple_of(pack.out_start(here, member), 16)
            add(own_out, w_out.at[pl.ds(start, pack.row_shard), :])
        elif kind == 1:
            start = pl.multiple_of(here * pack.row_shard, 16)
            add(own_up, w_up.at[pl.ds(start, pack.row_shard), :])
        else:
            start = pl.multiple_of(here * pack.feed_shard, 16)
            add(own_down, w_down.at[pl.ds(start, pack.feed_shard), :])
        for index, ref in enumerate(pieces):
            peer = lax.bitwise_xor(here, meta[8 + index])
            half = core if index < shards - 1 else 1 - core
            if kind == 0:
                start = pack.out_start(peer, member) + half * pack.out_rows
                start = pl.multiple_of(start, 16)
                add(
                    ref.at[pl.ds(pack.out_at, pack.out_rows), :],
                    w_out.at[pl.ds(start, pack.out_rows), :],
                )
            elif kind == 1:
                start = pl.multiple_of(peer * pack.row_shard, 16)
                for block in range(pack.blocks):
                    lane = pl.multiple_of(
                        (half * pack.blocks + block) * pack.model_width, CLUSTER_ROWS
                    )
                    add(
                        ref.at[pl.ds(pack.up_at + block * pack.row_shard, pack.row_shard), :],
                        w_up.at[pl.ds(start, pack.row_shard), pl.ds(lane, pack.model_width)],
                    )
            else:
                start = pl.multiple_of(peer * pack.feed_shard + half * pack.down_rows, 16)
                add(
                    ref.at[pl.ds(0, pack.down_rows), :],
                    w_down.at[pl.ds(start, pack.down_rows), :],
                )
        return copies

    @pl.when(step == 0)
    def _():
        for kind in range(3):
            for copy in loads(kind):
                copy.start()
        sums_ref[...] = jnp.zeros_like(sums_ref)
        up_sums_ref[...] = jnp.zeros_like(up_sums_ref)
        for copy in loads(0):
            copy.wait()

    bias_out, gain_one, gain_two = vec_ref[0:1, :], vec_ref[1:2, :], vec_ref[2:3, :]
    shift_one, shift_two, bias_down = vec_ref[3:4, :], vec_ref[4:5, :], vec_ref[5:6, :]
    att_width = att_refs[0].shape[1]
    summed = x_ref[...].astype(F32) + bias_out
    for index, ref in enumerate(att_refs):
        summed += dot(ref[...], w_out[index * att_width : (index + 1) * att_width, :])
    normed_one, inv_one = normalise(summed)
    first = normed_one * gain_one + shift_one
    first_low = first.astype(BF16)
    first_low_ref[...] = first_low

    @pl.when(step == 0)
    def _():
        for kind in (1, 2):
            for copy in loads(kind):
                copy.wait()

    second = first + bias_down
    for base in range(0, feed_width, FF_BLOCK):
        lanes = slice(base, base + FF_BLOCK)
        pre = dot(first_low, w_up[:, lanes]) + up_bias_ref[:, lanes]
        hidden, slope_now = gelu_parts(pre)
        hidden = hidden.astype(BF16)
        hidden_ref[:, lanes] = hidden
        slope[:, lanes] = slope_now
        second += dot(hidden, w_down[lanes, :])
    normed_two, inv_two = normalise(second)
    out_ref[...] = (normed_two * gain_two + shift_two).astype(BF16)
    top = cot_ref[...].astype(F32)
    d_second = normalise_back(top, normed_two, inv_two, gain_two)
    d_ffn = d_second.astype(BF16)
    d_ffn_ref[...] = d_ffn
    d_first = d_second
    for base in range(0, feed_width, FF_BLOCK):
        lanes = slice(base, base + FF_BLOCK)
        d_pre = (dot(d_ffn, w_down[lanes, :], NT) * slope[:, lanes]).astype(BF16)
        d_pre_ref[:, lanes] = d_pre
        up_sums_ref[:, lanes] += column_sum(d_pre.astype(F32))
        d_first += dot(d_pre, w_up[:, lanes], NT)
    d_lower = normalise_back(d_first, normed_one, inv_one, gain_one)
    d_h1_ref[...] = d_lower
    d_branch = d_lower.astype(BF16)
    d_branch_ref[...] = d_branch
    for index, ref in enumerate(d_att_refs):
        back = dot(d_branch, w_out[index * att_width : (index + 1) * att_width, :], NT)
        ref[...] = (0.5 * back).astype(BF16)
    sums_ref[0:1, :] += column_sum(d_branch.astype(F32))
    sums_ref[1:2, :] += column_sum(d_first * normed_one)
    sums_ref[2:3, :] += column_sum(top * normed_two)
    sums_ref[3:4, :] += column_sum(d_first)
    sums_ref[4:5, :] += column_sum(top)
    sums_ref[5:6, :] += column_sum(d_ffn.astype(F32))


def feed(pack, meta, x_own, cot_own, vectors, up_bias, att, own, pieces):
    row_count, model_width = x_own.shape
    feed_width = pack.feed_width
    att_width = att[0].shape[1]
    one = rows_of((ROW_BLOCK, model_width))
    wide = rows_of((ROW_BLOCK, feed_width))
    narrow = rows_of((ROW_BLOCK, att_width))

    def like(width, dtype=BF16):
        return jax.ShapeDtypeStruct((row_count, width), dtype)

    return pl.pallas_call(
        partial(feed_kernel, pack, len(att)),
        grid=(row_count // ROW_BLOCK,),
        in_specs=[IN_SMEM, one, one, whole(vectors.shape), whole(up_bias.shape)]
        + [narrow] * len(att)
        + [ANYWHERE] * (3 + len(pieces)),
        out_specs=[one, one, one, one, wide, wide, one]
        + [narrow] * len(att)
        + [whole((8, model_width)), whole((1, feed_width))],
        out_shape=[
            like(model_width),
            like(model_width),
            like(model_width),
            like(model_width),
            like(feed_width),
            like(feed_width),
            like(model_width, F32),
        ]
        + [like(att_width)] * len(att)
        + [
            jax.ShapeDtypeStruct((8, model_width), F32),
            jax.ShapeDtypeStruct((1, feed_width), F32),
        ],
        scratch_shapes=[
            pltpu.VMEM((model_width, model_width), BF16),
            pltpu.VMEM((model_width, feed_width), BF16),
            pltpu.VMEM((feed_width, model_width), BF16),
            pltpu.VMEM((ROW_BLOCK, feed_width), F32),
            pltpu.SemaphoreType.DMA((3, 1 + pack.blocks * len(pieces))),
        ],
        name="feed",
        **params(
            2 * row_count * model_width * (2 * model_width + 4 * feed_width), 40_000_000
        ),
    )(meta, x_own, cot_own, vectors, up_bias, *att, *own, *pieces)


def weight_grads_kernel(pack, split, att_count, table, hidden_ref, d_pre_ref, d_ffn_ref, *refs):
    first_low_ref, d_branch_ref = refs[:2]
    att_refs, (out_ref, tile) = refs[2 : 2 + att_count], refs[2 + att_count :]
    step = pl.program_id(0)
    half, member = table[0], table[1]

    @pl.when(step == 0)
    def _():
        spare = pack.rows - pack.used
        if spare:
            for shard in range(pack.shards):
                out_ref[shard, pack.used :, :] = jnp.zeros((spare, pack.model_width), BF16)

    @pl.when(step < pack.shards)
    def _():
        grad = dot(hidden_ref[...], d_ffn_ref[...], TN)
        if split:
            out_ref[step, : pack.down_rows, :] = grad.astype(BF16)
        else:
            tile[: pack.feed_shard, :] = grad
            start = pl.multiple_of(half * pack.down_rows, 16)
            out_ref[step, : pack.down_rows, :] = tile[pl.ds(start, pack.down_rows), :].astype(BF16)

    @pl.when(jnp.logical_and(step >= pack.shards, step < pack.shards + pack.blocks))
    def _():
        grad = dot(first_low_ref[...], d_pre_ref[...], TN)
        start = pack.up_at + (step - pack.shards) * pack.row_shard
        start = pl.multiple_of(start, 16)
        for shard in range(pack.shards):
            out_ref[shard, pl.ds(start, pack.row_shard), :] = grad[
                shard * pack.row_shard : (shard + 1) * pack.row_shard
            ].astype(BF16)

    @pl.when(step == pack.shards + pack.blocks)
    def _():
        width = att_refs[0].shape[1]
        for index, ref in enumerate(att_refs):
            tile[index * width : (index + 1) * width, :] = dot(ref[...], d_branch_ref[...], TN)
        for shard in range(pack.shards):
            start = pack.out_start(shard, member) + half * pack.out_rows
            start = pl.multiple_of(start, 16)
            out_ref[shard, pack.out_at : pack.out_at + pack.out_rows, :] = tile[
                pl.ds(start, pack.out_rows), :
            ].astype(BF16)


def weight_grads(pack, table, hidden, d_pre, d_ffn, first_low, d_branch, att):
    row_count, model_width = d_ffn.shape
    shards, blocks = pack.shards, pack.blocks
    split = pack.down_rows % CLUSTER_ROWS == 0
    wide = pack.down_rows if split else pack.feed_shard

    def hidden_at(step, table):
        shard = jnp.minimum(step, shards - 1)
        return (0, shard * CORES + table[0] if split else shard)

    def d_pre_at(step, table):
        return (0, table[0] * blocks + jnp.clip(step - shards, 0, blocks - 1))

    def all_of(shape):
        return pl.BlockSpec(shape, lambda step, table: (0,) * len(shape))

    shape = (shards, pack.rows, model_width)
    return pl.pallas_call(
        partial(weight_grads_kernel, pack, split, len(att)),
        grid_spec=pltpu.PrefetchScalarGridSpec(
            num_scalar_prefetch=1,
            grid=(shards + blocks + 1,),
            in_specs=[
                pl.BlockSpec((row_count, wide), hidden_at),
                pl.BlockSpec((row_count, model_width), d_pre_at),
                all_of(d_ffn.shape),
                all_of(first_low.shape),
                all_of(d_branch.shape),
            ]
            + [all_of(piece.shape) for piece in att],
            out_specs=all_of(shape),
            scratch_shapes=[pltpu.VMEM((max(model_width, pack.feed_shard), model_width), F32)],
        ),
        out_shape=jax.ShapeDtypeStruct(shape, BF16),
        name="weight_grads",
        **params(row_count * model_width * (2 * pack.feed_width + model_width), 20_000_000),
    )(table, hidden, d_pre, d_ffn, first_low, d_branch, *att)


def add_picked_kernel(count, first, table, *refs):
    in_refs, out_refs = refs[:count], refs[count:]
    total = in_refs[0][...].astype(F32)
    for ref in in_refs[1:]:
        total = total + ref[...].astype(F32)
    total = total.astype(BF16)
    if len(out_refs) == 1:
        out_refs[0][...] = total
        return

    @pl.when(pl.program_id(0) < first)
    def _():
        out_refs[0][...] = total

    @pl.when(pl.program_id(0) >= first)
    def _():
        out_refs[1][...] = total


def add_picked(table, arrays, steps, first=None):
    block = (1,) + arrays[0].shape[1:]
    spec = [
        pl.BlockSpec(block, lambda s, t, k=k: (t[k * steps + s], 0, 0)) for k in range(len(arrays))
    ]
    if first is None:
        out_specs = [pl.BlockSpec(block, lambda s, t: (s, 0, 0))]
        counts = [steps]
    else:
        out_specs = [
            pl.BlockSpec(block, lambda s, t: (jnp.minimum(s, first - 1), 0, 0)),
            pl.BlockSpec(block, lambda s, t: (jnp.maximum(s - first, 0), 0, 0)),
        ]
        counts = [first, steps - first]
    return pl.pallas_call(
        partial(add_picked_kernel, len(arrays), first),
        grid_spec=pltpu.PrefetchScalarGridSpec(
            num_scalar_prefetch=1, grid=(steps,), in_specs=spec, out_specs=out_specs
        ),
        out_shape=[jax.ShapeDtypeStruct((n,) + block[1:], BF16) for n in counts],
        name="add_picked",
        **params(0, 2 * steps * (len(arrays) + 1) * block[1] * block[2]),
    )(table, *arrays)


def unpack_kernel(pack, depth, meta, mine_ref, other_ref, down_ref, up_ref, out_ref, ordered):
    core, level = meta[2], meta[4]
    rows = pack.rows // depth
    for mask in range(depth):
        start = pl.multiple_of(lax.bitwise_xor(level, mask) * rows, 16)
        ordered[core, pl.ds(start, rows), :] = mine_ref[mask]
        ordered[1 - core, pl.ds(start, rows), :] = other_ref[mask]
    for half in range(CORES):
        down_ref[half * pack.down_rows : (half + 1) * pack.down_rows, :] = ordered[
            half, : pack.down_rows, :
        ].astype(F32)
        for block in range(pack.blocks):
            lane = (half * pack.blocks + block) * pack.model_width
            start = pack.up_at + block * pack.row_shard
            up_ref[:, lane : lane + pack.model_width] = ordered[
                half, start : start + pack.row_shard, :
            ].astype(F32)
        out_ref[half * pack.out_rows : (half + 1) * pack.out_rows, :] = ordered[
            half, pack.out_at : pack.out_at + pack.out_rows, :
        ].astype(F32)


def unpack(pack, depth, meta, mine, other):
    vmem = pl.BlockSpec(memory_space=pltpu.VMEM)
    return pl.pallas_call(
        partial(unpack_kernel, pack, depth),
        in_specs=[IN_SMEM, vmem, vmem],
        out_specs=[vmem] * 3,
        out_shape=[
            jax.ShapeDtypeStruct((pack.feed_shard, pack.model_width), F32),
            jax.ShapeDtypeStruct((pack.row_shard, pack.feed_width), F32),
            jax.ShapeDtypeStruct((pack.row_shard, pack.model_width), F32),
        ],
        scratch_shapes=[pltpu.VMEM((CORES, pack.rows, pack.model_width), BF16)],
        name="unpack",
        compiler_params=pltpu.CompilerParams(vmem_limit_bytes=VMEM_BYTES),
        cost_estimate=pl.CostEstimate(flops=0, bytes_accessed=10_000_000, transcendentals=0),
    )(meta, mine, other)


def after(value, *others):
    return lax.optimization_barrier((value,) + others)[0]


def body(
    tokens,
    cotangent,
    perms,
    unit_kind,
    w_qkv,
    bias_qv,
    w_out,
    bias_out,
    ln_gain,
    ln_bias,
    w_up,
    bias_up,
    w_down,
    bias_down,
):
    shards = lax.axis_size("fsdp")
    groups = lax.axis_size("dp")
    here = lax.axis_index("fsdp")
    dp_index = lax.axis_index("dp")
    core = dp_index % CORES
    level = dp_index // CORES
    depth = groups // CORES
    units, rounds, unit_len = perms.shape
    per_device = unit_len // shards
    model_width = tokens.shape[1]
    feed_width = w_up.shape[1]
    row_shard = model_width // shards
    members = shards // units
    member_rows = unit_len // members
    head_cols = model_width // members
    padded = -(-head_cols // CLUSTER_ROWS) * CLUSTER_ROWS
    spot = here * CORES + core
    home_core = spot // shards
    unit = (spot // members) % units
    member = spot % members
    pack = Pack(model_width, feed_width, shards, units, depth)
    bits = [1 << k for k in range(shards.bit_length() - 1)]
    bit_orders = (bits, bits[::-1])

    def plane_pairs(target):
        pairs = []
        for z in range(depth):
            for f_index in range(shards):
                for c_index in range(CORES):
                    f_new, c_new = target(f_index, c_index)
                    pairs.append(
                        (
                            (z * CORES + c_index) * shards + f_index,
                            (z * CORES + c_new) * shards + f_new,
                        )
                    )
        return pairs

    def send(value, pairs):
        return lax.ppermute(value, ("dp", "fsdp"), pairs)

    def cross(value, mask):
        return send(value, plane_pairs(lambda f, c: divmod((f * CORES + c) ^ mask, CORES)))

    def trade(value, stage):
        return send(value, plane_pairs(lambda f, c: (f ^ bit_orders[c][stage], c)))

    def trade_mask(index, which):
        mask = 0
        for stage in range(len(bits)):
            if index >> stage & 1:
                mask ^= bit_orders[which][stage]
        return mask

    def climb(value, mask):
        plane = CORES * shards
        pairs = []
        for z in range(depth):
            for rest in range(plane):
                pairs.append((z * plane + rest, (z ^ mask) * plane + rest))
        return send(value, pairs)

    def outward(step):
        def target(f, c):
            place_now = (c * units + (f % units + step) % units) * members + f // units
            return divmod(place_now, CORES)

        return plane_pairs(target)

    def homeward(step):
        return [(b, a) for a, b in outward(step)]

    def bring_start(value):
        blocks = value.reshape(units, per_device, model_width)
        return [
            lax.dynamic_index_in_dim(blocks, (here % units + step) % units, axis=0, keepdims=False)
            for step in range(units)
        ]

    def bring(chosen):
        return jnp.concatenate(
            [send(chosen[step], outward(step)) for step in range(units)], axis=0
        )

    def take_home(value, dtype):
        blocks = value.reshape(units, per_device, model_width)
        landed = [send(blocks[step], homeward(step)) for step in range(units)]
        if units == 2:
            swap = here % units == 1
            wanted = [
                jnp.where(swap, landed[1], landed[0]),
                jnp.where(swap, landed[0], landed[1]),
            ]
        else:
            stacked = jnp.stack(landed)
            wanted = [
                lax.dynamic_index_in_dim(stacked, (index - here % units) % units, 0, keepdims=False)
                for index in range(units)
            ]
        return jnp.concatenate(wanted, axis=0).astype(dtype)

    x_chosen = bring_start(tokens)
    x_own = bring(x_chosen)
    small = jnp.concatenate(
        [
            bias_qv.reshape(-1),
            bias_out,
            ln_gain.reshape(-1),
            ln_bias.reshape(-1),
            bias_up,
            bias_down,
        ]
    )
    small_rows = -(-small.shape[0] // (3 * padded))
    small_block = jnp.pad(
        jnp.pad(small, (0, small_rows * 3 * padded - small.shape[0])).reshape(
            small_rows, 3 * padded
        ),
        ((0, 16 - small_rows), (0, 0)),
    )
    w_qkv_now = after(w_qkv, *x_chosen)

    def columns_for(offset):
        start = lax.bitwise_xor(member, offset) * head_cols
        blocks = [
            jnp.pad(
                lax.dynamic_slice(
                    w_qkv_now, (0, kind * model_width + start), (row_shard, head_cols)
                ),
                ((0, 0), (0, padded - head_cols)),
            )
            for kind in range(3)
        ]
        return jnp.concatenate([jnp.concatenate(blocks, axis=1), small_block], axis=0)

    offsets = [(CORES * m) % members for m in range(shards)]
    piece_kinds = {offset: columns_for(offset) for offset in sorted(set(offsets))}
    qkv_pieces = [piece_kinds[0]] + [
        cross(piece_kinds[offsets[m]], CORES * m) for m in range(1, shards)
    ]
    order_pack = jnp.concatenate(
        [perms.reshape(-1), jnp.broadcast_to(unit_kind[:, None], (units, 128)).reshape(-1)]
    )
    order_other = cross(order_pack, 1)
    order_pack = jnp.where(home_core == core, order_pack, order_other)
    order_count = units * rounds * unit_len
    unit_perm = lax.dynamic_index_in_dim(
        order_pack[:order_count].reshape(units, rounds * unit_len), unit, 0, keepdims=False
    )
    kind_now = lax.dynamic_index_in_dim(
        order_pack[order_count:].reshape(units, 128), unit, 0, keepdims=False
    )[0]
    owner = unit_perm // per_device
    order = (
        lax.bitwise_xor(owner // units, member) * units + (unit - owner % units) % units
    ) * per_device + unit_perm % per_device
    order_row = order.reshape(1, rounds * unit_len)
    order = order.reshape(-1, CLUSTER_ROWS)
    own_masks = [
        jnp.where(core == 0, trade_mask(i, 0), trade_mask(i, 1)) for i in range(1, shards)
    ]
    other_masks = [
        jnp.where(core == 0, trade_mask(i, 1), trade_mask(i, 0)) for i in range(1, shards)
    ]
    zero = jnp.int32(0)
    meta = jnp.stack(
        [kind_now, here, core, member, level, zero, zero, zero] + own_masks + other_masks
    ).astype(jnp.int32)

    def half_of(value, axis, length, at):
        return lax.dynamic_slice_in_dim(value, at * length, length, axis=axis)

    packed = jnp.concatenate(
        [half_of(w_down, 0, pack.down_rows, core)]
        + [
            half_of(w_up, 1, model_width, core * pack.blocks + block)
            for block in range(pack.blocks)
        ]
        + [half_of(w_out, 0, pack.out_rows, core)],
        axis=0,
    )
    x_pieces = [x_own] + [cross(x_own, mask) for mask in range(1, members)]
    packed = after(packed, x_pieces[-1])
    weight_pieces = {0: packed}
    for stage in range(len(bits)):
        for index in range(1 << stage):
            weight_pieces[index | 1 << stage] = trade(weight_pieces[index], stage)

    smalls = jnp.stack(
        [
            piece[row_shard : row_shard + small_rows].reshape(-1)[: small.shape[0]]
            for piece in qkv_pieces
        ]
    )
    smalls = jnp.take(smalls, lax.bitwise_xor(here, jnp.arange(shards)), axis=0).astype(F32)

    def vectors_at(start, count, length):
        part = smalls[:, start * row_shard : start * row_shard + count * length]
        return (
            part.reshape(shards, count, length).transpose(1, 0, 2).reshape(count, shards * length)
        )

    my_bias = lax.dynamic_index_in_dim(
        vectors_at(0, 2, row_shard).reshape(2, members, head_cols), member, 1, keepdims=False
    )
    my_bias = jnp.pad(my_bias, ((0, 0), (0, padded - head_cols)))
    my_bias = jnp.stack([my_bias[0], jnp.zeros_like(my_bias[0]), my_bias[1]]).reshape(1, -1)
    up_bias = vectors_at(7, 1, feed_width // shards)
    down_bias = smalls[:, small.shape[0] - row_shard :].reshape(1, model_width)
    vectors = jnp.concatenate(
        [vectors_at(2, 5, row_shard), down_bias, jnp.zeros((2, model_width), F32)], axis=0
    )

    order_rows = unit_len // CLUSTER_ROWS
    x_now, arranged, probs, mixtures = [], [], [], []
    for index in range(rounds):
        bias_now = my_bias if index == 0 else after(my_bias, mixtures[-1])
        results = attend(
            meta, order, bias_now, x_pieces, qkv_pieces, row_shard, unit_len, index * order_rows
        )
        for kept, result in zip((x_now, arranged, probs, mixtures), results):
            kept.append(result)
    cot_own = bring(bring_start(after(cotangent, mixtures[0])))
    att_there = []
    for mask in range(1, members):
        there = place(order_row, mixtures, mask * member_rows, member_rows, 0.5)
        att_there.append(cross(there[:, :head_cols], mask))
    att_here = place(order_row, mixtures, 0, member_rows, 0.5)
    att_raw = [att_here[:, :head_cols]] + att_there
    if head_cols % CLUSTER_ROWS:
        att_raw = [jnp.concatenate(att_raw, axis=1)]

    direct = [weight_pieces[index] for index in range(1, shards)]
    swapped = [cross(piece, 1) for piece in direct]
    block_out, first_low, d_branch, d_ffn, hidden, d_pre, d_lower, *rest = feed(
        pack,
        meta,
        x_own,
        cot_own,
        vectors,
        up_bias,
        att_raw,
        [w_out, w_up, w_down],
        direct + swapped,
    )
    d_att, (row_sums, up_sums) = rest[: len(att_raw)], rest[len(att_raw) :]
    if head_cols % CLUSTER_ROWS:
        d_att = [d_att[0][:, mask * head_cols : (mask + 1) * head_cols] for mask in range(members)]
    d_att = [d_att[0]] + [cross(d_att[mask], mask) for mask in range(1, members)]
    d_att = [jnp.pad(piece, ((0, 0), (0, padded - head_cols))) for piece in d_att]

    def grads_of(half, *needed):
        table = after(jnp.stack([half, member]).astype(jnp.int32), *needed)
        return weight_grads(pack, table, hidden, d_pre, d_ffn, first_low, d_branch, att_raw)

    theirs = grads_of(1 - core)
    output = take_home(after(block_out, theirs), BF16)
    mine = grads_of(core, theirs)
    theirs = cross(theirs, 1)
    sending = [index for index in range(shards) if index & 1]
    keeping = [index for index in range(shards) if not index & 1]
    slots = jnp.stack(
        [
            lax.bitwise_xor(here, jnp.where(core == 0, trade_mask(i, 0), trade_mask(i, 1)))
            for i in sending + keeping
        ]
    )
    going, kept = add_picked(
        jnp.concatenate([slots, slots]).astype(jnp.int32), [mine, theirs], shards, len(sending)
    )

    grads, d_x, bias_sums = [], [], []
    first_needed = going
    for index in range(rounds):
        results = attend_back(
            after(meta, first_needed),
            order,
            arranged[index],
            probs[index],
            d_att,
            qkv_pieces,
            row_shard,
            index * order_rows,
        )
        for held, result in zip((grads, d_x, bias_sums), results):
            held.append(result)
        if index < len(bits):
            landed = trade(going, index)
            count = kept.shape[0]
            going_next = [i for i in range(count) if i & 1]
            keeping_next = [i for i in range(count) if not i & 1]
            if count > 1:
                picks = jnp.array((going_next + keeping_next) * 2, jnp.int32)
                going, kept = add_picked(
                    after(picks, results[0]), [kept, landed], count, len(going_next)
                )
            else:
                (kept,) = add_picked(
                    after(jnp.zeros((2,), jnp.int32), results[0]), [kept, landed], 1
                )
            first_needed = going if count > 1 else kept
    for stage in range(rounds, len(bits)):
        landed = trade(going, stage)
        count = kept.shape[0]
        if count > 1:
            order_now = [i for i in range(count) if i & 1] + [
                i for i in range(count) if not i & 1
            ]
            going, kept = add_picked(
                jnp.array(order_now * 2, jnp.int32), [kept, landed], count, count // 2
            )
        else:
            (kept,) = add_picked(jnp.zeros((2,), jnp.int32), [kept, landed], 1)

    def level_pieces(block):
        return block.reshape((depth, block.shape[0] // depth) + block.shape[1:])

    def level_scatter(cut):
        return [
            climb(
                lax.dynamic_index_in_dim(cut, lax.bitwise_xor(level, mask), 0, keepdims=False), mask
            )
            for mask in range(1, depth)
        ]

    def level_gather(piece):
        return jnp.stack([piece] + [climb(piece, mask) for mask in range(1, depth)])

    cut = level_pieces(kept[0])
    landed = level_scatter(cut)

    def grad_of(left, right):
        return lax.dot_general(left, right, TN, preferred_element_type=F32)

    qkv_grad = sum(grad_of(x_now[i], grads[i]) for i in range(rounds)).astype(BF16)
    bias_sum = sum(bias_sums)
    qkv_grad = qkv_grad.reshape(shards, row_shard, 3, padded)[..., :head_cols]
    qkv_grad = qkv_grad.reshape(shards, row_shard, 3 * head_cols)
    bias_sum = bias_sum.reshape(3, padded)[:, :head_cols]
    mine_now = (jnp.arange(members) == member)[None, :, None]
    bias_parts = jnp.where(mine_now, bias_sum[::2][:, None, :], 0.0).reshape(2, model_width)

    def by_shard(value):
        count, length = value.shape
        return (
            value.reshape(count, shards, length // shards)
            .transpose(1, 0, 2)
            .reshape(shards, count * length // shards)
        )

    small_grad = jnp.concatenate(
        [
            by_shard(bias_parts),
            by_shard(row_sums[:5]),
            by_shard(up_sums),
            by_shard(row_sums[5:6]),
        ],
        axis=1,
    ).astype(BF16)
    small_length = small_grad.shape[1]
    extra = -(-small_length // (3 * head_cols))
    extra_rows = -(-extra // 16) * 16
    small_grad = jnp.pad(
        small_grad, ((0, 0), (0, extra_rows * 3 * head_cols - small_length))
    ).reshape(shards, extra_rows, 3 * head_cols)
    joined = jnp.concatenate([qkv_grad, small_grad], axis=1)
    classes = max(1, members // CORES)
    totals = [None] * classes
    for m in range(shards):
        offset = offsets[m] // CORES
        piece = lax.dynamic_index_in_dim(joined, lax.bitwise_xor(here, m), 0, keepdims=False)
        piece = (piece if m == 0 else cross(piece, CORES * m)).astype(F32)
        totals[offset] = piece if totals[offset] is None else totals[offset] + piece

    d_there = []
    for mask in range(1, members):
        there = place(order_row, d_x, mask * member_rows, member_rows)
        d_there.append(cross(there, mask))
    if depth > 1:
        picks = jnp.concatenate([level[None], jnp.zeros((depth - 1,), level.dtype)])
        (kept,) = add_picked(
            picks.astype(jnp.int32), [cut] + [piece[None] for piece in landed], 1
        )
    stacked = level_gather(kept[0]) if depth > 1 else cut
    d_inputs = place(order_row, d_x, 0, member_rows, 1.0, F32, d_lower)
    for piece in d_there:
        d_inputs = d_inputs + piece.astype(F32)
    d_inputs = take_home(d_inputs.astype(BF16), F32)
    grad_down, grad_up, grad_out = unpack(pack, depth, meta, stacked, cross(stacked, 1))

    totals = jnp.concatenate(totals, axis=0).astype(BF16)
    rows_each = row_shard + extra_rows
    if depth > 1:
        cut = level_pieces(totals)
        total = lax.dynamic_index_in_dim(cut, level, 0, keepdims=False).astype(F32)
        for piece in level_scatter(cut):
            total = total + piece.astype(F32)
        gathered = level_gather(total.astype(BF16))
        gathered = jnp.take(gathered, lax.bitwise_xor(level, jnp.arange(depth)), axis=0)
        totals = gathered.reshape(totals.shape)
    landed = jnp.stack([totals, cross(totals, 1)], axis=0).reshape(
        CORES, classes, rows_each, 3 * head_cols
    )
    smalls_out = jnp.sum(landed[:, :, row_shard:].astype(F32), axis=(0, 1)).reshape(-1)
    smalls_out = smalls_out[:small_length]
    landed = (
        landed[:, :, :row_shard].transpose(1, 0, 2, 3).reshape(members, row_shard, 3, head_cols)
    )
    if members == 2:
        swap = member == 1
        landed = jnp.stack(
            [
                jnp.where(swap, landed[1], landed[0]),
                jnp.where(swap, landed[0], landed[1]),
            ]
        )
    else:
        landed = jnp.take(landed, lax.bitwise_xor(member, jnp.arange(members)), axis=0)
    grad_qkv = landed.transpose(1, 2, 0, 3).reshape(row_shard, 3 * model_width).astype(F32)

    feed_shard = feed_width // shards
    spots = [2 * row_shard, 3 * row_shard, 5 * row_shard, 7 * row_shard]
    return (
        output,
        d_inputs,
        grad_qkv,
        smalls_out[: spots[0]].reshape(2, row_shard),
        grad_out,
        smalls_out[spots[0] : spots[1]],
        smalls_out[spots[1] : spots[2]].reshape(2, row_shard),
        smalls_out[spots[2] : spots[3]].reshape(2, row_shard),
        grad_up,
        smalls_out[spots[3] : spots[3] + feed_shard],
        grad_down,
        smalls_out[spots[3] + feed_shard :],
    )


def solution(mesh):
    placed = (
        P(("dp", "fsdp"), None),
        P(("dp", "fsdp"), None),
        P("dp", None, None),
        P("dp"),
        P("fsdp", None),
        P(None, "fsdp"),
        P("fsdp", None),
        P("fsdp"),
        P(None, "fsdp"),
        P(None, "fsdp"),
        P("fsdp", None),
        P("fsdp"),
        P("fsdp", None),
        P("fsdp"),
    )
    return jax.shard_map(
        body,
        mesh=mesh,
        in_specs=placed,
        out_specs=(
            P(("dp", "fsdp"), None),
            P(("dp", "fsdp"), None),
            P("fsdp", None),
            P(None, "fsdp"),
            P("fsdp", None),
            P("fsdp"),
            P(None, "fsdp"),
            P(None, "fsdp"),
            P("fsdp", None),
            P("fsdp"),
            P("fsdp", None),
            P("fsdp"),
        ),
        check_vma=False,
    )
```

```python
from functools import partial

import jax
import jax.numpy as jnp
from jax import lax
from jax.experimental import pallas as pl
from jax.experimental.pallas import tpu as pltpu
from jax.sharding import PartitionSpec as P

HEAD_DIM = 64
CORES = 2
NEG_FILL = -1000000000.0
EPSILON = 1e-05
CLUSTER_ROWS = 128
HALF_ROWS = 64
POS_BLOCK = 512
TOKEN_BLOCK = 512
ROW_BLOCK = 256
FF_BLOCK = 512
VMEM_BYTES = 60 * 1024 * 1024
COST_SHARE = 16
NT = (((1,), (1,)), ((), ()))
TN = (((0,), (0,)), ((), ()))
F32 = jnp.float32
BF16 = jnp.bfloat16
ANYWHERE = pl.BlockSpec(memory_space=pl.ANY)
IN_SMEM = pl.BlockSpec(memory_space=pltpu.SMEM)


def whole(shape):
    return pl.BlockSpec(shape, lambda i: (0,) * len(shape))


def rows_of(shape):
    return pl.BlockSpec(shape, lambda i: (i,) + (0,) * (len(shape) - 1))


def dot(a, b, dims=(((1,), (0,)), ((), ()))):
    return lax.dot_general(a, b, dims, preferred_element_type=F32)


def params(flops=0, moved=0, turned=False):
    return dict(
        compiler_params=pltpu.CompilerParams(
            dimension_semantics=("arbitrary",),
            vmem_limit_bytes=VMEM_BYTES,
            fuse_transposed_lhs_in_matmul=turned,
        ),
        cost_estimate=pl.CostEstimate(
            flops=flops // COST_SHARE, bytes_accessed=moved // COST_SHARE, transcendentals=0
        ),
    )


def gated(kernel, used, needs):
    if not needs:
        return kernel

    def run(*refs):
        return kernel(*refs[:used], *refs[used + len(needs) :])

    return run


def lane_masks():
    lane = lax.broadcasted_iota(jnp.int32, (CLUSTER_ROWS, CLUSTER_ROWS), 1)
    low = (lane < HEAD_DIM).astype(F32)
    return low.astype(BF16), (1.0 - low).astype(BF16), lane < HEAD_DIM


def both_heads(rows_now, low, high):
    return jnp.concatenate([rows_now * low, rows_now * high], axis=0)


def equal_ones(left, right):
    return jnp.where(left == right, jnp.ones((), BF16), jnp.zeros((), BF16))


def pick_rows(order_ref, first_row, unit_len):
    parts = []
    lane = lax.broadcasted_iota(jnp.int16, (CLUSTER_ROWS, CLUSTER_ROWS), 1)
    for part in range(POS_BLOCK // CLUSTER_ROWS):
        row = order_ref[pl.ds(first_row + part, 1), :]
        column = jnp.transpose(jnp.broadcast_to(row, (CLUSTER_ROWS, CLUSTER_ROWS)))
        column = column.astype(jnp.int16)
        pieces = [
            equal_ones(column, lane + jnp.int16(base)) for base in range(0, unit_len, CLUSTER_ROWS)
        ]
        parts.append(jnp.concatenate(pieces, axis=1))
    return jnp.concatenate(parts, axis=0)


def load_pieces(meta, x_refs, w_refs, x_all, w_all, sems, row_shard):
    member_rows = x_all.shape[0] // max(1, len(x_refs))
    copies = []
    for index, ref in enumerate(x_refs):
        copies.append(
            pltpu.make_async_copy(
                ref, x_all.at[pl.ds(index * member_rows, member_rows), :], sems.at[index]
            )
        )
    for index, ref in enumerate(w_refs):
        start = pl.multiple_of(lax.bitwise_xor(meta[1], index) * row_shard, 16)
        copies.append(
            pltpu.make_async_copy(
                ref.at[pl.ds(0, row_shard), :],
                w_all.at[pl.ds(start, row_shard), :],
                sems.at[len(x_refs) + index],
            )
        )
    for copy in copies:
        copy.start()
    for copy in copies:
        copy.wait()


def arrange_kernel(unit_len, first_row, order_ref, *refs):
    x_refs, out_ref = refs[:-1], refs[-1]
    step = pl.program_id(0)
    picks = pick_rows(order_ref, first_row + step * (POS_BLOCK // CLUSTER_ROWS), unit_len)
    rows = x_refs[0].shape[0]
    total = None
    for index, ref in enumerate(x_refs):
        term = dot(picks[:, index * rows : (index + 1) * rows], ref[...])
        total = term if total is None else total + term
    out_ref[...] = total.astype(BF16)


def arrange(order, x_pieces, position_count, first_row):
    member_rows, width = x_pieces[0].shape
    unit_len = member_rows * len(x_pieces)
    return pl.pallas_call(
        partial(arrange_kernel, unit_len, first_row),
        grid=(position_count // POS_BLOCK,),
        in_specs=[whole(order.shape)] + [whole(piece.shape) for piece in x_pieces],
        out_specs=rows_of((POS_BLOCK, width)),
        out_shape=jax.ShapeDtypeStruct((position_count, width), BF16),
        name="arrange",
        **params(2 * position_count * unit_len * width, 6_000_000),
    )(order, *x_pieces)


def attend_kernel(sizes, meta, x_now_ref, bias_ref, *refs):
    shards, row_shard = sizes
    w_refs, refs = refs[:shards], refs[shards:]
    arranged_ref, probs_ref, mixture_ref, w_all, sems = refs
    width = w_all.shape[1] // 3
    step = pl.program_id(0)

    @pl.when(step == 0)
    def _():
        load_pieces(meta, [], w_refs, w_all, w_all, sems, row_shard)

    x_now = x_now_ref[...]
    arranged = (dot(x_now, w_all[...]) + bias_ref[...]).astype(BF16)
    arranged_ref[...] = arranged
    low, high, lane_low = lane_masks()
    position = lax.broadcasted_iota(jnp.int32, (CLUSTER_ROWS, CLUSTER_ROWS), 0)
    other = lax.broadcasted_iota(jnp.int32, (CLUSTER_ROWS, CLUSTER_ROWS), 1)
    same_half = (position < HALF_ROWS) == (other < HALF_ROWS)
    allowed = jnp.logical_or(same_half, meta[0] == 1)
    scale = HEAD_DIM ** (-0.5)
    for part in range(POS_BLOCK // CLUSTER_ROWS):
        rows_now = slice(part * CLUSTER_ROWS, (part + 1) * CLUSTER_ROWS)
        for pair in range(width // CLUSTER_ROWS):
            base = pair * CLUSTER_ROWS
            queries = arranged[rows_now, base : base + CLUSTER_ROWS]
            keys = arranged[rows_now, width + base : width + base + CLUSTER_ROWS]
            values = arranged[rows_now, 2 * width + base : 2 * width + base + CLUSTER_ROWS]
            scores = dot(queries, both_heads(keys, low, high), NT) * scale
            halves = []
            for head in range(2):
                one = scores[:, head * CLUSTER_ROWS : (head + 1) * CLUSTER_ROWS]
                one = jnp.where(allowed, one, NEG_FILL)
                top = jnp.max(one, axis=-1, keepdims=True)
                grown = jnp.exp(one - top)
                halves.append(grown * (1.0 / jnp.sum(grown, axis=-1, keepdims=True)))
            probs = jnp.concatenate(halves, axis=1).astype(BF16)
            probs_ref[rows_now, 2 * base : 2 * base + 2 * CLUSTER_ROWS] = probs
            mixture = dot(probs, both_heads(values, low, high)).astype(BF16)
            mixture_ref[rows_now, base : base + CLUSTER_ROWS] = mixture


def attend(meta, x_now, bias, w_pieces, row_shard, needs=()):
    shards = len(w_pieces)
    position_count, model_width = x_now.shape
    cols = w_pieces[0].shape[1]
    width = cols // 3
    outs = (cols, 2 * width, width)
    return pl.pallas_call(
        gated(partial(attend_kernel, (shards, row_shard)), 3 + shards, needs),
        grid=(position_count // POS_BLOCK,),
        in_specs=[IN_SMEM, rows_of((POS_BLOCK, model_width)), whole(bias.shape)]
        + [ANYWHERE] * (shards + len(needs)),
        out_specs=[rows_of((POS_BLOCK, length)) for length in outs],
        out_shape=[jax.ShapeDtypeStruct((position_count, length), BF16) for length in outs],
        scratch_shapes=[
            pltpu.VMEM((model_width, cols), BF16),
            pltpu.SemaphoreType.DMA((shards,)),
        ],
        name="attend",
        **params(
            2 * position_count * (model_width * cols + 4 * CLUSTER_ROWS * width), 18_000_000
        ),
    )(meta, x_now, bias, *w_pieces, *needs)


def place_kernel(sizes, scale, has_base, order_row_ref, *refs):
    unit_len, first_token, added = sizes
    base_ref = refs[0] if has_base else None
    refs = refs[1 if has_base else 0 :]
    if added:
        first_ref, second_ref, out_ref, held = refs

        @pl.when(pl.program_id(0) == 0)
        def _():
            held[...] = (first_ref[...].astype(F32) + second_ref[...].astype(F32)).astype(BF16)

        source_refs = [held]
    else:
        source_refs, out_ref = refs[:-1], refs[-1]
    block_rows = out_ref.shape[0]
    first = jnp.full((1, 1), first_token + pl.program_id(0) * block_rows, jnp.int32)
    token = lax.broadcasted_iota(jnp.int16, (block_rows, unit_len), 0)
    total = None
    for index, ref in enumerate(source_refs):
        row = order_row_ref[:, index * unit_len : (index + 1) * unit_len] - first
        row = jnp.broadcast_to(row, (16, unit_len)).astype(jnp.int16)
        row = jnp.concatenate([row] * (block_rows // 16), axis=0)
        term = dot(equal_ones(row, token), ref[...])
        total = term if total is None else total + term
    if scale != 1.0:
        total = total * scale
    if has_base:
        total = total + base_ref[...]
    out_ref[...] = total.astype(out_ref.dtype)


def place(
    order_row,
    sources,
    first_token,
    row_count,
    scale=1.0,
    dtype=BF16,
    base=None,
    added=False,
    needs=(),
):
    unit_len, width = sources[0].shape
    block_rows = min(TOKEN_BLOCK, row_count)
    extra = [] if base is None else [base]
    return pl.pallas_call(
        gated(
            partial(place_kernel, (unit_len, first_token, added), scale, base is not None),
            1 + len(extra) + len(sources),
            needs,
        ),
        grid=(row_count // block_rows,),
        in_specs=[whole(order_row.shape)]
        + [rows_of((block_rows, width))] * len(extra)
        + [whole(source.shape) for source in sources]
        + [ANYWHERE] * len(needs),
        out_specs=rows_of((block_rows, width)),
        out_shape=jax.ShapeDtypeStruct((row_count, width), dtype),
        scratch_shapes=[pltpu.VMEM((unit_len, width), BF16)] if added else [],
        name="place",
        **params(
            2 * row_count * unit_len * (1 if added else len(sources)) * width, 10_000_000
        ),
    )(order_row, *extra, *sources, *needs)


def attend_back_kernel(sizes, meta, order_ref, arranged_ref, probs_ref, *refs):
    members, shards, unit_len, row_shard, first_row = sizes
    g_refs, refs = refs[:members], refs[members:]
    w_refs, refs = refs[:shards], refs[shards:]
    grads_ref, d_x_ref, sums_ref, g_all, w_all, sems = refs
    width = w_all.shape[1] // 3
    step = pl.program_id(0)

    @pl.when(step == 0)
    def _():
        load_pieces(meta, g_refs, w_refs, g_all, w_all, sems, row_shard)
        sums_ref[...] = jnp.zeros_like(sums_ref)

    picks = pick_rows(order_ref, first_row + step * (POS_BLOCK // CLUSTER_ROWS), unit_len)
    d_mixture = dot(picks, g_all[...]).astype(BF16)
    low, high, lane_low = lane_masks()
    scale = HEAD_DIM ** (-0.5)
    for part in range(POS_BLOCK // CLUSTER_ROWS):
        rows_now = slice(part * CLUSTER_ROWS, (part + 1) * CLUSTER_ROWS)
        for pair in range(width // CLUSTER_ROWS):
            base = pair * CLUSTER_ROWS
            q_lanes = slice(base, base + CLUSTER_ROWS)
            k_lanes = slice(width + base, width + base + CLUSTER_ROWS)
            v_lanes = slice(2 * width + base, 2 * width + base + CLUSTER_ROWS)
            queries = arranged_ref[rows_now, q_lanes]
            keys = arranged_ref[rows_now, k_lanes]
            values = arranged_ref[rows_now, v_lanes]
            probs = probs_ref[rows_now, 2 * base : 2 * base + 2 * CLUSTER_ROWS]
            d_now = d_mixture[rows_now, base : base + CLUSTER_ROWS]
            d_probs = dot(d_now, both_heads(values, low, high), NT)
            pieces = []
            for head in range(2):
                lanes = slice(head * CLUSTER_ROWS, (head + 1) * CLUSTER_ROWS)
                weight = probs[:, lanes].astype(F32)
                d_one = d_probs[:, lanes]
                inner = jnp.sum(weight * d_one, axis=-1, keepdims=True)
                pieces.append(weight * (d_one - inner) * scale)
            d_scores = jnp.concatenate(pieces, axis=1).astype(BF16)
            d_query = dot(d_scores, both_heads(keys, low, high))
            d_keys = dot(d_scores, queries, TN)
            d_values = dot(probs, d_now, TN)
            grads_ref[rows_now, q_lanes] = d_query.astype(BF16)
            grads_ref[rows_now, k_lanes] = jnp.where(
                lane_low, d_keys[:CLUSTER_ROWS], d_keys[CLUSTER_ROWS:]
            ).astype(BF16)
            grads_ref[rows_now, v_lanes] = jnp.where(
                lane_low, d_values[:CLUSTER_ROWS], d_values[CLUSTER_ROWS:]
            ).astype(BF16)
    grads = grads_ref[...]
    sums_ref[...] += jnp.sum(grads.astype(F32), axis=0, keepdims=True)
    d_x_ref[...] = dot(grads, w_all[...], NT).astype(BF16)


def attend_back(
    meta, order, arranged, probs, g_pieces, w_pieces, row_shard, first_row, needs=()
):
    members, shards = len(g_pieces), len(w_pieces)
    member_rows, width = g_pieces[0].shape
    unit_len = members * member_rows
    position_count, cols = arranged.shape
    model_width = row_shard * shards
    return pl.pallas_call(
        gated(
            partial(attend_back_kernel, (members, shards, unit_len, row_shard, first_row)),
            4 + members + shards,
            needs,
        ),
        grid=(position_count // POS_BLOCK,),
        in_specs=[
            IN_SMEM,
            whole(order.shape),
            rows_of((POS_BLOCK, cols)),
            rows_of((POS_BLOCK, 2 * width)),
        ]
        + [ANYWHERE] * (members + shards + len(needs)),
        out_specs=[
            rows_of((POS_BLOCK, cols)),
            rows_of((POS_BLOCK, model_width)),
            whole((1, cols)),
        ],
        out_shape=[
            jax.ShapeDtypeStruct((position_count, cols), BF16),
            jax.ShapeDtypeStruct((position_count, model_width), BF16),
            jax.ShapeDtypeStruct((1, cols), F32),
        ],
        scratch_shapes=[
            pltpu.VMEM((unit_len, width), BF16),
            pltpu.VMEM((model_width, cols), BF16),
            pltpu.SemaphoreType.DMA((members + shards,)),
        ],
        name="attend_back",
        **params(
            2 * position_count * (unit_len * width + model_width * cols), 20_000_000, True
        ),
    )(meta, order, arranged, probs, *g_pieces, *w_pieces, *needs)


def normalise(summed):
    average = jnp.mean(summed, axis=-1, keepdims=True)
    centred = summed - average
    spread = jnp.mean(centred * centred, axis=-1, keepdims=True)
    scale_inv = lax.rsqrt(spread + EPSILON)
    return centred * scale_inv, scale_inv


def normalise_back(grad_out, normed, scale_inv, gain_row):
    scaled = grad_out * gain_row
    return scale_inv * (
        scaled
        - jnp.mean(scaled, axis=-1, keepdims=True)
        - normed * jnp.mean(scaled * normed, axis=-1, keepdims=True)
    )


def column_sum(rows_now):
    return jnp.sum(rows_now, axis=0, keepdims=True)


def gelu_parts(value):
    below = 0.5 + 0.5 * lax.erf(value * 0.7071067811865476)
    bell = jnp.exp(value * value * -0.5) * 0.3989422804014327
    return value * below, below + value * bell


class Pack:
    def __init__(self, model_width, feed_width, shards, units, depth):
        self.model_width, self.feed_width, self.shards = model_width, feed_width, shards
        self.row_shard = model_width // shards
        self.feed_shard = feed_width // shards
        self.down_rows = self.feed_shard // CORES
        self.blocks = feed_width // CORES // model_width
        self.up_at = self.down_rows
        self.out_at = self.up_at + self.blocks * self.row_shard
        self.out_rows = self.row_shard // CORES
        self.used = self.out_at + self.out_rows
        unit = 16 * depth
        self.rows = -(-self.used // unit) * unit
        self.units = units
        self.group = units * self.row_shard

    def out_start(self, shard, member):
        return (
            lax.bitwise_xor(jnp.int32(shard) // self.units, member) * self.group
            + (shard % self.units) * self.row_shard
        )


def feed_kernel(pack, att_count, meta, x_ref, cot_ref, vec_ref, up_bias_ref, *refs):
    shards = pack.shards
    att_refs, refs = refs[:att_count], refs[att_count:]
    own_out, own_up, own_down = refs[:3]
    refs = refs[3:]
    pieces, refs = refs[: 2 * (shards - 1)], refs[2 * (shards - 1) :]
    out_ref, first_low_ref, d_branch_ref, d_ffn_ref, hidden_ref, d_pre_ref, d_h1_ref = refs[:7]
    refs = refs[7:]
    d_att_refs, refs = refs[:att_count], refs[att_count:]
    sums_ref, up_sums_ref, w_out, w_up, w_down, slope, sems = refs
    step = pl.program_id(0)
    here, core, member = meta[1], meta[2], meta[3]
    feed_width = pack.feed_width

    def loads(kind):
        copies = []

        def add(source, target):
            copies.append(pltpu.make_async_copy(source, target, sems.at[kind, len(copies)]))

        if kind == 0:
            start = pl.multiple_of(pack.out_start(here, member), 16)
            add(own_out, w_out.at[pl.ds(start, pack.row_shard), :])
        elif kind == 1:
            start = pl.multiple_of(here * pack.row_shard, 16)
            add(own_up, w_up.at[pl.ds(start, pack.row_shard), :])
        else:
            start = pl.multiple_of(here * pack.feed_shard, 16)
            add(own_down, w_down.at[pl.ds(start, pack.feed_shard), :])
        for index, ref in enumerate(pieces):
            peer = lax.bitwise_xor(here, meta[8 + index])
            half = core if index < shards - 1 else 1 - core
            if kind == 0:
                start = pack.out_start(peer, member) + half * pack.out_rows
                start = pl.multiple_of(start, 16)
                add(
                    ref.at[pl.ds(pack.out_at, pack.out_rows), :],
                    w_out.at[pl.ds(start, pack.out_rows), :],
                )
            elif kind == 1:
                start = pl.multiple_of(peer * pack.row_shard, 16)
                for block in range(pack.blocks):
                    lane = pl.multiple_of(
                        (half * pack.blocks + block) * pack.model_width, CLUSTER_ROWS
                    )
                    add(
                        ref.at[pl.ds(pack.up_at + block * pack.row_shard, pack.row_shard), :],
                        w_up.at[pl.ds(start, pack.row_shard), pl.ds(lane, pack.model_width)],
                    )
            else:
                start = pl.multiple_of(peer * pack.feed_shard + half * pack.down_rows, 16)
                add(
                    ref.at[pl.ds(0, pack.down_rows), :],
                    w_down.at[pl.ds(start, pack.down_rows), :],
                )
        return copies

    @pl.when(step == 0)
    def _():
        for kind in range(3):
            for copy in loads(kind):
                copy.start()
        sums_ref[...] = jnp.zeros_like(sums_ref)
        up_sums_ref[...] = jnp.zeros_like(up_sums_ref)
        for copy in loads(0):
            copy.wait()

    bias_out, gain_one, gain_two = vec_ref[0:1, :], vec_ref[1:2, :], vec_ref[2:3, :]
    shift_one, shift_two, bias_down = vec_ref[3:4, :], vec_ref[4:5, :], vec_ref[5:6, :]
    att_width = att_refs[0].shape[1]
    summed = x_ref[...].astype(F32) + bias_out
    for index, ref in enumerate(att_refs):
        summed += dot(ref[...], w_out[index * att_width : (index + 1) * att_width, :])
    normed_one, inv_one = normalise(summed)
    first = normed_one * gain_one + shift_one
    first_low = first.astype(BF16)
    first_low_ref[...] = first_low

    @pl.when(step == 0)
    def _():
        for kind in (1, 2):
            for copy in loads(kind):
                copy.wait()

    second = first + bias_down
    starts = list(range(0, feed_width, FF_BLOCK))

    def raised(base):
        lanes = slice(base, base + FF_BLOCK)
        return dot(first_low, w_up[:, lanes]) + up_bias_ref[:, lanes]

    pre = raised(starts[0])
    for index, base in enumerate(starts):
        lanes = slice(base, base + FF_BLOCK)
        pre_next = raised(starts[index + 1]) if index + 1 < len(starts) else None
        hidden, slope_now = gelu_parts(pre)
        hidden = hidden.astype(BF16)
        hidden_ref[:, lanes] = hidden
        slope[:, lanes] = slope_now
        second += dot(hidden, w_down[lanes, :])
        pre = pre_next
    normed_two, inv_two = normalise(second)
    out_ref[...] = (normed_two * gain_two + shift_two).astype(BF16)
    top = cot_ref[...].astype(F32)
    d_second = normalise_back(top, normed_two, inv_two, gain_two)
    d_ffn = d_second.astype(BF16)
    d_ffn_ref[...] = d_ffn
    d_first = d_second
    d_hidden = dot(d_ffn, w_down[0:FF_BLOCK, :], NT)
    for index, base in enumerate(starts):
        lanes = slice(base, base + FF_BLOCK)
        if index + 1 < len(starts):
            d_next = dot(d_ffn, w_down[starts[index + 1] : starts[index + 1] + FF_BLOCK, :], NT)
        d_pre = (d_hidden * slope[:, lanes]).astype(BF16)
        d_pre_ref[:, lanes] = d_pre
        up_sums_ref[:, lanes] += column_sum(d_pre.astype(F32))
        d_first += dot(d_pre, w_up[:, lanes], NT)
        d_hidden = d_next
    d_lower = normalise_back(d_first, normed_one, inv_one, gain_one)
    d_h1_ref[...] = d_lower
    d_branch = d_lower.astype(BF16)
    d_branch_ref[...] = d_branch
    for index, ref in enumerate(d_att_refs):
        back = dot(d_branch, w_out[index * att_width : (index + 1) * att_width, :], NT)
        ref[...] = (0.5 * back).astype(BF16)
    sums_ref[0:1, :] += column_sum(d_branch.astype(F32))
    sums_ref[1:2, :] += column_sum(d_first * normed_one)
    sums_ref[2:3, :] += column_sum(top * normed_two)
    sums_ref[3:4, :] += column_sum(d_first)
    sums_ref[4:5, :] += column_sum(top)
    sums_ref[5:6, :] += column_sum(d_ffn.astype(F32))


def feed(pack, meta, x_own, cot_own, vectors, up_bias, att, own, pieces):
    row_count, model_width = x_own.shape
    feed_width = pack.feed_width
    att_width = att[0].shape[1]
    one = rows_of((ROW_BLOCK, model_width))
    wide = rows_of((ROW_BLOCK, feed_width))
    narrow = rows_of((ROW_BLOCK, att_width))

    def like(width, dtype=BF16):
        return jax.ShapeDtypeStruct((row_count, width), dtype)

    return pl.pallas_call(
        partial(feed_kernel, pack, len(att)),
        grid=(row_count // ROW_BLOCK,),
        in_specs=[IN_SMEM, one, one, whole(vectors.shape), whole(up_bias.shape)]
        + [narrow] * len(att)
        + [ANYWHERE] * (3 + len(pieces)),
        out_specs=[one, one, one, one, wide, wide, one]
        + [narrow] * len(att)
        + [whole((8, model_width)), whole((1, feed_width))],
        out_shape=[
            like(model_width),
            like(model_width),
            like(model_width),
            like(model_width),
            like(feed_width),
            like(feed_width),
            like(model_width, F32),
        ]
        + [like(att_width)] * len(att)
        + [
            jax.ShapeDtypeStruct((8, model_width), F32),
            jax.ShapeDtypeStruct((1, feed_width), F32),
        ],
        scratch_shapes=[
            pltpu.VMEM((model_width, model_width), BF16),
            pltpu.VMEM((model_width, feed_width), BF16),
            pltpu.VMEM((feed_width, model_width), BF16),
            pltpu.VMEM((ROW_BLOCK, feed_width), F32),
            pltpu.SemaphoreType.DMA((3, 1 + pack.blocks * len(pieces))),
        ],
        name="feed",
        **params(
            2 * row_count * model_width * (2 * model_width + 4 * feed_width), 40_000_000
        ),
    )(meta, x_own, cot_own, vectors, up_bias, *att, *own, *pieces)


def weight_grads_kernel(pack, split, att_count, table, hidden_ref, d_pre_ref, d_ffn_ref, *refs):
    first_low_ref, d_branch_ref = refs[:2]
    att_refs, (out_ref, tile) = refs[2 : 2 + att_count], refs[2 + att_count :]
    step = pl.program_id(0)
    half, member = table[0], table[1]

    @pl.when(step == 0)
    def _():
        spare = pack.rows - pack.used
        if spare:
            for shard in range(pack.shards):
                out_ref[shard, pack.used :, :] = jnp.zeros((spare, pack.model_width), BF16)

    @pl.when(step < pack.shards)
    def _():
        grad = dot(hidden_ref[...], d_ffn_ref[...], TN)
        if split:
            out_ref[step, : pack.down_rows, :] = grad.astype(BF16)
        else:
            tile[: pack.feed_shard, :] = grad
            start = pl.multiple_of(half * pack.down_rows, 16)
            out_ref[step, : pack.down_rows, :] = tile[pl.ds(start, pack.down_rows), :].astype(BF16)

    @pl.when(jnp.logical_and(step >= pack.shards, step < pack.shards + pack.blocks))
    def _():
        grad = dot(first_low_ref[...], d_pre_ref[...], TN)
        start = pack.up_at + (step - pack.shards) * pack.row_shard
        start = pl.multiple_of(start, 16)
        for shard in range(pack.shards):
            out_ref[shard, pl.ds(start, pack.row_shard), :] = grad[
                shard * pack.row_shard : (shard + 1) * pack.row_shard
            ].astype(BF16)

    @pl.when(step == pack.shards + pack.blocks)
    def _():
        width = att_refs[0].shape[1]
        for index, ref in enumerate(att_refs):
            tile[index * width : (index + 1) * width, :] = dot(ref[...], d_branch_ref[...], TN)
        for shard in range(pack.shards):
            start = pack.out_start(shard, member) + half * pack.out_rows
            start = pl.multiple_of(start, 16)
            out_ref[shard, pack.out_at : pack.out_at + pack.out_rows, :] = tile[
                pl.ds(start, pack.out_rows), :
            ].astype(BF16)


def weight_grads(pack, table, hidden, d_pre, d_ffn, first_low, d_branch, att, needs=()):
    row_count, model_width = d_ffn.shape
    shards, blocks = pack.shards, pack.blocks
    split = pack.down_rows % CLUSTER_ROWS == 0
    wide = pack.down_rows if split else pack.feed_shard

    def hidden_at(step, table):
        shard = jnp.minimum(step, shards - 1)
        return (0, shard * CORES + table[0] if split else shard)

    def d_pre_at(step, table):
        return (0, table[0] * blocks + jnp.clip(step - shards, 0, blocks - 1))

    def all_of(shape):
        return pl.BlockSpec(shape, lambda step, table: (0,) * len(shape))

    shape = (shards, pack.rows, model_width)
    return pl.pallas_call(
        gated(partial(weight_grads_kernel, pack, split, len(att)), 6 + len(att), needs),
        grid_spec=pltpu.PrefetchScalarGridSpec(
            num_scalar_prefetch=1,
            grid=(shards + blocks + 1,),
            in_specs=[
                pl.BlockSpec((row_count, wide), hidden_at),
                pl.BlockSpec((row_count, model_width), d_pre_at),
                all_of(d_ffn.shape),
                all_of(first_low.shape),
                all_of(d_branch.shape),
            ]
            + [all_of(piece.shape) for piece in att]
            + [ANYWHERE] * len(needs),
            out_specs=all_of(shape),
            scratch_shapes=[pltpu.VMEM((max(model_width, pack.feed_shard), model_width), F32)],
        ),
        out_shape=jax.ShapeDtypeStruct(shape, BF16),
        name="weight_grads",
        **params(
            row_count * model_width * (2 * pack.feed_width + model_width), 20_000_000, True
        ),
    )(table, hidden, d_pre, d_ffn, first_low, d_branch, *att, *needs)


def add_picked_kernel(count, first, table, *refs):
    in_refs, out_refs = refs[:count], refs[count:]
    total = in_refs[0][...].astype(F32)
    for ref in in_refs[1:]:
        total = total + ref[...].astype(F32)
    total = total.astype(BF16)
    if len(out_refs) == 1:
        out_refs[0][...] = total
        return

    @pl.when(pl.program_id(0) < first)
    def _():
        out_refs[0][...] = total

    @pl.when(pl.program_id(0) >= first)
    def _():
        out_refs[1][...] = total


def add_picked(table, arrays, steps, first=None, needs=()):
    block = (1,) + arrays[0].shape[1:]
    spec = [
        pl.BlockSpec(block, lambda s, t, k=k: (t[k * steps + s], 0, 0)) for k in range(len(arrays))
    ]
    if first is None:
        out_specs = [pl.BlockSpec(block, lambda s, t: (s, 0, 0))]
        counts = [steps]
    else:
        out_specs = [
            pl.BlockSpec(block, lambda s, t: (jnp.minimum(s, first - 1), 0, 0)),
            pl.BlockSpec(block, lambda s, t: (jnp.maximum(s - first, 0), 0, 0)),
        ]
        counts = [first, steps - first]
    return pl.pallas_call(
        gated(partial(add_picked_kernel, len(arrays), first), 1 + len(arrays), needs),
        grid_spec=pltpu.PrefetchScalarGridSpec(
            num_scalar_prefetch=1,
            grid=(steps,),
            in_specs=spec + [ANYWHERE] * len(needs),
            out_specs=out_specs,
        ),
        out_shape=[jax.ShapeDtypeStruct((n,) + block[1:], BF16) for n in counts],
        name="add_picked",
        **params(0, 2 * steps * (len(arrays) + 1) * block[1] * block[2]),
    )(table, *arrays, *needs)


def unpack_kernel(pack, depth, meta, mine_ref, other_ref, down_ref, up_ref, out_ref, ordered):
    core, level = meta[2], meta[4]
    rows = pack.rows // depth
    for mask in range(depth):
        start = pl.multiple_of(lax.bitwise_xor(level, mask) * rows, 16)
        ordered[core, pl.ds(start, rows), :] = mine_ref[mask]
        ordered[1 - core, pl.ds(start, rows), :] = other_ref[mask]
    for half in range(CORES):
        down_ref[half * pack.down_rows : (half + 1) * pack.down_rows, :] = ordered[
            half, : pack.down_rows, :
        ].astype(F32)
        for block in range(pack.blocks):
            lane = (half * pack.blocks + block) * pack.model_width
            start = pack.up_at + block * pack.row_shard
            up_ref[:, lane : lane + pack.model_width] = ordered[
                half, start : start + pack.row_shard, :
            ].astype(F32)
        out_ref[half * pack.out_rows : (half + 1) * pack.out_rows, :] = ordered[
            half, pack.out_at : pack.out_at + pack.out_rows, :
        ].astype(F32)


def unpack(pack, depth, meta, mine, other):
    vmem = pl.BlockSpec(memory_space=pltpu.VMEM)
    return pl.pallas_call(
        partial(unpack_kernel, pack, depth),
        in_specs=[IN_SMEM, vmem, vmem],
        out_specs=[vmem] * 3,
        out_shape=[
            jax.ShapeDtypeStruct((pack.feed_shard, pack.model_width), F32),
            jax.ShapeDtypeStruct((pack.row_shard, pack.feed_width), F32),
            jax.ShapeDtypeStruct((pack.row_shard, pack.model_width), F32),
        ],
        scratch_shapes=[pltpu.VMEM((CORES, pack.rows, pack.model_width), BF16)],
        name="unpack",
        compiler_params=pltpu.CompilerParams(vmem_limit_bytes=VMEM_BYTES),
        cost_estimate=pl.CostEstimate(flops=0, bytes_accessed=10_000_000, transcendentals=0),
    )(meta, mine, other)


def tie(*values):
    return lax.optimization_barrier(values)


def body(
    tokens,
    cotangent,
    perms,
    unit_kind,
    w_qkv,
    bias_qv,
    w_out,
    bias_out,
    ln_gain,
    ln_bias,
    w_up,
    bias_up,
    w_down,
    bias_down,
):
    shards = lax.axis_size("fsdp")
    groups = lax.axis_size("dp")
    here = lax.axis_index("fsdp")
    dp_index = lax.axis_index("dp")
    core = dp_index % CORES
    level = dp_index // CORES
    depth = groups // CORES
    units, rounds, unit_len = perms.shape
    per_device = unit_len // shards
    model_width = tokens.shape[1]
    feed_width = w_up.shape[1]
    row_shard = model_width // shards
    members = shards // units
    member_rows = unit_len // members
    head_cols = model_width // members
    padded = -(-head_cols // CLUSTER_ROWS) * CLUSTER_ROWS
    spot = here * CORES + core
    home_core = spot // shards
    unit = (spot // members) % units
    member = spot % members
    pack = Pack(model_width, feed_width, shards, units, depth)
    bits = [1 << k for k in range(shards.bit_length() - 1)]
    bit_orders = (bits, bits[::-1])

    def plane_pairs(target):
        pairs = []
        for z in range(depth):
            for f_index in range(shards):
                for c_index in range(CORES):
                    f_new, c_new = target(f_index, c_index)
                    pairs.append(
                        (
                            (z * CORES + c_index) * shards + f_index,
                            (z * CORES + c_new) * shards + f_new,
                        )
                    )
        return pairs

    def send(value, pairs):
        return lax.ppermute(value, ("dp", "fsdp"), pairs)

    def cross(value, mask):
        return send(value, plane_pairs(lambda f, c: divmod((f * CORES + c) ^ mask, CORES)))

    def trade(value, stage):
        return send(value, plane_pairs(lambda f, c: (f ^ bit_orders[c][stage], c)))

    def trade_mask(index, which):
        mask = 0
        for stage in range(len(bits)):
            if index >> stage & 1:
                mask ^= bit_orders[which][stage]
        return mask

    def climb(value, mask):
        plane = CORES * shards
        pairs = []
        for z in range(depth):
            for rest in range(plane):
                pairs.append((z * plane + rest, (z ^ mask) * plane + rest))
        return send(value, pairs)

    def outward(step):
        def target(f, c):
            place_now = (c * units + (f % units + step) % units) * members + f // units
            return divmod(place_now, CORES)

        return plane_pairs(target)

    def homeward(step):
        return [(b, a) for a, b in outward(step)]

    def bring_start(value):
        blocks = value.reshape(units, per_device, model_width)
        return [
            lax.dynamic_index_in_dim(blocks, (here % units + step) % units, axis=0, keepdims=False)
            for step in range(units)
        ]

    def bring(chosen):
        return jnp.concatenate(
            [send(chosen[step], outward(step)) for step in range(units)], axis=0
        )

    def send_home(value):
        blocks = value.reshape(units, per_device, model_width)
        return [send(blocks[step], homeward(step)) for step in range(units)]

    def in_order(landed, dtype):
        if units == 2:
            swap = here % units == 1
            wanted = [
                jnp.where(swap, landed[1], landed[0]),
                jnp.where(swap, landed[0], landed[1]),
            ]
        else:
            stacked = jnp.stack(landed)
            wanted = [
                lax.dynamic_index_in_dim(stacked, (index - here % units) % units, 0, keepdims=False)
                for index in range(units)
            ]
        return jnp.concatenate(wanted, axis=0).astype(dtype)

    x_chosen = bring_start(tokens)
    x_own = bring(x_chosen)
    small = jnp.concatenate(
        [
            bias_qv.reshape(-1),
            bias_out,
            ln_gain.reshape(-1),
            ln_bias.reshape(-1),
            bias_up,
            bias_down,
        ]
    )
    small_rows = -(-small.shape[0] // (3 * padded))
    small_block = jnp.pad(
        jnp.pad(small, (0, small_rows * 3 * padded - small.shape[0])).reshape(
            small_rows, 3 * padded
        ),
        ((0, 16 - small_rows), (0, 0)),
    )
    def columns_for(offset):
        start = lax.bitwise_xor(member, offset) * head_cols
        blocks = [
            jnp.pad(
                lax.dynamic_slice(
                    w_qkv, (0, kind * model_width + start), (row_shard, head_cols)
                ),
                ((0, 0), (0, padded - head_cols)),
            )
            for kind in range(3)
        ]
        return jnp.concatenate([jnp.concatenate(blocks, axis=1), small_block], axis=0)

    offsets = [(CORES * m) % members for m in range(shards)]
    kinds = sorted(set(offsets))
    *tied, x_own = tie(*[columns_for(offset) for offset in kinds], x_own)
    piece_kinds = dict(zip(kinds, tied))
    x_pieces = [x_own] + [cross(x_own, mask) for mask in range(1, members)]
    qkv_pieces = [piece_kinds[0]] + [
        cross(piece_kinds[offsets[m]], CORES * m) for m in range(1, shards)
    ]
    order_pack = jnp.concatenate(
        [perms.reshape(-1), jnp.broadcast_to(unit_kind[:, None], (units, 128)).reshape(-1)]
    )
    order_other = cross(order_pack, 1)
    order_pack = jnp.where(home_core == core, order_pack, order_other)
    order_count = units * rounds * unit_len
    unit_perm = lax.dynamic_index_in_dim(
        order_pack[:order_count].reshape(units, rounds * unit_len), unit, 0, keepdims=False
    )
    kind_now = lax.dynamic_index_in_dim(
        order_pack[order_count:].reshape(units, 128), unit, 0, keepdims=False
    )[0]
    owner = unit_perm // per_device
    order = (
        lax.bitwise_xor(owner // units, member) * units + (unit - owner % units) % units
    ) * per_device + unit_perm % per_device
    order = order.reshape(rounds, unit_len)
    order = jnp.where(core == 0, order, order[::-1])
    order_row = order.reshape(1, rounds * unit_len)
    order = order.reshape(-1, CLUSTER_ROWS)
    x_here = arrange(order, x_pieces, unit_len, 0)
    x_now = [x_here, cross(x_here, 1)]
    own_masks = [
        jnp.where(core == 0, trade_mask(i, 0), trade_mask(i, 1)) for i in range(1, shards)
    ]
    other_masks = [
        jnp.where(core == 0, trade_mask(i, 1), trade_mask(i, 0)) for i in range(1, shards)
    ]
    zero = jnp.int32(0)
    meta = jnp.stack(
        [kind_now, here, core, member, level, zero, zero, zero] + own_masks + other_masks
    ).astype(jnp.int32)

    def half_of(value, axis, length, at):
        return lax.dynamic_slice_in_dim(value, at * length, length, axis=axis)

    packed = jnp.concatenate(
        [half_of(w_down, 0, pack.down_rows, core)]
        + [
            half_of(w_up, 1, model_width, core * pack.blocks + block)
            for block in range(pack.blocks)
        ]
        + [half_of(w_out, 0, pack.out_rows, core)],
        axis=0,
    )
    smalls = jnp.stack(
        [
            piece[row_shard : row_shard + small_rows].reshape(-1)[: small.shape[0]]
            for piece in qkv_pieces
        ]
    )
    smalls = jnp.take(smalls, lax.bitwise_xor(here, jnp.arange(shards)), axis=0).astype(F32)

    def vectors_at(start, count, length):
        part = smalls[:, start * row_shard : start * row_shard + count * length]
        return (
            part.reshape(shards, count, length).transpose(1, 0, 2).reshape(count, shards * length)
        )

    my_bias = lax.dynamic_index_in_dim(
        vectors_at(0, 2, row_shard).reshape(2, members, head_cols), member, 1, keepdims=False
    )
    my_bias = jnp.pad(my_bias, ((0, 0), (0, padded - head_cols)))
    my_bias = jnp.stack([my_bias[0], jnp.zeros_like(my_bias[0]), my_bias[1]]).reshape(1, -1)
    up_bias = vectors_at(7, 1, feed_width // shards)
    down_bias = smalls[:, small.shape[0] - row_shard :].reshape(1, model_width)
    vectors = jnp.concatenate(
        [vectors_at(2, 5, row_shard), down_bias, jnp.zeros((2, model_width), F32)], axis=0
    )

    order_rows = unit_len // CLUSTER_ROWS
    arranged, probs, mixtures = [], [], []
    *tied, packed, x_now[0] = tie(*qkv_pieces[1:], packed, x_now[0])
    qkv_pieces = qkv_pieces[:1] + tied
    weight_pieces = {0: packed}
    for stage in range(len(bits)):
        weight_pieces[1 << stage] = trade(packed, stage)
    for index in range(rounds):
        results = attend(meta, x_now[index], my_bias, qkv_pieces, row_shard, mixtures[-1:])
        for kept, result in zip((arranged, probs, mixtures), results):
            kept.append(result)
    first_ones = [1 << stage for stage in range(len(bits))]
    *tied, cot_now, mixtures[0] = tie(
        *[weight_pieces[index] for index in first_ones], cotangent, mixtures[0]
    )
    weight_pieces.update(zip(first_ones, tied))
    for stage in range(1, len(bits)):
        for index in range(1, 1 << stage):
            weight_pieces[index | 1 << stage] = trade(weight_pieces[index], stage)
    cot_own = bring(bring_start(cot_now))
    last_ones = [index for index in range(1, shards) if index not in first_ones]
    *tied, mixtures[1] = tie(*[weight_pieces[index] for index in last_ones], mixtures[1])
    weight_pieces.update(zip(last_ones, tied))
    att_there = []
    for mask in range(1, members):
        there = place(order_row, mixtures, mask * member_rows, member_rows, 0.5)
        att_there.append(cross(there[:, :head_cols], mask))
    att_here = place(order_row, mixtures, 0, member_rows, 0.5)
    att_raw = [att_here[:, :head_cols]] + att_there
    if head_cols % CLUSTER_ROWS:
        att_raw = [jnp.concatenate(att_raw, axis=1)]

    direct = [weight_pieces[index] for index in range(1, shards)]
    swapped = [cross(piece, 1) for piece in direct]
    block_out, first_low, d_branch, d_ffn, hidden, d_pre, d_lower, *rest = feed(
        pack,
        meta,
        x_own,
        cot_own,
        vectors,
        up_bias,
        att_raw,
        [w_out, w_up, w_down],
        direct + swapped,
    )
    d_att, (row_sums, up_sums) = rest[: len(att_raw)], rest[len(att_raw) :]
    if head_cols % CLUSTER_ROWS:
        d_att = [d_att[0][:, mask * head_cols : (mask + 1) * head_cols] for mask in range(members)]
    d_att = [d_att[0]] + [cross(d_att[mask], mask) for mask in range(1, members)]
    d_att = [jnp.pad(piece, ((0, 0), (0, padded - head_cols))) for piece in d_att]

    def grads_of(half, *needed):
        table = jnp.stack([half, member]).astype(jnp.int32)
        return weight_grads(
            pack, table, hidden, d_pre, d_ffn, first_low, d_branch, att_raw, needed
        )

    theirs = grads_of(1 - core)
    output_landed = send_home(block_out)
    mine = grads_of(core, theirs)
    theirs = cross(theirs, 1)
    sending = [index for index in range(shards) if index & 1]
    keeping = [index for index in range(shards) if not index & 1]
    slots = jnp.stack(
        [
            lax.bitwise_xor(here, jnp.where(core == 0, trade_mask(i, 0), trade_mask(i, 1)))
            for i in sending + keeping
        ]
    )
    going, kept = add_picked(
        jnp.concatenate([slots, slots]).astype(jnp.int32),
        [mine, theirs],
        shards,
        len(sending),
        output_landed,
    )

    def merge(kept, landed, *needs):
        count = kept.shape[0]
        if count == 1:
            table = jnp.zeros((2,), jnp.int32)
            return None, add_picked(table, [kept, landed], 1, None, needs)[0]
        order_now = [i for i in range(count) if i & 1] + [i for i in range(count) if not i & 1]
        table = jnp.array(order_now * 2, jnp.int32)
        return add_picked(table, [kept, landed], count, count // 2, needs)

    grads, d_x, bias_sums = [None] * rounds, [None] * rounds, []
    needs = [going]
    for turn, index in enumerate(reversed(range(rounds))):
        results = attend_back(
            meta,
            order,
            arranged[index],
            probs[index],
            d_att,
            qkv_pieces,
            row_shard,
            index * order_rows,
            needs,
        )
        grads[index], d_x[index] = results[0], results[1]
        bias_sums.append(results[2])
        if turn < len(bits):
            going, kept = merge(kept, trade(going, turn), results[0])
            needs = [kept]
    for stage in range(rounds, len(bits)):
        going, kept = merge(kept, trade(going, stage))
    x_last, kept = tie(x_now[0], kept)

    def level_pieces(block):
        return block.reshape((depth, block.shape[0] // depth) + block.shape[1:])

    def level_scatter(cut):
        return [
            climb(
                lax.dynamic_index_in_dim(cut, lax.bitwise_xor(level, mask), 0, keepdims=False), mask
            )
            for mask in range(1, depth)
        ]

    def level_gather(piece):
        return jnp.stack([piece] + [climb(piece, mask) for mask in range(1, depth)])

    cut = level_pieces(kept[0])
    landed = level_scatter(cut)

    def grad_of(left, right):
        return lax.dot_general(left, right, TN, preferred_element_type=F32)

    qkv_grad = (grad_of(x_now[1], grads[1]) + grad_of(x_last, grads[0])).astype(BF16)
    bias_sum = sum(bias_sums)
    qkv_grad = qkv_grad.reshape(shards, row_shard, 3, padded)[..., :head_cols]
    qkv_grad = qkv_grad.reshape(shards, row_shard, 3 * head_cols)
    bias_sum = bias_sum.reshape(3, padded)[:, :head_cols]
    mine_now = (jnp.arange(members) == member)[None, :, None]
    bias_parts = jnp.where(mine_now, bias_sum[::2][:, None, :], 0.0).reshape(2, model_width)

    def by_shard(value):
        count, length = value.shape
        return (
            value.reshape(count, shards, length // shards)
            .transpose(1, 0, 2)
            .reshape(shards, count * length // shards)
        )

    small_grad = jnp.concatenate(
        [
            by_shard(bias_parts),
            by_shard(row_sums[:5]),
            by_shard(up_sums),
            by_shard(row_sums[5:6]),
        ],
        axis=1,
    ).astype(BF16)
    small_length = small_grad.shape[1]
    extra = -(-small_length // (3 * head_cols))
    extra_rows = -(-extra // 16) * 16
    small_grad = jnp.pad(
        small_grad, ((0, 0), (0, extra_rows * 3 * head_cols - small_length))
    ).reshape(shards, extra_rows, 3 * head_cols)
    joined = jnp.concatenate([qkv_grad, small_grad], axis=1)
    classes = max(1, members // CORES)
    d_x_parts = [d_x[0], cross(d_x[1], 1)]
    order_mine = order_row[:, :unit_len]
    d_there = [
        place(
            order_mine,
            d_x_parts,
            mask * member_rows,
            member_rows,
            added=True,
            needs=[joined],
        )
        for mask in range(1, members)
    ]
    early = []
    if classes == 1:
        slots_held = jnp.stack(
            [
                lax.bitwise_xor(here, jnp.where(core == 0, trade_mask(i, 0), trade_mask(i, 1)))
                for i in range(shards)
            ]
        )
        held = jnp.stack(
            [
                lax.dynamic_index_in_dim(joined, slots_held[i], 0, keepdims=False)
                for i in range(0, shards, 2)
            ]
        )
        leaving = jnp.stack(
            [
                lax.dynamic_index_in_dim(joined, slots_held[i], 0, keepdims=False)
                for i in range(1, shards, 2)
            ]
        )
        for stage in range(len(bits)):
            gate = d_there if stage == 0 else []
            leaving, held = merge(held, trade(leaving, stage), *gate)
            if stage == 0:
                early = [held]
        totals = [held[0]]
    else:
        totals = [None] * classes
        for m in range(shards):
            offset = offsets[m] // CORES
            piece = lax.dynamic_index_in_dim(joined, lax.bitwise_xor(here, m), 0, keepdims=False)
            piece = (piece if m == 0 else cross(piece, CORES * m)).astype(F32)
            totals[offset] = piece if totals[offset] is None else totals[offset] + piece

    d_inputs = place(
        order_mine,
        d_x_parts,
        0,
        member_rows,
        1.0,
        F32,
        d_lower,
        added=True,
        needs=early + d_there,
    )
    d_here = d_inputs
    for mask, there in enumerate(d_there, 1):
        d_inputs = d_inputs + cross(there, mask).astype(F32)
    d_inputs = d_inputs.astype(BF16)
    if depth > 1:
        picks = jnp.concatenate([level[None], jnp.zeros((depth - 1,), level.dtype)])
        (kept,) = add_picked(
            picks.astype(jnp.int32),
            [cut] + [piece[None] for piece in landed],
            1,
            None,
            [d_here],
        )
    stacked = level_gather(kept[0]) if depth > 1 else cut
    d_inputs = in_order(send_home(d_inputs), F32)
    output = in_order(output_landed, BF16)
    grad_down, grad_up, grad_out = unpack(pack, depth, meta, stacked, cross(stacked, 1))

    totals = jnp.concatenate(totals, axis=0).astype(BF16)
    rows_each = row_shard + extra_rows
    if depth > 1:
        cut = level_pieces(totals)
        total = lax.dynamic_index_in_dim(cut, level, 0, keepdims=False).astype(F32)
        for piece in level_scatter(cut):
            total = total + piece.astype(F32)
        gathered = level_gather(total.astype(BF16))
        gathered = jnp.take(gathered, lax.bitwise_xor(level, jnp.arange(depth)), axis=0)
        totals = gathered.reshape(totals.shape)
    landed = jnp.stack([totals, cross(totals, 1)], axis=0).reshape(
        CORES, classes, rows_each, 3 * head_cols
    )
    smalls_out = jnp.sum(landed[:, :, row_shard:].astype(F32), axis=(0, 1)).reshape(-1)
    smalls_out = smalls_out[:small_length]
    landed = (
        landed[:, :, :row_shard].transpose(1, 0, 2, 3).reshape(members, row_shard, 3, head_cols)
    )
    if members == 2:
        swap = member == 1
        landed = jnp.stack(
            [
                jnp.where(swap, landed[1], landed[0]),
                jnp.where(swap, landed[0], landed[1]),
            ]
        )
    else:
        landed = jnp.take(landed, lax.bitwise_xor(member, jnp.arange(members)), axis=0)
    grad_qkv = landed.transpose(1, 2, 0, 3).reshape(row_shard, 3 * model_width).astype(F32)

    feed_shard = feed_width // shards
    spots = [2 * row_shard, 3 * row_shard, 5 * row_shard, 7 * row_shard]
    return (
        output,
        d_inputs,
        grad_qkv,
        smalls_out[: spots[0]].reshape(2, row_shard),
        grad_out,
        smalls_out[spots[0] : spots[1]],
        smalls_out[spots[1] : spots[2]].reshape(2, row_shard),
        smalls_out[spots[2] : spots[3]].reshape(2, row_shard),
        grad_up,
        smalls_out[spots[3] : spots[3] + feed_shard],
        grad_down,
        smalls_out[spots[3] + feed_shard :],
    )


def solution(mesh):
    placed = (
        P(("dp", "fsdp"), None),
        P(("dp", "fsdp"), None),
        P("dp", None, None),
        P("dp"),
        P("fsdp", None),
        P(None, "fsdp"),
        P("fsdp", None),
        P("fsdp"),
        P(None, "fsdp"),
        P(None, "fsdp"),
        P("fsdp", None),
        P("fsdp"),
        P("fsdp", None),
        P("fsdp"),
    )
    return jax.shard_map(
        body,
        mesh=mesh,
        in_specs=placed,
        out_specs=(
            P(("dp", "fsdp"), None),
            P(("dp", "fsdp"), None),
            P("fsdp", None),
            P(None, "fsdp"),
            P("fsdp", None),
            P("fsdp"),
            P(None, "fsdp"),
            P(None, "fsdp"),
            P("fsdp", None),
            P("fsdp"),
            P("fsdp", None),
            P("fsdp"),
        ),
        check_vma=False,
    )
```

```python
from functools import partial

import jax
import jax.numpy as jnp
from jax import lax
from jax.experimental import pallas as pl
from jax.experimental.pallas import tpu as pltpu
from jax.sharding import PartitionSpec as P

HEAD_DIM = 64
CORES = 2
NEG_FILL = -1000000000.0
EPSILON = 1e-05
SCALE = HEAD_DIM ** (-0.5)
BIAS_ROW = 2
GRAD_LANES = 384
CLUSTER_ROWS = 128
HALF_ROWS = 64
POS_BLOCK = 512
TOKEN_BLOCK = 512
ROW_BLOCK = 256
FF_BLOCK = 512
VMEM_BYTES = 60 * 1024 * 1024
COST_SHARE = 16
NT = (((1,), (1,)), ((), ()))
TN = (((0,), (0,)), ((), ()))
F32 = jnp.float32
BF16 = jnp.bfloat16
ANYWHERE = pl.BlockSpec(memory_space=pl.ANY)
IN_SMEM = pl.BlockSpec(memory_space=pltpu.SMEM)


def whole(shape):
    return pl.BlockSpec(shape, lambda i: (0,) * len(shape))


def rows_of(shape):
    return pl.BlockSpec(shape, lambda i: (i,) + (0,) * (len(shape) - 1))


def dot(a, b, dims=(((1,), (0,)), ((), ()))):
    return lax.dot_general(a, b, dims, preferred_element_type=F32)


def params(flops=0, moved=0):
    return dict(
        compiler_params=pltpu.CompilerParams(
            dimension_semantics=("arbitrary",),
            vmem_limit_bytes=VMEM_BYTES,
        ),
        cost_estimate=pl.CostEstimate(
            flops=flops // COST_SHARE, bytes_accessed=moved // COST_SHARE, transcendentals=0
        ),
    )


def gated(kernel, used, needs):
    if not needs:
        return kernel

    def run(*refs):
        return kernel(*refs[:used], *refs[used + len(needs) :])

    return run


def lane_masks():
    lane = lax.broadcasted_iota(jnp.int32, (CLUSTER_ROWS, CLUSTER_ROWS), 1)
    low = (lane < HEAD_DIM).astype(F32)
    return low.astype(BF16), (1.0 - low).astype(BF16), lane < HEAD_DIM


def both_heads(rows_now, low, high):
    return jnp.concatenate([rows_now * low, rows_now * high], axis=0)


def equal_ones(left, right):
    return jnp.where(left == right, jnp.ones((), BF16), jnp.zeros((), BF16))


def pick_rows(order_ref, first_row, unit_len):
    parts = []
    lane = lax.broadcasted_iota(jnp.int16, (CLUSTER_ROWS, CLUSTER_ROWS), 1)
    for part in range(POS_BLOCK // CLUSTER_ROWS):
        row = order_ref[pl.ds(first_row + part, 1), :]
        column = jnp.transpose(jnp.broadcast_to(row, (CLUSTER_ROWS, CLUSTER_ROWS)))
        column = column.astype(jnp.int16)
        pieces = [
            equal_ones(column, lane + jnp.int16(base)) for base in range(0, unit_len, CLUSTER_ROWS)
        ]
        parts.append(jnp.concatenate(pieces, axis=1))
    return jnp.concatenate(parts, axis=0)


def load_pieces(meta, x_refs, w_refs, x_all, w_all, sems, row_shard):
    member_rows = x_all.shape[0] // max(1, len(x_refs))
    copies = []
    for index, ref in enumerate(x_refs):
        copies.append(
            pltpu.make_async_copy(
                ref, x_all.at[pl.ds(index * member_rows, member_rows), :], sems.at[index]
            )
        )
    for index, ref in enumerate(w_refs):
        start = pl.multiple_of(lax.bitwise_xor(meta[1], index) * row_shard, 16)
        copies.append(
            pltpu.make_async_copy(
                ref.at[pl.ds(0, row_shard), :],
                w_all.at[pl.ds(start, row_shard), :],
                sems.at[len(x_refs) + index],
            )
        )
    for copy in copies:
        copy.start()
    for copy in copies:
        copy.wait()


def arrange_kernel(unit_len, first_row, order_ref, *refs):
    x_refs, out_ref = refs[:-1], refs[-1]
    step = pl.program_id(0)
    picks = pick_rows(order_ref, first_row + step * (POS_BLOCK // CLUSTER_ROWS), unit_len)
    rows = x_refs[0].shape[0]
    total = None
    for index, ref in enumerate(x_refs):
        term = dot(picks[:, index * rows : (index + 1) * rows], ref[...])
        total = term if total is None else total + term
    out_ref[...] = total.astype(BF16)


def arrange(order, x_pieces, position_count, first_row):
    member_rows, width = x_pieces[0].shape
    unit_len = member_rows * len(x_pieces)
    return pl.pallas_call(
        partial(arrange_kernel, unit_len, first_row),
        grid=(position_count // POS_BLOCK,),
        in_specs=[whole(order.shape)] + [whole(piece.shape) for piece in x_pieces],
        out_specs=rows_of((POS_BLOCK, width)),
        out_shape=jax.ShapeDtypeStruct((position_count, width), BF16),
        name="arrange",
        **params(2 * position_count * unit_len * width, 6_000_000),
    )(order, *x_pieces)


def attend_kernel(sizes, meta, x_now_ref, bias_ref, *refs):
    shards, row_shard = sizes
    w_refs, refs = refs[:shards], refs[shards:]
    arranged_ref, probs_ref, mixture_ref, turned_ref, w_all, sems = refs
    width = w_all.shape[1] // 3
    step = pl.program_id(0)

    @pl.when(step == 0)
    def _():
        load_pieces(meta, [], w_refs, w_all, w_all, sems, row_shard)

    x_now = x_now_ref[...]
    turned_ref[...] = jnp.transpose(x_now)
    arranged = (dot(x_now, w_all[...]) + bias_ref[...]).astype(BF16)
    arranged_ref[...] = arranged
    low, high, lane_low = lane_masks()
    position = lax.broadcasted_iota(jnp.int32, (CLUSTER_ROWS, CLUSTER_ROWS), 0)
    other = lax.broadcasted_iota(jnp.int32, (CLUSTER_ROWS, CLUSTER_ROWS), 1)
    same_half = (position < HALF_ROWS) == (other < HALF_ROWS)
    allowed = jnp.logical_or(same_half, meta[0] == 1)
    pairs = width // CLUSTER_ROWS
    for part in range(POS_BLOCK // CLUSTER_ROWS):
        rows_now = slice(part * CLUSTER_ROWS, (part + 1) * CLUSTER_ROWS)
        for pair in range(pairs):
            base = pair * CLUSTER_ROWS
            queries = arranged[rows_now, base : base + CLUSTER_ROWS] * SCALE
            keys = arranged[rows_now, width + base : width + base + CLUSTER_ROWS]
            values = arranged[rows_now, 2 * width + base : 2 * width + base + CLUSTER_ROWS]
            scores = dot(both_heads(keys, low, high), queries, NT)
            halves = []
            for head in range(2):
                one = scores[head * CLUSTER_ROWS : (head + 1) * CLUSTER_ROWS]
                one = jnp.where(allowed, one, NEG_FILL)
                grown = jnp.exp(one - jnp.max(one, axis=0, keepdims=True))
                halves.append(grown * (1.0 / jnp.sum(grown, axis=0, keepdims=True)))
            probs = jnp.concatenate(halves, axis=0).astype(BF16)
            at = (part * pairs + pair) * 2 * CLUSTER_ROWS
            probs_ref[at : at + 2 * CLUSTER_ROWS, :] = probs
            mixture = dot(probs, both_heads(values, low, high), TN).astype(BF16)
            mixture_ref[rows_now, base : base + CLUSTER_ROWS] = mixture


def attend(meta, x_now, bias, w_pieces, row_shard, needs=()):
    shards = len(w_pieces)
    position_count, model_width = x_now.shape
    cols = w_pieces[0].shape[1]
    width = cols // 3
    pair_rows = 2 * width
    return pl.pallas_call(
        gated(partial(attend_kernel, (shards, row_shard)), 3 + shards, needs),
        grid=(position_count // POS_BLOCK,),
        in_specs=[IN_SMEM, rows_of((POS_BLOCK, model_width)), whole(bias.shape)]
        + [ANYWHERE] * (shards + len(needs)),
        out_specs=[
            rows_of((POS_BLOCK, cols)),
            rows_of((POS_BLOCK // CLUSTER_ROWS * pair_rows, CLUSTER_ROWS)),
            rows_of((POS_BLOCK, width)),
            pl.BlockSpec((model_width, POS_BLOCK), lambda i: (0, i)),
        ],
        out_shape=[
            jax.ShapeDtypeStruct((position_count, cols), BF16),
            jax.ShapeDtypeStruct((position_count // CLUSTER_ROWS * pair_rows, CLUSTER_ROWS), BF16),
            jax.ShapeDtypeStruct((position_count, width), BF16),
            jax.ShapeDtypeStruct((model_width, position_count), BF16),
        ],
        scratch_shapes=[
            pltpu.VMEM((model_width, cols), BF16),
            pltpu.SemaphoreType.DMA((shards,)),
        ],
        name="attend",
        **params(
            2 * position_count * (model_width * cols + 4 * CLUSTER_ROWS * width), 18_000_000
        ),
    )(meta, x_now, bias, *w_pieces, *needs)


def place_kernel(sizes, scale, has_base, order_row_ref, *refs):
    unit_len, first_token, added = sizes
    base_ref = refs[0] if has_base else None
    refs = refs[1 if has_base else 0 :]
    if added:
        first_ref, second_ref, out_ref, held = refs

        @pl.when(pl.program_id(0) == 0)
        def _():
            held[...] = (first_ref[...].astype(F32) + second_ref[...].astype(F32)).astype(BF16)

        source_refs = [held]
    else:
        source_refs, out_ref = refs[:-1], refs[-1]
    block_rows = out_ref.shape[0]
    first = jnp.full((1, 1), first_token + pl.program_id(0) * block_rows, jnp.int32)
    token = lax.broadcasted_iota(jnp.int16, (block_rows, unit_len), 0)
    total = None
    for index, ref in enumerate(source_refs):
        row = order_row_ref[:, index * unit_len : (index + 1) * unit_len] - first
        row = jnp.broadcast_to(row, (16, unit_len)).astype(jnp.int16)
        row = jnp.concatenate([row] * (block_rows // 16), axis=0)
        term = dot(equal_ones(row, token), ref[...])
        total = term if total is None else total + term
    if scale != 1.0:
        total = total * scale
    if has_base:
        total = total + base_ref[...]
    out_ref[...] = total.astype(out_ref.dtype)


def place(
    order_row,
    sources,
    first_token,
    row_count,
    scale=1.0,
    dtype=BF16,
    base=None,
    added=False,
    needs=(),
):
    unit_len, width = sources[0].shape
    block_rows = min(TOKEN_BLOCK, row_count)
    extra = [] if base is None else [base]
    return pl.pallas_call(
        gated(
            partial(place_kernel, (unit_len, first_token, added), scale, base is not None),
            1 + len(extra) + len(sources),
            needs,
        ),
        grid=(row_count // block_rows,),
        in_specs=[whole(order_row.shape)]
        + [rows_of((block_rows, width))] * len(extra)
        + [whole(source.shape) for source in sources]
        + [ANYWHERE] * len(needs),
        out_specs=rows_of((block_rows, width)),
        out_shape=jax.ShapeDtypeStruct((row_count, width), dtype),
        scratch_shapes=[pltpu.VMEM((unit_len, width), BF16)] if added else [],
        name="place",
        **params(
            2 * row_count * unit_len * (1 if added else len(sources)) * width, 10_000_000
        ),
    )(order_row, *extra, *sources, *needs)


def attend_back_kernel(sizes, meta, order_ref, arranged_ref, probs_ref, *refs):
    members, shards, unit_len, row_shard, first_row = sizes
    g_refs, refs = refs[:members], refs[members:]
    w_refs, refs = refs[:shards], refs[shards:]
    grads_ref, d_x_ref, g_all, w_all, sems = refs
    width = w_all.shape[1] // 3
    step = pl.program_id(0)

    @pl.when(step == 0)
    def _():
        load_pieces(meta, g_refs, w_refs, g_all, w_all, sems, row_shard)

    picks = pick_rows(order_ref, first_row + step * (POS_BLOCK // CLUSTER_ROWS), unit_len)
    d_mixture = dot(picks, g_all[...]).astype(BF16)
    low, high, lane_low = lane_masks()
    pairs = width // CLUSTER_ROWS
    for part in range(POS_BLOCK // CLUSTER_ROWS):
        rows_now = slice(part * CLUSTER_ROWS, (part + 1) * CLUSTER_ROWS)
        for pair in range(pairs):
            base = pair * CLUSTER_ROWS
            q_lanes = slice(base, base + CLUSTER_ROWS)
            k_lanes = slice(width + base, width + base + CLUSTER_ROWS)
            v_lanes = slice(2 * width + base, 2 * width + base + CLUSTER_ROWS)
            queries = arranged_ref[rows_now, q_lanes] * SCALE
            keys = arranged_ref[rows_now, k_lanes] * SCALE
            values = arranged_ref[rows_now, v_lanes]
            at = (part * pairs + pair) * 2 * CLUSTER_ROWS
            probs = probs_ref[at : at + 2 * CLUSTER_ROWS, :]
            d_now = d_mixture[rows_now, base : base + CLUSTER_ROWS]
            d_probs = dot(both_heads(values, low, high), d_now, NT)
            pieces = []
            for head in range(2):
                rows = slice(head * CLUSTER_ROWS, (head + 1) * CLUSTER_ROWS)
                weight = probs[rows].astype(F32)
                d_one = d_probs[rows]
                inner = jnp.sum(weight * d_one, axis=0, keepdims=True)
                pieces.append(weight * (d_one - inner))
            d_scores = jnp.concatenate(pieces, axis=0).astype(BF16)
            d_query = dot(d_scores, both_heads(keys, low, high), TN)
            d_keys = dot(d_scores, queries)
            d_values = dot(probs, d_now)
            grads_ref[rows_now, q_lanes] = d_query.astype(BF16)
            grads_ref[rows_now, k_lanes] = jnp.where(
                lane_low, d_keys[:CLUSTER_ROWS], d_keys[CLUSTER_ROWS:]
            ).astype(BF16)
            grads_ref[rows_now, v_lanes] = jnp.where(
                lane_low, d_values[:CLUSTER_ROWS], d_values[CLUSTER_ROWS:]
            ).astype(BF16)
    grads = grads_ref[...]
    d_x_ref[...] = dot(grads, w_all[...], NT).astype(BF16)


def attend_back(
    meta, order, arranged, probs, g_pieces, w_pieces, row_shard, first_row, needs=()
):
    members, shards = len(g_pieces), len(w_pieces)
    member_rows, width = g_pieces[0].shape
    unit_len = members * member_rows
    position_count, cols = arranged.shape
    model_width = row_shard * shards
    return pl.pallas_call(
        gated(
            partial(attend_back_kernel, (members, shards, unit_len, row_shard, first_row)),
            4 + members + shards,
            needs,
        ),
        grid=(position_count // POS_BLOCK,),
        in_specs=[
            IN_SMEM,
            whole(order.shape),
            rows_of((POS_BLOCK, cols)),
            rows_of((POS_BLOCK // CLUSTER_ROWS * 2 * width, CLUSTER_ROWS)),
        ]
        + [ANYWHERE] * (members + shards + len(needs)),
        out_specs=[
            rows_of((POS_BLOCK, cols)),
            rows_of((POS_BLOCK, model_width)),
        ],
        out_shape=[
            jax.ShapeDtypeStruct((position_count, cols), BF16),
            jax.ShapeDtypeStruct((position_count, model_width), BF16),
        ],
        scratch_shapes=[
            pltpu.VMEM((unit_len, width), BF16),
            pltpu.VMEM((model_width, cols), BF16),
            pltpu.SemaphoreType.DMA((members + shards,)),
        ],
        name="attend_back",
        **params(2 * position_count * (unit_len * width + model_width * cols), 20_000_000),
    )(meta, order, arranged, probs, *g_pieces, *w_pieces, *needs)


def normalise(summed):
    average = jnp.mean(summed, axis=-1, keepdims=True)
    centred = summed - average
    spread = jnp.mean(centred * centred, axis=-1, keepdims=True)
    scale_inv = lax.rsqrt(spread + EPSILON)
    return centred * scale_inv, scale_inv


def normalise_back(grad_out, normed, scale_inv, gain_row):
    scaled = grad_out * gain_row
    return scale_inv * (
        scaled
        - jnp.mean(scaled, axis=-1, keepdims=True)
        - normed * jnp.mean(scaled * normed, axis=-1, keepdims=True)
    )


def column_sum(rows_now):
    return jnp.sum(rows_now, axis=0, keepdims=True)


def gelu_parts(value):
    below = 0.5 + 0.5 * lax.erf(value * 0.7071067811865476)
    bell = jnp.exp(value * value * -0.5) * 0.3989422804014327
    return value * below, below + value * bell


class Pack:
    def __init__(self, model_width, feed_width, shards, units, depth):
        self.model_width, self.feed_width, self.shards = model_width, feed_width, shards
        self.row_shard = model_width // shards
        self.feed_shard = feed_width // shards
        self.down_rows = self.feed_shard // CORES
        self.blocks = feed_width // CORES // model_width
        self.up_at = self.down_rows
        self.out_at = self.up_at + self.blocks * self.row_shard
        self.out_rows = self.row_shard // CORES
        self.used = self.out_at + self.out_rows
        unit = 16 * depth
        self.rows = -(-self.used // unit) * unit
        self.units = units
        self.group = units * self.row_shard

    def out_start(self, shard, member):
        return (
            lax.bitwise_xor(jnp.int32(shard) // self.units, member) * self.group
            + (shard % self.units) * self.row_shard
        )


def feed_kernel(pack, att_count, meta, x_ref, cot_ref, vec_ref, up_bias_ref, *refs):
    shards = pack.shards
    att_refs, refs = refs[:att_count], refs[att_count:]
    own_out, own_up, own_down = refs[:3]
    refs = refs[3:]
    pieces, refs = refs[: 2 * (shards - 1)], refs[2 * (shards - 1) :]
    out_ref, first_turned_ref, d_branch_ref, d_ffn_turned_ref, hidden_ref, d_pre_ref = refs[:6]
    d_h1_ref, att_turned_ref = refs[6:8]
    refs = refs[8:]
    d_att_refs, refs = refs[:att_count], refs[att_count:]
    sums_ref, up_sums_ref, w_out, w_up, w_down, slope, sems = refs
    step = pl.program_id(0)
    here, core, member = meta[1], meta[2], meta[3]
    feed_width = pack.feed_width

    def loads(kind):
        copies = []

        def add(source, target):
            copies.append(pltpu.make_async_copy(source, target, sems.at[kind, len(copies)]))

        if kind == 0:
            start = pl.multiple_of(pack.out_start(here, member), 16)
            add(own_out, w_out.at[pl.ds(start, pack.row_shard), :])
        elif kind == 1:
            start = pl.multiple_of(here * pack.row_shard, 16)
            add(own_up, w_up.at[pl.ds(start, pack.row_shard), :])
        else:
            start = pl.multiple_of(here * pack.feed_shard, 16)
            add(own_down, w_down.at[pl.ds(start, pack.feed_shard), :])
        for index, ref in enumerate(pieces):
            peer = lax.bitwise_xor(here, meta[8 + index])
            half = core if index < shards - 1 else 1 - core
            if kind == 0:
                start = pack.out_start(peer, member) + half * pack.out_rows
                start = pl.multiple_of(start, 16)
                add(
                    ref.at[pl.ds(pack.out_at, pack.out_rows), :],
                    w_out.at[pl.ds(start, pack.out_rows), :],
                )
            elif kind == 1:
                start = pl.multiple_of(peer * pack.row_shard, 16)
                for block in range(pack.blocks):
                    lane = pl.multiple_of(
                        (half * pack.blocks + block) * pack.model_width, CLUSTER_ROWS
                    )
                    add(
                        ref.at[pl.ds(pack.up_at + block * pack.row_shard, pack.row_shard), :],
                        w_up.at[pl.ds(start, pack.row_shard), pl.ds(lane, pack.model_width)],
                    )
            else:
                start = pl.multiple_of(peer * pack.feed_shard + half * pack.down_rows, 16)
                add(
                    ref.at[pl.ds(0, pack.down_rows), :],
                    w_down.at[pl.ds(start, pack.down_rows), :],
                )
        return copies

    @pl.when(step == 0)
    def _():
        for kind in range(3):
            for copy in loads(kind):
                copy.start()
        sums_ref[...] = jnp.zeros_like(sums_ref)
        up_sums_ref[...] = jnp.zeros_like(up_sums_ref)
        for copy in loads(0):
            copy.wait()

    bias_out, gain_one, gain_two = vec_ref[0:1, :], vec_ref[1:2, :], vec_ref[2:3, :]
    shift_one, shift_two, bias_down = vec_ref[3:4, :], vec_ref[4:5, :], vec_ref[5:6, :]
    att_width = att_refs[0].shape[1]
    summed = x_ref[...].astype(F32) + bias_out
    for index, ref in enumerate(att_refs):
        summed += dot(ref[...], w_out[index * att_width : (index + 1) * att_width, :])
    normed_one, inv_one = normalise(summed)
    first = normed_one * gain_one + shift_one
    first_low = first.astype(BF16)
    first_turned_ref[...] = jnp.transpose(first_low)
    for index, ref in enumerate(att_refs):
        att_turned_ref[index * att_width : (index + 1) * att_width, :] = jnp.transpose(ref[...])

    @pl.when(step == 0)
    def _():
        for kind in (1, 2):
            for copy in loads(kind):
                copy.wait()

    second = first + bias_down
    starts = list(range(0, feed_width, FF_BLOCK))

    def raised(base):
        lanes = slice(base, base + FF_BLOCK)
        return dot(first_low, w_up[:, lanes]) + up_bias_ref[:, lanes]

    pre = raised(starts[0])
    for index, base in enumerate(starts):
        lanes = slice(base, base + FF_BLOCK)
        pre_next = raised(starts[index + 1]) if index + 1 < len(starts) else None
        hidden, slope_now = gelu_parts(pre)
        hidden = hidden.astype(BF16)
        hidden_ref[:, lanes] = hidden
        slope[:, lanes] = slope_now
        second += dot(hidden, w_down[lanes, :])
        pre = pre_next
    normed_two, inv_two = normalise(second)
    out_ref[...] = (normed_two * gain_two + shift_two).astype(BF16)
    top = cot_ref[...].astype(F32)
    d_second = normalise_back(top, normed_two, inv_two, gain_two)
    d_ffn = d_second.astype(BF16)
    d_ffn_turned_ref[...] = jnp.transpose(d_ffn)
    d_first = d_second
    d_hidden = dot(d_ffn, w_down[0:FF_BLOCK, :], NT)
    for index, base in enumerate(starts):
        lanes = slice(base, base + FF_BLOCK)
        if index + 1 < len(starts):
            d_next = dot(d_ffn, w_down[starts[index + 1] : starts[index + 1] + FF_BLOCK, :], NT)
        d_pre = (d_hidden * slope[:, lanes]).astype(BF16)
        d_pre_ref[:, lanes] = d_pre
        up_sums_ref[:, lanes] += column_sum(d_pre.astype(F32))
        d_first += dot(d_pre, w_up[:, lanes], NT)
        d_hidden = d_next
    d_lower = normalise_back(d_first, normed_one, inv_one, gain_one)
    d_h1_ref[...] = d_lower
    d_branch = d_lower.astype(BF16)
    d_branch_ref[...] = d_branch
    for index, ref in enumerate(d_att_refs):
        back = dot(d_branch, w_out[index * att_width : (index + 1) * att_width, :], NT)
        ref[...] = (0.5 * back).astype(BF16)
    sums_ref[0:1, :] += column_sum(d_branch.astype(F32))
    sums_ref[1:2, :] += column_sum(d_first * normed_one)
    sums_ref[2:3, :] += column_sum(top * normed_two)
    sums_ref[3:4, :] += column_sum(d_first)
    sums_ref[4:5, :] += column_sum(top)
    sums_ref[5:6, :] += column_sum(d_ffn.astype(F32))


def feed(pack, meta, x_own, cot_own, vectors, up_bias, att, own, pieces):
    row_count, model_width = x_own.shape
    feed_width = pack.feed_width
    att_width = att[0].shape[1]
    one = rows_of((ROW_BLOCK, model_width))
    wide = rows_of((ROW_BLOCK, feed_width))
    narrow = rows_of((ROW_BLOCK, att_width))
    turned = pl.BlockSpec((model_width, ROW_BLOCK), lambda i: (0, i))
    turned_shape = jax.ShapeDtypeStruct((model_width, row_count), BF16)

    def like(width, dtype=BF16):
        return jax.ShapeDtypeStruct((row_count, width), dtype)

    return pl.pallas_call(
        partial(feed_kernel, pack, len(att)),
        grid=(row_count // ROW_BLOCK,),
        in_specs=[IN_SMEM, one, one, whole(vectors.shape), whole(up_bias.shape)]
        + [narrow] * len(att)
        + [ANYWHERE] * (3 + len(pieces)),
        out_specs=[one, turned, one, turned, wide, wide, one, turned]
        + [narrow] * len(att)
        + [whole((8, model_width)), whole((1, feed_width))],
        out_shape=[
            like(model_width),
            turned_shape,
            like(model_width),
            turned_shape,
            like(feed_width),
            like(feed_width),
            like(model_width, F32),
            turned_shape,
        ]
        + [like(att_width)] * len(att)
        + [
            jax.ShapeDtypeStruct((8, model_width), F32),
            jax.ShapeDtypeStruct((1, feed_width), F32),
        ],
        scratch_shapes=[
            pltpu.VMEM((model_width, model_width), BF16),
            pltpu.VMEM((model_width, feed_width), BF16),
            pltpu.VMEM((feed_width, model_width), BF16),
            pltpu.VMEM((ROW_BLOCK, feed_width), F32),
            pltpu.SemaphoreType.DMA((3, 1 + pack.blocks * len(pieces))),
        ],
        name="feed",
        **params(
            2 * row_count * model_width * (2 * model_width + 4 * feed_width), 40_000_000
        ),
    )(meta, x_own, cot_own, vectors, up_bias, *att, *own, *pieces)


def weight_grads_kernel(
    pack, table, d_ffn_ref, hidden_ref, first_ref, d_pre_ref, att_ref, d_branch_ref, out_ref
):
    step = pl.program_id(0)
    half, member = table[0], table[1]

    @pl.when(step == 0)
    def _():
        spare = pack.rows - pack.used
        if spare:
            for shard in range(pack.shards):
                out_ref[shard, pack.used :, :] = jnp.zeros((spare, pack.model_width), BF16)

    @pl.when(step < pack.shards)
    def _():
        grad = dot(d_ffn_ref[...], hidden_ref[...]).astype(BF16)
        for lane in range(0, pack.model_width, pack.feed_shard):
            first = lane // pack.feed_shard * pack.down_rows
            out_ref[step, : pack.down_rows, lane : lane + pack.feed_shard] = grad[
                first : first + pack.down_rows
            ]

    @pl.when(jnp.logical_and(step >= pack.shards, step < pack.shards + pack.blocks))
    def _():
        grad = dot(first_ref[...], d_pre_ref[...]).astype(BF16)
        start = pack.up_at + (step - pack.shards) * pack.row_shard
        start = pl.multiple_of(start, 16)
        for shard in range(pack.shards):
            out_ref[shard, pl.ds(start, pack.row_shard), :] = grad[
                shard * pack.row_shard : (shard + 1) * pack.row_shard
            ]

    @pl.when(step == pack.shards + pack.blocks)
    def _():
        for shard in range(pack.shards):
            start = pack.out_start(shard, member) + half * pack.out_rows
            start = pl.multiple_of(start, 16)
            out_ref[shard, pack.out_at : pack.out_at + pack.out_rows, :] = dot(
                att_ref[pl.ds(start, pack.out_rows), :], d_branch_ref[...]
            ).astype(BF16)


def weight_grads(pack, table, d_ffn, hidden, first_low, d_pre, att, d_branch, needs=()):
    model_width, row_count = d_ffn.shape
    shards, blocks = pack.shards, pack.blocks

    def hidden_at(step, table):
        return (0, jnp.minimum(step, shards - 1))

    def d_pre_at(step, table):
        return (0, table[0] * blocks + jnp.clip(step - shards, 0, blocks - 1))

    def all_of(shape):
        return pl.BlockSpec(shape, lambda step, table: (0,) * len(shape))

    shape = (shards, pack.rows, model_width)
    return pl.pallas_call(
        gated(partial(weight_grads_kernel, pack), 7, needs),
        grid_spec=pltpu.PrefetchScalarGridSpec(
            num_scalar_prefetch=1,
            grid=(shards + blocks + 1,),
            in_specs=[
                pl.BlockSpec((model_width // CORES, row_count), lambda step, table: (table[0], 0)),
                pl.BlockSpec((row_count, pack.feed_shard), hidden_at),
                all_of(first_low.shape),
                pl.BlockSpec((row_count, model_width), d_pre_at),
                all_of(att.shape),
                all_of(d_branch.shape),
            ]
            + [ANYWHERE] * len(needs),
            out_specs=all_of(shape),
        ),
        out_shape=jax.ShapeDtypeStruct(shape, BF16),
        name="weight_grads",
        **params(row_count * model_width * (2 * pack.feed_width + model_width), 20_000_000),
    )(table, d_ffn, hidden, first_low, d_pre, att, d_branch, *needs)


def qkv_grads_kernel(rounds, x_refs_then, *refs):
    refs = (x_refs_then,) + refs
    x_refs, grad_refs = refs[:rounds], refs[rounds : 2 * rounds]
    small_ref, out_ref = refs[2 * rounds :]
    shards, rows, _ = out_ref.shape
    row_shard = rows - small_ref.shape[1]
    total, sums = None, None
    for x_ref, grad_ref in zip(x_refs, grad_refs):
        grads = grad_ref[...]
        term = dot(x_ref[...], grads)
        down = column_sum(grads.astype(F32))
        total = term if total is None else total + term
        sums = down if sums is None else sums + down
    total = total.astype(BF16)
    row = lax.broadcasted_iota(jnp.int32, small_ref.shape[1:], 0)
    for shard in range(shards):
        out_ref[shard, :row_shard, :] = total[shard * row_shard : (shard + 1) * row_shard]
        last = jnp.where(row == BIAS_ROW, sums, small_ref[shard])
        out_ref[shard, row_shard:, :] = last.astype(BF16)


def qkv_grads(x_turned, grads, small, row_shard):
    rounds = len(grads)
    model_width, positions = x_turned[0].shape
    cols = grads[0].shape[1]
    shards, extra, _ = small.shape
    block = GRAD_LANES if cols % GRAD_LANES == 0 else cols
    return pl.pallas_call(
        partial(qkv_grads_kernel, rounds),
        grid=(cols // block,),
        in_specs=[whole((model_width, positions))] * rounds
        + [pl.BlockSpec((positions, block), lambda i: (0, i))] * rounds
        + [pl.BlockSpec((shards, extra, block), lambda i: (0, 0, i))],
        out_specs=pl.BlockSpec((shards, row_shard + extra, block), lambda i: (0, 0, i)),
        out_shape=jax.ShapeDtypeStruct((shards, row_shard + extra, cols), BF16),
        name="qkv_grads",
        **params(2 * rounds * positions * model_width * cols, 18_000_000),
    )(*x_turned, *grads, small)


def add_picked_kernel(count, first, table, *refs):
    in_refs, out_refs = refs[:count], refs[count:]
    if count == 2:
        total = in_refs[0][...] + in_refs[1][...]
    else:
        total = in_refs[0][...].astype(F32)
        for ref in in_refs[1:]:
            total = total + ref[...].astype(F32)
        total = total.astype(BF16)
    if len(out_refs) == 1:
        out_refs[0][...] = total
        return

    @pl.when(pl.program_id(0) < first)
    def _():
        out_refs[0][...] = total

    @pl.when(pl.program_id(0) >= first)
    def _():
        out_refs[1][...] = total


def add_picked(table, arrays, steps, first=None, needs=()):
    _, rows, cols = arrays[0].shape
    parts = 2 if rows % 32 == 0 else 1
    block = (1, rows // parts, cols)
    spec = [
        pl.BlockSpec(block, lambda s, p, t, k=k: (t[k * steps + s], p, 0))
        for k in range(len(arrays))
    ]
    if first is None:
        out_specs = [pl.BlockSpec(block, lambda s, p, t: (s, p, 0))]
        counts = [steps]
    else:
        out_specs = [
            pl.BlockSpec(
                block,
                lambda s, p, t: (
                    jnp.minimum(s, first - 1),
                    jnp.where(s < first, p, parts - 1),
                    0,
                ),
            ),
            pl.BlockSpec(
                block,
                lambda s, p, t: (jnp.maximum(s - first, 0), jnp.where(s < first, 0, p), 0),
            ),
        ]
        counts = [first, steps - first]
    return pl.pallas_call(
        gated(partial(add_picked_kernel, len(arrays), first), 1 + len(arrays), needs),
        grid_spec=pltpu.PrefetchScalarGridSpec(
            num_scalar_prefetch=1,
            grid=(steps, parts),
            in_specs=spec + [ANYWHERE] * len(needs),
            out_specs=out_specs,
        ),
        out_shape=[jax.ShapeDtypeStruct((n, rows, cols), BF16) for n in counts],
        name="add_picked",
        compiler_params=pltpu.CompilerParams(
            dimension_semantics=("arbitrary", "arbitrary"), vmem_limit_bytes=VMEM_BYTES
        ),
        cost_estimate=pl.CostEstimate(flops=0, bytes_accessed=rows * cols, transcendentals=0),
    )(table, *arrays, *needs)


def stack_kernel(count, *refs):
    for index in range(count):
        refs[count][index] = refs[index][...]


def stack_up(pieces, needs=()):
    vmem = pl.BlockSpec(memory_space=pltpu.VMEM)
    return pl.pallas_call(
        gated(partial(stack_kernel, len(pieces)), len(pieces), needs),
        in_specs=[vmem] * len(pieces) + [ANYWHERE] * len(needs),
        out_specs=vmem,
        out_shape=jax.ShapeDtypeStruct((len(pieces),) + pieces[0].shape, BF16),
        name="stack_up",
        compiler_params=pltpu.CompilerParams(vmem_limit_bytes=VMEM_BYTES),
        cost_estimate=pl.CostEstimate(flops=0, bytes_accessed=100_000, transcendentals=0),
    )(*pieces, *needs)


def unpack_kernel(pack, depth, meta, mine_ref, other_ref, down_ref, up_ref, out_ref, ordered):
    core, level = meta[2], meta[4]
    rows = pack.rows // depth
    for mask in range(depth):
        start = pl.multiple_of(lax.bitwise_xor(level, mask) * rows, 16)
        ordered[core, pl.ds(start, rows), :] = mine_ref[mask]
        ordered[1 - core, pl.ds(start, rows), :] = other_ref[mask]
    turned = []
    for half in range(CORES):
        for lane in range(0, pack.model_width, pack.feed_shard):
            turned.append(ordered[half, : pack.down_rows, lane : lane + pack.feed_shard])
    down_ref[...] = jnp.transpose(jnp.concatenate(turned, axis=0)).astype(F32)
    for half in range(CORES):
        for block in range(pack.blocks):
            lane = (half * pack.blocks + block) * pack.model_width
            start = pack.up_at + block * pack.row_shard
            up_ref[:, lane : lane + pack.model_width] = ordered[
                half, start : start + pack.row_shard, :
            ].astype(F32)
        out_ref[half * pack.out_rows : (half + 1) * pack.out_rows, :] = ordered[
            half, pack.out_at : pack.out_at + pack.out_rows, :
        ].astype(F32)


def unpack(pack, depth, meta, mine, other):
    vmem = pl.BlockSpec(memory_space=pltpu.VMEM)
    return pl.pallas_call(
        partial(unpack_kernel, pack, depth),
        in_specs=[IN_SMEM, vmem, vmem],
        out_specs=[vmem] * 3,
        out_shape=[
            jax.ShapeDtypeStruct((pack.feed_shard, pack.model_width), F32),
            jax.ShapeDtypeStruct((pack.row_shard, pack.feed_width), F32),
            jax.ShapeDtypeStruct((pack.row_shard, pack.model_width), F32),
        ],
        scratch_shapes=[pltpu.VMEM((CORES, pack.rows, pack.model_width), BF16)],
        name="unpack",
        compiler_params=pltpu.CompilerParams(vmem_limit_bytes=VMEM_BYTES),
        cost_estimate=pl.CostEstimate(flops=0, bytes_accessed=10_000_000, transcendentals=0),
    )(meta, mine, other)


def tie(*values):
    return lax.optimization_barrier(values)


def body(
    tokens,
    cotangent,
    perms,
    unit_kind,
    w_qkv,
    bias_qv,
    w_out,
    bias_out,
    ln_gain,
    ln_bias,
    w_up,
    bias_up,
    w_down,
    bias_down,
):
    shards = lax.axis_size("fsdp")
    groups = lax.axis_size("dp")
    here = lax.axis_index("fsdp")
    dp_index = lax.axis_index("dp")
    core = dp_index % CORES
    level = dp_index // CORES
    depth = groups // CORES
    units, rounds, unit_len = perms.shape
    per_device = unit_len // shards
    model_width = tokens.shape[1]
    feed_width = w_up.shape[1]
    row_shard = model_width // shards
    members = shards // units
    member_rows = unit_len // members
    head_cols = model_width // members
    padded = -(-head_cols // CLUSTER_ROWS) * CLUSTER_ROWS
    spot = here * CORES + core
    home_core = spot // shards
    unit = (spot // members) % units
    member = spot % members
    pack = Pack(model_width, feed_width, shards, units, depth)
    bits = [1 << k for k in range(shards.bit_length() - 1)]
    bit_orders = (bits, bits[::-1])

    def plane_pairs(target):
        pairs = []
        for z in range(depth):
            for f_index in range(shards):
                for c_index in range(CORES):
                    f_new, c_new = target(f_index, c_index)
                    pairs.append(
                        (
                            (z * CORES + c_index) * shards + f_index,
                            (z * CORES + c_new) * shards + f_new,
                        )
                    )
        return pairs

    def send(value, pairs):
        return lax.ppermute(value, ("dp", "fsdp"), pairs)

    def cross(value, mask):
        return send(value, plane_pairs(lambda f, c: divmod((f * CORES + c) ^ mask, CORES)))

    def trade(value, stage):
        return send(value, plane_pairs(lambda f, c: (f ^ bit_orders[c][stage], c)))

    def trade_mask(index, which):
        mask = 0
        for stage in range(len(bits)):
            if index >> stage & 1:
                mask ^= bit_orders[which][stage]
        return mask

    def climb(value, mask):
        plane = CORES * shards
        pairs = []
        for z in range(depth):
            for rest in range(plane):
                pairs.append((z * plane + rest, (z ^ mask) * plane + rest))
        return send(value, pairs)

    def outward(step):
        def target(f, c):
            place_now = (c * units + (f % units + step) % units) * members + f // units
            return divmod(place_now, CORES)

        return plane_pairs(target)

    def homeward(step):
        return [(b, a) for a, b in outward(step)]

    def bring_start(value):
        blocks = value.reshape(units, per_device, model_width)
        return [
            lax.dynamic_index_in_dim(blocks, (here % units + step) % units, axis=0, keepdims=False)
            for step in range(units)
        ]

    def bring(chosen):
        return jnp.concatenate(
            [send(chosen[step], outward(step)) for step in range(units)], axis=0
        )

    def send_home(value):
        blocks = value.reshape(units, per_device, model_width)
        return [send(blocks[step], homeward(step)) for step in range(units)]

    def in_order(landed, dtype):
        if units == 2:
            swap = here % units == 1
            wanted = [
                jnp.where(swap, landed[1], landed[0]),
                jnp.where(swap, landed[0], landed[1]),
            ]
        else:
            stacked = jnp.stack(landed)
            wanted = [
                lax.dynamic_index_in_dim(stacked, (index - here % units) % units, 0, keepdims=False)
                for index in range(units)
            ]
        return jnp.concatenate(wanted, axis=0).astype(dtype)

    x_chosen = bring_start(tokens)
    x_own = bring(x_chosen)
    small = jnp.concatenate(
        [
            bias_qv.reshape(-1),
            bias_out,
            ln_gain.reshape(-1),
            ln_bias.reshape(-1),
            bias_up,
            bias_down,
        ]
    )
    small_rows = -(-small.shape[0] // (3 * padded))
    small_block = jnp.pad(
        jnp.pad(small, (0, small_rows * 3 * padded - small.shape[0])).reshape(
            small_rows, 3 * padded
        ),
        ((0, 16 - small_rows), (0, 0)),
    )
    def columns_for(offset):
        start = lax.bitwise_xor(member, offset) * head_cols
        blocks = [
            jnp.pad(
                lax.dynamic_slice(
                    w_qkv, (0, kind * model_width + start), (row_shard, head_cols)
                ),
                ((0, 0), (0, padded - head_cols)),
            )
            for kind in range(3)
        ]
        return jnp.concatenate([jnp.concatenate(blocks, axis=1), small_block], axis=0)

    offsets = [(CORES * m) % members for m in range(shards)]
    kinds = sorted(set(offsets))
    *tied, x_own = tie(*[columns_for(offset) for offset in kinds], x_own)
    piece_kinds = dict(zip(kinds, tied))
    x_pieces = [x_own] + [cross(x_own, mask) for mask in range(1, members)]
    qkv_pieces = [piece_kinds[0]] + [
        cross(piece_kinds[offsets[m]], CORES * m) for m in range(1, shards)
    ]
    order_pack = jnp.concatenate(
        [perms.reshape(-1), jnp.broadcast_to(unit_kind[:, None], (units, 128)).reshape(-1)]
    )
    order_other = cross(order_pack, 1)
    order_pack = jnp.where(home_core == core, order_pack, order_other)
    order_count = units * rounds * unit_len
    unit_perm = lax.dynamic_index_in_dim(
        order_pack[:order_count].reshape(units, rounds * unit_len), unit, 0, keepdims=False
    )
    kind_now = lax.dynamic_index_in_dim(
        order_pack[order_count:].reshape(units, 128), unit, 0, keepdims=False
    )[0]
    owner = unit_perm // per_device
    order = (
        lax.bitwise_xor(owner // units, member) * units + (unit - owner % units) % units
    ) * per_device + unit_perm % per_device
    order = order.reshape(rounds, unit_len)
    order = jnp.where(core == 0, order, order[::-1])
    order_row = order.reshape(1, rounds * unit_len)
    order = order.reshape(-1, CLUSTER_ROWS)
    x_here = arrange(order, x_pieces, unit_len, 0)
    x_now = [x_here, cross(x_here, 1)]
    own_masks = [
        jnp.where(core == 0, trade_mask(i, 0), trade_mask(i, 1)) for i in range(1, shards)
    ]
    other_masks = [
        jnp.where(core == 0, trade_mask(i, 1), trade_mask(i, 0)) for i in range(1, shards)
    ]
    zero = jnp.int32(0)
    meta = jnp.stack(
        [kind_now, here, core, member, level, zero, zero, zero] + own_masks + other_masks
    ).astype(jnp.int32)

    def half_of(value, axis, length, at):
        return lax.dynamic_slice_in_dim(value, at * length, length, axis=axis)

    packed = jnp.concatenate(
        [half_of(w_down, 0, pack.down_rows, core)]
        + [
            half_of(w_up, 1, model_width, core * pack.blocks + block)
            for block in range(pack.blocks)
        ]
        + [half_of(w_out, 0, pack.out_rows, core)],
        axis=0,
    )
    smalls = jnp.stack(
        [
            piece[row_shard : row_shard + small_rows].reshape(-1)[: small.shape[0]]
            for piece in qkv_pieces
        ]
    )
    smalls = jnp.take(smalls, lax.bitwise_xor(here, jnp.arange(shards)), axis=0).astype(F32)

    def vectors_at(start, count, length):
        part = smalls[:, start * row_shard : start * row_shard + count * length]
        return (
            part.reshape(shards, count, length).transpose(1, 0, 2).reshape(count, shards * length)
        )

    my_bias = lax.dynamic_index_in_dim(
        vectors_at(0, 2, row_shard).reshape(2, members, head_cols), member, 1, keepdims=False
    )
    my_bias = jnp.pad(my_bias, ((0, 0), (0, padded - head_cols)))
    my_bias = jnp.stack([my_bias[0], jnp.zeros_like(my_bias[0]), my_bias[1]]).reshape(1, -1)
    up_bias = vectors_at(7, 1, feed_width // shards)
    down_bias = smalls[:, small.shape[0] - row_shard :].reshape(1, model_width)
    vectors = jnp.concatenate(
        [vectors_at(2, 5, row_shard), down_bias, jnp.zeros((2, model_width), F32)], axis=0
    )

    order_rows = unit_len // CLUSTER_ROWS
    arranged, probs, mixtures, x_turned = [], [], [], []
    *tied, packed, x_now[0] = tie(*qkv_pieces[1:], packed, x_now[0])
    qkv_pieces = qkv_pieces[:1] + tied
    weight_pieces = {0: packed}
    for stage in range(len(bits)):
        weight_pieces[1 << stage] = trade(packed, stage)
    for index in range(rounds):
        results = attend(meta, x_now[index], my_bias, qkv_pieces, row_shard, mixtures[-1:])
        for kept, result in zip((arranged, probs, mixtures, x_turned), results):
            kept.append(result)
    first_ones = [1 << stage for stage in range(len(bits))]
    *tied, cot_now, mixtures[0] = tie(
        *[weight_pieces[index] for index in first_ones], cotangent, mixtures[0]
    )
    weight_pieces.update(zip(first_ones, tied))
    for stage in range(1, len(bits)):
        for index in range(1, 1 << stage):
            weight_pieces[index | 1 << stage] = trade(weight_pieces[index], stage)
    cot_own = bring(bring_start(cot_now))
    last_ones = [index for index in range(1, shards) if index not in first_ones]
    *tied, mixtures[1] = tie(*[weight_pieces[index] for index in last_ones], mixtures[1])
    weight_pieces.update(zip(last_ones, tied))
    att_there = []
    for mask in range(1, members):
        there = place(order_row, mixtures, mask * member_rows, member_rows, 0.5)
        att_there.append(cross(there[:, :head_cols], mask))
    att_here = place(order_row, mixtures, 0, member_rows, 0.5)
    att_raw = [att_here[:, :head_cols]] + att_there
    if head_cols % CLUSTER_ROWS:
        att_raw = [jnp.concatenate(att_raw, axis=1)]

    direct = [weight_pieces[index] for index in range(1, shards)]
    swapped = [cross(piece, 1) for piece in direct]
    block_out, first_low, d_branch, d_ffn, hidden, d_pre, d_lower, att_turned, *rest = feed(
        pack,
        meta,
        x_own,
        cot_own,
        vectors,
        up_bias,
        att_raw,
        [w_out, w_up, w_down],
        direct + swapped,
    )
    d_att, (row_sums, up_sums) = rest[: len(att_raw)], rest[len(att_raw) :]
    if head_cols % CLUSTER_ROWS:
        d_att = [d_att[0][:, mask * head_cols : (mask + 1) * head_cols] for mask in range(members)]
    d_att = [d_att[0]] + [cross(d_att[mask], mask) for mask in range(1, members)]
    d_att = [jnp.pad(piece, ((0, 0), (0, padded - head_cols))) for piece in d_att]

    def grads_of(half, *needed):
        table = jnp.stack([half, member]).astype(jnp.int32)
        return weight_grads(
            pack, table, d_ffn, hidden, first_low, d_pre, att_turned, d_branch, needed
        )

    theirs = grads_of(1 - core)
    output_landed = send_home(block_out)
    mine = grads_of(core, theirs)
    theirs = cross(theirs, 1)
    sending = [index for index in range(shards) if index & 1]
    keeping = [index for index in range(shards) if not index & 1]
    slots = jnp.stack(
        [
            lax.bitwise_xor(here, jnp.where(core == 0, trade_mask(i, 0), trade_mask(i, 1)))
            for i in sending + keeping
        ]
    )
    going, kept = add_picked(
        jnp.concatenate([slots, slots]).astype(jnp.int32),
        [mine, theirs],
        shards,
        len(sending),
        output_landed,
    )

    def merge(kept, landed, *needs):
        count = kept.shape[0]
        if count == 1:
            table = jnp.zeros((2,), jnp.int32)
            return None, add_picked(table, [kept, landed], 1, None, needs)[0]
        order_now = [i for i in range(count) if i & 1] + [i for i in range(count) if not i & 1]
        table = jnp.array(order_now * 2, jnp.int32)
        return add_picked(table, [kept, landed], count, count // 2, needs)

    grads, d_x = [None] * rounds, [None] * rounds
    needs = [going]
    for turn, index in enumerate(reversed(range(rounds))):
        results = attend_back(
            meta,
            order,
            arranged[index],
            probs[index],
            d_att,
            qkv_pieces,
            row_shard,
            index * order_rows,
            needs,
        )
        grads[index], d_x[index] = results
        if turn < len(bits):
            going, kept = merge(kept, trade(going, turn), results[0])
            needs = [kept]
    for stage in range(rounds, len(bits)):
        going, kept = merge(kept, trade(going, stage))

    def level_pieces(block):
        return block.reshape((depth, block.shape[0] // depth) + block.shape[1:])

    def level_scatter(cut):
        return [
            climb(
                lax.dynamic_index_in_dim(cut, lax.bitwise_xor(level, mask), 0, keepdims=False), mask
            )
            for mask in range(1, depth)
        ]

    def level_gather(piece):
        return [piece] + [climb(piece, mask) for mask in range(1, depth)]

    def by_shard(value):
        count, length = value.shape
        return (
            value.reshape(count, shards, length // shards)
            .transpose(1, 0, 2)
            .reshape(shards, count * length // shards)
        )

    small_grad = jnp.concatenate(
        [by_shard(row_sums[:5]), by_shard(up_sums), by_shard(row_sums[5:6])], axis=1
    )
    small_length = small_grad.shape[1]
    small_lanes = 3 * head_cols
    small_grad = jnp.pad(small_grad, ((0, 0), (0, BIAS_ROW * small_lanes - small_length)))
    small_grad = jnp.pad(
        small_grad.reshape(shards, BIAS_ROW, small_lanes), ((0, 0), (0, 16 - BIAS_ROW), (0, 0))
    )
    extra_rows = 16
    x_last, kept, small_grad = tie(x_turned[0], kept, small_grad)
    if padded == head_cols:
        joined = qkv_grads([x_last, x_turned[1]], grads, small_grad, row_shard)
    else:
        qkv_grad = dot(x_last, grads[0]) + dot(x_turned[1], grads[1])
        qkv_grad = qkv_grad.reshape(shards, row_shard, 3, padded)[..., :head_cols]
        bias_sum = sum(jnp.sum(value.astype(F32), axis=0) for value in grads)
        bias_sum = bias_sum.reshape(3, padded)[:, :head_cols].reshape(small_lanes)
        small_grad = small_grad.at[:, BIAS_ROW].set(bias_sum[None])
        joined = jnp.concatenate(
            [qkv_grad.reshape(shards, row_shard, small_lanes), small_grad], axis=1
        ).astype(BF16)
    cut = level_pieces(kept[0])
    landed = level_scatter(cut)
    classes = max(1, members // CORES)
    d_x_parts = [d_x[0], cross(d_x[1], 1)]
    order_mine = order_row[:, :unit_len]
    d_there = [
        place(
            order_mine,
            d_x_parts,
            mask * member_rows,
            member_rows,
            added=True,
            needs=[joined],
        )
        for mask in range(1, members)
    ]
    early = []
    if classes == 1:
        slots_held = jnp.stack(
            [
                lax.bitwise_xor(here, jnp.where(core == 0, trade_mask(i, 0), trade_mask(i, 1)))
                for i in range(shards)
            ]
        )
        held = jnp.stack(
            [
                lax.dynamic_index_in_dim(joined, slots_held[i], 0, keepdims=False)
                for i in range(0, shards, 2)
            ]
        )
        leaving = jnp.stack(
            [
                lax.dynamic_index_in_dim(joined, slots_held[i], 0, keepdims=False)
                for i in range(1, shards, 2)
            ]
        )
        for stage in range(len(bits)):
            gate = d_there if stage == 0 else []
            leaving, held = merge(held, trade(leaving, stage), *gate)
            if stage == 0:
                early = [held]
        totals = [held[0]]
    else:
        totals = [None] * classes
        for m in range(shards):
            offset = offsets[m] // CORES
            piece = lax.dynamic_index_in_dim(joined, lax.bitwise_xor(here, m), 0, keepdims=False)
            piece = (piece if m == 0 else cross(piece, CORES * m)).astype(F32)
            totals[offset] = piece if totals[offset] is None else totals[offset] + piece

    d_inputs = place(
        order_mine,
        d_x_parts,
        0,
        member_rows,
        1.0,
        F32,
        d_lower,
        added=True,
        needs=early + d_there,
    )

    for mask, there in enumerate(d_there, 1):
        d_inputs = d_inputs + cross(there, mask).astype(F32)
    d_inputs = d_inputs.astype(BF16)
    if depth > 1:
        picks = jnp.concatenate([level[None], jnp.zeros((depth - 1,), level.dtype)])
        (kept,) = add_picked(
            picks.astype(jnp.int32),
            [cut] + [piece[None] for piece in landed],
            1,
            None,
            [d_inputs],
        )
    gathered = level_gather(kept[0]) if depth > 1 else [cut[0]]
    d_inputs = in_order(send_home(d_inputs), F32)
    output = in_order(output_landed, BF16)
    totals = jnp.concatenate(totals, axis=0).astype(BF16)
    rows_each = row_shard + extra_rows
    mask = 1
    while mask < depth:
        totals = (totals.astype(F32) + climb(totals, mask).astype(F32)).astype(BF16)
        mask *= 2
    stacked = stack_up(gathered, [totals])
    grad_down, grad_up, grad_out = unpack(pack, depth, meta, stacked, cross(stacked, 1))
    landed = jnp.stack([totals, cross(totals, 1)], axis=0).reshape(
        CORES, classes, rows_each, 3 * head_cols
    )
    smalls_out = jnp.sum(
        landed[:, :, row_shard : row_shard + BIAS_ROW].astype(F32), axis=(0, 1)
    ).reshape(-1)[:small_length]
    landed = (
        landed.transpose(1, 0, 2, 3)
        .reshape(members, rows_each, 3, head_cols)[:, : row_shard + BIAS_ROW + 1]
    )
    if members == 2:
        swap = member == 1
        landed = jnp.stack(
            [
                jnp.where(swap, landed[1], landed[0]),
                jnp.where(swap, landed[0], landed[1]),
            ]
        )
    else:
        landed = jnp.take(landed, lax.bitwise_xor(member, jnp.arange(members)), axis=0)
    grad_qkv = landed[:, :row_shard].transpose(1, 2, 0, 3)
    grad_qkv = grad_qkv.reshape(row_shard, 3 * model_width).astype(F32)
    bias_out_row = landed[:, row_shard + BIAS_ROW].astype(F32).transpose(1, 0, 2)
    bias_out_row = lax.dynamic_slice(
        bias_out_row.reshape(3, model_width), (0, here * row_shard), (3, row_shard)
    )

    feed_shard = feed_width // shards
    spots = [0, row_shard, 3 * row_shard, 5 * row_shard]
    return (
        output,
        d_inputs,
        grad_qkv,
        bias_out_row[::2],
        grad_out,
        smalls_out[spots[0] : spots[1]],
        smalls_out[spots[1] : spots[2]].reshape(2, row_shard),
        smalls_out[spots[2] : spots[3]].reshape(2, row_shard),
        grad_up,
        smalls_out[spots[3] : spots[3] + feed_shard],
        grad_down,
        smalls_out[spots[3] + feed_shard :],
    )


def solution(mesh):
    placed = (
        P(("dp", "fsdp"), None),
        P(("dp", "fsdp"), None),
        P("dp", None, None),
        P("dp"),
        P("fsdp", None),
        P(None, "fsdp"),
        P("fsdp", None),
        P("fsdp"),
        P(None, "fsdp"),
        P(None, "fsdp"),
        P("fsdp", None),
        P("fsdp"),
        P("fsdp", None),
        P("fsdp"),
    )
    return jax.shard_map(
        body,
        mesh=mesh,
        in_specs=placed,
        out_specs=(
            P(("dp", "fsdp"), None),
            P(("dp", "fsdp"), None),
            P("fsdp", None),
            P(None, "fsdp"),
            P("fsdp", None),
            P("fsdp"),
            P(None, "fsdp"),
            P(None, "fsdp"),
            P("fsdp", None),
            P("fsdp"),
            P("fsdp", None),
            P("fsdp"),
        ),
        check_vma=False,
    )
```

```python
from functools import partial

import jax
import jax.numpy as jnp
from jax import lax
from jax.experimental import pallas as pl
from jax.experimental.pallas import tpu as pltpu
from jax.sharding import PartitionSpec as P

HEAD_DIM = 64
CORES = 2
NEG_FILL = -1000000000.0
EPSILON = 1e-05
SCALE = HEAD_DIM ** (-0.5)
BIAS_ROW = 2
GRAD_LANES = 384
CLUSTER_ROWS = 128
HALF_ROWS = 64
POS_BLOCK = 512
TOKEN_BLOCK = 512
ROW_BLOCK = 256
FF_BLOCK = 512
MIB = 1024 * 1024
NT = (((1,), (1,)), ((), ()))
TN = (((0,), (0,)), ((), ()))
F32 = jnp.float32
BF16 = jnp.bfloat16
ANYWHERE = pl.BlockSpec(memory_space=pl.ANY)
IN_SMEM = pl.BlockSpec(memory_space=pltpu.SMEM)


def whole(shape):
    return pl.BlockSpec(shape, lambda i: (0,) * len(shape))


def rows_of(shape):
    return pl.BlockSpec(shape, lambda i: (i,) + (0,) * (len(shape) - 1))


def dot(a, b, dims=(((1,), (0,)), ((), ()))):
    return lax.dot_general(a, b, dims, preferred_element_type=F32)


def params(mib, flops=0, moved=0, share=16):
    return dict(
        compiler_params=pltpu.CompilerParams(
            dimension_semantics=("arbitrary",),
            vmem_limit_bytes=mib * MIB,
        ),
        cost_estimate=pl.CostEstimate(
            flops=flops // share, bytes_accessed=moved // share, transcendentals=0
        ),
    )


def gated(kernel, used, needs):
    if not needs:
        return kernel

    def run(*refs):
        return kernel(*refs[:used], *refs[used + len(needs) :])

    return run


def lane_masks():
    lane = lax.broadcasted_iota(jnp.int32, (CLUSTER_ROWS, CLUSTER_ROWS), 1)
    low = (lane < HEAD_DIM).astype(F32)
    return low.astype(BF16), (1.0 - low).astype(BF16), lane < HEAD_DIM


def both_heads(rows_now, low, high):
    return jnp.concatenate([rows_now * low, rows_now * high], axis=0)


def equal_ones(left, right):
    return jnp.where(left == right, jnp.ones((), BF16), jnp.zeros((), BF16))


def pick_rows(order_ref, first_row, unit_len):
    parts = []
    lane = lax.broadcasted_iota(jnp.int16, (CLUSTER_ROWS, CLUSTER_ROWS), 1)
    for part in range(POS_BLOCK // CLUSTER_ROWS):
        row = order_ref[pl.ds(first_row + part, 1), :]
        column = jnp.transpose(jnp.broadcast_to(row, (CLUSTER_ROWS, CLUSTER_ROWS)))
        column = column.astype(jnp.int16)
        pieces = [
            equal_ones(column, lane + jnp.int16(base)) for base in range(0, unit_len, CLUSTER_ROWS)
        ]
        parts.append(jnp.concatenate(pieces, axis=1))
    return jnp.concatenate(parts, axis=0)


def load_pieces(meta, x_refs, w_refs, x_all, w_all, sems, row_shard):
    member_rows = x_all.shape[0] // max(1, len(x_refs))
    copies = []
    for index, ref in enumerate(x_refs):
        copies.append(
            pltpu.make_async_copy(
                ref, x_all.at[pl.ds(index * member_rows, member_rows), :], sems.at[index]
            )
        )
    for index, ref in enumerate(w_refs):
        start = pl.multiple_of(lax.bitwise_xor(meta[1], index) * row_shard, 16)
        copies.append(
            pltpu.make_async_copy(
                ref.at[pl.ds(0, row_shard), :],
                w_all.at[pl.ds(start, row_shard), :],
                sems.at[len(x_refs) + index],
            )
        )
    for copy in copies:
        copy.start()
    for copy in copies:
        copy.wait()


def arrange_kernel(unit_len, first_row, order_ref, *refs):
    x_refs, out_ref = refs[:-1], refs[-1]
    step = pl.program_id(0)
    picks = pick_rows(order_ref, first_row + step * (POS_BLOCK // CLUSTER_ROWS), unit_len)
    rows = x_refs[0].shape[0]
    total = None
    for index, ref in enumerate(x_refs):
        term = dot(picks[:, index * rows : (index + 1) * rows], ref[...])
        total = term if total is None else total + term
    out_ref[...] = total.astype(BF16)


def arrange(order, x_pieces, position_count, first_row):
    member_rows, width = x_pieces[0].shape
    unit_len = member_rows * len(x_pieces)
    return pl.pallas_call(
        partial(arrange_kernel, unit_len, first_row),
        grid=(position_count // POS_BLOCK,),
        in_specs=[whole(order.shape)] + [whole(piece.shape) for piece in x_pieces],
        out_specs=rows_of((POS_BLOCK, width)),
        out_shape=jax.ShapeDtypeStruct((position_count, width), BF16),
        name="arrange",
        **params(20, 2 * position_count * unit_len * width, 6_000_000),
    )(order, *x_pieces)


def attend_kernel(sizes, meta, x_now_ref, bias_ref, *refs):
    shards, row_shard = sizes
    w_refs, refs = refs[:shards], refs[shards:]
    arranged_ref, probs_ref, mixture_ref, turned_ref, w_all, sems = refs
    width = w_all.shape[1] // 3
    step = pl.program_id(0)

    @pl.when(step == 0)
    def _():
        load_pieces(meta, [], w_refs, w_all, w_all, sems, row_shard)

    x_now = x_now_ref[...]
    turned_ref[...] = jnp.transpose(x_now)
    arranged = (dot(x_now, w_all[...]) + bias_ref[...]).astype(BF16)
    arranged_ref[...] = arranged
    low, high, lane_low = lane_masks()
    position = lax.broadcasted_iota(jnp.int32, (CLUSTER_ROWS, CLUSTER_ROWS), 0)
    other = lax.broadcasted_iota(jnp.int32, (CLUSTER_ROWS, CLUSTER_ROWS), 1)
    same_half = (position < HALF_ROWS) == (other < HALF_ROWS)
    allowed = jnp.logical_or(same_half, meta[0] == 1)
    pairs = width // CLUSTER_ROWS
    for part in range(POS_BLOCK // CLUSTER_ROWS):
        rows_now = slice(part * CLUSTER_ROWS, (part + 1) * CLUSTER_ROWS)
        for pair in range(pairs):
            base = pair * CLUSTER_ROWS
            queries = arranged[rows_now, base : base + CLUSTER_ROWS] * SCALE
            keys = arranged[rows_now, width + base : width + base + CLUSTER_ROWS]
            values = arranged[rows_now, 2 * width + base : 2 * width + base + CLUSTER_ROWS]
            scores = dot(both_heads(keys, low, high), queries, NT)
            halves = []
            for head in range(2):
                one = scores[head * CLUSTER_ROWS : (head + 1) * CLUSTER_ROWS]
                one = jnp.where(allowed, one, NEG_FILL)
                grown = jnp.exp(one - jnp.max(one, axis=0, keepdims=True))
                halves.append(grown * (1.0 / jnp.sum(grown, axis=0, keepdims=True)))
            probs = jnp.concatenate(halves, axis=0).astype(BF16)
            at = (part * pairs + pair) * 2 * CLUSTER_ROWS
            probs_ref[at : at + 2 * CLUSTER_ROWS, :] = probs
            mixture = dot(probs, both_heads(values, low, high), TN).astype(BF16)
            mixture_ref[rows_now, base : base + CLUSTER_ROWS] = mixture


def attend(meta, x_now, bias, w_pieces, row_shard, needs=()):
    shards = len(w_pieces)
    position_count, model_width = x_now.shape
    cols = w_pieces[0].shape[1]
    width = cols // 3
    pair_rows = 2 * width
    return pl.pallas_call(
        gated(partial(attend_kernel, (shards, row_shard)), 3 + shards, needs),
        grid=(position_count // POS_BLOCK,),
        in_specs=[IN_SMEM, rows_of((POS_BLOCK, model_width)), whole(bias.shape)]
        + [ANYWHERE] * (shards + len(needs)),
        out_specs=[
            rows_of((POS_BLOCK, cols)),
            rows_of((POS_BLOCK // CLUSTER_ROWS * pair_rows, CLUSTER_ROWS)),
            rows_of((POS_BLOCK, width)),
            pl.BlockSpec((model_width, POS_BLOCK), lambda i: (0, i)),
        ],
        out_shape=[
            jax.ShapeDtypeStruct((position_count, cols), BF16),
            jax.ShapeDtypeStruct((position_count // CLUSTER_ROWS * pair_rows, CLUSTER_ROWS), BF16),
            jax.ShapeDtypeStruct((position_count, width), BF16),
            jax.ShapeDtypeStruct((model_width, position_count), BF16),
        ],
        scratch_shapes=[
            pltpu.VMEM((model_width, cols), BF16),
            pltpu.SemaphoreType.DMA((shards,)),
        ],
        name="attend",
        **params(
            22, 8 * position_count * (model_width * cols + 4 * CLUSTER_ROWS * width), 18_000_000, 1
        ),
    )(meta, x_now, bias, *w_pieces, *needs)


def place_kernel(sizes, scale, has_base, order_row_ref, *refs):
    unit_len, first_token, added = sizes
    base_ref = refs[0] if has_base else None
    refs = refs[1 if has_base else 0 :]
    if added:
        first_ref, second_ref, out_ref, held = refs

        @pl.when(pl.program_id(0) == 0)
        def _():
            held[...] = (first_ref[...].astype(F32) + second_ref[...].astype(F32)).astype(BF16)

        source_refs = [held]
    else:
        source_refs, out_ref = refs[:-1], refs[-1]
    block_rows = out_ref.shape[0]
    first = jnp.full((1, 1), first_token + pl.program_id(0) * block_rows, jnp.int32)
    token = lax.broadcasted_iota(jnp.int16, (block_rows, unit_len), 0)
    total = None
    for index, ref in enumerate(source_refs):
        row = order_row_ref[:, index * unit_len : (index + 1) * unit_len] - first
        row = jnp.broadcast_to(row, (16, unit_len)).astype(jnp.int16)
        row = jnp.concatenate([row] * (block_rows // 16), axis=0)
        term = dot(equal_ones(row, token), ref[...])
        total = term if total is None else total + term
    if scale != 1.0:
        total = total * scale
    if has_base:
        total = total + base_ref[...]
    out_ref[...] = total.astype(out_ref.dtype)


def place(
    order_row,
    sources,
    first_token,
    row_count,
    scale=1.0,
    dtype=BF16,
    base=None,
    added=False,
    needs=(),
):
    unit_len, width = sources[0].shape
    block_rows = min(TOKEN_BLOCK, row_count)
    extra = [] if base is None else [base]
    return pl.pallas_call(
        gated(
            partial(place_kernel, (unit_len, first_token, added), scale, base is not None),
            1 + len(extra) + len(sources),
            needs,
        ),
        grid=(row_count // block_rows,),
        in_specs=[whole(order_row.shape)]
        + [rows_of((block_rows, width))] * len(extra)
        + [whole(source.shape) for source in sources]
        + [ANYWHERE] * len(needs),
        out_specs=rows_of((block_rows, width)),
        out_shape=jax.ShapeDtypeStruct((row_count, width), dtype),
        scratch_shapes=[pltpu.VMEM((unit_len, width), BF16)] if added else [],
        name="place",
        **params(
            32 if added else 20,
            16 * row_count * unit_len * width,
            10_000_000,
            1 if added else 16,
        ),
    )(order_row, *extra, *sources, *needs)


def attend_back_kernel(sizes, meta, order_ref, arranged_ref, probs_ref, *refs):
    members, shards, unit_len, row_shard, first_row, start = sizes
    g_refs, refs = refs[:members], refs[members:]
    w_refs, refs = refs[:shards], refs[shards:]
    grads_ref, d_x_ref, g_all, w_all, sems = refs
    width = w_all.shape[1] // 3
    step = pl.program_id(0)

    @pl.when(step == 0)
    def _():
        load_pieces(meta, g_refs, w_refs, g_all, w_all, sems, row_shard)

    at_row = first_row + (start + step) * (POS_BLOCK // CLUSTER_ROWS)
    picks = pick_rows(order_ref, at_row, unit_len)
    d_mixture = dot(picks, g_all[...]).astype(BF16)
    low, high, lane_low = lane_masks()
    pairs = width // CLUSTER_ROWS
    for part in range(POS_BLOCK // CLUSTER_ROWS):
        rows_now = slice(part * CLUSTER_ROWS, (part + 1) * CLUSTER_ROWS)
        for pair in range(pairs):
            base = pair * CLUSTER_ROWS
            q_lanes = slice(base, base + CLUSTER_ROWS)
            k_lanes = slice(width + base, width + base + CLUSTER_ROWS)
            v_lanes = slice(2 * width + base, 2 * width + base + CLUSTER_ROWS)
            queries = arranged_ref[rows_now, q_lanes] * SCALE
            keys = arranged_ref[rows_now, k_lanes] * SCALE
            values = arranged_ref[rows_now, v_lanes]
            at = (part * pairs + pair) * 2 * CLUSTER_ROWS
            probs = probs_ref[at : at + 2 * CLUSTER_ROWS, :]
            d_now = d_mixture[rows_now, base : base + CLUSTER_ROWS]
            d_probs = dot(both_heads(values, low, high), d_now, NT)
            pieces = []
            for head in range(2):
                rows = slice(head * CLUSTER_ROWS, (head + 1) * CLUSTER_ROWS)
                weight = probs[rows].astype(F32)
                d_one = d_probs[rows]
                inner = jnp.sum(weight * d_one, axis=0, keepdims=True)
                pieces.append(weight * (d_one - inner))
            d_scores = jnp.concatenate(pieces, axis=0).astype(BF16)
            d_query = dot(d_scores, both_heads(keys, low, high), TN)
            d_keys = dot(d_scores, queries)
            d_values = dot(probs, d_now)
            grads_ref[rows_now, q_lanes] = d_query.astype(BF16)
            grads_ref[rows_now, k_lanes] = jnp.where(
                lane_low, d_keys[:CLUSTER_ROWS], d_keys[CLUSTER_ROWS:]
            ).astype(BF16)
            grads_ref[rows_now, v_lanes] = jnp.where(
                lane_low, d_values[:CLUSTER_ROWS], d_values[CLUSTER_ROWS:]
            ).astype(BF16)
    grads = grads_ref[...]
    d_x_ref[...] = dot(grads, w_all[...], NT).astype(BF16)


def attend_back(
    meta, order, arranged, probs, g_pieces, w_pieces, row_shard, first_row, needs, span, into
):
    members, shards = len(g_pieces), len(w_pieces)
    member_rows, width = g_pieces[0].shape
    unit_len = members * member_rows
    position_count, cols = arranged.shape
    model_width = row_shard * shards
    start, stop = span
    pair_rows = POS_BLOCK // CLUSTER_ROWS * 2 * width
    used = 4 + members + shards

    def block(shape):
        return pl.BlockSpec(shape, lambda i: (start + i, 0))

    return pl.pallas_call(
        gated(
            partial(attend_back_kernel, (members, shards, unit_len, row_shard, first_row, start)),
            used,
            list(into) + list(needs),
        ),
        grid=(stop - start,),
        in_specs=[
            IN_SMEM,
            whole(order.shape),
            block((POS_BLOCK, cols)),
            block((pair_rows, CLUSTER_ROWS)),
        ]
        + [ANYWHERE] * (members + shards + len(into) + len(needs)),
        out_specs=[block((POS_BLOCK, cols)), block((POS_BLOCK, model_width))],
        out_shape=[
            jax.ShapeDtypeStruct((position_count, cols), BF16),
            jax.ShapeDtypeStruct((position_count, model_width), BF16),
        ],
        input_output_aliases={used + index: index for index in range(len(into))},
        scratch_shapes=[
            pltpu.VMEM((unit_len, width), BF16),
            pltpu.VMEM((model_width, cols), BF16),
            pltpu.SemaphoreType.DMA((members + shards,)),
        ],
        name="attend_back",
        **params(26, 2 * position_count * (unit_len * width + model_width * cols), 20_000_000),
    )(meta, order, arranged, probs, *g_pieces, *w_pieces, *into, *needs)


def normalise(summed):
    average = jnp.mean(summed, axis=-1, keepdims=True)
    centred = summed - average
    spread = jnp.mean(centred * centred, axis=-1, keepdims=True)
    scale_inv = lax.rsqrt(spread + EPSILON)
    return centred * scale_inv, scale_inv


def normalise_back(grad_out, normed, scale_inv, gain_row):
    scaled = grad_out * gain_row
    return scale_inv * (
        scaled
        - jnp.mean(scaled, axis=-1, keepdims=True)
        - normed * jnp.mean(scaled * normed, axis=-1, keepdims=True)
    )


def column_sum(rows_now):
    return jnp.sum(rows_now, axis=0, keepdims=True)


def gelu_parts(value):
    below = 0.5 + 0.5 * lax.erf(value * 0.7071067811865476)
    bell = jnp.exp(value * value * -0.5) * 0.3989422804014327
    return value * below, below + value * bell


class Pack:
    def __init__(self, model_width, feed_width, shards, units, depth):
        self.model_width, self.feed_width, self.shards = model_width, feed_width, shards
        self.row_shard = model_width // shards
        self.feed_shard = feed_width // shards
        self.down_rows = self.feed_shard // CORES
        self.blocks = feed_width // CORES // model_width
        self.up_at = self.down_rows
        self.out_at = self.up_at + self.blocks * self.row_shard
        self.out_rows = self.row_shard // CORES
        self.used = self.out_at + self.out_rows
        unit = 16 * depth
        self.rows = -(-self.used // unit) * unit
        self.units = units
        self.group = units * self.row_shard

    def out_start(self, shard, member):
        return (
            lax.bitwise_xor(jnp.int32(shard) // self.units, member) * self.group
            + (shard % self.units) * self.row_shard
        )


def feed_kernel(pack, att_count, meta, x_ref, cot_ref, vec_ref, up_bias_ref, *refs):
    shards = pack.shards
    att_refs, refs = refs[:att_count], refs[att_count:]
    own_out, own_up, own_down = refs[:3]
    refs = refs[3:]
    pieces, refs = refs[: 2 * (shards - 1)], refs[2 * (shards - 1) :]
    out_ref, first_turned_ref, d_branch_ref, d_ffn_turned_ref, hidden_ref, d_pre_ref = refs[:6]
    d_h1_ref, att_turned_ref = refs[6:8]
    refs = refs[8:]
    d_att_refs, refs = refs[:att_count], refs[att_count:]
    sums_ref, up_sums_ref, w_out, w_up, w_down, slope, sems = refs
    step = pl.program_id(0)
    here, core, member = meta[1], meta[2], meta[3]
    feed_width = pack.feed_width

    def loads(kind):
        copies = []

        def add(source, target):
            copies.append(pltpu.make_async_copy(source, target, sems.at[kind, len(copies)]))

        if kind == 0:
            start = pl.multiple_of(pack.out_start(here, member), 16)
            add(own_out, w_out.at[pl.ds(start, pack.row_shard), :])
        elif kind == 1:
            start = pl.multiple_of(here * pack.row_shard, 16)
            add(own_up, w_up.at[pl.ds(start, pack.row_shard), :])
        else:
            start = pl.multiple_of(here * pack.feed_shard, 16)
            add(own_down, w_down.at[pl.ds(start, pack.feed_shard), :])
        for index, ref in enumerate(pieces):
            peer = lax.bitwise_xor(here, meta[8 + index])
            half = core if index < shards - 1 else 1 - core
            if kind == 0:
                start = pack.out_start(peer, member) + half * pack.out_rows
                start = pl.multiple_of(start, 16)
                add(
                    ref.at[pl.ds(pack.out_at, pack.out_rows), :],
                    w_out.at[pl.ds(start, pack.out_rows), :],
                )
            elif kind == 1:
                start = pl.multiple_of(peer * pack.row_shard, 16)
                for block in range(pack.blocks):
                    lane = pl.multiple_of(
                        (half * pack.blocks + block) * pack.model_width, CLUSTER_ROWS
                    )
                    add(
                        ref.at[pl.ds(pack.up_at + block * pack.row_shard, pack.row_shard), :],
                        w_up.at[pl.ds(start, pack.row_shard), pl.ds(lane, pack.model_width)],
                    )
            else:
                start = pl.multiple_of(peer * pack.feed_shard + half * pack.down_rows, 16)
                add(
                    ref.at[pl.ds(0, pack.down_rows), :],
                    w_down.at[pl.ds(start, pack.down_rows), :],
                )
        return copies

    @pl.when(step == 0)
    def _():
        for kind in range(3):
            for copy in loads(kind):
                copy.start()
        sums_ref[...] = jnp.zeros_like(sums_ref)
        up_sums_ref[...] = jnp.zeros_like(up_sums_ref)
        for copy in loads(0):
            copy.wait()

    bias_out, gain_one, gain_two = vec_ref[0:1, :], vec_ref[1:2, :], vec_ref[2:3, :]
    shift_one, shift_two, bias_down = vec_ref[3:4, :], vec_ref[4:5, :], vec_ref[5:6, :]
    att_width = att_refs[0].shape[1]
    summed = x_ref[...].astype(F32) + bias_out
    for index, ref in enumerate(att_refs):
        summed += dot(ref[...], w_out[index * att_width : (index + 1) * att_width, :])
    normed_one, inv_one = normalise(summed)
    first = normed_one * gain_one + shift_one
    first_low = first.astype(BF16)
    first_turned_ref[...] = jnp.transpose(first_low)
    for index, ref in enumerate(att_refs):
        att_turned_ref[index * att_width : (index + 1) * att_width, :] = jnp.transpose(ref[...])

    @pl.when(step == 0)
    def _():
        for kind in (1, 2):
            for copy in loads(kind):
                copy.wait()

    second = first + bias_down
    starts = list(range(0, feed_width, FF_BLOCK))

    def raised(base):
        lanes = slice(base, base + FF_BLOCK)
        return dot(first_low, w_up[:, lanes]) + up_bias_ref[:, lanes]

    pre = raised(starts[0])
    for index, base in enumerate(starts):
        lanes = slice(base, base + FF_BLOCK)
        pre_next = raised(starts[index + 1]) if index + 1 < len(starts) else None
        hidden, slope_now = gelu_parts(pre)
        hidden = hidden.astype(BF16)
        hidden_ref[:, lanes] = hidden
        slope[:, lanes] = slope_now
        second += dot(hidden, w_down[lanes, :])
        pre = pre_next
    normed_two, inv_two = normalise(second)
    out_ref[...] = (normed_two * gain_two + shift_two).astype(BF16)
    top = cot_ref[...].astype(F32)
    d_second = normalise_back(top, normed_two, inv_two, gain_two)
    d_ffn = d_second.astype(BF16)
    d_ffn_turned_ref[...] = jnp.transpose(d_ffn)
    d_first = d_second
    d_hidden = dot(d_ffn, w_down[0:FF_BLOCK, :], NT)
    for index, base in enumerate(starts):
        lanes = slice(base, base + FF_BLOCK)
        if index + 1 < len(starts):
            d_next = dot(d_ffn, w_down[starts[index + 1] : starts[index + 1] + FF_BLOCK, :], NT)
        d_pre = (d_hidden * slope[:, lanes]).astype(BF16)
        d_pre_ref[:, lanes] = d_pre
        up_sums_ref[:, lanes] += column_sum(d_pre.astype(F32))
        d_first += dot(d_pre, w_up[:, lanes], NT)
        d_hidden = d_next
    d_lower = normalise_back(d_first, normed_one, inv_one, gain_one)
    d_h1_ref[...] = d_lower
    d_branch = d_lower.astype(BF16)
    d_branch_ref[...] = d_branch
    for index, ref in enumerate(d_att_refs):
        back = dot(d_branch, w_out[index * att_width : (index + 1) * att_width, :], NT)
        ref[...] = (0.5 * back).astype(BF16)
    sums_ref[0:1, :] += column_sum(d_branch.astype(F32))
    sums_ref[1:2, :] += column_sum(d_first * normed_one)
    sums_ref[2:3, :] += column_sum(top * normed_two)
    sums_ref[3:4, :] += column_sum(d_first)
    sums_ref[4:5, :] += column_sum(top)
    sums_ref[5:6, :] += column_sum(d_ffn.astype(F32))


def feed(pack, meta, x_own, cot_own, vectors, up_bias, att, own, pieces):
    row_count, model_width = x_own.shape
    feed_width = pack.feed_width
    att_width = att[0].shape[1]
    one = rows_of((ROW_BLOCK, model_width))
    wide = rows_of((ROW_BLOCK, feed_width))
    narrow = rows_of((ROW_BLOCK, att_width))
    turned = pl.BlockSpec((model_width, ROW_BLOCK), lambda i: (0, i))
    turned_shape = jax.ShapeDtypeStruct((model_width, row_count), BF16)

    def like(width, dtype=BF16):
        return jax.ShapeDtypeStruct((row_count, width), dtype)

    return pl.pallas_call(
        partial(feed_kernel, pack, len(att)),
        grid=(row_count // ROW_BLOCK,),
        in_specs=[IN_SMEM, one, one, whole(vectors.shape), whole(up_bias.shape)]
        + [narrow] * len(att)
        + [ANYWHERE] * (3 + len(pieces)),
        out_specs=[one, turned, one, turned, wide, wide, one, turned]
        + [narrow] * len(att)
        + [whole((8, model_width)), whole((1, feed_width))],
        out_shape=[
            like(model_width),
            turned_shape,
            like(model_width),
            turned_shape,
            like(feed_width),
            like(feed_width),
            like(model_width, F32),
            turned_shape,
        ]
        + [like(att_width)] * len(att)
        + [
            jax.ShapeDtypeStruct((8, model_width), F32),
            jax.ShapeDtypeStruct((1, feed_width), F32),
        ],
        scratch_shapes=[
            pltpu.VMEM((model_width, model_width), BF16),
            pltpu.VMEM((model_width, feed_width), BF16),
            pltpu.VMEM((feed_width, model_width), BF16),
            pltpu.VMEM((ROW_BLOCK, feed_width), F32),
            pltpu.SemaphoreType.DMA((3, 1 + pack.blocks * len(pieces))),
        ],
        name="feed",
        **params(
            40, 2 * row_count * model_width * (2 * model_width + 4 * feed_width), 40_000_000
        ),
    )(meta, x_own, cot_own, vectors, up_bias, *att, *own, *pieces)


def weight_grads_kernel(
    pack, table, d_ffn_ref, hidden_ref, first_ref, d_pre_ref, att_ref, d_branch_ref, out_ref
):
    step = pl.program_id(0)
    half, member = table[0], table[1]

    @pl.when(step == 0)
    def _():
        spare = pack.rows - pack.used
        if spare:
            for shard in range(pack.shards):
                out_ref[shard, pack.used :, :] = jnp.zeros((spare, pack.model_width), BF16)

    @pl.when(step < pack.shards)
    def _():
        grad = dot(d_ffn_ref[...], hidden_ref[...]).astype(BF16)
        for lane in range(0, pack.model_width, pack.feed_shard):
            first = lane // pack.feed_shard * pack.down_rows
            out_ref[step, : pack.down_rows, lane : lane + pack.feed_shard] = grad[
                first : first + pack.down_rows
            ]

    @pl.when(jnp.logical_and(step >= pack.shards, step < pack.shards + pack.blocks))
    def _():
        grad = dot(first_ref[...], d_pre_ref[...]).astype(BF16)
        start = pack.up_at + (step - pack.shards) * pack.row_shard
        start = pl.multiple_of(start, 16)
        for shard in range(pack.shards):
            out_ref[shard, pl.ds(start, pack.row_shard), :] = grad[
                shard * pack.row_shard : (shard + 1) * pack.row_shard
            ]

    @pl.when(step == pack.shards + pack.blocks)
    def _():
        for shard in range(pack.shards):
            start = pack.out_start(shard, member) + half * pack.out_rows
            start = pl.multiple_of(start, 16)
            out_ref[shard, pack.out_at : pack.out_at + pack.out_rows, :] = dot(
                att_ref[pl.ds(start, pack.out_rows), :], d_branch_ref[...]
            ).astype(BF16)


def weight_grads(pack, table, d_ffn, hidden, first_low, d_pre, att, d_branch, needs=()):
    model_width, row_count = d_ffn.shape
    shards, blocks = pack.shards, pack.blocks

    def hidden_at(step, table):
        return (0, jnp.minimum(step, shards - 1))

    def d_pre_at(step, table):
        return (0, table[0] * blocks + jnp.clip(step - shards, 0, blocks - 1))

    def all_of(shape):
        return pl.BlockSpec(shape, lambda step, table: (0,) * len(shape))

    shape = (shards, pack.rows, model_width)
    return pl.pallas_call(
        gated(partial(weight_grads_kernel, pack), 7, needs),
        grid_spec=pltpu.PrefetchScalarGridSpec(
            num_scalar_prefetch=1,
            grid=(shards + blocks + 1,),
            in_specs=[
                pl.BlockSpec((model_width // CORES, row_count), lambda step, table: (table[0], 0)),
                pl.BlockSpec((row_count, pack.feed_shard), hidden_at),
                all_of(first_low.shape),
                pl.BlockSpec((row_count, model_width), d_pre_at),
                all_of(att.shape),
                all_of(d_branch.shape),
            ]
            + [ANYWHERE] * len(needs),
            out_specs=all_of(shape),
        ),
        out_shape=jax.ShapeDtypeStruct(shape, BF16),
        name="weight_grads",
        **params(36, row_count * model_width * (2 * pack.feed_width + model_width), 20_000_000),
    )(table, d_ffn, hidden, first_low, d_pre, att, d_branch, *needs)


def qkv_grads_kernel(rounds, x_refs_then, *refs):
    refs = (x_refs_then,) + refs
    x_refs, grad_refs = refs[:rounds], refs[rounds : 2 * rounds]
    small_ref, out_ref = refs[2 * rounds :]
    shards, rows, _ = out_ref.shape
    row_shard = rows - small_ref.shape[1]
    total, sums = None, None
    for x_ref, grad_ref in zip(x_refs, grad_refs):
        grads = grad_ref[...]
        term = dot(x_ref[...], grads)
        down = column_sum(grads.astype(F32))
        total = term if total is None else total + term
        sums = down if sums is None else sums + down
    total = total.astype(BF16)
    row = lax.broadcasted_iota(jnp.int32, small_ref.shape[1:], 0)
    for shard in range(shards):
        out_ref[shard, :row_shard, :] = total[shard * row_shard : (shard + 1) * row_shard]
        last = jnp.where(row == BIAS_ROW, sums, small_ref[shard])
        out_ref[shard, row_shard:, :] = last.astype(BF16)


def qkv_grads(x_turned, grads, small, row_shard):
    rounds = len(grads)
    model_width, positions = x_turned[0].shape
    cols = grads[0].shape[1]
    shards, extra, _ = small.shape
    block = GRAD_LANES if cols % GRAD_LANES == 0 else cols
    return pl.pallas_call(
        partial(qkv_grads_kernel, rounds),
        grid=(cols // block,),
        in_specs=[whole((model_width, positions))] * rounds
        + [pl.BlockSpec((positions, block), lambda i: (0, i))] * rounds
        + [pl.BlockSpec((shards, extra, block), lambda i: (0, 0, i))],
        out_specs=pl.BlockSpec((shards, row_shard + extra, block), lambda i: (0, 0, i)),
        out_shape=jax.ShapeDtypeStruct((shards, row_shard + extra, cols), BF16),
        name="qkv_grads",
        **params(28, 2 * rounds * positions * model_width * cols, 18_000_000),
    )(*x_turned, *grads, small)


def add_picked_kernel(count, first, table, *refs):
    in_refs, out_refs = refs[:count], refs[count:]
    if count == 2:
        total = in_refs[0][...] + in_refs[1][...]
    else:
        total = in_refs[0][...].astype(F32)
        for ref in in_refs[1:]:
            total = total + ref[...].astype(F32)
        total = total.astype(BF16)
    if len(out_refs) == 1:
        out_refs[0][...] = total
        return

    @pl.when(pl.program_id(0) < first)
    def _():
        out_refs[0][...] = total

    @pl.when(pl.program_id(0) >= first)
    def _():
        out_refs[1][...] = total


def add_picked(table, arrays, steps, first=None, needs=()):
    _, rows, cols = arrays[0].shape
    parts = 2 if rows % 32 == 0 else 1
    block = (1, rows // parts, cols)
    spec = [
        pl.BlockSpec(block, lambda s, p, t, k=k: (t[k * steps + s], p, 0))
        for k in range(len(arrays))
    ]
    if first is None:
        out_specs = [pl.BlockSpec(block, lambda s, p, t: (s, p, 0))]
        counts = [steps]
    else:
        out_specs = [
            pl.BlockSpec(
                block,
                lambda s, p, t: (
                    jnp.minimum(s, first - 1),
                    jnp.where(s < first, p, parts - 1),
                    0,
                ),
            ),
            pl.BlockSpec(
                block,
                lambda s, p, t: (jnp.maximum(s - first, 0), jnp.where(s < first, 0, p), 0),
            ),
        ]
        counts = [first, steps - first]
    return pl.pallas_call(
        gated(partial(add_picked_kernel, len(arrays), first), 1 + len(arrays), needs),
        grid_spec=pltpu.PrefetchScalarGridSpec(
            num_scalar_prefetch=1,
            grid=(steps, parts),
            in_specs=spec + [ANYWHERE] * len(needs),
            out_specs=out_specs,
        ),
        out_shape=[jax.ShapeDtypeStruct((n, rows, cols), BF16) for n in counts],
        name="add_picked",
        compiler_params=pltpu.CompilerParams(
            dimension_semantics=("arbitrary", "arbitrary"), vmem_limit_bytes=12 * MIB
        ),
        cost_estimate=pl.CostEstimate(flops=0, bytes_accessed=rows * cols, transcendentals=0),
    )(table, *arrays, *needs)


def stack_kernel(count, *refs):
    for index in range(count):
        refs[count][index] = refs[index][...]


def stack_up(pieces, needs=()):
    vmem = pl.BlockSpec(memory_space=pltpu.VMEM)
    return pl.pallas_call(
        gated(partial(stack_kernel, len(pieces)), len(pieces), needs),
        in_specs=[vmem] * len(pieces) + [ANYWHERE] * len(needs),
        out_specs=vmem,
        out_shape=jax.ShapeDtypeStruct((len(pieces),) + pieces[0].shape, BF16),
        name="stack_up",
        compiler_params=pltpu.CompilerParams(vmem_limit_bytes=24 * MIB),
        cost_estimate=pl.CostEstimate(flops=0, bytes_accessed=100_000, transcendentals=0),
    )(*pieces, *needs)


def unpack_kernel(pack, depth, meta, mine_ref, other_ref, down_ref, up_ref, out_ref, ordered):
    core, level = meta[2], meta[4]
    rows = pack.rows // depth
    for mask in range(depth):
        start = pl.multiple_of(lax.bitwise_xor(level, mask) * rows, 16)
        ordered[core, pl.ds(start, rows), :] = mine_ref[mask]
        ordered[1 - core, pl.ds(start, rows), :] = other_ref[mask]
    turned = []
    for half in range(CORES):
        for lane in range(0, pack.model_width, pack.feed_shard):
            turned.append(ordered[half, : pack.down_rows, lane : lane + pack.feed_shard])
    down_ref[...] = jnp.transpose(jnp.concatenate(turned, axis=0)).astype(F32)
    for half in range(CORES):
        for block in range(pack.blocks):
            lane = (half * pack.blocks + block) * pack.model_width
            start = pack.up_at + block * pack.row_shard
            up_ref[:, lane : lane + pack.model_width] = ordered[
                half, start : start + pack.row_shard, :
            ].astype(F32)
        out_ref[half * pack.out_rows : (half + 1) * pack.out_rows, :] = ordered[
            half, pack.out_at : pack.out_at + pack.out_rows, :
        ].astype(F32)


def unpack(pack, depth, meta, mine, other):
    vmem = pl.BlockSpec(memory_space=pltpu.VMEM)
    return pl.pallas_call(
        partial(unpack_kernel, pack, depth),
        in_specs=[IN_SMEM, vmem, vmem],
        out_specs=[vmem] * 3,
        out_shape=[
            jax.ShapeDtypeStruct((pack.feed_shard, pack.model_width), F32),
            jax.ShapeDtypeStruct((pack.row_shard, pack.feed_width), F32),
            jax.ShapeDtypeStruct((pack.row_shard, pack.model_width), F32),
        ],
        scratch_shapes=[pltpu.VMEM((CORES, pack.rows, pack.model_width), BF16)],
        name="unpack",
        compiler_params=pltpu.CompilerParams(vmem_limit_bytes=24 * MIB),
        cost_estimate=pl.CostEstimate(flops=0, bytes_accessed=10_000_000, transcendentals=0),
    )(meta, mine, other)


def unpack_qkv_kernel(meta, mine_ref, other_ref, grad_ref, bias_ref, small_ref):
    member = meta[3]
    row_shard, width = grad_ref.shape[0], grad_ref.shape[1] // 3
    part = mine_ref.shape[1] // 3
    for ref, at in ((mine_ref, member), (other_ref, 1 - member)):
        for kind in range(3):
            lane = pl.multiple_of(kind * width + at * part, CLUSTER_ROWS)
            from_lanes = slice(kind * part, (kind + 1) * part)
            grad_ref[:, pl.ds(lane, part)] = ref[:row_shard, from_lanes].astype(F32)
            lane = pl.multiple_of(at * part, CLUSTER_ROWS)
            bias_ref[kind : kind + 1, pl.ds(lane, part)] = ref[row_shard:, from_lanes].astype(F32)[
                BIAS_ROW : BIAS_ROW + 1
            ]
    small_ref[...] = (mine_ref[row_shard:, :].astype(F32) + other_ref[row_shard:, :].astype(F32))[
        :BIAS_ROW
    ]


def unpack_qkv(meta, mine, other, row_shard):
    cols = mine.shape[1]
    vmem = pl.BlockSpec(memory_space=pltpu.VMEM)
    return pl.pallas_call(
        unpack_qkv_kernel,
        in_specs=[IN_SMEM, vmem, vmem],
        out_specs=[vmem] * 3,
        out_shape=[
            jax.ShapeDtypeStruct((row_shard, CORES * cols), F32),
            jax.ShapeDtypeStruct((3, CORES * cols // 3), F32),
            jax.ShapeDtypeStruct((BIAS_ROW, cols), F32),
        ],
        name="unpack_qkv",
        compiler_params=pltpu.CompilerParams(vmem_limit_bytes=16 * MIB),
        cost_estimate=pl.CostEstimate(flops=0, bytes_accessed=200_000, transcendentals=0),
    )(meta, mine, other)


def tie(*values):
    return lax.optimization_barrier(values)


def body(
    tokens,
    cotangent,
    perms,
    unit_kind,
    w_qkv,
    bias_qv,
    w_out,
    bias_out,
    ln_gain,
    ln_bias,
    w_up,
    bias_up,
    w_down,
    bias_down,
):
    shards = lax.axis_size("fsdp")
    groups = lax.axis_size("dp")
    here = lax.axis_index("fsdp")
    dp_index = lax.axis_index("dp")
    core = dp_index % CORES
    level = dp_index // CORES
    depth = groups // CORES
    units, rounds, unit_len = perms.shape
    per_device = unit_len // shards
    model_width = tokens.shape[1]
    feed_width = w_up.shape[1]
    row_shard = model_width // shards
    members = shards // units
    member_rows = unit_len // members
    head_cols = model_width // members
    padded = -(-head_cols // CLUSTER_ROWS) * CLUSTER_ROWS
    spot = here * CORES + core
    home_core = spot // shards
    unit = (spot // members) % units
    member = spot % members
    pack = Pack(model_width, feed_width, shards, units, depth)
    bits = [1 << k for k in range(shards.bit_length() - 1)]
    bit_orders = (bits, bits[::-1])

    def plane_pairs(target):
        pairs = []
        for z in range(depth):
            for f_index in range(shards):
                for c_index in range(CORES):
                    f_new, c_new = target(f_index, c_index)
                    pairs.append(
                        (
                            (z * CORES + c_index) * shards + f_index,
                            (z * CORES + c_new) * shards + f_new,
                        )
                    )
        return pairs

    def send(value, pairs):
        return lax.ppermute(value, ("dp", "fsdp"), pairs)

    def cross(value, mask):
        return send(value, plane_pairs(lambda f, c: divmod((f * CORES + c) ^ mask, CORES)))

    def trade(value, stage):
        return send(value, plane_pairs(lambda f, c: (f ^ bit_orders[c][stage], c)))

    def trade_mask(index, which):
        mask = 0
        for stage in range(len(bits)):
            if index >> stage & 1:
                mask ^= bit_orders[which][stage]
        return mask

    def climb(value, mask):
        plane = CORES * shards
        pairs = []
        for z in range(depth):
            for rest in range(plane):
                pairs.append((z * plane + rest, (z ^ mask) * plane + rest))
        return send(value, pairs)

    def outward(step):
        def target(f, c):
            place_now = (c * units + (f % units + step) % units) * members + f // units
            return divmod(place_now, CORES)

        return plane_pairs(target)

    def homeward(step):
        return [(b, a) for a, b in outward(step)]

    def bring_start(value):
        blocks = value.reshape(units, per_device, model_width)
        return [
            lax.dynamic_index_in_dim(blocks, (here % units + step) % units, axis=0, keepdims=False)
            for step in range(units)
        ]

    def bring(chosen):
        return jnp.concatenate(
            [send(chosen[step], outward(step)) for step in range(units)], axis=0
        )

    def send_home(value):
        blocks = value.reshape(units, per_device, model_width)
        return [send(blocks[step], homeward(step)) for step in range(units)]

    def in_order(landed, dtype):
        if units == 2:
            swap = here % units == 1
            wanted = [
                jnp.where(swap, landed[1], landed[0]),
                jnp.where(swap, landed[0], landed[1]),
            ]
        else:
            stacked = jnp.stack(landed)
            wanted = [
                lax.dynamic_index_in_dim(stacked, (index - here % units) % units, 0, keepdims=False)
                for index in range(units)
            ]
        return jnp.concatenate(wanted, axis=0).astype(dtype)

    x_chosen = bring_start(tokens)
    x_own = bring(x_chosen)
    small = jnp.concatenate(
        [
            bias_qv.reshape(-1),
            bias_out,
            ln_gain.reshape(-1),
            ln_bias.reshape(-1),
            bias_up,
            bias_down,
        ]
    )
    small_rows = -(-small.shape[0] // (3 * padded))
    small_block = jnp.pad(
        jnp.pad(small, (0, small_rows * 3 * padded - small.shape[0])).reshape(
            small_rows, 3 * padded
        ),
        ((0, 16 - small_rows), (0, 0)),
    )
    def columns_for(offset):
        start = lax.bitwise_xor(member, offset) * head_cols
        blocks = [
            jnp.pad(
                lax.dynamic_slice(
                    w_qkv, (0, kind * model_width + start), (row_shard, head_cols)
                ),
                ((0, 0), (0, padded - head_cols)),
            )
            for kind in range(3)
        ]
        return jnp.concatenate([jnp.concatenate(blocks, axis=1), small_block], axis=0)

    offsets = [(CORES * m) % members for m in range(shards)]
    kinds = sorted(set(offsets))
    *tied, x_own = tie(*[columns_for(offset) for offset in kinds], x_own)
    piece_kinds = dict(zip(kinds, tied))
    x_pieces = [x_own] + [cross(x_own, mask) for mask in range(1, members)]
    qkv_pieces = [piece_kinds[0]] + [
        cross(piece_kinds[offsets[m]], CORES * m) for m in range(1, shards)
    ]
    order_pack = jnp.concatenate(
        [perms.reshape(-1), jnp.broadcast_to(unit_kind[:, None], (units, 128)).reshape(-1)]
    )
    order_other = cross(order_pack, 1)
    order_pack = jnp.where(home_core == core, order_pack, order_other)
    order_count = units * rounds * unit_len
    unit_perm = lax.dynamic_index_in_dim(
        order_pack[:order_count].reshape(units, rounds * unit_len), unit, 0, keepdims=False
    )
    kind_now = lax.dynamic_index_in_dim(
        order_pack[order_count:].reshape(units, 128), unit, 0, keepdims=False
    )[0]
    owner = unit_perm // per_device
    order = (
        lax.bitwise_xor(owner // units, member) * units + (unit - owner % units) % units
    ) * per_device + unit_perm % per_device
    order = order.reshape(rounds, unit_len)
    order = jnp.where(core == 0, order, order[::-1])
    order_row = order.reshape(1, rounds * unit_len)
    order = order.reshape(-1, CLUSTER_ROWS)
    x_here = arrange(order, x_pieces, unit_len, 0)
    x_now = [x_here, cross(x_here, 1)]
    own_masks = [
        jnp.where(core == 0, trade_mask(i, 0), trade_mask(i, 1)) for i in range(1, shards)
    ]
    other_masks = [
        jnp.where(core == 0, trade_mask(i, 1), trade_mask(i, 0)) for i in range(1, shards)
    ]
    zero = jnp.int32(0)
    meta = jnp.stack(
        [kind_now, here, core, member, level, zero, zero, zero] + own_masks + other_masks
    ).astype(jnp.int32)

    def half_of(value, axis, length, at):
        return lax.dynamic_slice_in_dim(value, at * length, length, axis=axis)

    packed = jnp.concatenate(
        [half_of(w_down, 0, pack.down_rows, core)]
        + [
            half_of(w_up, 1, model_width, core * pack.blocks + block)
            for block in range(pack.blocks)
        ]
        + [half_of(w_out, 0, pack.out_rows, core)],
        axis=0,
    )
    order_rows = unit_len // CLUSTER_ROWS
    arranged, probs, mixtures, x_turned = [], [], [], []
    *tied, packed, x_now[0] = tie(*qkv_pieces[1:], packed, x_now[0])
    qkv_pieces = qkv_pieces[:1] + tied
    smalls = jnp.stack(
        [
            piece[row_shard : row_shard + small_rows].reshape(-1)[: small.shape[0]]
            for piece in qkv_pieces
        ]
    )
    smalls = jnp.take(smalls, lax.bitwise_xor(here, jnp.arange(shards)), axis=0).astype(F32)

    def vectors_at(start, count, length):
        part = smalls[:, start * row_shard : start * row_shard + count * length]
        return (
            part.reshape(shards, count, length).transpose(1, 0, 2).reshape(count, shards * length)
        )

    my_bias = lax.dynamic_index_in_dim(
        vectors_at(0, 2, row_shard).reshape(2, members, head_cols), member, 1, keepdims=False
    )
    my_bias = jnp.pad(my_bias, ((0, 0), (0, padded - head_cols)))
    my_bias = jnp.stack([my_bias[0], jnp.zeros_like(my_bias[0]), my_bias[1]]).reshape(1, -1)
    up_bias = vectors_at(7, 1, feed_width // shards)
    down_bias = smalls[:, small.shape[0] - row_shard :].reshape(1, model_width)
    vectors = jnp.concatenate(
        [vectors_at(2, 5, row_shard), down_bias, jnp.zeros((2, model_width), F32)], axis=0
    )

    weight_pieces = {0: packed}
    for stage in range(len(bits)):
        weight_pieces[1 << stage] = trade(packed, stage)
    for index in range(rounds):
        results = attend(meta, x_now[index], my_bias, qkv_pieces, row_shard, mixtures[-1:])
        for kept, result in zip((arranged, probs, mixtures, x_turned), results):
            kept.append(result)
    cot_now, mixtures[0] = tie(cotangent, mixtures[0])
    cot_landed = [
        send(value, outward(step)) for step, value in enumerate(bring_start(cot_now))
    ]
    cot_own = jnp.concatenate(cot_landed, axis=0)
    first_ones = [1 << stage for stage in range(len(bits))]
    *tied, mixtures[1] = tie(*[weight_pieces[index] for index in first_ones], mixtures[1])
    weight_pieces.update(zip(first_ones, tied))
    for stage in range(1, len(bits)):
        for index in range(1, 1 << stage):
            weight_pieces[index | 1 << stage] = trade(weight_pieces[index], stage)
    att_there, att_sent = [], []
    for mask in range(1, members):
        there = place(order_row, mixtures, mask * member_rows, member_rows, 0.5)
        att_sent.append(there)
        att_there.append(cross(there[:, :head_cols], mask))
    att_here = place(order_row, mixtures, 0, member_rows, 0.5, needs=att_sent + cot_landed)

    direct = [weight_pieces[index] for index in range(1, shards)]
    swapped = [cross(piece, 1) for piece in direct[:-1]]
    last_piece, att_here = tie(direct[-1], att_here)
    swapped.append(cross(last_piece, 1))
    att_raw = [att_here[:, :head_cols]] + att_there
    if head_cols % CLUSTER_ROWS:
        att_raw = [jnp.concatenate(att_raw, axis=1)]
    block_out, first_low, d_branch, d_ffn, hidden, d_pre, d_lower, att_turned, *rest = feed(
        pack,
        meta,
        x_own,
        cot_own,
        vectors,
        up_bias,
        att_raw,
        [w_out, w_up, w_down],
        direct + swapped,
    )
    d_att, (row_sums, up_sums) = rest[: len(att_raw)], rest[len(att_raw) :]
    if head_cols % CLUSTER_ROWS:
        d_att = [d_att[0][:, mask * head_cols : (mask + 1) * head_cols] for mask in range(members)]
    d_att = [d_att[0]] + [cross(d_att[mask], mask) for mask in range(1, members)]
    d_att = [jnp.pad(piece, ((0, 0), (0, padded - head_cols))) for piece in d_att]

    def grads_of(half, *needed):
        table = jnp.stack([half, member]).astype(jnp.int32)
        return weight_grads(
            pack, table, d_ffn, hidden, first_low, d_pre, att_turned, d_branch, needed
        )

    theirs = grads_of(1 - core)
    output_landed = send_home(block_out)
    mine = grads_of(core, theirs)
    theirs = cross(theirs, 1)
    sending = [index for index in range(shards) if index & 1]
    keeping = [index for index in range(shards) if not index & 1]
    slots = jnp.stack(
        [
            lax.bitwise_xor(here, jnp.where(core == 0, trade_mask(i, 0), trade_mask(i, 1)))
            for i in sending + keeping
        ]
    )
    going, kept = add_picked(
        jnp.concatenate([slots, slots]).astype(jnp.int32),
        [mine, theirs],
        shards,
        len(sending),
        output_landed + d_att[1:],
    )

    def merge(kept, landed, *needs):
        count = kept.shape[0]
        if count == 1:
            table = jnp.zeros((2,), jnp.int32)
            return None, add_picked(table, [kept, landed], 1, None, needs)[0]
        order_now = [i for i in range(count) if i & 1] + [i for i in range(count) if not i & 1]
        table = jnp.array(order_now * 2, jnp.int32)
        return add_picked(table, [kept, landed], count, count // 2, needs)

    grads, d_x = [None] * rounds, [None] * rounds
    needs = [going]
    blocks = unit_len // POS_BLOCK
    spans = [(rounds - 1, (0, blocks))]
    for index in reversed(range(rounds - 1)):
        spans += [(index, (0, blocks // 2)), (index, (blocks // 2, blocks))]
    results = []
    for turn, (index, span) in enumerate(spans):
        results = attend_back(
            meta,
            order,
            arranged[index],
            probs[index],
            d_att,
            qkv_pieces,
            row_shard,
            index * order_rows,
            needs,
            span,
            results if span[0] else [],
        )
        grads[index], d_x[index] = results
        if turn < len(bits):
            going, kept = merge(kept, trade(going, turn), results[0])
            needs = [kept]
    for stage in range(len(spans), len(bits)):
        going, kept = merge(kept, trade(going, stage))

    def level_pieces(block):
        return block.reshape((depth, block.shape[0] // depth) + block.shape[1:])

    def level_scatter(cut):
        return [
            climb(
                lax.dynamic_index_in_dim(cut, lax.bitwise_xor(level, mask), 0, keepdims=False), mask
            )
            for mask in range(1, depth)
        ]

    def level_gather(piece):
        pieces = {0: piece}
        mask = depth // 2
        while mask:
            pieces.update({index | mask: climb(held, mask) for index, held in pieces.items()})
            mask //= 2
        return [pieces[index] for index in range(depth)]

    def by_shard(value):
        count, length = value.shape
        return (
            value.reshape(count, shards, length // shards)
            .transpose(1, 0, 2)
            .reshape(shards, count * length // shards)
        )

    small_grad = jnp.concatenate(
        [by_shard(row_sums[:5]), by_shard(up_sums), by_shard(row_sums[5:6])], axis=1
    )
    small_length = small_grad.shape[1]
    small_lanes = 3 * head_cols
    small_grad = jnp.pad(small_grad, ((0, 0), (0, BIAS_ROW * small_lanes - small_length)))
    small_grad = jnp.pad(
        small_grad.reshape(shards, BIAS_ROW, small_lanes), ((0, 0), (0, 16 - BIAS_ROW), (0, 0))
    )
    extra_rows = 16
    x_last, kept, small_grad = tie(x_turned[0], kept, small_grad)
    if padded == head_cols:
        joined = qkv_grads([x_last, x_turned[1]], grads, small_grad, row_shard)
    else:
        qkv_grad = dot(x_last, grads[0]) + dot(x_turned[1], grads[1])
        qkv_grad = qkv_grad.reshape(shards, row_shard, 3, padded)[..., :head_cols]
        bias_sum = sum(jnp.sum(value.astype(F32), axis=0) for value in grads)
        bias_sum = bias_sum.reshape(3, padded)[:, :head_cols].reshape(small_lanes)
        small_grad = small_grad.at[:, BIAS_ROW].set(bias_sum[None])
        joined = jnp.concatenate(
            [qkv_grad.reshape(shards, row_shard, small_lanes), small_grad], axis=1
        ).astype(BF16)
    cut = level_pieces(kept[0])
    landed = level_scatter(cut)
    classes = max(1, members // CORES)
    d_x_parts = [d_x[0], cross(d_x[1], 1)]
    order_mine = order_row[:, :unit_len]
    if classes == 1:
        slots_held = jnp.stack(
            [
                lax.bitwise_xor(here, jnp.where(core == 0, trade_mask(i, 0), trade_mask(i, 1)))
                for i in range(shards)
            ]
        )
        held = jnp.stack(
            [
                lax.dynamic_index_in_dim(joined, slots_held[i], 0, keepdims=False)
                for i in range(0, shards, 2)
            ]
        )
        leaving = jnp.stack(
            [
                lax.dynamic_index_in_dim(joined, slots_held[i], 0, keepdims=False)
                for i in range(1, shards, 2)
            ]
        )
        totals = None
    else:
        totals = [None] * classes
        for m in range(shards):
            offset = offsets[m] // CORES
            piece = lax.dynamic_index_in_dim(joined, lax.bitwise_xor(here, m), 0, keepdims=False)
            piece = (piece if m == 0 else cross(piece, CORES * m)).astype(F32)
            totals[offset] = piece if totals[offset] is None else totals[offset] + piece

    if depth > 1:
        picks = jnp.concatenate([level[None], jnp.zeros((depth - 1,), level.dtype)])
        (kept,) = add_picked(
            picks.astype(jnp.int32),
            [cut] + [piece[None] for piece in landed],
            1,
            None,
            [joined],
        )
    d_there = [
        place(
            order_mine,
            d_x_parts,
            mask * member_rows,
            member_rows,
            added=True,
            needs=[kept],
        )
        for mask in range(1, members)
    ]
    gathered = level_gather(kept[0]) if depth > 1 else [cut[0]]
    early = list(d_there)
    if totals is None:
        leaving, held = merge(held, trade(leaving, 0), *d_there)
        early.append(held)
    d_here = place(
        order_mine,
        d_x_parts,
        0,
        member_rows,
        1.0,
        F32,
        d_lower,
        added=True,
        needs=early,
    )
    d_inputs = d_here
    for mask, there in enumerate(d_there, 1):
        d_inputs = d_inputs + cross(there, mask).astype(F32)
    d_inputs = d_inputs.astype(BF16)
    if totals is None:
        for stage in range(1, len(bits)):
            leaving, held = merge(held, trade(leaving, stage), d_here, gathered[depth // 2])
        totals = [held[0]]
    d_inputs = in_order(send_home(d_inputs), F32)
    output = in_order(output_landed, BF16)
    totals = jnp.concatenate(totals, axis=0).astype(BF16)
    rows_each = row_shard + extra_rows
    mask = 1
    while mask < depth:
        totals = (totals.astype(F32) + climb(totals, mask).astype(F32)).astype(BF16)
        mask *= 2
    stacked = stack_up(gathered, [totals])
    grad_down, grad_up, grad_out = unpack(pack, depth, meta, stacked, cross(stacked, 1))
    if padded == head_cols and members == CORES:
        grad_qkv, bias_out_row, smalls_out = unpack_qkv(
            meta, totals, cross(totals, 1), row_shard
        )
        smalls_out = smalls_out.reshape(-1)[:small_length]
        bias_out_row = lax.dynamic_slice(bias_out_row, (0, here * row_shard), (3, row_shard))
    else:
        landed = jnp.stack([totals, cross(totals, 1)], axis=0).reshape(
            CORES, classes, rows_each, 3 * head_cols
        )
        smalls_out = jnp.sum(
            landed[:, :, row_shard : row_shard + BIAS_ROW].astype(F32), axis=(0, 1)
        ).reshape(-1)[:small_length]
        landed = (
            landed.transpose(1, 0, 2, 3)
            .reshape(members, rows_each, 3, head_cols)[:, : row_shard + BIAS_ROW + 1]
        )
        if members == 2:
            swap = member == 1
            landed = jnp.stack(
                [
                    jnp.where(swap, landed[1], landed[0]),
                    jnp.where(swap, landed[0], landed[1]),
                ]
            )
        else:
            landed = jnp.take(landed, lax.bitwise_xor(member, jnp.arange(members)), axis=0)
        grad_qkv = landed[:, :row_shard].transpose(1, 2, 0, 3)
        grad_qkv = grad_qkv.reshape(row_shard, 3 * model_width).astype(F32)
        bias_out_row = landed[:, row_shard + BIAS_ROW].astype(F32).transpose(1, 0, 2)
        bias_out_row = lax.dynamic_slice(
            bias_out_row.reshape(3, model_width), (0, here * row_shard), (3, row_shard)
        )

    feed_shard = feed_width // shards
    spots = [0, row_shard, 3 * row_shard, 5 * row_shard]
    return (
        output,
        d_inputs,
        grad_qkv,
        bias_out_row[::2],
        grad_out,
        smalls_out[spots[0] : spots[1]],
        smalls_out[spots[1] : spots[2]].reshape(2, row_shard),
        smalls_out[spots[2] : spots[3]].reshape(2, row_shard),
        grad_up,
        smalls_out[spots[3] : spots[3] + feed_shard],
        grad_down,
        smalls_out[spots[3] + feed_shard :],
    )


def solution(mesh):
    placed = (
        P(("dp", "fsdp"), None),
        P(("dp", "fsdp"), None),
        P("dp", None, None),
        P("dp"),
        P("fsdp", None),
        P(None, "fsdp"),
        P("fsdp", None),
        P("fsdp"),
        P(None, "fsdp"),
        P(None, "fsdp"),
        P("fsdp", None),
        P("fsdp"),
        P("fsdp", None),
        P("fsdp"),
    )
    return jax.shard_map(
        body,
        mesh=mesh,
        in_specs=placed,
        out_specs=(
            P(("dp", "fsdp"), None),
            P(("dp", "fsdp"), None),
            P("fsdp", None),
            P(None, "fsdp"),
            P("fsdp", None),
            P("fsdp"),
            P(None, "fsdp"),
            P(None, "fsdp"),
            P("fsdp", None),
            P("fsdp"),
            P("fsdp", None),
            P("fsdp"),
        ),
        check_vma=False,
    )
```

```python
from functools import partial

import jax
import jax.numpy as jnp
from jax import lax
from jax.experimental import pallas as pl
from jax.experimental.pallas import tpu as pltpu
from jax.sharding import PartitionSpec as P

HEAD_DIM = 64
CORES = 2
NEG_FILL = -1000000000.0
EPSILON = 1e-05
SCALE = HEAD_DIM ** (-0.5)
BIAS_ROW = 2
GRAD_LANES = 384
CLUSTER_ROWS = 128
HALF_ROWS = 64
POS_BLOCK = 512
TOKEN_BLOCK = 512
ROW_BLOCK = 256
FF_BLOCK = 512
MIB = 1024 * 1024
NT = (((1,), (1,)), ((), ()))
TN = (((0,), (0,)), ((), ()))
F32 = jnp.float32
BF16 = jnp.bfloat16
ANYWHERE = pl.BlockSpec(memory_space=pl.ANY)
IN_SMEM = pl.BlockSpec(memory_space=pltpu.SMEM)


def whole(shape):
    return pl.BlockSpec(shape, lambda i: (0,) * len(shape))


def rows_of(shape):
    return pl.BlockSpec(shape, lambda i: (i,) + (0,) * (len(shape) - 1))


def dot(a, b, dims=(((1,), (0,)), ((), ()))):
    return lax.dot_general(a, b, dims, preferred_element_type=F32)


def params(mib, flops=0, moved=0, share=16):
    return dict(
        compiler_params=pltpu.CompilerParams(
            dimension_semantics=("arbitrary",),
            vmem_limit_bytes=mib * MIB,
        ),
        cost_estimate=pl.CostEstimate(
            flops=flops // share, bytes_accessed=moved // share, transcendentals=0
        ),
    )


def gated(kernel, used, needs):
    if not needs:
        return kernel

    def run(*refs):
        return kernel(*refs[:used], *refs[used + len(needs) :])

    return run


def lane_masks():
    lane = lax.broadcasted_iota(jnp.int32, (CLUSTER_ROWS, CLUSTER_ROWS), 1)
    low = (lane < HEAD_DIM).astype(F32)
    return low.astype(BF16), (1.0 - low).astype(BF16), lane < HEAD_DIM


def both_heads(rows_now, low, high):
    return jnp.concatenate([rows_now * low, rows_now * high], axis=0)


def equal_ones(left, right):
    return jnp.where(left == right, jnp.ones((), BF16), jnp.zeros((), BF16))


def pick_rows(order_ref, first_row, unit_len):
    parts = []
    lane = lax.broadcasted_iota(jnp.int16, (CLUSTER_ROWS, CLUSTER_ROWS), 1)
    for part in range(POS_BLOCK // CLUSTER_ROWS):
        row = order_ref[pl.ds(first_row + part, 1), :]
        column = jnp.transpose(jnp.broadcast_to(row, (CLUSTER_ROWS, CLUSTER_ROWS)))
        column = column.astype(jnp.int16)
        pieces = [
            equal_ones(column, lane + jnp.int16(base)) for base in range(0, unit_len, CLUSTER_ROWS)
        ]
        parts.append(jnp.concatenate(pieces, axis=1))
    return jnp.concatenate(parts, axis=0)


def load_pieces(meta, x_refs, w_refs, x_all, w_all, sems, row_shard):
    member_rows = x_all.shape[0] // max(1, len(x_refs))
    copies = []
    for index, ref in enumerate(x_refs):
        copies.append(
            pltpu.make_async_copy(
                ref, x_all.at[pl.ds(index * member_rows, member_rows), :], sems.at[index]
            )
        )
    for index, ref in enumerate(w_refs):
        start = pl.multiple_of(lax.bitwise_xor(meta[1], index) * row_shard, 16)
        copies.append(
            pltpu.make_async_copy(
                ref.at[pl.ds(0, row_shard), :],
                w_all.at[pl.ds(start, row_shard), :],
                sems.at[len(x_refs) + index],
            )
        )
    for copy in copies:
        copy.start()
    for copy in copies:
        copy.wait()


def arrange_kernel(unit_len, first_row, order_ref, *refs):
    x_refs, out_ref = refs[:-1], refs[-1]
    step = pl.program_id(0)
    picks = pick_rows(order_ref, first_row + step * (POS_BLOCK // CLUSTER_ROWS), unit_len)
    rows = x_refs[0].shape[0]
    total = None
    for index, ref in enumerate(x_refs):
        term = dot(picks[:, index * rows : (index + 1) * rows], ref[...])
        total = term if total is None else total + term
    out_ref[...] = total.astype(BF16)


def arrange(order, x_pieces, position_count, first_row):
    member_rows, width = x_pieces[0].shape
    unit_len = member_rows * len(x_pieces)
    return pl.pallas_call(
        partial(arrange_kernel, unit_len, first_row),
        grid=(position_count // POS_BLOCK,),
        in_specs=[whole(order.shape)] + [whole(piece.shape) for piece in x_pieces],
        out_specs=rows_of((POS_BLOCK, width)),
        out_shape=jax.ShapeDtypeStruct((position_count, width), BF16),
        name="arrange",
        **params(20, 2 * position_count * unit_len * width, 6_000_000),
    )(order, *x_pieces)


def attend_kernel(sizes, meta, x_now_ref, bias_ref, *refs):
    shards, row_shard = sizes
    w_refs, refs = refs[:shards], refs[shards:]
    arranged_ref, probs_ref, mixture_ref, turned_ref, w_all, sems = refs
    width = w_all.shape[1] // 3
    step = pl.program_id(0)

    @pl.when(step == 0)
    def _():
        load_pieces(meta, [], w_refs, w_all, w_all, sems, row_shard)

    x_now = x_now_ref[...]
    turned_ref[...] = jnp.transpose(x_now)
    arranged = (dot(x_now, w_all[...]) + bias_ref[...]).astype(BF16)
    arranged_ref[...] = arranged
    low, high, lane_low = lane_masks()
    position = lax.broadcasted_iota(jnp.int32, (CLUSTER_ROWS, CLUSTER_ROWS), 0)
    other = lax.broadcasted_iota(jnp.int32, (CLUSTER_ROWS, CLUSTER_ROWS), 1)
    same_half = (position < HALF_ROWS) == (other < HALF_ROWS)
    allowed = jnp.logical_or(same_half, meta[0] == 1)
    pairs = width // CLUSTER_ROWS
    for part in range(POS_BLOCK // CLUSTER_ROWS):
        rows_now = slice(part * CLUSTER_ROWS, (part + 1) * CLUSTER_ROWS)
        for pair in range(pairs):
            base = pair * CLUSTER_ROWS
            queries = arranged[rows_now, base : base + CLUSTER_ROWS] * SCALE
            keys = arranged[rows_now, width + base : width + base + CLUSTER_ROWS]
            values = arranged[rows_now, 2 * width + base : 2 * width + base + CLUSTER_ROWS]
            scores = dot(both_heads(keys, low, high), queries, NT)
            halves = []
            for head in range(2):
                one = scores[head * CLUSTER_ROWS : (head + 1) * CLUSTER_ROWS]
                one = jnp.where(allowed, one, NEG_FILL)
                grown = jnp.exp(one - jnp.max(one, axis=0, keepdims=True))
                halves.append(grown * (1.0 / jnp.sum(grown, axis=0, keepdims=True)))
            probs = jnp.concatenate(halves, axis=0).astype(BF16)
            at = (part * pairs + pair) * 2 * CLUSTER_ROWS
            probs_ref[at : at + 2 * CLUSTER_ROWS, :] = probs
            mixture = dot(probs, both_heads(values, low, high), TN).astype(BF16)
            mixture_ref[rows_now, base : base + CLUSTER_ROWS] = mixture


def attend(meta, x_now, bias, w_pieces, row_shard, needs=()):
    shards = len(w_pieces)
    position_count, model_width = x_now.shape
    cols = w_pieces[0].shape[1]
    width = cols // 3
    pair_rows = 2 * width
    return pl.pallas_call(
        gated(partial(attend_kernel, (shards, row_shard)), 3 + shards, needs),
        grid=(position_count // POS_BLOCK,),
        in_specs=[IN_SMEM, rows_of((POS_BLOCK, model_width)), whole(bias.shape)]
        + [ANYWHERE] * (shards + len(needs)),
        out_specs=[
            rows_of((POS_BLOCK, cols)),
            rows_of((POS_BLOCK // CLUSTER_ROWS * pair_rows, CLUSTER_ROWS)),
            rows_of((POS_BLOCK, width)),
            pl.BlockSpec((model_width, POS_BLOCK), lambda i: (0, i)),
        ],
        out_shape=[
            jax.ShapeDtypeStruct((position_count, cols), BF16),
            jax.ShapeDtypeStruct((position_count // CLUSTER_ROWS * pair_rows, CLUSTER_ROWS), BF16),
            jax.ShapeDtypeStruct((position_count, width), BF16),
            jax.ShapeDtypeStruct((model_width, position_count), BF16),
        ],
        scratch_shapes=[
            pltpu.VMEM((model_width, cols), BF16),
            pltpu.SemaphoreType.DMA((shards,)),
        ],
        name="attend",
        **params(
            48, 8 * position_count * (model_width * cols + 4 * CLUSTER_ROWS * width), 18_000_000, 1
        ),
    )(meta, x_now, bias, *w_pieces, *needs)


def place_kernel(sizes, scale, has_base, order_row_ref, *refs):
    unit_len, first_token, added = sizes
    base_ref = refs[0] if has_base else None
    refs = refs[1 if has_base else 0 :]
    if added:
        first_ref, second_ref, out_ref, held = refs

        @pl.when(pl.program_id(0) == 0)
        def _():
            held[...] = (first_ref[...].astype(F32) + second_ref[...].astype(F32)).astype(BF16)

        source_refs = [held]
    else:
        source_refs, out_ref = refs[:-1], refs[-1]
    block_rows = out_ref.shape[0]
    first = jnp.full((1, 1), first_token + pl.program_id(0) * block_rows, jnp.int32)
    token = lax.broadcasted_iota(jnp.int16, (block_rows, unit_len), 0)
    total = None
    for index, ref in enumerate(source_refs):
        row = order_row_ref[:, index * unit_len : (index + 1) * unit_len] - first
        row = jnp.broadcast_to(row, (16, unit_len)).astype(jnp.int16)
        row = jnp.concatenate([row] * (block_rows // 16), axis=0)
        term = dot(equal_ones(row, token), ref[...])
        total = term if total is None else total + term
    if scale != 1.0:
        total = total * scale
    if has_base:
        total = total + base_ref[...]
    out_ref[...] = total.astype(out_ref.dtype)


def place(
    order_row,
    sources,
    first_token,
    row_count,
    scale=1.0,
    dtype=BF16,
    base=None,
    added=False,
    needs=(),
):
    unit_len, width = sources[0].shape
    block_rows = min(TOKEN_BLOCK, row_count)
    extra = [] if base is None else [base]
    return pl.pallas_call(
        gated(
            partial(place_kernel, (unit_len, first_token, added), scale, base is not None),
            1 + len(extra) + len(sources),
            needs,
        ),
        grid=(row_count // block_rows,),
        in_specs=[whole(order_row.shape)]
        + [rows_of((block_rows, width))] * len(extra)
        + [whole(source.shape) for source in sources]
        + [ANYWHERE] * len(needs),
        out_specs=rows_of((block_rows, width)),
        out_shape=jax.ShapeDtypeStruct((row_count, width), dtype),
        scratch_shapes=[pltpu.VMEM((unit_len, width), BF16)] if added else [],
        name="place",
        **params(
            32 if added else 20,
            16 * row_count * unit_len * width,
            10_000_000,
            1,
        ),
    )(order_row, *extra, *sources, *needs)


def attend_back_kernel(sizes, meta, order_ref, arranged_ref, probs_ref, *refs):
    members, shards, unit_len, row_shard, first_row, start = sizes
    g_refs, refs = refs[:members], refs[members:]
    w_refs, refs = refs[:shards], refs[shards:]
    grads_ref, d_x_ref, g_all, w_all, sems = refs
    width = w_all.shape[1] // 3
    step = pl.program_id(0)

    @pl.when(step == 0)
    def _():
        load_pieces(meta, g_refs, w_refs, g_all, w_all, sems, row_shard)

    at_row = first_row + (start + step) * (POS_BLOCK // CLUSTER_ROWS)
    picks = pick_rows(order_ref, at_row, unit_len)
    d_mixture = dot(picks, g_all[...]).astype(BF16)
    low, high, lane_low = lane_masks()
    pairs = width // CLUSTER_ROWS
    for part in range(POS_BLOCK // CLUSTER_ROWS):
        rows_now = slice(part * CLUSTER_ROWS, (part + 1) * CLUSTER_ROWS)
        for pair in range(pairs):
            base = pair * CLUSTER_ROWS
            q_lanes = slice(base, base + CLUSTER_ROWS)
            k_lanes = slice(width + base, width + base + CLUSTER_ROWS)
            v_lanes = slice(2 * width + base, 2 * width + base + CLUSTER_ROWS)
            queries = arranged_ref[rows_now, q_lanes] * SCALE
            keys = arranged_ref[rows_now, k_lanes] * SCALE
            values = arranged_ref[rows_now, v_lanes]
            at = (part * pairs + pair) * 2 * CLUSTER_ROWS
            probs = probs_ref[at : at + 2 * CLUSTER_ROWS, :]
            d_now = d_mixture[rows_now, base : base + CLUSTER_ROWS]
            d_probs = dot(both_heads(values, low, high), d_now, NT)
            pieces = []
            for head in range(2):
                rows = slice(head * CLUSTER_ROWS, (head + 1) * CLUSTER_ROWS)
                weight = probs[rows].astype(F32)
                d_one = d_probs[rows]
                inner = jnp.sum(weight * d_one, axis=0, keepdims=True)
                pieces.append(weight * (d_one - inner))
            d_scores = jnp.concatenate(pieces, axis=0).astype(BF16)
            d_query = dot(d_scores, both_heads(keys, low, high), TN)
            d_keys = dot(d_scores, queries)
            d_values = dot(probs, d_now)
            grads_ref[rows_now, q_lanes] = d_query.astype(BF16)
            grads_ref[rows_now, k_lanes] = jnp.where(
                lane_low, d_keys[:CLUSTER_ROWS], d_keys[CLUSTER_ROWS:]
            ).astype(BF16)
            grads_ref[rows_now, v_lanes] = jnp.where(
                lane_low, d_values[:CLUSTER_ROWS], d_values[CLUSTER_ROWS:]
            ).astype(BF16)
    grads = grads_ref[...]
    d_x_ref[...] = dot(grads, w_all[...], NT).astype(BF16)


def attend_back(
    meta, order, arranged, probs, g_pieces, w_pieces, row_shard, first_row, needs, span, into
):
    members, shards = len(g_pieces), len(w_pieces)
    member_rows, width = g_pieces[0].shape
    unit_len = members * member_rows
    position_count, cols = arranged.shape
    model_width = row_shard * shards
    start, stop = span
    pair_rows = POS_BLOCK // CLUSTER_ROWS * 2 * width
    used = 4 + members + shards

    def block(shape):
        return pl.BlockSpec(shape, lambda i: (start + i, 0))

    return pl.pallas_call(
        gated(
            partial(attend_back_kernel, (members, shards, unit_len, row_shard, first_row, start)),
            used,
            list(into) + list(needs),
        ),
        grid=(stop - start,),
        in_specs=[
            IN_SMEM,
            whole(order.shape),
            block((POS_BLOCK, cols)),
            block((pair_rows, CLUSTER_ROWS)),
        ]
        + [ANYWHERE] * (members + shards + len(into) + len(needs)),
        out_specs=[block((POS_BLOCK, cols)), block((POS_BLOCK, model_width))],
        out_shape=[
            jax.ShapeDtypeStruct((position_count, cols), BF16),
            jax.ShapeDtypeStruct((position_count, model_width), BF16),
        ],
        input_output_aliases={used + index: index for index in range(len(into))},
        scratch_shapes=[
            pltpu.VMEM((unit_len, width), BF16),
            pltpu.VMEM((model_width, cols), BF16),
            pltpu.SemaphoreType.DMA((members + shards,)),
        ],
        name="attend_back",
        **params(48, 2 * position_count * (unit_len * width + model_width * cols), 20_000_000),
    )(meta, order, arranged, probs, *g_pieces, *w_pieces, *into, *needs)


def normalise(summed):
    average = jnp.mean(summed, axis=-1, keepdims=True)
    centred = summed - average
    spread = jnp.mean(centred * centred, axis=-1, keepdims=True)
    scale_inv = lax.rsqrt(spread + EPSILON)
    return centred * scale_inv, scale_inv


def normalise_back(grad_out, normed, scale_inv, gain_row):
    scaled = grad_out * gain_row
    return scale_inv * (
        scaled
        - jnp.mean(scaled, axis=-1, keepdims=True)
        - normed * jnp.mean(scaled * normed, axis=-1, keepdims=True)
    )


def column_sum(rows_now):
    return jnp.sum(rows_now, axis=0, keepdims=True)


def gelu_parts(value):
    below = 0.5 + 0.5 * lax.erf(value * 0.7071067811865476)
    bell = jnp.exp(value * value * -0.5) * 0.3989422804014327
    return value * below, below + value * bell


class Pack:
    def __init__(self, model_width, feed_width, shards, units, depth):
        self.model_width, self.feed_width, self.shards = model_width, feed_width, shards
        self.row_shard = model_width // shards
        self.feed_shard = feed_width // shards
        self.down_rows = self.feed_shard // CORES
        self.blocks = feed_width // CORES // model_width
        self.up_at = self.down_rows
        self.out_at = self.up_at + self.blocks * self.row_shard
        self.out_rows = self.row_shard // CORES
        self.used = self.out_at + self.out_rows
        unit = 16 * depth
        self.rows = -(-self.used // unit) * unit
        self.units = units
        self.group = units * self.row_shard

    def out_start(self, shard, member):
        return (
            lax.bitwise_xor(jnp.int32(shard) // self.units, member) * self.group
            + (shard % self.units) * self.row_shard
        )


def feed_kernel(pack, att_count, meta, x_ref, cot_ref, vec_ref, up_bias_ref, *refs):
    shards = pack.shards
    att_refs, refs = refs[:att_count], refs[att_count:]
    own_out, own_up, own_down = refs[:3]
    refs = refs[3:]
    pieces, refs = refs[: 2 * (shards - 1)], refs[2 * (shards - 1) :]
    out_ref, first_turned_ref, d_branch_ref, d_ffn_turned_ref, hidden_ref, d_pre_ref = refs[:6]
    d_h1_ref, att_turned_ref = refs[6:8]
    refs = refs[8:]
    d_att_refs, refs = refs[:att_count], refs[att_count:]
    sums_ref, up_sums_ref, w_out, w_up, w_down, slope, sems = refs
    step = pl.program_id(0)
    here, core, member = meta[1], meta[2], meta[3]
    feed_width = pack.feed_width

    def loads(kind):
        copies = []

        def add(source, target):
            copies.append(pltpu.make_async_copy(source, target, sems.at[kind, len(copies)]))

        if kind == 0:
            start = pl.multiple_of(pack.out_start(here, member), 16)
            add(own_out, w_out.at[pl.ds(start, pack.row_shard), :])
        elif kind == 1:
            start = pl.multiple_of(here * pack.row_shard, 16)
            add(own_up, w_up.at[pl.ds(start, pack.row_shard), :])
        else:
            start = pl.multiple_of(here * pack.feed_shard, 16)
            add(own_down, w_down.at[pl.ds(start, pack.feed_shard), :])
        for index, ref in enumerate(pieces):
            peer = lax.bitwise_xor(here, meta[8 + index])
            half = core if index < shards - 1 else 1 - core
            if kind == 0:
                start = pack.out_start(peer, member) + half * pack.out_rows
                start = pl.multiple_of(start, 16)
                add(
                    ref.at[pl.ds(pack.out_at, pack.out_rows), :],
                    w_out.at[pl.ds(start, pack.out_rows), :],
                )
            elif kind == 1:
                start = pl.multiple_of(peer * pack.row_shard, 16)
                for block in range(pack.blocks):
                    lane = pl.multiple_of(
                        (half * pack.blocks + block) * pack.model_width, CLUSTER_ROWS
                    )
                    add(
                        ref.at[pl.ds(pack.up_at + block * pack.row_shard, pack.row_shard), :],
                        w_up.at[pl.ds(start, pack.row_shard), pl.ds(lane, pack.model_width)],
                    )
            else:
                start = pl.multiple_of(peer * pack.feed_shard + half * pack.down_rows, 16)
                add(
                    ref.at[pl.ds(0, pack.down_rows), :],
                    w_down.at[pl.ds(start, pack.down_rows), :],
                )
        return copies

    @pl.when(step == 0)
    def _():
        for kind in range(3):
            for copy in loads(kind):
                copy.start()
        sums_ref[...] = jnp.zeros_like(sums_ref)
        up_sums_ref[...] = jnp.zeros_like(up_sums_ref)
        for copy in loads(0):
            copy.wait()

    bias_out, gain_one, gain_two = vec_ref[0:1, :], vec_ref[1:2, :], vec_ref[2:3, :]
    shift_one, shift_two, bias_down = vec_ref[3:4, :], vec_ref[4:5, :], vec_ref[5:6, :]
    att_width = att_refs[0].shape[1]
    summed = x_ref[...].astype(F32) + bias_out
    for index, ref in enumerate(att_refs):
        summed += dot(ref[...], w_out[index * att_width : (index + 1) * att_width, :])
    normed_one, inv_one = normalise(summed)
    first = normed_one * gain_one + shift_one
    first_low = first.astype(BF16)
    first_turned_ref[...] = jnp.transpose(first_low)
    for index, ref in enumerate(att_refs):
        att_turned_ref[index * att_width : (index + 1) * att_width, :] = jnp.transpose(ref[...])

    @pl.when(step == 0)
    def _():
        for kind in (1, 2):
            for copy in loads(kind):
                copy.wait()

    second = first + bias_down
    starts = list(range(0, feed_width, FF_BLOCK))

    def raised(base):
        lanes = slice(base, base + FF_BLOCK)
        return dot(first_low, w_up[:, lanes]) + up_bias_ref[:, lanes]

    pre = raised(starts[0])
    for index, base in enumerate(starts):
        lanes = slice(base, base + FF_BLOCK)
        pre_next = raised(starts[index + 1]) if index + 1 < len(starts) else None
        hidden, slope_now = gelu_parts(pre)
        hidden = hidden.astype(BF16)
        hidden_ref[:, lanes] = hidden
        slope[:, lanes] = slope_now
        second += dot(hidden, w_down[lanes, :])
        pre = pre_next
    normed_two, inv_two = normalise(second)
    out_ref[...] = (normed_two * gain_two + shift_two).astype(BF16)
    top = cot_ref[...].astype(F32)
    d_second = normalise_back(top, normed_two, inv_two, gain_two)
    d_ffn = d_second.astype(BF16)
    d_ffn_turned_ref[...] = jnp.transpose(d_ffn)
    d_first = d_second
    d_hidden = dot(d_ffn, w_down[0:FF_BLOCK, :], NT)
    for index, base in enumerate(starts):
        lanes = slice(base, base + FF_BLOCK)
        if index + 1 < len(starts):
            d_next = dot(d_ffn, w_down[starts[index + 1] : starts[index + 1] + FF_BLOCK, :], NT)
        d_pre = (d_hidden * slope[:, lanes]).astype(BF16)
        d_pre_ref[:, lanes] = d_pre
        up_sums_ref[:, lanes] += column_sum(d_pre.astype(F32))
        d_first += dot(d_pre, w_up[:, lanes], NT)
        d_hidden = d_next
    d_lower = normalise_back(d_first, normed_one, inv_one, gain_one)
    d_h1_ref[...] = d_lower
    d_branch = d_lower.astype(BF16)
    d_branch_ref[...] = d_branch
    for index, ref in enumerate(d_att_refs):
        back = dot(d_branch, w_out[index * att_width : (index + 1) * att_width, :], NT)
        ref[...] = (0.5 * back).astype(BF16)
    sums_ref[0:1, :] += column_sum(d_branch.astype(F32))
    sums_ref[1:2, :] += column_sum(d_first * normed_one)
    sums_ref[2:3, :] += column_sum(top * normed_two)
    sums_ref[3:4, :] += column_sum(d_first)
    sums_ref[4:5, :] += column_sum(top)
    sums_ref[5:6, :] += column_sum(d_ffn.astype(F32))


def feed(pack, meta, x_own, cot_own, vectors, up_bias, att, own, pieces):
    row_count, model_width = x_own.shape
    feed_width = pack.feed_width
    att_width = att[0].shape[1]
    one = rows_of((ROW_BLOCK, model_width))
    wide = rows_of((ROW_BLOCK, feed_width))
    narrow = rows_of((ROW_BLOCK, att_width))
    turned = pl.BlockSpec((model_width, ROW_BLOCK), lambda i: (0, i))
    turned_shape = jax.ShapeDtypeStruct((model_width, row_count), BF16)

    def like(width, dtype=BF16):
        return jax.ShapeDtypeStruct((row_count, width), dtype)

    return pl.pallas_call(
        partial(feed_kernel, pack, len(att)),
        grid=(row_count // ROW_BLOCK,),
        in_specs=[IN_SMEM, one, one, whole(vectors.shape), whole(up_bias.shape)]
        + [narrow] * len(att)
        + [ANYWHERE] * (3 + len(pieces)),
        out_specs=[one, turned, one, turned, wide, wide, one, turned]
        + [narrow] * len(att)
        + [whole((8, model_width)), whole((1, feed_width))],
        out_shape=[
            like(model_width),
            turned_shape,
            like(model_width),
            turned_shape,
            like(feed_width),
            like(feed_width),
            like(model_width, F32),
            turned_shape,
        ]
        + [like(att_width)] * len(att)
        + [
            jax.ShapeDtypeStruct((8, model_width), F32),
            jax.ShapeDtypeStruct((1, feed_width), F32),
        ],
        scratch_shapes=[
            pltpu.VMEM((model_width, model_width), BF16),
            pltpu.VMEM((model_width, feed_width), BF16),
            pltpu.VMEM((feed_width, model_width), BF16),
            pltpu.VMEM((ROW_BLOCK, feed_width), F32),
            pltpu.SemaphoreType.DMA((3, 1 + pack.blocks * len(pieces))),
        ],
        name="feed",
        **params(
            40, 2 * row_count * model_width * (2 * model_width + 4 * feed_width), 40_000_000
        ),
    )(meta, x_own, cot_own, vectors, up_bias, *att, *own, *pieces)


def weight_grads_kernel(
    pack,
    table,
    hidden_ref,
    d_ffn_ref,
    first_ref,
    d_pre_ref,
    att_ref,
    d_branch_ref,
    out_ref,
    d_ffn,
    first,
    d_pre,
    att,
    d_branch,
    made,
    in_sems,
    out_sems,
):
    step = pl.program_id(0)
    half, member = table[0], table[1]
    width, shards = pack.model_width, pack.shards

    def loads():
        start = pl.multiple_of(half * (width // CORES), 16)
        pairs = [(d_ffn_ref.at[pl.ds(start, width // CORES), :], d_ffn), (first_ref, first)]
        for block in range(pack.blocks):
            lane = pl.multiple_of((half * pack.blocks + block) * width, CLUSTER_ROWS)
            pairs.append((d_pre_ref.at[:, pl.ds(lane, width)], d_pre.at[block]))
        pairs += [(att_ref, att), (d_branch_ref, d_branch)]
        return [
            pltpu.make_async_copy(source, target, in_sems.at[index])
            for index, (source, target) in enumerate(pairs)
        ]

    def store(shard, start, rows, sem):
        there = (shard, pl.ds(start, rows), slice(None))
        return pltpu.make_async_copy(made.at[there], out_ref.at[there], out_sems.at[sem])

    def up_store(shard, block):
        at = pack.up_at + block * pack.row_shard
        return store(shard, at, pack.row_shard, shards + block * shards + shard)

    def out_store(shard):
        sem = shards * (1 + pack.blocks) + shard
        return store(shard, pack.out_at, pack.rows - pack.out_at, sem)

    @pl.when(step == 0)
    def _():
        for copy in loads():
            copy.start()
        loads()[0].wait()

    @pl.when(step < shards)
    def _():
        grad = dot(d_ffn[...], hidden_ref[...]).astype(BF16)
        for lane in range(0, width, pack.feed_shard):
            begin = lane // pack.feed_shard * pack.down_rows
            made[step, : pack.down_rows, lane : lane + pack.feed_shard] = grad[
                begin : begin + pack.down_rows
            ]
        store(step, 0, pack.down_rows, step).start()

    for block in range(pack.blocks):

        @pl.when(step == shards + block)
        def _(block=block):
            if block == 0:
                loads()[1].wait()
            loads()[2 + block].wait()
            grad = dot(first[...], d_pre[block]).astype(BF16)
            start = pack.up_at + block * pack.row_shard
            for shard in range(shards):
                made[shard, start : start + pack.row_shard, :] = grad[
                    shard * pack.row_shard : (shard + 1) * pack.row_shard
                ]
                up_store(shard, block).start()

    @pl.when(step == shards + pack.blocks)
    def _():
        for copy in loads()[2 + pack.blocks :]:
            copy.wait()
        for shard in range(shards):
            start = pack.out_start(shard, member) + half * pack.out_rows
            start = pl.multiple_of(start, 16)
            made[shard, pack.out_at : pack.out_at + pack.out_rows, :] = dot(
                att[pl.ds(start, pack.out_rows), :], d_branch[...]
            ).astype(BF16)
            if pack.rows > pack.used:
                made[shard, pack.used :, :] = jnp.zeros((pack.rows - pack.used, width), BF16)
            out_store(shard).start()
        for shard in range(shards):
            store(shard, 0, pack.down_rows, shard).wait()
            for block in range(pack.blocks):
                up_store(shard, block).wait()
            out_store(shard).wait()


def weight_grads(pack, table, d_ffn, hidden, first_low, d_pre, att, d_branch, needs=()):
    model_width, row_count = d_ffn.shape
    shards, blocks = pack.shards, pack.blocks
    shape = (shards, pack.rows, model_width)
    return pl.pallas_call(
        gated(partial(weight_grads_kernel, pack), 7, needs),
        grid_spec=pltpu.PrefetchScalarGridSpec(
            num_scalar_prefetch=1,
            grid=(shards + blocks + 1,),
            in_specs=[
                pl.BlockSpec(
                    (row_count, pack.feed_shard),
                    lambda step, table: (0, jnp.minimum(step, shards - 1)),
                )
            ]
            + [ANYWHERE] * (5 + len(needs)),
            out_specs=ANYWHERE,
            scratch_shapes=[
                pltpu.VMEM((model_width // CORES, row_count), BF16),
                pltpu.VMEM((model_width, row_count), BF16),
                pltpu.VMEM((blocks, row_count, model_width), BF16),
                pltpu.VMEM((model_width, row_count), BF16),
                pltpu.VMEM((row_count, model_width), BF16),
                pltpu.VMEM(shape, BF16),
                pltpu.SemaphoreType.DMA((4 + blocks,)),
                pltpu.SemaphoreType.DMA((shards * (2 + blocks),)),
            ],
        ),
        out_shape=jax.ShapeDtypeStruct(shape, BF16),
        name="weight_grads",
        **params(60, row_count * model_width * (2 * pack.feed_width + model_width), 20_000_000),
    )(table, hidden, d_ffn, first_low, d_pre, att, d_branch, *needs)


def qkv_grads_kernel(rounds, x_refs_then, *refs):
    refs = (x_refs_then,) + refs
    x_refs, grad_refs = refs[:rounds], refs[rounds : 2 * rounds]
    small_ref, out_ref = refs[2 * rounds :]
    shards, rows, _ = out_ref.shape
    row_shard = rows - small_ref.shape[1]
    total, sums = None, None
    for x_ref, grad_ref in zip(x_refs, grad_refs):
        grads = grad_ref[...]
        term = dot(x_ref[...], grads)
        down = column_sum(grads.astype(F32))
        total = term if total is None else total + term
        sums = down if sums is None else sums + down
    total = total.astype(BF16)
    row = lax.broadcasted_iota(jnp.int32, small_ref.shape[1:], 0)
    for shard in range(shards):
        out_ref[shard, :row_shard, :] = total[shard * row_shard : (shard + 1) * row_shard]
        last = jnp.where(row == BIAS_ROW, sums, small_ref[shard])
        out_ref[shard, row_shard:, :] = last.astype(BF16)


def qkv_grads(x_turned, grads, small, row_shard):
    rounds = len(grads)
    model_width, positions = x_turned[0].shape
    cols = grads[0].shape[1]
    shards, extra, _ = small.shape
    block = GRAD_LANES if cols % GRAD_LANES == 0 else cols
    return pl.pallas_call(
        partial(qkv_grads_kernel, rounds),
        grid=(cols // block,),
        in_specs=[whole((model_width, positions))] * rounds
        + [pl.BlockSpec((positions, block), lambda i: (0, i))] * rounds
        + [pl.BlockSpec((shards, extra, block), lambda i: (0, 0, i))],
        out_specs=pl.BlockSpec((shards, row_shard + extra, block), lambda i: (0, 0, i)),
        out_shape=jax.ShapeDtypeStruct((shards, row_shard + extra, cols), BF16),
        name="qkv_grads",
        **params(28, 2 * rounds * positions * model_width * cols, 18_000_000),
    )(*x_turned, *grads, small)


def add_picked_kernel(count, first, table, *refs):
    in_refs, out_refs = refs[:count], refs[count:]
    if count == 2:
        total = in_refs[0][...] + in_refs[1][...]
    else:
        total = in_refs[0][...].astype(F32)
        for ref in in_refs[1:]:
            total = total + ref[...].astype(F32)
        total = total.astype(BF16)
    if len(out_refs) == 1:
        out_refs[0][...] = total
        return

    @pl.when(pl.program_id(0) < first)
    def _():
        out_refs[0][...] = total

    @pl.when(pl.program_id(0) >= first)
    def _():
        out_refs[1][...] = total


def add_picked(table, arrays, steps, first=None, needs=()):
    _, rows, cols = arrays[0].shape
    parts = 2 if rows % 32 == 0 else 1
    block = (1, rows // parts, cols)
    spec = [
        pl.BlockSpec(block, lambda s, p, t, k=k: (t[k * steps + s], p, 0))
        for k in range(len(arrays))
    ]
    if first is None:
        out_specs = [pl.BlockSpec(block, lambda s, p, t: (s, p, 0))]
        counts = [steps]
    else:
        out_specs = [
            pl.BlockSpec(
                block,
                lambda s, p, t: (
                    jnp.minimum(s, first - 1),
                    jnp.where(s < first, p, parts - 1),
                    0,
                ),
            ),
            pl.BlockSpec(
                block,
                lambda s, p, t: (jnp.maximum(s - first, 0), jnp.where(s < first, 0, p), 0),
            ),
        ]
        counts = [first, steps - first]
    return pl.pallas_call(
        gated(partial(add_picked_kernel, len(arrays), first), 1 + len(arrays), needs),
        grid_spec=pltpu.PrefetchScalarGridSpec(
            num_scalar_prefetch=1,
            grid=(steps, parts),
            in_specs=spec + [ANYWHERE] * len(needs),
            out_specs=out_specs,
        ),
        out_shape=[jax.ShapeDtypeStruct((n, rows, cols), BF16) for n in counts],
        name="add_picked",
        compiler_params=pltpu.CompilerParams(
            dimension_semantics=("arbitrary", "arbitrary"), vmem_limit_bytes=12 * MIB
        ),
        cost_estimate=pl.CostEstimate(flops=0, bytes_accessed=rows * cols, transcendentals=0),
    )(table, *arrays, *needs)


def stack_kernel(count, *refs):
    for index in range(count):
        refs[count][index] = refs[index][...]


def stack_up(pieces, needs=()):
    vmem = pl.BlockSpec(memory_space=pltpu.VMEM)
    return pl.pallas_call(
        gated(partial(stack_kernel, len(pieces)), len(pieces), needs),
        in_specs=[vmem] * len(pieces) + [ANYWHERE] * len(needs),
        out_specs=vmem,
        out_shape=jax.ShapeDtypeStruct((len(pieces),) + pieces[0].shape, BF16),
        name="stack_up",
        compiler_params=pltpu.CompilerParams(vmem_limit_bytes=24 * MIB),
        cost_estimate=pl.CostEstimate(flops=0, bytes_accessed=100_000, transcendentals=0),
    )(*pieces, *needs)


def unpack_kernel(pack, depth, meta, mine_ref, other_ref, down_ref, up_ref, out_ref, ordered):
    core, level = meta[2], meta[4]
    rows = pack.rows // depth
    for mask in range(depth):
        start = pl.multiple_of(lax.bitwise_xor(level, mask) * rows, 16)
        ordered[core, pl.ds(start, rows), :] = mine_ref[mask]
        ordered[1 - core, pl.ds(start, rows), :] = other_ref[mask]
    turned = []
    for half in range(CORES):
        for lane in range(0, pack.model_width, pack.feed_shard):
            turned.append(ordered[half, : pack.down_rows, lane : lane + pack.feed_shard])
    down_ref[...] = jnp.transpose(jnp.concatenate(turned, axis=0)).astype(F32)
    for half in range(CORES):
        for block in range(pack.blocks):
            lane = (half * pack.blocks + block) * pack.model_width
            start = pack.up_at + block * pack.row_shard
            up_ref[:, lane : lane + pack.model_width] = ordered[
                half, start : start + pack.row_shard, :
            ].astype(F32)
        out_ref[half * pack.out_rows : (half + 1) * pack.out_rows, :] = ordered[
            half, pack.out_at : pack.out_at + pack.out_rows, :
        ].astype(F32)


def unpack(pack, depth, meta, mine, other):
    vmem = pl.BlockSpec(memory_space=pltpu.VMEM)
    return pl.pallas_call(
        partial(unpack_kernel, pack, depth),
        in_specs=[IN_SMEM, vmem, vmem],
        out_specs=[vmem] * 3,
        out_shape=[
            jax.ShapeDtypeStruct((pack.feed_shard, pack.model_width), F32),
            jax.ShapeDtypeStruct((pack.row_shard, pack.feed_width), F32),
            jax.ShapeDtypeStruct((pack.row_shard, pack.model_width), F32),
        ],
        scratch_shapes=[pltpu.VMEM((CORES, pack.rows, pack.model_width), BF16)],
        name="unpack",
        compiler_params=pltpu.CompilerParams(vmem_limit_bytes=24 * MIB),
        cost_estimate=pl.CostEstimate(flops=0, bytes_accessed=10_000_000, transcendentals=0),
    )(meta, mine, other)


def unpack_qkv_kernel(meta, mine_ref, other_ref, grad_ref, bias_ref, small_ref):
    member = meta[3]
    row_shard, width = grad_ref.shape[0], grad_ref.shape[1] // 3
    part = mine_ref.shape[1] // 3
    for ref, at in ((mine_ref, member), (other_ref, 1 - member)):
        for kind in range(3):
            lane = pl.multiple_of(kind * width + at * part, CLUSTER_ROWS)
            from_lanes = slice(kind * part, (kind + 1) * part)
            grad_ref[:, pl.ds(lane, part)] = ref[:row_shard, from_lanes].astype(F32)
            lane = pl.multiple_of(at * part, CLUSTER_ROWS)
            bias_ref[kind : kind + 1, pl.ds(lane, part)] = ref[row_shard:, from_lanes].astype(F32)[
                BIAS_ROW : BIAS_ROW + 1
            ]
    small_ref[...] = (mine_ref[row_shard:, :].astype(F32) + other_ref[row_shard:, :].astype(F32))[
        :BIAS_ROW
    ]


def unpack_qkv(meta, mine, other, row_shard):
    cols = mine.shape[1]
    vmem = pl.BlockSpec(memory_space=pltpu.VMEM)
    return pl.pallas_call(
        unpack_qkv_kernel,
        in_specs=[IN_SMEM, vmem, vmem],
        out_specs=[vmem] * 3,
        out_shape=[
            jax.ShapeDtypeStruct((row_shard, CORES * cols), F32),
            jax.ShapeDtypeStruct((3, CORES * cols // 3), F32),
            jax.ShapeDtypeStruct((BIAS_ROW, cols), F32),
        ],
        name="unpack_qkv",
        compiler_params=pltpu.CompilerParams(vmem_limit_bytes=16 * MIB),
        cost_estimate=pl.CostEstimate(flops=0, bytes_accessed=200_000, transcendentals=0),
    )(meta, mine, other)


def tie(*values):
    return lax.optimization_barrier(values)


def body(
    tokens,
    cotangent,
    perms,
    unit_kind,
    w_qkv,
    bias_qv,
    w_out,
    bias_out,
    ln_gain,
    ln_bias,
    w_up,
    bias_up,
    w_down,
    bias_down,
):
    shards = lax.axis_size("fsdp")
    groups = lax.axis_size("dp")
    here = lax.axis_index("fsdp")
    dp_index = lax.axis_index("dp")
    core = dp_index % CORES
    level = dp_index // CORES
    depth = groups // CORES
    units, rounds, unit_len = perms.shape
    per_device = unit_len // shards
    model_width = tokens.shape[1]
    feed_width = w_up.shape[1]
    row_shard = model_width // shards
    members = shards // units
    member_rows = unit_len // members
    head_cols = model_width // members
    padded = -(-head_cols // CLUSTER_ROWS) * CLUSTER_ROWS
    spot = here * CORES + core
    home_core = spot // shards
    unit = (spot // members) % units
    member = spot % members
    pack = Pack(model_width, feed_width, shards, units, depth)
    bits = [1 << k for k in range(shards.bit_length() - 1)]
    bit_orders = (bits, bits[::-1])

    def plane_pairs(target):
        pairs = []
        for z in range(depth):
            for f_index in range(shards):
                for c_index in range(CORES):
                    f_new, c_new = target(f_index, c_index)
                    pairs.append(
                        (
                            (z * CORES + c_index) * shards + f_index,
                            (z * CORES + c_new) * shards + f_new,
                        )
                    )
        return pairs

    def send(value, pairs):
        return lax.ppermute(value, ("dp", "fsdp"), pairs)

    def cross(value, mask):
        return send(value, plane_pairs(lambda f, c: divmod((f * CORES + c) ^ mask, CORES)))

    def trade(value, stage):
        return send(value, plane_pairs(lambda f, c: (f ^ bit_orders[c][stage], c)))

    def trade_mask(index, which):
        mask = 0
        for stage in range(len(bits)):
            if index >> stage & 1:
                mask ^= bit_orders[which][stage]
        return mask

    def climb(value, mask):
        plane = CORES * shards
        pairs = []
        for z in range(depth):
            for rest in range(plane):
                pairs.append((z * plane + rest, (z ^ mask) * plane + rest))
        return send(value, pairs)

    def outward(step):
        def target(f, c):
            place_now = (c * units + (f % units + step) % units) * members + f // units
            return divmod(place_now, CORES)

        return plane_pairs(target)

    def homeward(step):
        return [(b, a) for a, b in outward(step)]

    def bring_start(value):
        blocks = value.reshape(units, per_device, model_width)
        return [
            lax.dynamic_index_in_dim(blocks, (here % units + step) % units, axis=0, keepdims=False)
            for step in range(units)
        ]

    def bring(chosen):
        return jnp.concatenate(
            [send(chosen[step], outward(step)) for step in range(units)], axis=0
        )

    def send_home(value):
        blocks = value.reshape(units, per_device, model_width)
        return [send(blocks[step], homeward(step)) for step in range(units)]

    def in_order(landed, dtype):
        if units == 2:
            swap = here % units == 1
            wanted = [
                jnp.where(swap, landed[1], landed[0]),
                jnp.where(swap, landed[0], landed[1]),
            ]
        else:
            stacked = jnp.stack(landed)
            wanted = [
                lax.dynamic_index_in_dim(stacked, (index - here % units) % units, 0, keepdims=False)
                for index in range(units)
            ]
        return jnp.concatenate(wanted, axis=0).astype(dtype)

    x_chosen = bring_start(tokens)
    x_own = bring(x_chosen)
    small = jnp.concatenate(
        [
            bias_qv.reshape(-1),
            bias_out,
            ln_gain.reshape(-1),
            ln_bias.reshape(-1),
            bias_up,
            bias_down,
        ]
    )
    small_rows = -(-small.shape[0] // (3 * padded))
    small_block = jnp.pad(
        jnp.pad(small, (0, small_rows * 3 * padded - small.shape[0])).reshape(
            small_rows, 3 * padded
        ),
        ((0, 16 - small_rows), (0, 0)),
    )
    def columns_for(offset):
        start = lax.bitwise_xor(member, offset) * head_cols
        blocks = [
            jnp.pad(
                lax.dynamic_slice(
                    w_qkv, (0, kind * model_width + start), (row_shard, head_cols)
                ),
                ((0, 0), (0, padded - head_cols)),
            )
            for kind in range(3)
        ]
        return jnp.concatenate([jnp.concatenate(blocks, axis=1), small_block], axis=0)

    offsets = [(CORES * m) % members for m in range(shards)]
    kinds = sorted(set(offsets))
    order_pack = jnp.concatenate(
        [perms.reshape(-1), jnp.broadcast_to(unit_kind[:, None], (units, 128)).reshape(-1)]
    )
    order_other = cross(order_pack, 1)
    *tied, order_other = tie(*[columns_for(offset) for offset in kinds], order_other)
    piece_kinds = dict(zip(kinds, tied))
    x_pieces = [x_own] + [cross(x_own, mask) for mask in range(1, members)]
    qkv_pieces = [piece_kinds[0]] + [
        cross(piece_kinds[offsets[m]], CORES * m) for m in range(1, shards)
    ]
    order_pack = jnp.where(home_core == core, order_pack, order_other)
    order_count = units * rounds * unit_len
    unit_perm = lax.dynamic_index_in_dim(
        order_pack[:order_count].reshape(units, rounds * unit_len), unit, 0, keepdims=False
    )
    kind_now = lax.dynamic_index_in_dim(
        order_pack[order_count:].reshape(units, 128), unit, 0, keepdims=False
    )[0]
    owner = unit_perm // per_device
    order = (
        lax.bitwise_xor(owner // units, member) * units + (unit - owner % units) % units
    ) * per_device + unit_perm % per_device
    order = order.reshape(rounds, unit_len)
    order = jnp.where(core == 0, order, order[::-1])
    order_row = order.reshape(1, rounds * unit_len)
    order = order.reshape(-1, CLUSTER_ROWS)
    x_here = arrange(order, x_pieces, unit_len, 0)
    x_now = [x_here, cross(x_here, 1)]
    own_masks = [
        jnp.where(core == 0, trade_mask(i, 0), trade_mask(i, 1)) for i in range(1, shards)
    ]
    other_masks = [
        jnp.where(core == 0, trade_mask(i, 1), trade_mask(i, 0)) for i in range(1, shards)
    ]
    zero = jnp.int32(0)
    meta = jnp.stack(
        [kind_now, here, core, member, level, zero, zero, zero] + own_masks + other_masks
    ).astype(jnp.int32)

    def half_of(value, axis, length, at):
        return lax.dynamic_slice_in_dim(value, at * length, length, axis=axis)

    packed = jnp.concatenate(
        [half_of(w_down, 0, pack.down_rows, core)]
        + [
            half_of(w_up, 1, model_width, core * pack.blocks + block)
            for block in range(pack.blocks)
        ]
        + [half_of(w_out, 0, pack.out_rows, core)],
        axis=0,
    )
    order_rows = unit_len // CLUSTER_ROWS
    arranged, probs, mixtures, x_turned = [], [], [], []
    *tied, packed, x_now[0] = tie(*qkv_pieces[1:], packed, x_now[0])
    qkv_pieces = qkv_pieces[:1] + tied
    smalls = jnp.stack(
        [
            piece[row_shard : row_shard + small_rows].reshape(-1)[: small.shape[0]]
            for piece in qkv_pieces
        ]
    )
    smalls = jnp.take(smalls, lax.bitwise_xor(here, jnp.arange(shards)), axis=0).astype(F32)

    def vectors_at(start, count, length):
        part = smalls[:, start * row_shard : start * row_shard + count * length]
        return (
            part.reshape(shards, count, length).transpose(1, 0, 2).reshape(count, shards * length)
        )

    my_bias = lax.dynamic_index_in_dim(
        vectors_at(0, 2, row_shard).reshape(2, members, head_cols), member, 1, keepdims=False
    )
    my_bias = jnp.pad(my_bias, ((0, 0), (0, padded - head_cols)))
    my_bias = jnp.stack([my_bias[0], jnp.zeros_like(my_bias[0]), my_bias[1]]).reshape(1, -1)
    up_bias = vectors_at(7, 1, feed_width // shards)
    down_bias = smalls[:, small.shape[0] - row_shard :].reshape(1, model_width)
    vectors = jnp.concatenate(
        [vectors_at(2, 5, row_shard), down_bias, jnp.zeros((2, model_width), F32)], axis=0
    )

    weight_pieces = {0: packed}
    for stage in range(len(bits)):
        weight_pieces[1 << stage] = trade(packed, stage)
    for index in range(rounds):
        results = attend(meta, x_now[index], my_bias, qkv_pieces, row_shard, mixtures[-1:])
        for kept, result in zip((arranged, probs, mixtures, x_turned), results):
            kept.append(result)
    cot_now, mixtures[0] = tie(cotangent, mixtures[0])
    cot_landed = [
        send(value, outward(step)) for step, value in enumerate(bring_start(cot_now))
    ]
    cot_own = jnp.concatenate(cot_landed, axis=0)
    for stage in range(1, len(bits)):
        for index in range(1, 1 << stage):
            weight_pieces[index | 1 << stage] = trade(weight_pieces[index], stage)
    att_there, att_sent = [], []
    for mask in range(1, members):
        there = place(
            order_row, mixtures, mask * member_rows, member_rows, 0.5, needs=cot_landed
        )
        att_sent.append(there)
        att_there.append(cross(there[:, :head_cols], mask))
    att_here = place(order_row, mixtures, 0, member_rows, 0.5, needs=att_sent)

    direct = [weight_pieces[index] for index in range(1, shards)]
    swapped = [cross(piece, 1) for piece in direct[:-1]]
    last_piece, att_here = tie(direct[-1], att_here)
    swapped.append(cross(last_piece, 1))
    att_raw = [att_here[:, :head_cols]] + att_there
    if head_cols % CLUSTER_ROWS:
        att_raw = [jnp.concatenate(att_raw, axis=1)]
    block_out, first_low, d_branch, d_ffn, hidden, d_pre, d_lower, att_turned, *rest = feed(
        pack,
        meta,
        x_own,
        cot_own,
        vectors,
        up_bias,
        att_raw,
        [w_out, w_up, w_down],
        direct + swapped,
    )
    d_att, (row_sums, up_sums) = rest[: len(att_raw)], rest[len(att_raw) :]
    if head_cols % CLUSTER_ROWS:
        d_att = [d_att[0][:, mask * head_cols : (mask + 1) * head_cols] for mask in range(members)]
    d_att = [d_att[0]] + [cross(d_att[mask], mask) for mask in range(1, members)]
    d_att = [jnp.pad(piece, ((0, 0), (0, padded - head_cols))) for piece in d_att]

    def grads_of(half, *needed):
        table = jnp.stack([half, member]).astype(jnp.int32)
        return weight_grads(
            pack, table, d_ffn, hidden, first_low, d_pre, att_turned, d_branch, needed
        )

    theirs = grads_of(1 - core)
    output_landed = send_home(block_out)
    mine = grads_of(core, theirs)
    theirs = cross(theirs, 1)
    sending = [index for index in range(shards) if index & 1]
    keeping = [index for index in range(shards) if not index & 1]
    slots = jnp.stack(
        [
            lax.bitwise_xor(here, jnp.where(core == 0, trade_mask(i, 0), trade_mask(i, 1)))
            for i in sending + keeping
        ]
    )
    going, kept = add_picked(
        jnp.concatenate([slots, slots]).astype(jnp.int32),
        [mine, theirs],
        shards,
        len(sending),
        output_landed + d_att[1:],
    )

    def merge(kept, landed, *needs):
        count = kept.shape[0]
        if count == 1:
            table = jnp.zeros((2,), jnp.int32)
            return None, add_picked(table, [kept, landed], 1, None, needs)[0]
        order_now = [i for i in range(count) if i & 1] + [i for i in range(count) if not i & 1]
        table = jnp.array(order_now * 2, jnp.int32)
        return add_picked(table, [kept, landed], count, count // 2, needs)

    grads, d_x = [None] * rounds, [None] * rounds
    needs = [going]
    blocks = unit_len // POS_BLOCK
    spans = [(rounds - 1, (0, blocks))]
    for index in reversed(range(rounds - 1)):
        spans += [(index, (0, blocks // 2)), (index, (blocks // 2, blocks))]
    results = []
    for turn, (index, span) in enumerate(spans):
        results = attend_back(
            meta,
            order,
            arranged[index],
            probs[index],
            d_att,
            qkv_pieces,
            row_shard,
            index * order_rows,
            needs,
            span,
            results if span[0] else [],
        )
        grads[index], d_x[index] = results
        if turn < len(bits):
            going, kept = merge(kept, trade(going, turn), results[0])
            needs = [kept]
    for stage in range(len(spans), len(bits)):
        going, kept = merge(kept, trade(going, stage))

    def level_pieces(block):
        return block.reshape((depth, block.shape[0] // depth) + block.shape[1:])

    def level_scatter(cut):
        return [
            climb(
                lax.dynamic_index_in_dim(cut, lax.bitwise_xor(level, mask), 0, keepdims=False), mask
            )
            for mask in range(1, depth)
        ]

    def level_gather(piece):
        pieces = {0: piece}
        mask = depth // 2
        while mask:
            pieces.update({index | mask: climb(held, mask) for index, held in pieces.items()})
            mask //= 2
        return [pieces[index] for index in range(depth)]

    def by_shard(value):
        count, length = value.shape
        return (
            value.reshape(count, shards, length // shards)
            .transpose(1, 0, 2)
            .reshape(shards, count * length // shards)
        )

    small_grad = jnp.concatenate(
        [by_shard(row_sums[:5]), by_shard(up_sums), by_shard(row_sums[5:6])], axis=1
    )
    small_length = small_grad.shape[1]
    small_lanes = 3 * head_cols
    small_grad = jnp.pad(small_grad, ((0, 0), (0, BIAS_ROW * small_lanes - small_length)))
    small_grad = jnp.pad(
        small_grad.reshape(shards, BIAS_ROW, small_lanes), ((0, 0), (0, 16 - BIAS_ROW), (0, 0))
    )
    extra_rows = 16
    x_last, kept, small_grad = tie(x_turned[0], kept, small_grad)
    if padded == head_cols:
        joined = qkv_grads([x_last, x_turned[1]], grads, small_grad, row_shard)
    else:
        qkv_grad = dot(x_last, grads[0]) + dot(x_turned[1], grads[1])
        qkv_grad = qkv_grad.reshape(shards, row_shard, 3, padded)[..., :head_cols]
        bias_sum = sum(jnp.sum(value.astype(F32), axis=0) for value in grads)
        bias_sum = bias_sum.reshape(3, padded)[:, :head_cols].reshape(small_lanes)
        small_grad = small_grad.at[:, BIAS_ROW].set(bias_sum[None])
        joined = jnp.concatenate(
            [qkv_grad.reshape(shards, row_shard, small_lanes), small_grad], axis=1
        ).astype(BF16)
    cut = level_pieces(kept[0])
    landed = level_scatter(cut)
    classes = max(1, members // CORES)
    d_x_parts = [d_x[0], cross(d_x[1], 1)]
    order_mine = order_row[:, :unit_len]
    if classes == 1:
        slots_held = jnp.stack(
            [
                lax.bitwise_xor(here, jnp.where(core == 0, trade_mask(i, 0), trade_mask(i, 1)))
                for i in range(shards)
            ]
        )
        held = jnp.stack(
            [
                lax.dynamic_index_in_dim(joined, slots_held[i], 0, keepdims=False)
                for i in range(0, shards, 2)
            ]
        )
        leaving = jnp.stack(
            [
                lax.dynamic_index_in_dim(joined, slots_held[i], 0, keepdims=False)
                for i in range(1, shards, 2)
            ]
        )
        totals = None
    else:
        totals = [None] * classes
        for m in range(shards):
            offset = offsets[m] // CORES
            piece = lax.dynamic_index_in_dim(joined, lax.bitwise_xor(here, m), 0, keepdims=False)
            piece = (piece if m == 0 else cross(piece, CORES * m)).astype(F32)
            totals[offset] = piece if totals[offset] is None else totals[offset] + piece

    if depth > 1:
        picks = jnp.concatenate([level[None], jnp.zeros((depth - 1,), level.dtype)])
        (kept,) = add_picked(
            picks.astype(jnp.int32),
            [cut] + [piece[None] for piece in landed],
            1,
            None,
            [joined],
        )
    d_there = [
        place(
            order_mine,
            d_x_parts,
            mask * member_rows,
            member_rows,
            added=True,
            needs=[kept],
        )
        for mask in range(1, members)
    ]
    gathered = level_gather(kept[0]) if depth > 1 else [cut[0]]
    early = list(d_there)
    if totals is None:
        leaving, held = merge(held, trade(leaving, 0), *d_there)
        early.append(held)
    d_here = place(
        order_mine,
        d_x_parts,
        0,
        member_rows,
        1.0,
        F32,
        d_lower,
        added=True,
        needs=early,
    )
    d_inputs = d_here
    for mask, there in enumerate(d_there, 1):
        d_inputs = d_inputs + cross(there, mask).astype(F32)
    d_inputs = d_inputs.astype(BF16)
    if totals is None:
        for stage in range(1, len(bits)):
            leaving, held = merge(held, trade(leaving, stage), d_here, gathered[depth // 2])
        totals = [held[0]]
    d_inputs = in_order(send_home(d_inputs), F32)
    output = in_order(output_landed, BF16)
    totals = jnp.concatenate(totals, axis=0).astype(BF16)
    rows_each = row_shard + extra_rows
    mask = 1
    while mask < depth:
        totals = (totals.astype(F32) + climb(totals, mask).astype(F32)).astype(BF16)
        mask *= 2
    stacked = stack_up(gathered, [totals])
    grad_down, grad_up, grad_out = unpack(pack, depth, meta, stacked, cross(stacked, 1))
    if padded == head_cols and members == CORES:
        grad_qkv, bias_out_row, smalls_out = unpack_qkv(
            meta, totals, cross(totals, 1), row_shard
        )
        smalls_out = smalls_out.reshape(-1)[:small_length]
        bias_out_row = lax.dynamic_slice(bias_out_row, (0, here * row_shard), (3, row_shard))
    else:
        landed = jnp.stack([totals, cross(totals, 1)], axis=0).reshape(
            CORES, classes, rows_each, 3 * head_cols
        )
        smalls_out = jnp.sum(
            landed[:, :, row_shard : row_shard + BIAS_ROW].astype(F32), axis=(0, 1)
        ).reshape(-1)[:small_length]
        landed = (
            landed.transpose(1, 0, 2, 3)
            .reshape(members, rows_each, 3, head_cols)[:, : row_shard + BIAS_ROW + 1]
        )
        if members == 2:
            swap = member == 1
            landed = jnp.stack(
                [
                    jnp.where(swap, landed[1], landed[0]),
                    jnp.where(swap, landed[0], landed[1]),
                ]
            )
        else:
            landed = jnp.take(landed, lax.bitwise_xor(member, jnp.arange(members)), axis=0)
        grad_qkv = landed[:, :row_shard].transpose(1, 2, 0, 3)
        grad_qkv = grad_qkv.reshape(row_shard, 3 * model_width).astype(F32)
        bias_out_row = landed[:, row_shard + BIAS_ROW].astype(F32).transpose(1, 0, 2)
        bias_out_row = lax.dynamic_slice(
            bias_out_row.reshape(3, model_width), (0, here * row_shard), (3, row_shard)
        )

    feed_shard = feed_width // shards
    spots = [0, row_shard, 3 * row_shard, 5 * row_shard]
    return (
        output,
        d_inputs,
        grad_qkv,
        bias_out_row[::2],
        grad_out,
        smalls_out[spots[0] : spots[1]],
        smalls_out[spots[1] : spots[2]].reshape(2, row_shard),
        smalls_out[spots[2] : spots[3]].reshape(2, row_shard),
        grad_up,
        smalls_out[spots[3] : spots[3] + feed_shard],
        grad_down,
        smalls_out[spots[3] + feed_shard :],
    )


def solution(mesh):
    placed = (
        P(("dp", "fsdp"), None),
        P(("dp", "fsdp"), None),
        P("dp", None, None),
        P("dp"),
        P("fsdp", None),
        P(None, "fsdp"),
        P("fsdp", None),
        P("fsdp"),
        P(None, "fsdp"),
        P(None, "fsdp"),
        P("fsdp", None),
        P("fsdp"),
        P("fsdp", None),
        P("fsdp"),
    )
    return jax.shard_map(
        body,
        mesh=mesh,
        in_specs=placed,
        out_specs=(
            P(("dp", "fsdp"), None),
            P(("dp", "fsdp"), None),
            P("fsdp", None),
            P(None, "fsdp"),
            P("fsdp", None),
            P("fsdp"),
            P(None, "fsdp"),
            P(None, "fsdp"),
            P("fsdp", None),
            P("fsdp"),
            P("fsdp", None),
            P("fsdp"),
        ),
        check_vma=False,
    )
```

```python
from functools import partial

import jax
import jax.numpy as jnp
from jax import lax
from jax.experimental import pallas as pl
from jax.experimental.pallas import tpu as pltpu
from jax.sharding import PartitionSpec as P

HEAD_DIM = 64
CORES = 2
NEG_FILL = -1000000000.0
EPSILON = 1e-05
SCALE = HEAD_DIM ** (-0.5)
BIAS_ROW = 2
GRAD_LANES = 384
CLUSTER_ROWS = 128
HALF_ROWS = 64
POS_BLOCK = 512
TOKEN_BLOCK = 512
ROW_BLOCK = 512
FF_BLOCK = 512
MIB = 1024 * 1024
NT = (((1,), (1,)), ((), ()))
TN = (((0,), (0,)), ((), ()))
F32 = jnp.float32
BF16 = jnp.bfloat16
ANYWHERE = pl.BlockSpec(memory_space=pl.ANY)
IN_SMEM = pl.BlockSpec(memory_space=pltpu.SMEM)


def whole(shape):
    return pl.BlockSpec(shape, lambda i: (0,) * len(shape))


def rows_of(shape):
    return pl.BlockSpec(shape, lambda i: (i,) + (0,) * (len(shape) - 1))


def dot(a, b, dims=(((1,), (0,)), ((), ()))):
    return lax.dot_general(a, b, dims, preferred_element_type=F32)


def params(mib, flops=0, moved=0, share=16):
    return dict(
        compiler_params=pltpu.CompilerParams(
            dimension_semantics=("arbitrary",),
            vmem_limit_bytes=mib * MIB,
        ),
        cost_estimate=pl.CostEstimate(
            flops=flops // share, bytes_accessed=moved // share, transcendentals=0
        ),
    )


def gated(kernel, used, needs):
    if not needs:
        return kernel

    def run(*refs):
        return kernel(*refs[:used], *refs[used + len(needs) :])

    return run


def lane_masks():
    lane = lax.broadcasted_iota(jnp.int32, (CLUSTER_ROWS, CLUSTER_ROWS), 1)
    low = (lane < HEAD_DIM).astype(F32)
    return low.astype(BF16), (1.0 - low).astype(BF16), lane < HEAD_DIM


def corners(first, second):
    blank = jnp.zeros_like(first)
    return jnp.concatenate(
        [
            jnp.concatenate([first, blank], axis=1),
            jnp.concatenate([blank, second], axis=1),
        ],
        axis=0,
    )


def both_heads(rows_now, low, high):
    return jnp.concatenate([rows_now * low, rows_now * high], axis=0)


def equal_ones(left, right):
    return jnp.where(left == right, jnp.ones((), BF16), jnp.zeros((), BF16))


def pick_rows(order_ref, first_row, unit_len):
    parts = []
    lane = lax.broadcasted_iota(jnp.int16, (CLUSTER_ROWS, CLUSTER_ROWS), 1)
    for part in range(POS_BLOCK // CLUSTER_ROWS):
        row = order_ref[pl.ds(first_row + part, 1), :]
        column = jnp.transpose(jnp.broadcast_to(row, (CLUSTER_ROWS, CLUSTER_ROWS)))
        column = column.astype(jnp.int16)
        pieces = [
            equal_ones(column, lane + jnp.int16(base)) for base in range(0, unit_len, CLUSTER_ROWS)
        ]
        parts.append(jnp.concatenate(pieces, axis=1))
    return jnp.concatenate(parts, axis=0)


def load_pieces(meta, x_refs, w_refs, x_all, w_all, sems, row_shard):
    member_rows = x_all.shape[0] // max(1, len(x_refs))
    copies = []
    for index, ref in enumerate(x_refs):
        copies.append(
            pltpu.make_async_copy(
                ref, x_all.at[pl.ds(index * member_rows, member_rows), :], sems.at[index]
            )
        )
    for index, ref in enumerate(w_refs):
        start = pl.multiple_of(lax.bitwise_xor(meta[1], index) * row_shard, 16)
        copies.append(
            pltpu.make_async_copy(
                ref.at[pl.ds(0, row_shard), :],
                w_all.at[pl.ds(start, row_shard), :],
                sems.at[len(x_refs) + index],
            )
        )
    for copy in copies:
        copy.start()
    for copy in copies:
        copy.wait()


def arrange_kernel(unit_len, first_row, order_ref, *refs):
    x_refs, out_ref = refs[:-1], refs[-1]
    step = pl.program_id(0)
    picks = pick_rows(order_ref, first_row + step * (POS_BLOCK // CLUSTER_ROWS), unit_len)
    rows = x_refs[0].shape[0]
    total = None
    for index, ref in enumerate(x_refs):
        term = dot(picks[:, index * rows : (index + 1) * rows], ref[...])
        total = term if total is None else total + term
    out_ref[...] = total.astype(BF16)


def arrange(order, x_pieces, position_count, first_row):
    member_rows, width = x_pieces[0].shape
    unit_len = member_rows * len(x_pieces)
    return pl.pallas_call(
        partial(arrange_kernel, unit_len, first_row),
        grid=(position_count // POS_BLOCK,),
        in_specs=[whole(order.shape)] + [whole(piece.shape) for piece in x_pieces],
        out_specs=rows_of((POS_BLOCK, width)),
        out_shape=jax.ShapeDtypeStruct((position_count, width), BF16),
        name="arrange",
        **params(20, 2 * position_count * unit_len * width, 6_000_000),
    )(order, *x_pieces)


def attend_kernel(sizes, meta, x_now_ref, bias_ref, *refs):
    shards, row_shard = sizes
    w_refs, refs = refs[:shards], refs[shards:]
    arranged_ref, probs_ref, mixture_ref, turned_ref, w_all, sems = refs
    width = w_all.shape[1] // 3
    step = pl.program_id(0)

    @pl.when(step == 0)
    def _():
        load_pieces(meta, [], w_refs, w_all, w_all, sems, row_shard)

    x_now = x_now_ref[...]
    turned_ref[...] = jnp.transpose(x_now)
    arranged = (dot(x_now, w_all[...]) + bias_ref[...]).astype(BF16)
    arranged_ref[...] = arranged
    low, high, lane_low = lane_masks()
    position = lax.broadcasted_iota(jnp.int32, (CLUSTER_ROWS, CLUSTER_ROWS), 0)
    other = lax.broadcasted_iota(jnp.int32, (CLUSTER_ROWS, CLUSTER_ROWS), 1)
    same_half = (position < HALF_ROWS) == (other < HALF_ROWS)
    allowed = jnp.logical_or(same_half, meta[0] == 1)
    pairs = width // CLUSTER_ROWS
    units = [(part, pair) for part in range(POS_BLOCK // CLUSTER_ROWS) for pair in range(pairs)]
    for index in range(0, len(units), 2):
        queries, keys, values = [], [], []
        for part, pair in units[index : index + 2]:
            rows_now = slice(part * CLUSTER_ROWS, (part + 1) * CLUSTER_ROWS)
            base = pair * CLUSTER_ROWS
            queries.append(arranged[rows_now, base : base + CLUSTER_ROWS] * SCALE)
            one_key = arranged[rows_now, width + base : width + base + CLUSTER_ROWS]
            keys.append(both_heads(one_key, low, high))
            one_value = arranged[rows_now, 2 * width + base : 2 * width + base + CLUSTER_ROWS]
            values.append(both_heads(one_value, low, high))
        both_scores = dot(jnp.concatenate(keys, axis=1), corners(*queries), NT)
        for which, (part, pair) in enumerate(units[index : index + 2]):
            halves = []
            for head in range(2):
                one = both_scores[
                    head * CLUSTER_ROWS : (head + 1) * CLUSTER_ROWS,
                    which * CLUSTER_ROWS : (which + 1) * CLUSTER_ROWS,
                ]
                one = jnp.where(allowed, one, NEG_FILL)
                grown = jnp.exp(one - jnp.max(one, axis=0, keepdims=True))
                halves.append(grown * (1.0 / jnp.sum(grown, axis=0, keepdims=True)))
            probs = jnp.concatenate(halves, axis=0).astype(BF16)
            at = (part * pairs + pair) * 2 * CLUSTER_ROWS
            probs_ref[at : at + 2 * CLUSTER_ROWS, :] = probs
            mixture_ref[
                part * CLUSTER_ROWS : (part + 1) * CLUSTER_ROWS,
                pair * CLUSTER_ROWS : (pair + 1) * CLUSTER_ROWS,
            ] = dot(probs, values[which], TN).astype(BF16)


def attend(meta, x_now, bias, w_pieces, row_shard, needs=()):
    shards = len(w_pieces)
    position_count, model_width = x_now.shape
    cols = w_pieces[0].shape[1]
    width = cols // 3
    pair_rows = 2 * width
    return pl.pallas_call(
        gated(partial(attend_kernel, (shards, row_shard)), 3 + shards, needs),
        grid=(position_count // POS_BLOCK,),
        in_specs=[IN_SMEM, rows_of((POS_BLOCK, model_width)), whole(bias.shape)]
        + [ANYWHERE] * (shards + len(needs)),
        out_specs=[
            rows_of((POS_BLOCK, cols)),
            rows_of((POS_BLOCK // CLUSTER_ROWS * pair_rows, CLUSTER_ROWS)),
            rows_of((POS_BLOCK, width)),
            pl.BlockSpec((model_width, POS_BLOCK), lambda i: (0, i)),
        ],
        out_shape=[
            jax.ShapeDtypeStruct((position_count, cols), BF16),
            jax.ShapeDtypeStruct((position_count // CLUSTER_ROWS * pair_rows, CLUSTER_ROWS), BF16),
            jax.ShapeDtypeStruct((position_count, width), BF16),
            jax.ShapeDtypeStruct((model_width, position_count), BF16),
        ],
        scratch_shapes=[
            pltpu.VMEM((model_width, cols), BF16),
            pltpu.SemaphoreType.DMA((shards,)),
        ],
        name="attend",
        **params(
            48, 8 * position_count * (model_width * cols + 4 * CLUSTER_ROWS * width), 18_000_000, 1
        ),
    )(meta, x_now, bias, *w_pieces, *needs)


def place_kernel(sizes, scale, has_base, order_row_ref, *refs):
    unit_len, first_token, added = sizes
    base_ref = refs[0] if has_base else None
    refs = refs[1 if has_base else 0 :]
    if added:
        first_ref, second_ref, out_ref, held = refs

        @pl.when(pl.program_id(0) == 0)
        def _():
            held[...] = (first_ref[...].astype(F32) + second_ref[...].astype(F32)).astype(BF16)

        source_refs = [held]
    else:
        source_refs, out_ref = refs[:-1], refs[-1]
    block_rows = out_ref.shape[0]
    first = jnp.full((1, 1), first_token + pl.program_id(0) * block_rows, jnp.int32)
    token = lax.broadcasted_iota(jnp.int16, (block_rows, unit_len), 0)
    total = None
    for index, ref in enumerate(source_refs):
        row = order_row_ref[:, index * unit_len : (index + 1) * unit_len] - first
        row = jnp.broadcast_to(row, (16, unit_len)).astype(jnp.int16)
        row = jnp.concatenate([row] * (block_rows // 16), axis=0)
        term = dot(equal_ones(row, token), ref[...])
        total = term if total is None else total + term
    if scale != 1.0:
        total = total * scale
    if has_base:
        total = total + base_ref[...]
    out_ref[...] = total.astype(out_ref.dtype)


def place(
    order_row,
    sources,
    first_token,
    row_count,
    scale=1.0,
    dtype=BF16,
    base=None,
    added=False,
    needs=(),
):
    unit_len, width = sources[0].shape
    block_rows = min(TOKEN_BLOCK, row_count)
    extra = [] if base is None else [base]
    return pl.pallas_call(
        gated(
            partial(place_kernel, (unit_len, first_token, added), scale, base is not None),
            1 + len(extra) + len(sources),
            needs,
        ),
        grid=(row_count // block_rows,),
        in_specs=[whole(order_row.shape)]
        + [rows_of((block_rows, width))] * len(extra)
        + [whole(source.shape) for source in sources]
        + [ANYWHERE] * len(needs),
        out_specs=rows_of((block_rows, width)),
        out_shape=jax.ShapeDtypeStruct((row_count, width), dtype),
        scratch_shapes=[pltpu.VMEM((unit_len, width), BF16)] if added else [],
        name="place",
        **params(
            32 if added else 20,
            16 * row_count * unit_len * width,
            10_000_000,
            1,
        ),
    )(order_row, *extra, *sources, *needs)


def attend_back_kernel(sizes, meta, order_ref, arranged_ref, probs_ref, *refs):
    members, shards, unit_len, row_shard, first_row, start = sizes
    g_refs, refs = refs[:members], refs[members:]
    w_refs, refs = refs[:shards], refs[shards:]
    grads_ref, d_x_ref, g_all, w_all, sems = refs
    width = w_all.shape[1] // 3
    step = pl.program_id(0)

    @pl.when(step == 0)
    def _():
        load_pieces(meta, g_refs, w_refs, g_all, w_all, sems, row_shard)

    at_row = first_row + (start + step) * (POS_BLOCK // CLUSTER_ROWS)
    picks = pick_rows(order_ref, at_row, unit_len)
    d_mixture = dot(picks, g_all[...]).astype(BF16)
    low, high, lane_low = lane_masks()
    pairs = width // CLUSTER_ROWS
    units = [(part, pair) for part in range(POS_BLOCK // CLUSTER_ROWS) for pair in range(pairs)]
    for index in range(0, len(units), 2):
        values, d_rows = [], []
        for part, pair in units[index : index + 2]:
            rows_now = slice(part * CLUSTER_ROWS, (part + 1) * CLUSTER_ROWS)
            base = pair * CLUSTER_ROWS
            one_value = arranged_ref[rows_now, 2 * width + base : 2 * width + base + CLUSTER_ROWS]
            values.append(both_heads(one_value, low, high))
            d_rows.append(d_mixture[rows_now, base : base + CLUSTER_ROWS])
        both_probs = dot(jnp.concatenate(values, axis=1), corners(*d_rows), NT)
        for which, (part, pair) in enumerate(units[index : index + 2]):
            rows_now = slice(part * CLUSTER_ROWS, (part + 1) * CLUSTER_ROWS)
            base = pair * CLUSTER_ROWS
            q_lanes = slice(base, base + CLUSTER_ROWS)
            k_lanes = slice(width + base, width + base + CLUSTER_ROWS)
            v_lanes = slice(2 * width + base, 2 * width + base + CLUSTER_ROWS)
            queries = arranged_ref[rows_now, q_lanes] * SCALE
            keys = arranged_ref[rows_now, k_lanes] * SCALE
            at = (part * pairs + pair) * 2 * CLUSTER_ROWS
            probs = probs_ref[at : at + 2 * CLUSTER_ROWS, :]
            d_probs = both_probs[:, which * CLUSTER_ROWS : (which + 1) * CLUSTER_ROWS]
            pieces = []
            for head in range(2):
                rows = slice(head * CLUSTER_ROWS, (head + 1) * CLUSTER_ROWS)
                weight = probs[rows].astype(F32)
                d_one = d_probs[rows]
                inner = jnp.sum(weight * d_one, axis=0, keepdims=True)
                pieces.append(weight * (d_one - inner))
            d_scores = jnp.concatenate(pieces, axis=0).astype(BF16)
            d_query = dot(d_scores, both_heads(keys, low, high), TN)
            d_pair = dot(
                jnp.concatenate([probs, d_scores], axis=1), corners(d_rows[which], queries)
            )
            d_values, d_keys = d_pair[:, :CLUSTER_ROWS], d_pair[:, CLUSTER_ROWS:]
            grads_ref[rows_now, q_lanes] = d_query.astype(BF16)
            grads_ref[rows_now, k_lanes] = jnp.where(
                lane_low, d_keys[:CLUSTER_ROWS], d_keys[CLUSTER_ROWS:]
            ).astype(BF16)
            grads_ref[rows_now, v_lanes] = jnp.where(
                lane_low, d_values[:CLUSTER_ROWS], d_values[CLUSTER_ROWS:]
            ).astype(BF16)
    grads = grads_ref[...]
    d_x_ref[...] = dot(grads, w_all[...], NT).astype(BF16)


def attend_back(
    meta, order, arranged, probs, g_pieces, w_pieces, row_shard, first_row, needs, span, into
):
    members, shards = len(g_pieces), len(w_pieces)
    member_rows, width = g_pieces[0].shape
    unit_len = members * member_rows
    position_count, cols = arranged.shape
    model_width = row_shard * shards
    start, stop = span
    pair_rows = POS_BLOCK // CLUSTER_ROWS * 2 * width
    used = 4 + members + shards

    def block(shape):
        return pl.BlockSpec(shape, lambda i: (start + i, 0))

    return pl.pallas_call(
        gated(
            partial(attend_back_kernel, (members, shards, unit_len, row_shard, first_row, start)),
            used,
            list(into) + list(needs),
        ),
        grid=(stop - start,),
        in_specs=[
            IN_SMEM,
            whole(order.shape),
            block((POS_BLOCK, cols)),
            block((pair_rows, CLUSTER_ROWS)),
        ]
        + [ANYWHERE] * (members + shards + len(into) + len(needs)),
        out_specs=[block((POS_BLOCK, cols)), block((POS_BLOCK, model_width))],
        out_shape=[
            jax.ShapeDtypeStruct((position_count, cols), BF16),
            jax.ShapeDtypeStruct((position_count, model_width), BF16),
        ],
        input_output_aliases={used + index: index for index in range(len(into))},
        scratch_shapes=[
            pltpu.VMEM((unit_len, width), BF16),
            pltpu.VMEM((model_width, cols), BF16),
            pltpu.SemaphoreType.DMA((members + shards,)),
        ],
        name="attend_back",
        **params(
            48,
            12 * (stop - start) * POS_BLOCK * (unit_len * width + model_width * cols),
            20_000_000,
            1,
        ),
    )(meta, order, arranged, probs, *g_pieces, *w_pieces, *into, *needs)


def normalise(summed):
    average = jnp.mean(summed, axis=-1, keepdims=True)
    centred = summed - average
    spread = jnp.mean(centred * centred, axis=-1, keepdims=True)
    scale_inv = lax.rsqrt(spread + EPSILON)
    return centred * scale_inv, scale_inv


def normalise_back(grad_out, normed, scale_inv, gain_row):
    scaled = grad_out * gain_row
    return scale_inv * (
        scaled
        - jnp.mean(scaled, axis=-1, keepdims=True)
        - normed * jnp.mean(scaled * normed, axis=-1, keepdims=True)
    )


def column_sum(rows_now):
    return jnp.sum(rows_now, axis=0, keepdims=True)


def gelu_parts(value):
    below = 0.5 + 0.5 * lax.erf(value * 0.7071067811865476)
    bell = jnp.exp(value * value * -0.5) * 0.3989422804014327
    return value * below, below + value * bell


class Pack:
    def __init__(self, model_width, feed_width, shards, units, depth):
        self.model_width, self.feed_width, self.shards = model_width, feed_width, shards
        self.row_shard = model_width // shards
        self.feed_shard = feed_width // shards
        self.down_rows = self.feed_shard // CORES
        self.blocks = feed_width // CORES // model_width
        self.up_at = self.down_rows
        self.out_at = self.up_at + self.blocks * self.row_shard
        self.out_rows = self.row_shard // CORES
        self.used = self.out_at + self.out_rows
        unit = 16 * depth
        self.rows = -(-self.used // unit) * unit
        self.rest_rows = self.rows - self.down_rows
        self.units = units
        self.group = units * self.row_shard

    def out_start(self, shard, member):
        return (
            lax.bitwise_xor(jnp.int32(shard) // self.units, member) * self.group
            + (shard % self.units) * self.row_shard
        )


def feed_kernel(pack, att_count, meta, x_ref, cot_ref, vec_ref, up_bias_ref, *refs):
    shards = pack.shards
    att_refs, refs = refs[:att_count], refs[att_count:]
    own_out, own_up, own_down = refs[:3]
    refs = refs[3:]
    pieces, refs = refs[: 2 * (shards - 1)], refs[2 * (shards - 1) :]
    out_ref, first_turned_ref, d_branch_ref, d_ffn_turned_ref, hidden_ref, d_pre_ref = refs[:6]
    d_h1_ref, att_turned_ref = refs[6:8]
    refs = refs[8:]
    d_att_refs, refs = refs[:att_count], refs[att_count:]
    sums_ref, up_sums_ref, w_out, w_up, w_down, slope, sems = refs
    step = pl.program_id(0)
    here, core, member = meta[1], meta[2], meta[3]
    feed_width = pack.feed_width

    def loads(kind):
        copies = []

        def add(source, target):
            copies.append(pltpu.make_async_copy(source, target, sems.at[kind, len(copies)]))

        if kind == 0:
            start = pl.multiple_of(pack.out_start(here, member), 16)
            add(own_out, w_out.at[pl.ds(start, pack.row_shard), :])
        elif kind == 1:
            start = pl.multiple_of(here * pack.row_shard, 16)
            add(own_up, w_up.at[pl.ds(start, pack.row_shard), :])
        else:
            start = pl.multiple_of(here * pack.feed_shard, 16)
            add(own_down, w_down.at[pl.ds(start, pack.feed_shard), :])
        for index, ref in enumerate(pieces):
            peer = lax.bitwise_xor(here, meta[8 + index])
            half = core if index < shards - 1 else 1 - core
            if kind == 0:
                start = pack.out_start(peer, member) + half * pack.out_rows
                start = pl.multiple_of(start, 16)
                add(
                    ref.at[pl.ds(pack.out_at, pack.out_rows), :],
                    w_out.at[pl.ds(start, pack.out_rows), :],
                )
            elif kind == 1:
                start = pl.multiple_of(peer * pack.row_shard, 16)
                for block in range(pack.blocks):
                    lane = pl.multiple_of(
                        (half * pack.blocks + block) * pack.model_width, CLUSTER_ROWS
                    )
                    add(
                        ref.at[pl.ds(pack.up_at + block * pack.row_shard, pack.row_shard), :],
                        w_up.at[pl.ds(start, pack.row_shard), pl.ds(lane, pack.model_width)],
                    )
            else:
                start = pl.multiple_of(peer * pack.feed_shard + half * pack.down_rows, 16)
                add(
                    ref.at[pl.ds(0, pack.down_rows), :],
                    w_down.at[pl.ds(start, pack.down_rows), :],
                )
        return copies

    @pl.when(step == 0)
    def _():
        for kind in range(3):
            for copy in loads(kind):
                copy.start()
        sums_ref[...] = jnp.zeros_like(sums_ref)
        up_sums_ref[...] = jnp.zeros_like(up_sums_ref)
        for copy in loads(0):
            copy.wait()

    bias_out, gain_one, gain_two = vec_ref[0:1, :], vec_ref[1:2, :], vec_ref[2:3, :]
    shift_one, shift_two, bias_down = vec_ref[3:4, :], vec_ref[4:5, :], vec_ref[5:6, :]
    att_width = att_refs[0].shape[1]
    summed = x_ref[...].astype(F32) + bias_out
    for index, ref in enumerate(att_refs):
        summed += dot(ref[...], w_out[index * att_width : (index + 1) * att_width, :])
    normed_one, inv_one = normalise(summed)
    first = normed_one * gain_one + shift_one
    first_low = first.astype(BF16)
    first_turned_ref[...] = jnp.transpose(first_low)
    for index, ref in enumerate(att_refs):
        att_turned_ref[index * att_width : (index + 1) * att_width, :] = jnp.transpose(ref[...])

    @pl.when(step == 0)
    def _():
        for kind in (1, 2):
            for copy in loads(kind):
                copy.wait()

    second = first + bias_down
    starts = list(range(0, feed_width, FF_BLOCK))

    def raised(base):
        lanes = slice(base, base + FF_BLOCK)
        return dot(first_low, w_up[:, lanes]) + up_bias_ref[:, lanes]

    pre = raised(starts[0])
    for index, base in enumerate(starts):
        lanes = slice(base, base + FF_BLOCK)
        pre_next = raised(starts[index + 1]) if index + 1 < len(starts) else None
        hidden, slope_now = gelu_parts(pre)
        hidden = hidden.astype(BF16)
        hidden_ref[:, lanes] = hidden
        slope[:, lanes] = slope_now
        second += dot(hidden, w_down[lanes, :])
        pre = pre_next
    normed_two, inv_two = normalise(second)
    out_ref[...] = (normed_two * gain_two + shift_two).astype(BF16)
    top = cot_ref[...].astype(F32)
    d_second = normalise_back(top, normed_two, inv_two, gain_two)
    d_ffn = d_second.astype(BF16)
    d_ffn_turned_ref[...] = jnp.transpose(d_ffn)
    d_first = d_second
    d_hidden = dot(d_ffn, w_down[0:FF_BLOCK, :], NT)
    for index, base in enumerate(starts):
        lanes = slice(base, base + FF_BLOCK)
        if index + 1 < len(starts):
            d_next = dot(d_ffn, w_down[starts[index + 1] : starts[index + 1] + FF_BLOCK, :], NT)
        d_pre = (d_hidden * slope[:, lanes]).astype(BF16)
        d_pre_ref[:, lanes] = d_pre
        up_sums_ref[:, lanes] += column_sum(d_pre.astype(F32))
        d_first += dot(d_pre, w_up[:, lanes], NT)
        d_hidden = d_next
    d_lower = normalise_back(d_first, normed_one, inv_one, gain_one)
    d_h1_ref[...] = d_lower
    d_branch = d_lower.astype(BF16)
    d_branch_ref[...] = d_branch
    for index, ref in enumerate(d_att_refs):
        back = dot(d_branch, w_out[index * att_width : (index + 1) * att_width, :], NT)
        ref[...] = (0.5 * back).astype(BF16)
    sums_ref[0:1, :] += column_sum(d_branch.astype(F32))
    sums_ref[1:2, :] += column_sum(d_first * normed_one)
    sums_ref[2:3, :] += column_sum(top * normed_two)
    sums_ref[3:4, :] += column_sum(d_first)
    sums_ref[4:5, :] += column_sum(top)
    sums_ref[5:6, :] += column_sum(d_ffn.astype(F32))


def feed(pack, meta, x_own, cot_own, vectors, up_bias, att, own, pieces):
    row_count, model_width = x_own.shape
    feed_width = pack.feed_width
    att_width = att[0].shape[1]
    one = rows_of((ROW_BLOCK, model_width))
    wide = rows_of((ROW_BLOCK, feed_width))
    narrow = rows_of((ROW_BLOCK, att_width))
    turned = pl.BlockSpec((model_width, ROW_BLOCK), lambda i: (0, i))
    turned_shape = jax.ShapeDtypeStruct((model_width, row_count), BF16)

    def like(width, dtype=BF16):
        return jax.ShapeDtypeStruct((row_count, width), dtype)

    return pl.pallas_call(
        partial(feed_kernel, pack, len(att)),
        grid=(row_count // ROW_BLOCK,),
        in_specs=[IN_SMEM, one, one, whole(vectors.shape), whole(up_bias.shape)]
        + [narrow] * len(att)
        + [ANYWHERE] * (3 + len(pieces)),
        out_specs=[one, turned, one, turned, wide, wide, one, turned]
        + [narrow] * len(att)
        + [whole((8, model_width)), whole((1, feed_width))],
        out_shape=[
            like(model_width),
            turned_shape,
            like(model_width),
            turned_shape,
            like(feed_width),
            like(feed_width),
            like(model_width, F32),
            turned_shape,
        ]
        + [like(att_width)] * len(att)
        + [
            jax.ShapeDtypeStruct((8, model_width), F32),
            jax.ShapeDtypeStruct((1, feed_width), F32),
        ],
        scratch_shapes=[
            pltpu.VMEM((model_width, model_width), BF16),
            pltpu.VMEM((model_width, feed_width), BF16),
            pltpu.VMEM((feed_width, model_width), BF16),
            pltpu.VMEM((ROW_BLOCK, feed_width), F32),
            pltpu.SemaphoreType.DMA((3, 1 + pack.blocks * len(pieces))),
        ],
        name="feed",
        **params(
            60, 2 * row_count * model_width * (2 * model_width + 4 * feed_width), 40_000_000
        ),
    )(meta, x_own, cot_own, vectors, up_bias, *att, *own, *pieces)


def down_grads_kernel(pack, table, d_ffn_ref, hidden_ref, theirs_ref, mine_ref, made, sems):
    step = pl.program_id(0)
    core = table[0]

    def stores(shard):
        return [
            pltpu.make_async_copy(made.at[1 - core, shard], theirs_ref.at[shard], sems.at[0, shard]),
            pltpu.make_async_copy(made.at[core, shard], mine_ref.at[shard], sems.at[1, shard]),
        ]

    grad = dot(d_ffn_ref[...], hidden_ref[...]).astype(BF16)
    for half in range(CORES):
        for lane in range(0, pack.model_width, pack.feed_shard):
            begin = half * (pack.model_width // CORES) + lane // pack.feed_shard * pack.down_rows
            made[half, step, :, lane : lane + pack.feed_shard] = grad[
                begin : begin + pack.down_rows
            ]
    for copy in stores(step):
        copy.start()

    @pl.when(step == pack.shards - 1)
    def _():
        for shard in range(pack.shards):
            for copy in stores(shard):
                copy.wait()


def down_grads(pack, table, d_ffn, hidden):
    model_width, row_count = d_ffn.shape
    shape = (pack.shards, pack.down_rows, model_width)
    return pl.pallas_call(
        partial(down_grads_kernel, pack),
        grid_spec=pltpu.PrefetchScalarGridSpec(
            num_scalar_prefetch=1,
            grid=(pack.shards,),
            in_specs=[
                pl.BlockSpec(d_ffn.shape, lambda step, table: (0, 0)),
                pl.BlockSpec((row_count, pack.feed_shard), lambda step, table: (0, step)),
            ],
            out_specs=[ANYWHERE] * 2,
            scratch_shapes=[
                pltpu.VMEM((CORES,) + shape, BF16),
                pltpu.SemaphoreType.DMA((CORES, pack.shards)),
            ],
        ),
        out_shape=[jax.ShapeDtypeStruct(shape, BF16)] * 2,
        name="down_grads",
        **params(60, 2 * row_count * model_width * pack.feed_width, 10_000_000),
    )(table, d_ffn, hidden)


def rest_grads_kernel(
    pack, table, first_ref, d_pre_ref, att_ref, d_branch_ref, theirs_ref, mine_ref, *scratch
):
    att, d_branch, tile, made, in_sems, sems = scratch
    step = pl.program_id(0)
    core, member = table[0], table[1]
    shards, blocks = pack.shards, pack.blocks
    out_at = pack.out_at - pack.down_rows

    loads = [
        pltpu.make_async_copy(att_ref, att, in_sems.at[0]),
        pltpu.make_async_copy(d_branch_ref, d_branch, in_sems.at[1]),
    ]

    def store(half, start, rows, sem):
        there = (slice(None), pl.ds(start, rows), slice(None))

        def copy(target):
            return pltpu.make_async_copy(
                made.at[(half,) + there], target.at[there], sems.at[half, sem]
            )

        return copy

    def both(half, start, rows, sem, act):
        copy = store(half, start, rows, sem)

        @pl.when(core == half)
        def _():
            act(copy(mine_ref))

        @pl.when(core != half)
        def _():
            act(copy(theirs_ref))

    @pl.when(step == 0)
    def _():
        for copy in loads:
            copy.start()

    @pl.when(step < CORES * blocks)
    def _():
        grad = dot(first_ref[...], d_pre_ref[...]).astype(BF16)
        start = pl.multiple_of(step % blocks * pack.row_shard, 16)
        for shard in range(shards):
            made[step // blocks, shard, pl.ds(start, pack.row_shard), :] = grad[
                shard * pack.row_shard : (shard + 1) * pack.row_shard
            ]

    for half in range(CORES):

        @pl.when(step == (half + 1) * blocks - 1)
        def _(half=half):
            both(half, 0, out_at, 0, lambda copy: copy.start())

    @pl.when(step == CORES * blocks)
    def _():
        for copy in loads:
            copy.wait()
        tile[...] = dot(att[...], d_branch[...])
        spare = pack.rows - pack.used
        for half in range(CORES):
            for shard in range(shards):
                start = pack.out_start(shard, member) + half * pack.out_rows
                start = pl.multiple_of(start, 16)
                made[half, shard, out_at : out_at + pack.out_rows, :] = tile[
                    pl.ds(start, pack.out_rows), :
                ].astype(BF16)
                if spare:
                    made[half, shard, out_at + pack.out_rows :, :] = jnp.zeros(
                        (spare, pack.model_width), BF16
                    )
            both(half, out_at, pack.rest_rows - out_at, 1, lambda copy: copy.start())
        for half in range(CORES):
            both(half, 0, out_at, 0, lambda copy: copy.wait())
            both(half, out_at, pack.rest_rows - out_at, 1, lambda copy: copy.wait())


def rest_grads(pack, table, first_low, d_pre, att, d_branch, needs=()):
    model_width, row_count = first_low.shape
    shape = (pack.shards, pack.rest_rows, model_width)
    steps = CORES * pack.blocks
    return pl.pallas_call(
        gated(partial(rest_grads_kernel, pack), 5, needs),
        grid_spec=pltpu.PrefetchScalarGridSpec(
            num_scalar_prefetch=1,
            grid=(steps + 1,),
            in_specs=[
                pl.BlockSpec(first_low.shape, lambda step, table: (0, 0)),
                pl.BlockSpec(
                    (row_count, model_width),
                    lambda step, table: (0, jnp.minimum(step, steps - 1)),
                ),
            ]
            + [ANYWHERE] * (2 + len(needs)),
            out_specs=[ANYWHERE] * 2,
            scratch_shapes=[
                pltpu.VMEM((model_width, row_count), BF16),
                pltpu.VMEM((row_count, model_width), BF16),
                pltpu.VMEM((model_width, model_width), F32),
                pltpu.VMEM((CORES,) + shape, BF16),
                pltpu.SemaphoreType.DMA((2,)),
                pltpu.SemaphoreType.DMA((CORES, 2)),
            ],
        ),
        out_shape=[jax.ShapeDtypeStruct(shape, BF16)] * 2,
        name="rest_grads",
        **params(60, 2 * row_count * model_width * (pack.feed_width + model_width), 10_000_000),
    )(table, first_low, d_pre, att, d_branch, *needs)


def qkv_grads_kernel(rounds, x_refs_then, *refs):
    refs = (x_refs_then,) + refs
    x_refs, grad_refs = refs[:rounds], refs[rounds : 2 * rounds]
    small_ref, out_ref = refs[2 * rounds :]
    shards, rows, _ = out_ref.shape
    row_shard = rows - small_ref.shape[1]
    total, sums = None, None
    for x_ref, grad_ref in zip(x_refs, grad_refs):
        grads = grad_ref[...]
        term = dot(x_ref[...], grads)
        down = column_sum(grads.astype(F32))
        total = term if total is None else total + term
        sums = down if sums is None else sums + down
    total = total.astype(BF16)
    row = lax.broadcasted_iota(jnp.int32, small_ref.shape[1:], 0)
    for shard in range(shards):
        out_ref[shard, :row_shard, :] = total[shard * row_shard : (shard + 1) * row_shard]
        last = jnp.where(row == BIAS_ROW, sums, small_ref[shard])
        out_ref[shard, row_shard:, :] = last.astype(BF16)


def qkv_grads(x_turned, grads, small, row_shard, needs=()):
    rounds = len(grads)
    model_width, positions = x_turned[0].shape
    cols = grads[0].shape[1]
    shards, extra, _ = small.shape
    block = GRAD_LANES if cols % GRAD_LANES == 0 else cols
    return pl.pallas_call(
        gated(partial(qkv_grads_kernel, rounds), 2 * rounds + 1, needs),
        grid=(cols // block,),
        in_specs=[whole((model_width, positions))] * rounds
        + [pl.BlockSpec((positions, block), lambda i: (0, i))] * rounds
        + [pl.BlockSpec((shards, extra, block), lambda i: (0, 0, i))]
        + [ANYWHERE] * len(needs),
        out_specs=pl.BlockSpec((shards, row_shard + extra, block), lambda i: (0, 0, i)),
        out_shape=jax.ShapeDtypeStruct((shards, row_shard + extra, cols), BF16),
        name="qkv_grads",
        **params(28, 2 * rounds * positions * model_width * cols, 18_000_000),
    )(*x_turned, *grads, small, *needs)


def add_picked_kernel(count, first, table, *refs):
    in_refs, out_refs = refs[:count], refs[count:]
    if count == 2:
        total = in_refs[0][...] + in_refs[1][...]
    else:
        total = in_refs[0][...].astype(F32)
        for ref in in_refs[1:]:
            total = total + ref[...].astype(F32)
        total = total.astype(BF16)
    if len(out_refs) == 1:
        out_refs[0][...] = total
        return

    @pl.when(pl.program_id(0) < first)
    def _():
        out_refs[0][...] = total

    @pl.when(pl.program_id(0) >= first)
    def _():
        out_refs[1][...] = total


def add_picked(table, arrays, steps, first=None, needs=(), work=0):
    _, rows, cols = arrays[0].shape
    parts = 2 if rows % 32 == 0 else 1
    block = (1, rows // parts, cols)
    spec = [
        pl.BlockSpec(block, lambda s, p, t, k=k: (t[k * steps + s], p, 0))
        for k in range(len(arrays))
    ]
    if first is None:
        out_specs = [pl.BlockSpec(block, lambda s, p, t: (s, p, 0))]
        counts = [steps]
    else:
        out_specs = [
            pl.BlockSpec(
                block,
                lambda s, p, t: (
                    jnp.minimum(s, first - 1),
                    jnp.where(s < first, p, parts - 1),
                    0,
                ),
            ),
            pl.BlockSpec(
                block,
                lambda s, p, t: (jnp.maximum(s - first, 0), jnp.where(s < first, 0, p), 0),
            ),
        ]
        counts = [first, steps - first]
    return pl.pallas_call(
        gated(partial(add_picked_kernel, len(arrays), first), 1 + len(arrays), needs),
        grid_spec=pltpu.PrefetchScalarGridSpec(
            num_scalar_prefetch=1,
            grid=(steps, parts),
            in_specs=spec + [ANYWHERE] * len(needs),
            out_specs=out_specs,
        ),
        out_shape=[jax.ShapeDtypeStruct((n, rows, cols), BF16) for n in counts],
        name="add_picked",
        compiler_params=pltpu.CompilerParams(
            dimension_semantics=("arbitrary", "arbitrary"), vmem_limit_bytes=12 * MIB
        ),
        cost_estimate=pl.CostEstimate(flops=work, bytes_accessed=1_000_000, transcendentals=0),
    )(table, *arrays, *needs)


def join_kernel(count, down_kept, down_landed, rest_kept, rest_landed, *outs):
    rows = down_kept.shape[1]
    for index in range(count):
        target = outs[1 - index % 2] if count > 1 else outs[0]
        place_now = index // 2
        target[place_now, :rows, :] = down_kept[index] + down_landed[index]
        target[place_now, rows:, :] = rest_kept[index] + rest_landed[index]


def join(kept, landed, needs=()):
    count = kept[0].shape[0]
    rows = kept[0].shape[1] + kept[1].shape[1]
    shape = jax.ShapeDtypeStruct(((count + 1) // 2, rows, kept[0].shape[2]), BF16)
    vmem = pl.BlockSpec(memory_space=pltpu.VMEM)
    outs = pl.pallas_call(
        gated(partial(join_kernel, count), 4, needs),
        in_specs=[vmem] * 4 + [ANYWHERE] * len(needs),
        out_specs=[vmem] * min(count, 2),
        out_shape=[shape] * min(count, 2),
        name="join",
        compiler_params=pltpu.CompilerParams(vmem_limit_bytes=24 * MIB),
        cost_estimate=pl.CostEstimate(flops=0, bytes_accessed=200_000, transcendentals=0),
    )(kept[0], landed[0], kept[1], landed[1], *needs)
    return outs if count > 1 else (None, outs[0])


def stack_kernel(count, *refs):
    for index in range(count):
        refs[count][index] = refs[index][...]


def split_kernel(in_ref, *out_refs):
    rows = out_refs[0].shape[0]
    for index, ref in enumerate(out_refs):
        ref[...] = in_ref[index * rows : (index + 1) * rows, :]


def split_rows(value, count, needs=()):
    rows = value.shape[0] // count
    vmem = pl.BlockSpec(memory_space=pltpu.VMEM)
    return pl.pallas_call(
        gated(split_kernel, 1, needs),
        in_specs=[vmem] + [ANYWHERE] * len(needs),
        out_specs=[vmem] * count,
        out_shape=[jax.ShapeDtypeStruct((rows, value.shape[1]), value.dtype)] * count,
        name="split_rows",
        compiler_params=pltpu.CompilerParams(vmem_limit_bytes=12 * MIB),
        cost_estimate=pl.CostEstimate(flops=0, bytes_accessed=100_000, transcendentals=0),
    )(value, *needs)


def stack_up(pieces, needs=()):
    vmem = pl.BlockSpec(memory_space=pltpu.VMEM)
    return pl.pallas_call(
        gated(partial(stack_kernel, len(pieces)), len(pieces), needs),
        in_specs=[vmem] * len(pieces) + [ANYWHERE] * len(needs),
        out_specs=vmem,
        out_shape=jax.ShapeDtypeStruct((len(pieces),) + pieces[0].shape, BF16),
        name="stack_up",
        compiler_params=pltpu.CompilerParams(vmem_limit_bytes=24 * MIB),
        cost_estimate=pl.CostEstimate(flops=0, bytes_accessed=100_000, transcendentals=0),
    )(*pieces, *needs)


def unpack_kernel(pack, depth, meta, mine_ref, other_ref, down_ref, up_ref, out_ref, ordered):
    core, level = meta[2], meta[4]
    rows = pack.rows // depth
    for mask in range(depth):
        start = pl.multiple_of(lax.bitwise_xor(level, mask) * rows, 16)
        ordered[core, pl.ds(start, rows), :] = mine_ref[mask]
        ordered[1 - core, pl.ds(start, rows), :] = other_ref[mask]
    turned = []
    for half in range(CORES):
        for lane in range(0, pack.model_width, pack.feed_shard):
            turned.append(ordered[half, : pack.down_rows, lane : lane + pack.feed_shard])
    down_ref[...] = jnp.transpose(jnp.concatenate(turned, axis=0)).astype(F32)
    for half in range(CORES):
        for block in range(pack.blocks):
            lane = (half * pack.blocks + block) * pack.model_width
            start = pack.up_at + block * pack.row_shard
            up_ref[:, lane : lane + pack.model_width] = ordered[
                half, start : start + pack.row_shard, :
            ].astype(F32)
        out_ref[half * pack.out_rows : (half + 1) * pack.out_rows, :] = ordered[
            half, pack.out_at : pack.out_at + pack.out_rows, :
        ].astype(F32)


def unpack(pack, depth, meta, mine, other):
    vmem = pl.BlockSpec(memory_space=pltpu.VMEM)
    return pl.pallas_call(
        partial(unpack_kernel, pack, depth),
        in_specs=[IN_SMEM, vmem, vmem],
        out_specs=[vmem] * 3,
        out_shape=[
            jax.ShapeDtypeStruct((pack.feed_shard, pack.model_width), F32),
            jax.ShapeDtypeStruct((pack.row_shard, pack.feed_width), F32),
            jax.ShapeDtypeStruct((pack.row_shard, pack.model_width), F32),
        ],
        scratch_shapes=[pltpu.VMEM((CORES, pack.rows, pack.model_width), BF16)],
        name="unpack",
        compiler_params=pltpu.CompilerParams(vmem_limit_bytes=24 * MIB),
        cost_estimate=pl.CostEstimate(flops=0, bytes_accessed=10_000_000, transcendentals=0),
    )(meta, mine, other)


def unpack_qkv_kernel(meta, mine_ref, other_ref, grad_ref, bias_ref, small_ref):
    member = meta[3]
    row_shard, width = grad_ref.shape[0], grad_ref.shape[1] // 3
    part = mine_ref.shape[1] // 3
    for ref, at in ((mine_ref, member), (other_ref, 1 - member)):
        for kind in range(3):
            lane = pl.multiple_of(kind * width + at * part, CLUSTER_ROWS)
            from_lanes = slice(kind * part, (kind + 1) * part)
            grad_ref[:, pl.ds(lane, part)] = ref[:row_shard, from_lanes].astype(F32)
            lane = pl.multiple_of(at * part, CLUSTER_ROWS)
            bias_ref[kind : kind + 1, pl.ds(lane, part)] = ref[row_shard:, from_lanes].astype(F32)[
                BIAS_ROW : BIAS_ROW + 1
            ]
    small_ref[...] = (mine_ref[row_shard:, :].astype(F32) + other_ref[row_shard:, :].astype(F32))[
        :BIAS_ROW
    ]


def unpack_qkv(meta, mine, other, row_shard, needs=()):
    cols = mine.shape[1]
    vmem = pl.BlockSpec(memory_space=pltpu.VMEM)
    return pl.pallas_call(
        gated(unpack_qkv_kernel, 3, needs),
        in_specs=[IN_SMEM, vmem, vmem] + [ANYWHERE] * len(needs),
        out_specs=[vmem] * 3,
        out_shape=[
            jax.ShapeDtypeStruct((row_shard, CORES * cols), F32),
            jax.ShapeDtypeStruct((3, CORES * cols // 3), F32),
            jax.ShapeDtypeStruct((BIAS_ROW, cols), F32),
        ],
        name="unpack_qkv",
        compiler_params=pltpu.CompilerParams(vmem_limit_bytes=16 * MIB),
        cost_estimate=pl.CostEstimate(flops=0, bytes_accessed=200_000, transcendentals=0),
    )(meta, mine, other, *needs)


def tie(*values):
    return lax.optimization_barrier(values)


def body(
    tokens,
    cotangent,
    perms,
    unit_kind,
    w_qkv,
    bias_qv,
    w_out,
    bias_out,
    ln_gain,
    ln_bias,
    w_up,
    bias_up,
    w_down,
    bias_down,
):
    shards = lax.axis_size("fsdp")
    groups = lax.axis_size("dp")
    here = lax.axis_index("fsdp")
    dp_index = lax.axis_index("dp")
    core = dp_index % CORES
    level = dp_index // CORES
    depth = groups // CORES
    units, rounds, unit_len = perms.shape
    per_device = unit_len // shards
    model_width = tokens.shape[1]
    feed_width = w_up.shape[1]
    row_shard = model_width // shards
    members = shards // units
    member_rows = unit_len // members
    head_cols = model_width // members
    padded = -(-head_cols // CLUSTER_ROWS) * CLUSTER_ROWS
    spot = here * CORES + core
    home_core = spot // shards
    unit = (spot // members) % units
    member = spot % members
    pack = Pack(model_width, feed_width, shards, units, depth)
    bits = [1 << k for k in range(shards.bit_length() - 1)]
    bit_orders = (bits, bits[::-1])

    def plane_pairs(target):
        pairs = []
        for z in range(depth):
            for f_index in range(shards):
                for c_index in range(CORES):
                    f_new, c_new = target(f_index, c_index)
                    pairs.append(
                        (
                            (z * CORES + c_index) * shards + f_index,
                            (z * CORES + c_new) * shards + f_new,
                        )
                    )
        return pairs

    def send(value, pairs):
        return lax.ppermute(value, ("dp", "fsdp"), pairs)

    def cross(value, mask):
        return send(value, plane_pairs(lambda f, c: divmod((f * CORES + c) ^ mask, CORES)))

    def trade(value, stage):
        return send(value, plane_pairs(lambda f, c: (f ^ bit_orders[c][stage], c)))

    def trade_mask(index, which):
        mask = 0
        for stage in range(len(bits)):
            if index >> stage & 1:
                mask ^= bit_orders[which][stage]
        return mask

    def climb(value, mask):
        plane = CORES * shards
        pairs = []
        for z in range(depth):
            for rest in range(plane):
                pairs.append((z * plane + rest, (z ^ mask) * plane + rest))
        return send(value, pairs)

    def outward(step):
        def target(f, c):
            place_now = (c * units + (f % units + step) % units) * members + f // units
            return divmod(place_now, CORES)

        return plane_pairs(target)

    def homeward(step):
        return [(b, a) for a, b in outward(step)]

    def bring_start(value):
        blocks = value.reshape(units, per_device, model_width)
        return [
            lax.dynamic_index_in_dim(blocks, (here % units + step) % units, axis=0, keepdims=False)
            for step in range(units)
        ]

    def bring(chosen):
        return jnp.concatenate(
            [send(chosen[step], outward(step)) for step in range(units)], axis=0
        )

    def send_home(blocks):
        return [send(blocks[step], homeward(step)) for step in range(units)]

    def in_order(landed, dtype):
        if units == 2:
            swap = here % units == 1
            wanted = [
                jnp.where(swap, landed[1], landed[0]),
                jnp.where(swap, landed[0], landed[1]),
            ]
        else:
            stacked = jnp.stack(landed)
            wanted = [
                lax.dynamic_index_in_dim(stacked, (index - here % units) % units, 0, keepdims=False)
                for index in range(units)
            ]
        return jnp.concatenate(wanted, axis=0).astype(dtype)

    x_chosen = bring_start(tokens)
    x_own = bring(x_chosen)
    small = jnp.concatenate(
        [
            bias_qv.reshape(-1),
            bias_out,
            ln_gain.reshape(-1),
            ln_bias.reshape(-1),
            bias_up,
            bias_down,
        ]
    )
    small_rows = -(-small.shape[0] // (3 * padded))
    small_block = jnp.pad(
        jnp.pad(small, (0, small_rows * 3 * padded - small.shape[0])).reshape(
            small_rows, 3 * padded
        ),
        ((0, 16 - small_rows), (0, 0)),
    )
    def columns_for(offset):
        start = lax.bitwise_xor(member, offset) * head_cols
        blocks = [
            jnp.pad(
                lax.dynamic_slice(
                    w_qkv, (0, kind * model_width + start), (row_shard, head_cols)
                ),
                ((0, 0), (0, padded - head_cols)),
            )
            for kind in range(3)
        ]
        return jnp.concatenate([jnp.concatenate(blocks, axis=1), small_block], axis=0)

    offsets = [(CORES * m) % members for m in range(shards)]
    kinds = sorted(set(offsets))
    order_pack = jnp.concatenate(
        [perms.reshape(-1), jnp.broadcast_to(unit_kind[:, None], (units, 128)).reshape(-1)]
    )
    order_other = cross(order_pack, 1)
    *tied, order_other = tie(*[columns_for(offset) for offset in kinds], order_other)
    piece_kinds = dict(zip(kinds, tied))
    x_pieces = [x_own] + [cross(x_own, mask) for mask in range(1, members)]
    qkv_pieces = [piece_kinds[0]] + [
        cross(piece_kinds[offsets[m]], CORES * m) for m in range(1, shards)
    ]
    order_pack = jnp.where(home_core == core, order_pack, order_other)
    order_count = units * rounds * unit_len
    unit_perm = lax.dynamic_index_in_dim(
        order_pack[:order_count].reshape(units, rounds * unit_len), unit, 0, keepdims=False
    )
    kind_now = lax.dynamic_index_in_dim(
        order_pack[order_count:].reshape(units, 128), unit, 0, keepdims=False
    )[0]
    owner = unit_perm // per_device
    order = (
        lax.bitwise_xor(owner // units, member) * units + (unit - owner % units) % units
    ) * per_device + unit_perm % per_device
    order = order.reshape(rounds, unit_len)
    order = jnp.where(core == 0, order, order[::-1])
    order_row = order.reshape(1, rounds * unit_len)
    order = order.reshape(-1, CLUSTER_ROWS)
    x_here = arrange(order, x_pieces, unit_len, 0)
    x_now = [x_here, cross(x_here, 1)]
    own_masks = [
        jnp.where(core == 0, trade_mask(i, 0), trade_mask(i, 1)) for i in range(1, shards)
    ]
    other_masks = [
        jnp.where(core == 0, trade_mask(i, 1), trade_mask(i, 0)) for i in range(1, shards)
    ]
    zero = jnp.int32(0)
    meta = jnp.stack(
        [kind_now, here, core, member, level, zero, zero, zero] + own_masks + other_masks
    ).astype(jnp.int32)

    def half_of(value, axis, length, at):
        return lax.dynamic_slice_in_dim(value, at * length, length, axis=axis)

    packed = jnp.concatenate(
        [half_of(w_down, 0, pack.down_rows, core)]
        + [
            half_of(w_up, 1, model_width, core * pack.blocks + block)
            for block in range(pack.blocks)
        ]
        + [half_of(w_out, 0, pack.out_rows, core)],
        axis=0,
    )
    order_rows = unit_len // CLUSTER_ROWS
    arranged, probs, mixtures, x_turned = [], [], [], []
    *tied, packed, x_now[0] = tie(*qkv_pieces[1:], packed, x_now[0])
    qkv_pieces = qkv_pieces[:1] + tied
    smalls = jnp.stack(
        [
            piece[row_shard : row_shard + small_rows].reshape(-1)[: small.shape[0]]
            for piece in qkv_pieces
        ]
    )
    smalls = jnp.take(smalls, lax.bitwise_xor(here, jnp.arange(shards)), axis=0).astype(F32)

    def vectors_at(start, count, length):
        part = smalls[:, start * row_shard : start * row_shard + count * length]
        return (
            part.reshape(shards, count, length).transpose(1, 0, 2).reshape(count, shards * length)
        )

    my_bias = lax.dynamic_index_in_dim(
        vectors_at(0, 2, row_shard).reshape(2, members, head_cols), member, 1, keepdims=False
    )
    my_bias = jnp.pad(my_bias, ((0, 0), (0, padded - head_cols)))
    my_bias = jnp.stack([my_bias[0], jnp.zeros_like(my_bias[0]), my_bias[1]]).reshape(1, -1)
    up_bias = vectors_at(7, 1, feed_width // shards)
    down_bias = smalls[:, small.shape[0] - row_shard :].reshape(1, model_width)
    vectors = jnp.concatenate(
        [vectors_at(2, 5, row_shard), down_bias, jnp.zeros((2, model_width), F32)], axis=0
    )

    weight_pieces = {0: packed}
    for stage in range(len(bits)):
        weight_pieces[1 << stage] = trade(packed, stage)
    for index in range(rounds):
        results = attend(meta, x_now[index], my_bias, qkv_pieces, row_shard, mixtures[-1:])
        for kept, result in zip((arranged, probs, mixtures, x_turned), results):
            kept.append(result)
    cot_now, mixtures[0] = tie(cotangent, mixtures[0])
    cot_landed = [
        send(value, outward(step)) for step, value in enumerate(bring_start(cot_now))
    ]
    cot_own = jnp.concatenate(cot_landed, axis=0)
    for stage in range(1, len(bits)):
        for index in range(1, 1 << stage):
            weight_pieces[index | 1 << stage] = trade(weight_pieces[index], stage)
    att_there, att_sent = [], []
    for mask in range(1, members):
        there = place(
            order_row, mixtures, mask * member_rows, member_rows, 0.5, needs=cot_landed
        )
        att_sent.append(there)
        att_there.append(cross(there[:, :head_cols], mask))
    att_here = place(order_row, mixtures, 0, member_rows, 0.5, needs=att_sent)

    direct = [weight_pieces[index] for index in range(1, shards)]
    swapped = [cross(piece, 1) for piece in direct[:-1]]
    last_piece, att_here = tie(direct[-1], att_here)
    swapped.append(cross(last_piece, 1))
    att_raw = [att_here[:, :head_cols]] + att_there
    if head_cols % CLUSTER_ROWS:
        att_raw = [jnp.concatenate(att_raw, axis=1)]
    block_out, first_low, d_branch, d_ffn, hidden, d_pre, d_lower, att_turned, *rest = feed(
        pack,
        meta,
        x_own,
        cot_own,
        vectors,
        up_bias,
        att_raw,
        [w_out, w_up, w_down],
        direct + swapped,
    )
    d_att, (row_sums, up_sums) = rest[: len(att_raw)], rest[len(att_raw) :]
    if head_cols % CLUSTER_ROWS:
        d_att = [d_att[0][:, mask * head_cols : (mask + 1) * head_cols] for mask in range(members)]
    d_att = [d_att[0]] + [cross(d_att[mask], mask) for mask in range(1, members)]
    d_att = [jnp.pad(piece, ((0, 0), (0, padded - head_cols))) for piece in d_att]

    table = jnp.stack([core, member]).astype(jnp.int32)
    sending = [index for index in range(shards) if index & 1]
    keeping = [index for index in range(shards) if not index & 1]
    slots = jnp.stack(
        [
            lax.bitwise_xor(here, jnp.where(core == 0, trade_mask(i, 0), trade_mask(i, 1)))
            for i in sending + keeping
        ]
    )
    slots = jnp.concatenate([slots, slots]).astype(jnp.int32)

    def pair_sum(mine, theirs, needs):
        return add_picked(
            slots, [mine, cross(theirs, 1)], shards, len(sending), needs, 20_000_000_000
        )

    theirs_down, mine_down = down_grads(pack, table, d_ffn, hidden)
    theirs_rest, mine_rest = rest_grads(
        pack, table, first_low, d_pre, att_turned, d_branch, [theirs_down]
    )
    down_going, down_kept = pair_sum(mine_down, theirs_down, [theirs_rest])
    rest_going, rest_kept = pair_sum(mine_rest, theirs_rest, [down_going] + d_att[1:])

    def merge(kept, landed, *needs):
        count = kept.shape[0]
        if count == 1:
            table = jnp.zeros((2,), jnp.int32)
            return None, add_picked(table, [kept, landed], 1, None, needs)[0]
        order_now = [i for i in range(count) if i & 1] + [i for i in range(count) if not i & 1]
        table = jnp.array(order_now * 2, jnp.int32)
        return add_picked(table, [kept, landed], count, count // 2, needs)

    grads, d_x = [None] * rounds, [None] * rounds
    needs = [rest_going]
    blocks = unit_len // POS_BLOCK
    spans = [(rounds - 1, (0, blocks))]
    for index in reversed(range(rounds - 1)):
        spans += [(index, (0, blocks // 2)), (index, (blocks // 2, blocks))]
    results = []
    for turn, (index, span) in enumerate(spans):
        results = attend_back(
            meta,
            order,
            arranged[index],
            probs[index],
            d_att,
            qkv_pieces,
            row_shard,
            index * order_rows,
            needs,
            span,
            results if span[0] else [],
        )
        grads[index], d_x[index] = results
        if turn == 0:
            d_x_there = cross(d_x[index], 1)
        if turn == 0:
            going, kept = join(
                [down_kept, rest_kept], [trade(down_going, 0), trade(rest_going, 0)], [results[0]]
            )
            needs = [kept]
        elif turn < len(bits):
            going, kept = merge(kept, trade(going, turn), results[0])
            needs = [kept, d_x_there]
        if turn == len(spans) - 2:
            output_landed = send_home(split_rows(block_out, units, [kept]))
    for stage in range(len(spans), len(bits)):
        going, kept = merge(kept, trade(going, stage))

    def level_pieces(block):
        return block.reshape((depth, block.shape[0] // depth) + block.shape[1:])

    def level_scatter(cut):
        return [
            climb(
                lax.dynamic_index_in_dim(cut, lax.bitwise_xor(level, mask), 0, keepdims=False), mask
            )
            for mask in range(1, depth)
        ]

    def level_gather(piece):
        pieces = {0: piece}
        mask = depth // 2
        while mask:
            pieces.update({index | mask: climb(held, mask) for index, held in pieces.items()})
            mask //= 2
        return [pieces[index] for index in range(depth)]

    def by_shard(value):
        count, length = value.shape
        return (
            value.reshape(count, shards, length // shards)
            .transpose(1, 0, 2)
            .reshape(shards, count * length // shards)
        )

    small_grad = jnp.concatenate(
        [by_shard(row_sums[:5]), by_shard(up_sums), by_shard(row_sums[5:6])], axis=1
    )
    small_length = small_grad.shape[1]
    small_lanes = 3 * head_cols
    small_grad = jnp.pad(small_grad, ((0, 0), (0, BIAS_ROW * small_lanes - small_length)))
    small_grad = jnp.pad(
        small_grad.reshape(shards, BIAS_ROW, small_lanes), ((0, 0), (0, 16 - BIAS_ROW), (0, 0))
    )
    extra_rows = 16
    x_last, kept, small_grad = tie(x_turned[0], kept, small_grad)
    if padded == head_cols:
        joined = qkv_grads(
            [x_last, x_turned[1]], grads, small_grad, row_shard, output_landed
        )
    else:
        qkv_grad = dot(x_last, grads[0]) + dot(x_turned[1], grads[1])
        qkv_grad = qkv_grad.reshape(shards, row_shard, 3, padded)[..., :head_cols]
        bias_sum = sum(jnp.sum(value.astype(F32), axis=0) for value in grads)
        bias_sum = bias_sum.reshape(3, padded)[:, :head_cols].reshape(small_lanes)
        small_grad = small_grad.at[:, BIAS_ROW].set(bias_sum[None])
        joined = jnp.concatenate(
            [qkv_grad.reshape(shards, row_shard, small_lanes), small_grad], axis=1
        ).astype(BF16)
    cut = level_pieces(kept[0])
    landed = level_scatter(cut)
    classes = max(1, members // CORES)
    d_x_parts = [d_x[0], d_x_there]
    order_mine = order_row[:, :unit_len]
    if classes == 1:
        slots_held = jnp.stack(
            [
                lax.bitwise_xor(here, jnp.where(core == 0, trade_mask(i, 0), trade_mask(i, 1)))
                for i in range(shards)
            ]
        )
        held = jnp.stack(
            [
                lax.dynamic_index_in_dim(joined, slots_held[i], 0, keepdims=False)
                for i in range(0, shards, 2)
            ]
        )
        leaving = jnp.stack(
            [
                lax.dynamic_index_in_dim(joined, slots_held[i], 0, keepdims=False)
                for i in range(1, shards, 2)
            ]
        )
        totals = None
    else:
        totals = [None] * classes
        for m in range(shards):
            offset = offsets[m] // CORES
            piece = lax.dynamic_index_in_dim(joined, lax.bitwise_xor(here, m), 0, keepdims=False)
            piece = (piece if m == 0 else cross(piece, CORES * m)).astype(F32)
            totals[offset] = piece if totals[offset] is None else totals[offset] + piece

    if depth > 1:
        picks = jnp.concatenate([level[None], jnp.zeros((depth - 1,), level.dtype)])
        (kept,) = add_picked(
            picks.astype(jnp.int32),
            [cut] + [piece[None] for piece in landed],
            1,
            None,
            [joined],
        )
    d_there = [
        place(
            order_mine,
            d_x_parts,
            mask * member_rows,
            member_rows,
            added=True,
            needs=[kept],
        )
        for mask in range(1, members)
    ]
    gathered = level_gather(kept[0]) if depth > 1 else [cut[0]]
    early = list(d_there) + gathered[depth // 2 : depth // 2 + 1]
    if totals is None:
        leaving, held = merge(held, trade(leaving, 0), *d_there)
        early.append(held)
    d_here = place(
        order_mine,
        d_x_parts,
        0,
        member_rows,
        1.0,
        F32,
        d_lower,
        added=True,
        needs=early,
    )
    d_inputs = d_here
    for mask, there in enumerate(d_there, 1):
        d_inputs = d_inputs + cross(there, mask).astype(F32)
    d_inputs = d_inputs.astype(BF16)
    if totals is None:
        for stage in range(1, len(bits)):
            leaving, held = merge(held, trade(leaving, stage), d_here)
        totals = [held[0]]
    d_inputs = in_order(
        send_home(d_inputs.reshape(units, per_device, model_width)), F32
    )
    output = in_order(output_landed, BF16)
    totals = jnp.concatenate(totals, axis=0).astype(BF16)
    rows_each = row_shard + extra_rows
    mask = 1
    while mask < depth:
        totals = (totals.astype(F32) + climb(totals, mask).astype(F32)).astype(BF16)
        mask *= 2
    stacked = stack_up(gathered)
    grad_down, grad_up, grad_out = unpack(pack, depth, meta, stacked, cross(stacked, 1))
    if padded == head_cols and members == CORES:
        grad_qkv, bias_out_row, smalls_out = unpack_qkv(
            meta, totals, cross(totals, 1), row_shard, [grad_down, d_inputs, output]
        )
        smalls_out = smalls_out.reshape(-1)[:small_length]
        bias_out_row = lax.dynamic_slice(bias_out_row, (0, here * row_shard), (3, row_shard))
    else:
        landed = jnp.stack([totals, cross(totals, 1)], axis=0).reshape(
            CORES, classes, rows_each, 3 * head_cols
        )
        smalls_out = jnp.sum(
            landed[:, :, row_shard : row_shard + BIAS_ROW].astype(F32), axis=(0, 1)
        ).reshape(-1)[:small_length]
        landed = (
            landed.transpose(1, 0, 2, 3)
            .reshape(members, rows_each, 3, head_cols)[:, : row_shard + BIAS_ROW + 1]
        )
        if members == 2:
            swap = member == 1
            landed = jnp.stack(
                [
                    jnp.where(swap, landed[1], landed[0]),
                    jnp.where(swap, landed[0], landed[1]),
                ]
            )
        else:
            landed = jnp.take(landed, lax.bitwise_xor(member, jnp.arange(members)), axis=0)
        grad_qkv = landed[:, :row_shard].transpose(1, 2, 0, 3)
        grad_qkv = grad_qkv.reshape(row_shard, 3 * model_width).astype(F32)
        bias_out_row = landed[:, row_shard + BIAS_ROW].astype(F32).transpose(1, 0, 2)
        bias_out_row = lax.dynamic_slice(
            bias_out_row.reshape(3, model_width), (0, here * row_shard), (3, row_shard)
        )

    feed_shard = feed_width // shards
    spots = [0, row_shard, 3 * row_shard, 5 * row_shard]
    return (
        output,
        d_inputs,
        grad_qkv,
        bias_out_row[::2],
        grad_out,
        smalls_out[spots[0] : spots[1]],
        smalls_out[spots[1] : spots[2]].reshape(2, row_shard),
        smalls_out[spots[2] : spots[3]].reshape(2, row_shard),
        grad_up,
        smalls_out[spots[3] : spots[3] + feed_shard],
        grad_down,
        smalls_out[spots[3] + feed_shard :],
    )


def solution(mesh):
    placed = (
        P(("dp", "fsdp"), None),
        P(("dp", "fsdp"), None),
        P("dp", None, None),
        P("dp"),
        P("fsdp", None),
        P(None, "fsdp"),
        P("fsdp", None),
        P("fsdp"),
        P(None, "fsdp"),
        P(None, "fsdp"),
        P("fsdp", None),
        P("fsdp"),
        P("fsdp", None),
        P("fsdp"),
    )
    return jax.shard_map(
        body,
        mesh=mesh,
        in_specs=placed,
        out_specs=(
            P(("dp", "fsdp"), None),
            P(("dp", "fsdp"), None),
            P("fsdp", None),
            P(None, "fsdp"),
            P("fsdp", None),
            P("fsdp"),
            P(None, "fsdp"),
            P(None, "fsdp"),
            P("fsdp", None),
            P("fsdp"),
            P("fsdp", None),
            P("fsdp"),
        ),
        check_vma=False,
    )
```

```python
from functools import partial

import jax
import jax.numpy as jnp
from jax import lax
from jax.experimental import pallas as pl
from jax.experimental.pallas import tpu as pltpu
from jax.sharding import PartitionSpec as P

HEAD_DIM = 64
CORES = 2
NEG_FILL = -1000000000.0
EPSILON = 1e-05
SCALE = HEAD_DIM ** (-0.5)
BIAS_ROW = 2
GRAD_LANES = 384
CLUSTER_ROWS = 128
HALF_ROWS = 64
POS_BLOCK = 512
TOKEN_BLOCK = 512
ROW_BLOCK = 256
FF_BLOCK = 512
MIB = 1024 * 1024
NT = (((1,), (1,)), ((), ()))
TN = (((0,), (0,)), ((), ()))
F32 = jnp.float32
BF16 = jnp.bfloat16
ANYWHERE = pl.BlockSpec(memory_space=pl.ANY)
IN_SMEM = pl.BlockSpec(memory_space=pltpu.SMEM)


def whole(shape):
    return pl.BlockSpec(shape, lambda i: (0,) * len(shape))


def rows_of(shape):
    return pl.BlockSpec(shape, lambda i: (i,) + (0,) * (len(shape) - 1))


def dot(a, b, dims=(((1,), (0,)), ((), ()))):
    return lax.dot_general(a, b, dims, preferred_element_type=F32)


def params(mib, flops=0, moved=0, share=16):
    return dict(
        compiler_params=pltpu.CompilerParams(
            dimension_semantics=("arbitrary",),
            vmem_limit_bytes=mib * MIB,
        ),
        cost_estimate=pl.CostEstimate(
            flops=flops // share, bytes_accessed=moved // share, transcendentals=0
        ),
    )


def gated(kernel, used, needs):
    if not needs:
        return kernel

    def run(*refs):
        return kernel(*refs[:used], *refs[used + len(needs) :])

    return run


def lane_masks():
    lane = lax.broadcasted_iota(jnp.int32, (CLUSTER_ROWS, CLUSTER_ROWS), 1)
    low = (lane < HEAD_DIM).astype(F32)
    return low.astype(BF16), (1.0 - low).astype(BF16), lane < HEAD_DIM


def corners(first, second):
    blank = jnp.zeros_like(first)
    return jnp.concatenate(
        [
            jnp.concatenate([first, blank], axis=1),
            jnp.concatenate([blank, second], axis=1),
        ],
        axis=0,
    )


def both_heads(rows_now, low, high):
    return jnp.concatenate([rows_now * low, rows_now * high], axis=0)


def equal_ones(left, right):
    return jnp.where(left == right, jnp.ones((), BF16), jnp.zeros((), BF16))


def pick_rows(order_ref, first_row, unit_len):
    parts = []
    lane = lax.broadcasted_iota(jnp.int16, (CLUSTER_ROWS, CLUSTER_ROWS), 1)
    for part in range(POS_BLOCK // CLUSTER_ROWS):
        row = order_ref[pl.ds(first_row + part, 1), :]
        column = jnp.transpose(jnp.broadcast_to(row, (CLUSTER_ROWS, CLUSTER_ROWS)))
        column = column.astype(jnp.int16)
        pieces = [
            equal_ones(column, lane + jnp.int16(base)) for base in range(0, unit_len, CLUSTER_ROWS)
        ]
        parts.append(jnp.concatenate(pieces, axis=1))
    return jnp.concatenate(parts, axis=0)


def load_pieces(meta, x_refs, w_refs, x_all, w_all, sems, row_shard):
    member_rows = x_all.shape[0] // max(1, len(x_refs))
    copies = []
    for index, ref in enumerate(x_refs):
        copies.append(
            pltpu.make_async_copy(
                ref, x_all.at[pl.ds(index * member_rows, member_rows), :], sems.at[index]
            )
        )
    for index, ref in enumerate(w_refs):
        start = pl.multiple_of(lax.bitwise_xor(meta[1], index) * row_shard, 16)
        copies.append(
            pltpu.make_async_copy(
                ref.at[pl.ds(0, row_shard), :],
                w_all.at[pl.ds(start, row_shard), :],
                sems.at[len(x_refs) + index],
            )
        )
    for copy in copies:
        copy.start()
    for copy in copies:
        copy.wait()


def arrange_kernel(unit_len, first_row, order_ref, *refs):
    x_refs, out_ref = refs[:-1], refs[-1]
    step = pl.program_id(0)
    picks = pick_rows(order_ref, first_row + step * (POS_BLOCK // CLUSTER_ROWS), unit_len)
    rows = x_refs[0].shape[0]
    total = None
    for index, ref in enumerate(x_refs):
        term = dot(picks[:, index * rows : (index + 1) * rows], ref[...])
        total = term if total is None else total + term
    out_ref[...] = total.astype(BF16)


def arrange(order, x_pieces, position_count, first_row):
    member_rows, width = x_pieces[0].shape
    unit_len = member_rows * len(x_pieces)
    return pl.pallas_call(
        partial(arrange_kernel, unit_len, first_row),
        grid=(position_count // POS_BLOCK,),
        in_specs=[whole(order.shape)] + [whole(piece.shape) for piece in x_pieces],
        out_specs=rows_of((POS_BLOCK, width)),
        out_shape=jax.ShapeDtypeStruct((position_count, width), BF16),
        name="arrange",
        **params(20, 2 * position_count * unit_len * width, 6_000_000),
    )(order, *x_pieces)


def attend_kernel(sizes, meta, x_now_ref, bias_ref, *refs):
    shards, row_shard = sizes
    w_refs, refs = refs[:shards], refs[shards:]
    arranged_ref, probs_ref, mixture_ref, turned_ref, w_all, sems = refs
    width = w_all.shape[1] // 3
    step = pl.program_id(0)

    @pl.when(step == 0)
    def _():
        load_pieces(meta, [], w_refs, w_all, w_all, sems, row_shard)

    x_now = x_now_ref[...]
    turned_ref[...] = jnp.transpose(x_now)
    arranged = (dot(x_now, w_all[...]) + bias_ref[...]).astype(BF16)
    arranged_ref[...] = arranged
    low, high, lane_low = lane_masks()
    position = lax.broadcasted_iota(jnp.int32, (CLUSTER_ROWS, CLUSTER_ROWS), 0)
    other = lax.broadcasted_iota(jnp.int32, (CLUSTER_ROWS, CLUSTER_ROWS), 1)
    same_half = (position < HALF_ROWS) == (other < HALF_ROWS)
    allowed = jnp.logical_or(same_half, meta[0] == 1)
    pairs = width // CLUSTER_ROWS
    units = [(part, pair) for part in range(POS_BLOCK // CLUSTER_ROWS) for pair in range(pairs)]
    for index in range(0, len(units), 2):
        queries, keys, values = [], [], []
        for part, pair in units[index : index + 2]:
            rows_now = slice(part * CLUSTER_ROWS, (part + 1) * CLUSTER_ROWS)
            base = pair * CLUSTER_ROWS
            queries.append(arranged[rows_now, base : base + CLUSTER_ROWS] * SCALE)
            one_key = arranged[rows_now, width + base : width + base + CLUSTER_ROWS]
            keys.append(both_heads(one_key, low, high))
            one_value = arranged[rows_now, 2 * width + base : 2 * width + base + CLUSTER_ROWS]
            values.append(both_heads(one_value, low, high))
        both_scores = dot(jnp.concatenate(keys, axis=1), corners(*queries), NT)
        for which, (part, pair) in enumerate(units[index : index + 2]):
            halves = []
            for head in range(2):
                one = both_scores[
                    head * CLUSTER_ROWS : (head + 1) * CLUSTER_ROWS,
                    which * CLUSTER_ROWS : (which + 1) * CLUSTER_ROWS,
                ]
                one = jnp.where(allowed, one, NEG_FILL)
                grown = jnp.exp(one - jnp.max(one, axis=0, keepdims=True))
                halves.append(grown * (1.0 / jnp.sum(grown, axis=0, keepdims=True)))
            probs = jnp.concatenate(halves, axis=0).astype(BF16)
            at = (part * pairs + pair) * 2 * CLUSTER_ROWS
            probs_ref[at : at + 2 * CLUSTER_ROWS, :] = probs
            mixture_ref[
                part * CLUSTER_ROWS : (part + 1) * CLUSTER_ROWS,
                pair * CLUSTER_ROWS : (pair + 1) * CLUSTER_ROWS,
            ] = dot(probs, values[which], TN).astype(BF16)


def attend(meta, x_now, bias, w_pieces, row_shard, needs=()):
    shards = len(w_pieces)
    position_count, model_width = x_now.shape
    cols = w_pieces[0].shape[1]
    width = cols // 3
    pair_rows = 2 * width
    return pl.pallas_call(
        gated(partial(attend_kernel, (shards, row_shard)), 3 + shards, needs),
        grid=(position_count // POS_BLOCK,),
        in_specs=[IN_SMEM, rows_of((POS_BLOCK, model_width)), whole(bias.shape)]
        + [ANYWHERE] * (shards + len(needs)),
        out_specs=[
            rows_of((POS_BLOCK, cols)),
            rows_of((POS_BLOCK // CLUSTER_ROWS * pair_rows, CLUSTER_ROWS)),
            rows_of((POS_BLOCK, width)),
            pl.BlockSpec((model_width, POS_BLOCK), lambda i: (0, i)),
        ],
        out_shape=[
            jax.ShapeDtypeStruct((position_count, cols), BF16),
            jax.ShapeDtypeStruct((position_count // CLUSTER_ROWS * pair_rows, CLUSTER_ROWS), BF16),
            jax.ShapeDtypeStruct((position_count, width), BF16),
            jax.ShapeDtypeStruct((model_width, position_count), BF16),
        ],
        scratch_shapes=[
            pltpu.VMEM((model_width, cols), BF16),
            pltpu.SemaphoreType.DMA((shards,)),
        ],
        name="attend",
        **params(
            60, 8 * position_count * (model_width * cols + 4 * CLUSTER_ROWS * width), 18_000_000, 1
        ),
    )(meta, x_now, bias, *w_pieces, *needs)


def place_kernel(sizes, scale, has_base, order_row_ref, *refs):
    unit_len, first_token, added = sizes
    base_ref = refs[0] if has_base else None
    refs = refs[1 if has_base else 0 :]
    if added:
        first_ref, second_ref, out_ref, held = refs

        @pl.when(pl.program_id(0) == 0)
        def _():
            held[...] = (first_ref[...].astype(F32) + second_ref[...].astype(F32)).astype(BF16)

        source_refs = [held]
    else:
        source_refs, out_ref = refs[:-1], refs[-1]
    block_rows = out_ref.shape[0]
    first = jnp.full((1, 1), first_token + pl.program_id(0) * block_rows, jnp.int32)
    token = lax.broadcasted_iota(jnp.int16, (block_rows, unit_len), 0)
    total = None
    for index, ref in enumerate(source_refs):
        row = order_row_ref[:, index * unit_len : (index + 1) * unit_len] - first
        row = jnp.broadcast_to(row, (16, unit_len)).astype(jnp.int16)
        row = jnp.concatenate([row] * (block_rows // 16), axis=0)
        term = dot(equal_ones(row, token), ref[...])
        total = term if total is None else total + term
    if scale != 1.0:
        total = total * scale
    if has_base:
        total = total + base_ref[...]
    out_ref[...] = total.astype(out_ref.dtype)


def place(
    order_row,
    sources,
    first_token,
    row_count,
    scale=1.0,
    dtype=BF16,
    base=None,
    added=False,
    needs=(),
):
    unit_len, width = sources[0].shape
    block_rows = min(TOKEN_BLOCK, row_count)
    extra = [] if base is None else [base]
    return pl.pallas_call(
        gated(
            partial(place_kernel, (unit_len, first_token, added), scale, base is not None),
            1 + len(extra) + len(sources),
            needs,
        ),
        grid=(row_count // block_rows,),
        in_specs=[whole(order_row.shape)]
        + [rows_of((block_rows, width))] * len(extra)
        + [whole(source.shape) for source in sources]
        + [ANYWHERE] * len(needs),
        out_specs=rows_of((block_rows, width)),
        out_shape=jax.ShapeDtypeStruct((row_count, width), dtype),
        scratch_shapes=[pltpu.VMEM((unit_len, width), BF16)] if added else [],
        name="place",
        **params(
            32 if added else 20,
            16 * row_count * unit_len * width,
            10_000_000,
            1,
        ),
    )(order_row, *extra, *sources, *needs)


def attend_back_kernel(sizes, meta, order_ref, arranged_ref, probs_ref, *refs):
    members, shards, unit_len, row_shard, first_row, start = sizes
    g_refs, refs = refs[:members], refs[members:]
    w_refs, refs = refs[:shards], refs[shards:]
    grads_ref, d_x_ref, g_all, w_all, sems = refs
    width = w_all.shape[1] // 3
    step = pl.program_id(0)

    @pl.when(step == 0)
    def _():
        load_pieces(meta, g_refs, w_refs, g_all, w_all, sems, row_shard)

    at_row = first_row + (start + step) * (POS_BLOCK // CLUSTER_ROWS)
    picks = pick_rows(order_ref, at_row, unit_len)
    d_mixture = dot(picks, g_all[...]).astype(BF16)
    low, high, lane_low = lane_masks()
    pairs = width // CLUSTER_ROWS
    units = [(part, pair) for part in range(POS_BLOCK // CLUSTER_ROWS) for pair in range(pairs)]
    for index in range(0, len(units), 2):
        values, d_rows = [], []
        for part, pair in units[index : index + 2]:
            rows_now = slice(part * CLUSTER_ROWS, (part + 1) * CLUSTER_ROWS)
            base = pair * CLUSTER_ROWS
            one_value = arranged_ref[rows_now, 2 * width + base : 2 * width + base + CLUSTER_ROWS]
            values.append(both_heads(one_value, low, high))
            d_rows.append(d_mixture[rows_now, base : base + CLUSTER_ROWS])
        both_probs = dot(jnp.concatenate(values, axis=1), corners(*d_rows), NT)
        for which, (part, pair) in enumerate(units[index : index + 2]):
            rows_now = slice(part * CLUSTER_ROWS, (part + 1) * CLUSTER_ROWS)
            base = pair * CLUSTER_ROWS
            q_lanes = slice(base, base + CLUSTER_ROWS)
            k_lanes = slice(width + base, width + base + CLUSTER_ROWS)
            v_lanes = slice(2 * width + base, 2 * width + base + CLUSTER_ROWS)
            queries = arranged_ref[rows_now, q_lanes] * SCALE
            keys = arranged_ref[rows_now, k_lanes] * SCALE
            at = (part * pairs + pair) * 2 * CLUSTER_ROWS
            probs = probs_ref[at : at + 2 * CLUSTER_ROWS, :]
            d_probs = both_probs[:, which * CLUSTER_ROWS : (which + 1) * CLUSTER_ROWS]
            pieces = []
            for head in range(2):
                rows = slice(head * CLUSTER_ROWS, (head + 1) * CLUSTER_ROWS)
                weight = probs[rows].astype(F32)
                d_one = d_probs[rows]
                inner = jnp.sum(weight * d_one, axis=0, keepdims=True)
                pieces.append(weight * (d_one - inner))
            d_scores = jnp.concatenate(pieces, axis=0).astype(BF16)
            d_query = dot(d_scores, both_heads(keys, low, high), TN)
            d_pair = dot(
                jnp.concatenate([probs, d_scores], axis=1), corners(d_rows[which], queries)
            )
            d_values, d_keys = d_pair[:, :CLUSTER_ROWS], d_pair[:, CLUSTER_ROWS:]
            grads_ref[rows_now, q_lanes] = d_query.astype(BF16)
            grads_ref[rows_now, k_lanes] = jnp.where(
                lane_low, d_keys[:CLUSTER_ROWS], d_keys[CLUSTER_ROWS:]
            ).astype(BF16)
            grads_ref[rows_now, v_lanes] = jnp.where(
                lane_low, d_values[:CLUSTER_ROWS], d_values[CLUSTER_ROWS:]
            ).astype(BF16)
    grads = grads_ref[...]
    d_x_ref[...] = dot(grads, w_all[...], NT).astype(BF16)


def attend_back(
    meta, order, arranged, probs, g_pieces, w_pieces, row_shard, first_row, needs, span, into
):
    members, shards = len(g_pieces), len(w_pieces)
    member_rows, width = g_pieces[0].shape
    unit_len = members * member_rows
    position_count, cols = arranged.shape
    model_width = row_shard * shards
    start, stop = span
    pair_rows = POS_BLOCK // CLUSTER_ROWS * 2 * width
    used = 4 + members + shards

    def block(shape):
        return pl.BlockSpec(shape, lambda i: (start + i, 0))

    return pl.pallas_call(
        gated(
            partial(attend_back_kernel, (members, shards, unit_len, row_shard, first_row, start)),
            used,
            list(into) + list(needs),
        ),
        grid=(stop - start,),
        in_specs=[
            IN_SMEM,
            whole(order.shape),
            block((POS_BLOCK, cols)),
            block((pair_rows, CLUSTER_ROWS)),
        ]
        + [ANYWHERE] * (members + shards + len(into) + len(needs)),
        out_specs=[block((POS_BLOCK, cols)), block((POS_BLOCK, model_width))],
        out_shape=[
            jax.ShapeDtypeStruct((position_count, cols), BF16),
            jax.ShapeDtypeStruct((position_count, model_width), BF16),
        ],
        input_output_aliases={used + index: index for index in range(len(into))},
        scratch_shapes=[
            pltpu.VMEM((unit_len, width), BF16),
            pltpu.VMEM((model_width, cols), BF16),
            pltpu.SemaphoreType.DMA((members + shards,)),
        ],
        name="attend_back",
        **params(
            60,
            12 * (stop - start) * POS_BLOCK * (unit_len * width + model_width * cols),
            20_000_000,
            1,
        ),
    )(meta, order, arranged, probs, *g_pieces, *w_pieces, *into, *needs)


def normalise(summed):
    average = jnp.mean(summed, axis=-1, keepdims=True)
    centred = summed - average
    spread = jnp.mean(centred * centred, axis=-1, keepdims=True)
    scale_inv = lax.rsqrt(spread + EPSILON)
    return centred * scale_inv, scale_inv


def normalise_back(grad_out, normed, scale_inv, gain_row):
    scaled = grad_out * gain_row
    return scale_inv * (
        scaled
        - jnp.mean(scaled, axis=-1, keepdims=True)
        - normed * jnp.mean(scaled * normed, axis=-1, keepdims=True)
    )


def column_sum(rows_now):
    return jnp.sum(rows_now, axis=0, keepdims=True)


def gelu_parts(value):
    below = 0.5 + 0.5 * lax.erf(value * 0.7071067811865476)
    bell = jnp.exp(value * value * -0.5) * 0.3989422804014327
    return value * below, below + value * bell


class Pack:
    def __init__(self, model_width, feed_width, shards, units, depth):
        self.model_width, self.feed_width, self.shards = model_width, feed_width, shards
        self.row_shard = model_width // shards
        self.feed_shard = feed_width // shards
        self.down_rows = self.feed_shard // CORES
        self.blocks = feed_width // CORES // model_width
        self.up_at = self.down_rows
        self.out_at = self.up_at + self.blocks * self.row_shard
        self.out_rows = self.row_shard // CORES
        self.used = self.out_at + self.out_rows
        unit = 16 * depth
        self.rows = -(-self.used // unit) * unit
        self.rest_rows = self.rows - self.down_rows
        self.units = units
        self.group = units * self.row_shard

    def out_start(self, shard, member):
        return (
            lax.bitwise_xor(jnp.int32(shard) // self.units, member) * self.group
            + (shard % self.units) * self.row_shard
        )


def feed_kernel(pack, att_count, meta, x_ref, cot_ref, vec_ref, up_bias_ref, *refs):
    shards = pack.shards
    att_refs, refs = refs[:att_count], refs[att_count:]
    own_out, own_up, own_down = refs[:3]
    refs = refs[3:]
    pieces, refs = refs[: 2 * (shards - 1)], refs[2 * (shards - 1) :]
    out_ref, first_turned_ref, d_branch_ref, d_ffn_turned_ref, hidden_ref, d_pre_ref = refs[:6]
    d_h1_ref, att_turned_ref = refs[6:8]
    refs = refs[8:]
    d_att_refs, refs = refs[:att_count], refs[att_count:]
    sums_ref, up_sums_ref, w_out, w_up, w_down, slope, sems = refs
    step = pl.program_id(0)
    here, core, member = meta[1], meta[2], meta[3]
    feed_width = pack.feed_width

    def loads(kind):
        copies = []

        def add(source, target):
            copies.append(pltpu.make_async_copy(source, target, sems.at[kind, len(copies)]))

        if kind == 0:
            start = pl.multiple_of(pack.out_start(here, member), 16)
            add(own_out, w_out.at[pl.ds(start, pack.row_shard), :])
        elif kind == 1:
            start = pl.multiple_of(here * pack.row_shard, 16)
            add(own_up, w_up.at[pl.ds(start, pack.row_shard), :])
        else:
            start = pl.multiple_of(here * pack.feed_shard, 16)
            add(own_down, w_down.at[pl.ds(start, pack.feed_shard), :])
        for index, ref in enumerate(pieces):
            peer = lax.bitwise_xor(here, meta[8 + index])
            half = core if index < shards - 1 else 1 - core
            if kind == 0:
                start = pack.out_start(peer, member) + half * pack.out_rows
                start = pl.multiple_of(start, 16)
                add(
                    ref.at[pl.ds(pack.out_at, pack.out_rows), :],
                    w_out.at[pl.ds(start, pack.out_rows), :],
                )
            elif kind == 1:
                start = pl.multiple_of(peer * pack.row_shard, 16)
                for block in range(pack.blocks):
                    lane = pl.multiple_of(
                        (half * pack.blocks + block) * pack.model_width, CLUSTER_ROWS
                    )
                    add(
                        ref.at[pl.ds(pack.up_at + block * pack.row_shard, pack.row_shard), :],
                        w_up.at[pl.ds(start, pack.row_shard), pl.ds(lane, pack.model_width)],
                    )
            else:
                start = pl.multiple_of(peer * pack.feed_shard + half * pack.down_rows, 16)
                add(
                    ref.at[pl.ds(0, pack.down_rows), :],
                    w_down.at[pl.ds(start, pack.down_rows), :],
                )
        return copies

    @pl.when(step == 0)
    def _():
        for kind in range(3):
            for copy in loads(kind):
                copy.start()
        sums_ref[...] = jnp.zeros_like(sums_ref)
        up_sums_ref[...] = jnp.zeros_like(up_sums_ref)
        for copy in loads(0):
            copy.wait()

    bias_out, gain_one, gain_two = vec_ref[0:1, :], vec_ref[1:2, :], vec_ref[2:3, :]
    shift_one, shift_two, bias_down = vec_ref[3:4, :], vec_ref[4:5, :], vec_ref[5:6, :]
    att_width = att_refs[0].shape[1]
    summed = x_ref[...].astype(F32) + bias_out
    for index, ref in enumerate(att_refs):
        summed += dot(ref[...], w_out[index * att_width : (index + 1) * att_width, :])
    normed_one, inv_one = normalise(summed)
    first = normed_one * gain_one + shift_one
    first_low = first.astype(BF16)
    first_turned_ref[...] = jnp.transpose(first_low)
    for index, ref in enumerate(att_refs):
        att_turned_ref[index * att_width : (index + 1) * att_width, :] = jnp.transpose(ref[...])

    @pl.when(step == 0)
    def _():
        for kind in (1, 2):
            for copy in loads(kind):
                copy.wait()

    second = first + bias_down
    starts = list(range(0, feed_width, FF_BLOCK))

    def raised(base):
        lanes = slice(base, base + FF_BLOCK)
        return dot(first_low, w_up[:, lanes]) + up_bias_ref[:, lanes]

    pre = raised(starts[0])
    for index, base in enumerate(starts):
        lanes = slice(base, base + FF_BLOCK)
        pre_next = raised(starts[index + 1]) if index + 1 < len(starts) else None
        hidden, slope_now = gelu_parts(pre)
        hidden = hidden.astype(BF16)
        hidden_ref[:, lanes] = hidden
        slope[:, lanes] = slope_now
        second += dot(hidden, w_down[lanes, :])
        pre = pre_next
    normed_two, inv_two = normalise(second)
    out_ref[...] = (normed_two * gain_two + shift_two).astype(BF16)
    top = cot_ref[...].astype(F32)
    d_second = normalise_back(top, normed_two, inv_two, gain_two)
    d_ffn = d_second.astype(BF16)
    d_ffn_turned_ref[...] = jnp.transpose(d_ffn)
    d_first = d_second
    d_hidden = dot(d_ffn, w_down[0:FF_BLOCK, :], NT)
    for index, base in enumerate(starts):
        lanes = slice(base, base + FF_BLOCK)
        if index + 1 < len(starts):
            d_next = dot(d_ffn, w_down[starts[index + 1] : starts[index + 1] + FF_BLOCK, :], NT)
        d_pre = (d_hidden * slope[:, lanes]).astype(BF16)
        d_pre_ref[:, lanes] = d_pre
        up_sums_ref[:, lanes] += column_sum(d_pre.astype(F32))
        d_first += dot(d_pre, w_up[:, lanes], NT)
        d_hidden = d_next
    d_lower = normalise_back(d_first, normed_one, inv_one, gain_one)
    d_h1_ref[...] = d_lower
    d_branch = d_lower.astype(BF16)
    d_branch_ref[...] = d_branch
    for index, ref in enumerate(d_att_refs):
        back = dot(d_branch, w_out[index * att_width : (index + 1) * att_width, :], NT)
        ref[...] = (0.5 * back).astype(BF16)
    sums_ref[0:1, :] += column_sum(d_branch.astype(F32))
    sums_ref[1:2, :] += column_sum(d_first * normed_one)
    sums_ref[2:3, :] += column_sum(top * normed_two)
    sums_ref[3:4, :] += column_sum(d_first)
    sums_ref[4:5, :] += column_sum(top)
    sums_ref[5:6, :] += column_sum(d_ffn.astype(F32))


def feed(pack, meta, x_own, cot_own, vectors, up_bias, att, own, pieces):
    row_count, model_width = x_own.shape
    feed_width = pack.feed_width
    att_width = att[0].shape[1]
    one = rows_of((ROW_BLOCK, model_width))
    wide = rows_of((ROW_BLOCK, feed_width))
    narrow = rows_of((ROW_BLOCK, att_width))
    turned = pl.BlockSpec((model_width, ROW_BLOCK), lambda i: (0, i))
    turned_shape = jax.ShapeDtypeStruct((model_width, row_count), BF16)

    def like(width, dtype=BF16):
        return jax.ShapeDtypeStruct((row_count, width), dtype)

    return pl.pallas_call(
        partial(feed_kernel, pack, len(att)),
        grid=(row_count // ROW_BLOCK,),
        in_specs=[IN_SMEM, one, one, whole(vectors.shape), whole(up_bias.shape)]
        + [narrow] * len(att)
        + [ANYWHERE] * (3 + len(pieces)),
        out_specs=[one, turned, one, turned, wide, wide, one, turned]
        + [narrow] * len(att)
        + [whole((8, model_width)), whole((1, feed_width))],
        out_shape=[
            like(model_width),
            turned_shape,
            like(model_width),
            turned_shape,
            like(feed_width),
            like(feed_width),
            like(model_width, F32),
            turned_shape,
        ]
        + [like(att_width)] * len(att)
        + [
            jax.ShapeDtypeStruct((8, model_width), F32),
            jax.ShapeDtypeStruct((1, feed_width), F32),
        ],
        scratch_shapes=[
            pltpu.VMEM((model_width, model_width), BF16),
            pltpu.VMEM((model_width, feed_width), BF16),
            pltpu.VMEM((feed_width, model_width), BF16),
            pltpu.VMEM((ROW_BLOCK, feed_width), F32),
            pltpu.SemaphoreType.DMA((3, 1 + pack.blocks * len(pieces))),
        ],
        name="feed",
        **params(
            40, 2 * row_count * model_width * (2 * model_width + 4 * feed_width), 40_000_000
        ),
    )(meta, x_own, cot_own, vectors, up_bias, *att, *own, *pieces)


def down_grads_kernel(pack, table, d_ffn_ref, hidden_ref, theirs_ref, mine_ref, made, sems):
    step = pl.program_id(0)
    core = table[0]

    def stores(shard):
        return [
            pltpu.make_async_copy(made.at[1 - core, shard], theirs_ref.at[shard], sems.at[0, shard]),
            pltpu.make_async_copy(made.at[core, shard], mine_ref.at[shard], sems.at[1, shard]),
        ]

    grad = dot(d_ffn_ref[...], hidden_ref[...]).astype(BF16)
    for half in range(CORES):
        for lane in range(0, pack.model_width, pack.feed_shard):
            begin = half * (pack.model_width // CORES) + lane // pack.feed_shard * pack.down_rows
            made[half, step, :, lane : lane + pack.feed_shard] = grad[
                begin : begin + pack.down_rows
            ]
    for copy in stores(step):
        copy.start()

    @pl.when(step == pack.shards - 1)
    def _():
        for shard in range(pack.shards):
            for copy in stores(shard):
                copy.wait()


def down_grads(pack, table, d_ffn, hidden):
    model_width, row_count = d_ffn.shape
    shape = (pack.shards, pack.down_rows, model_width)
    return pl.pallas_call(
        partial(down_grads_kernel, pack),
        grid_spec=pltpu.PrefetchScalarGridSpec(
            num_scalar_prefetch=1,
            grid=(pack.shards,),
            in_specs=[
                pl.BlockSpec(d_ffn.shape, lambda step, table: (0, 0)),
                pl.BlockSpec((row_count, pack.feed_shard), lambda step, table: (0, step)),
            ],
            out_specs=[ANYWHERE] * 2,
            scratch_shapes=[
                pltpu.VMEM((CORES,) + shape, BF16),
                pltpu.SemaphoreType.DMA((CORES, pack.shards)),
            ],
        ),
        out_shape=[jax.ShapeDtypeStruct(shape, BF16)] * 2,
        name="down_grads",
        **params(60, 2 * row_count * model_width * pack.feed_width, 10_000_000),
    )(table, d_ffn, hidden)


def rest_grads_kernel(
    pack, table, first_ref, d_pre_ref, att_ref, d_branch_ref, theirs_ref, mine_ref, *scratch
):
    att, d_branch, tile, made, in_sems, sems = scratch
    step = pl.program_id(0)
    core, member = table[0], table[1]
    shards, blocks = pack.shards, pack.blocks
    out_at = pack.out_at - pack.down_rows

    loads = [
        pltpu.make_async_copy(att_ref, att, in_sems.at[0]),
        pltpu.make_async_copy(d_branch_ref, d_branch, in_sems.at[1]),
    ]

    def store(half, start, rows, sem):
        there = (slice(None), pl.ds(start, rows), slice(None))

        def copy(target):
            return pltpu.make_async_copy(
                made.at[(half,) + there], target.at[there], sems.at[half, sem]
            )

        return copy

    def both(half, start, rows, sem, act):
        copy = store(half, start, rows, sem)

        @pl.when(core == half)
        def _():
            act(copy(mine_ref))

        @pl.when(core != half)
        def _():
            act(copy(theirs_ref))

    @pl.when(step == 0)
    def _():
        for copy in loads:
            copy.start()

    @pl.when(step < CORES * blocks)
    def _():
        grad = dot(first_ref[...], d_pre_ref[...]).astype(BF16)
        start = pl.multiple_of(step % blocks * pack.row_shard, 16)
        for shard in range(shards):
            made[step // blocks, shard, pl.ds(start, pack.row_shard), :] = grad[
                shard * pack.row_shard : (shard + 1) * pack.row_shard
            ]

    for half in range(CORES):

        @pl.when(step == (half + 1) * blocks - 1)
        def _(half=half):
            both(half, 0, out_at, 0, lambda copy: copy.start())

    @pl.when(step == CORES * blocks)
    def _():
        for copy in loads:
            copy.wait()
        tile[...] = dot(att[...], d_branch[...])
        spare = pack.rows - pack.used
        for half in range(CORES):
            for shard in range(shards):
                start = pack.out_start(shard, member) + half * pack.out_rows
                start = pl.multiple_of(start, 16)
                made[half, shard, out_at : out_at + pack.out_rows, :] = tile[
                    pl.ds(start, pack.out_rows), :
                ].astype(BF16)
                if spare:
                    made[half, shard, out_at + pack.out_rows :, :] = jnp.zeros(
                        (spare, pack.model_width), BF16
                    )
            both(half, out_at, pack.rest_rows - out_at, 1, lambda copy: copy.start())
        for half in range(CORES):
            both(half, 0, out_at, 0, lambda copy: copy.wait())
            both(half, out_at, pack.rest_rows - out_at, 1, lambda copy: copy.wait())


def rest_grads(pack, table, first_low, d_pre, att, d_branch, needs=()):
    model_width, row_count = first_low.shape
    shape = (pack.shards, pack.rest_rows, model_width)
    steps = CORES * pack.blocks
    return pl.pallas_call(
        gated(partial(rest_grads_kernel, pack), 5, needs),
        grid_spec=pltpu.PrefetchScalarGridSpec(
            num_scalar_prefetch=1,
            grid=(steps + 1,),
            in_specs=[
                pl.BlockSpec(first_low.shape, lambda step, table: (0, 0)),
                pl.BlockSpec(
                    (row_count, model_width),
                    lambda step, table: (0, jnp.minimum(step, steps - 1)),
                ),
            ]
            + [ANYWHERE] * (2 + len(needs)),
            out_specs=[ANYWHERE] * 2,
            scratch_shapes=[
                pltpu.VMEM((model_width, row_count), BF16),
                pltpu.VMEM((row_count, model_width), BF16),
                pltpu.VMEM((model_width, model_width), F32),
                pltpu.VMEM((CORES,) + shape, BF16),
                pltpu.SemaphoreType.DMA((2,)),
                pltpu.SemaphoreType.DMA((CORES, 2)),
            ],
        ),
        out_shape=[jax.ShapeDtypeStruct(shape, BF16)] * 2,
        name="rest_grads",
        **params(60, 2 * row_count * model_width * (pack.feed_width + model_width), 10_000_000),
    )(table, first_low, d_pre, att, d_branch, *needs)


def qkv_grads_kernel(rounds, x_refs_then, *refs):
    refs = (x_refs_then,) + refs
    x_refs, grad_refs = refs[:rounds], refs[rounds : 2 * rounds]
    small_ref, out_ref = refs[2 * rounds :]
    shards, rows, _ = out_ref.shape
    row_shard = rows - small_ref.shape[1]
    total, sums = None, None
    for x_ref, grad_ref in zip(x_refs, grad_refs):
        grads = grad_ref[...]
        term = dot(x_ref[...], grads)
        down = column_sum(grads.astype(F32))
        total = term if total is None else total + term
        sums = down if sums is None else sums + down
    total = total.astype(BF16)
    row = lax.broadcasted_iota(jnp.int32, small_ref.shape[1:], 0)
    for shard in range(shards):
        out_ref[shard, :row_shard, :] = total[shard * row_shard : (shard + 1) * row_shard]
        last = jnp.where(row == BIAS_ROW, sums, small_ref[shard])
        out_ref[shard, row_shard:, :] = last.astype(BF16)


def qkv_grads(x_turned, grads, small, row_shard, needs=()):
    rounds = len(grads)
    model_width, positions = x_turned[0].shape
    cols = grads[0].shape[1]
    shards, extra, _ = small.shape
    block = GRAD_LANES if cols % GRAD_LANES == 0 else cols
    return pl.pallas_call(
        gated(partial(qkv_grads_kernel, rounds), 2 * rounds + 1, needs),
        grid=(cols // block,),
        in_specs=[whole((model_width, positions))] * rounds
        + [pl.BlockSpec((positions, block), lambda i: (0, i))] * rounds
        + [pl.BlockSpec((shards, extra, block), lambda i: (0, 0, i))]
        + [ANYWHERE] * len(needs),
        out_specs=pl.BlockSpec((shards, row_shard + extra, block), lambda i: (0, 0, i)),
        out_shape=jax.ShapeDtypeStruct((shards, row_shard + extra, cols), BF16),
        name="qkv_grads",
        **params(28, 2 * rounds * positions * model_width * cols, 18_000_000),
    )(*x_turned, *grads, small, *needs)


def add_picked_kernel(count, first, table, *refs):
    in_refs, out_refs = refs[:count], refs[count:]
    if count == 2:
        total = in_refs[0][...] + in_refs[1][...]
    else:
        total = in_refs[0][...].astype(F32)
        for ref in in_refs[1:]:
            total = total + ref[...].astype(F32)
        total = total.astype(BF16)
    if len(out_refs) == 1:
        out_refs[0][...] = total
        return

    @pl.when(pl.program_id(0) < first)
    def _():
        out_refs[0][...] = total

    @pl.when(pl.program_id(0) >= first)
    def _():
        out_refs[1][...] = total


def add_picked(table, arrays, steps, first=None, needs=(), work=0):
    _, rows, cols = arrays[0].shape
    parts = 2 if rows % 32 == 0 and steps == 1 else 1
    block = (1, rows // parts, cols)
    spec = [
        pl.BlockSpec(block, lambda s, p, t, k=k: (t[k * steps + s], p, 0))
        for k in range(len(arrays))
    ]
    if first is None:
        out_specs = [pl.BlockSpec(block, lambda s, p, t: (s, p, 0))]
        counts = [steps]
    else:
        out_specs = [
            pl.BlockSpec(
                block,
                lambda s, p, t: (
                    jnp.minimum(s, first - 1),
                    jnp.where(s < first, p, parts - 1),
                    0,
                ),
            ),
            pl.BlockSpec(
                block,
                lambda s, p, t: (jnp.maximum(s - first, 0), jnp.where(s < first, 0, p), 0),
            ),
        ]
        counts = [first, steps - first]
    return pl.pallas_call(
        gated(partial(add_picked_kernel, len(arrays), first), 1 + len(arrays), needs),
        grid_spec=pltpu.PrefetchScalarGridSpec(
            num_scalar_prefetch=1,
            grid=(steps, parts),
            in_specs=spec + [ANYWHERE] * len(needs),
            out_specs=out_specs,
        ),
        out_shape=[jax.ShapeDtypeStruct((n, rows, cols), BF16) for n in counts],
        name="add_picked",
        compiler_params=pltpu.CompilerParams(
            dimension_semantics=("arbitrary", "arbitrary"), vmem_limit_bytes=12 * MIB
        ),
        cost_estimate=pl.CostEstimate(flops=work, bytes_accessed=1_000_000, transcendentals=0),
    )(table, *arrays, *needs)


def join_kernel(count, down_kept, down_landed, rest_kept, rest_landed, *outs):
    rows = down_kept.shape[1]
    for index in range(count):
        target = outs[1 - index % 2] if count > 1 else outs[0]
        place_now = index // 2
        target[place_now, :rows, :] = down_kept[index] + down_landed[index]
        target[place_now, rows:, :] = rest_kept[index] + rest_landed[index]


def join(kept, landed, needs=()):
    count = kept[0].shape[0]
    rows = kept[0].shape[1] + kept[1].shape[1]
    shape = jax.ShapeDtypeStruct(((count + 1) // 2, rows, kept[0].shape[2]), BF16)
    vmem = pl.BlockSpec(memory_space=pltpu.VMEM)
    outs = pl.pallas_call(
        gated(partial(join_kernel, count), 4, needs),
        in_specs=[vmem] * 4 + [ANYWHERE] * len(needs),
        out_specs=[vmem] * min(count, 2),
        out_shape=[shape] * min(count, 2),
        name="join",
        compiler_params=pltpu.CompilerParams(vmem_limit_bytes=24 * MIB),
        cost_estimate=pl.CostEstimate(flops=0, bytes_accessed=200_000, transcendentals=0),
    )(kept[0], landed[0], kept[1], landed[1], *needs)
    return outs if count > 1 else (None, outs[0])


def stack_kernel(count, *refs):
    for index in range(count):
        refs[count][index] = refs[index][...]


def split_kernel(in_ref, *out_refs):
    rows = out_refs[0].shape[0]
    for index, ref in enumerate(out_refs):
        ref[...] = in_ref[index * rows : (index + 1) * rows, :]


def split_rows(value, count, needs=()):
    rows = value.shape[0] // count
    vmem = pl.BlockSpec(memory_space=pltpu.VMEM)
    return pl.pallas_call(
        gated(split_kernel, 1, needs),
        in_specs=[vmem] + [ANYWHERE] * len(needs),
        out_specs=[vmem] * count,
        out_shape=[jax.ShapeDtypeStruct((rows, value.shape[1]), value.dtype)] * count,
        name="split_rows",
        compiler_params=pltpu.CompilerParams(vmem_limit_bytes=12 * MIB),
        cost_estimate=pl.CostEstimate(flops=0, bytes_accessed=100_000, transcendentals=0),
    )(value, *needs)


def stack_up(pieces, needs=()):
    vmem = pl.BlockSpec(memory_space=pltpu.VMEM)
    return pl.pallas_call(
        gated(partial(stack_kernel, len(pieces)), len(pieces), needs),
        in_specs=[vmem] * len(pieces) + [ANYWHERE] * len(needs),
        out_specs=vmem,
        out_shape=jax.ShapeDtypeStruct((len(pieces),) + pieces[0].shape, BF16),
        name="stack_up",
        compiler_params=pltpu.CompilerParams(vmem_limit_bytes=24 * MIB),
        cost_estimate=pl.CostEstimate(flops=0, bytes_accessed=100_000, transcendentals=0),
    )(*pieces, *needs)


def unpack_kernel(pack, depth, meta, mine_ref, other_ref, down_ref, up_ref, out_ref, ordered):
    core, level = meta[2], meta[4]
    rows = pack.rows // depth
    for mask in range(depth):
        start = pl.multiple_of(lax.bitwise_xor(level, mask) * rows, 16)
        ordered[core, pl.ds(start, rows), :] = mine_ref[mask]
        ordered[1 - core, pl.ds(start, rows), :] = other_ref[mask]
    turned = []
    for half in range(CORES):
        for lane in range(0, pack.model_width, pack.feed_shard):
            turned.append(ordered[half, : pack.down_rows, lane : lane + pack.feed_shard])
    down_ref[...] = jnp.transpose(jnp.concatenate(turned, axis=0)).astype(F32)
    for half in range(CORES):
        for block in range(pack.blocks):
            lane = (half * pack.blocks + block) * pack.model_width
            start = pack.up_at + block * pack.row_shard
            up_ref[:, lane : lane + pack.model_width] = ordered[
                half, start : start + pack.row_shard, :
            ].astype(F32)
        out_ref[half * pack.out_rows : (half + 1) * pack.out_rows, :] = ordered[
            half, pack.out_at : pack.out_at + pack.out_rows, :
        ].astype(F32)


def unpack(pack, depth, meta, mine, other):
    vmem = pl.BlockSpec(memory_space=pltpu.VMEM)
    return pl.pallas_call(
        partial(unpack_kernel, pack, depth),
        in_specs=[IN_SMEM, vmem, vmem],
        out_specs=[vmem] * 3,
        out_shape=[
            jax.ShapeDtypeStruct((pack.feed_shard, pack.model_width), F32),
            jax.ShapeDtypeStruct((pack.row_shard, pack.feed_width), F32),
            jax.ShapeDtypeStruct((pack.row_shard, pack.model_width), F32),
        ],
        scratch_shapes=[pltpu.VMEM((CORES, pack.rows, pack.model_width), BF16)],
        name="unpack",
        compiler_params=pltpu.CompilerParams(vmem_limit_bytes=24 * MIB),
        cost_estimate=pl.CostEstimate(flops=0, bytes_accessed=10_000_000, transcendentals=0),
    )(meta, mine, other)


def unpack_qkv_kernel(meta, mine_ref, other_ref, grad_ref, bias_ref, small_ref):
    member = meta[3]
    row_shard, width = grad_ref.shape[0], grad_ref.shape[1] // 3
    part = mine_ref.shape[1] // 3
    for ref, at in ((mine_ref, member), (other_ref, 1 - member)):
        for kind in range(3):
            lane = pl.multiple_of(kind * width + at * part, CLUSTER_ROWS)
            from_lanes = slice(kind * part, (kind + 1) * part)
            grad_ref[:, pl.ds(lane, part)] = ref[:row_shard, from_lanes].astype(F32)
            lane = pl.multiple_of(at * part, CLUSTER_ROWS)
            bias_ref[kind : kind + 1, pl.ds(lane, part)] = ref[row_shard:, from_lanes].astype(F32)[
                BIAS_ROW : BIAS_ROW + 1
            ]
    small_ref[...] = (mine_ref[row_shard:, :].astype(F32) + other_ref[row_shard:, :].astype(F32))[
        :BIAS_ROW
    ]


def unpack_qkv(meta, mine, other, row_shard, needs=()):
    cols = mine.shape[1]
    vmem = pl.BlockSpec(memory_space=pltpu.VMEM)
    return pl.pallas_call(
        gated(unpack_qkv_kernel, 3, needs),
        in_specs=[IN_SMEM, vmem, vmem] + [ANYWHERE] * len(needs),
        out_specs=[vmem] * 3,
        out_shape=[
            jax.ShapeDtypeStruct((row_shard, CORES * cols), F32),
            jax.ShapeDtypeStruct((3, CORES * cols // 3), F32),
            jax.ShapeDtypeStruct((BIAS_ROW, cols), F32),
        ],
        name="unpack_qkv",
        compiler_params=pltpu.CompilerParams(vmem_limit_bytes=16 * MIB),
        cost_estimate=pl.CostEstimate(flops=0, bytes_accessed=200_000, transcendentals=0),
    )(meta, mine, other, *needs)


def tie(*values):
    return lax.optimization_barrier(values)


def body(
    tokens,
    cotangent,
    perms,
    unit_kind,
    w_qkv,
    bias_qv,
    w_out,
    bias_out,
    ln_gain,
    ln_bias,
    w_up,
    bias_up,
    w_down,
    bias_down,
):
    shards = lax.axis_size("fsdp")
    groups = lax.axis_size("dp")
    here = lax.axis_index("fsdp")
    dp_index = lax.axis_index("dp")
    core = dp_index % CORES
    level = dp_index // CORES
    depth = groups // CORES
    units, rounds, unit_len = perms.shape
    per_device = unit_len // shards
    model_width = tokens.shape[1]
    feed_width = w_up.shape[1]
    row_shard = model_width // shards
    members = shards // units
    member_rows = unit_len // members
    head_cols = model_width // members
    padded = -(-head_cols // CLUSTER_ROWS) * CLUSTER_ROWS
    spot = here * CORES + core
    home_core = spot // shards
    unit = (spot // members) % units
    member = spot % members
    pack = Pack(model_width, feed_width, shards, units, depth)
    bits = [1 << k for k in range(shards.bit_length() - 1)]
    bit_orders = (bits, bits[::-1])

    def plane_pairs(target):
        pairs = []
        for z in range(depth):
            for f_index in range(shards):
                for c_index in range(CORES):
                    f_new, c_new = target(f_index, c_index)
                    pairs.append(
                        (
                            (z * CORES + c_index) * shards + f_index,
                            (z * CORES + c_new) * shards + f_new,
                        )
                    )
        return pairs

    def send(value, pairs):
        return lax.ppermute(value, ("dp", "fsdp"), pairs)

    def cross(value, mask):
        return send(value, plane_pairs(lambda f, c: divmod((f * CORES + c) ^ mask, CORES)))

    def trade(value, stage):
        return send(value, plane_pairs(lambda f, c: (f ^ bit_orders[c][stage], c)))

    def trade_mask(index, which):
        mask = 0
        for stage in range(len(bits)):
            if index >> stage & 1:
                mask ^= bit_orders[which][stage]
        return mask

    def climb(value, mask):
        plane = CORES * shards
        pairs = []
        for z in range(depth):
            for rest in range(plane):
                pairs.append((z * plane + rest, (z ^ mask) * plane + rest))
        return send(value, pairs)

    def outward(step):
        def target(f, c):
            place_now = (c * units + (f % units + step) % units) * members + f // units
            return divmod(place_now, CORES)

        return plane_pairs(target)

    def homeward(step):
        return [(b, a) for a, b in outward(step)]

    def bring_start(value):
        blocks = value.reshape(units, per_device, model_width)
        return [
            lax.dynamic_index_in_dim(blocks, (here % units + step) % units, axis=0, keepdims=False)
            for step in range(units)
        ]

    def bring(chosen):
        return jnp.concatenate(
            [send(chosen[step], outward(step)) for step in range(units)], axis=0
        )

    def send_home(blocks):
        return [send(blocks[step], homeward(step)) for step in range(units)]

    def in_order(landed, dtype):
        if units == 2:
            swap = here % units == 1
            wanted = [
                jnp.where(swap, landed[1], landed[0]),
                jnp.where(swap, landed[0], landed[1]),
            ]
        else:
            stacked = jnp.stack(landed)
            wanted = [
                lax.dynamic_index_in_dim(stacked, (index - here % units) % units, 0, keepdims=False)
                for index in range(units)
            ]
        return jnp.concatenate(wanted, axis=0).astype(dtype)

    x_chosen = bring_start(tokens)
    x_own = bring(x_chosen)
    small = jnp.concatenate(
        [
            bias_qv.reshape(-1),
            bias_out,
            ln_gain.reshape(-1),
            ln_bias.reshape(-1),
            bias_up,
            bias_down,
        ]
    )
    small_rows = -(-small.shape[0] // (3 * padded))
    small_block = jnp.pad(
        jnp.pad(small, (0, small_rows * 3 * padded - small.shape[0])).reshape(
            small_rows, 3 * padded
        ),
        ((0, 16 - small_rows), (0, 0)),
    )
    def columns_for(offset):
        start = lax.bitwise_xor(member, offset) * head_cols
        blocks = [
            jnp.pad(
                lax.dynamic_slice(
                    w_qkv, (0, kind * model_width + start), (row_shard, head_cols)
                ),
                ((0, 0), (0, padded - head_cols)),
            )
            for kind in range(3)
        ]
        return jnp.concatenate([jnp.concatenate(blocks, axis=1), small_block], axis=0)

    offsets = [(CORES * m) % members for m in range(shards)]
    kinds = sorted(set(offsets))
    order_pack = jnp.concatenate(
        [perms.reshape(-1), jnp.broadcast_to(unit_kind[:, None], (units, 128)).reshape(-1)]
    )
    order_other = cross(order_pack, 1)
    *tied, order_other = tie(*[columns_for(offset) for offset in kinds], order_other)
    piece_kinds = dict(zip(kinds, tied))
    x_pieces = [x_own] + [cross(x_own, mask) for mask in range(1, members)]
    qkv_pieces = [piece_kinds[0]] + [
        cross(piece_kinds[offsets[m]], CORES * m) for m in range(1, shards)
    ]
    order_pack = jnp.where(home_core == core, order_pack, order_other)
    order_count = units * rounds * unit_len
    unit_perm = lax.dynamic_index_in_dim(
        order_pack[:order_count].reshape(units, rounds * unit_len), unit, 0, keepdims=False
    )
    kind_now = lax.dynamic_index_in_dim(
        order_pack[order_count:].reshape(units, 128), unit, 0, keepdims=False
    )[0]
    owner = unit_perm // per_device
    order = (
        lax.bitwise_xor(owner // units, member) * units + (unit - owner % units) % units
    ) * per_device + unit_perm % per_device
    order = order.reshape(rounds, unit_len)
    order = jnp.where(core == 0, order, order[::-1])
    order_row = order.reshape(1, rounds * unit_len)
    order = order.reshape(-1, CLUSTER_ROWS)
    x_here = arrange(order, x_pieces, unit_len, 0)
    x_now = [x_here, cross(x_here, 1)]
    own_masks = [
        jnp.where(core == 0, trade_mask(i, 0), trade_mask(i, 1)) for i in range(1, shards)
    ]
    other_masks = [
        jnp.where(core == 0, trade_mask(i, 1), trade_mask(i, 0)) for i in range(1, shards)
    ]
    zero = jnp.int32(0)
    meta = jnp.stack(
        [kind_now, here, core, member, level, zero, zero, zero] + own_masks + other_masks
    ).astype(jnp.int32)

    def half_of(value, axis, length, at):
        return lax.dynamic_slice_in_dim(value, at * length, length, axis=axis)

    packed = jnp.concatenate(
        [half_of(w_down, 0, pack.down_rows, core)]
        + [
            half_of(w_up, 1, model_width, core * pack.blocks + block)
            for block in range(pack.blocks)
        ]
        + [half_of(w_out, 0, pack.out_rows, core)],
        axis=0,
    )
    order_rows = unit_len // CLUSTER_ROWS
    arranged, probs, mixtures, x_turned = [], [], [], []
    *tied, packed, x_now[0] = tie(*qkv_pieces[1:], packed, x_now[0])
    qkv_pieces = qkv_pieces[:1] + tied
    smalls = jnp.stack(
        [
            piece[row_shard : row_shard + small_rows].reshape(-1)[: small.shape[0]]
            for piece in qkv_pieces
        ]
    )
    smalls = jnp.take(smalls, lax.bitwise_xor(here, jnp.arange(shards)), axis=0).astype(F32)

    def vectors_at(start, count, length):
        part = smalls[:, start * row_shard : start * row_shard + count * length]
        return (
            part.reshape(shards, count, length).transpose(1, 0, 2).reshape(count, shards * length)
        )

    my_bias = lax.dynamic_index_in_dim(
        vectors_at(0, 2, row_shard).reshape(2, members, head_cols), member, 1, keepdims=False
    )
    my_bias = jnp.pad(my_bias, ((0, 0), (0, padded - head_cols)))
    my_bias = jnp.stack([my_bias[0], jnp.zeros_like(my_bias[0]), my_bias[1]]).reshape(1, -1)
    up_bias = vectors_at(7, 1, feed_width // shards)
    down_bias = smalls[:, small.shape[0] - row_shard :].reshape(1, model_width)
    vectors = jnp.concatenate(
        [vectors_at(2, 5, row_shard), down_bias, jnp.zeros((2, model_width), F32)], axis=0
    )

    weight_pieces = {0: packed}
    for stage in range(len(bits)):
        weight_pieces[1 << stage] = trade(packed, stage)
    for index in range(rounds):
        results = attend(meta, x_now[index], my_bias, qkv_pieces, row_shard, mixtures[-1:])
        for kept, result in zip((arranged, probs, mixtures, x_turned), results):
            kept.append(result)
    cot_now, mixtures[0] = tie(cotangent, mixtures[0])
    cot_landed = [
        send(value, outward(step)) for step, value in enumerate(bring_start(cot_now))
    ]
    cot_own = jnp.concatenate(cot_landed, axis=0)
    for stage in range(1, len(bits)):
        for index in range(1, 1 << stage):
            weight_pieces[index | 1 << stage] = trade(weight_pieces[index], stage)
    att_there, att_sent = [], []
    for mask in range(1, members):
        there = place(
            order_row, mixtures, mask * member_rows, member_rows, 0.5, needs=cot_landed
        )
        att_sent.append(there)
        att_there.append(cross(there[:, :head_cols], mask))
    att_here = place(order_row, mixtures, 0, member_rows, 0.5, needs=att_sent)

    direct = [weight_pieces[index] for index in range(1, shards)]
    swapped = [cross(piece, 1) for piece in direct[:-1]]
    last_piece, att_here = tie(direct[-1], att_here)
    swapped.append(cross(last_piece, 1))
    att_raw = [att_here[:, :head_cols]] + att_there
    if head_cols % CLUSTER_ROWS:
        att_raw = [jnp.concatenate(att_raw, axis=1)]
    block_out, first_low, d_branch, d_ffn, hidden, d_pre, d_lower, att_turned, *rest = feed(
        pack,
        meta,
        x_own,
        cot_own,
        vectors,
        up_bias,
        att_raw,
        [w_out, w_up, w_down],
        direct + swapped,
    )
    d_att, (row_sums, up_sums) = rest[: len(att_raw)], rest[len(att_raw) :]
    if head_cols % CLUSTER_ROWS:
        d_att = [d_att[0][:, mask * head_cols : (mask + 1) * head_cols] for mask in range(members)]
    d_att = [d_att[0]] + [cross(d_att[mask], mask) for mask in range(1, members)]
    d_att = [jnp.pad(piece, ((0, 0), (0, padded - head_cols))) for piece in d_att]

    table = jnp.stack([core, member]).astype(jnp.int32)
    sending = [index for index in range(shards) if index & 1]
    keeping = [index for index in range(shards) if not index & 1]
    slots = jnp.stack(
        [
            lax.bitwise_xor(here, jnp.where(core == 0, trade_mask(i, 0), trade_mask(i, 1)))
            for i in sending + keeping
        ]
    )
    slots = jnp.concatenate([slots, slots]).astype(jnp.int32)

    def pair_sum(mine, theirs, needs):
        return add_picked(
            slots, [mine, cross(theirs, 1)], shards, len(sending), needs, 20_000_000_000
        )

    theirs_down, mine_down = down_grads(pack, table, d_ffn, hidden)
    theirs_rest, mine_rest = rest_grads(
        pack, table, first_low, d_pre, att_turned, d_branch, [theirs_down]
    )
    down_going, down_kept = pair_sum(mine_down, theirs_down, [theirs_rest])
    rest_going, rest_kept = pair_sum(mine_rest, theirs_rest, [down_going] + d_att[1:])

    def merge(kept, landed, *needs):
        count = kept.shape[0]
        if count == 1:
            table = jnp.zeros((2,), jnp.int32)
            return None, add_picked(table, [kept, landed], 1, None, needs)[0]
        order_now = [i for i in range(count) if i & 1] + [i for i in range(count) if not i & 1]
        table = jnp.array(order_now * 2, jnp.int32)
        return add_picked(table, [kept, landed], count, count // 2, needs)

    grads, d_x = [None] * rounds, [None] * rounds
    needs = [rest_going]
    blocks = unit_len // POS_BLOCK
    spans = [(rounds - 1, (0, blocks))]
    for index in reversed(range(rounds - 1)):
        spans += [(index, (0, blocks // 2)), (index, (blocks // 2, blocks))]
    results = []
    for turn, (index, span) in enumerate(spans):
        results = attend_back(
            meta,
            order,
            arranged[index],
            probs[index],
            d_att,
            qkv_pieces,
            row_shard,
            index * order_rows,
            needs,
            span,
            results if span[0] else [],
        )
        grads[index], d_x[index] = results
        if turn == 0:
            d_x_there = cross(d_x[index], 1)
        if turn == 0:
            going, kept = join(
                [down_kept, rest_kept], [trade(down_going, 0), trade(rest_going, 0)], [results[0]]
            )
            needs = [kept]
        elif turn < len(bits):
            going, kept = merge(kept, trade(going, turn), results[0])
            needs = [kept, d_x_there]
        if turn == len(spans) - 2:
            output_landed = send_home(split_rows(block_out, units, [kept]))
    for stage in range(len(spans), len(bits)):
        going, kept = merge(kept, trade(going, stage))

    def level_pieces(block):
        return block.reshape((depth, block.shape[0] // depth) + block.shape[1:])

    def level_scatter(cut):
        return [
            climb(
                lax.dynamic_index_in_dim(cut, lax.bitwise_xor(level, mask), 0, keepdims=False), mask
            )
            for mask in range(1, depth)
        ]

    def level_gather(piece):
        pieces = {0: piece}
        mask = depth // 2
        while mask:
            pieces[mask] = climb(piece, mask)
            mask //= 2
        return pieces

    def level_forward(pieces):
        for index in sorted(range(depth), key=lambda value: value.bit_count()):
            if index not in pieces:
                low = index & -index
                pieces[index] = climb(pieces[index ^ low], low)
        return [pieces[index] for index in range(depth)]

    def by_shard(value):
        count, length = value.shape
        return (
            value.reshape(count, shards, length // shards)
            .transpose(1, 0, 2)
            .reshape(shards, count * length // shards)
        )

    small_grad = jnp.concatenate(
        [by_shard(row_sums[:5]), by_shard(up_sums), by_shard(row_sums[5:6])], axis=1
    )
    small_length = small_grad.shape[1]
    small_lanes = 3 * head_cols
    small_grad = jnp.pad(small_grad, ((0, 0), (0, BIAS_ROW * small_lanes - small_length)))
    small_grad = jnp.pad(
        small_grad.reshape(shards, BIAS_ROW, small_lanes), ((0, 0), (0, 16 - BIAS_ROW), (0, 0))
    )
    extra_rows = 16
    x_last, kept, small_grad = tie(x_turned[0], kept, small_grad)
    if padded == head_cols:
        joined = qkv_grads(
            [x_last, x_turned[1]], grads, small_grad, row_shard, output_landed
        )
    else:
        qkv_grad = dot(x_last, grads[0]) + dot(x_turned[1], grads[1])
        qkv_grad = qkv_grad.reshape(shards, row_shard, 3, padded)[..., :head_cols]
        bias_sum = sum(jnp.sum(value.astype(F32), axis=0) for value in grads)
        bias_sum = bias_sum.reshape(3, padded)[:, :head_cols].reshape(small_lanes)
        small_grad = small_grad.at[:, BIAS_ROW].set(bias_sum[None])
        joined = jnp.concatenate(
            [qkv_grad.reshape(shards, row_shard, small_lanes), small_grad], axis=1
        ).astype(BF16)
    cut = level_pieces(kept[0])
    landed = level_scatter(cut)
    classes = max(1, members // CORES)
    d_x_parts = [d_x[0], d_x_there]
    order_mine = order_row[:, :unit_len]
    if classes == 1:
        slots_held = jnp.stack(
            [
                lax.bitwise_xor(here, jnp.where(core == 0, trade_mask(i, 0), trade_mask(i, 1)))
                for i in range(shards)
            ]
        )
        held = jnp.stack(
            [
                lax.dynamic_index_in_dim(joined, slots_held[i], 0, keepdims=False)
                for i in range(0, shards, 2)
            ]
        )
        leaving = jnp.stack(
            [
                lax.dynamic_index_in_dim(joined, slots_held[i], 0, keepdims=False)
                for i in range(1, shards, 2)
            ]
        )
        totals = None
    else:
        totals = [None] * classes
        for m in range(shards):
            offset = offsets[m] // CORES
            piece = lax.dynamic_index_in_dim(joined, lax.bitwise_xor(here, m), 0, keepdims=False)
            piece = (piece if m == 0 else cross(piece, CORES * m)).astype(F32)
            totals[offset] = piece if totals[offset] is None else totals[offset] + piece

    if depth > 1:
        picks = jnp.concatenate([level[None], jnp.zeros((depth - 1,), level.dtype)])
        (kept,) = add_picked(
            picks.astype(jnp.int32),
            [cut] + [piece[None] for piece in landed],
            1,
            None,
            [joined] if totals is not None else [leaving],
        )
    d_there = [
        place(
            order_mine,
            d_x_parts,
            mask * member_rows,
            member_rows,
            added=True,
            needs=[kept],
        )
        for mask in range(1, members)
    ]
    gathered = level_gather(kept[0]) if depth > 1 else {0: cut[0]}
    early = list(d_there)
    if totals is None:
        leaving, held = merge(held, trade(leaving, 0), *d_there)
        early.append(held)
    d_here = place(
        order_mine,
        d_x_parts,
        0,
        member_rows,
        1.0,
        F32,
        d_lower,
        added=True,
        needs=early,
    )
    d_inputs = d_here
    for mask, there in enumerate(d_there, 1):
        d_inputs = d_inputs + cross(there, mask).astype(F32)
    d_inputs = d_inputs.astype(BF16)
    if totals is None:
        for stage in range(1, len(bits)):
            leaving, held = merge(held, trade(leaving, stage), d_inputs)
        masks = [mask for mask in gathered if mask]
        *tied, held = tie(*[gathered[mask] for mask in masks], held)
        gathered.update(zip(masks, tied))
        totals = [held[0]]
    home = send_home(d_inputs.reshape(units, per_device, model_width))
    output = in_order(output_landed, BF16)
    totals = jnp.concatenate(totals, axis=0).astype(BF16)
    rows_each = row_shard + extra_rows
    if depth > 1:
        halves = totals.reshape((2, totals.shape[0] // 2) + totals.shape[1:])
        side = level % 2
        mine = lax.dynamic_index_in_dim(halves, side, 0, keepdims=False)
        theirs = lax.dynamic_index_in_dim(halves, 1 - side, 0, keepdims=False)
        half = (mine.astype(F32) + climb(theirs, 1).astype(F32)).astype(BF16)
        mask = 2
        while mask < depth:
            half = (half.astype(F32) + climb(half, mask).astype(F32)).astype(BF16)
            mask *= 2
        *home, half = tie(*home, half)
        other_half = climb(half, 1)
        totals = jnp.concatenate(
            [
                jnp.where(side == 0, half, other_half),
                jnp.where(side == 0, other_half, half),
            ],
            axis=0,
        )
    d_inputs = in_order(home, F32)
    stacked = stack_up(level_forward(gathered))
    grad_down, grad_up, grad_out = unpack(pack, depth, meta, stacked, cross(stacked, 1))
    if padded == head_cols and members == CORES:
        grad_qkv, bias_out_row, smalls_out = unpack_qkv(
            meta, totals, cross(totals, 1), row_shard, [grad_down, d_inputs, output]
        )
        smalls_out = smalls_out.reshape(-1)[:small_length]
        bias_out_row = lax.dynamic_slice(bias_out_row, (0, here * row_shard), (3, row_shard))
    else:
        landed = jnp.stack([totals, cross(totals, 1)], axis=0).reshape(
            CORES, classes, rows_each, 3 * head_cols
        )
        smalls_out = jnp.sum(
            landed[:, :, row_shard : row_shard + BIAS_ROW].astype(F32), axis=(0, 1)
        ).reshape(-1)[:small_length]
        landed = (
            landed.transpose(1, 0, 2, 3)
            .reshape(members, rows_each, 3, head_cols)[:, : row_shard + BIAS_ROW + 1]
        )
        if members == 2:
            swap = member == 1
            landed = jnp.stack(
                [
                    jnp.where(swap, landed[1], landed[0]),
                    jnp.where(swap, landed[0], landed[1]),
                ]
            )
        else:
            landed = jnp.take(landed, lax.bitwise_xor(member, jnp.arange(members)), axis=0)
        grad_qkv = landed[:, :row_shard].transpose(1, 2, 0, 3)
        grad_qkv = grad_qkv.reshape(row_shard, 3 * model_width).astype(F32)
        bias_out_row = landed[:, row_shard + BIAS_ROW].astype(F32).transpose(1, 0, 2)
        bias_out_row = lax.dynamic_slice(
            bias_out_row.reshape(3, model_width), (0, here * row_shard), (3, row_shard)
        )

    feed_shard = feed_width // shards
    spots = [0, row_shard, 3 * row_shard, 5 * row_shard]
    return (
        output,
        d_inputs,
        grad_qkv,
        bias_out_row[::2],
        grad_out,
        smalls_out[spots[0] : spots[1]],
        smalls_out[spots[1] : spots[2]].reshape(2, row_shard),
        smalls_out[spots[2] : spots[3]].reshape(2, row_shard),
        grad_up,
        smalls_out[spots[3] : spots[3] + feed_shard],
        grad_down,
        smalls_out[spots[3] + feed_shard :],
    )


def solution(mesh):
    placed = (
        P(("dp", "fsdp"), None),
        P(("dp", "fsdp"), None),
        P("dp", None, None),
        P("dp"),
        P("fsdp", None),
        P(None, "fsdp"),
        P("fsdp", None),
        P("fsdp"),
        P(None, "fsdp"),
        P(None, "fsdp"),
        P("fsdp", None),
        P("fsdp"),
        P("fsdp", None),
        P("fsdp"),
    )
    return jax.shard_map(
        body,
        mesh=mesh,
        in_specs=placed,
        out_specs=(
            P(("dp", "fsdp"), None),
            P(("dp", "fsdp"), None),
            P("fsdp", None),
            P(None, "fsdp"),
            P("fsdp", None),
            P("fsdp"),
            P(None, "fsdp"),
            P(None, "fsdp"),
            P("fsdp", None),
            P("fsdp"),
            P("fsdp", None),
            P("fsdp"),
        ),
        check_vma=False,
    )
```

```python
from functools import partial

import jax
import jax.numpy as jnp
from jax import lax
from jax.experimental import pallas as pl
from jax.experimental.pallas import tpu as pltpu
from jax.sharding import PartitionSpec as P

HEAD_DIM = 64
CORES = 2
NEG_FILL = -1000000000.0
EPSILON = 1e-05
SCALE = HEAD_DIM ** (-0.5)
BIAS_ROW = 2
GRAD_LANES = 384
CLUSTER_ROWS = 128
HALF_ROWS = 64
POS_BLOCK = 512
TOKEN_BLOCK = 512
ROW_BLOCK = 256
FF_BLOCK = 512
MIB = 1024 * 1024
NT = (((1,), (1,)), ((), ()))
TN = (((0,), (0,)), ((), ()))
F32 = jnp.float32
BF16 = jnp.bfloat16
ANYWHERE = pl.BlockSpec(memory_space=pl.ANY)
IN_SMEM = pl.BlockSpec(memory_space=pltpu.SMEM)


def whole(shape):
    return pl.BlockSpec(shape, lambda i: (0,) * len(shape))


def rows_of(shape):
    return pl.BlockSpec(shape, lambda i: (i,) + (0,) * (len(shape) - 1))


def dot(a, b, dims=(((1,), (0,)), ((), ()))):
    return lax.dot_general(a, b, dims, preferred_element_type=F32)


def params(mib, flops=0, moved=0, share=16):
    return dict(
        compiler_params=pltpu.CompilerParams(
            dimension_semantics=("arbitrary",),
            vmem_limit_bytes=mib * MIB,
        ),
        cost_estimate=pl.CostEstimate(
            flops=flops // share, bytes_accessed=moved // share, transcendentals=0
        ),
    )


def gated(kernel, used, needs):
    if not needs:
        return kernel

    def run(*refs):
        return kernel(*refs[:used], *refs[used + len(needs) :])

    return run


def lane_masks():
    lane = lax.broadcasted_iota(jnp.int32, (CLUSTER_ROWS, CLUSTER_ROWS), 1)
    low = (lane < HEAD_DIM).astype(F32)
    return low.astype(BF16), (1.0 - low).astype(BF16), lane < HEAD_DIM


def corners(first, second):
    blank = jnp.zeros_like(first)
    return jnp.concatenate(
        [
            jnp.concatenate([first, blank], axis=1),
            jnp.concatenate([blank, second], axis=1),
        ],
        axis=0,
    )


def both_heads(rows_now, low, high):
    return jnp.concatenate([rows_now * low, rows_now * high], axis=0)


def equal_ones(left, right):
    return jnp.where(left == right, jnp.ones((), BF16), jnp.zeros((), BF16))


def pick_rows(order_ref, first_row, unit_len):
    parts = []
    lane = lax.broadcasted_iota(jnp.int16, (CLUSTER_ROWS, CLUSTER_ROWS), 1)
    for part in range(POS_BLOCK // CLUSTER_ROWS):
        row = order_ref[pl.ds(first_row + part, 1), :]
        column = jnp.transpose(jnp.broadcast_to(row, (CLUSTER_ROWS, CLUSTER_ROWS)))
        column = column.astype(jnp.int16)
        pieces = [
            equal_ones(column, lane + jnp.int16(base)) for base in range(0, unit_len, CLUSTER_ROWS)
        ]
        parts.append(jnp.concatenate(pieces, axis=1))
    return jnp.concatenate(parts, axis=0)


def load_pieces(meta, x_refs, w_refs, x_all, w_all, sems, row_shard):
    member_rows = x_all.shape[0] // max(1, len(x_refs))
    copies = []
    for index, ref in enumerate(x_refs):
        copies.append(
            pltpu.make_async_copy(
                ref, x_all.at[pl.ds(index * member_rows, member_rows), :], sems.at[index]
            )
        )
    for index, ref in enumerate(w_refs):
        mask = meta[meta.shape[0] - len(w_refs) + index]
        start = pl.multiple_of(lax.bitwise_xor(meta[1], mask) * row_shard, 16)
        copies.append(
            pltpu.make_async_copy(
                ref.at[pl.ds(0, row_shard), :],
                w_all.at[pl.ds(start, row_shard), :],
                sems.at[len(x_refs) + index],
            )
        )
    for copy in copies:
        copy.start()
    for copy in copies:
        copy.wait()


def arrange_kernel(unit_len, first_row, order_ref, *refs):
    x_refs, out_ref = refs[:-1], refs[-1]
    step = pl.program_id(0)
    picks = pick_rows(order_ref, first_row + step * (POS_BLOCK // CLUSTER_ROWS), unit_len)
    rows = x_refs[0].shape[0]
    total = None
    for index, ref in enumerate(x_refs):
        term = dot(picks[:, index * rows : (index + 1) * rows], ref[...])
        total = term if total is None else total + term
    out_ref[...] = total.astype(BF16)


def arrange(order, x_pieces, position_count, first_row):
    member_rows, width = x_pieces[0].shape
    unit_len = member_rows * len(x_pieces)
    return pl.pallas_call(
        partial(arrange_kernel, unit_len, first_row),
        grid=(position_count // POS_BLOCK,),
        in_specs=[whole(order.shape)] + [whole(piece.shape) for piece in x_pieces],
        out_specs=rows_of((POS_BLOCK, width)),
        out_shape=jax.ShapeDtypeStruct((position_count, width), BF16),
        name="arrange",
        **params(20, 2 * position_count * unit_len * width, 6_000_000),
    )(order, *x_pieces)


def attend_kernel(sizes, meta, x_now_ref, bias_ref, *refs):
    shards, row_shard = sizes
    w_refs, refs = refs[:shards], refs[shards:]
    arranged_ref, probs_ref, mixture_ref, turned_ref, w_all, sems = refs
    width = w_all.shape[1] // 3
    step = pl.program_id(0)

    @pl.when(step == 0)
    def _():
        load_pieces(meta, [], w_refs, w_all, w_all, sems, row_shard)

    x_now = x_now_ref[...]
    turned_ref[...] = jnp.transpose(x_now)
    arranged = (dot(x_now, w_all[...]) + bias_ref[...]).astype(BF16)
    arranged_ref[...] = arranged
    low, high, lane_low = lane_masks()
    position = lax.broadcasted_iota(jnp.int32, (CLUSTER_ROWS, CLUSTER_ROWS), 0)
    other = lax.broadcasted_iota(jnp.int32, (CLUSTER_ROWS, CLUSTER_ROWS), 1)
    same_half = (position < HALF_ROWS) == (other < HALF_ROWS)
    allowed = jnp.logical_or(same_half, meta[0] == 1)
    pairs = width // CLUSTER_ROWS
    units = [(part, pair) for part in range(POS_BLOCK // CLUSTER_ROWS) for pair in range(pairs)]
    for index in range(0, len(units), 2):
        queries, keys, values = [], [], []
        for part, pair in units[index : index + 2]:
            rows_now = slice(part * CLUSTER_ROWS, (part + 1) * CLUSTER_ROWS)
            base = pair * CLUSTER_ROWS
            queries.append(arranged[rows_now, base : base + CLUSTER_ROWS] * SCALE)
            one_key = arranged[rows_now, width + base : width + base + CLUSTER_ROWS]
            keys.append(both_heads(one_key, low, high))
            one_value = arranged[rows_now, 2 * width + base : 2 * width + base + CLUSTER_ROWS]
            values.append(both_heads(one_value, low, high))
        both_scores = dot(jnp.concatenate(keys, axis=1), corners(*queries), NT)
        for which, (part, pair) in enumerate(units[index : index + 2]):
            halves = []
            for head in range(2):
                one = both_scores[
                    head * CLUSTER_ROWS : (head + 1) * CLUSTER_ROWS,
                    which * CLUSTER_ROWS : (which + 1) * CLUSTER_ROWS,
                ]
                one = jnp.where(allowed, one, NEG_FILL)
                grown = jnp.exp(one - jnp.max(one, axis=0, keepdims=True))
                halves.append(grown * (1.0 / jnp.sum(grown, axis=0, keepdims=True)))
            probs = jnp.concatenate(halves, axis=0).astype(BF16)
            at = (part * pairs + pair) * 2 * CLUSTER_ROWS
            probs_ref[at : at + 2 * CLUSTER_ROWS, :] = probs
            mixture_ref[
                part * CLUSTER_ROWS : (part + 1) * CLUSTER_ROWS,
                pair * CLUSTER_ROWS : (pair + 1) * CLUSTER_ROWS,
            ] = dot(probs, values[which], TN).astype(BF16)


def attend(meta, x_now, bias, w_pieces, row_shard, needs=()):
    shards = len(w_pieces)
    position_count, model_width = x_now.shape
    cols = w_pieces[0].shape[1]
    width = cols // 3
    pair_rows = 2 * width
    return pl.pallas_call(
        gated(partial(attend_kernel, (shards, row_shard)), 3 + shards, needs),
        grid=(position_count // POS_BLOCK,),
        in_specs=[IN_SMEM, rows_of((POS_BLOCK, model_width)), whole(bias.shape)]
        + [ANYWHERE] * (shards + len(needs)),
        out_specs=[
            rows_of((POS_BLOCK, cols)),
            rows_of((POS_BLOCK // CLUSTER_ROWS * pair_rows, CLUSTER_ROWS)),
            rows_of((POS_BLOCK, width)),
            pl.BlockSpec((model_width, POS_BLOCK), lambda i: (0, i)),
        ],
        out_shape=[
            jax.ShapeDtypeStruct((position_count, cols), BF16),
            jax.ShapeDtypeStruct((position_count // CLUSTER_ROWS * pair_rows, CLUSTER_ROWS), BF16),
            jax.ShapeDtypeStruct((position_count, width), BF16),
            jax.ShapeDtypeStruct((model_width, position_count), BF16),
        ],
        scratch_shapes=[
            pltpu.VMEM((model_width, cols), BF16),
            pltpu.SemaphoreType.DMA((shards,)),
        ],
        name="attend",
        **params(
            60, 8 * position_count * (model_width * cols + 4 * CLUSTER_ROWS * width), 18_000_000, 1
        ),
    )(meta, x_now, bias, *w_pieces, *needs)


def place_kernel(sizes, scale, has_base, order_row_ref, *refs):
    unit_len, first_token, added = sizes
    base_ref = refs[0] if has_base else None
    refs = refs[1 if has_base else 0 :]
    if added:
        first_ref, second_ref, out_ref, held = refs

        @pl.when(pl.program_id(0) == 0)
        def _():
            held[...] = (first_ref[...].astype(F32) + second_ref[...].astype(F32)).astype(BF16)

        source_refs = [held]
    else:
        source_refs, out_ref = refs[:-1], refs[-1]
    block_rows = out_ref.shape[0]
    first = jnp.full((1, 1), first_token + pl.program_id(0) * block_rows, jnp.int32)
    token = lax.broadcasted_iota(jnp.int16, (block_rows, unit_len), 0)
    total = None
    for index, ref in enumerate(source_refs):
        row = order_row_ref[:, index * unit_len : (index + 1) * unit_len] - first
        row = jnp.broadcast_to(row, (16, unit_len)).astype(jnp.int16)
        row = jnp.concatenate([row] * (block_rows // 16), axis=0)
        term = dot(equal_ones(row, token), ref[...])
        total = term if total is None else total + term
    if scale != 1.0:
        total = total * scale
    if has_base:
        total = total + base_ref[...]
    out_ref[...] = total.astype(out_ref.dtype)


def place(
    order_row,
    sources,
    first_token,
    row_count,
    scale=1.0,
    dtype=BF16,
    base=None,
    added=False,
    needs=(),
):
    unit_len, width = sources[0].shape
    block_rows = min(TOKEN_BLOCK, row_count)
    extra = [] if base is None else [base]
    return pl.pallas_call(
        gated(
            partial(place_kernel, (unit_len, first_token, added), scale, base is not None),
            1 + len(extra) + len(sources),
            needs,
        ),
        grid=(row_count // block_rows,),
        in_specs=[whole(order_row.shape)]
        + [rows_of((block_rows, width))] * len(extra)
        + [whole(source.shape) for source in sources]
        + [ANYWHERE] * len(needs),
        out_specs=rows_of((block_rows, width)),
        out_shape=jax.ShapeDtypeStruct((row_count, width), dtype),
        scratch_shapes=[pltpu.VMEM((unit_len, width), BF16)] if added else [],
        name="place",
        **params(
            32 if added else 20,
            16 * row_count * unit_len * width,
            10_000_000,
            1,
        ),
    )(order_row, *extra, *sources, *needs)


def attend_back_kernel(sizes, meta, order_ref, arranged_ref, probs_ref, *refs):
    members, shards, unit_len, row_shard, first_row, start = sizes
    g_refs, refs = refs[:members], refs[members:]
    w_refs, refs = refs[:shards], refs[shards:]
    grads_ref, d_x_ref, token_ref, g_all, w_all, sems = refs
    width = w_all.shape[1] // 3
    step = pl.program_id(0)

    @pl.when(step == 0)
    def _():
        load_pieces(meta, g_refs, w_refs, g_all, w_all, sems, row_shard)
        token_ref[...] = jnp.zeros_like(token_ref)

    at_row = first_row + (start + step) * (POS_BLOCK // CLUSTER_ROWS)
    picks = pick_rows(order_ref, at_row, unit_len)
    d_mixture = dot(picks, g_all[...]).astype(BF16)
    low, high, lane_low = lane_masks()
    pairs = width // CLUSTER_ROWS
    units = [(part, pair) for part in range(POS_BLOCK // CLUSTER_ROWS) for pair in range(pairs)]
    for index in range(0, len(units), 2):
        values, d_rows = [], []
        for part, pair in units[index : index + 2]:
            rows_now = slice(part * CLUSTER_ROWS, (part + 1) * CLUSTER_ROWS)
            base = pair * CLUSTER_ROWS
            one_value = arranged_ref[rows_now, 2 * width + base : 2 * width + base + CLUSTER_ROWS]
            values.append(both_heads(one_value, low, high))
            d_rows.append(d_mixture[rows_now, base : base + CLUSTER_ROWS])
        both_probs = dot(jnp.concatenate(values, axis=1), corners(*d_rows), NT)
        for which, (part, pair) in enumerate(units[index : index + 2]):
            rows_now = slice(part * CLUSTER_ROWS, (part + 1) * CLUSTER_ROWS)
            base = pair * CLUSTER_ROWS
            q_lanes = slice(base, base + CLUSTER_ROWS)
            k_lanes = slice(width + base, width + base + CLUSTER_ROWS)
            v_lanes = slice(2 * width + base, 2 * width + base + CLUSTER_ROWS)
            queries = arranged_ref[rows_now, q_lanes] * SCALE
            keys = arranged_ref[rows_now, k_lanes] * SCALE
            at = (part * pairs + pair) * 2 * CLUSTER_ROWS
            probs = probs_ref[at : at + 2 * CLUSTER_ROWS, :]
            d_probs = both_probs[:, which * CLUSTER_ROWS : (which + 1) * CLUSTER_ROWS]
            pieces = []
            for head in range(2):
                rows = slice(head * CLUSTER_ROWS, (head + 1) * CLUSTER_ROWS)
                weight = probs[rows].astype(F32)
                d_one = d_probs[rows]
                inner = jnp.sum(weight * d_one, axis=0, keepdims=True)
                pieces.append(weight * (d_one - inner))
            d_scores = jnp.concatenate(pieces, axis=0).astype(BF16)
            d_query = dot(d_scores, both_heads(keys, low, high), TN)
            d_pair = dot(
                jnp.concatenate([probs, d_scores], axis=1), corners(d_rows[which], queries)
            )
            d_values, d_keys = d_pair[:, :CLUSTER_ROWS], d_pair[:, CLUSTER_ROWS:]
            grads_ref[rows_now, q_lanes] = d_query.astype(BF16)
            grads_ref[rows_now, k_lanes] = jnp.where(
                lane_low, d_keys[:CLUSTER_ROWS], d_keys[CLUSTER_ROWS:]
            ).astype(BF16)
            grads_ref[rows_now, v_lanes] = jnp.where(
                lane_low, d_values[:CLUSTER_ROWS], d_values[CLUSTER_ROWS:]
            ).astype(BF16)
    grads = grads_ref[...]
    d_x_ref[...] = dot(grads, w_all[...], NT).astype(BF16)


def attend_back(
    meta, order, arranged, probs, g_pieces, w_pieces, row_shard, first_row, needs, span, into
):
    members, shards = len(g_pieces), len(w_pieces)
    member_rows, width = g_pieces[0].shape
    unit_len = members * member_rows
    position_count, cols = arranged.shape
    model_width = row_shard * shards
    start, stop = span
    pair_rows = POS_BLOCK // CLUSTER_ROWS * 2 * width
    used = 4 + members + shards

    def block(shape):
        return pl.BlockSpec(shape, lambda i: (start + i, 0))

    return pl.pallas_call(
        gated(
            partial(attend_back_kernel, (members, shards, unit_len, row_shard, first_row, start)),
            used,
            list(into) + list(needs),
        ),
        grid=(stop - start,),
        in_specs=[
            IN_SMEM,
            whole(order.shape),
            block((POS_BLOCK, cols)),
            block((pair_rows, CLUSTER_ROWS)),
        ]
        + [ANYWHERE] * (members + shards + len(into) + len(needs)),
        out_specs=[block((POS_BLOCK, cols)), block((POS_BLOCK, model_width)), whole((8, 128))],
        out_shape=[
            jax.ShapeDtypeStruct((position_count, cols), BF16),
            jax.ShapeDtypeStruct((position_count, model_width), BF16),
            jax.ShapeDtypeStruct((8, 128), F32),
        ],
        input_output_aliases={used + index: index for index in range(len(into))},
        scratch_shapes=[
            pltpu.VMEM((unit_len, width), BF16),
            pltpu.VMEM((model_width, cols), BF16),
            pltpu.SemaphoreType.DMA((members + shards,)),
        ],
        name="attend_back",
        **params(
            60,
            12 * (stop - start) * POS_BLOCK * (unit_len * width + model_width * cols),
            20_000_000,
            1,
        ),
    )(meta, order, arranged, probs, *g_pieces, *w_pieces, *into, *needs)


def normalise(summed):
    average = jnp.mean(summed, axis=-1, keepdims=True)
    centred = summed - average
    spread = jnp.mean(centred * centred, axis=-1, keepdims=True)
    scale_inv = lax.rsqrt(spread + EPSILON)
    return centred * scale_inv, scale_inv


def normalise_back(grad_out, normed, scale_inv, gain_row):
    scaled = grad_out * gain_row
    return scale_inv * (
        scaled
        - jnp.mean(scaled, axis=-1, keepdims=True)
        - normed * jnp.mean(scaled * normed, axis=-1, keepdims=True)
    )


def column_sum(rows_now):
    return jnp.sum(rows_now, axis=0, keepdims=True)


def gelu_parts(value):
    below = 0.5 + 0.5 * lax.erf(value * 0.7071067811865476)
    bell = jnp.exp(value * value * -0.5) * 0.3989422804014327
    return value * below, below + value * bell


class Pack:
    def __init__(self, model_width, feed_width, shards, units, depth):
        self.model_width, self.feed_width, self.shards = model_width, feed_width, shards
        self.row_shard = model_width // shards
        self.feed_shard = feed_width // shards
        self.down_rows = self.feed_shard // CORES
        self.blocks = feed_width // CORES // model_width
        self.up_at = self.down_rows
        self.out_at = self.up_at + self.blocks * self.row_shard
        self.out_rows = self.row_shard // CORES
        self.used = self.out_at + self.out_rows
        unit = 16 * depth
        self.rows = -(-self.used // unit) * unit
        self.rest_rows = self.rows - self.down_rows
        self.units = units
        self.group = units * self.row_shard

    def out_start(self, shard, member):
        return (
            lax.bitwise_xor(jnp.int32(shard) // self.units, member) * self.group
            + (shard % self.units) * self.row_shard
        )


def feed_kernel(pack, att_count, meta, x_ref, cot_ref, vec_ref, up_bias_ref, *refs):
    shards = pack.shards
    att_refs, refs = refs[:att_count], refs[att_count:]
    own_out, own_up, own_down = refs[:3]
    refs = refs[3:]
    pieces, refs = refs[: 2 * (shards - 1)], refs[2 * (shards - 1) :]
    out_ref, first_turned_ref, d_branch_ref, d_ffn_turned_ref, hidden_ref, d_pre_ref = refs[:6]
    d_h1_ref, att_turned_ref = refs[6:8]
    refs = refs[8:]
    d_att_refs, refs = refs[:att_count], refs[att_count:]
    sums_ref, up_sums_ref, w_out, w_up, w_down, slope, sems = refs
    step = pl.program_id(0)
    here, core, member = meta[1], meta[2], meta[3]
    feed_width = pack.feed_width

    def loads(kind):
        copies = []

        def add(source, target):
            copies.append(pltpu.make_async_copy(source, target, sems.at[kind, len(copies)]))

        if kind == 0:
            start = pl.multiple_of(pack.out_start(here, member), 16)
            add(own_out, w_out.at[pl.ds(start, pack.row_shard), :])
        elif kind == 1:
            start = pl.multiple_of(here * pack.row_shard, 16)
            add(own_up, w_up.at[pl.ds(start, pack.row_shard), :])
        else:
            start = pl.multiple_of(here * pack.feed_shard, 16)
            add(own_down, w_down.at[pl.ds(start, pack.feed_shard), :])
        for index, ref in enumerate(pieces):
            peer = lax.bitwise_xor(here, meta[8 + index])
            half = core if index < shards - 1 else 1 - core
            if kind == 0:
                start = pack.out_start(peer, member) + half * pack.out_rows
                start = pl.multiple_of(start, 16)
                add(
                    ref.at[pl.ds(pack.out_at, pack.out_rows), :],
                    w_out.at[pl.ds(start, pack.out_rows), :],
                )
            elif kind == 1:
                start = pl.multiple_of(peer * pack.row_shard, 16)
                for block in range(pack.blocks):
                    lane = pl.multiple_of(
                        (half * pack.blocks + block) * pack.model_width, CLUSTER_ROWS
                    )
                    add(
                        ref.at[pl.ds(pack.up_at + block * pack.row_shard, pack.row_shard), :],
                        w_up.at[pl.ds(start, pack.row_shard), pl.ds(lane, pack.model_width)],
                    )
            else:
                start = pl.multiple_of(peer * pack.feed_shard + half * pack.down_rows, 16)
                add(
                    ref.at[pl.ds(0, pack.down_rows), :],
                    w_down.at[pl.ds(start, pack.down_rows), :],
                )
        return copies

    @pl.when(step == 0)
    def _():
        for kind in range(3):
            for copy in loads(kind):
                copy.start()
        sums_ref[...] = jnp.zeros_like(sums_ref)
        up_sums_ref[...] = jnp.zeros_like(up_sums_ref)
        for copy in loads(0):
            copy.wait()

    bias_out, gain_one, gain_two = vec_ref[0:1, :], vec_ref[1:2, :], vec_ref[2:3, :]
    shift_one, shift_two, bias_down = vec_ref[3:4, :], vec_ref[4:5, :], vec_ref[5:6, :]
    att_width = att_refs[0].shape[1]
    summed = x_ref[...].astype(F32) + bias_out
    for index, ref in enumerate(att_refs):
        summed += dot(ref[...], w_out[index * att_width : (index + 1) * att_width, :])
    normed_one, inv_one = normalise(summed)
    first = normed_one * gain_one + shift_one
    first_low = first.astype(BF16)
    first_turned_ref[...] = jnp.transpose(first_low)
    for index, ref in enumerate(att_refs):
        att_turned_ref[index * att_width : (index + 1) * att_width, :] = jnp.transpose(ref[...])

    @pl.when(step == 0)
    def _():
        for kind in (1, 2):
            for copy in loads(kind):
                copy.wait()

    second = first + bias_down
    starts = list(range(0, feed_width, FF_BLOCK))

    def raised(base):
        lanes = slice(base, base + FF_BLOCK)
        return dot(first_low, w_up[:, lanes]) + up_bias_ref[:, lanes]

    pre = raised(starts[0])
    for index, base in enumerate(starts):
        lanes = slice(base, base + FF_BLOCK)
        pre_next = raised(starts[index + 1]) if index + 1 < len(starts) else None
        hidden, slope_now = gelu_parts(pre)
        hidden = hidden.astype(BF16)
        hidden_ref[:, lanes] = hidden
        slope[:, lanes] = slope_now
        second += dot(hidden, w_down[lanes, :])
        pre = pre_next
    normed_two, inv_two = normalise(second)
    out_ref[...] = (normed_two * gain_two + shift_two).astype(BF16)
    top = cot_ref[...].astype(F32)
    d_second = normalise_back(top, normed_two, inv_two, gain_two)
    d_ffn = d_second.astype(BF16)
    d_ffn_turned_ref[...] = jnp.transpose(d_ffn)
    d_first = d_second
    d_hidden = dot(d_ffn, w_down[0:FF_BLOCK, :], NT)
    for index, base in enumerate(starts):
        lanes = slice(base, base + FF_BLOCK)
        if index + 1 < len(starts):
            d_next = dot(d_ffn, w_down[starts[index + 1] : starts[index + 1] + FF_BLOCK, :], NT)
        d_pre = (d_hidden * slope[:, lanes]).astype(BF16)
        d_pre_ref[:, lanes] = d_pre
        up_sums_ref[:, lanes] += column_sum(d_pre.astype(F32))
        d_first += dot(d_pre, w_up[:, lanes], NT)
        d_hidden = d_next
    d_lower = normalise_back(d_first, normed_one, inv_one, gain_one)
    d_h1_ref[...] = d_lower
    d_branch = d_lower.astype(BF16)
    d_branch_ref[...] = d_branch
    for index, ref in enumerate(d_att_refs):
        back = dot(d_branch, w_out[index * att_width : (index + 1) * att_width, :], NT)
        ref[...] = (0.5 * back).astype(BF16)
    sums_ref[0:1, :] += column_sum(d_branch.astype(F32))
    sums_ref[1:2, :] += column_sum(d_first * normed_one)
    sums_ref[2:3, :] += column_sum(top * normed_two)
    sums_ref[3:4, :] += column_sum(d_first)
    sums_ref[4:5, :] += column_sum(top)
    sums_ref[5:6, :] += column_sum(d_ffn.astype(F32))


def feed(pack, meta, x_own, cot_own, vectors, up_bias, att, own, pieces):
    row_count, model_width = x_own.shape
    feed_width = pack.feed_width
    att_width = att[0].shape[1]
    one = rows_of((ROW_BLOCK, model_width))
    wide = rows_of((ROW_BLOCK, feed_width))
    narrow = rows_of((ROW_BLOCK, att_width))
    turned = pl.BlockSpec((model_width, ROW_BLOCK), lambda i: (0, i))
    turned_shape = jax.ShapeDtypeStruct((model_width, row_count), BF16)

    def like(width, dtype=BF16):
        return jax.ShapeDtypeStruct((row_count, width), dtype)

    return pl.pallas_call(
        partial(feed_kernel, pack, len(att)),
        grid=(row_count // ROW_BLOCK,),
        in_specs=[IN_SMEM, one, one, whole(vectors.shape), whole(up_bias.shape)]
        + [narrow] * len(att)
        + [ANYWHERE] * (3 + len(pieces)),
        out_specs=[one, turned, one, turned, wide, wide, one, turned]
        + [narrow] * len(att)
        + [whole((8, model_width)), whole((1, feed_width))],
        out_shape=[
            like(model_width),
            turned_shape,
            like(model_width),
            turned_shape,
            like(feed_width),
            like(feed_width),
            like(model_width, F32),
            turned_shape,
        ]
        + [like(att_width)] * len(att)
        + [
            jax.ShapeDtypeStruct((8, model_width), F32),
            jax.ShapeDtypeStruct((1, feed_width), F32),
        ],
        scratch_shapes=[
            pltpu.VMEM((model_width, model_width), BF16),
            pltpu.VMEM((model_width, feed_width), BF16),
            pltpu.VMEM((feed_width, model_width), BF16),
            pltpu.VMEM((ROW_BLOCK, feed_width), F32),
            pltpu.SemaphoreType.DMA((3, 1 + pack.blocks * len(pieces))),
        ],
        name="feed",
        **params(
            40, 2 * row_count * model_width * (2 * model_width + 4 * feed_width), 40_000_000
        ),
    )(meta, x_own, cot_own, vectors, up_bias, *att, *own, *pieces)


def down_grads_kernel(pack, table, d_ffn_ref, hidden_ref, theirs_ref, mine_ref, made, sems):
    step = pl.program_id(0)
    core = table[0]

    def stores(shard):
        return [
            pltpu.make_async_copy(made.at[1 - core, shard], theirs_ref.at[shard], sems.at[0, shard]),
            pltpu.make_async_copy(made.at[core, shard], mine_ref.at[shard], sems.at[1, shard]),
        ]

    grad = dot(d_ffn_ref[...], hidden_ref[...]).astype(BF16)
    for half in range(CORES):
        for lane in range(0, pack.model_width, pack.feed_shard):
            begin = half * (pack.model_width // CORES) + lane // pack.feed_shard * pack.down_rows
            made[half, step, :, lane : lane + pack.feed_shard] = grad[
                begin : begin + pack.down_rows
            ]
    for copy in stores(step):
        copy.start()

    @pl.when(step == pack.shards - 1)
    def _():
        for shard in range(pack.shards):
            for copy in stores(shard):
                copy.wait()


def down_grads(pack, table, d_ffn, hidden):
    model_width, row_count = d_ffn.shape
    shape = (pack.shards, pack.down_rows, model_width)
    return pl.pallas_call(
        partial(down_grads_kernel, pack),
        grid_spec=pltpu.PrefetchScalarGridSpec(
            num_scalar_prefetch=1,
            grid=(pack.shards,),
            in_specs=[
                pl.BlockSpec(d_ffn.shape, lambda step, table: (0, 0)),
                pl.BlockSpec((row_count, pack.feed_shard), lambda step, table: (0, step)),
            ],
            out_specs=[ANYWHERE] * 2,
            scratch_shapes=[
                pltpu.VMEM((CORES,) + shape, BF16),
                pltpu.SemaphoreType.DMA((CORES, pack.shards)),
            ],
        ),
        out_shape=[jax.ShapeDtypeStruct(shape, BF16)] * 2,
        name="down_grads",
        **params(60, 2 * row_count * model_width * pack.feed_width, 10_000_000),
    )(table, d_ffn, hidden)


def rest_grads_kernel(
    pack, table, first_ref, d_pre_ref, att_ref, d_branch_ref, theirs_ref, mine_ref, *scratch
):
    att, d_branch, tile, made, in_sems, sems = scratch
    step = pl.program_id(0)
    core, member = table[0], table[1]
    shards, blocks = pack.shards, pack.blocks
    out_at = pack.out_at - pack.down_rows

    loads = [
        pltpu.make_async_copy(att_ref, att, in_sems.at[0]),
        pltpu.make_async_copy(d_branch_ref, d_branch, in_sems.at[1]),
    ]

    def store(half, start, rows, sem):
        there = (slice(None), pl.ds(start, rows), slice(None))

        def copy(target):
            return pltpu.make_async_copy(
                made.at[(half,) + there], target.at[there], sems.at[half, sem]
            )

        return copy

    def both(half, start, rows, sem, act):
        copy = store(half, start, rows, sem)

        @pl.when(core == half)
        def _():
            act(copy(mine_ref))

        @pl.when(core != half)
        def _():
            act(copy(theirs_ref))

    @pl.when(step == 0)
    def _():
        for copy in loads:
            copy.start()

    @pl.when(step < CORES * blocks)
    def _():
        grad = dot(first_ref[...], d_pre_ref[...]).astype(BF16)
        start = pl.multiple_of(step % blocks * pack.row_shard, 16)
        for shard in range(shards):
            made[step // blocks, shard, pl.ds(start, pack.row_shard), :] = grad[
                shard * pack.row_shard : (shard + 1) * pack.row_shard
            ]

    for half in range(CORES):

        @pl.when(step == (half + 1) * blocks - 1)
        def _(half=half):
            both(half, 0, out_at, 0, lambda copy: copy.start())

    @pl.when(step == CORES * blocks)
    def _():
        for copy in loads:
            copy.wait()
        tile[...] = dot(att[...], d_branch[...])
        spare = pack.rows - pack.used
        for half in range(CORES):
            for shard in range(shards):
                start = pack.out_start(shard, member) + half * pack.out_rows
                start = pl.multiple_of(start, 16)
                made[half, shard, out_at : out_at + pack.out_rows, :] = tile[
                    pl.ds(start, pack.out_rows), :
                ].astype(BF16)
                if spare:
                    made[half, shard, out_at + pack.out_rows :, :] = jnp.zeros(
                        (spare, pack.model_width), BF16
                    )
            both(half, out_at, pack.rest_rows - out_at, 1, lambda copy: copy.start())
        for half in range(CORES):
            both(half, 0, out_at, 0, lambda copy: copy.wait())
            both(half, out_at, pack.rest_rows - out_at, 1, lambda copy: copy.wait())


def rest_grads(pack, table, first_low, d_pre, att, d_branch, needs=()):
    model_width, row_count = first_low.shape
    shape = (pack.shards, pack.rest_rows, model_width)
    steps = CORES * pack.blocks
    return pl.pallas_call(
        gated(partial(rest_grads_kernel, pack), 5, needs),
        grid_spec=pltpu.PrefetchScalarGridSpec(
            num_scalar_prefetch=1,
            grid=(steps + 1,),
            in_specs=[
                pl.BlockSpec(first_low.shape, lambda step, table: (0, 0)),
                pl.BlockSpec(
                    (row_count, model_width),
                    lambda step, table: (0, jnp.minimum(step, steps - 1)),
                ),
            ]
            + [ANYWHERE] * (2 + len(needs)),
            out_specs=[ANYWHERE] * 2,
            scratch_shapes=[
                pltpu.VMEM((model_width, row_count), BF16),
                pltpu.VMEM((row_count, model_width), BF16),
                pltpu.VMEM((model_width, model_width), F32),
                pltpu.VMEM((CORES,) + shape, BF16),
                pltpu.SemaphoreType.DMA((2,)),
                pltpu.SemaphoreType.DMA((CORES, 2)),
            ],
        ),
        out_shape=[jax.ShapeDtypeStruct(shape, BF16)] * 2,
        name="rest_grads",
        **params(60, 2 * row_count * model_width * (pack.feed_width + model_width), 10_000_000),
    )(table, first_low, d_pre, att, d_branch, *needs)


def qkv_grads_kernel(rounds, x_refs_then, *refs):
    refs = (x_refs_then,) + refs
    x_refs, grad_refs = refs[:rounds], refs[rounds : 2 * rounds]
    small_ref, out_ref = refs[2 * rounds :]
    shards, rows, _ = out_ref.shape
    row_shard = rows - small_ref.shape[1]
    total, sums = None, None
    for x_ref, grad_ref in zip(x_refs, grad_refs):
        grads = grad_ref[...]
        term = dot(x_ref[...], grads)
        down = column_sum(grads.astype(F32))
        total = term if total is None else total + term
        sums = down if sums is None else sums + down
    total = total.astype(BF16)
    row = lax.broadcasted_iota(jnp.int32, small_ref.shape[1:], 0)
    for shard in range(shards):
        out_ref[shard, :row_shard, :] = total[shard * row_shard : (shard + 1) * row_shard]
        last = jnp.where(row == BIAS_ROW, sums, small_ref[shard])
        out_ref[shard, row_shard:, :] = last.astype(BF16)


def qkv_grads(x_turned, grads, small, row_shard, needs=()):
    rounds = len(grads)
    model_width, positions = x_turned[0].shape
    cols = grads[0].shape[1]
    shards, extra, _ = small.shape
    block = GRAD_LANES if cols % GRAD_LANES == 0 else cols
    return pl.pallas_call(
        gated(partial(qkv_grads_kernel, rounds), 2 * rounds + 1, needs),
        grid=(cols // block,),
        in_specs=[whole((model_width, positions))] * rounds
        + [pl.BlockSpec((positions, block), lambda i: (0, i))] * rounds
        + [pl.BlockSpec((shards, extra, block), lambda i: (0, 0, i))]
        + [ANYWHERE] * len(needs),
        out_specs=pl.BlockSpec((shards, row_shard + extra, block), lambda i: (0, 0, i)),
        out_shape=jax.ShapeDtypeStruct((shards, row_shard + extra, cols), BF16),
        name="qkv_grads",
        **params(60, 2 * rounds * positions * model_width * cols, 18_000_000),
    )(*x_turned, *grads, small, *needs)


def add_picked_kernel(count, first, table, *refs):
    in_refs, out_refs = refs[:count], refs[count:]
    if count == 2:
        total = in_refs[0][...] + in_refs[1][...]
    else:
        total = in_refs[0][...].astype(F32)
        for ref in in_refs[1:]:
            total = total + ref[...].astype(F32)
        total = total.astype(BF16)
    if len(out_refs) == 1:
        out_refs[0][...] = total
        return

    @pl.when(pl.program_id(0) < first)
    def _():
        out_refs[0][...] = total

    @pl.when(pl.program_id(0) >= first)
    def _():
        out_refs[1][...] = total


def add_picked(table, arrays, steps, first=None, needs=(), work=0):
    _, rows, cols = arrays[0].shape
    parts = 2 if rows % 32 == 0 and steps == 1 else 1
    block = (1, rows // parts, cols)
    spec = [
        pl.BlockSpec(block, lambda s, p, t, k=k: (t[k * steps + s], p, 0))
        for k in range(len(arrays))
    ]
    if first is None:
        out_specs = [pl.BlockSpec(block, lambda s, p, t: (s, p, 0))]
        counts = [steps]
    else:
        out_specs = [
            pl.BlockSpec(
                block,
                lambda s, p, t: (
                    jnp.minimum(s, first - 1),
                    jnp.where(s < first, p, parts - 1),
                    0,
                ),
            ),
            pl.BlockSpec(
                block,
                lambda s, p, t: (jnp.maximum(s - first, 0), jnp.where(s < first, 0, p), 0),
            ),
        ]
        counts = [first, steps - first]
    return pl.pallas_call(
        gated(partial(add_picked_kernel, len(arrays), first), 1 + len(arrays), needs),
        grid_spec=pltpu.PrefetchScalarGridSpec(
            num_scalar_prefetch=1,
            grid=(steps, parts),
            in_specs=spec + [ANYWHERE] * len(needs),
            out_specs=out_specs,
        ),
        out_shape=[jax.ShapeDtypeStruct((n, rows, cols), BF16) for n in counts],
        name="add_picked",
        compiler_params=pltpu.CompilerParams(
            dimension_semantics=("arbitrary", "arbitrary"),
            vmem_limit_bytes=(60 if steps > 1 else 12) * MIB,
        ),
        cost_estimate=pl.CostEstimate(flops=work, bytes_accessed=1_000_000, transcendentals=0),
    )(table, *arrays, *needs)


def join_kernel(count, down_kept, down_landed, rest_kept, rest_landed, *outs):
    rows = down_kept.shape[1]
    for index in range(count):
        target = outs[1 - index % 2] if count > 1 else outs[0]
        place_now = index // 2
        target[place_now, :rows, :] = down_kept[index] + down_landed[index]
        target[place_now, rows:, :] = rest_kept[index] + rest_landed[index]


def join(kept, landed, needs=()):
    count = kept[0].shape[0]
    rows = kept[0].shape[1] + kept[1].shape[1]
    shape = jax.ShapeDtypeStruct(((count + 1) // 2, rows, kept[0].shape[2]), BF16)
    vmem = pl.BlockSpec(memory_space=pltpu.VMEM)
    outs = pl.pallas_call(
        gated(partial(join_kernel, count), 4, needs),
        in_specs=[vmem] * 4 + [ANYWHERE] * len(needs),
        out_specs=[vmem] * min(count, 2),
        out_shape=[shape] * min(count, 2),
        name="join",
        compiler_params=pltpu.CompilerParams(vmem_limit_bytes=24 * MIB),
        cost_estimate=pl.CostEstimate(flops=0, bytes_accessed=200_000, transcendentals=0),
    )(kept[0], landed[0], kept[1], landed[1], *needs)
    return outs if count > 1 else (None, outs[0])


def stack_kernel(count, *refs):
    for index in range(count):
        refs[count][index] = refs[index][...]


def split_kernel(in_ref, *out_refs):
    rows = out_refs[0].shape[0]
    for index, ref in enumerate(out_refs):
        ref[...] = in_ref[index * rows : (index + 1) * rows, :]


def split_rows(value, count, needs=()):
    rows = value.shape[0] // count
    vmem = pl.BlockSpec(memory_space=pltpu.VMEM)
    return pl.pallas_call(
        gated(split_kernel, 1, needs),
        in_specs=[vmem] + [ANYWHERE] * len(needs),
        out_specs=[vmem] * count,
        out_shape=[jax.ShapeDtypeStruct((rows, value.shape[1]), value.dtype)] * count,
        name="split_rows",
        compiler_params=pltpu.CompilerParams(vmem_limit_bytes=12 * MIB),
        cost_estimate=pl.CostEstimate(flops=0, bytes_accessed=100_000, transcendentals=0),
    )(value, *needs)


def stack_up(pieces, needs=()):
    vmem = pl.BlockSpec(memory_space=pltpu.VMEM)
    return pl.pallas_call(
        gated(partial(stack_kernel, len(pieces)), len(pieces), needs),
        in_specs=[vmem] * len(pieces) + [ANYWHERE] * len(needs),
        out_specs=vmem,
        out_shape=jax.ShapeDtypeStruct((len(pieces),) + pieces[0].shape, BF16),
        name="stack_up",
        compiler_params=pltpu.CompilerParams(vmem_limit_bytes=24 * MIB),
        cost_estimate=pl.CostEstimate(flops=0, bytes_accessed=100_000, transcendentals=0),
    )(*pieces, *needs)


def unpack_kernel(pack, depth, meta, mine_ref, other_ref, down_ref, up_ref, out_ref, ordered):
    core, level = meta[2], meta[4]
    rows = pack.rows // depth
    for mask in range(depth):
        start = pl.multiple_of(lax.bitwise_xor(level, mask) * rows, 16)
        ordered[core, pl.ds(start, rows), :] = mine_ref[mask]
        ordered[1 - core, pl.ds(start, rows), :] = other_ref[mask]
    turned = []
    for half in range(CORES):
        for lane in range(0, pack.model_width, pack.feed_shard):
            turned.append(ordered[half, : pack.down_rows, lane : lane + pack.feed_shard])
    down_ref[...] = jnp.transpose(jnp.concatenate(turned, axis=0)).astype(F32)
    for half in range(CORES):
        for block in range(pack.blocks):
            lane = (half * pack.blocks + block) * pack.model_width
            start = pack.up_at + block * pack.row_shard
            up_ref[:, lane : lane + pack.model_width] = ordered[
                half, start : start + pack.row_shard, :
            ].astype(F32)
        out_ref[half * pack.out_rows : (half + 1) * pack.out_rows, :] = ordered[
            half, pack.out_at : pack.out_at + pack.out_rows, :
        ].astype(F32)


def unpack(pack, depth, meta, mine, other):
    vmem = pl.BlockSpec(memory_space=pltpu.VMEM)
    return pl.pallas_call(
        partial(unpack_kernel, pack, depth),
        in_specs=[IN_SMEM, vmem, vmem],
        out_specs=[vmem] * 3,
        out_shape=[
            jax.ShapeDtypeStruct((pack.feed_shard, pack.model_width), F32),
            jax.ShapeDtypeStruct((pack.row_shard, pack.feed_width), F32),
            jax.ShapeDtypeStruct((pack.row_shard, pack.model_width), F32),
        ],
        scratch_shapes=[pltpu.VMEM((CORES, pack.rows, pack.model_width), BF16)],
        name="unpack",
        compiler_params=pltpu.CompilerParams(vmem_limit_bytes=60 * MIB),
        cost_estimate=pl.CostEstimate(flops=0, bytes_accessed=10_000_000, transcendentals=0),
    )(meta, mine, other)


def unpack_qkv_kernel(meta, mine_ref, other_ref, grad_ref, bias_ref, small_ref):
    member = meta[3]
    row_shard, width = grad_ref.shape[0], grad_ref.shape[1] // 3
    part = mine_ref.shape[1] // 3
    for ref, at in ((mine_ref, member), (other_ref, 1 - member)):
        for kind in range(3):
            lane = pl.multiple_of(kind * width + at * part, CLUSTER_ROWS)
            from_lanes = slice(kind * part, (kind + 1) * part)
            grad_ref[:, pl.ds(lane, part)] = ref[:row_shard, from_lanes].astype(F32)
            lane = pl.multiple_of(at * part, CLUSTER_ROWS)
            bias_ref[kind : kind + 1, pl.ds(lane, part)] = ref[row_shard:, from_lanes].astype(F32)[
                BIAS_ROW : BIAS_ROW + 1
            ]
    small_ref[...] = (mine_ref[row_shard:, :].astype(F32) + other_ref[row_shard:, :].astype(F32))[
        :BIAS_ROW
    ]


def unpack_qkv(meta, mine, other, row_shard, needs=()):
    cols = mine.shape[1]
    vmem = pl.BlockSpec(memory_space=pltpu.VMEM)
    return pl.pallas_call(
        gated(unpack_qkv_kernel, 3, needs),
        in_specs=[IN_SMEM, vmem, vmem] + [ANYWHERE] * len(needs),
        out_specs=[vmem] * 3,
        out_shape=[
            jax.ShapeDtypeStruct((row_shard, CORES * cols), F32),
            jax.ShapeDtypeStruct((3, CORES * cols // 3), F32),
            jax.ShapeDtypeStruct((BIAS_ROW, cols), F32),
        ],
        name="unpack_qkv",
        compiler_params=pltpu.CompilerParams(vmem_limit_bytes=60 * MIB),
        cost_estimate=pl.CostEstimate(flops=0, bytes_accessed=200_000, transcendentals=0),
    )(meta, mine, other, *needs)


def tie(*values):
    return lax.optimization_barrier(values)


def body(
    tokens,
    cotangent,
    perms,
    unit_kind,
    w_qkv,
    bias_qv,
    w_out,
    bias_out,
    ln_gain,
    ln_bias,
    w_up,
    bias_up,
    w_down,
    bias_down,
):
    shards = lax.axis_size("fsdp")
    groups = lax.axis_size("dp")
    here = lax.axis_index("fsdp")
    dp_index = lax.axis_index("dp")
    core = dp_index % CORES
    level = dp_index // CORES
    depth = groups // CORES
    units, rounds, unit_len = perms.shape
    per_device = unit_len // shards
    model_width = tokens.shape[1]
    feed_width = w_up.shape[1]
    row_shard = model_width // shards
    members = shards // units
    member_rows = unit_len // members
    head_cols = model_width // members
    padded = -(-head_cols // CLUSTER_ROWS) * CLUSTER_ROWS
    spot = here * CORES + core
    home_core = spot // shards
    unit = (spot // members) % units
    member = spot % members
    pack = Pack(model_width, feed_width, shards, units, depth)
    bits = [1 << k for k in range(shards.bit_length() - 1)]
    bit_orders = (bits, bits[::-1])

    def plane_pairs(target):
        pairs = []
        for z in range(depth):
            for f_index in range(shards):
                for c_index in range(CORES):
                    f_new, c_new = target(f_index, c_index)
                    pairs.append(
                        (
                            (z * CORES + c_index) * shards + f_index,
                            (z * CORES + c_new) * shards + f_new,
                        )
                    )
        return pairs

    def send(value, pairs):
        return lax.ppermute(value, ("dp", "fsdp"), pairs)

    def cross(value, mask):
        return send(value, plane_pairs(lambda f, c: divmod((f * CORES + c) ^ mask, CORES)))

    def trade(value, stage):
        return send(value, plane_pairs(lambda f, c: (f ^ bit_orders[c][stage], c)))

    def trade_mask(index, which):
        mask = 0
        for stage in range(len(bits)):
            if index >> stage & 1:
                mask ^= bit_orders[which][stage]
        return mask

    def climb(value, mask):
        plane = CORES * shards
        pairs = []
        for z in range(depth):
            for rest in range(plane):
                pairs.append((z * plane + rest, (z ^ mask) * plane + rest))
        return send(value, pairs)

    def outward(step):
        def target(f, c):
            place_now = (c * units + (f % units + step) % units) * members + f // units
            return divmod(place_now, CORES)

        return plane_pairs(target)

    def homeward(step):
        return [(b, a) for a, b in outward(step)]

    def bring_start(value):
        blocks = value.reshape(units, per_device, model_width)
        return [
            lax.dynamic_index_in_dim(blocks, (here % units + step) % units, axis=0, keepdims=False)
            for step in range(units)
        ]

    def bring(chosen):
        return jnp.concatenate(
            [send(chosen[step], outward(step)) for step in range(units)], axis=0
        )

    def send_home(blocks):
        return [send(blocks[step], homeward(step)) for step in range(units)]

    def in_order(landed, dtype):
        if units == 2:
            swap = here % units == 1
            wanted = [
                jnp.where(swap, landed[1], landed[0]),
                jnp.where(swap, landed[0], landed[1]),
            ]
        else:
            stacked = jnp.stack(landed)
            wanted = [
                lax.dynamic_index_in_dim(stacked, (index - here % units) % units, 0, keepdims=False)
                for index in range(units)
            ]
        return jnp.concatenate(wanted, axis=0).astype(dtype)

    x_chosen = bring_start(tokens)
    x_own = bring(x_chosen)
    small = jnp.concatenate(
        [
            bias_qv.reshape(-1),
            bias_out,
            ln_gain.reshape(-1),
            ln_bias.reshape(-1),
            bias_up,
            bias_down,
        ]
    )
    small_rows = -(-small.shape[0] // (3 * padded))
    small_block = jnp.pad(
        jnp.pad(small, (0, small_rows * 3 * padded - small.shape[0])).reshape(
            small_rows, 3 * padded
        ),
        ((0, 16 - small_rows), (0, 0)),
    )
    def columns_for(offset):
        start = lax.bitwise_xor(member, offset) * head_cols
        blocks = [
            jnp.pad(
                lax.dynamic_slice(
                    w_qkv, (0, kind * model_width + start), (row_shard, head_cols)
                ),
                ((0, 0), (0, padded - head_cols)),
            )
            for kind in range(3)
        ]
        return jnp.concatenate([jnp.concatenate(blocks, axis=1), small_block], axis=0)

    offsets = [(CORES * m) % members for m in range(shards)]
    kinds = sorted(set(offsets))
    order_pack = jnp.concatenate(
        [perms.reshape(-1), jnp.broadcast_to(unit_kind[:, None], (units, 128)).reshape(-1)]
    )
    order_other = cross(order_pack, 1)
    *tied, order_other = tie(*[columns_for(offset) for offset in kinds], order_other)
    piece_kinds = dict(zip(kinds, tied))
    x_pieces = [x_own] + [cross(x_own, mask) for mask in range(1, members)]
    if members == CORES:
        qkv_pieces = {0: piece_kinds[0]}
        for stage in range(len(bits)):
            qkv_pieces[1 << stage] = trade(piece_kinds[0], stage)
        for stage in range(1, len(bits)):
            for index in range(1, 1 << stage):
                qkv_pieces[index | 1 << stage] = trade(qkv_pieces[index], stage)
        qkv_pieces = [qkv_pieces[index] for index in range(shards)]
        qkv_masks = [[trade_mask(index, which) for index in range(shards)] for which in (0, 1)]
    else:
        qkv_pieces = [piece_kinds[0]] + [
            cross(piece_kinds[offsets[m]], CORES * m) for m in range(1, shards)
        ]
        qkv_masks = [list(range(shards))] * 2
    order_pack = jnp.where(home_core == core, order_pack, order_other)
    order_count = units * rounds * unit_len
    unit_perm = lax.dynamic_index_in_dim(
        order_pack[:order_count].reshape(units, rounds * unit_len), unit, 0, keepdims=False
    )
    kind_now = lax.dynamic_index_in_dim(
        order_pack[order_count:].reshape(units, 128), unit, 0, keepdims=False
    )[0]
    owner = unit_perm // per_device
    order = (
        lax.bitwise_xor(owner // units, member) * units + (unit - owner % units) % units
    ) * per_device + unit_perm % per_device
    order = order.reshape(rounds, unit_len)
    order = jnp.where(core == 0, order, order[::-1])
    order_row = order.reshape(1, rounds * unit_len)
    order = order.reshape(-1, CLUSTER_ROWS)
    x_here = arrange(order, x_pieces, unit_len, 0)
    x_now = [x_here, cross(x_here, 1)]
    own_masks = [
        jnp.where(core == 0, trade_mask(i, 0), trade_mask(i, 1)) for i in range(1, shards)
    ]
    other_masks = [
        jnp.where(core == 0, trade_mask(i, 1), trade_mask(i, 0)) for i in range(1, shards)
    ]
    zero = jnp.int32(0)
    meta = jnp.stack(
        [kind_now, here, core, member, level, zero, zero, zero]
        + own_masks
        + other_masks
        + [jnp.where(core == 0, first, second) for first, second in zip(*qkv_masks)]
    ).astype(jnp.int32)

    def half_of(value, axis, length, at):
        return lax.dynamic_slice_in_dim(value, at * length, length, axis=axis)

    packed = jnp.concatenate(
        [half_of(w_down, 0, pack.down_rows, core)]
        + [
            half_of(w_up, 1, model_width, core * pack.blocks + block)
            for block in range(pack.blocks)
        ]
        + [half_of(w_out, 0, pack.out_rows, core)],
        axis=0,
    )
    order_rows = unit_len // CLUSTER_ROWS
    arranged, probs, mixtures, x_turned = [], [], [], []
    *tied, packed, x_now[0] = tie(*qkv_pieces[1:], packed, x_now[0])
    qkv_pieces = qkv_pieces[:1] + tied
    smalls = jnp.stack(
        [
            piece[row_shard : row_shard + small_rows].reshape(-1)[: small.shape[0]]
            for piece in qkv_pieces
        ]
    )
    spots_of = [[masks.index(mask) for mask in range(shards)] for masks in qkv_masks]
    spots_of = jnp.where(core == 0, jnp.array(spots_of[0]), jnp.array(spots_of[1]))
    spots_of = jnp.take(spots_of, lax.bitwise_xor(here, jnp.arange(shards)))
    smalls = jnp.take(smalls, spots_of, axis=0).astype(F32)

    def vectors_at(start, count, length):
        part = smalls[:, start * row_shard : start * row_shard + count * length]
        return (
            part.reshape(shards, count, length).transpose(1, 0, 2).reshape(count, shards * length)
        )

    my_bias = lax.dynamic_index_in_dim(
        vectors_at(0, 2, row_shard).reshape(2, members, head_cols), member, 1, keepdims=False
    )
    my_bias = jnp.pad(my_bias, ((0, 0), (0, padded - head_cols)))
    my_bias = jnp.stack([my_bias[0], jnp.zeros_like(my_bias[0]), my_bias[1]]).reshape(1, -1)
    up_bias = vectors_at(7, 1, feed_width // shards)
    down_bias = smalls[:, small.shape[0] - row_shard :].reshape(1, model_width)
    vectors = jnp.concatenate(
        [vectors_at(2, 5, row_shard), down_bias, jnp.zeros((2, model_width), F32)], axis=0
    )

    weight_pieces = {0: packed}
    for stage in range(len(bits)):
        weight_pieces[1 << stage] = trade(packed, stage)
    for index in range(rounds):
        results = attend(meta, x_now[index], my_bias, qkv_pieces, row_shard, mixtures[-1:])
        for kept, result in zip((arranged, probs, mixtures, x_turned), results):
            kept.append(result)
    cot_now, mixtures[0] = tie(cotangent, mixtures[0])
    cot_landed = [
        send(value, outward(step)) for step, value in enumerate(bring_start(cot_now))
    ]
    cot_own = jnp.concatenate(cot_landed, axis=0)
    for stage in range(1, len(bits)):
        for index in range(1, 1 << stage):
            weight_pieces[index | 1 << stage] = trade(weight_pieces[index], stage)
    att_there, att_sent = [], []
    for mask in range(1, members):
        there = place(
            order_row, mixtures, mask * member_rows, member_rows, 0.5, needs=cot_landed
        )
        att_sent.append(there)
        att_there.append(cross(there[:, :head_cols], mask))
    att_here = place(order_row, mixtures, 0, member_rows, 0.5, needs=att_sent)

    direct = [weight_pieces[index] for index in range(1, shards)]
    swapped = [cross(piece, 1) for piece in direct[:-1]]
    last_piece, att_here = tie(direct[-1], att_here)
    swapped.append(cross(last_piece, 1))
    att_raw = [att_here[:, :head_cols]] + att_there
    if head_cols % CLUSTER_ROWS:
        att_raw = [jnp.concatenate(att_raw, axis=1)]
    block_out, first_low, d_branch, d_ffn, hidden, d_pre, d_lower, att_turned, *rest = feed(
        pack,
        meta,
        x_own,
        cot_own,
        vectors,
        up_bias,
        att_raw,
        [w_out, w_up, w_down],
        direct + swapped,
    )
    d_att, (row_sums, up_sums) = rest[: len(att_raw)], rest[len(att_raw) :]
    if head_cols % CLUSTER_ROWS:
        d_att = [d_att[0][:, mask * head_cols : (mask + 1) * head_cols] for mask in range(members)]
    d_att = [d_att[0]] + [cross(d_att[mask], mask) for mask in range(1, members)]
    d_att = [jnp.pad(piece, ((0, 0), (0, padded - head_cols))) for piece in d_att]

    table = jnp.stack([core, member]).astype(jnp.int32)
    sending = [index for index in range(shards) if index & 1]
    keeping = [index for index in range(shards) if not index & 1]
    slots = jnp.stack(
        [
            lax.bitwise_xor(here, jnp.where(core == 0, trade_mask(i, 0), trade_mask(i, 1)))
            for i in sending + keeping
        ]
    )
    slots = jnp.concatenate([slots, slots]).astype(jnp.int32)

    def pair_sum(mine, theirs, needs):
        return add_picked(
            slots, [mine, cross(theirs, 1)], shards, len(sending), needs, 20_000_000_000
        )

    theirs_down, mine_down = down_grads(pack, table, d_ffn, hidden)
    theirs_rest, mine_rest = rest_grads(
        pack, table, first_low, d_pre, att_turned, d_branch, [theirs_down]
    )
    down_going, down_kept = pair_sum(mine_down, theirs_down, [theirs_rest])
    rest_going, rest_kept = pair_sum(mine_rest, theirs_rest, [down_going] + d_att[1:])

    def merge(kept, landed, *needs):
        count = kept.shape[0]
        if count == 1:
            table = jnp.zeros((2,), jnp.int32)
            return None, add_picked(table, [kept, landed], 1, None, needs)[0]
        order_now = [i for i in range(count) if i & 1] + [i for i in range(count) if not i & 1]
        table = jnp.array(order_now * 2, jnp.int32)
        return add_picked(table, [kept, landed], count, count // 2, needs)

    grads, d_x = [None] * rounds, [None] * rounds
    needs = [rest_going]
    blocks = unit_len // POS_BLOCK
    spans = [(rounds - 1, (0, blocks))]
    for index in reversed(range(rounds - 1)):
        spans += [(index, (0, blocks // 2)), (index, (blocks // 2, blocks))]
    results = []
    for turn, (index, span) in enumerate(spans):
        results = attend_back(
            meta,
            order,
            arranged[index],
            probs[index],
            d_att,
            qkv_pieces,
            row_shard,
            index * order_rows,
            needs,
            span,
            results[:2] if span[0] else [],
        )
        grads[index], d_x[index], token = results
        if turn == 0:
            d_x_there = cross(d_x[index], 1)
        if turn == 0:
            going, kept = join(
                [down_kept, rest_kept], [trade(down_going, 0), trade(rest_going, 0)], [token]
            )
            needs = [kept]
        elif turn < len(bits):
            going, kept = merge(kept, trade(going, turn), token)
            needs = [kept, d_x_there]
        if turn == len(spans) - 2:
            output_landed = send_home(split_rows(block_out, units, [kept]))
    for stage in range(len(spans), len(bits)):
        going, kept = merge(kept, trade(going, stage))

    def level_pieces(block):
        return block.reshape((depth, block.shape[0] // depth) + block.shape[1:])

    def level_scatter(cut):
        return [
            climb(
                lax.dynamic_index_in_dim(cut, lax.bitwise_xor(level, mask), 0, keepdims=False), mask
            )
            for mask in range(1, depth)
        ]

    def level_gather(piece):
        pieces = {0: piece}
        mask = depth // 2
        while mask:
            pieces[mask] = climb(piece, mask)
            mask //= 2
        return pieces

    def level_forward(pieces):
        for index in sorted(range(depth), key=lambda value: value.bit_count()):
            if index not in pieces:
                low = index & -index
                pieces[index] = climb(pieces[index ^ low], low)
        return [pieces[index] for index in range(depth)]

    def by_shard(value):
        count, length = value.shape
        return (
            value.reshape(count, shards, length // shards)
            .transpose(1, 0, 2)
            .reshape(shards, count * length // shards)
        )

    small_grad = jnp.concatenate(
        [by_shard(row_sums[:5]), by_shard(up_sums), by_shard(row_sums[5:6])], axis=1
    )
    small_length = small_grad.shape[1]
    small_lanes = 3 * head_cols
    small_grad = jnp.pad(small_grad, ((0, 0), (0, BIAS_ROW * small_lanes - small_length)))
    small_grad = jnp.pad(
        small_grad.reshape(shards, BIAS_ROW, small_lanes), ((0, 0), (0, 16 - BIAS_ROW), (0, 0))
    )
    extra_rows = 16
    x_last, kept, small_grad = tie(x_turned[0], kept, small_grad)
    if padded == head_cols:
        joined = qkv_grads(
            [x_last, x_turned[1]], grads, small_grad, row_shard, output_landed
        )
    else:
        qkv_grad = dot(x_last, grads[0]) + dot(x_turned[1], grads[1])
        qkv_grad = qkv_grad.reshape(shards, row_shard, 3, padded)[..., :head_cols]
        bias_sum = sum(jnp.sum(value.astype(F32), axis=0) for value in grads)
        bias_sum = bias_sum.reshape(3, padded)[:, :head_cols].reshape(small_lanes)
        small_grad = small_grad.at[:, BIAS_ROW].set(bias_sum[None])
        joined = jnp.concatenate(
            [qkv_grad.reshape(shards, row_shard, small_lanes), small_grad], axis=1
        ).astype(BF16)
    cut = level_pieces(kept[0])
    landed = level_scatter(cut)
    classes = max(1, members // CORES)
    d_x_parts = [d_x[0], d_x_there]
    order_mine = order_row[:, :unit_len]
    if classes == 1:
        slots_held = jnp.stack(
            [
                lax.bitwise_xor(here, jnp.where(core == 0, trade_mask(i, 0), trade_mask(i, 1)))
                for i in range(shards)
            ]
        )
        held = jnp.stack(
            [
                lax.dynamic_index_in_dim(joined, slots_held[i], 0, keepdims=False)
                for i in range(0, shards, 2)
            ]
        )
        leaving = jnp.stack(
            [
                lax.dynamic_index_in_dim(joined, slots_held[i], 0, keepdims=False)
                for i in range(1, shards, 2)
            ]
        )
        totals = None
    else:
        totals = [None] * classes
        for m in range(shards):
            offset = offsets[m] // CORES
            piece = lax.dynamic_index_in_dim(joined, lax.bitwise_xor(here, m), 0, keepdims=False)
            piece = (piece if m == 0 else cross(piece, CORES * m)).astype(F32)
            totals[offset] = piece if totals[offset] is None else totals[offset] + piece

    if depth > 1:
        picks = jnp.concatenate([level[None], jnp.zeros((depth - 1,), level.dtype)])
        (kept,) = add_picked(
            picks.astype(jnp.int32),
            [cut] + [piece[None] for piece in landed],
            1,
            None,
            [joined] if totals is not None else [leaving],
        )
    d_there = [
        place(
            order_mine,
            d_x_parts,
            mask * member_rows,
            member_rows,
            added=True,
            needs=[kept],
        )
        for mask in range(1, members)
    ]
    gathered = level_gather(kept[0]) if depth > 1 else {0: cut[0]}
    early = list(d_there)
    if totals is None:
        leaving, held = merge(held, trade(leaving, 0), *d_there)
        early.append(held)
    d_here = place(
        order_mine,
        d_x_parts,
        0,
        member_rows,
        1.0,
        F32,
        d_lower,
        added=True,
        needs=early,
    )
    d_inputs = d_here
    for mask, there in enumerate(d_there, 1):
        d_inputs = d_inputs + cross(there, mask).astype(F32)
    d_inputs = d_inputs.astype(BF16)
    if totals is None:
        for stage in range(1, len(bits)):
            leaving, held = merge(held, trade(leaving, stage), d_inputs)
        masks = [mask for mask in gathered if mask]
        *tied, held = tie(*[gathered[mask] for mask in masks], held)
        gathered.update(zip(masks, tied))
        totals = [held[0]]
    home = send_home(d_inputs.reshape(units, per_device, model_width))
    output = in_order(output_landed, BF16)
    totals = jnp.concatenate(totals, axis=0).astype(BF16)
    rows_each = row_shard + extra_rows
    if depth > 1:
        halves = totals.reshape((2, totals.shape[0] // 2) + totals.shape[1:])
        side = level % 2
        mine = lax.dynamic_index_in_dim(halves, side, 0, keepdims=False)
        theirs = lax.dynamic_index_in_dim(halves, 1 - side, 0, keepdims=False)
        half = (mine.astype(F32) + climb(theirs, 1).astype(F32)).astype(BF16)
        mask = 2
        while mask < depth:
            half = (half.astype(F32) + climb(half, mask).astype(F32)).astype(BF16)
            mask *= 2
        *home, half = tie(*home, half)
        other_half = climb(half, 1)
        totals = jnp.concatenate(
            [
                jnp.where(side == 0, half, other_half),
                jnp.where(side == 0, other_half, half),
            ],
            axis=0,
        )
    d_inputs = in_order(home, F32)
    stacked = stack_up(level_forward(gathered))
    grad_down, grad_up, grad_out = unpack(pack, depth, meta, stacked, cross(stacked, 1))
    if padded == head_cols and members == CORES:
        grad_qkv, bias_out_row, smalls_out = unpack_qkv(
            meta, totals, cross(totals, 1), row_shard, [grad_down, d_inputs, output]
        )
        smalls_out = smalls_out.reshape(-1)[:small_length]
        bias_out_row = lax.dynamic_slice(bias_out_row, (0, here * row_shard), (3, row_shard))
    else:
        landed = jnp.stack([totals, cross(totals, 1)], axis=0).reshape(
            CORES, classes, rows_each, 3 * head_cols
        )
        smalls_out = jnp.sum(
            landed[:, :, row_shard : row_shard + BIAS_ROW].astype(F32), axis=(0, 1)
        ).reshape(-1)[:small_length]
        landed = (
            landed.transpose(1, 0, 2, 3)
            .reshape(members, rows_each, 3, head_cols)[:, : row_shard + BIAS_ROW + 1]
        )
        if members == 2:
            swap = member == 1
            landed = jnp.stack(
                [
                    jnp.where(swap, landed[1], landed[0]),
                    jnp.where(swap, landed[0], landed[1]),
                ]
            )
        else:
            landed = jnp.take(landed, lax.bitwise_xor(member, jnp.arange(members)), axis=0)
        grad_qkv = landed[:, :row_shard].transpose(1, 2, 0, 3)
        grad_qkv = grad_qkv.reshape(row_shard, 3 * model_width).astype(F32)
        bias_out_row = landed[:, row_shard + BIAS_ROW].astype(F32).transpose(1, 0, 2)
        bias_out_row = lax.dynamic_slice(
            bias_out_row.reshape(3, model_width), (0, here * row_shard), (3, row_shard)
        )

    feed_shard = feed_width // shards
    spots = [0, row_shard, 3 * row_shard, 5 * row_shard]
    return (
        output,
        d_inputs,
        grad_qkv,
        bias_out_row[::2],
        grad_out,
        smalls_out[spots[0] : spots[1]],
        smalls_out[spots[1] : spots[2]].reshape(2, row_shard),
        smalls_out[spots[2] : spots[3]].reshape(2, row_shard),
        grad_up,
        smalls_out[spots[3] : spots[3] + feed_shard],
        grad_down,
        smalls_out[spots[3] + feed_shard :],
    )


def solution(mesh):
    placed = (
        P(("dp", "fsdp"), None),
        P(("dp", "fsdp"), None),
        P("dp", None, None),
        P("dp"),
        P("fsdp", None),
        P(None, "fsdp"),
        P("fsdp", None),
        P("fsdp"),
        P(None, "fsdp"),
        P(None, "fsdp"),
        P("fsdp", None),
        P("fsdp"),
        P("fsdp", None),
        P("fsdp"),
    )
    return jax.shard_map(
        body,
        mesh=mesh,
        in_specs=placed,
        out_specs=(
            P(("dp", "fsdp"), None),
            P(("dp", "fsdp"), None),
            P("fsdp", None),
            P(None, "fsdp"),
            P("fsdp", None),
            P("fsdp"),
            P(None, "fsdp"),
            P(None, "fsdp"),
            P("fsdp", None),
            P("fsdp"),
            P("fsdp", None),
            P("fsdp"),
        ),
        check_vma=False,
    )
```

```python
from functools import partial

import jax
import jax.numpy as jnp
from jax import lax
from jax.experimental import pallas as pl
from jax.experimental.pallas import tpu as pltpu
from jax.sharding import PartitionSpec as P

HEAD_DIM = 64
CORES = 2
NEG_FILL = -1000000000.0
EPSILON = 1e-05
SCALE = HEAD_DIM ** (-0.5)
BIAS_ROW = 2
GRAD_LANES = 384
CLUSTER_ROWS = 128
HALF_ROWS = 64
POS_BLOCK = 512
TOKEN_BLOCK = 512
ROW_BLOCK = 256
FF_BLOCK = 512
MIB = 1024 * 1024
NT = (((1,), (1,)), ((), ()))
TN = (((0,), (0,)), ((), ()))
F32 = jnp.float32
BF16 = jnp.bfloat16
ANYWHERE = pl.BlockSpec(memory_space=pl.ANY)
IN_SMEM = pl.BlockSpec(memory_space=pltpu.SMEM)


def whole(shape):
    return pl.BlockSpec(shape, lambda i: (0,) * len(shape))


def rows_of(shape):
    return pl.BlockSpec(shape, lambda i: (i,) + (0,) * (len(shape) - 1))


def dot(a, b, dims=(((1,), (0,)), ((), ()))):
    return lax.dot_general(a, b, dims, preferred_element_type=F32)


def params(mib, flops=0, moved=0, share=16):
    return dict(
        compiler_params=pltpu.CompilerParams(
            dimension_semantics=("arbitrary",),
            vmem_limit_bytes=mib * MIB,
        ),
        cost_estimate=pl.CostEstimate(
            flops=flops // share, bytes_accessed=moved // share, transcendentals=0
        ),
    )


def gated(kernel, used, needs):
    if not needs:
        return kernel

    def run(*refs):
        return kernel(*refs[:used], *refs[used + len(needs) :])

    return run


def lane_masks():
    lane = lax.broadcasted_iota(jnp.int32, (CLUSTER_ROWS, CLUSTER_ROWS), 1)
    low = (lane < HEAD_DIM).astype(F32)
    return low.astype(BF16), (1.0 - low).astype(BF16), lane < HEAD_DIM


def corners(first, second):
    blank = jnp.zeros_like(first)
    return jnp.concatenate(
        [
            jnp.concatenate([first, blank], axis=1),
            jnp.concatenate([blank, second], axis=1),
        ],
        axis=0,
    )


def both_heads(rows_now, low, high):
    return jnp.concatenate([rows_now * low, rows_now * high], axis=0)


def equal_ones(left, right):
    return jnp.where(left == right, jnp.ones((), BF16), jnp.zeros((), BF16))


def pick_rows(order_ref, first_row, unit_len):
    parts = []
    lane = lax.broadcasted_iota(jnp.int16, (CLUSTER_ROWS, CLUSTER_ROWS), 1)
    for part in range(POS_BLOCK // CLUSTER_ROWS):
        row = order_ref[pl.ds(first_row + part, 1), :]
        column = jnp.transpose(jnp.broadcast_to(row, (CLUSTER_ROWS, CLUSTER_ROWS)))
        column = column.astype(jnp.int16)
        pieces = [
            equal_ones(column, lane + jnp.int16(base)) for base in range(0, unit_len, CLUSTER_ROWS)
        ]
        parts.append(jnp.concatenate(pieces, axis=1))
    return jnp.concatenate(parts, axis=0)


def load_pieces(meta, x_refs, w_refs, x_all, w_all, sems, row_shard):
    member_rows = x_all.shape[0] // max(1, len(x_refs))
    copies = []
    for index, ref in enumerate(x_refs):
        copies.append(
            pltpu.make_async_copy(
                ref, x_all.at[pl.ds(index * member_rows, member_rows), :], sems.at[index]
            )
        )
    for index, ref in enumerate(w_refs):
        mask = meta[meta.shape[0] - len(w_refs) + index]
        start = pl.multiple_of(lax.bitwise_xor(meta[1], mask) * row_shard, 16)
        copies.append(
            pltpu.make_async_copy(
                ref.at[pl.ds(0, row_shard), :],
                w_all.at[pl.ds(start, row_shard), :],
                sems.at[len(x_refs) + index],
            )
        )
    for copy in copies:
        copy.start()
    for copy in copies:
        copy.wait()


def arrange_kernel(unit_len, first_row, order_ref, *refs):
    x_refs, out_ref = refs[:-1], refs[-1]
    step = pl.program_id(0)
    picks = pick_rows(order_ref, first_row + step * (POS_BLOCK // CLUSTER_ROWS), unit_len)
    rows = x_refs[0].shape[0]
    total = None
    for index, ref in enumerate(x_refs):
        term = dot(picks[:, index * rows : (index + 1) * rows], ref[...])
        total = term if total is None else total + term
    out_ref[...] = total.astype(BF16)


def arrange(order, x_pieces, position_count, first_row):
    member_rows, width = x_pieces[0].shape
    unit_len = member_rows * len(x_pieces)
    return pl.pallas_call(
        partial(arrange_kernel, unit_len, first_row),
        grid=(position_count // POS_BLOCK,),
        in_specs=[whole(order.shape)] + [whole(piece.shape) for piece in x_pieces],
        out_specs=rows_of((POS_BLOCK, width)),
        out_shape=jax.ShapeDtypeStruct((position_count, width), BF16),
        name="arrange",
        **params(20, 2 * position_count * unit_len * width, 6_000_000),
    )(order, *x_pieces)


def attend_kernel(sizes, meta, x_now_ref, bias_ref, *refs):
    shards, row_shard = sizes
    w_refs, refs = refs[:shards], refs[shards:]
    arranged_ref, probs_ref, mixture_ref, turned_ref, w_all, sems = refs
    width = w_all.shape[1] // 3
    step = pl.program_id(0)

    @pl.when(step == 0)
    def _():
        load_pieces(meta, [], w_refs, w_all, w_all, sems, row_shard)

    x_now = x_now_ref[...]
    turned_ref[...] = jnp.transpose(x_now)
    arranged = (dot(x_now, w_all[...]) + bias_ref[...]).astype(BF16)
    arranged_ref[...] = arranged
    low, high, lane_low = lane_masks()
    position = lax.broadcasted_iota(jnp.int32, (CLUSTER_ROWS, CLUSTER_ROWS), 0)
    other = lax.broadcasted_iota(jnp.int32, (CLUSTER_ROWS, CLUSTER_ROWS), 1)
    same_half = (position < HALF_ROWS) == (other < HALF_ROWS)
    allowed = jnp.logical_or(same_half, meta[0] == 1)
    pairs = width // CLUSTER_ROWS
    units = [(part, pair) for part in range(POS_BLOCK // CLUSTER_ROWS) for pair in range(pairs)]
    for index in range(0, len(units), 2):
        queries, keys, values = [], [], []
        for part, pair in units[index : index + 2]:
            rows_now = slice(part * CLUSTER_ROWS, (part + 1) * CLUSTER_ROWS)
            base = pair * CLUSTER_ROWS
            queries.append(arranged[rows_now, base : base + CLUSTER_ROWS] * SCALE)
            one_key = arranged[rows_now, width + base : width + base + CLUSTER_ROWS]
            keys.append(both_heads(one_key, low, high))
            one_value = arranged[rows_now, 2 * width + base : 2 * width + base + CLUSTER_ROWS]
            values.append(both_heads(one_value, low, high))
        both_scores = dot(jnp.concatenate(keys, axis=1), corners(*queries), NT)
        for which, (part, pair) in enumerate(units[index : index + 2]):
            halves = []
            for head in range(2):
                one = both_scores[
                    head * CLUSTER_ROWS : (head + 1) * CLUSTER_ROWS,
                    which * CLUSTER_ROWS : (which + 1) * CLUSTER_ROWS,
                ]
                one = jnp.where(allowed, one, NEG_FILL)
                grown = jnp.exp(one - jnp.max(one, axis=0, keepdims=True))
                halves.append(grown * (1.0 / jnp.sum(grown, axis=0, keepdims=True)))
            probs = jnp.concatenate(halves, axis=0).astype(BF16)
            at = (part * pairs + pair) * 2 * CLUSTER_ROWS
            probs_ref[at : at + 2 * CLUSTER_ROWS, :] = probs
            mixture_ref[
                part * CLUSTER_ROWS : (part + 1) * CLUSTER_ROWS,
                pair * CLUSTER_ROWS : (pair + 1) * CLUSTER_ROWS,
            ] = dot(probs, values[which], TN).astype(BF16)


def attend(meta, x_now, bias, w_pieces, row_shard, needs=()):
    shards = len(w_pieces)
    position_count, model_width = x_now.shape
    cols = w_pieces[0].shape[1]
    width = cols // 3
    pair_rows = 2 * width
    return pl.pallas_call(
        gated(partial(attend_kernel, (shards, row_shard)), 3 + shards, needs),
        grid=(position_count // POS_BLOCK,),
        in_specs=[IN_SMEM, rows_of((POS_BLOCK, model_width)), whole(bias.shape)]
        + [ANYWHERE] * (shards + len(needs)),
        out_specs=[
            rows_of((POS_BLOCK, cols)),
            rows_of((POS_BLOCK // CLUSTER_ROWS * pair_rows, CLUSTER_ROWS)),
            rows_of((POS_BLOCK, width)),
            pl.BlockSpec((model_width, POS_BLOCK), lambda i: (0, i)),
        ],
        out_shape=[
            jax.ShapeDtypeStruct((position_count, cols), BF16),
            jax.ShapeDtypeStruct((position_count // CLUSTER_ROWS * pair_rows, CLUSTER_ROWS), BF16),
            jax.ShapeDtypeStruct((position_count, width), BF16),
            jax.ShapeDtypeStruct((model_width, position_count), BF16),
        ],
        scratch_shapes=[
            pltpu.VMEM((model_width, cols), BF16),
            pltpu.SemaphoreType.DMA((shards,)),
        ],
        name="attend",
        **params(
            60, 8 * position_count * (model_width * cols + 4 * CLUSTER_ROWS * width), 18_000_000, 1
        ),
    )(meta, x_now, bias, *w_pieces, *needs)


def place_kernel(sizes, scale, has_base, order_row_ref, *refs):
    unit_len, first_token, added = sizes
    base_ref = refs[0] if has_base else None
    refs = refs[1 if has_base else 0 :]
    if added:
        first_ref, second_ref, out_ref, held = refs

        @pl.when(pl.program_id(0) == 0)
        def _():
            held[...] = (first_ref[...].astype(F32) + second_ref[...].astype(F32)).astype(BF16)

        source_refs = [held]
    else:
        source_refs, out_ref = refs[:-1], refs[-1]
    block_rows = out_ref.shape[0]
    first = jnp.full((1, 1), first_token + pl.program_id(0) * block_rows, jnp.int32)
    token = lax.broadcasted_iota(jnp.int16, (block_rows, unit_len), 0)
    total = None
    for index, ref in enumerate(source_refs):
        row = order_row_ref[:, index * unit_len : (index + 1) * unit_len] - first
        row = jnp.broadcast_to(row, (16, unit_len)).astype(jnp.int16)
        row = jnp.concatenate([row] * (block_rows // 16), axis=0)
        term = dot(equal_ones(row, token), ref[...])
        total = term if total is None else total + term
    if scale != 1.0:
        total = total * scale
    if has_base:
        total = total + base_ref[...].astype(F32)
    out_ref[...] = total.astype(out_ref.dtype)


def place(
    order_row,
    sources,
    first_token,
    row_count,
    scale=1.0,
    dtype=BF16,
    base=None,
    added=False,
    needs=(),
):
    unit_len, width = sources[0].shape
    block_rows = min(TOKEN_BLOCK, row_count)
    extra = [] if base is None else [base]
    return pl.pallas_call(
        gated(
            partial(place_kernel, (unit_len, first_token, added), scale, base is not None),
            1 + len(extra) + len(sources),
            needs,
        ),
        grid=(row_count // block_rows,),
        in_specs=[whole(order_row.shape)]
        + [rows_of((block_rows, width))] * len(extra)
        + [whole(source.shape) for source in sources]
        + [ANYWHERE] * len(needs),
        out_specs=rows_of((block_rows, width)),
        out_shape=jax.ShapeDtypeStruct((row_count, width), dtype),
        scratch_shapes=[pltpu.VMEM((unit_len, width), BF16)] if added else [],
        name="place",
        **params(
            32 if added else 20,
            16 * row_count * unit_len * width,
            10_000_000,
            1,
        ),
    )(order_row, *extra, *sources, *needs)


def attend_back_kernel(sizes, meta, order_ref, arranged_ref, probs_ref, *refs):
    members, shards, unit_len, row_shard, first_row, start = sizes
    g_refs, refs = refs[:members], refs[members:]
    w_refs, refs = refs[:shards], refs[shards:]
    grads_ref, d_x_ref, token_ref, g_all, w_all, sems = refs
    width = w_all.shape[1] // 3
    step = pl.program_id(0)

    @pl.when(step == 0)
    def _():
        load_pieces(meta, g_refs, w_refs, g_all, w_all, sems, row_shard)
        token_ref[...] = jnp.zeros_like(token_ref)

    at_row = first_row + (start + step) * (POS_BLOCK // CLUSTER_ROWS)
    picks = pick_rows(order_ref, at_row, unit_len)
    d_mixture = dot(picks, g_all[...]).astype(BF16)
    low, high, lane_low = lane_masks()
    pairs = width // CLUSTER_ROWS
    units = [(part, pair) for part in range(POS_BLOCK // CLUSTER_ROWS) for pair in range(pairs)]
    for index in range(0, len(units), 2):
        values, d_rows = [], []
        for part, pair in units[index : index + 2]:
            rows_now = slice(part * CLUSTER_ROWS, (part + 1) * CLUSTER_ROWS)
            base = pair * CLUSTER_ROWS
            one_value = arranged_ref[rows_now, 2 * width + base : 2 * width + base + CLUSTER_ROWS]
            values.append(both_heads(one_value, low, high))
            d_rows.append(d_mixture[rows_now, base : base + CLUSTER_ROWS])
        both_probs = dot(jnp.concatenate(values, axis=1), corners(*d_rows), NT)
        for which, (part, pair) in enumerate(units[index : index + 2]):
            rows_now = slice(part * CLUSTER_ROWS, (part + 1) * CLUSTER_ROWS)
            base = pair * CLUSTER_ROWS
            q_lanes = slice(base, base + CLUSTER_ROWS)
            k_lanes = slice(width + base, width + base + CLUSTER_ROWS)
            v_lanes = slice(2 * width + base, 2 * width + base + CLUSTER_ROWS)
            queries = arranged_ref[rows_now, q_lanes] * SCALE
            keys = arranged_ref[rows_now, k_lanes] * SCALE
            at = (part * pairs + pair) * 2 * CLUSTER_ROWS
            probs = probs_ref[at : at + 2 * CLUSTER_ROWS, :]
            d_probs = both_probs[:, which * CLUSTER_ROWS : (which + 1) * CLUSTER_ROWS]
            pieces = []
            for head in range(2):
                rows = slice(head * CLUSTER_ROWS, (head + 1) * CLUSTER_ROWS)
                weight = probs[rows].astype(F32)
                d_one = d_probs[rows]
                inner = jnp.sum(weight * d_one, axis=0, keepdims=True)
                pieces.append(weight * (d_one - inner))
            d_scores = jnp.concatenate(pieces, axis=0).astype(BF16)
            d_query = dot(d_scores, both_heads(keys, low, high), TN)
            d_pair = dot(
                jnp.concatenate([probs, d_scores], axis=1), corners(d_rows[which], queries)
            )
            d_values, d_keys = d_pair[:, :CLUSTER_ROWS], d_pair[:, CLUSTER_ROWS:]
            grads_ref[rows_now, q_lanes] = d_query.astype(BF16)
            grads_ref[rows_now, k_lanes] = jnp.where(
                lane_low, d_keys[:CLUSTER_ROWS], d_keys[CLUSTER_ROWS:]
            ).astype(BF16)
            grads_ref[rows_now, v_lanes] = jnp.where(
                lane_low, d_values[:CLUSTER_ROWS], d_values[CLUSTER_ROWS:]
            ).astype(BF16)
    grads = grads_ref[...]
    d_x_ref[...] = dot(grads, w_all[...], NT).astype(BF16)


def attend_back(
    meta, order, arranged, probs, g_pieces, w_pieces, row_shard, first_row, needs, span, into
):
    members, shards = len(g_pieces), len(w_pieces)
    member_rows, width = g_pieces[0].shape
    unit_len = members * member_rows
    position_count, cols = arranged.shape
    model_width = row_shard * shards
    start, stop = span
    pair_rows = POS_BLOCK // CLUSTER_ROWS * 2 * width
    used = 4 + members + shards

    def block(shape):
        return pl.BlockSpec(shape, lambda i: (start + i, 0))

    return pl.pallas_call(
        gated(
            partial(attend_back_kernel, (members, shards, unit_len, row_shard, first_row, start)),
            used,
            list(into) + list(needs),
        ),
        grid=(stop - start,),
        in_specs=[
            IN_SMEM,
            whole(order.shape),
            block((POS_BLOCK, cols)),
            block((pair_rows, CLUSTER_ROWS)),
        ]
        + [ANYWHERE] * (members + shards + len(into) + len(needs)),
        out_specs=[block((POS_BLOCK, cols)), block((POS_BLOCK, model_width)), whole((8, 128))],
        out_shape=[
            jax.ShapeDtypeStruct((position_count, cols), BF16),
            jax.ShapeDtypeStruct((position_count, model_width), BF16),
            jax.ShapeDtypeStruct((8, 128), F32),
        ],
        input_output_aliases={used + index: index for index in range(len(into))},
        scratch_shapes=[
            pltpu.VMEM((unit_len, width), BF16),
            pltpu.VMEM((model_width, cols), BF16),
            pltpu.SemaphoreType.DMA((members + shards,)),
        ],
        name="attend_back",
        **params(
            60,
            12 * (stop - start) * POS_BLOCK * (unit_len * width + model_width * cols),
            20_000_000,
            1,
        ),
    )(meta, order, arranged, probs, *g_pieces, *w_pieces, *into, *needs)


def normalise(summed):
    average = jnp.mean(summed, axis=-1, keepdims=True)
    centred = summed - average
    spread = jnp.mean(centred * centred, axis=-1, keepdims=True)
    scale_inv = lax.rsqrt(spread + EPSILON)
    return centred * scale_inv, scale_inv


def normalise_back(grad_out, normed, scale_inv, gain_row):
    scaled = grad_out * gain_row
    return scale_inv * (
        scaled
        - jnp.mean(scaled, axis=-1, keepdims=True)
        - normed * jnp.mean(scaled * normed, axis=-1, keepdims=True)
    )


def column_sum(rows_now):
    return jnp.sum(rows_now, axis=0, keepdims=True)


def gelu_parts(value):
    below = 0.5 + 0.5 * lax.erf(value * 0.7071067811865476)
    bell = jnp.exp(value * value * -0.5) * 0.3989422804014327
    return value * below, below + value * bell


class Pack:
    def __init__(self, model_width, feed_width, shards, units, depth):
        self.model_width, self.feed_width, self.shards = model_width, feed_width, shards
        self.row_shard = model_width // shards
        self.feed_shard = feed_width // shards
        self.down_rows = self.feed_shard // CORES
        self.blocks = feed_width // CORES // model_width
        self.up_at = self.down_rows
        self.out_at = self.up_at + self.blocks * self.row_shard
        self.out_rows = self.row_shard // CORES
        self.used = self.out_at + self.out_rows
        unit = 16 * depth
        self.rows = -(-self.used // unit) * unit
        self.rest_rows = self.rows - self.down_rows
        self.units = units
        self.group = units * self.row_shard

    def out_start(self, shard, member):
        return (
            lax.bitwise_xor(jnp.int32(shard) // self.units, member) * self.group
            + (shard % self.units) * self.row_shard
        )


def feed_kernel(pack, att_count, meta, x_ref, cot_ref, vec_ref, up_bias_ref, *refs):
    shards = pack.shards
    att_refs, refs = refs[:att_count], refs[att_count:]
    own_out, own_up, own_down = refs[:3]
    refs = refs[3:]
    pieces, refs = refs[: 2 * (shards - 1)], refs[2 * (shards - 1) :]
    out_ref, first_turned_ref, d_branch_ref, d_ffn_turned_ref, hidden_ref, d_pre_ref = refs[:6]
    att_turned_ref = refs[6]
    refs = refs[7:]
    d_att_refs, refs = refs[:att_count], refs[att_count:]
    sums_ref, up_sums_ref, w_out, w_up, w_down, slope, sems = refs
    step = pl.program_id(0)
    here, core, member = meta[1], meta[2], meta[3]
    feed_width = pack.feed_width

    def loads(kind):
        copies = []

        def add(source, target):
            copies.append(pltpu.make_async_copy(source, target, sems.at[kind, len(copies)]))

        if kind == 0:
            start = pl.multiple_of(pack.out_start(here, member), 16)
            add(own_out, w_out.at[pl.ds(start, pack.row_shard), :])
        elif kind == 1:
            start = pl.multiple_of(here * pack.row_shard, 16)
            add(own_up, w_up.at[pl.ds(start, pack.row_shard), :])
        else:
            start = pl.multiple_of(here * pack.feed_shard, 16)
            add(own_down, w_down.at[pl.ds(start, pack.feed_shard), :])
        for index, ref in enumerate(pieces):
            peer = lax.bitwise_xor(here, meta[8 + index])
            half = core if index < shards - 1 else 1 - core
            if kind == 0:
                start = pack.out_start(peer, member) + half * pack.out_rows
                start = pl.multiple_of(start, 16)
                add(
                    ref.at[pl.ds(pack.out_at, pack.out_rows), :],
                    w_out.at[pl.ds(start, pack.out_rows), :],
                )
            elif kind == 1:
                start = pl.multiple_of(peer * pack.row_shard, 16)
                for block in range(pack.blocks):
                    lane = pl.multiple_of(
                        (half * pack.blocks + block) * pack.model_width, CLUSTER_ROWS
                    )
                    add(
                        ref.at[pl.ds(pack.up_at + block * pack.row_shard, pack.row_shard), :],
                        w_up.at[pl.ds(start, pack.row_shard), pl.ds(lane, pack.model_width)],
                    )
            else:
                start = pl.multiple_of(peer * pack.feed_shard + half * pack.down_rows, 16)
                add(
                    ref.at[pl.ds(0, pack.down_rows), :],
                    w_down.at[pl.ds(start, pack.down_rows), :],
                )
        return copies

    @pl.when(step == 0)
    def _():
        for kind in range(3):
            for copy in loads(kind):
                copy.start()
        sums_ref[...] = jnp.zeros_like(sums_ref)
        up_sums_ref[...] = jnp.zeros_like(up_sums_ref)
        for copy in loads(0):
            copy.wait()

    bias_out, gain_one, gain_two = vec_ref[0:1, :], vec_ref[1:2, :], vec_ref[2:3, :]
    shift_one, shift_two, bias_down = vec_ref[3:4, :], vec_ref[4:5, :], vec_ref[5:6, :]
    att_width = att_refs[0].shape[1]
    summed = x_ref[...].astype(F32) + bias_out
    for index, ref in enumerate(att_refs):
        summed += dot(ref[...], w_out[index * att_width : (index + 1) * att_width, :])
    normed_one, inv_one = normalise(summed)
    first = normed_one * gain_one + shift_one
    first_low = first.astype(BF16)
    first_turned_ref[...] = jnp.transpose(first_low)
    for index, ref in enumerate(att_refs):
        att_turned_ref[index * att_width : (index + 1) * att_width, :] = jnp.transpose(ref[...])

    @pl.when(step == 0)
    def _():
        for kind in (1, 2):
            for copy in loads(kind):
                copy.wait()

    second = first + bias_down
    starts = list(range(0, feed_width, FF_BLOCK))

    def raised(base):
        lanes = slice(base, base + FF_BLOCK)
        return dot(first_low, w_up[:, lanes]) + up_bias_ref[:, lanes]

    pre = raised(starts[0])
    for index, base in enumerate(starts):
        lanes = slice(base, base + FF_BLOCK)
        pre_next = raised(starts[index + 1]) if index + 1 < len(starts) else None
        hidden, slope_now = gelu_parts(pre)
        hidden = hidden.astype(BF16)
        hidden_ref[:, lanes] = hidden
        slope[:, lanes] = slope_now
        second += dot(hidden, w_down[lanes, :])
        pre = pre_next
    normed_two, inv_two = normalise(second)
    out_ref[...] = (normed_two * gain_two + shift_two).astype(BF16)
    top = cot_ref[...].astype(F32)
    d_second = normalise_back(top, normed_two, inv_two, gain_two)
    d_ffn = d_second.astype(BF16)
    d_ffn_turned_ref[...] = jnp.transpose(d_ffn)
    d_first = d_second
    d_hidden = dot(d_ffn, w_down[0:FF_BLOCK, :], NT)
    for index, base in enumerate(starts):
        lanes = slice(base, base + FF_BLOCK)
        if index + 1 < len(starts):
            d_next = dot(d_ffn, w_down[starts[index + 1] : starts[index + 1] + FF_BLOCK, :], NT)
        d_pre = (d_hidden * slope[:, lanes]).astype(BF16)
        d_pre_ref[:, lanes] = d_pre
        up_sums_ref[:, lanes] += column_sum(d_pre.astype(F32))
        d_first += dot(d_pre, w_up[:, lanes], NT)
        d_hidden = d_next
    d_lower = normalise_back(d_first, normed_one, inv_one, gain_one)
    d_branch = d_lower.astype(BF16)
    d_branch_ref[...] = d_branch
    for index, ref in enumerate(d_att_refs):
        back = dot(d_branch, w_out[index * att_width : (index + 1) * att_width, :], NT)
        ref[...] = (0.5 * back).astype(BF16)
    sums_ref[0:1, :] += column_sum(d_branch.astype(F32))
    sums_ref[1:2, :] += column_sum(d_first * normed_one)
    sums_ref[2:3, :] += column_sum(top * normed_two)
    sums_ref[3:4, :] += column_sum(d_first)
    sums_ref[4:5, :] += column_sum(top)
    sums_ref[5:6, :] += column_sum(d_ffn.astype(F32))


def feed(pack, meta, x_own, cot_own, vectors, up_bias, att, own, pieces):
    row_count, model_width = x_own.shape
    feed_width = pack.feed_width
    att_width = att[0].shape[1]
    one = rows_of((ROW_BLOCK, model_width))
    wide = rows_of((ROW_BLOCK, feed_width))
    narrow = rows_of((ROW_BLOCK, att_width))
    turned = pl.BlockSpec((model_width, ROW_BLOCK), lambda i: (0, i))
    turned_shape = jax.ShapeDtypeStruct((model_width, row_count), BF16)

    def like(width):
        return jax.ShapeDtypeStruct((row_count, width), BF16)

    return pl.pallas_call(
        partial(feed_kernel, pack, len(att)),
        grid=(row_count // ROW_BLOCK,),
        in_specs=[IN_SMEM, one, one, whole(vectors.shape), whole(up_bias.shape)]
        + [narrow] * len(att)
        + [ANYWHERE] * (3 + len(pieces)),
        out_specs=[one, turned, one, turned, wide, wide, turned]
        + [narrow] * len(att)
        + [whole((8, model_width)), whole((1, feed_width))],
        out_shape=[
            like(model_width),
            turned_shape,
            like(model_width),
            turned_shape,
            like(feed_width),
            like(feed_width),
            turned_shape,
        ]
        + [like(att_width)] * len(att)
        + [
            jax.ShapeDtypeStruct((8, model_width), F32),
            jax.ShapeDtypeStruct((1, feed_width), F32),
        ],
        scratch_shapes=[
            pltpu.VMEM((model_width, model_width), BF16),
            pltpu.VMEM((model_width, feed_width), BF16),
            pltpu.VMEM((feed_width, model_width), BF16),
            pltpu.VMEM((ROW_BLOCK, feed_width), F32),
            pltpu.SemaphoreType.DMA((3, 1 + pack.blocks * len(pieces))),
        ],
        name="feed",
        **params(
            40, 2 * row_count * model_width * (2 * model_width + 4 * feed_width), 40_000_000
        ),
    )(meta, x_own, cot_own, vectors, up_bias, *att, *own, *pieces)


def down_grads_kernel(pack, table, d_ffn_ref, hidden_ref, theirs_ref, mine_ref, made, sems):
    step = pl.program_id(0)
    core = table[0]

    def stores(shard):
        return [
            pltpu.make_async_copy(made.at[1 - core, shard], theirs_ref.at[shard], sems.at[0, shard]),
            pltpu.make_async_copy(made.at[core, shard], mine_ref.at[shard], sems.at[1, shard]),
        ]

    grad = dot(d_ffn_ref[...], hidden_ref[...]).astype(BF16)
    for half in range(CORES):
        for lane in range(0, pack.model_width, pack.feed_shard):
            begin = half * (pack.model_width // CORES) + lane // pack.feed_shard * pack.down_rows
            made[half, step, :, lane : lane + pack.feed_shard] = grad[
                begin : begin + pack.down_rows
            ]
    for copy in stores(step):
        copy.start()

    @pl.when(step == pack.shards - 1)
    def _():
        for shard in range(pack.shards):
            for copy in stores(shard):
                copy.wait()


def down_grads(pack, table, d_ffn, hidden):
    model_width, row_count = d_ffn.shape
    shape = (pack.shards, pack.down_rows, model_width)
    return pl.pallas_call(
        partial(down_grads_kernel, pack),
        grid_spec=pltpu.PrefetchScalarGridSpec(
            num_scalar_prefetch=1,
            grid=(pack.shards,),
            in_specs=[
                pl.BlockSpec(d_ffn.shape, lambda step, table: (0, 0)),
                pl.BlockSpec((row_count, pack.feed_shard), lambda step, table: (0, step)),
            ],
            out_specs=[ANYWHERE] * 2,
            scratch_shapes=[
                pltpu.VMEM((CORES,) + shape, BF16),
                pltpu.SemaphoreType.DMA((CORES, pack.shards)),
            ],
        ),
        out_shape=[jax.ShapeDtypeStruct(shape, BF16)] * 2,
        name="down_grads",
        **params(60, 2 * row_count * model_width * pack.feed_width, 10_000_000),
    )(table, d_ffn, hidden)


def rest_grads_kernel(
    pack, table, first_ref, d_pre_ref, att_ref, d_branch_ref, theirs_ref, mine_ref, *scratch
):
    att, d_branch, tile, made, in_sems, sems = scratch
    step = pl.program_id(0)
    core, member = table[0], table[1]
    shards, blocks = pack.shards, pack.blocks
    out_at = pack.out_at - pack.down_rows

    loads = [
        pltpu.make_async_copy(att_ref, att, in_sems.at[0]),
        pltpu.make_async_copy(d_branch_ref, d_branch, in_sems.at[1]),
    ]

    def store(half, start, rows, sem):
        there = (slice(None), pl.ds(start, rows), slice(None))

        def copy(target):
            return pltpu.make_async_copy(
                made.at[(half,) + there], target.at[there], sems.at[half, sem]
            )

        return copy

    def both(half, start, rows, sem, act):
        copy = store(half, start, rows, sem)

        @pl.when(core == half)
        def _():
            act(copy(mine_ref))

        @pl.when(core != half)
        def _():
            act(copy(theirs_ref))

    @pl.when(step == 0)
    def _():
        for copy in loads:
            copy.start()

    @pl.when(step < CORES * blocks)
    def _():
        grad = dot(first_ref[...], d_pre_ref[...]).astype(BF16)
        start = pl.multiple_of(step % blocks * pack.row_shard, 16)
        for shard in range(shards):
            made[step // blocks, shard, pl.ds(start, pack.row_shard), :] = grad[
                shard * pack.row_shard : (shard + 1) * pack.row_shard
            ]

    for half in range(CORES):

        @pl.when(step == (half + 1) * blocks - 1)
        def _(half=half):
            both(half, 0, out_at, 0, lambda copy: copy.start())

    @pl.when(step == CORES * blocks)
    def _():
        for copy in loads:
            copy.wait()
        tile[...] = dot(att[...], d_branch[...])
        spare = pack.rows - pack.used
        for half in range(CORES):
            for shard in range(shards):
                start = pack.out_start(shard, member) + half * pack.out_rows
                start = pl.multiple_of(start, 16)
                made[half, shard, out_at : out_at + pack.out_rows, :] = tile[
                    pl.ds(start, pack.out_rows), :
                ].astype(BF16)
                if spare:
                    made[half, shard, out_at + pack.out_rows :, :] = jnp.zeros(
                        (spare, pack.model_width), BF16
                    )
            both(half, out_at, pack.rest_rows - out_at, 1, lambda copy: copy.start())
        for half in range(CORES):
            both(half, 0, out_at, 0, lambda copy: copy.wait())
            both(half, out_at, pack.rest_rows - out_at, 1, lambda copy: copy.wait())


def rest_grads(pack, table, first_low, d_pre, att, d_branch, needs=()):
    model_width, row_count = first_low.shape
    shape = (pack.shards, pack.rest_rows, model_width)
    steps = CORES * pack.blocks
    return pl.pallas_call(
        gated(partial(rest_grads_kernel, pack), 5, needs),
        grid_spec=pltpu.PrefetchScalarGridSpec(
            num_scalar_prefetch=1,
            grid=(steps + 1,),
            in_specs=[
                pl.BlockSpec(first_low.shape, lambda step, table: (0, 0)),
                pl.BlockSpec(
                    (row_count, model_width),
                    lambda step, table: (0, jnp.minimum(step, steps - 1)),
                ),
            ]
            + [ANYWHERE] * (2 + len(needs)),
            out_specs=[ANYWHERE] * 2,
            scratch_shapes=[
                pltpu.VMEM((model_width, row_count), BF16),
                pltpu.VMEM((row_count, model_width), BF16),
                pltpu.VMEM((model_width, model_width), F32),
                pltpu.VMEM((CORES,) + shape, BF16),
                pltpu.SemaphoreType.DMA((2,)),
                pltpu.SemaphoreType.DMA((CORES, 2)),
            ],
        ),
        out_shape=[jax.ShapeDtypeStruct(shape, BF16)] * 2,
        name="rest_grads",
        **params(60, 2 * row_count * model_width * (pack.feed_width + model_width), 10_000_000),
    )(table, first_low, d_pre, att, d_branch, *needs)


def qkv_grads_kernel(rounds, x_refs_then, *refs):
    refs = (x_refs_then,) + refs
    x_refs, grad_refs = refs[:rounds], refs[rounds : 2 * rounds]
    small_ref, out_ref = refs[2 * rounds :]
    shards, rows, _ = out_ref.shape
    row_shard = rows - small_ref.shape[1]
    total, sums = None, None
    for x_ref, grad_ref in zip(x_refs, grad_refs):
        grads = grad_ref[...]
        term = dot(x_ref[...], grads)
        down = column_sum(grads.astype(F32))
        total = term if total is None else total + term
        sums = down if sums is None else sums + down
    total = total.astype(BF16)
    row = lax.broadcasted_iota(jnp.int32, small_ref.shape[1:], 0)
    for shard in range(shards):
        out_ref[shard, :row_shard, :] = total[shard * row_shard : (shard + 1) * row_shard]
        last = jnp.where(row == BIAS_ROW, sums, small_ref[shard])
        out_ref[shard, row_shard:, :] = last.astype(BF16)


def qkv_grads(x_turned, grads, small, row_shard, needs=()):
    rounds = len(grads)
    model_width, positions = x_turned[0].shape
    cols = grads[0].shape[1]
    shards, extra, _ = small.shape
    block = GRAD_LANES if cols % GRAD_LANES == 0 else cols
    return pl.pallas_call(
        gated(partial(qkv_grads_kernel, rounds), 2 * rounds + 1, needs),
        grid=(cols // block,),
        in_specs=[whole((model_width, positions))] * rounds
        + [pl.BlockSpec((positions, block), lambda i: (0, i))] * rounds
        + [pl.BlockSpec((shards, extra, block), lambda i: (0, 0, i))]
        + [ANYWHERE] * len(needs),
        out_specs=pl.BlockSpec((shards, row_shard + extra, block), lambda i: (0, 0, i)),
        out_shape=jax.ShapeDtypeStruct((shards, row_shard + extra, cols), BF16),
        name="qkv_grads",
        **params(60, 2 * rounds * positions * model_width * cols, 18_000_000),
    )(*x_turned, *grads, small, *needs)


def add_picked_kernel(count, first, table, *refs):
    in_refs, out_refs = refs[:count], refs[count:]
    if count == 2:
        total = in_refs[0][...] + in_refs[1][...]
    else:
        total = in_refs[0][...].astype(F32)
        for ref in in_refs[1:]:
            total = total + ref[...].astype(F32)
        total = total.astype(BF16)
    if len(out_refs) == 1:
        out_refs[0][...] = total
        return

    @pl.when(pl.program_id(0) < first)
    def _():
        out_refs[0][...] = total

    @pl.when(pl.program_id(0) >= first)
    def _():
        out_refs[1][...] = total


def add_picked(table, arrays, steps, first=None, needs=(), work=0):
    _, rows, cols = arrays[0].shape
    parts = 2 if rows % 32 == 0 and steps == 1 else 1
    block = (1, rows // parts, cols)
    spec = [
        pl.BlockSpec(block, lambda s, p, t, k=k: (t[k * steps + s], p, 0))
        for k in range(len(arrays))
    ]
    if first is None:
        out_specs = [pl.BlockSpec(block, lambda s, p, t: (s, p, 0))]
        counts = [steps]
    else:
        out_specs = [
            pl.BlockSpec(
                block,
                lambda s, p, t: (
                    jnp.minimum(s, first - 1),
                    jnp.where(s < first, p, parts - 1),
                    0,
                ),
            ),
            pl.BlockSpec(
                block,
                lambda s, p, t: (jnp.maximum(s - first, 0), jnp.where(s < first, 0, p), 0),
            ),
        ]
        counts = [first, steps - first]
    return pl.pallas_call(
        gated(partial(add_picked_kernel, len(arrays), first), 1 + len(arrays), needs),
        grid_spec=pltpu.PrefetchScalarGridSpec(
            num_scalar_prefetch=1,
            grid=(steps, parts),
            in_specs=spec + [ANYWHERE] * len(needs),
            out_specs=out_specs,
        ),
        out_shape=[jax.ShapeDtypeStruct((n, rows, cols), BF16) for n in counts],
        name="add_picked",
        compiler_params=pltpu.CompilerParams(
            dimension_semantics=("arbitrary", "arbitrary"),
            vmem_limit_bytes=(60 if steps > 1 else 12) * MIB,
        ),
        cost_estimate=pl.CostEstimate(flops=work, bytes_accessed=1_000_000, transcendentals=0),
    )(table, *arrays, *needs)


def join_kernel(count, down_kept, down_landed, rest_kept, rest_landed, *outs):
    rows = down_kept.shape[1]
    for index in range(count):
        target = outs[1 - index % 2] if count > 1 else outs[0]
        place_now = index // 2
        target[place_now, :rows, :] = down_kept[index] + down_landed[index]
        target[place_now, rows:, :] = rest_kept[index] + rest_landed[index]


def join(kept, landed, needs=()):
    count = kept[0].shape[0]
    rows = kept[0].shape[1] + kept[1].shape[1]
    shape = jax.ShapeDtypeStruct(((count + 1) // 2, rows, kept[0].shape[2]), BF16)
    vmem = pl.BlockSpec(memory_space=pltpu.VMEM)
    outs = pl.pallas_call(
        gated(partial(join_kernel, count), 4, needs),
        in_specs=[vmem] * 4 + [ANYWHERE] * len(needs),
        out_specs=[vmem] * min(count, 2),
        out_shape=[shape] * min(count, 2),
        name="join",
        compiler_params=pltpu.CompilerParams(vmem_limit_bytes=24 * MIB),
        cost_estimate=pl.CostEstimate(flops=0, bytes_accessed=200_000, transcendentals=0),
    )(kept[0], landed[0], kept[1], landed[1], *needs)
    return outs if count > 1 else (None, outs[0])


def stack_kernel(count, *refs):
    for index in range(count):
        refs[count][index] = refs[index][...]


def home_kernel(count, meta, *refs):
    out_ref = refs[count]
    rows = refs[0].shape[0]
    for index in range(count):
        start = pl.multiple_of((meta[5] + index) % count * rows, 16)
        out_ref[pl.ds(start, rows), :] = refs[index][...].astype(out_ref.dtype)


def home_rows(meta, landed, dtype, needs=()):
    rows, cols = landed[0].shape
    vmem = pl.BlockSpec(memory_space=pltpu.VMEM)
    return pl.pallas_call(
        gated(partial(home_kernel, len(landed)), 1 + len(landed), needs),
        in_specs=[IN_SMEM] + [vmem] * len(landed) + [ANYWHERE] * len(needs),
        out_specs=vmem,
        out_shape=jax.ShapeDtypeStruct((len(landed) * rows, cols), dtype),
        name="home_rows",
        compiler_params=pltpu.CompilerParams(vmem_limit_bytes=60 * MIB),
        cost_estimate=pl.CostEstimate(flops=0, bytes_accessed=100_000, transcendentals=0),
    )(meta, *landed, *needs)


def split_kernel(in_ref, *out_refs):
    rows = out_refs[0].shape[0]
    for index, ref in enumerate(out_refs):
        ref[...] = in_ref[index * rows : (index + 1) * rows, :]


def split_rows(value, count, needs=()):
    rows = value.shape[0] // count
    vmem = pl.BlockSpec(memory_space=pltpu.VMEM)
    return pl.pallas_call(
        gated(split_kernel, 1, needs),
        in_specs=[vmem] + [ANYWHERE] * len(needs),
        out_specs=[vmem] * count,
        out_shape=[jax.ShapeDtypeStruct((rows, value.shape[1]), value.dtype)] * count,
        name="split_rows",
        compiler_params=pltpu.CompilerParams(vmem_limit_bytes=12 * MIB),
        cost_estimate=pl.CostEstimate(flops=0, bytes_accessed=100_000, transcendentals=0),
    )(value, *needs)


def stack_up(pieces, needs=()):
    vmem = pl.BlockSpec(memory_space=pltpu.VMEM)
    return pl.pallas_call(
        gated(partial(stack_kernel, len(pieces)), len(pieces), needs),
        in_specs=[vmem] * len(pieces) + [ANYWHERE] * len(needs),
        out_specs=vmem,
        out_shape=jax.ShapeDtypeStruct((len(pieces),) + pieces[0].shape, BF16),
        name="stack_up",
        compiler_params=pltpu.CompilerParams(vmem_limit_bytes=24 * MIB),
        cost_estimate=pl.CostEstimate(flops=0, bytes_accessed=100_000, transcendentals=0),
    )(*pieces, *needs)


def unpack_kernel(pack, depth, meta, mine_ref, other_ref, down_ref, up_ref, out_ref, ordered):
    core, level = meta[2], meta[4]
    rows = pack.rows // depth
    for mask in range(depth):
        start = pl.multiple_of(lax.bitwise_xor(level, mask) * rows, 16)
        ordered[core, pl.ds(start, rows), :] = mine_ref[mask]
        ordered[1 - core, pl.ds(start, rows), :] = other_ref[mask]
    turned = []
    for half in range(CORES):
        for lane in range(0, pack.model_width, pack.feed_shard):
            turned.append(ordered[half, : pack.down_rows, lane : lane + pack.feed_shard])
    down_ref[...] = jnp.transpose(jnp.concatenate(turned, axis=0)).astype(F32)
    for half in range(CORES):
        for block in range(pack.blocks):
            lane = (half * pack.blocks + block) * pack.model_width
            start = pack.up_at + block * pack.row_shard
            up_ref[:, lane : lane + pack.model_width] = ordered[
                half, start : start + pack.row_shard, :
            ].astype(F32)
        out_ref[half * pack.out_rows : (half + 1) * pack.out_rows, :] = ordered[
            half, pack.out_at : pack.out_at + pack.out_rows, :
        ].astype(F32)


def unpack(pack, depth, meta, mine, other):
    vmem = pl.BlockSpec(memory_space=pltpu.VMEM)
    return pl.pallas_call(
        partial(unpack_kernel, pack, depth),
        in_specs=[IN_SMEM, vmem, vmem],
        out_specs=[vmem] * 3,
        out_shape=[
            jax.ShapeDtypeStruct((pack.feed_shard, pack.model_width), F32),
            jax.ShapeDtypeStruct((pack.row_shard, pack.feed_width), F32),
            jax.ShapeDtypeStruct((pack.row_shard, pack.model_width), F32),
        ],
        scratch_shapes=[pltpu.VMEM((CORES, pack.rows, pack.model_width), BF16)],
        name="unpack",
        compiler_params=pltpu.CompilerParams(vmem_limit_bytes=60 * MIB),
        cost_estimate=pl.CostEstimate(flops=0, bytes_accessed=10_000_000, transcendentals=0),
    )(meta, mine, other)


def unpack_qkv_kernel(meta, mine_ref, other_ref, grad_ref, bias_ref, small_ref):
    member = meta[3]
    row_shard, width = grad_ref.shape[0], grad_ref.shape[1] // 3
    part = mine_ref.shape[1] // 3
    for ref, at in ((mine_ref, member), (other_ref, 1 - member)):
        for kind in range(3):
            lane = pl.multiple_of(kind * width + at * part, CLUSTER_ROWS)
            from_lanes = slice(kind * part, (kind + 1) * part)
            grad_ref[:, pl.ds(lane, part)] = ref[:row_shard, from_lanes].astype(F32)
            lane = pl.multiple_of(at * part, CLUSTER_ROWS)
            bias_ref[kind : kind + 1, pl.ds(lane, part)] = ref[row_shard:, from_lanes].astype(F32)[
                BIAS_ROW : BIAS_ROW + 1
            ]
    small_ref[...] = (mine_ref[row_shard:, :].astype(F32) + other_ref[row_shard:, :].astype(F32))[
        :BIAS_ROW
    ]


def unpack_qkv(meta, mine, other, row_shard, needs=()):
    cols = mine.shape[1]
    vmem = pl.BlockSpec(memory_space=pltpu.VMEM)
    return pl.pallas_call(
        gated(unpack_qkv_kernel, 3, needs),
        in_specs=[IN_SMEM, vmem, vmem] + [ANYWHERE] * len(needs),
        out_specs=[vmem] * 3,
        out_shape=[
            jax.ShapeDtypeStruct((row_shard, CORES * cols), F32),
            jax.ShapeDtypeStruct((3, CORES * cols // 3), F32),
            jax.ShapeDtypeStruct((BIAS_ROW, cols), F32),
        ],
        name="unpack_qkv",
        compiler_params=pltpu.CompilerParams(vmem_limit_bytes=60 * MIB),
        cost_estimate=pl.CostEstimate(flops=0, bytes_accessed=200_000, transcendentals=0),
    )(meta, mine, other, *needs)


def tie(*values):
    return lax.optimization_barrier(values)


def body(
    tokens,
    cotangent,
    perms,
    unit_kind,
    w_qkv,
    bias_qv,
    w_out,
    bias_out,
    ln_gain,
    ln_bias,
    w_up,
    bias_up,
    w_down,
    bias_down,
):
    shards = lax.axis_size("fsdp")
    groups = lax.axis_size("dp")
    here = lax.axis_index("fsdp")
    dp_index = lax.axis_index("dp")
    core = dp_index % CORES
    level = dp_index // CORES
    depth = groups // CORES
    units, rounds, unit_len = perms.shape
    per_device = unit_len // shards
    model_width = tokens.shape[1]
    feed_width = w_up.shape[1]
    row_shard = model_width // shards
    members = shards // units
    member_rows = unit_len // members
    head_cols = model_width // members
    padded = -(-head_cols // CLUSTER_ROWS) * CLUSTER_ROWS
    spot = here * CORES + core
    home_core = spot // shards
    unit = (spot // members) % units
    member = spot % members
    pack = Pack(model_width, feed_width, shards, units, depth)
    bits = [1 << k for k in range(shards.bit_length() - 1)]
    bit_orders = (bits, bits[::-1])

    def plane_pairs(target):
        pairs = []
        for z in range(depth):
            for f_index in range(shards):
                for c_index in range(CORES):
                    f_new, c_new = target(f_index, c_index)
                    pairs.append(
                        (
                            (z * CORES + c_index) * shards + f_index,
                            (z * CORES + c_new) * shards + f_new,
                        )
                    )
        return pairs

    def send(value, pairs):
        return lax.ppermute(value, ("dp", "fsdp"), pairs)

    def cross(value, mask):
        return send(value, plane_pairs(lambda f, c: divmod((f * CORES + c) ^ mask, CORES)))

    def trade(value, stage):
        return send(value, plane_pairs(lambda f, c: (f ^ bit_orders[c][stage], c)))

    def trade_mask(index, which):
        mask = 0
        for stage in range(len(bits)):
            if index >> stage & 1:
                mask ^= bit_orders[which][stage]
        return mask

    def climb(value, mask):
        plane = CORES * shards
        pairs = []
        for z in range(depth):
            for rest in range(plane):
                pairs.append((z * plane + rest, (z ^ mask) * plane + rest))
        return send(value, pairs)

    def outward(step):
        def target(f, c):
            place_now = (c * units + (f % units + step) % units) * members + f // units
            return divmod(place_now, CORES)

        return plane_pairs(target)

    def homeward(step):
        return [(b, a) for a, b in outward(step)]

    def bring_start(value):
        blocks = value.reshape(units, per_device, model_width)
        return [
            lax.dynamic_index_in_dim(blocks, (here % units + step) % units, axis=0, keepdims=False)
            for step in range(units)
        ]

    def bring(chosen):
        return jnp.concatenate(
            [send(chosen[step], outward(step)) for step in range(units)], axis=0
        )

    def send_home(blocks):
        return [send(blocks[step], homeward(step)) for step in range(units)]

    x_chosen = bring_start(tokens)
    x_own = bring(x_chosen)
    small = jnp.concatenate(
        [
            bias_qv.reshape(-1),
            bias_out,
            ln_gain.reshape(-1),
            ln_bias.reshape(-1),
            bias_up,
            bias_down,
        ]
    )
    small_rows = -(-small.shape[0] // (3 * padded))
    small_block = jnp.pad(
        jnp.pad(small, (0, small_rows * 3 * padded - small.shape[0])).reshape(
            small_rows, 3 * padded
        ),
        ((0, 16 - small_rows), (0, 0)),
    )
    def columns_for(offset):
        start = lax.bitwise_xor(member, offset) * head_cols
        blocks = [
            jnp.pad(
                lax.dynamic_slice(
                    w_qkv, (0, kind * model_width + start), (row_shard, head_cols)
                ),
                ((0, 0), (0, padded - head_cols)),
            )
            for kind in range(3)
        ]
        return jnp.concatenate([jnp.concatenate(blocks, axis=1), small_block], axis=0)

    offsets = [(CORES * m) % members for m in range(shards)]
    kinds = sorted(set(offsets))
    order_pack = jnp.concatenate(
        [perms.reshape(-1), jnp.broadcast_to(unit_kind[:, None], (units, 128)).reshape(-1)]
    )
    order_other = cross(order_pack, 1)
    *tied, order_other = tie(*[columns_for(offset) for offset in kinds], order_other)
    piece_kinds = dict(zip(kinds, tied))
    x_pieces = [x_own] + [cross(x_own, mask) for mask in range(1, members)]
    if members == CORES:
        qkv_pieces = {0: piece_kinds[0]}
        for stage in range(len(bits)):
            qkv_pieces[1 << stage] = trade(piece_kinds[0], stage)
        for stage in range(1, len(bits)):
            for index in range(1, 1 << stage):
                qkv_pieces[index | 1 << stage] = trade(qkv_pieces[index], stage)
        qkv_pieces = [qkv_pieces[index] for index in range(shards)]
        qkv_masks = [[trade_mask(index, which) for index in range(shards)] for which in (0, 1)]
    else:
        qkv_pieces = [piece_kinds[0]] + [
            cross(piece_kinds[offsets[m]], CORES * m) for m in range(1, shards)
        ]
        qkv_masks = [list(range(shards))] * 2
    order_pack = jnp.where(home_core == core, order_pack, order_other)
    order_count = units * rounds * unit_len
    unit_perm = lax.dynamic_index_in_dim(
        order_pack[:order_count].reshape(units, rounds * unit_len), unit, 0, keepdims=False
    )
    kind_now = lax.dynamic_index_in_dim(
        order_pack[order_count:].reshape(units, 128), unit, 0, keepdims=False
    )[0]
    owner = unit_perm // per_device
    order = (
        lax.bitwise_xor(owner // units, member) * units + (unit - owner % units) % units
    ) * per_device + unit_perm % per_device
    order = order.reshape(rounds, unit_len)
    order = jnp.where(core == 0, order, order[::-1])
    order_row = order.reshape(1, rounds * unit_len)
    order = order.reshape(-1, CLUSTER_ROWS)
    x_here = arrange(order, x_pieces, unit_len, 0)
    x_now = [x_here, cross(x_here, 1)]
    own_masks = [
        jnp.where(core == 0, trade_mask(i, 0), trade_mask(i, 1)) for i in range(1, shards)
    ]
    other_masks = [
        jnp.where(core == 0, trade_mask(i, 1), trade_mask(i, 0)) for i in range(1, shards)
    ]
    zero = jnp.int32(0)
    meta = jnp.stack(
        [kind_now, here, core, member, level, here % units, zero, zero]
        + own_masks
        + other_masks
        + [jnp.where(core == 0, first, second) for first, second in zip(*qkv_masks)]
    ).astype(jnp.int32)

    def half_of(value, axis, length, at):
        return lax.dynamic_slice_in_dim(value, at * length, length, axis=axis)

    packed = jnp.concatenate(
        [half_of(w_down, 0, pack.down_rows, core)]
        + [
            half_of(w_up, 1, model_width, core * pack.blocks + block)
            for block in range(pack.blocks)
        ]
        + [half_of(w_out, 0, pack.out_rows, core)],
        axis=0,
    )
    order_rows = unit_len // CLUSTER_ROWS
    arranged, probs, mixtures, x_turned = [], [], [], []
    *tied, packed, x_now[0] = tie(*qkv_pieces[1:], packed, x_now[0])
    qkv_pieces = qkv_pieces[:1] + tied
    smalls = jnp.stack(
        [
            piece[row_shard : row_shard + small_rows].reshape(-1)[: small.shape[0]]
            for piece in qkv_pieces
        ]
    )
    spots_of = [[masks.index(mask) for mask in range(shards)] for masks in qkv_masks]
    spots_of = jnp.where(core == 0, jnp.array(spots_of[0]), jnp.array(spots_of[1]))
    spots_of = jnp.take(spots_of, lax.bitwise_xor(here, jnp.arange(shards)))
    smalls = jnp.take(smalls, spots_of, axis=0).astype(F32)

    def vectors_at(start, count, length):
        part = smalls[:, start * row_shard : start * row_shard + count * length]
        return (
            part.reshape(shards, count, length).transpose(1, 0, 2).reshape(count, shards * length)
        )

    my_bias = lax.dynamic_index_in_dim(
        vectors_at(0, 2, row_shard).reshape(2, members, head_cols), member, 1, keepdims=False
    )
    my_bias = jnp.pad(my_bias, ((0, 0), (0, padded - head_cols)))
    my_bias = jnp.stack([my_bias[0], jnp.zeros_like(my_bias[0]), my_bias[1]]).reshape(1, -1)
    up_bias = vectors_at(7, 1, feed_width // shards)
    down_bias = smalls[:, small.shape[0] - row_shard :].reshape(1, model_width)
    vectors = jnp.concatenate(
        [vectors_at(2, 5, row_shard), down_bias, jnp.zeros((2, model_width), F32)], axis=0
    )

    weight_pieces = {0: packed}
    for stage in range(len(bits)):
        weight_pieces[1 << stage] = trade(packed, stage)
    for index in range(rounds):
        results = attend(meta, x_now[index], my_bias, qkv_pieces, row_shard, mixtures[-1:])
        for kept, result in zip((arranged, probs, mixtures, x_turned), results):
            kept.append(result)
    cot_now, mixtures[0] = tie(cotangent, mixtures[0])
    cot_landed = [
        send(value, outward(step)) for step, value in enumerate(bring_start(cot_now))
    ]
    cot_own = jnp.concatenate(cot_landed, axis=0)
    for stage in range(1, len(bits)):
        for index in range(1, 1 << stage):
            weight_pieces[index | 1 << stage] = trade(weight_pieces[index], stage)
    att_there, att_sent = [], []
    for mask in range(1, members):
        there = place(
            order_row, mixtures, mask * member_rows, member_rows, 0.5, needs=cot_landed
        )
        att_sent.append(there)
        att_there.append(cross(there[:, :head_cols], mask))
    att_here = place(order_row, mixtures, 0, member_rows, 0.5, needs=att_sent)

    direct = [weight_pieces[index] for index in range(1, shards)]
    swapped = [cross(piece, 1) for piece in direct[:-1]]
    last_piece, att_here = tie(direct[-1], att_here)
    swapped.append(cross(last_piece, 1))
    att_raw = [att_here[:, :head_cols]] + att_there
    if head_cols % CLUSTER_ROWS:
        att_raw = [jnp.concatenate(att_raw, axis=1)]
    block_out, first_low, d_branch, d_ffn, hidden, d_pre, att_turned, *rest = feed(
        pack,
        meta,
        x_own,
        cot_own,
        vectors,
        up_bias,
        att_raw,
        [w_out, w_up, w_down],
        direct + swapped,
    )
    d_att, (row_sums, up_sums) = rest[: len(att_raw)], rest[len(att_raw) :]
    if head_cols % CLUSTER_ROWS:
        d_att = [d_att[0][:, mask * head_cols : (mask + 1) * head_cols] for mask in range(members)]
    d_att = [d_att[0]] + [cross(d_att[mask], mask) for mask in range(1, members)]
    d_att = [jnp.pad(piece, ((0, 0), (0, padded - head_cols))) for piece in d_att]

    table = jnp.stack([core, member]).astype(jnp.int32)
    sending = [index for index in range(shards) if index & 1]
    keeping = [index for index in range(shards) if not index & 1]
    slots = jnp.stack(
        [
            lax.bitwise_xor(here, jnp.where(core == 0, trade_mask(i, 0), trade_mask(i, 1)))
            for i in sending + keeping
        ]
    )
    slots = jnp.concatenate([slots, slots]).astype(jnp.int32)

    def pair_sum(mine, theirs, needs):
        return add_picked(
            slots, [mine, cross(theirs, 1)], shards, len(sending), needs, 20_000_000_000
        )

    theirs_down, mine_down = down_grads(pack, table, d_ffn, hidden)
    theirs_rest, mine_rest = rest_grads(
        pack, table, first_low, d_pre, att_turned, d_branch, [theirs_down]
    )
    down_going, down_kept = pair_sum(mine_down, theirs_down, [theirs_rest])
    rest_going, rest_kept = pair_sum(mine_rest, theirs_rest, [down_going] + d_att[1:])

    def merge(kept, landed, *needs):
        count = kept.shape[0]
        if count == 1:
            table = jnp.zeros((2,), jnp.int32)
            return None, add_picked(table, [kept, landed], 1, None, needs)[0]
        order_now = [i for i in range(count) if i & 1] + [i for i in range(count) if not i & 1]
        table = jnp.array(order_now * 2, jnp.int32)
        return add_picked(table, [kept, landed], count, count // 2, needs)

    grads, d_x = [None] * rounds, [None] * rounds
    needs = [rest_going]
    blocks = unit_len // POS_BLOCK
    spans = [(index, (0, blocks)) for index in reversed(range(rounds))]
    for turn, (index, span) in enumerate(spans):
        grads[index], d_x[index], token = attend_back(
            meta,
            order,
            arranged[index],
            probs[index],
            d_att,
            qkv_pieces,
            row_shard,
            index * order_rows,
            needs,
            span,
            [],
        )
        if turn == 0:
            d_x_there = cross(d_x[index], 1)
            going, kept = join(
                [down_kept, rest_kept], [trade(down_going, 0), trade(rest_going, 0)], [token]
            )
            output_landed = send_home(split_rows(block_out, units, [token]))
            needs = [kept]
    for stage in range(1, len(bits)):
        going, kept = merge(kept, trade(going, stage), token)

    def level_pieces(block):
        return block.reshape((depth, block.shape[0] // depth) + block.shape[1:])

    def level_scatter(cut):
        return [
            climb(
                lax.dynamic_index_in_dim(cut, lax.bitwise_xor(level, mask), 0, keepdims=False), mask
            )
            for mask in range(1, depth)
        ]

    def level_gather(piece):
        pieces = {0: piece}
        mask = depth // 2
        while mask:
            pieces[mask] = climb(piece, mask)
            mask //= 2
        return pieces

    def level_forward(pieces):
        for index in sorted(range(depth), key=lambda value: value.bit_count()):
            if index not in pieces:
                low = index & -index
                pieces[index] = climb(pieces[index ^ low], low)
        return [pieces[index] for index in range(depth)]

    def by_shard(value):
        count, length = value.shape
        return (
            value.reshape(count, shards, length // shards)
            .transpose(1, 0, 2)
            .reshape(shards, count * length // shards)
        )

    small_grad = jnp.concatenate(
        [by_shard(row_sums[:5]), by_shard(up_sums), by_shard(row_sums[5:6])], axis=1
    )
    small_length = small_grad.shape[1]
    small_lanes = 3 * head_cols
    small_grad = jnp.pad(small_grad, ((0, 0), (0, BIAS_ROW * small_lanes - small_length)))
    small_grad = jnp.pad(
        small_grad.reshape(shards, BIAS_ROW, small_lanes), ((0, 0), (0, 16 - BIAS_ROW), (0, 0))
    )
    extra_rows = 16
    if padded == head_cols:
        joined = qkv_grads(
            x_turned, grads, small_grad, row_shard, output_landed + [kept]
        )
    else:
        qkv_grad = dot(x_turned[0], grads[0]) + dot(x_turned[1], grads[1])
        qkv_grad = qkv_grad.reshape(shards, row_shard, 3, padded)[..., :head_cols]
        bias_sum = sum(jnp.sum(value.astype(F32), axis=0) for value in grads)
        bias_sum = bias_sum.reshape(3, padded)[:, :head_cols].reshape(small_lanes)
        small_grad = small_grad.at[:, BIAS_ROW].set(bias_sum[None])
        joined = jnp.concatenate(
            [qkv_grad.reshape(shards, row_shard, small_lanes), small_grad], axis=1
        ).astype(BF16)
    cut = level_pieces(kept[0])
    landed = level_scatter(cut)
    classes = max(1, members // CORES)
    d_x_parts = [d_x[0], d_x_there]
    order_mine = order_row[:, :unit_len]
    if classes == 1:
        slots_held = jnp.stack(
            [
                lax.bitwise_xor(here, jnp.where(core == 0, trade_mask(i, 0), trade_mask(i, 1)))
                for i in range(shards)
            ]
        )
        held = jnp.stack(
            [
                lax.dynamic_index_in_dim(joined, slots_held[i], 0, keepdims=False)
                for i in range(0, shards, 2)
            ]
        )
        leaving = jnp.stack(
            [
                lax.dynamic_index_in_dim(joined, slots_held[i], 0, keepdims=False)
                for i in range(1, shards, 2)
            ]
        )
        totals = None
    else:
        totals = [None] * classes
        for m in range(shards):
            offset = offsets[m] // CORES
            piece = lax.dynamic_index_in_dim(joined, lax.bitwise_xor(here, m), 0, keepdims=False)
            piece = (piece if m == 0 else cross(piece, CORES * m)).astype(F32)
            totals[offset] = piece if totals[offset] is None else totals[offset] + piece

    d_there = [
        place(
            order_mine,
            d_x_parts,
            mask * member_rows,
            member_rows,
            added=True,
            needs=[joined],
        )
        for mask in range(1, members)
    ]
    if depth > 1:
        picks = jnp.concatenate([level[None], jnp.zeros((depth - 1,), level.dtype)])
        (kept,) = add_picked(
            picks.astype(jnp.int32),
            [cut] + [piece[None] for piece in landed],
            1,
            None,
            d_there,
        )
    gathered = level_gather(kept[0]) if depth > 1 else {0: cut[0]}
    early = [kept] + d_there
    if totals is None:
        leaving, held = merge(held, trade(leaving, 0), *d_there)
        early.append(held)
    d_here = place(
        order_mine,
        d_x_parts,
        0,
        member_rows,
        1.0,
        F32,
        d_branch,
        added=True,
        needs=early,
    )
    d_inputs = d_here
    for mask, there in enumerate(d_there, 1):
        d_inputs = d_inputs + cross(there, mask).astype(F32)
    d_inputs = d_inputs.astype(BF16)
    home = send_home(d_inputs.reshape(units, per_device, model_width))
    last = d_inputs
    if totals is None:
        for stage in range(1, len(bits)):
            leaving, held = merge(held, trade(leaving, stage), d_inputs)
        masks = [mask for mask in gathered if mask]
        *tied, held = tie(*[gathered[mask] for mask in masks], held)
        gathered.update(zip(masks, tied))
        last = held
        totals = [held[0]]
    output = home_rows(meta, output_landed, BF16, [last])
    totals = jnp.concatenate(totals, axis=0).astype(BF16)
    rows_each = row_shard + extra_rows
    if depth > 1:
        halves = totals.reshape((2, totals.shape[0] // 2) + totals.shape[1:])
        side = level % 2
        mine = lax.dynamic_index_in_dim(halves, side, 0, keepdims=False)
        theirs = lax.dynamic_index_in_dim(halves, 1 - side, 0, keepdims=False)
        half = (mine.astype(F32) + climb(theirs, 1).astype(F32)).astype(BF16)
        mask = 2
        while mask < depth:
            half = (half.astype(F32) + climb(half, mask).astype(F32)).astype(BF16)
            mask *= 2
        *home, half = tie(*home, half)
        other_half = climb(half, 1)
        totals = jnp.concatenate(
            [
                jnp.where(side == 0, half, other_half),
                jnp.where(side == 0, other_half, half),
            ],
            axis=0,
        )
    d_inputs = home_rows(meta, home, F32)
    stacked = stack_up(level_forward(gathered))
    grad_down, grad_up, grad_out = unpack(pack, depth, meta, stacked, cross(stacked, 1))
    if padded == head_cols and members == CORES:
        grad_qkv, bias_out_row, smalls_out = unpack_qkv(
            meta, totals, cross(totals, 1), row_shard, [grad_down, d_inputs, output]
        )
        smalls_out = smalls_out.reshape(-1)[:small_length]
        bias_out_row = lax.dynamic_slice(bias_out_row, (0, here * row_shard), (3, row_shard))
    else:
        landed = jnp.stack([totals, cross(totals, 1)], axis=0).reshape(
            CORES, classes, rows_each, 3 * head_cols
        )
        smalls_out = jnp.sum(
            landed[:, :, row_shard : row_shard + BIAS_ROW].astype(F32), axis=(0, 1)
        ).reshape(-1)[:small_length]
        landed = (
            landed.transpose(1, 0, 2, 3)
            .reshape(members, rows_each, 3, head_cols)[:, : row_shard + BIAS_ROW + 1]
        )
        if members == 2:
            swap = member == 1
            landed = jnp.stack(
                [
                    jnp.where(swap, landed[1], landed[0]),
                    jnp.where(swap, landed[0], landed[1]),
                ]
            )
        else:
            landed = jnp.take(landed, lax.bitwise_xor(member, jnp.arange(members)), axis=0)
        grad_qkv = landed[:, :row_shard].transpose(1, 2, 0, 3)
        grad_qkv = grad_qkv.reshape(row_shard, 3 * model_width).astype(F32)
        bias_out_row = landed[:, row_shard + BIAS_ROW].astype(F32).transpose(1, 0, 2)
        bias_out_row = lax.dynamic_slice(
            bias_out_row.reshape(3, model_width), (0, here * row_shard), (3, row_shard)
        )

    feed_shard = feed_width // shards
    spots = [0, row_shard, 3 * row_shard, 5 * row_shard]
    return (
        output,
        d_inputs,
        grad_qkv,
        bias_out_row[::2],
        grad_out,
        smalls_out[spots[0] : spots[1]],
        smalls_out[spots[1] : spots[2]].reshape(2, row_shard),
        smalls_out[spots[2] : spots[3]].reshape(2, row_shard),
        grad_up,
        smalls_out[spots[3] : spots[3] + feed_shard],
        grad_down,
        smalls_out[spots[3] + feed_shard :],
    )


def solution(mesh):
    placed = (
        P(("dp", "fsdp"), None),
        P(("dp", "fsdp"), None),
        P("dp", None, None),
        P("dp"),
        P("fsdp", None),
        P(None, "fsdp"),
        P("fsdp", None),
        P("fsdp"),
        P(None, "fsdp"),
        P(None, "fsdp"),
        P("fsdp", None),
        P("fsdp"),
        P("fsdp", None),
        P("fsdp"),
    )
    return jax.shard_map(
        body,
        mesh=mesh,
        in_specs=placed,
        out_specs=(
            P(("dp", "fsdp"), None),
            P(("dp", "fsdp"), None),
            P("fsdp", None),
            P(None, "fsdp"),
            P("fsdp", None),
            P("fsdp"),
            P(None, "fsdp"),
            P(None, "fsdp"),
            P("fsdp", None),
            P("fsdp"),
            P("fsdp", None),
            P("fsdp"),
        ),
        check_vma=False,
    )
```

```python
from functools import partial

import jax
import jax.numpy as jnp
from jax import lax
from jax.experimental import pallas as pl
from jax.experimental.pallas import tpu as pltpu
from jax.sharding import PartitionSpec as P

HEAD_DIM = 64
CORES = 2
NEG_FILL = -1000000000.0
EPSILON = 1e-05
SCALE = HEAD_DIM ** (-0.5)
BIAS_ROW = 2
GRAD_LANES = 384
CLUSTER_ROWS = 128
HALF_ROWS = 64
POS_BLOCK = 512
TOKEN_BLOCK = 512
ROW_BLOCK = 256
FF_BLOCK = 512
MIB = 1024 * 1024
NT = (((1,), (1,)), ((), ()))
TN = (((0,), (0,)), ((), ()))
F32 = jnp.float32
BF16 = jnp.bfloat16
ANYWHERE = pl.BlockSpec(memory_space=pl.ANY)
IN_SMEM = pl.BlockSpec(memory_space=pltpu.SMEM)


def whole(shape):
    return pl.BlockSpec(shape, lambda i: (0,) * len(shape))


def rows_of(shape):
    return pl.BlockSpec(shape, lambda i: (i,) + (0,) * (len(shape) - 1))


def dot(a, b, dims=(((1,), (0,)), ((), ()))):
    return lax.dot_general(a, b, dims, preferred_element_type=F32)


def params(mib, flops=0, moved=0, share=16):
    return dict(
        compiler_params=pltpu.CompilerParams(
            dimension_semantics=("arbitrary",),
            vmem_limit_bytes=mib * MIB,
        ),
        cost_estimate=pl.CostEstimate(
            flops=flops // share, bytes_accessed=moved // share, transcendentals=0
        ),
    )


def gated(kernel, used, needs):
    if not needs:
        return kernel

    def run(*refs):
        return kernel(*refs[:used], *refs[used + len(needs) :])

    return run


def lane_masks():
    lane = lax.broadcasted_iota(jnp.int32, (CLUSTER_ROWS, CLUSTER_ROWS), 1)
    low = (lane < HEAD_DIM).astype(F32)
    return low.astype(BF16), (1.0 - low).astype(BF16), lane < HEAD_DIM


def corners(first, second):
    blank = jnp.zeros_like(first)
    return jnp.concatenate(
        [
            jnp.concatenate([first, blank], axis=1),
            jnp.concatenate([blank, second], axis=1),
        ],
        axis=0,
    )


def both_heads(rows_now, low, high):
    return jnp.concatenate([rows_now * low, rows_now * high], axis=0)


def equal_ones(left, right):
    return jnp.where(left == right, jnp.ones((), BF16), jnp.zeros((), BF16))


def pick_rows(order_ref, first_row, unit_len):
    parts = []
    lane = lax.broadcasted_iota(jnp.int16, (CLUSTER_ROWS, CLUSTER_ROWS), 1)
    for part in range(POS_BLOCK // CLUSTER_ROWS):
        row = order_ref[pl.ds(first_row + part, 1), :]
        column = jnp.transpose(jnp.broadcast_to(row, (CLUSTER_ROWS, CLUSTER_ROWS)))
        column = column.astype(jnp.int16)
        pieces = [
            equal_ones(column, lane + jnp.int16(base)) for base in range(0, unit_len, CLUSTER_ROWS)
        ]
        parts.append(jnp.concatenate(pieces, axis=1))
    return jnp.concatenate(parts, axis=0)


def load_pieces(meta, x_refs, w_refs, x_all, w_all, sems, row_shard):
    member_rows = x_all.shape[0] // max(1, len(x_refs))
    copies = []
    for index, ref in enumerate(x_refs):
        copies.append(
            pltpu.make_async_copy(
                ref, x_all.at[pl.ds(index * member_rows, member_rows), :], sems.at[index]
            )
        )
    for index, ref in enumerate(w_refs):
        mask = meta[meta.shape[0] - len(w_refs) + index]
        start = pl.multiple_of(lax.bitwise_xor(meta[1], mask) * row_shard, 16)
        copies.append(
            pltpu.make_async_copy(
                ref.at[pl.ds(0, row_shard), :],
                w_all.at[pl.ds(start, row_shard), :],
                sems.at[len(x_refs) + index],
            )
        )
    for copy in copies:
        copy.start()
    for copy in copies:
        copy.wait()


def arrange_kernel(unit_len, first_row, order_ref, *refs):
    x_refs, out_ref = refs[:-1], refs[-1]
    step = pl.program_id(0)
    picks = pick_rows(order_ref, first_row + step * (POS_BLOCK // CLUSTER_ROWS), unit_len)
    rows = x_refs[0].shape[0]
    total = None
    for index, ref in enumerate(x_refs):
        term = dot(picks[:, index * rows : (index + 1) * rows], ref[...])
        total = term if total is None else total + term
    out_ref[...] = total.astype(BF16)


def arrange(order, x_pieces, position_count, first_row):
    member_rows, width = x_pieces[0].shape
    unit_len = member_rows * len(x_pieces)
    return pl.pallas_call(
        partial(arrange_kernel, unit_len, first_row),
        grid=(position_count // POS_BLOCK,),
        in_specs=[whole(order.shape)] + [whole(piece.shape) for piece in x_pieces],
        out_specs=rows_of((POS_BLOCK, width)),
        out_shape=jax.ShapeDtypeStruct((position_count, width), BF16),
        name="arrange",
        **params(20, 2 * position_count * unit_len * width, 6_000_000),
    )(order, *x_pieces)


def attend_kernel(sizes, meta, x_now_ref, bias_ref, *refs):
    shards, row_shard = sizes
    w_refs, refs = refs[:shards], refs[shards:]
    arranged_ref, probs_ref, mixture_ref, turned_ref, w_all, sems = refs
    width = w_all.shape[1] // 3
    step = pl.program_id(0)

    @pl.when(step == 0)
    def _():
        load_pieces(meta, [], w_refs, w_all, w_all, sems, row_shard)

    x_now = x_now_ref[...]
    turned_ref[...] = jnp.transpose(x_now)
    arranged = (dot(x_now, w_all[...]) + bias_ref[...]).astype(BF16)
    arranged_ref[...] = arranged
    low, high, lane_low = lane_masks()
    position = lax.broadcasted_iota(jnp.int32, (CLUSTER_ROWS, CLUSTER_ROWS), 0)
    other = lax.broadcasted_iota(jnp.int32, (CLUSTER_ROWS, CLUSTER_ROWS), 1)
    same_half = (position < HALF_ROWS) == (other < HALF_ROWS)
    allowed = jnp.logical_or(same_half, meta[0] == 1)
    pairs = width // CLUSTER_ROWS
    units = [(part, pair) for part in range(POS_BLOCK // CLUSTER_ROWS) for pair in range(pairs)]
    for index in range(0, len(units), 2):
        queries, keys, values = [], [], []
        for part, pair in units[index : index + 2]:
            rows_now = slice(part * CLUSTER_ROWS, (part + 1) * CLUSTER_ROWS)
            base = pair * CLUSTER_ROWS
            queries.append(arranged[rows_now, base : base + CLUSTER_ROWS] * SCALE)
            one_key = arranged[rows_now, width + base : width + base + CLUSTER_ROWS]
            keys.append(both_heads(one_key, low, high))
            one_value = arranged[rows_now, 2 * width + base : 2 * width + base + CLUSTER_ROWS]
            values.append(both_heads(one_value, low, high))
        both_scores = dot(jnp.concatenate(keys, axis=1), corners(*queries), NT)
        for which, (part, pair) in enumerate(units[index : index + 2]):
            halves = []
            for head in range(2):
                one = both_scores[
                    head * CLUSTER_ROWS : (head + 1) * CLUSTER_ROWS,
                    which * CLUSTER_ROWS : (which + 1) * CLUSTER_ROWS,
                ]
                one = jnp.where(allowed, one, NEG_FILL)
                grown = jnp.exp(one - jnp.max(one, axis=0, keepdims=True))
                halves.append(grown * (1.0 / jnp.sum(grown, axis=0, keepdims=True)))
            probs = jnp.concatenate(halves, axis=0).astype(BF16)
            at = (part * pairs + pair) * 2 * CLUSTER_ROWS
            probs_ref[at : at + 2 * CLUSTER_ROWS, :] = probs
            mixture_ref[
                part * CLUSTER_ROWS : (part + 1) * CLUSTER_ROWS,
                pair * CLUSTER_ROWS : (pair + 1) * CLUSTER_ROWS,
            ] = dot(probs, values[which], TN).astype(BF16)


def attend(meta, x_now, bias, w_pieces, row_shard, needs=()):
    shards = len(w_pieces)
    position_count, model_width = x_now.shape
    cols = w_pieces[0].shape[1]
    width = cols // 3
    pair_rows = 2 * width
    return pl.pallas_call(
        gated(partial(attend_kernel, (shards, row_shard)), 3 + shards, needs),
        grid=(position_count // POS_BLOCK,),
        in_specs=[IN_SMEM, rows_of((POS_BLOCK, model_width)), whole(bias.shape)]
        + [ANYWHERE] * (shards + len(needs)),
        out_specs=[
            rows_of((POS_BLOCK, cols)),
            rows_of((POS_BLOCK // CLUSTER_ROWS * pair_rows, CLUSTER_ROWS)),
            rows_of((POS_BLOCK, width)),
            pl.BlockSpec((model_width, POS_BLOCK), lambda i: (0, i)),
        ],
        out_shape=[
            jax.ShapeDtypeStruct((position_count, cols), BF16),
            jax.ShapeDtypeStruct((position_count // CLUSTER_ROWS * pair_rows, CLUSTER_ROWS), BF16),
            jax.ShapeDtypeStruct((position_count, width), BF16),
            jax.ShapeDtypeStruct((model_width, position_count), BF16),
        ],
        scratch_shapes=[
            pltpu.VMEM((model_width, cols), BF16),
            pltpu.SemaphoreType.DMA((shards,)),
        ],
        name="attend",
        **params(
            60, 8 * position_count * (model_width * cols + 4 * CLUSTER_ROWS * width), 18_000_000, 1
        ),
    )(meta, x_now, bias, *w_pieces, *needs)


def place_kernel(sizes, scale, has_base, order_row_ref, *refs):
    unit_len, first_token, added = sizes
    base_ref = refs[0] if has_base else None
    refs = refs[1 if has_base else 0 :]
    if added:
        first_ref, second_ref, out_ref, held = refs

        @pl.when(pl.program_id(0) == 0)
        def _():
            held[...] = (first_ref[...].astype(F32) + second_ref[...].astype(F32)).astype(BF16)

        source_refs = [held]
    else:
        source_refs, out_ref = refs[:-1], refs[-1]
    block_rows = out_ref.shape[0]
    first = jnp.full((1, 1), first_token + pl.program_id(0) * block_rows, jnp.int32)
    token = lax.broadcasted_iota(jnp.int16, (block_rows, unit_len), 0)
    total = None
    for index, ref in enumerate(source_refs):
        row = order_row_ref[:, index * unit_len : (index + 1) * unit_len] - first
        row = jnp.broadcast_to(row, (16, unit_len)).astype(jnp.int16)
        row = jnp.concatenate([row] * (block_rows // 16), axis=0)
        term = dot(equal_ones(row, token), ref[...])
        total = term if total is None else total + term
    if scale != 1.0:
        total = total * scale
    if has_base:
        total = total + base_ref[...].astype(F32)
    out_ref[...] = total.astype(out_ref.dtype)


def place(
    order_row,
    sources,
    first_token,
    row_count,
    scale=1.0,
    dtype=BF16,
    base=None,
    added=False,
    needs=(),
    share=64,
):
    unit_len, width = sources[0].shape
    block_rows = min(TOKEN_BLOCK, row_count)
    extra = [] if base is None else [base]
    return pl.pallas_call(
        gated(
            partial(place_kernel, (unit_len, first_token, added), scale, base is not None),
            1 + len(extra) + len(sources),
            needs,
        ),
        grid=(row_count // block_rows,),
        in_specs=[whole(order_row.shape)]
        + [rows_of((block_rows, width))] * len(extra)
        + [whole(source.shape) for source in sources]
        + [ANYWHERE] * len(needs),
        out_specs=rows_of((block_rows, width)),
        out_shape=jax.ShapeDtypeStruct((row_count, width), dtype),
        scratch_shapes=[pltpu.VMEM((unit_len, width), BF16)] if added else [],
        name="place",
        **params(
            32 if added else 20,
            16 * row_count * unit_len * width,
            10_000_000,
            1 if added else share,
        ),
    )(order_row, *extra, *sources, *needs)


def attend_back_kernel(sizes, meta, order_ref, arranged_ref, probs_ref, *refs):
    members, shards, unit_len, row_shard, first_row, start = sizes
    g_refs, refs = refs[:members], refs[members:]
    w_refs, refs = refs[:shards], refs[shards:]
    grads_ref, d_x_ref, token_ref, g_all, w_all, sems = refs
    width = w_all.shape[1] // 3
    step = pl.program_id(0)

    @pl.when(step == 0)
    def _():
        load_pieces(meta, g_refs, w_refs, g_all, w_all, sems, row_shard)
        token_ref[...] = jnp.zeros_like(token_ref)

    at_row = first_row + (start + step) * (POS_BLOCK // CLUSTER_ROWS)
    picks = pick_rows(order_ref, at_row, unit_len)
    d_mixture = dot(picks, g_all[...]).astype(BF16)
    low, high, lane_low = lane_masks()
    pairs = width // CLUSTER_ROWS
    units = [(part, pair) for part in range(POS_BLOCK // CLUSTER_ROWS) for pair in range(pairs)]
    for index in range(0, len(units), 2):
        values, d_rows = [], []
        for part, pair in units[index : index + 2]:
            rows_now = slice(part * CLUSTER_ROWS, (part + 1) * CLUSTER_ROWS)
            base = pair * CLUSTER_ROWS
            one_value = arranged_ref[rows_now, 2 * width + base : 2 * width + base + CLUSTER_ROWS]
            values.append(both_heads(one_value, low, high))
            d_rows.append(d_mixture[rows_now, base : base + CLUSTER_ROWS])
        both_probs = dot(jnp.concatenate(values, axis=1), corners(*d_rows), NT)
        for which, (part, pair) in enumerate(units[index : index + 2]):
            rows_now = slice(part * CLUSTER_ROWS, (part + 1) * CLUSTER_ROWS)
            base = pair * CLUSTER_ROWS
            q_lanes = slice(base, base + CLUSTER_ROWS)
            k_lanes = slice(width + base, width + base + CLUSTER_ROWS)
            v_lanes = slice(2 * width + base, 2 * width + base + CLUSTER_ROWS)
            queries = arranged_ref[rows_now, q_lanes] * SCALE
            keys = arranged_ref[rows_now, k_lanes] * SCALE
            at = (part * pairs + pair) * 2 * CLUSTER_ROWS
            probs = probs_ref[at : at + 2 * CLUSTER_ROWS, :]
            d_probs = both_probs[:, which * CLUSTER_ROWS : (which + 1) * CLUSTER_ROWS]
            pieces = []
            for head in range(2):
                rows = slice(head * CLUSTER_ROWS, (head + 1) * CLUSTER_ROWS)
                weight = probs[rows].astype(F32)
                d_one = d_probs[rows]
                inner = jnp.sum(weight * d_one, axis=0, keepdims=True)
                pieces.append(weight * (d_one - inner))
            d_scores = jnp.concatenate(pieces, axis=0).astype(BF16)
            d_query = dot(d_scores, both_heads(keys, low, high), TN)
            d_pair = dot(
                jnp.concatenate([probs, d_scores], axis=1), corners(d_rows[which], queries)
            )
            d_values, d_keys = d_pair[:, :CLUSTER_ROWS], d_pair[:, CLUSTER_ROWS:]
            grads_ref[rows_now, q_lanes] = d_query.astype(BF16)
            grads_ref[rows_now, k_lanes] = jnp.where(
                lane_low, d_keys[:CLUSTER_ROWS], d_keys[CLUSTER_ROWS:]
            ).astype(BF16)
            grads_ref[rows_now, v_lanes] = jnp.where(
                lane_low, d_values[:CLUSTER_ROWS], d_values[CLUSTER_ROWS:]
            ).astype(BF16)
    grads = grads_ref[...]
    d_x_ref[...] = dot(grads, w_all[...], NT).astype(BF16)


def attend_back(
    meta, order, arranged, probs, g_pieces, w_pieces, row_shard, first_row, needs, span, into
):
    members, shards = len(g_pieces), len(w_pieces)
    member_rows, width = g_pieces[0].shape
    unit_len = members * member_rows
    position_count, cols = arranged.shape
    model_width = row_shard * shards
    start, stop = span
    pair_rows = POS_BLOCK // CLUSTER_ROWS * 2 * width
    used = 4 + members + shards

    def block(shape):
        return pl.BlockSpec(shape, lambda i: (start + i, 0))

    return pl.pallas_call(
        gated(
            partial(attend_back_kernel, (members, shards, unit_len, row_shard, first_row, start)),
            used,
            list(into) + list(needs),
        ),
        grid=(stop - start,),
        in_specs=[
            IN_SMEM,
            whole(order.shape),
            block((POS_BLOCK, cols)),
            block((pair_rows, CLUSTER_ROWS)),
        ]
        + [ANYWHERE] * (members + shards + len(into) + len(needs)),
        out_specs=[block((POS_BLOCK, cols)), block((POS_BLOCK, model_width)), whole((8, 128))],
        out_shape=[
            jax.ShapeDtypeStruct((position_count, cols), BF16),
            jax.ShapeDtypeStruct((position_count, model_width), BF16),
            jax.ShapeDtypeStruct((8, 128), F32),
        ],
        input_output_aliases={used + index: index for index in range(len(into))},
        scratch_shapes=[
            pltpu.VMEM((unit_len, width), BF16),
            pltpu.VMEM((model_width, cols), BF16),
            pltpu.SemaphoreType.DMA((members + shards,)),
        ],
        name="attend_back",
        **params(
            60,
            12 * (stop - start) * POS_BLOCK * (unit_len * width + model_width * cols),
            20_000_000,
            1,
        ),
    )(meta, order, arranged, probs, *g_pieces, *w_pieces, *into, *needs)


def normalise(summed):
    average = jnp.mean(summed, axis=-1, keepdims=True)
    centred = summed - average
    spread = jnp.mean(centred * centred, axis=-1, keepdims=True)
    scale_inv = lax.rsqrt(spread + EPSILON)
    return centred * scale_inv, scale_inv


def normalise_back(grad_out, normed, scale_inv, gain_row):
    scaled = grad_out * gain_row
    return scale_inv * (
        scaled
        - jnp.mean(scaled, axis=-1, keepdims=True)
        - normed * jnp.mean(scaled * normed, axis=-1, keepdims=True)
    )


def column_sum(rows_now):
    return jnp.sum(rows_now, axis=0, keepdims=True)


def gelu_parts(value):
    below = 0.5 + 0.5 * lax.erf(value * 0.7071067811865476)
    bell = jnp.exp(value * value * -0.5) * 0.3989422804014327
    return value * below, below + value * bell


class Pack:
    def __init__(self, model_width, feed_width, shards, units, depth):
        self.model_width, self.feed_width, self.shards = model_width, feed_width, shards
        self.row_shard = model_width // shards
        self.feed_shard = feed_width // shards
        self.down_rows = self.feed_shard // CORES
        self.blocks = feed_width // CORES // model_width
        self.up_at = self.down_rows
        self.out_at = self.up_at + self.blocks * self.row_shard
        self.out_rows = self.row_shard // CORES
        self.used = self.out_at + self.out_rows
        unit = 16 * depth
        self.rows = -(-self.used // unit) * unit
        self.rest_rows = self.rows - self.down_rows
        self.units = units
        self.group = units * self.row_shard

    def out_start(self, shard, member):
        return (
            lax.bitwise_xor(jnp.int32(shard) // self.units, member) * self.group
            + (shard % self.units) * self.row_shard
        )


def feed_kernel(pack, att_count, meta, x_ref, cot_ref, vec_ref, up_bias_ref, *refs):
    shards = pack.shards
    att_refs, refs = refs[:att_count], refs[att_count:]
    own_out, own_up, own_down = refs[:3]
    refs = refs[3:]
    pieces, refs = refs[: 2 * (shards - 1)], refs[2 * (shards - 1) :]
    out_ref, first_turned_ref, d_branch_ref, d_ffn_turned_ref, hidden_ref, d_pre_ref = refs[:6]
    att_turned_ref = refs[6]
    refs = refs[7:]
    d_att_refs, refs = refs[:att_count], refs[att_count:]
    sums_ref, up_sums_ref, w_out, w_up, w_down, slope, sems = refs
    step = pl.program_id(0)
    here, core, member = meta[1], meta[2], meta[3]
    feed_width = pack.feed_width

    def loads(kind):
        copies = []

        def add(source, target):
            copies.append(pltpu.make_async_copy(source, target, sems.at[kind, len(copies)]))

        if kind == 0:
            start = pl.multiple_of(pack.out_start(here, member), 16)
            add(own_out, w_out.at[pl.ds(start, pack.row_shard), :])
        elif kind == 1:
            start = pl.multiple_of(here * pack.row_shard, 16)
            add(own_up, w_up.at[pl.ds(start, pack.row_shard), :])
        else:
            start = pl.multiple_of(here * pack.feed_shard, 16)
            add(own_down, w_down.at[pl.ds(start, pack.feed_shard), :])
        for index, ref in enumerate(pieces):
            peer = lax.bitwise_xor(here, meta[8 + index])
            half = core if index < shards - 1 else 1 - core
            if kind == 0:
                start = pack.out_start(peer, member) + half * pack.out_rows
                start = pl.multiple_of(start, 16)
                add(
                    ref.at[pl.ds(pack.out_at, pack.out_rows), :],
                    w_out.at[pl.ds(start, pack.out_rows), :],
                )
            elif kind == 1:
                start = pl.multiple_of(peer * pack.row_shard, 16)
                for block in range(pack.blocks):
                    lane = pl.multiple_of(
                        (half * pack.blocks + block) * pack.model_width, CLUSTER_ROWS
                    )
                    add(
                        ref.at[pl.ds(pack.up_at + block * pack.row_shard, pack.row_shard), :],
                        w_up.at[pl.ds(start, pack.row_shard), pl.ds(lane, pack.model_width)],
                    )
            else:
                start = pl.multiple_of(peer * pack.feed_shard + half * pack.down_rows, 16)
                add(
                    ref.at[pl.ds(0, pack.down_rows), :],
                    w_down.at[pl.ds(start, pack.down_rows), :],
                )
        return copies

    @pl.when(step == 0)
    def _():
        for kind in range(3):
            for copy in loads(kind):
                copy.start()
        sums_ref[...] = jnp.zeros_like(sums_ref)
        up_sums_ref[...] = jnp.zeros_like(up_sums_ref)
        for copy in loads(0):
            copy.wait()

    bias_out, gain_one, gain_two = vec_ref[0:1, :], vec_ref[1:2, :], vec_ref[2:3, :]
    shift_one, shift_two, bias_down = vec_ref[3:4, :], vec_ref[4:5, :], vec_ref[5:6, :]
    att_width = att_refs[0].shape[1]
    summed = x_ref[...].astype(F32) + bias_out
    for index, ref in enumerate(att_refs):
        summed += dot(ref[...], w_out[index * att_width : (index + 1) * att_width, :])
    normed_one, inv_one = normalise(summed)
    first = normed_one * gain_one + shift_one
    first_low = first.astype(BF16)
    first_turned_ref[...] = jnp.transpose(first_low)
    for index, ref in enumerate(att_refs):
        att_turned_ref[index * att_width : (index + 1) * att_width, :] = jnp.transpose(ref[...])

    @pl.when(step == 0)
    def _():
        for kind in (1, 2):
            for copy in loads(kind):
                copy.wait()

    second = first + bias_down
    starts = list(range(0, feed_width, FF_BLOCK))

    def raised(base):
        lanes = slice(base, base + FF_BLOCK)
        return dot(first_low, w_up[:, lanes]) + up_bias_ref[:, lanes]

    pre = raised(starts[0])
    for index, base in enumerate(starts):
        lanes = slice(base, base + FF_BLOCK)
        pre_next = raised(starts[index + 1]) if index + 1 < len(starts) else None
        hidden, slope_now = gelu_parts(pre)
        hidden = hidden.astype(BF16)
        hidden_ref[:, lanes] = hidden
        slope[:, lanes] = slope_now
        second += dot(hidden, w_down[lanes, :])
        pre = pre_next
    normed_two, inv_two = normalise(second)
    out_ref[...] = (normed_two * gain_two + shift_two).astype(BF16)
    top = cot_ref[...].astype(F32)
    d_second = normalise_back(top, normed_two, inv_two, gain_two)
    d_ffn = d_second.astype(BF16)
    d_ffn_turned_ref[...] = jnp.transpose(d_ffn)
    d_first = d_second
    d_hidden = dot(d_ffn, w_down[0:FF_BLOCK, :], NT)
    for index, base in enumerate(starts):
        lanes = slice(base, base + FF_BLOCK)
        if index + 1 < len(starts):
            d_next = dot(d_ffn, w_down[starts[index + 1] : starts[index + 1] + FF_BLOCK, :], NT)
        d_pre = (d_hidden * slope[:, lanes]).astype(BF16)
        d_pre_ref[:, lanes] = d_pre
        up_sums_ref[:, lanes] += column_sum(d_pre.astype(F32))
        d_first += dot(d_pre, w_up[:, lanes], NT)
        d_hidden = d_next
    d_lower = normalise_back(d_first, normed_one, inv_one, gain_one)
    d_branch = d_lower.astype(BF16)
    d_branch_ref[...] = d_branch
    for index, ref in enumerate(d_att_refs):
        back = dot(d_branch, w_out[index * att_width : (index + 1) * att_width, :], NT)
        ref[...] = (0.5 * back).astype(BF16)
    sums_ref[0:1, :] += column_sum(d_branch.astype(F32))
    sums_ref[1:2, :] += column_sum(d_first * normed_one)
    sums_ref[2:3, :] += column_sum(top * normed_two)
    sums_ref[3:4, :] += column_sum(d_first)
    sums_ref[4:5, :] += column_sum(top)
    sums_ref[5:6, :] += column_sum(d_ffn.astype(F32))


def feed(pack, meta, x_own, cot_own, vectors, up_bias, att, own, pieces):
    row_count, model_width = x_own.shape
    feed_width = pack.feed_width
    att_width = att[0].shape[1]
    one = rows_of((ROW_BLOCK, model_width))
    wide = rows_of((ROW_BLOCK, feed_width))
    narrow = rows_of((ROW_BLOCK, att_width))
    turned = pl.BlockSpec((model_width, ROW_BLOCK), lambda i: (0, i))
    turned_shape = jax.ShapeDtypeStruct((model_width, row_count), BF16)

    def like(width):
        return jax.ShapeDtypeStruct((row_count, width), BF16)

    return pl.pallas_call(
        partial(feed_kernel, pack, len(att)),
        grid=(row_count // ROW_BLOCK,),
        in_specs=[IN_SMEM, one, one, whole(vectors.shape), whole(up_bias.shape)]
        + [narrow] * len(att)
        + [ANYWHERE] * (3 + len(pieces)),
        out_specs=[one, turned, one, turned, wide, wide, turned]
        + [narrow] * len(att)
        + [whole((8, model_width)), whole((1, feed_width))],
        out_shape=[
            like(model_width),
            turned_shape,
            like(model_width),
            turned_shape,
            like(feed_width),
            like(feed_width),
            turned_shape,
        ]
        + [like(att_width)] * len(att)
        + [
            jax.ShapeDtypeStruct((8, model_width), F32),
            jax.ShapeDtypeStruct((1, feed_width), F32),
        ],
        scratch_shapes=[
            pltpu.VMEM((model_width, model_width), BF16),
            pltpu.VMEM((model_width, feed_width), BF16),
            pltpu.VMEM((feed_width, model_width), BF16),
            pltpu.VMEM((ROW_BLOCK, feed_width), F32),
            pltpu.SemaphoreType.DMA((3, 1 + pack.blocks * len(pieces))),
        ],
        name="feed",
        **params(
            40, 2 * row_count * model_width * (2 * model_width + 4 * feed_width), 40_000_000
        ),
    )(meta, x_own, cot_own, vectors, up_bias, *att, *own, *pieces)


def down_grads_kernel(pack, table, d_ffn_ref, hidden_ref, theirs_ref, mine_ref, made, sems):
    step = pl.program_id(0)
    core = table[0]

    def stores(shard):
        return [
            pltpu.make_async_copy(made.at[1 - core, shard], theirs_ref.at[shard], sems.at[0, shard]),
            pltpu.make_async_copy(made.at[core, shard], mine_ref.at[shard], sems.at[1, shard]),
        ]

    grad = dot(d_ffn_ref[...], hidden_ref[...]).astype(BF16)
    for half in range(CORES):
        for lane in range(0, pack.model_width, pack.feed_shard):
            begin = half * (pack.model_width // CORES) + lane // pack.feed_shard * pack.down_rows
            made[half, step, :, lane : lane + pack.feed_shard] = grad[
                begin : begin + pack.down_rows
            ]
    for copy in stores(step):
        copy.start()

    @pl.when(step == pack.shards - 1)
    def _():
        for shard in range(pack.shards):
            for copy in stores(shard):
                copy.wait()


def down_grads(pack, table, d_ffn, hidden):
    model_width, row_count = d_ffn.shape
    shape = (pack.shards, pack.down_rows, model_width)
    return pl.pallas_call(
        partial(down_grads_kernel, pack),
        grid_spec=pltpu.PrefetchScalarGridSpec(
            num_scalar_prefetch=1,
            grid=(pack.shards,),
            in_specs=[
                pl.BlockSpec(d_ffn.shape, lambda step, table: (0, 0)),
                pl.BlockSpec((row_count, pack.feed_shard), lambda step, table: (0, step)),
            ],
            out_specs=[ANYWHERE] * 2,
            scratch_shapes=[
                pltpu.VMEM((CORES,) + shape, BF16),
                pltpu.SemaphoreType.DMA((CORES, pack.shards)),
            ],
        ),
        out_shape=[jax.ShapeDtypeStruct(shape, BF16)] * 2,
        name="down_grads",
        **params(60, 2 * row_count * model_width * pack.feed_width, 10_000_000),
    )(table, d_ffn, hidden)


def rest_grads_kernel(
    pack, table, first_ref, d_pre_ref, att_ref, d_branch_ref, theirs_ref, mine_ref, *scratch
):
    att, d_branch, tile, made, in_sems, sems = scratch
    step = pl.program_id(0)
    core, member = table[0], table[1]
    shards, blocks = pack.shards, pack.blocks
    out_at = pack.out_at - pack.down_rows

    loads = [
        pltpu.make_async_copy(att_ref, att, in_sems.at[0]),
        pltpu.make_async_copy(d_branch_ref, d_branch, in_sems.at[1]),
    ]

    def store(half, start, rows, sem):
        there = (slice(None), pl.ds(start, rows), slice(None))

        def copy(target):
            return pltpu.make_async_copy(
                made.at[(half,) + there], target.at[there], sems.at[half, sem]
            )

        return copy

    def both(half, start, rows, sem, act):
        copy = store(half, start, rows, sem)

        @pl.when(core == half)
        def _():
            act(copy(mine_ref))

        @pl.when(core != half)
        def _():
            act(copy(theirs_ref))

    @pl.when(step == 0)
    def _():
        for copy in loads:
            copy.start()

    @pl.when(step < CORES * blocks)
    def _():
        grad = dot(first_ref[...], d_pre_ref[...]).astype(BF16)
        start = pl.multiple_of(step % blocks * pack.row_shard, 16)
        for shard in range(shards):
            made[step // blocks, shard, pl.ds(start, pack.row_shard), :] = grad[
                shard * pack.row_shard : (shard + 1) * pack.row_shard
            ]

    for half in range(CORES):

        @pl.when(step == (half + 1) * blocks - 1)
        def _(half=half):
            both(half, 0, out_at, 0, lambda copy: copy.start())

    @pl.when(step == CORES * blocks)
    def _():
        for copy in loads:
            copy.wait()
        tile[...] = dot(att[...], d_branch[...])
        spare = pack.rows - pack.used
        for half in range(CORES):
            for shard in range(shards):
                start = pack.out_start(shard, member) + half * pack.out_rows
                start = pl.multiple_of(start, 16)
                made[half, shard, out_at : out_at + pack.out_rows, :] = tile[
                    pl.ds(start, pack.out_rows), :
                ].astype(BF16)
                if spare:
                    made[half, shard, out_at + pack.out_rows :, :] = jnp.zeros(
                        (spare, pack.model_width), BF16
                    )
            both(half, out_at, pack.rest_rows - out_at, 1, lambda copy: copy.start())
        for half in range(CORES):
            both(half, 0, out_at, 0, lambda copy: copy.wait())
            both(half, out_at, pack.rest_rows - out_at, 1, lambda copy: copy.wait())


def rest_grads(pack, table, first_low, d_pre, att, d_branch, needs=()):
    model_width, row_count = first_low.shape
    shape = (pack.shards, pack.rest_rows, model_width)
    steps = CORES * pack.blocks
    return pl.pallas_call(
        gated(partial(rest_grads_kernel, pack), 5, needs),
        grid_spec=pltpu.PrefetchScalarGridSpec(
            num_scalar_prefetch=1,
            grid=(steps + 1,),
            in_specs=[
                pl.BlockSpec(first_low.shape, lambda step, table: (0, 0)),
                pl.BlockSpec(
                    (row_count, model_width),
                    lambda step, table: (0, jnp.minimum(step, steps - 1)),
                ),
            ]
            + [ANYWHERE] * (2 + len(needs)),
            out_specs=[ANYWHERE] * 2,
            scratch_shapes=[
                pltpu.VMEM((model_width, row_count), BF16),
                pltpu.VMEM((row_count, model_width), BF16),
                pltpu.VMEM((model_width, model_width), F32),
                pltpu.VMEM((CORES,) + shape, BF16),
                pltpu.SemaphoreType.DMA((2,)),
                pltpu.SemaphoreType.DMA((CORES, 2)),
            ],
        ),
        out_shape=[jax.ShapeDtypeStruct(shape, BF16)] * 2,
        name="rest_grads",
        **params(60, 2 * row_count * model_width * (pack.feed_width + model_width), 10_000_000),
    )(table, first_low, d_pre, att, d_branch, *needs)


def qkv_grads_kernel(rounds, x_refs_then, *refs):
    refs = (x_refs_then,) + refs
    x_refs, grad_refs = refs[:rounds], refs[rounds : 2 * rounds]
    small_ref, out_ref = refs[2 * rounds :]
    shards, rows, _ = out_ref.shape
    row_shard = rows - small_ref.shape[1]
    total, sums = None, None
    for x_ref, grad_ref in zip(x_refs, grad_refs):
        grads = grad_ref[...]
        term = dot(x_ref[...], grads)
        down = column_sum(grads.astype(F32))
        total = term if total is None else total + term
        sums = down if sums is None else sums + down
    total = total.astype(BF16)
    row = lax.broadcasted_iota(jnp.int32, small_ref.shape[1:], 0)
    for shard in range(shards):
        out_ref[shard, :row_shard, :] = total[shard * row_shard : (shard + 1) * row_shard]
        last = jnp.where(row == BIAS_ROW, sums, small_ref[shard])
        out_ref[shard, row_shard:, :] = last.astype(BF16)


def qkv_grads(x_turned, grads, small, row_shard, needs=()):
    rounds = len(grads)
    model_width, positions = x_turned[0].shape
    cols = grads[0].shape[1]
    shards, extra, _ = small.shape
    block = GRAD_LANES if cols % GRAD_LANES == 0 else cols
    return pl.pallas_call(
        gated(partial(qkv_grads_kernel, rounds), 2 * rounds + 1, needs),
        grid=(cols // block,),
        in_specs=[whole((model_width, positions))] * rounds
        + [pl.BlockSpec((positions, block), lambda i: (0, i))] * rounds
        + [pl.BlockSpec((shards, extra, block), lambda i: (0, 0, i))]
        + [ANYWHERE] * len(needs),
        out_specs=pl.BlockSpec((shards, row_shard + extra, block), lambda i: (0, 0, i)),
        out_shape=jax.ShapeDtypeStruct((shards, row_shard + extra, cols), BF16),
        name="qkv_grads",
        **params(60, 2 * rounds * positions * model_width * cols, 18_000_000),
    )(*x_turned, *grads, small, *needs)


def add_picked_kernel(count, first, table, *refs):
    in_refs, out_refs = refs[:count], refs[count:]
    if count == 2:
        total = in_refs[0][...] + in_refs[1][...]
    else:
        total = in_refs[0][...].astype(F32)
        for ref in in_refs[1:]:
            total = total + ref[...].astype(F32)
        total = total.astype(BF16)
    if len(out_refs) == 1:
        out_refs[0][...] = total
        return

    @pl.when(pl.program_id(0) < first)
    def _():
        out_refs[0][...] = total

    @pl.when(pl.program_id(0) >= first)
    def _():
        out_refs[1][...] = total


def add_picked(table, arrays, steps, first=None, needs=(), work=0):
    _, rows, cols = arrays[0].shape
    parts = 2 if rows % 32 == 0 and steps == 1 else 1
    block = (1, rows // parts, cols)
    spec = [
        pl.BlockSpec(block, lambda s, p, t, k=k: (t[k * steps + s], p, 0))
        for k in range(len(arrays))
    ]
    if first is None:
        out_specs = [pl.BlockSpec(block, lambda s, p, t: (s, p, 0))]
        counts = [steps]
    else:
        out_specs = [
            pl.BlockSpec(
                block,
                lambda s, p, t: (
                    jnp.minimum(s, first - 1),
                    jnp.where(s < first, p, parts - 1),
                    0,
                ),
            ),
            pl.BlockSpec(
                block,
                lambda s, p, t: (jnp.maximum(s - first, 0), jnp.where(s < first, 0, p), 0),
            ),
        ]
        counts = [first, steps - first]
    return pl.pallas_call(
        gated(partial(add_picked_kernel, len(arrays), first), 1 + len(arrays), needs),
        grid_spec=pltpu.PrefetchScalarGridSpec(
            num_scalar_prefetch=1,
            grid=(steps, parts),
            in_specs=spec + [ANYWHERE] * len(needs),
            out_specs=out_specs,
        ),
        out_shape=[jax.ShapeDtypeStruct((n, rows, cols), BF16) for n in counts],
        name="add_picked",
        compiler_params=pltpu.CompilerParams(
            dimension_semantics=("arbitrary", "arbitrary"),
            vmem_limit_bytes=(60 if steps > 1 else 12) * MIB,
        ),
        cost_estimate=pl.CostEstimate(flops=work, bytes_accessed=1_000_000, transcendentals=0),
    )(table, *arrays, *needs)


def join_kernel(count, down_kept, down_landed, rest_kept, rest_landed, *outs):
    rows = down_kept.shape[1]
    for index in range(count):
        target = outs[1 - index % 2] if count > 1 else outs[0]
        place_now = index // 2
        target[place_now, :rows, :] = down_kept[index] + down_landed[index]
        target[place_now, rows:, :] = rest_kept[index] + rest_landed[index]


def join(kept, landed, needs=()):
    count = kept[0].shape[0]
    rows = kept[0].shape[1] + kept[1].shape[1]
    shape = jax.ShapeDtypeStruct(((count + 1) // 2, rows, kept[0].shape[2]), BF16)
    vmem = pl.BlockSpec(memory_space=pltpu.VMEM)
    outs = pl.pallas_call(
        gated(partial(join_kernel, count), 4, needs),
        in_specs=[vmem] * 4 + [ANYWHERE] * len(needs),
        out_specs=[vmem] * min(count, 2),
        out_shape=[shape] * min(count, 2),
        name="join",
        compiler_params=pltpu.CompilerParams(vmem_limit_bytes=24 * MIB),
        cost_estimate=pl.CostEstimate(flops=0, bytes_accessed=200_000, transcendentals=0),
    )(kept[0], landed[0], kept[1], landed[1], *needs)
    return outs if count > 1 else (None, outs[0])


def stack_kernel(count, *refs):
    for index in range(count):
        refs[count][index] = refs[index][...]


def home_kernel(count, meta, *refs):
    out_ref = refs[count]
    rows = refs[0].shape[0]
    for index in range(count):
        start = pl.multiple_of((meta[5] + index) % count * rows, 16)
        out_ref[pl.ds(start, rows), :] = refs[index][...].astype(out_ref.dtype)


def home_rows(meta, landed, dtype, needs=()):
    rows, cols = landed[0].shape
    vmem = pl.BlockSpec(memory_space=pltpu.VMEM)
    return pl.pallas_call(
        gated(partial(home_kernel, len(landed)), 1 + len(landed), needs),
        in_specs=[IN_SMEM] + [vmem] * len(landed) + [ANYWHERE] * len(needs),
        out_specs=vmem,
        out_shape=jax.ShapeDtypeStruct((len(landed) * rows, cols), dtype),
        name="home_rows",
        compiler_params=pltpu.CompilerParams(vmem_limit_bytes=60 * MIB),
        cost_estimate=pl.CostEstimate(flops=0, bytes_accessed=100_000, transcendentals=0),
    )(meta, *landed, *needs)


def split_kernel(in_ref, *out_refs):
    rows = out_refs[0].shape[0]
    for index, ref in enumerate(out_refs):
        ref[...] = in_ref[index * rows : (index + 1) * rows, :]


def split_rows(value, count, needs=()):
    rows = value.shape[0] // count
    vmem = pl.BlockSpec(memory_space=pltpu.VMEM)
    return pl.pallas_call(
        gated(split_kernel, 1, needs),
        in_specs=[vmem] + [ANYWHERE] * len(needs),
        out_specs=[vmem] * count,
        out_shape=[jax.ShapeDtypeStruct((rows, value.shape[1]), value.dtype)] * count,
        name="split_rows",
        compiler_params=pltpu.CompilerParams(vmem_limit_bytes=12 * MIB),
        cost_estimate=pl.CostEstimate(flops=0, bytes_accessed=100_000, transcendentals=0),
    )(value, *needs)


def stack_up(pieces, needs=()):
    vmem = pl.BlockSpec(memory_space=pltpu.VMEM)
    return pl.pallas_call(
        gated(partial(stack_kernel, len(pieces)), len(pieces), needs),
        in_specs=[vmem] * len(pieces) + [ANYWHERE] * len(needs),
        out_specs=vmem,
        out_shape=jax.ShapeDtypeStruct((len(pieces),) + pieces[0].shape, BF16),
        name="stack_up",
        compiler_params=pltpu.CompilerParams(vmem_limit_bytes=24 * MIB),
        cost_estimate=pl.CostEstimate(flops=0, bytes_accessed=100_000, transcendentals=0),
    )(*pieces, *needs)


def unpack_kernel(pack, depth, meta, mine_ref, other_ref, down_ref, up_ref, out_ref, ordered):
    core, level = meta[2], meta[4]
    rows = pack.rows // depth
    for mask in range(depth):
        start = pl.multiple_of(lax.bitwise_xor(level, mask) * rows, 16)
        ordered[core, pl.ds(start, rows), :] = mine_ref[mask]
        ordered[1 - core, pl.ds(start, rows), :] = other_ref[mask]
    turned = []
    for half in range(CORES):
        for lane in range(0, pack.model_width, pack.feed_shard):
            turned.append(ordered[half, : pack.down_rows, lane : lane + pack.feed_shard])
    down_ref[...] = jnp.transpose(jnp.concatenate(turned, axis=0)).astype(F32)
    for half in range(CORES):
        for block in range(pack.blocks):
            lane = (half * pack.blocks + block) * pack.model_width
            start = pack.up_at + block * pack.row_shard
            up_ref[:, lane : lane + pack.model_width] = ordered[
                half, start : start + pack.row_shard, :
            ].astype(F32)
        out_ref[half * pack.out_rows : (half + 1) * pack.out_rows, :] = ordered[
            half, pack.out_at : pack.out_at + pack.out_rows, :
        ].astype(F32)


def unpack(pack, depth, meta, mine, other):
    vmem = pl.BlockSpec(memory_space=pltpu.VMEM)
    return pl.pallas_call(
        partial(unpack_kernel, pack, depth),
        in_specs=[IN_SMEM, vmem, vmem],
        out_specs=[vmem] * 3,
        out_shape=[
            jax.ShapeDtypeStruct((pack.feed_shard, pack.model_width), F32),
            jax.ShapeDtypeStruct((pack.row_shard, pack.feed_width), F32),
            jax.ShapeDtypeStruct((pack.row_shard, pack.model_width), F32),
        ],
        scratch_shapes=[pltpu.VMEM((CORES, pack.rows, pack.model_width), BF16)],
        name="unpack",
        compiler_params=pltpu.CompilerParams(vmem_limit_bytes=60 * MIB),
        cost_estimate=pl.CostEstimate(flops=0, bytes_accessed=10_000_000, transcendentals=0),
    )(meta, mine, other)


def unpack_qkv_kernel(meta, mine_ref, other_ref, grad_ref, bias_ref, small_ref):
    member = meta[3]
    row_shard, width = grad_ref.shape[0], grad_ref.shape[1] // 3
    part = mine_ref.shape[1] // 3
    for ref, at in ((mine_ref, member), (other_ref, 1 - member)):
        for kind in range(3):
            lane = pl.multiple_of(kind * width + at * part, CLUSTER_ROWS)
            from_lanes = slice(kind * part, (kind + 1) * part)
            grad_ref[:, pl.ds(lane, part)] = ref[:row_shard, from_lanes].astype(F32)
            lane = pl.multiple_of(at * part, CLUSTER_ROWS)
            bias_ref[kind : kind + 1, pl.ds(lane, part)] = ref[row_shard:, from_lanes].astype(F32)[
                BIAS_ROW : BIAS_ROW + 1
            ]
    small_ref[...] = (mine_ref[row_shard:, :].astype(F32) + other_ref[row_shard:, :].astype(F32))[
        :BIAS_ROW
    ]


def unpack_qkv(meta, mine, other, row_shard, needs=()):
    cols = mine.shape[1]
    vmem = pl.BlockSpec(memory_space=pltpu.VMEM)
    return pl.pallas_call(
        gated(unpack_qkv_kernel, 3, needs),
        in_specs=[IN_SMEM, vmem, vmem] + [ANYWHERE] * len(needs),
        out_specs=[vmem] * 3,
        out_shape=[
            jax.ShapeDtypeStruct((row_shard, CORES * cols), F32),
            jax.ShapeDtypeStruct((3, CORES * cols // 3), F32),
            jax.ShapeDtypeStruct((BIAS_ROW, cols), F32),
        ],
        name="unpack_qkv",
        compiler_params=pltpu.CompilerParams(vmem_limit_bytes=60 * MIB),
        cost_estimate=pl.CostEstimate(flops=0, bytes_accessed=200_000, transcendentals=0),
    )(meta, mine, other, *needs)


def tie(*values):
    return lax.optimization_barrier(values)


def body(
    tokens,
    cotangent,
    perms,
    unit_kind,
    w_qkv,
    bias_qv,
    w_out,
    bias_out,
    ln_gain,
    ln_bias,
    w_up,
    bias_up,
    w_down,
    bias_down,
):
    shards = lax.axis_size("fsdp")
    groups = lax.axis_size("dp")
    here = lax.axis_index("fsdp")
    dp_index = lax.axis_index("dp")
    core = dp_index % CORES
    level = dp_index // CORES
    depth = groups // CORES
    units, rounds, unit_len = perms.shape
    per_device = unit_len // shards
    model_width = tokens.shape[1]
    feed_width = w_up.shape[1]
    row_shard = model_width // shards
    members = shards // units
    member_rows = unit_len // members
    head_cols = model_width // members
    padded = -(-head_cols // CLUSTER_ROWS) * CLUSTER_ROWS
    spot = here * CORES + core
    home_core = spot // shards
    unit = (spot // members) % units
    member = spot % members
    pack = Pack(model_width, feed_width, shards, units, depth)
    bits = [1 << k for k in range(shards.bit_length() - 1)]
    bit_orders = (bits, bits[::-1])

    def plane_pairs(target):
        pairs = []
        for z in range(depth):
            for f_index in range(shards):
                for c_index in range(CORES):
                    f_new, c_new = target(f_index, c_index)
                    pairs.append(
                        (
                            (z * CORES + c_index) * shards + f_index,
                            (z * CORES + c_new) * shards + f_new,
                        )
                    )
        return pairs

    def send(value, pairs):
        return lax.ppermute(value, ("dp", "fsdp"), pairs)

    def cross(value, mask):
        return send(value, plane_pairs(lambda f, c: divmod((f * CORES + c) ^ mask, CORES)))

    def trade(value, stage):
        return send(value, plane_pairs(lambda f, c: (f ^ bit_orders[c][stage], c)))

    def trade_mask(index, which):
        mask = 0
        for stage in range(len(bits)):
            if index >> stage & 1:
                mask ^= bit_orders[which][stage]
        return mask

    def climb(value, mask):
        plane = CORES * shards
        pairs = []
        for z in range(depth):
            for rest in range(plane):
                pairs.append((z * plane + rest, (z ^ mask) * plane + rest))
        return send(value, pairs)

    def outward(step):
        def target(f, c):
            place_now = (c * units + (f % units + step) % units) * members + f // units
            return divmod(place_now, CORES)

        return plane_pairs(target)

    def homeward(step):
        return [(b, a) for a, b in outward(step)]

    def bring_start(value):
        blocks = value.reshape(units, per_device, model_width)
        return [
            lax.dynamic_index_in_dim(blocks, (here % units + step) % units, axis=0, keepdims=False)
            for step in range(units)
        ]

    def bring(chosen):
        return jnp.concatenate(
            [send(chosen[step], outward(step)) for step in range(units)], axis=0
        )

    def send_home(blocks):
        return [send(blocks[step], homeward(step)) for step in range(units)]

    x_chosen = bring_start(tokens)
    x_own = bring(x_chosen)

    def half_of(value, axis, length, at):
        return lax.dynamic_slice_in_dim(value, at * length, length, axis=axis)

    packed = jnp.concatenate(
        [half_of(w_down, 0, pack.down_rows, core)]
        + [
            half_of(w_up, 1, model_width, core * pack.blocks + block)
            for block in range(pack.blocks)
        ]
        + [half_of(w_out, 0, pack.out_rows, core)],
        axis=0,
    )
    small = jnp.concatenate(
        [
            bias_qv.reshape(-1),
            bias_out,
            ln_gain.reshape(-1),
            ln_bias.reshape(-1),
            bias_up,
            bias_down,
        ]
    )
    small_rows = -(-small.shape[0] // (3 * padded))
    small_block = jnp.pad(
        jnp.pad(small, (0, small_rows * 3 * padded - small.shape[0])).reshape(
            small_rows, 3 * padded
        ),
        ((0, 16 - small_rows), (0, 0)),
    )
    def columns_for(offset):
        start = lax.bitwise_xor(member, offset) * head_cols
        blocks = [
            jnp.pad(
                lax.dynamic_slice(
                    w_qkv, (0, kind * model_width + start), (row_shard, head_cols)
                ),
                ((0, 0), (0, padded - head_cols)),
            )
            for kind in range(3)
        ]
        return jnp.concatenate([jnp.concatenate(blocks, axis=1), small_block], axis=0)

    offsets = [(CORES * m) % members for m in range(shards)]
    kinds = sorted(set(offsets))
    order_pack = jnp.concatenate(
        [perms.reshape(-1), jnp.broadcast_to(unit_kind[:, None], (units, 128)).reshape(-1)]
    )
    order_other = cross(order_pack, 1)
    *tied, order_other = tie(*[columns_for(offset) for offset in kinds], order_other)
    piece_kinds = dict(zip(kinds, tied))
    x_pieces = [x_own] + [cross(x_own, mask) for mask in range(1, members)]
    packed, x_pieces[-1] = tie(packed, x_pieces[-1])
    weight_pieces = {0: packed, 1: trade(packed, 0)}
    if members == CORES:
        qkv_pieces = {0: piece_kinds[0]}
        for stage in range(len(bits)):
            qkv_pieces[1 << stage] = trade(piece_kinds[0], stage)
        for stage in range(1, len(bits)):
            for index in range(1, 1 << stage):
                qkv_pieces[index | 1 << stage] = trade(qkv_pieces[index], stage)
        qkv_pieces = [qkv_pieces[index] for index in range(shards)]
        qkv_masks = [[trade_mask(index, which) for index in range(shards)] for which in (0, 1)]
    else:
        qkv_pieces = [piece_kinds[0]] + [
            cross(piece_kinds[offsets[m]], CORES * m) for m in range(1, shards)
        ]
        qkv_masks = [list(range(shards))] * 2
    order_pack = jnp.where(home_core == core, order_pack, order_other)
    order_count = units * rounds * unit_len
    unit_perm = lax.dynamic_index_in_dim(
        order_pack[:order_count].reshape(units, rounds * unit_len), unit, 0, keepdims=False
    )
    kind_now = lax.dynamic_index_in_dim(
        order_pack[order_count:].reshape(units, 128), unit, 0, keepdims=False
    )[0]
    owner = unit_perm // per_device
    order = (
        lax.bitwise_xor(owner // units, member) * units + (unit - owner % units) % units
    ) * per_device + unit_perm % per_device
    order = order.reshape(rounds, unit_len)
    order = jnp.where(core == 0, order, order[::-1])
    order_row = order.reshape(1, rounds * unit_len)
    order = order.reshape(-1, CLUSTER_ROWS)
    x_here = arrange(order, x_pieces, unit_len, 0)
    x_now = [x_here, cross(x_here, 1)]
    own_masks = [
        jnp.where(core == 0, trade_mask(i, 0), trade_mask(i, 1)) for i in range(1, shards)
    ]
    other_masks = [
        jnp.where(core == 0, trade_mask(i, 1), trade_mask(i, 0)) for i in range(1, shards)
    ]
    zero = jnp.int32(0)
    meta = jnp.stack(
        [kind_now, here, core, member, level, here % units, zero, zero]
        + own_masks
        + other_masks
        + [jnp.where(core == 0, first, second) for first, second in zip(*qkv_masks)]
    ).astype(jnp.int32)

    order_rows = unit_len // CLUSTER_ROWS
    arranged, probs, mixtures, x_turned = [], [], [], []
    *tied, packed, weight_pieces[1], x_now[0] = tie(
        *qkv_pieces[1:], packed, weight_pieces[1], x_now[0]
    )
    qkv_pieces = qkv_pieces[:1] + tied
    smalls = jnp.stack(
        [
            piece[row_shard : row_shard + small_rows].reshape(-1)[: small.shape[0]]
            for piece in qkv_pieces
        ]
    )
    spots_of = [[masks.index(mask) for mask in range(shards)] for masks in qkv_masks]
    spots_of = jnp.where(core == 0, jnp.array(spots_of[0]), jnp.array(spots_of[1]))
    spots_of = jnp.take(spots_of, lax.bitwise_xor(here, jnp.arange(shards)))
    smalls = jnp.take(smalls, spots_of, axis=0).astype(F32)

    def vectors_at(start, count, length):
        part = smalls[:, start * row_shard : start * row_shard + count * length]
        return (
            part.reshape(shards, count, length).transpose(1, 0, 2).reshape(count, shards * length)
        )

    my_bias = lax.dynamic_index_in_dim(
        vectors_at(0, 2, row_shard).reshape(2, members, head_cols), member, 1, keepdims=False
    )
    my_bias = jnp.pad(my_bias, ((0, 0), (0, padded - head_cols)))
    my_bias = jnp.stack([my_bias[0], jnp.zeros_like(my_bias[0]), my_bias[1]]).reshape(1, -1)
    up_bias = vectors_at(7, 1, feed_width // shards)
    down_bias = smalls[:, small.shape[0] - row_shard :].reshape(1, model_width)
    vectors = jnp.concatenate(
        [vectors_at(2, 5, row_shard), down_bias, jnp.zeros((2, model_width), F32)], axis=0
    )

    for stage in range(1, len(bits)):
        weight_pieces[1 << stage] = trade(packed, stage)
    for index in range(rounds):
        needs = [weight_pieces[1]] if index == 0 else [mixtures[-1], weight_pieces[2]]
        results = attend(meta, x_now[index], my_bias, qkv_pieces, row_shard, needs)
        for kept, result in zip((arranged, probs, mixtures, x_turned), results):
            kept.append(result)
    cot_now, mixtures[0] = tie(cotangent, mixtures[0])
    cot_landed = [
        send(value, outward(step)) for step, value in enumerate(bring_start(cot_now))
    ]
    cot_own = jnp.concatenate(cot_landed, axis=0)
    *tied, mixtures[1] = tie(*weight_pieces.values(), mixtures[1])
    forwarded = dict(zip(weight_pieces, tied))
    for stage in range(1, len(bits)):
        for index in range(1, 1 << stage):
            forwarded[index | 1 << stage] = trade(forwarded[index], stage)
    weight_pieces = {**forwarded, **weight_pieces}
    direct = [weight_pieces[index] for index in range(1, shards)]
    swapped = [cross(piece, 1) for piece in direct[:-1]]
    att_there, att_sent = [], []
    for mask in range(1, members):
        there = place(
            order_row, mixtures, mask * member_rows, member_rows, 0.5, needs=swapped
        )
        att_sent.append(there)
        att_there.append(cross(there[:, :head_cols], mask))
    att_here = place(
        order_row, mixtures, 0, member_rows, 0.5, needs=att_sent + cot_landed, share=1
    )

    last_piece, att_here = tie(direct[-1], att_here)
    swapped.append(cross(last_piece, 1))
    att_raw = [att_here[:, :head_cols]] + att_there
    if head_cols % CLUSTER_ROWS:
        att_raw = [jnp.concatenate(att_raw, axis=1)]
    block_out, first_low, d_branch, d_ffn, hidden, d_pre, att_turned, *rest = feed(
        pack,
        meta,
        x_own,
        cot_own,
        vectors,
        up_bias,
        att_raw,
        [w_out, w_up, w_down],
        direct + swapped,
    )
    d_att, (row_sums, up_sums) = rest[: len(att_raw)], rest[len(att_raw) :]
    if head_cols % CLUSTER_ROWS:
        d_att = [d_att[0][:, mask * head_cols : (mask + 1) * head_cols] for mask in range(members)]
    d_att = [d_att[0]] + [cross(d_att[mask], mask) for mask in range(1, members)]
    d_att = [jnp.pad(piece, ((0, 0), (0, padded - head_cols))) for piece in d_att]

    table = jnp.stack([core, member]).astype(jnp.int32)
    sending = [index for index in range(shards) if index & 1]
    keeping = [index for index in range(shards) if not index & 1]
    slots = jnp.stack(
        [
            lax.bitwise_xor(here, jnp.where(core == 0, trade_mask(i, 0), trade_mask(i, 1)))
            for i in sending + keeping
        ]
    )
    slots = jnp.concatenate([slots, slots]).astype(jnp.int32)

    def pair_sum(mine, theirs, needs):
        return add_picked(
            slots, [mine, cross(theirs, 1)], shards, len(sending), needs, 20_000_000_000
        )

    theirs_down, mine_down = down_grads(pack, table, d_ffn, hidden)
    theirs_rest, mine_rest = rest_grads(
        pack, table, first_low, d_pre, att_turned, d_branch, [theirs_down]
    )
    down_going, down_kept = pair_sum(mine_down, theirs_down, [theirs_rest])
    rest_going, rest_kept = pair_sum(mine_rest, theirs_rest, [down_going] + d_att[1:])

    def merge(kept, landed, *needs):
        count = kept.shape[0]
        if count == 1:
            table = jnp.zeros((2,), jnp.int32)
            return None, add_picked(table, [kept, landed], 1, None, needs)[0]
        order_now = [i for i in range(count) if i & 1] + [i for i in range(count) if not i & 1]
        table = jnp.array(order_now * 2, jnp.int32)
        return add_picked(table, [kept, landed], count, count // 2, needs)

    grads, d_x = [None] * rounds, [None] * rounds
    needs = [rest_going]
    blocks = unit_len // POS_BLOCK
    spans = [(index, (0, blocks)) for index in reversed(range(rounds))]
    for turn, (index, span) in enumerate(spans):
        grads[index], d_x[index], token = attend_back(
            meta,
            order,
            arranged[index],
            probs[index],
            d_att,
            qkv_pieces,
            row_shard,
            index * order_rows,
            needs,
            span,
            [],
        )
        if turn == 0:
            d_x_there = cross(d_x[index], 1)
            going, kept = join(
                [down_kept, rest_kept], [trade(down_going, 0), trade(rest_going, 0)], [token]
            )
            output_landed = send_home(split_rows(block_out, units, [token]))
            needs = [kept]
    for stage in range(1, len(bits)):
        going, kept = merge(kept, trade(going, stage), token)

    def level_pieces(block):
        return block.reshape((depth, block.shape[0] // depth) + block.shape[1:])

    def level_scatter(cut):
        return [
            climb(
                lax.dynamic_index_in_dim(cut, lax.bitwise_xor(level, mask), 0, keepdims=False), mask
            )
            for mask in range(1, depth)
        ]

    def level_gather(piece):
        pieces = {0: piece}
        mask = depth // 2
        while mask:
            pieces[mask] = climb(piece, mask)
            mask //= 2
        return pieces

    def level_forward(pieces):
        for index in sorted(range(depth), key=lambda value: value.bit_count()):
            if index not in pieces:
                low = index & -index
                pieces[index] = climb(pieces[index ^ low], low)
        return [pieces[index] for index in range(depth)]

    def by_shard(value):
        count, length = value.shape
        return (
            value.reshape(count, shards, length // shards)
            .transpose(1, 0, 2)
            .reshape(shards, count * length // shards)
        )

    small_grad = jnp.concatenate(
        [by_shard(row_sums[:5]), by_shard(up_sums), by_shard(row_sums[5:6])], axis=1
    )
    small_length = small_grad.shape[1]
    small_lanes = 3 * head_cols
    small_grad = jnp.pad(small_grad, ((0, 0), (0, BIAS_ROW * small_lanes - small_length)))
    small_grad = jnp.pad(
        small_grad.reshape(shards, BIAS_ROW, small_lanes), ((0, 0), (0, 16 - BIAS_ROW), (0, 0))
    )
    extra_rows = 16
    if padded == head_cols:
        joined = qkv_grads(
            x_turned, grads, small_grad, row_shard, output_landed + [kept]
        )
    else:
        qkv_grad = dot(x_turned[0], grads[0]) + dot(x_turned[1], grads[1])
        qkv_grad = qkv_grad.reshape(shards, row_shard, 3, padded)[..., :head_cols]
        bias_sum = sum(jnp.sum(value.astype(F32), axis=0) for value in grads)
        bias_sum = bias_sum.reshape(3, padded)[:, :head_cols].reshape(small_lanes)
        small_grad = small_grad.at[:, BIAS_ROW].set(bias_sum[None])
        joined = jnp.concatenate(
            [qkv_grad.reshape(shards, row_shard, small_lanes), small_grad], axis=1
        ).astype(BF16)
    cut = level_pieces(kept[0])
    landed = level_scatter(cut)
    classes = max(1, members // CORES)
    d_x_parts = [d_x[0], d_x_there]
    order_mine = order_row[:, :unit_len]
    if classes == 1:
        slots_held = jnp.stack(
            [
                lax.bitwise_xor(here, jnp.where(core == 0, trade_mask(i, 0), trade_mask(i, 1)))
                for i in range(shards)
            ]
        )
        held = jnp.stack(
            [
                lax.dynamic_index_in_dim(joined, slots_held[i], 0, keepdims=False)
                for i in range(0, shards, 2)
            ]
        )
        leaving = jnp.stack(
            [
                lax.dynamic_index_in_dim(joined, slots_held[i], 0, keepdims=False)
                for i in range(1, shards, 2)
            ]
        )
        totals = None
    else:
        totals = [None] * classes
        for m in range(shards):
            offset = offsets[m] // CORES
            piece = lax.dynamic_index_in_dim(joined, lax.bitwise_xor(here, m), 0, keepdims=False)
            piece = (piece if m == 0 else cross(piece, CORES * m)).astype(F32)
            totals[offset] = piece if totals[offset] is None else totals[offset] + piece

    d_there = [
        place(
            order_mine,
            d_x_parts,
            mask * member_rows,
            member_rows,
            added=True,
            needs=[joined],
        )
        for mask in range(1, members)
    ]
    if depth > 1:
        picks = jnp.concatenate([level[None], jnp.zeros((depth - 1,), level.dtype)])
        (kept,) = add_picked(
            picks.astype(jnp.int32),
            [cut] + [piece[None] for piece in landed],
            1,
            None,
            d_there,
        )
    gathered = level_gather(kept[0]) if depth > 1 else {0: cut[0]}
    early = [kept] + d_there
    if totals is None:
        leaving, held = merge(held, trade(leaving, 0), *d_there)
        early.append(held)
    d_here = place(
        order_mine,
        d_x_parts,
        0,
        member_rows,
        1.0,
        F32,
        d_branch,
        added=True,
        needs=early,
    )
    d_inputs = d_here
    for mask, there in enumerate(d_there, 1):
        d_inputs = d_inputs + cross(there, mask).astype(F32)
    d_inputs = d_inputs.astype(BF16)
    home = send_home(d_inputs.reshape(units, per_device, model_width))
    last = d_inputs
    if totals is None:
        for stage in range(1, len(bits)):
            leaving, held = merge(held, trade(leaving, stage), d_inputs)
        masks = [mask for mask in gathered if mask]
        *tied, held = tie(*[gathered[mask] for mask in masks], held)
        gathered.update(zip(masks, tied))
        last = held
        totals = [held[0]]
    output = home_rows(meta, output_landed, BF16, [last])
    totals = jnp.concatenate(totals, axis=0).astype(BF16)
    rows_each = row_shard + extra_rows
    if depth > 1:
        halves = totals.reshape((2, totals.shape[0] // 2) + totals.shape[1:])
        side = level % 2
        mine = lax.dynamic_index_in_dim(halves, side, 0, keepdims=False)
        theirs = lax.dynamic_index_in_dim(halves, 1 - side, 0, keepdims=False)
        half = (mine.astype(F32) + climb(theirs, 1).astype(F32)).astype(BF16)
        mask = 2
        while mask < depth:
            half = (half.astype(F32) + climb(half, mask).astype(F32)).astype(BF16)
            mask *= 2
        *home, output, half = tie(*home, output, half)
        other_half = climb(half, 1)
        d_inputs = home_rows(meta, home, F32)
        d_inputs, other_half = tie(d_inputs, other_half)
        totals = jnp.concatenate(
            [
                jnp.where(side == 0, half, other_half),
                jnp.where(side == 0, other_half, half),
            ],
            axis=0,
        )
    else:
        d_inputs = home_rows(meta, home, F32)
    stacked = stack_up(level_forward(gathered))
    grad_down, grad_up, grad_out = unpack(pack, depth, meta, stacked, cross(stacked, 1))
    if padded == head_cols and members == CORES:
        grad_qkv, bias_out_row, smalls_out = unpack_qkv(
            meta, totals, cross(totals, 1), row_shard, [grad_down]
        )
        smalls_out = smalls_out.reshape(-1)[:small_length]
        bias_out_row = lax.dynamic_slice(bias_out_row, (0, here * row_shard), (3, row_shard))
    else:
        landed = jnp.stack([totals, cross(totals, 1)], axis=0).reshape(
            CORES, classes, rows_each, 3 * head_cols
        )
        smalls_out = jnp.sum(
            landed[:, :, row_shard : row_shard + BIAS_ROW].astype(F32), axis=(0, 1)
        ).reshape(-1)[:small_length]
        landed = (
            landed.transpose(1, 0, 2, 3)
            .reshape(members, rows_each, 3, head_cols)[:, : row_shard + BIAS_ROW + 1]
        )
        if members == 2:
            swap = member == 1
            landed = jnp.stack(
                [
                    jnp.where(swap, landed[1], landed[0]),
                    jnp.where(swap, landed[0], landed[1]),
                ]
            )
        else:
            landed = jnp.take(landed, lax.bitwise_xor(member, jnp.arange(members)), axis=0)
        grad_qkv = landed[:, :row_shard].transpose(1, 2, 0, 3)
        grad_qkv = grad_qkv.reshape(row_shard, 3 * model_width).astype(F32)
        bias_out_row = landed[:, row_shard + BIAS_ROW].astype(F32).transpose(1, 0, 2)
        bias_out_row = lax.dynamic_slice(
            bias_out_row.reshape(3, model_width), (0, here * row_shard), (3, row_shard)
        )

    feed_shard = feed_width // shards
    spots = [0, row_shard, 3 * row_shard, 5 * row_shard]
    return (
        output,
        d_inputs,
        grad_qkv,
        bias_out_row[::2],
        grad_out,
        smalls_out[spots[0] : spots[1]],
        smalls_out[spots[1] : spots[2]].reshape(2, row_shard),
        smalls_out[spots[2] : spots[3]].reshape(2, row_shard),
        grad_up,
        smalls_out[spots[3] : spots[3] + feed_shard],
        grad_down,
        smalls_out[spots[3] + feed_shard :],
    )


def solution(mesh):
    placed = (
        P(("dp", "fsdp"), None),
        P(("dp", "fsdp"), None),
        P("dp", None, None),
        P("dp"),
        P("fsdp", None),
        P(None, "fsdp"),
        P("fsdp", None),
        P("fsdp"),
        P(None, "fsdp"),
        P(None, "fsdp"),
        P("fsdp", None),
        P("fsdp"),
        P("fsdp", None),
        P("fsdp"),
    )
    return jax.shard_map(
        body,
        mesh=mesh,
        in_specs=placed,
        out_specs=(
            P(("dp", "fsdp"), None),
            P(("dp", "fsdp"), None),
            P("fsdp", None),
            P(None, "fsdp"),
            P("fsdp", None),
            P("fsdp"),
            P(None, "fsdp"),
            P(None, "fsdp"),
            P("fsdp", None),
            P("fsdp"),
            P("fsdp", None),
            P("fsdp"),
        ),
        check_vma=False,
    )
```

```python
from functools import partial

import jax
import jax.numpy as jnp
from jax import lax
from jax.experimental import pallas as pl
from jax.experimental.pallas import tpu as pltpu
from jax.sharding import PartitionSpec as P

HEAD_DIM = 64
CORES = 2
NEG_FILL = -1000000000.0
EPSILON = 1e-05
SCALE = HEAD_DIM ** (-0.5)
BIAS_ROW = 2
GRAD_LANES = 384
CLUSTER_ROWS = 128
HALF_ROWS = 64
POS_BLOCK = 512
TOKEN_BLOCK = 512
ROW_BLOCK = 256
FF_BLOCK = 512
MIB = 1024 * 1024
NT = (((1,), (1,)), ((), ()))
TN = (((0,), (0,)), ((), ()))
F32 = jnp.float32
BF16 = jnp.bfloat16
ANYWHERE = pl.BlockSpec(memory_space=pl.ANY)
IN_SMEM = pl.BlockSpec(memory_space=pltpu.SMEM)
IN_HBM = pl.BlockSpec(memory_space=pltpu.HBM)


def whole(shape):
    return pl.BlockSpec(shape, lambda i: (0,) * len(shape))


def rows_of(shape):
    return pl.BlockSpec(shape, lambda i: (i,) + (0,) * (len(shape) - 1))


def dot(a, b, dims=(((1,), (0,)), ((), ()))):
    return lax.dot_general(a, b, dims, preferred_element_type=F32)


def params(mib, flops=0, moved=0, share=16):
    return dict(
        compiler_params=pltpu.CompilerParams(
            dimension_semantics=("arbitrary",),
            vmem_limit_bytes=mib * MIB,
        ),
        cost_estimate=pl.CostEstimate(
            flops=flops // share, bytes_accessed=moved // share, transcendentals=0
        ),
    )


def gated(kernel, used, needs):
    if not needs:
        return kernel

    def run(*refs):
        return kernel(*refs[:used], *refs[used + len(needs) :])

    return run


def lane_masks():
    lane = lax.broadcasted_iota(jnp.int32, (CLUSTER_ROWS, CLUSTER_ROWS), 1)
    low = (lane < HEAD_DIM).astype(F32)
    return low.astype(BF16), (1.0 - low).astype(BF16), lane < HEAD_DIM


def corners(first, second):
    blank = jnp.zeros_like(first)
    return jnp.concatenate(
        [
            jnp.concatenate([first, blank], axis=1),
            jnp.concatenate([blank, second], axis=1),
        ],
        axis=0,
    )


def both_heads(rows_now, low, high):
    return jnp.concatenate([rows_now * low, rows_now * high], axis=0)


def equal_ones(left, right):
    return jnp.where(left == right, jnp.ones((), BF16), jnp.zeros((), BF16))


def pick_rows(order_ref, first_row, unit_len):
    parts = []
    lane = lax.broadcasted_iota(jnp.int16, (CLUSTER_ROWS, CLUSTER_ROWS), 1)
    for part in range(POS_BLOCK // CLUSTER_ROWS):
        row = order_ref[pl.ds(first_row + part, 1), :]
        column = jnp.transpose(jnp.broadcast_to(row, (CLUSTER_ROWS, CLUSTER_ROWS)))
        column = column.astype(jnp.int16)
        pieces = [
            equal_ones(column, lane + jnp.int16(base)) for base in range(0, unit_len, CLUSTER_ROWS)
        ]
        parts.append(jnp.concatenate(pieces, axis=1))
    return jnp.concatenate(parts, axis=0)


def load_pieces(meta, x_refs, w_refs, x_all, w_all, sems, row_shard):
    member_rows = x_all.shape[0] // max(1, len(x_refs))
    copies = []
    for index, ref in enumerate(x_refs):
        copies.append(
            pltpu.make_async_copy(
                ref, x_all.at[pl.ds(index * member_rows, member_rows), :], sems.at[index]
            )
        )
    for index, ref in enumerate(w_refs):
        mask = meta[meta.shape[0] - len(w_refs) + index]
        start = pl.multiple_of(lax.bitwise_xor(meta[1], mask) * row_shard, 16)
        copies.append(
            pltpu.make_async_copy(
                ref.at[pl.ds(0, row_shard), :],
                w_all.at[pl.ds(start, row_shard), :],
                sems.at[len(x_refs) + index],
            )
        )
    for copy in copies:
        copy.start()
    for copy in copies:
        copy.wait()


def arrange_kernel(unit_len, first_row, order_ref, *refs):
    x_refs, out_ref = refs[:-1], refs[-1]
    step = pl.program_id(0)
    picks = pick_rows(order_ref, first_row + step * (POS_BLOCK // CLUSTER_ROWS), unit_len)
    rows = x_refs[0].shape[0]
    total = None
    for index, ref in enumerate(x_refs):
        term = dot(picks[:, index * rows : (index + 1) * rows], ref[...])
        total = term if total is None else total + term
    out_ref[...] = total.astype(BF16)


def arrange(order, x_pieces, position_count, first_row):
    member_rows, width = x_pieces[0].shape
    unit_len = member_rows * len(x_pieces)
    return pl.pallas_call(
        partial(arrange_kernel, unit_len, first_row),
        grid=(position_count // POS_BLOCK,),
        in_specs=[whole(order.shape)] + [whole(piece.shape) for piece in x_pieces],
        out_specs=rows_of((POS_BLOCK, width)),
        out_shape=jax.ShapeDtypeStruct((position_count, width), BF16),
        name="arrange",
        **params(20, 2 * position_count * unit_len * width, 6_000_000),
    )(order, *x_pieces)


def attend_kernel(sizes, meta, x_now_ref, bias_ref, *refs):
    shards, row_shard = sizes
    w_refs, refs = refs[:shards], refs[shards:]
    arranged_ref, probs_ref, mixture_ref, turned_ref, w_all, sems = refs
    width = w_all.shape[1] // 3
    step = pl.program_id(0)

    @pl.when(step == 0)
    def _():
        load_pieces(meta, [], w_refs, w_all, w_all, sems, row_shard)

    x_now = x_now_ref[...]
    turned_ref[...] = jnp.transpose(x_now)
    arranged = (dot(x_now, w_all[...]) + bias_ref[...]).astype(BF16)
    arranged_ref[...] = arranged
    low, high, lane_low = lane_masks()
    position = lax.broadcasted_iota(jnp.int32, (CLUSTER_ROWS, CLUSTER_ROWS), 0)
    other = lax.broadcasted_iota(jnp.int32, (CLUSTER_ROWS, CLUSTER_ROWS), 1)
    same_half = (position < HALF_ROWS) == (other < HALF_ROWS)
    allowed = jnp.logical_or(same_half, meta[0] == 1)
    pairs = width // CLUSTER_ROWS
    units = [(part, pair) for part in range(POS_BLOCK // CLUSTER_ROWS) for pair in range(pairs)]
    for index in range(0, len(units), 2):
        queries, keys, values = [], [], []
        for part, pair in units[index : index + 2]:
            rows_now = slice(part * CLUSTER_ROWS, (part + 1) * CLUSTER_ROWS)
            base = pair * CLUSTER_ROWS
            queries.append(arranged[rows_now, base : base + CLUSTER_ROWS] * SCALE)
            one_key = arranged[rows_now, width + base : width + base + CLUSTER_ROWS]
            keys.append(both_heads(one_key, low, high))
            one_value = arranged[rows_now, 2 * width + base : 2 * width + base + CLUSTER_ROWS]
            values.append(both_heads(one_value, low, high))
        both_scores = dot(jnp.concatenate(keys, axis=1), corners(*queries), NT)
        for which, (part, pair) in enumerate(units[index : index + 2]):
            halves = []
            for head in range(2):
                one = both_scores[
                    head * CLUSTER_ROWS : (head + 1) * CLUSTER_ROWS,
                    which * CLUSTER_ROWS : (which + 1) * CLUSTER_ROWS,
                ]
                one = jnp.where(allowed, one, NEG_FILL)
                grown = jnp.exp(one - jnp.max(one, axis=0, keepdims=True))
                halves.append(grown * (1.0 / jnp.sum(grown, axis=0, keepdims=True)))
            probs = jnp.concatenate(halves, axis=0).astype(BF16)
            at = (part * pairs + pair) * 2 * CLUSTER_ROWS
            probs_ref[at : at + 2 * CLUSTER_ROWS, :] = probs
            mixture_ref[
                part * CLUSTER_ROWS : (part + 1) * CLUSTER_ROWS,
                pair * CLUSTER_ROWS : (pair + 1) * CLUSTER_ROWS,
            ] = dot(probs, values[which], TN).astype(BF16)


def attend(meta, x_now, bias, w_pieces, row_shard, needs=()):
    shards = len(w_pieces)
    position_count, model_width = x_now.shape
    cols = w_pieces[0].shape[1]
    width = cols // 3
    pair_rows = 2 * width
    return pl.pallas_call(
        gated(partial(attend_kernel, (shards, row_shard)), 3 + shards, needs),
        grid=(position_count // POS_BLOCK,),
        in_specs=[IN_SMEM, rows_of((POS_BLOCK, model_width)), whole(bias.shape)]
        + [ANYWHERE] * (shards + len(needs)),
        out_specs=[
            rows_of((POS_BLOCK, cols)),
            rows_of((POS_BLOCK // CLUSTER_ROWS * pair_rows, CLUSTER_ROWS)),
            rows_of((POS_BLOCK, width)),
            pl.BlockSpec((model_width, POS_BLOCK), lambda i: (0, i)),
        ],
        out_shape=[
            jax.ShapeDtypeStruct((position_count, cols), BF16),
            jax.ShapeDtypeStruct((position_count // CLUSTER_ROWS * pair_rows, CLUSTER_ROWS), BF16),
            jax.ShapeDtypeStruct((position_count, width), BF16),
            jax.ShapeDtypeStruct((model_width, position_count), BF16),
        ],
        scratch_shapes=[
            pltpu.VMEM((model_width, cols), BF16),
            pltpu.SemaphoreType.DMA((shards,)),
        ],
        name="attend",
        **params(
            60, 8 * position_count * (model_width * cols + 4 * CLUSTER_ROWS * width), 18_000_000, 1
        ),
    )(meta, x_now, bias, *w_pieces, *needs)


def place_kernel(sizes, scale, has_base, order_row_ref, *refs):
    unit_len, first_token, added = sizes
    base_ref = refs[0] if has_base else None
    refs = refs[1 if has_base else 0 :]
    if added:
        first_ref, second_ref, out_ref, held = refs

        @pl.when(pl.program_id(0) == 0)
        def _():
            held[...] = (first_ref[...].astype(F32) + second_ref[...].astype(F32)).astype(BF16)

        source_refs = [held]
    else:
        source_refs, out_ref = refs[:-1], refs[-1]
    block_rows = out_ref.shape[0]
    first = jnp.full((1, 1), first_token + pl.program_id(0) * block_rows, jnp.int32)
    token = lax.broadcasted_iota(jnp.int16, (block_rows, unit_len), 0)
    total = None
    for index, ref in enumerate(source_refs):
        row = order_row_ref[:, index * unit_len : (index + 1) * unit_len] - first
        row = jnp.broadcast_to(row, (16, unit_len)).astype(jnp.int16)
        row = jnp.concatenate([row] * (block_rows // 16), axis=0)
        term = dot(equal_ones(row, token), ref[...])
        total = term if total is None else total + term
    if scale != 1.0:
        total = total * scale
    if has_base:
        total = total + base_ref[...].astype(F32)
    out_ref[...] = total.astype(out_ref.dtype)


def place(
    order_row,
    sources,
    first_token,
    row_count,
    scale=1.0,
    dtype=BF16,
    base=None,
    added=False,
    needs=(),
):
    unit_len, width = sources[0].shape
    block_rows = min(TOKEN_BLOCK, row_count)
    extra = [] if base is None else [base]
    return pl.pallas_call(
        gated(
            partial(place_kernel, (unit_len, first_token, added), scale, base is not None),
            1 + len(extra) + len(sources),
            needs,
        ),
        grid=(row_count // block_rows,),
        in_specs=[whole(order_row.shape)]
        + [rows_of((block_rows, width))] * len(extra)
        + [whole(source.shape) for source in sources]
        + [ANYWHERE] * len(needs),
        out_specs=rows_of((block_rows, width)),
        out_shape=jax.ShapeDtypeStruct((row_count, width), dtype),
        scratch_shapes=[pltpu.VMEM((unit_len, width), BF16)] if added else [],
        name="place",
        **params(
            32 if added else 20,
            16 * row_count * unit_len * width,
            10_000_000,
            1,
        ),
    )(order_row, *extra, *sources, *needs)


def attend_back_kernel(sizes, meta, order_ref, arranged_ref, probs_ref, *refs):
    members, shards, unit_len, row_shard, first_row, start = sizes
    g_refs, refs = refs[:members], refs[members:]
    w_refs, refs = refs[:shards], refs[shards:]
    grads_ref, d_x_ref, token_ref, g_all, w_all, sems = refs
    width = w_all.shape[1] // 3
    step = pl.program_id(0)

    @pl.when(step == 0)
    def _():
        load_pieces(meta, g_refs, w_refs, g_all, w_all, sems, row_shard)
        token_ref[...] = jnp.zeros_like(token_ref)

    at_row = first_row + (start + step) * (POS_BLOCK // CLUSTER_ROWS)
    picks = pick_rows(order_ref, at_row, unit_len)
    d_mixture = dot(picks, g_all[...]).astype(BF16)
    low, high, lane_low = lane_masks()
    pairs = width // CLUSTER_ROWS
    units = [(part, pair) for part in range(POS_BLOCK // CLUSTER_ROWS) for pair in range(pairs)]
    for index in range(0, len(units), 2):
        values, d_rows = [], []
        for part, pair in units[index : index + 2]:
            rows_now = slice(part * CLUSTER_ROWS, (part + 1) * CLUSTER_ROWS)
            base = pair * CLUSTER_ROWS
            one_value = arranged_ref[rows_now, 2 * width + base : 2 * width + base + CLUSTER_ROWS]
            values.append(both_heads(one_value, low, high))
            d_rows.append(d_mixture[rows_now, base : base + CLUSTER_ROWS])
        both_probs = dot(jnp.concatenate(values, axis=1), corners(*d_rows), NT)
        for which, (part, pair) in enumerate(units[index : index + 2]):
            rows_now = slice(part * CLUSTER_ROWS, (part + 1) * CLUSTER_ROWS)
            base = pair * CLUSTER_ROWS
            q_lanes = slice(base, base + CLUSTER_ROWS)
            k_lanes = slice(width + base, width + base + CLUSTER_ROWS)
            v_lanes = slice(2 * width + base, 2 * width + base + CLUSTER_ROWS)
            queries = arranged_ref[rows_now, q_lanes] * SCALE
            keys = arranged_ref[rows_now, k_lanes] * SCALE
            at = (part * pairs + pair) * 2 * CLUSTER_ROWS
            probs = probs_ref[at : at + 2 * CLUSTER_ROWS, :]
            d_probs = both_probs[:, which * CLUSTER_ROWS : (which + 1) * CLUSTER_ROWS]
            pieces = []
            for head in range(2):
                rows = slice(head * CLUSTER_ROWS, (head + 1) * CLUSTER_ROWS)
                weight = probs[rows].astype(F32)
                d_one = d_probs[rows]
                inner = jnp.sum(weight * d_one, axis=0, keepdims=True)
                pieces.append(weight * (d_one - inner))
            d_scores = jnp.concatenate(pieces, axis=0).astype(BF16)
            d_query = dot(d_scores, both_heads(keys, low, high), TN)
            d_pair = dot(
                jnp.concatenate([probs, d_scores], axis=1), corners(d_rows[which], queries)
            )
            d_values, d_keys = d_pair[:, :CLUSTER_ROWS], d_pair[:, CLUSTER_ROWS:]
            grads_ref[rows_now, q_lanes] = d_query.astype(BF16)
            grads_ref[rows_now, k_lanes] = jnp.where(
                lane_low, d_keys[:CLUSTER_ROWS], d_keys[CLUSTER_ROWS:]
            ).astype(BF16)
            grads_ref[rows_now, v_lanes] = jnp.where(
                lane_low, d_values[:CLUSTER_ROWS], d_values[CLUSTER_ROWS:]
            ).astype(BF16)
    grads = grads_ref[...]
    d_x_ref[...] = dot(grads, w_all[...], NT).astype(BF16)


def attend_back(
    meta, order, arranged, probs, g_pieces, w_pieces, row_shard, first_row, needs, span, into
):
    members, shards = len(g_pieces), len(w_pieces)
    member_rows, width = g_pieces[0].shape
    unit_len = members * member_rows
    position_count, cols = arranged.shape
    model_width = row_shard * shards
    start, stop = span
    pair_rows = POS_BLOCK // CLUSTER_ROWS * 2 * width
    used = 4 + members + shards

    def block(shape):
        return pl.BlockSpec(shape, lambda i: (start + i, 0))

    return pl.pallas_call(
        gated(
            partial(attend_back_kernel, (members, shards, unit_len, row_shard, first_row, start)),
            used,
            list(into) + list(needs),
        ),
        grid=(stop - start,),
        in_specs=[
            IN_SMEM,
            whole(order.shape),
            block((POS_BLOCK, cols)),
            block((pair_rows, CLUSTER_ROWS)),
        ]
        + [ANYWHERE] * (members + shards + len(into) + len(needs)),
        out_specs=[block((POS_BLOCK, cols)), block((POS_BLOCK, model_width)), whole((8, 128))],
        out_shape=[
            jax.ShapeDtypeStruct((position_count, cols), BF16),
            jax.ShapeDtypeStruct((position_count, model_width), BF16),
            jax.ShapeDtypeStruct((8, 128), F32),
        ],
        input_output_aliases={used + index: index for index in range(len(into))},
        scratch_shapes=[
            pltpu.VMEM((unit_len, width), BF16),
            pltpu.VMEM((model_width, cols), BF16),
            pltpu.SemaphoreType.DMA((members + shards,)),
        ],
        name="attend_back",
        **params(
            60,
            12 * (stop - start) * POS_BLOCK * (unit_len * width + model_width * cols),
            20_000_000,
            1,
        ),
    )(meta, order, arranged, probs, *g_pieces, *w_pieces, *into, *needs)


def normalise(summed):
    average = jnp.mean(summed, axis=-1, keepdims=True)
    centred = summed - average
    spread = jnp.mean(centred * centred, axis=-1, keepdims=True)
    scale_inv = lax.rsqrt(spread + EPSILON)
    return centred * scale_inv, scale_inv


def normalise_back(grad_out, normed, scale_inv, gain_row):
    scaled = grad_out * gain_row
    return scale_inv * (
        scaled
        - jnp.mean(scaled, axis=-1, keepdims=True)
        - normed * jnp.mean(scaled * normed, axis=-1, keepdims=True)
    )


def column_sum(rows_now):
    return jnp.sum(rows_now, axis=0, keepdims=True)


def gelu_parts(value):
    below = 0.5 + 0.5 * lax.erf(value * 0.7071067811865476)
    bell = jnp.exp(value * value * -0.5) * 0.3989422804014327
    return value * below, below + value * bell


class Pack:
    def __init__(self, model_width, feed_width, shards, units, depth):
        self.model_width, self.feed_width, self.shards = model_width, feed_width, shards
        self.row_shard = model_width // shards
        self.feed_shard = feed_width // shards
        self.down_rows = self.feed_shard // CORES
        self.blocks = feed_width // CORES // model_width
        self.up_at = self.down_rows
        self.out_at = self.up_at + self.blocks * self.row_shard
        self.out_rows = self.row_shard // CORES
        self.used = self.out_at + self.out_rows
        unit = 16 * depth
        self.rows = -(-self.used // unit) * unit
        self.rest_rows = self.rows - self.down_rows
        self.units = units
        self.group = units * self.row_shard

    def out_start(self, shard, member):
        return (
            lax.bitwise_xor(jnp.int32(shard) // self.units, member) * self.group
            + (shard % self.units) * self.row_shard
        )


def feed_kernel(pack, att_count, meta, x_ref, cot_ref, vec_ref, up_bias_ref, *refs):
    shards = pack.shards
    att_refs, refs = refs[:att_count], refs[att_count:]
    own_out, own_up, own_down = refs[:3]
    refs = refs[3:]
    pieces, refs = refs[: 2 * (shards - 1)], refs[2 * (shards - 1) :]
    out_ref, first_turned_ref, d_branch_ref, d_ffn_turned_ref, hidden_ref, d_pre_ref = refs[:6]
    att_turned_ref = refs[6]
    refs = refs[7:]
    d_att_refs, refs = refs[:att_count], refs[att_count:]
    sums_ref, up_sums_ref, w_out, w_up, w_down, slope, sems = refs
    step = pl.program_id(0)
    here, core, member = meta[1], meta[2], meta[3]
    feed_width = pack.feed_width

    def loads(kind):
        copies = []

        def add(source, target):
            copies.append(pltpu.make_async_copy(source, target, sems.at[kind, len(copies)]))

        if kind == 0:
            start = pl.multiple_of(pack.out_start(here, member), 16)
            add(own_out, w_out.at[pl.ds(start, pack.row_shard), :])
        elif kind == 1:
            start = pl.multiple_of(here * pack.row_shard, 16)
            add(own_up, w_up.at[pl.ds(start, pack.row_shard), :])
        else:
            start = pl.multiple_of(here * pack.feed_shard, 16)
            add(own_down, w_down.at[pl.ds(start, pack.feed_shard), :])
        for index, ref in enumerate(pieces):
            peer = lax.bitwise_xor(here, meta[8 + index])
            half = core if index < shards - 1 else 1 - core
            if kind == 0:
                start = pack.out_start(peer, member) + half * pack.out_rows
                start = pl.multiple_of(start, 16)
                add(
                    ref.at[pl.ds(pack.out_at, pack.out_rows), :],
                    w_out.at[pl.ds(start, pack.out_rows), :],
                )
            elif kind == 1:
                start = pl.multiple_of(peer * pack.row_shard, 16)
                for block in range(pack.blocks):
                    lane = pl.multiple_of(
                        (half * pack.blocks + block) * pack.model_width, CLUSTER_ROWS
                    )
                    add(
                        ref.at[pl.ds(pack.up_at + block * pack.row_shard, pack.row_shard), :],
                        w_up.at[pl.ds(start, pack.row_shard), pl.ds(lane, pack.model_width)],
                    )
            else:
                start = pl.multiple_of(peer * pack.feed_shard + half * pack.down_rows, 16)
                add(
                    ref.at[pl.ds(0, pack.down_rows), :],
                    w_down.at[pl.ds(start, pack.down_rows), :],
                )
        return copies

    @pl.when(step == 0)
    def _():
        for kind in range(3):
            for copy in loads(kind):
                copy.start()
        sums_ref[...] = jnp.zeros_like(sums_ref)
        up_sums_ref[...] = jnp.zeros_like(up_sums_ref)
        for copy in loads(0):
            copy.wait()

    bias_out, gain_one, gain_two = vec_ref[0:1, :], vec_ref[1:2, :], vec_ref[2:3, :]
    shift_one, shift_two, bias_down = vec_ref[3:4, :], vec_ref[4:5, :], vec_ref[5:6, :]
    att_width = att_refs[0].shape[1]
    summed = x_ref[...].astype(F32) + bias_out
    for index, ref in enumerate(att_refs):
        summed += dot(ref[...], w_out[index * att_width : (index + 1) * att_width, :])
    normed_one, inv_one = normalise(summed)
    first = normed_one * gain_one + shift_one
    first_low = first.astype(BF16)
    first_turned_ref[...] = jnp.transpose(first_low)
    for index, ref in enumerate(att_refs):
        att_turned_ref[index * att_width : (index + 1) * att_width, :] = jnp.transpose(ref[...])

    @pl.when(step == 0)
    def _():
        for kind in (1, 2):
            for copy in loads(kind):
                copy.wait()

    second = first + bias_down
    starts = list(range(0, feed_width, FF_BLOCK))

    def raised(base):
        lanes = slice(base, base + FF_BLOCK)
        return dot(first_low, w_up[:, lanes]) + up_bias_ref[:, lanes]

    pre = raised(starts[0])
    for index, base in enumerate(starts):
        lanes = slice(base, base + FF_BLOCK)
        pre_next = raised(starts[index + 1]) if index + 1 < len(starts) else None
        hidden, slope_now = gelu_parts(pre)
        hidden = hidden.astype(BF16)
        hidden_ref[:, lanes] = hidden
        slope[:, lanes] = slope_now
        second += dot(hidden, w_down[lanes, :])
        pre = pre_next
    normed_two, inv_two = normalise(second)
    out_ref[...] = (normed_two * gain_two + shift_two).astype(BF16)
    top = cot_ref[...].astype(F32)
    d_second = normalise_back(top, normed_two, inv_two, gain_two)
    d_ffn = d_second.astype(BF16)
    d_ffn_turned_ref[...] = jnp.transpose(d_ffn)
    d_first = d_second
    d_hidden = dot(d_ffn, w_down[0:FF_BLOCK, :], NT)
    for index, base in enumerate(starts):
        lanes = slice(base, base + FF_BLOCK)
        if index + 1 < len(starts):
            d_next = dot(d_ffn, w_down[starts[index + 1] : starts[index + 1] + FF_BLOCK, :], NT)
        d_pre = (d_hidden * slope[:, lanes]).astype(BF16)
        d_pre_ref[:, lanes] = d_pre
        up_sums_ref[:, lanes] += column_sum(d_pre.astype(F32))
        d_first += dot(d_pre, w_up[:, lanes], NT)
        d_hidden = d_next
    d_lower = normalise_back(d_first, normed_one, inv_one, gain_one)
    d_branch = d_lower.astype(BF16)
    d_branch_ref[...] = d_branch
    for index, ref in enumerate(d_att_refs):
        back = dot(d_branch, w_out[index * att_width : (index + 1) * att_width, :], NT)
        ref[...] = (0.5 * back).astype(BF16)
    sums_ref[0:1, :] += column_sum(d_branch.astype(F32))
    sums_ref[1:2, :] += column_sum(d_first * normed_one)
    sums_ref[2:3, :] += column_sum(top * normed_two)
    sums_ref[3:4, :] += column_sum(d_first)
    sums_ref[4:5, :] += column_sum(top)
    sums_ref[5:6, :] += column_sum(d_ffn.astype(F32))


def feed(pack, meta, x_own, cot_own, vectors, up_bias, att, own, pieces):
    row_count, model_width = x_own.shape
    feed_width = pack.feed_width
    att_width = att[0].shape[1]
    one = rows_of((ROW_BLOCK, model_width))
    wide = rows_of((ROW_BLOCK, feed_width))
    narrow = rows_of((ROW_BLOCK, att_width))
    turned = pl.BlockSpec((model_width, ROW_BLOCK), lambda i: (0, i))
    turned_shape = jax.ShapeDtypeStruct((model_width, row_count), BF16)

    def like(width):
        return jax.ShapeDtypeStruct((row_count, width), BF16)

    return pl.pallas_call(
        partial(feed_kernel, pack, len(att)),
        grid=(row_count // ROW_BLOCK,),
        in_specs=[IN_SMEM, one, one, whole(vectors.shape), whole(up_bias.shape)]
        + [narrow] * len(att)
        + [IN_HBM] * (3 + len(pieces)),
        out_specs=[one, turned, one, turned, wide, wide, turned]
        + [narrow] * len(att)
        + [whole((8, model_width)), whole((1, feed_width))],
        out_shape=[
            like(model_width),
            turned_shape,
            like(model_width),
            turned_shape,
            like(feed_width),
            like(feed_width),
            turned_shape,
        ]
        + [like(att_width)] * len(att)
        + [
            jax.ShapeDtypeStruct((8, model_width), F32),
            jax.ShapeDtypeStruct((1, feed_width), F32),
        ],
        scratch_shapes=[
            pltpu.VMEM((model_width, model_width), BF16),
            pltpu.VMEM((model_width, feed_width), BF16),
            pltpu.VMEM((feed_width, model_width), BF16),
            pltpu.VMEM((ROW_BLOCK, feed_width), F32),
            pltpu.SemaphoreType.DMA((3, 1 + pack.blocks * len(pieces))),
        ],
        name="feed",
        **params(
            40, 2 * row_count * model_width * (2 * model_width + 4 * feed_width), 40_000_000
        ),
    )(meta, x_own, cot_own, vectors, up_bias, *att, *own, *pieces)


def down_grads_kernel(pack, table, d_ffn_ref, hidden_ref, theirs_ref, mine_ref, made, sems):
    step = pl.program_id(0)
    core = table[0]

    def stores(shard):
        return [
            pltpu.make_async_copy(made.at[1 - core, shard], theirs_ref.at[shard], sems.at[0, shard]),
            pltpu.make_async_copy(made.at[core, shard], mine_ref.at[shard], sems.at[1, shard]),
        ]

    grad = dot(d_ffn_ref[...], hidden_ref[...]).astype(BF16)
    for half in range(CORES):
        for lane in range(0, pack.model_width, pack.feed_shard):
            begin = half * (pack.model_width // CORES) + lane // pack.feed_shard * pack.down_rows
            made[half, step, :, lane : lane + pack.feed_shard] = grad[
                begin : begin + pack.down_rows
            ]
    for copy in stores(step):
        copy.start()

    @pl.when(step == pack.shards - 1)
    def _():
        for shard in range(pack.shards):
            for copy in stores(shard):
                copy.wait()


def down_grads(pack, table, d_ffn, hidden):
    model_width, row_count = d_ffn.shape
    shape = (pack.shards, pack.down_rows, model_width)
    return pl.pallas_call(
        partial(down_grads_kernel, pack),
        grid_spec=pltpu.PrefetchScalarGridSpec(
            num_scalar_prefetch=1,
            grid=(pack.shards,),
            in_specs=[
                pl.BlockSpec(d_ffn.shape, lambda step, table: (0, 0)),
                pl.BlockSpec((row_count, pack.feed_shard), lambda step, table: (0, step)),
            ],
            out_specs=[ANYWHERE] * 2,
            scratch_shapes=[
                pltpu.VMEM((CORES,) + shape, BF16),
                pltpu.SemaphoreType.DMA((CORES, pack.shards)),
            ],
        ),
        out_shape=[jax.ShapeDtypeStruct(shape, BF16)] * 2,
        name="down_grads",
        **params(60, 2 * row_count * model_width * pack.feed_width, 10_000_000),
    )(table, d_ffn, hidden)


def rest_grads_kernel(
    pack, table, first_ref, d_pre_ref, att_ref, d_branch_ref, theirs_ref, mine_ref, *scratch
):
    att, d_branch, tile, made, in_sems, sems = scratch
    step = pl.program_id(0)
    core, member = table[0], table[1]
    shards, blocks = pack.shards, pack.blocks
    out_at = pack.out_at - pack.down_rows

    loads = [
        pltpu.make_async_copy(att_ref, att, in_sems.at[0]),
        pltpu.make_async_copy(d_branch_ref, d_branch, in_sems.at[1]),
    ]

    def store(half, start, rows, sem):
        there = (slice(None), pl.ds(start, rows), slice(None))

        def copy(target):
            return pltpu.make_async_copy(
                made.at[(half,) + there], target.at[there], sems.at[half, sem]
            )

        return copy

    def both(half, start, rows, sem, act):
        copy = store(half, start, rows, sem)

        @pl.when(core == half)
        def _():
            act(copy(mine_ref))

        @pl.when(core != half)
        def _():
            act(copy(theirs_ref))

    @pl.when(step == 0)
    def _():
        for copy in loads:
            copy.start()

    @pl.when(step < CORES * blocks)
    def _():
        grad = dot(first_ref[...], d_pre_ref[...]).astype(BF16)
        start = pl.multiple_of(step % blocks * pack.row_shard, 16)
        for shard in range(shards):
            made[step // blocks, shard, pl.ds(start, pack.row_shard), :] = grad[
                shard * pack.row_shard : (shard + 1) * pack.row_shard
            ]

    for half in range(CORES):

        @pl.when(step == (half + 1) * blocks - 1)
        def _(half=half):
            both(half, 0, out_at, 0, lambda copy: copy.start())

    @pl.when(step == CORES * blocks)
    def _():
        for copy in loads:
            copy.wait()
        tile[...] = dot(att[...], d_branch[...])
        spare = pack.rows - pack.used
        for half in range(CORES):
            for shard in range(shards):
                start = pack.out_start(shard, member) + half * pack.out_rows
                start = pl.multiple_of(start, 16)
                made[half, shard, out_at : out_at + pack.out_rows, :] = tile[
                    pl.ds(start, pack.out_rows), :
                ].astype(BF16)
                if spare:
                    made[half, shard, out_at + pack.out_rows :, :] = jnp.zeros(
                        (spare, pack.model_width), BF16
                    )
            both(half, out_at, pack.rest_rows - out_at, 1, lambda copy: copy.start())
        for half in range(CORES):
            both(half, 0, out_at, 0, lambda copy: copy.wait())
            both(half, out_at, pack.rest_rows - out_at, 1, lambda copy: copy.wait())


def rest_grads(pack, table, first_low, d_pre, att, d_branch, needs=()):
    model_width, row_count = first_low.shape
    shape = (pack.shards, pack.rest_rows, model_width)
    steps = CORES * pack.blocks
    return pl.pallas_call(
        gated(partial(rest_grads_kernel, pack), 5, needs),
        grid_spec=pltpu.PrefetchScalarGridSpec(
            num_scalar_prefetch=1,
            grid=(steps + 1,),
            in_specs=[
                pl.BlockSpec(first_low.shape, lambda step, table: (0, 0)),
                pl.BlockSpec(
                    (row_count, model_width),
                    lambda step, table: (0, jnp.minimum(step, steps - 1)),
                ),
            ]
            + [ANYWHERE] * (2 + len(needs)),
            out_specs=[ANYWHERE] * 2,
            scratch_shapes=[
                pltpu.VMEM((model_width, row_count), BF16),
                pltpu.VMEM((row_count, model_width), BF16),
                pltpu.VMEM((model_width, model_width), F32),
                pltpu.VMEM((CORES,) + shape, BF16),
                pltpu.SemaphoreType.DMA((2,)),
                pltpu.SemaphoreType.DMA((CORES, 2)),
            ],
        ),
        out_shape=[jax.ShapeDtypeStruct(shape, BF16)] * 2,
        name="rest_grads",
        **params(60, 2 * row_count * model_width * (pack.feed_width + model_width), 10_000_000),
    )(table, first_low, d_pre, att, d_branch, *needs)


def qkv_grads_kernel(rounds, x_refs_then, *refs):
    refs = (x_refs_then,) + refs
    x_refs, grad_refs = refs[:rounds], refs[rounds : 2 * rounds]
    small_ref, out_ref = refs[2 * rounds :]
    shards, rows, _ = out_ref.shape
    row_shard = rows - small_ref.shape[1]
    total, sums = None, None
    for x_ref, grad_ref in zip(x_refs, grad_refs):
        grads = grad_ref[...]
        term = dot(x_ref[...], grads)
        down = column_sum(grads.astype(F32))
        total = term if total is None else total + term
        sums = down if sums is None else sums + down
    total = total.astype(BF16)
    row = lax.broadcasted_iota(jnp.int32, small_ref.shape[1:], 0)
    for shard in range(shards):
        out_ref[shard, :row_shard, :] = total[shard * row_shard : (shard + 1) * row_shard]
        last = jnp.where(row == BIAS_ROW, sums, small_ref[shard])
        out_ref[shard, row_shard:, :] = last.astype(BF16)


def qkv_grads(x_turned, grads, small, row_shard, needs=()):
    rounds = len(grads)
    model_width, positions = x_turned[0].shape
    cols = grads[0].shape[1]
    shards, extra, _ = small.shape
    block = GRAD_LANES if cols % GRAD_LANES == 0 else cols
    return pl.pallas_call(
        gated(partial(qkv_grads_kernel, rounds), 2 * rounds + 1, needs),
        grid=(cols // block,),
        in_specs=[whole((model_width, positions))] * rounds
        + [pl.BlockSpec((positions, block), lambda i: (0, i))] * rounds
        + [pl.BlockSpec((shards, extra, block), lambda i: (0, 0, i))]
        + [ANYWHERE] * len(needs),
        out_specs=pl.BlockSpec((shards, row_shard + extra, block), lambda i: (0, 0, i)),
        out_shape=jax.ShapeDtypeStruct((shards, row_shard + extra, cols), BF16),
        name="qkv_grads",
        **params(60, 2 * rounds * positions * model_width * cols, 18_000_000),
    )(*x_turned, *grads, small, *needs)


def add_picked_kernel(count, first, table, *refs):
    in_refs, out_refs = refs[:count], refs[count:]
    if count == 2:
        total = in_refs[0][...] + in_refs[1][...]
    else:
        total = in_refs[0][...].astype(F32)
        for ref in in_refs[1:]:
            total = total + ref[...].astype(F32)
        total = total.astype(BF16)
    if len(out_refs) == 1:
        out_refs[0][...] = total
        return

    @pl.when(pl.program_id(0) < first)
    def _():
        out_refs[0][...] = total

    @pl.when(pl.program_id(0) >= first)
    def _():
        out_refs[1][...] = total


def add_picked(table, arrays, steps, first=None, needs=(), work=0):
    _, rows, cols = arrays[0].shape
    parts = 2 if rows % 32 == 0 and steps == 1 else 1
    block = (1, rows // parts, cols)
    spec = [
        pl.BlockSpec(block, lambda s, p, t, k=k: (t[k * steps + s], p, 0))
        for k in range(len(arrays))
    ]
    if first is None:
        out_specs = [pl.BlockSpec(block, lambda s, p, t: (s, p, 0))]
        counts = [steps]
    else:
        out_specs = [
            pl.BlockSpec(
                block,
                lambda s, p, t: (
                    jnp.minimum(s, first - 1),
                    jnp.where(s < first, p, parts - 1),
                    0,
                ),
            ),
            pl.BlockSpec(
                block,
                lambda s, p, t: (jnp.maximum(s - first, 0), jnp.where(s < first, 0, p), 0),
            ),
        ]
        counts = [first, steps - first]
    return pl.pallas_call(
        gated(partial(add_picked_kernel, len(arrays), first), 1 + len(arrays), needs),
        grid_spec=pltpu.PrefetchScalarGridSpec(
            num_scalar_prefetch=1,
            grid=(steps, parts),
            in_specs=spec + [ANYWHERE] * len(needs),
            out_specs=out_specs,
        ),
        out_shape=[jax.ShapeDtypeStruct((n, rows, cols), BF16) for n in counts],
        name="add_picked",
        compiler_params=pltpu.CompilerParams(
            dimension_semantics=("arbitrary", "arbitrary"),
            vmem_limit_bytes=(60 if steps > 1 else 12) * MIB,
        ),
        cost_estimate=pl.CostEstimate(flops=work, bytes_accessed=1_000_000, transcendentals=0),
    )(table, *arrays, *needs)


def join_kernel(count, down_kept, down_landed, rest_kept, rest_landed, *outs):
    rows = down_kept.shape[1]
    for index in range(count):
        target = outs[1 - index % 2] if count > 1 else outs[0]
        place_now = index // 2
        target[place_now, :rows, :] = down_kept[index] + down_landed[index]
        target[place_now, rows:, :] = rest_kept[index] + rest_landed[index]


def join(kept, landed, needs=()):
    count = kept[0].shape[0]
    rows = kept[0].shape[1] + kept[1].shape[1]
    shape = jax.ShapeDtypeStruct(((count + 1) // 2, rows, kept[0].shape[2]), BF16)
    vmem = pl.BlockSpec(memory_space=pltpu.VMEM)
    outs = pl.pallas_call(
        gated(partial(join_kernel, count), 4, needs),
        in_specs=[vmem] * 4 + [ANYWHERE] * len(needs),
        out_specs=[vmem] * min(count, 2),
        out_shape=[shape] * min(count, 2),
        name="join",
        compiler_params=pltpu.CompilerParams(vmem_limit_bytes=24 * MIB),
        cost_estimate=pl.CostEstimate(flops=0, bytes_accessed=200_000, transcendentals=0),
    )(kept[0], landed[0], kept[1], landed[1], *needs)
    return outs if count > 1 else (None, outs[0])


def stack_kernel(count, *refs):
    for index in range(count):
        refs[count][index] = refs[index][...]


def home_kernel(count, meta, *refs):
    out_ref = refs[count]
    rows = refs[0].shape[0]
    for index in range(count):
        start = pl.multiple_of((meta[5] + index) % count * rows, 16)
        out_ref[pl.ds(start, rows), :] = refs[index][...].astype(out_ref.dtype)


def home_rows(meta, landed, dtype, needs=()):
    rows, cols = landed[0].shape
    vmem = pl.BlockSpec(memory_space=pltpu.VMEM)
    return pl.pallas_call(
        gated(partial(home_kernel, len(landed)), 1 + len(landed), needs),
        in_specs=[IN_SMEM] + [vmem] * len(landed) + [ANYWHERE] * len(needs),
        out_specs=vmem,
        out_shape=jax.ShapeDtypeStruct((len(landed) * rows, cols), dtype),
        name="home_rows",
        compiler_params=pltpu.CompilerParams(vmem_limit_bytes=60 * MIB),
        cost_estimate=pl.CostEstimate(flops=0, bytes_accessed=100_000, transcendentals=0),
    )(meta, *landed, *needs)


def split_kernel(in_ref, *out_refs):
    rows = out_refs[0].shape[0]
    for index, ref in enumerate(out_refs):
        ref[...] = in_ref[index * rows : (index + 1) * rows, :]


def split_rows(value, count, needs=()):
    rows = value.shape[0] // count
    vmem = pl.BlockSpec(memory_space=pltpu.VMEM)
    return pl.pallas_call(
        gated(split_kernel, 1, needs),
        in_specs=[vmem] + [ANYWHERE] * len(needs),
        out_specs=[vmem] * count,
        out_shape=[jax.ShapeDtypeStruct((rows, value.shape[1]), value.dtype)] * count,
        name="split_rows",
        compiler_params=pltpu.CompilerParams(vmem_limit_bytes=12 * MIB),
        cost_estimate=pl.CostEstimate(flops=0, bytes_accessed=100_000, transcendentals=0),
    )(value, *needs)


def stack_up(pieces, needs=()):
    vmem = pl.BlockSpec(memory_space=pltpu.VMEM)
    return pl.pallas_call(
        gated(partial(stack_kernel, len(pieces)), len(pieces), needs),
        in_specs=[vmem] * len(pieces) + [ANYWHERE] * len(needs),
        out_specs=vmem,
        out_shape=jax.ShapeDtypeStruct((len(pieces),) + pieces[0].shape, BF16),
        name="stack_up",
        compiler_params=pltpu.CompilerParams(vmem_limit_bytes=24 * MIB),
        cost_estimate=pl.CostEstimate(flops=0, bytes_accessed=100_000, transcendentals=0),
    )(*pieces, *needs)


def unpack_kernel(pack, depth, meta, mine_ref, other_ref, down_ref, up_ref, out_ref, ordered):
    core, level = meta[2], meta[4]
    rows = pack.rows // depth
    for mask in range(depth):
        start = pl.multiple_of(lax.bitwise_xor(level, mask) * rows, 16)
        ordered[core, pl.ds(start, rows), :] = mine_ref[mask]
        ordered[1 - core, pl.ds(start, rows), :] = other_ref[mask]
    turned = []
    for half in range(CORES):
        for lane in range(0, pack.model_width, pack.feed_shard):
            turned.append(ordered[half, : pack.down_rows, lane : lane + pack.feed_shard])
    down_ref[...] = jnp.transpose(jnp.concatenate(turned, axis=0)).astype(F32)
    for half in range(CORES):
        for block in range(pack.blocks):
            lane = (half * pack.blocks + block) * pack.model_width
            start = pack.up_at + block * pack.row_shard
            up_ref[:, lane : lane + pack.model_width] = ordered[
                half, start : start + pack.row_shard, :
            ].astype(F32)
        out_ref[half * pack.out_rows : (half + 1) * pack.out_rows, :] = ordered[
            half, pack.out_at : pack.out_at + pack.out_rows, :
        ].astype(F32)


def unpack(pack, depth, meta, mine, other):
    vmem = pl.BlockSpec(memory_space=pltpu.VMEM)
    return pl.pallas_call(
        partial(unpack_kernel, pack, depth),
        in_specs=[IN_SMEM, vmem, vmem],
        out_specs=[vmem] * 3,
        out_shape=[
            jax.ShapeDtypeStruct((pack.feed_shard, pack.model_width), F32),
            jax.ShapeDtypeStruct((pack.row_shard, pack.feed_width), F32),
            jax.ShapeDtypeStruct((pack.row_shard, pack.model_width), F32),
        ],
        scratch_shapes=[pltpu.VMEM((CORES, pack.rows, pack.model_width), BF16)],
        name="unpack",
        compiler_params=pltpu.CompilerParams(vmem_limit_bytes=60 * MIB),
        cost_estimate=pl.CostEstimate(flops=0, bytes_accessed=10_000_000, transcendentals=0),
    )(meta, mine, other)


def unpack_qkv_kernel(meta, mine_ref, other_ref, grad_ref, bias_ref, small_ref):
    member = meta[3]
    row_shard, width = grad_ref.shape[0], grad_ref.shape[1] // 3
    part = mine_ref.shape[1] // 3
    for ref, at in ((mine_ref, member), (other_ref, 1 - member)):
        for kind in range(3):
            lane = pl.multiple_of(kind * width + at * part, CLUSTER_ROWS)
            from_lanes = slice(kind * part, (kind + 1) * part)
            grad_ref[:, pl.ds(lane, part)] = ref[:row_shard, from_lanes].astype(F32)
            lane = pl.multiple_of(at * part, CLUSTER_ROWS)
            bias_ref[kind : kind + 1, pl.ds(lane, part)] = ref[row_shard:, from_lanes].astype(F32)[
                BIAS_ROW : BIAS_ROW + 1
            ]
    small_ref[...] = (mine_ref[row_shard:, :].astype(F32) + other_ref[row_shard:, :].astype(F32))[
        :BIAS_ROW
    ]


def unpack_qkv(meta, mine, other, row_shard, needs=()):
    cols = mine.shape[1]
    vmem = pl.BlockSpec(memory_space=pltpu.VMEM)
    return pl.pallas_call(
        gated(unpack_qkv_kernel, 3, needs),
        in_specs=[IN_SMEM, vmem, vmem] + [ANYWHERE] * len(needs),
        out_specs=[vmem] * 3,
        out_shape=[
            jax.ShapeDtypeStruct((row_shard, CORES * cols), F32),
            jax.ShapeDtypeStruct((3, CORES * cols // 3), F32),
            jax.ShapeDtypeStruct((BIAS_ROW, cols), F32),
        ],
        name="unpack_qkv",
        compiler_params=pltpu.CompilerParams(vmem_limit_bytes=60 * MIB),
        cost_estimate=pl.CostEstimate(flops=0, bytes_accessed=200_000, transcendentals=0),
    )(meta, mine, other, *needs)


def tie(*values):
    return lax.optimization_barrier(values)


def body(
    tokens,
    cotangent,
    perms,
    unit_kind,
    w_qkv,
    bias_qv,
    w_out,
    bias_out,
    ln_gain,
    ln_bias,
    w_up,
    bias_up,
    w_down,
    bias_down,
):
    shards = lax.axis_size("fsdp")
    groups = lax.axis_size("dp")
    here = lax.axis_index("fsdp")
    dp_index = lax.axis_index("dp")
    core = dp_index % CORES
    level = dp_index // CORES
    depth = groups // CORES
    units, rounds, unit_len = perms.shape
    per_device = unit_len // shards
    model_width = tokens.shape[1]
    feed_width = w_up.shape[1]
    row_shard = model_width // shards
    members = shards // units
    member_rows = unit_len // members
    head_cols = model_width // members
    padded = -(-head_cols // CLUSTER_ROWS) * CLUSTER_ROWS
    spot = here * CORES + core
    home_core = spot // shards
    unit = (spot // members) % units
    member = spot % members
    pack = Pack(model_width, feed_width, shards, units, depth)
    bits = [1 << k for k in range(shards.bit_length() - 1)]
    bit_orders = (bits, bits[::-1])

    def plane_pairs(target):
        pairs = []
        for z in range(depth):
            for f_index in range(shards):
                for c_index in range(CORES):
                    f_new, c_new = target(f_index, c_index)
                    pairs.append(
                        (
                            (z * CORES + c_index) * shards + f_index,
                            (z * CORES + c_new) * shards + f_new,
                        )
                    )
        return pairs

    def send(value, pairs):
        return lax.ppermute(value, ("dp", "fsdp"), pairs)

    def cross(value, mask):
        return send(value, plane_pairs(lambda f, c: divmod((f * CORES + c) ^ mask, CORES)))

    def trade(value, stage):
        return send(value, plane_pairs(lambda f, c: (f ^ bit_orders[c][stage], c)))

    def trade_mask(index, which):
        mask = 0
        for stage in range(len(bits)):
            if index >> stage & 1:
                mask ^= bit_orders[which][stage]
        return mask

    def climb(value, mask):
        plane = CORES * shards
        pairs = []
        for z in range(depth):
            for rest in range(plane):
                pairs.append((z * plane + rest, (z ^ mask) * plane + rest))
        return send(value, pairs)

    def outward(step):
        def target(f, c):
            place_now = (c * units + (f % units + step) % units) * members + f // units
            return divmod(place_now, CORES)

        return plane_pairs(target)

    def homeward(step):
        return [(b, a) for a, b in outward(step)]

    def bring_start(value):
        blocks = value.reshape(units, per_device, model_width)
        return [
            lax.dynamic_index_in_dim(blocks, (here % units + step) % units, axis=0, keepdims=False)
            for step in range(units)
        ]

    def bring(chosen):
        return jnp.concatenate(
            [send(chosen[step], outward(step)) for step in range(units)], axis=0
        )

    def send_home(blocks):
        return [send(blocks[step], homeward(step)) for step in range(units)]

    x_chosen = bring_start(tokens)
    x_own = bring(x_chosen)
    small = jnp.concatenate(
        [
            bias_qv.reshape(-1),
            bias_out,
            ln_gain.reshape(-1),
            ln_bias.reshape(-1),
            bias_up,
            bias_down,
        ]
    )
    small_rows = -(-small.shape[0] // (3 * padded))
    small_block = jnp.pad(
        jnp.pad(small, (0, small_rows * 3 * padded - small.shape[0])).reshape(
            small_rows, 3 * padded
        ),
        ((0, 16 - small_rows), (0, 0)),
    )
    def columns_for(offset):
        start = lax.bitwise_xor(member, offset) * head_cols
        blocks = [
            jnp.pad(
                lax.dynamic_slice(
                    w_qkv, (0, kind * model_width + start), (row_shard, head_cols)
                ),
                ((0, 0), (0, padded - head_cols)),
            )
            for kind in range(3)
        ]
        return jnp.concatenate([jnp.concatenate(blocks, axis=1), small_block], axis=0)

    offsets = [(CORES * m) % members for m in range(shards)]
    kinds = sorted(set(offsets))
    order_pack = jnp.concatenate(
        [perms.reshape(-1), jnp.broadcast_to(unit_kind[:, None], (units, 128)).reshape(-1)]
    )
    order_other = cross(order_pack, 1)
    *tied, order_other = tie(*[columns_for(offset) for offset in kinds], order_other)
    piece_kinds = dict(zip(kinds, tied))
    x_pieces = [x_own] + [cross(x_own, mask) for mask in range(1, members)]
    if members == CORES:
        qkv_pieces = {0: piece_kinds[0]}
        for stage in range(len(bits)):
            qkv_pieces[1 << stage] = trade(piece_kinds[0], stage)
        for stage in range(1, len(bits)):
            for index in range(1, 1 << stage):
                qkv_pieces[index | 1 << stage] = trade(qkv_pieces[index], stage)
        qkv_pieces = [qkv_pieces[index] for index in range(shards)]
        qkv_masks = [[trade_mask(index, which) for index in range(shards)] for which in (0, 1)]
    else:
        qkv_pieces = [piece_kinds[0]] + [
            cross(piece_kinds[offsets[m]], CORES * m) for m in range(1, shards)
        ]
        qkv_masks = [list(range(shards))] * 2
    order_pack = jnp.where(home_core == core, order_pack, order_other)
    order_count = units * rounds * unit_len
    unit_perm = lax.dynamic_index_in_dim(
        order_pack[:order_count].reshape(units, rounds * unit_len), unit, 0, keepdims=False
    )
    kind_now = lax.dynamic_index_in_dim(
        order_pack[order_count:].reshape(units, 128), unit, 0, keepdims=False
    )[0]
    owner = unit_perm // per_device
    order = (
        lax.bitwise_xor(owner // units, member) * units + (unit - owner % units) % units
    ) * per_device + unit_perm % per_device
    order = order.reshape(rounds, unit_len)
    order = jnp.where(core == 0, order, order[::-1])
    order_row = order.reshape(1, rounds * unit_len)
    order = order.reshape(-1, CLUSTER_ROWS)
    x_here = arrange(order, x_pieces, unit_len, 0)
    x_now = [x_here, cross(x_here, 1)]
    own_masks = [
        jnp.where(core == 0, trade_mask(i, 0), trade_mask(i, 1)) for i in range(1, shards)
    ]
    other_masks = [
        jnp.where(core == 0, trade_mask(i, 1), trade_mask(i, 0)) for i in range(1, shards)
    ]
    zero = jnp.int32(0)
    meta = jnp.stack(
        [kind_now, here, core, member, level, here % units, zero, zero]
        + own_masks
        + other_masks
        + [jnp.where(core == 0, first, second) for first, second in zip(*qkv_masks)]
    ).astype(jnp.int32)

    def half_of(value, axis, length, at):
        return lax.dynamic_slice_in_dim(value, at * length, length, axis=axis)

    packed = jnp.concatenate(
        [half_of(w_down, 0, pack.down_rows, core)]
        + [
            half_of(w_up, 1, model_width, core * pack.blocks + block)
            for block in range(pack.blocks)
        ]
        + [half_of(w_out, 0, pack.out_rows, core)],
        axis=0,
    )
    order_rows = unit_len // CLUSTER_ROWS
    arranged, probs, mixtures, x_turned = [], [], [], []
    *tied, packed, x_now[0] = tie(*qkv_pieces[1:], packed, x_now[0])
    qkv_pieces = qkv_pieces[:1] + tied
    smalls = jnp.stack(
        [
            piece[row_shard : row_shard + small_rows].reshape(-1)[: small.shape[0]]
            for piece in qkv_pieces
        ]
    )
    spots_of = [[masks.index(mask) for mask in range(shards)] for masks in qkv_masks]
    spots_of = jnp.where(core == 0, jnp.array(spots_of[0]), jnp.array(spots_of[1]))
    spots_of = jnp.take(spots_of, lax.bitwise_xor(here, jnp.arange(shards)))
    smalls = jnp.take(smalls, spots_of, axis=0).astype(F32)

    def vectors_at(start, count, length):
        part = smalls[:, start * row_shard : start * row_shard + count * length]
        return (
            part.reshape(shards, count, length).transpose(1, 0, 2).reshape(count, shards * length)
        )

    my_bias = lax.dynamic_index_in_dim(
        vectors_at(0, 2, row_shard).reshape(2, members, head_cols), member, 1, keepdims=False
    )
    my_bias = jnp.pad(my_bias, ((0, 0), (0, padded - head_cols)))
    my_bias = jnp.stack([my_bias[0], jnp.zeros_like(my_bias[0]), my_bias[1]]).reshape(1, -1)
    up_bias = vectors_at(7, 1, feed_width // shards)
    down_bias = smalls[:, small.shape[0] - row_shard :].reshape(1, model_width)
    vectors = jnp.concatenate(
        [vectors_at(2, 5, row_shard), down_bias, jnp.zeros((2, model_width), F32)], axis=0
    )

    weight_pieces = {0: packed}
    for stage in range(len(bits)):
        weight_pieces[1 << stage] = trade(packed, stage)
    for index in range(rounds):
        results = attend(meta, x_now[index], my_bias, qkv_pieces, row_shard, mixtures[-1:])
        for kept, result in zip((arranged, probs, mixtures, x_turned), results):
            kept.append(result)
    cot_now, mixtures[0] = tie(cotangent, mixtures[0])
    cot_landed = [
        send(value, outward(step)) for step, value in enumerate(bring_start(cot_now))
    ]
    cot_own = jnp.concatenate(cot_landed, axis=0)
    for stage in range(1, len(bits)):
        for index in range(1, 1 << stage):
            weight_pieces[index | 1 << stage] = trade(weight_pieces[index], stage)
    att_there, att_sent = [], []
    for mask in range(1, members):
        there = place(
            order_row, mixtures, mask * member_rows, member_rows, 0.5, needs=cot_landed
        )
        att_sent.append(there)
        att_there.append(cross(there[:, :head_cols], mask))
    att_here = place(order_row, mixtures, 0, member_rows, 0.5, needs=att_sent)

    direct = [weight_pieces[index] for index in range(1, shards)]
    swapped = [cross(piece, 1) for piece in direct[:-1]]
    last_piece, att_here = tie(direct[-1], att_here)
    swapped.append(cross(last_piece, 1))
    att_raw = [att_here[:, :head_cols]] + att_there
    if head_cols % CLUSTER_ROWS:
        att_raw = [jnp.concatenate(att_raw, axis=1)]
    block_out, first_low, d_branch, d_ffn, hidden, d_pre, att_turned, *rest = feed(
        pack,
        meta,
        x_own,
        cot_own,
        vectors,
        up_bias,
        att_raw,
        [w_out, w_up, w_down],
        direct + swapped,
    )
    d_att, (row_sums, up_sums) = rest[: len(att_raw)], rest[len(att_raw) :]
    if head_cols % CLUSTER_ROWS:
        d_att = [d_att[0][:, mask * head_cols : (mask + 1) * head_cols] for mask in range(members)]
    d_att = [d_att[0]] + [cross(d_att[mask], mask) for mask in range(1, members)]
    d_att = [jnp.pad(piece, ((0, 0), (0, padded - head_cols))) for piece in d_att]

    table = jnp.stack([core, member]).astype(jnp.int32)
    sending = [index for index in range(shards) if index & 1]
    keeping = [index for index in range(shards) if not index & 1]
    slots = jnp.stack(
        [
            lax.bitwise_xor(here, jnp.where(core == 0, trade_mask(i, 0), trade_mask(i, 1)))
            for i in sending + keeping
        ]
    )
    slots = jnp.concatenate([slots, slots]).astype(jnp.int32)

    def pair_sum(mine, theirs, needs):
        return add_picked(
            slots, [mine, cross(theirs, 1)], shards, len(sending), needs, 20_000_000_000
        )

    theirs_down, mine_down = down_grads(pack, table, d_ffn, hidden)
    theirs_rest, mine_rest = rest_grads(
        pack, table, first_low, d_pre, att_turned, d_branch, [theirs_down]
    )
    down_going, down_kept = pair_sum(mine_down, theirs_down, [theirs_rest])
    rest_going, rest_kept = pair_sum(mine_rest, theirs_rest, [down_going] + d_att[1:])

    def merge(kept, landed, *needs):
        count = kept.shape[0]
        if count == 1:
            table = jnp.zeros((2,), jnp.int32)
            return None, add_picked(table, [kept, landed], 1, None, needs)[0]
        order_now = [i for i in range(count) if i & 1] + [i for i in range(count) if not i & 1]
        table = jnp.array(order_now * 2, jnp.int32)
        return add_picked(table, [kept, landed], count, count // 2, needs)

    grads, d_x = [None] * rounds, [None] * rounds
    needs = [rest_going]
    blocks = unit_len // POS_BLOCK
    spans = [(index, (0, blocks)) for index in reversed(range(rounds))]
    for turn, (index, span) in enumerate(spans):
        grads[index], d_x[index], token = attend_back(
            meta,
            order,
            arranged[index],
            probs[index],
            d_att,
            qkv_pieces,
            row_shard,
            index * order_rows,
            needs,
            span,
            [],
        )
        if turn == 0:
            d_x_there = cross(d_x[index], 1)
            going, kept = join(
                [down_kept, rest_kept], [trade(down_going, 0), trade(rest_going, 0)], [token]
            )
            output_landed = send_home(split_rows(block_out, units, [token]))
            needs = [kept]
    for stage in range(1, len(bits)):
        going, kept = merge(kept, trade(going, stage), token)

    def level_pieces(block):
        return block.reshape((depth, block.shape[0] // depth) + block.shape[1:])

    def level_scatter(cut):
        return [
            climb(
                lax.dynamic_index_in_dim(cut, lax.bitwise_xor(level, mask), 0, keepdims=False), mask
            )
            for mask in range(1, depth)
        ]

    def level_gather(piece):
        pieces = {0: piece}
        mask = depth // 2
        while mask:
            pieces[mask] = climb(piece, mask)
            mask //= 2
        return pieces

    def level_forward(pieces):
        for index in sorted(range(depth), key=lambda value: value.bit_count()):
            if index not in pieces:
                low = index & -index
                pieces[index] = climb(pieces[index ^ low], low)
        return [pieces[index] for index in range(depth)]

    def by_shard(value):
        count, length = value.shape
        return (
            value.reshape(count, shards, length // shards)
            .transpose(1, 0, 2)
            .reshape(shards, count * length // shards)
        )

    small_grad = jnp.concatenate(
        [by_shard(row_sums[:5]), by_shard(up_sums), by_shard(row_sums[5:6])], axis=1
    )
    small_length = small_grad.shape[1]
    small_lanes = 3 * head_cols
    small_grad = jnp.pad(small_grad, ((0, 0), (0, BIAS_ROW * small_lanes - small_length)))
    small_grad = jnp.pad(
        small_grad.reshape(shards, BIAS_ROW, small_lanes), ((0, 0), (0, 16 - BIAS_ROW), (0, 0))
    )
    extra_rows = 16
    if padded == head_cols:
        joined = qkv_grads(
            x_turned, grads, small_grad, row_shard, output_landed + [kept]
        )
    else:
        qkv_grad = dot(x_turned[0], grads[0]) + dot(x_turned[1], grads[1])
        qkv_grad = qkv_grad.reshape(shards, row_shard, 3, padded)[..., :head_cols]
        bias_sum = sum(jnp.sum(value.astype(F32), axis=0) for value in grads)
        bias_sum = bias_sum.reshape(3, padded)[:, :head_cols].reshape(small_lanes)
        small_grad = small_grad.at[:, BIAS_ROW].set(bias_sum[None])
        joined = jnp.concatenate(
            [qkv_grad.reshape(shards, row_shard, small_lanes), small_grad], axis=1
        ).astype(BF16)
    cut = level_pieces(kept[0])
    landed = level_scatter(cut)
    classes = max(1, members // CORES)
    d_x_parts = [d_x[0], d_x_there]
    order_mine = order_row[:, :unit_len]
    if classes == 1:
        slots_held = jnp.stack(
            [
                lax.bitwise_xor(here, jnp.where(core == 0, trade_mask(i, 0), trade_mask(i, 1)))
                for i in range(shards)
            ]
        )
        held = jnp.stack(
            [
                lax.dynamic_index_in_dim(joined, slots_held[i], 0, keepdims=False)
                for i in range(0, shards, 2)
            ]
        )
        leaving = jnp.stack(
            [
                lax.dynamic_index_in_dim(joined, slots_held[i], 0, keepdims=False)
                for i in range(1, shards, 2)
            ]
        )
        totals = None
    else:
        totals = [None] * classes
        for m in range(shards):
            offset = offsets[m] // CORES
            piece = lax.dynamic_index_in_dim(joined, lax.bitwise_xor(here, m), 0, keepdims=False)
            piece = (piece if m == 0 else cross(piece, CORES * m)).astype(F32)
            totals[offset] = piece if totals[offset] is None else totals[offset] + piece

    d_there = [
        place(
            order_mine,
            d_x_parts,
            mask * member_rows,
            member_rows,
            added=True,
            needs=[joined],
        )
        for mask in range(1, members)
    ]
    if depth > 1:
        picks = jnp.concatenate([level[None], jnp.zeros((depth - 1,), level.dtype)])
        (kept,) = add_picked(
            picks.astype(jnp.int32),
            [cut] + [piece[None] for piece in landed],
            1,
            None,
            d_there,
        )
    gathered = level_gather(kept[0]) if depth > 1 else {0: cut[0]}
    early = [kept] + d_there
    if totals is None:
        held = held + trade(leaving, 0)
        early.append(held)
    d_here = place(
        order_mine,
        d_x_parts,
        0,
        member_rows,
        1.0,
        F32,
        d_branch,
        added=True,
        needs=early,
    )
    d_inputs = d_here
    for mask, there in enumerate(d_there, 1):
        d_inputs = d_inputs + cross(there, mask).astype(F32)
    d_inputs = d_inputs.astype(BF16)
    home = send_home(d_inputs.reshape(units, per_device, model_width))
    last = d_inputs
    if totals is None:
        for stage in range(1, len(bits)):
            held = held[::2] + trade(held[1::2], stage)
        masks = [mask for mask in gathered if mask]
        *tied, held = tie(*[gathered[mask] for mask in masks], held)
        gathered.update(zip(masks, tied))
        last = held
        totals = [held[0]]
    output = home_rows(meta, output_landed, BF16, [last])
    totals = jnp.concatenate(totals, axis=0).astype(BF16)
    rows_each = row_shard + extra_rows
    if depth > 1:
        halves = totals.reshape((2, totals.shape[0] // 2) + totals.shape[1:])
        side = level % 2
        mine = lax.dynamic_index_in_dim(halves, side, 0, keepdims=False)
        theirs = lax.dynamic_index_in_dim(halves, 1 - side, 0, keepdims=False)
        half = (mine.astype(F32) + climb(theirs, 1).astype(F32)).astype(BF16)
        mask = 2
        while mask < depth:
            half = (half.astype(F32) + climb(half, mask).astype(F32)).astype(BF16)
            mask *= 2
        *home, output, half = tie(*home, output, half)
        other_half = climb(half, 1)
        d_inputs = home_rows(meta, home, F32)
        d_inputs, other_half = tie(d_inputs, other_half)
        totals = jnp.concatenate(
            [
                jnp.where(side == 0, half, other_half),
                jnp.where(side == 0, other_half, half),
            ],
            axis=0,
        )
    else:
        d_inputs = home_rows(meta, home, F32)
    stacked = stack_up(level_forward(gathered))
    grad_down, grad_up, grad_out = unpack(pack, depth, meta, stacked, cross(stacked, 1))
    if padded == head_cols and members == CORES:
        grad_qkv, bias_out_row, smalls_out = unpack_qkv(
            meta, totals, cross(totals, 1), row_shard, [grad_down]
        )
        smalls_out = smalls_out.reshape(-1)[:small_length]
        bias_out_row = lax.dynamic_slice(bias_out_row, (0, here * row_shard), (3, row_shard))
    else:
        landed = jnp.stack([totals, cross(totals, 1)], axis=0).reshape(
            CORES, classes, rows_each, 3 * head_cols
        )
        smalls_out = jnp.sum(
            landed[:, :, row_shard : row_shard + BIAS_ROW].astype(F32), axis=(0, 1)
        ).reshape(-1)[:small_length]
        landed = (
            landed.transpose(1, 0, 2, 3)
            .reshape(members, rows_each, 3, head_cols)[:, : row_shard + BIAS_ROW + 1]
        )
        if members == 2:
            swap = member == 1
            landed = jnp.stack(
                [
                    jnp.where(swap, landed[1], landed[0]),
                    jnp.where(swap, landed[0], landed[1]),
                ]
            )
        else:
            landed = jnp.take(landed, lax.bitwise_xor(member, jnp.arange(members)), axis=0)
        grad_qkv = landed[:, :row_shard].transpose(1, 2, 0, 3)
        grad_qkv = grad_qkv.reshape(row_shard, 3 * model_width).astype(F32)
        bias_out_row = landed[:, row_shard + BIAS_ROW].astype(F32).transpose(1, 0, 2)
        bias_out_row = lax.dynamic_slice(
            bias_out_row.reshape(3, model_width), (0, here * row_shard), (3, row_shard)
        )

    feed_shard = feed_width // shards
    spots = [0, row_shard, 3 * row_shard, 5 * row_shard]
    return (
        output,
        d_inputs,
        grad_qkv,
        bias_out_row[::2],
        grad_out,
        smalls_out[spots[0] : spots[1]],
        smalls_out[spots[1] : spots[2]].reshape(2, row_shard),
        smalls_out[spots[2] : spots[3]].reshape(2, row_shard),
        grad_up,
        smalls_out[spots[3] : spots[3] + feed_shard],
        grad_down,
        smalls_out[spots[3] + feed_shard :],
    )


def solution(mesh):
    placed = (
        P(("dp", "fsdp"), None),
        P(("dp", "fsdp"), None),
        P("dp", None, None),
        P("dp"),
        P("fsdp", None),
        P(None, "fsdp"),
        P("fsdp", None),
        P("fsdp"),
        P(None, "fsdp"),
        P(None, "fsdp"),
        P("fsdp", None),
        P("fsdp"),
        P("fsdp", None),
        P("fsdp"),
    )
    return jax.shard_map(
        body,
        mesh=mesh,
        in_specs=placed,
        out_specs=(
            P(("dp", "fsdp"), None),
            P(("dp", "fsdp"), None),
            P("fsdp", None),
            P(None, "fsdp"),
            P("fsdp", None),
            P("fsdp"),
            P(None, "fsdp"),
            P(None, "fsdp"),
            P("fsdp", None),
            P("fsdp"),
            P("fsdp", None),
            P("fsdp"),
        ),
        check_vma=False,
    )
```

```python
from functools import partial

import jax
import jax.numpy as jnp
from jax import lax
from jax.experimental import pallas as pl
from jax.experimental.pallas import tpu as pltpu
from jax.sharding import PartitionSpec as P

HEAD_DIM = 64
CORES = 2
NEG_FILL = -1000000000.0
EPSILON = 1e-05
SCALE = HEAD_DIM ** (-0.5)
BIAS_ROW = 2
GRAD_LANES = 384
CLUSTER_ROWS = 128
HALF_ROWS = 64
POS_BLOCK = 512
TOKEN_BLOCK = 512
ROW_BLOCK = 256
FF_BLOCK = 512
MIB = 1024 * 1024
NT = (((1,), (1,)), ((), ()))
TN = (((0,), (0,)), ((), ()))
F32 = jnp.float32
BF16 = jnp.bfloat16
ANYWHERE = pl.BlockSpec(memory_space=pl.ANY)
IN_SMEM = pl.BlockSpec(memory_space=pltpu.SMEM)


def whole(shape):
    return pl.BlockSpec(shape, lambda i: (0,) * len(shape))


def rows_of(shape):
    return pl.BlockSpec(shape, lambda i: (i,) + (0,) * (len(shape) - 1))


def dot(a, b, dims=(((1,), (0,)), ((), ()))):
    return lax.dot_general(a, b, dims, preferred_element_type=F32)


def params(mib, flops=0, moved=0, share=16):
    return dict(
        compiler_params=pltpu.CompilerParams(
            dimension_semantics=("arbitrary",),
            vmem_limit_bytes=mib * MIB,
        ),
        cost_estimate=pl.CostEstimate(
            flops=flops // share, bytes_accessed=moved // share, transcendentals=0
        ),
    )


def gated(kernel, used, needs):
    if not needs:
        return kernel

    def run(*refs):
        return kernel(*refs[:used], *refs[used + len(needs) :])

    return run


def lane_masks():
    lane = lax.broadcasted_iota(jnp.int32, (CLUSTER_ROWS, CLUSTER_ROWS), 1)
    low = (lane < HEAD_DIM).astype(F32)
    return low.astype(BF16), (1.0 - low).astype(BF16), lane < HEAD_DIM


def corners(first, second):
    blank = jnp.zeros_like(first)
    return jnp.concatenate(
        [
            jnp.concatenate([first, blank], axis=1),
            jnp.concatenate([blank, second], axis=1),
        ],
        axis=0,
    )


def both_heads(rows_now, low, high):
    return jnp.concatenate([rows_now * low, rows_now * high], axis=0)


def equal_ones(left, right):
    return jnp.where(left == right, jnp.ones((), BF16), jnp.zeros((), BF16))


def pick_rows(order_ref, first_row, unit_len):
    parts = []
    lane = lax.broadcasted_iota(jnp.int16, (CLUSTER_ROWS, CLUSTER_ROWS), 1)
    for part in range(POS_BLOCK // CLUSTER_ROWS):
        row = order_ref[pl.ds(first_row + part, 1), :]
        column = jnp.transpose(jnp.broadcast_to(row, (CLUSTER_ROWS, CLUSTER_ROWS)))
        column = column.astype(jnp.int16)
        pieces = [
            equal_ones(column, lane + jnp.int16(base)) for base in range(0, unit_len, CLUSTER_ROWS)
        ]
        parts.append(jnp.concatenate(pieces, axis=1))
    return jnp.concatenate(parts, axis=0)


def load_pieces(meta, x_refs, w_refs, x_all, w_all, sems, row_shard):
    member_rows = x_all.shape[0] // max(1, len(x_refs))
    copies = []
    for index, ref in enumerate(x_refs):
        copies.append(
            pltpu.make_async_copy(
                ref, x_all.at[pl.ds(index * member_rows, member_rows), :], sems.at[index]
            )
        )
    for index, ref in enumerate(w_refs):
        mask = meta[meta.shape[0] - len(w_refs) + index]
        start = pl.multiple_of(lax.bitwise_xor(meta[1], mask) * row_shard, 16)
        copies.append(
            pltpu.make_async_copy(
                ref.at[pl.ds(0, row_shard), :],
                w_all.at[pl.ds(start, row_shard), :],
                sems.at[len(x_refs) + index],
            )
        )
    for copy in copies:
        copy.start()
    for copy in copies:
        copy.wait()


def arrange_kernel(unit_len, first_row, order_ref, *refs):
    x_refs, out_ref = refs[:-1], refs[-1]
    step = pl.program_id(0)
    picks = pick_rows(order_ref, first_row + step * (POS_BLOCK // CLUSTER_ROWS), unit_len)
    rows = x_refs[0].shape[0]
    total = None
    for index, ref in enumerate(x_refs):
        term = dot(picks[:, index * rows : (index + 1) * rows], ref[...])
        total = term if total is None else total + term
    out_ref[...] = total.astype(BF16)


def arrange(order, x_pieces, position_count, first_row):
    member_rows, width = x_pieces[0].shape
    unit_len = member_rows * len(x_pieces)
    return pl.pallas_call(
        partial(arrange_kernel, unit_len, first_row),
        grid=(position_count // POS_BLOCK,),
        in_specs=[whole(order.shape)] + [whole(piece.shape) for piece in x_pieces],
        out_specs=rows_of((POS_BLOCK, width)),
        out_shape=jax.ShapeDtypeStruct((position_count, width), BF16),
        name="arrange",
        **params(20, 2 * position_count * unit_len * width, 6_000_000),
    )(order, *x_pieces)


def attend_kernel(sizes, meta, x_now_ref, bias_ref, *refs):
    shards, row_shard = sizes
    w_refs, refs = refs[:shards], refs[shards:]
    arranged_ref, probs_ref, mixture_ref, turned_ref, w_all, sems = refs
    width = w_all.shape[1] // 3
    step = pl.program_id(0)

    @pl.when(step == 0)
    def _():
        load_pieces(meta, [], w_refs, w_all, w_all, sems, row_shard)

    x_now = x_now_ref[...]
    turned_ref[...] = jnp.transpose(x_now)
    arranged = (dot(x_now, w_all[...]) + bias_ref[...]).astype(BF16)
    arranged_ref[...] = arranged
    low, high, lane_low = lane_masks()
    position = lax.broadcasted_iota(jnp.int32, (CLUSTER_ROWS, CLUSTER_ROWS), 0)
    other = lax.broadcasted_iota(jnp.int32, (CLUSTER_ROWS, CLUSTER_ROWS), 1)
    same_half = (position < HALF_ROWS) == (other < HALF_ROWS)
    allowed = jnp.logical_or(same_half, meta[0] == 1)
    pairs = width // CLUSTER_ROWS
    units = [(part, pair) for part in range(POS_BLOCK // CLUSTER_ROWS) for pair in range(pairs)]
    for index in range(0, len(units), 2):
        queries, keys, values = [], [], []
        for part, pair in units[index : index + 2]:
            rows_now = slice(part * CLUSTER_ROWS, (part + 1) * CLUSTER_ROWS)
            base = pair * CLUSTER_ROWS
            queries.append(arranged[rows_now, base : base + CLUSTER_ROWS] * SCALE)
            one_key = arranged[rows_now, width + base : width + base + CLUSTER_ROWS]
            keys.append(both_heads(one_key, low, high))
            one_value = arranged[rows_now, 2 * width + base : 2 * width + base + CLUSTER_ROWS]
            values.append(both_heads(one_value, low, high))
        both_scores = dot(jnp.concatenate(keys, axis=1), corners(*queries), NT)
        for which, (part, pair) in enumerate(units[index : index + 2]):
            halves = []
            for head in range(2):
                one = both_scores[
                    head * CLUSTER_ROWS : (head + 1) * CLUSTER_ROWS,
                    which * CLUSTER_ROWS : (which + 1) * CLUSTER_ROWS,
                ]
                one = jnp.where(allowed, one, NEG_FILL)
                grown = jnp.exp(one - jnp.max(one, axis=0, keepdims=True))
                halves.append(grown * (1.0 / jnp.sum(grown, axis=0, keepdims=True)))
            probs = jnp.concatenate(halves, axis=0).astype(BF16)
            at = (part * pairs + pair) * 2 * CLUSTER_ROWS
            probs_ref[at : at + 2 * CLUSTER_ROWS, :] = probs
            mixture_ref[
                part * CLUSTER_ROWS : (part + 1) * CLUSTER_ROWS,
                pair * CLUSTER_ROWS : (pair + 1) * CLUSTER_ROWS,
            ] = dot(probs, values[which], TN).astype(BF16)


def attend(meta, x_now, bias, w_pieces, row_shard, needs=()):
    shards = len(w_pieces)
    position_count, model_width = x_now.shape
    cols = w_pieces[0].shape[1]
    width = cols // 3
    pair_rows = 2 * width
    return pl.pallas_call(
        gated(partial(attend_kernel, (shards, row_shard)), 3 + shards, needs),
        grid=(position_count // POS_BLOCK,),
        in_specs=[IN_SMEM, rows_of((POS_BLOCK, model_width)), whole(bias.shape)]
        + [ANYWHERE] * (shards + len(needs)),
        out_specs=[
            rows_of((POS_BLOCK, cols)),
            rows_of((POS_BLOCK // CLUSTER_ROWS * pair_rows, CLUSTER_ROWS)),
            rows_of((POS_BLOCK, width)),
            pl.BlockSpec((model_width, POS_BLOCK), lambda i: (0, i)),
        ],
        out_shape=[
            jax.ShapeDtypeStruct((position_count, cols), BF16),
            jax.ShapeDtypeStruct((position_count // CLUSTER_ROWS * pair_rows, CLUSTER_ROWS), BF16),
            jax.ShapeDtypeStruct((position_count, width), BF16),
            jax.ShapeDtypeStruct((model_width, position_count), BF16),
        ],
        scratch_shapes=[
            pltpu.VMEM((model_width, cols), BF16),
            pltpu.SemaphoreType.DMA((shards,)),
        ],
        name="attend",
        **params(
            60, 8 * position_count * (model_width * cols + 4 * CLUSTER_ROWS * width), 18_000_000, 1
        ),
    )(meta, x_now, bias, *w_pieces, *needs)


def place_kernel(sizes, scale, has_base, order_row_ref, *refs):
    unit_len, first_token, added = sizes
    base_ref = refs[0] if has_base else None
    refs = refs[1 if has_base else 0 :]
    if added:
        first_ref, second_ref, out_ref, held = refs

        @pl.when(pl.program_id(0) == 0)
        def _():
            held[...] = (first_ref[...].astype(F32) + second_ref[...].astype(F32)).astype(BF16)

        source_refs = [held]
    else:
        source_refs, out_ref = refs[:-1], refs[-1]
    block_rows = out_ref.shape[0]
    first = jnp.full((1, 1), first_token + pl.program_id(0) * block_rows, jnp.int32)
    token = lax.broadcasted_iota(jnp.int16, (block_rows, unit_len), 0)
    total = None
    for index, ref in enumerate(source_refs):
        row = order_row_ref[:, index * unit_len : (index + 1) * unit_len] - first
        row = jnp.broadcast_to(row, (16, unit_len)).astype(jnp.int16)
        row = jnp.concatenate([row] * (block_rows // 16), axis=0)
        term = dot(equal_ones(row, token), ref[...])
        total = term if total is None else total + term
    if scale != 1.0:
        total = total * scale
    if has_base:
        total = total + base_ref[...].astype(F32)
    out_ref[...] = total.astype(out_ref.dtype)


def place(
    order_row,
    sources,
    first_token,
    row_count,
    scale=1.0,
    dtype=BF16,
    base=None,
    added=False,
    needs=(),
):
    unit_len, width = sources[0].shape
    block_rows = min(TOKEN_BLOCK, row_count)
    extra = [] if base is None else [base]
    return pl.pallas_call(
        gated(
            partial(place_kernel, (unit_len, first_token, added), scale, base is not None),
            1 + len(extra) + len(sources),
            needs,
        ),
        grid=(row_count // block_rows,),
        in_specs=[whole(order_row.shape)]
        + [rows_of((block_rows, width))] * len(extra)
        + [whole(source.shape) for source in sources]
        + [ANYWHERE] * len(needs),
        out_specs=rows_of((block_rows, width)),
        out_shape=jax.ShapeDtypeStruct((row_count, width), dtype),
        scratch_shapes=[pltpu.VMEM((unit_len, width), BF16)] if added else [],
        name="place",
        **params(
            32 if added else 20,
            16 * row_count * unit_len * width,
            10_000_000,
            1,
        ),
    )(order_row, *extra, *sources, *needs)


def attend_back_kernel(sizes, meta, order_ref, arranged_ref, probs_ref, *refs):
    members, shards, unit_len, row_shard, first_row, start = sizes
    g_refs, refs = refs[:members], refs[members:]
    w_refs, refs = refs[:shards], refs[shards:]
    grads_ref, d_x_ref, token_ref, g_all, w_all, sems = refs
    width = w_all.shape[1] // 3
    step = pl.program_id(0)

    @pl.when(step == 0)
    def _():
        load_pieces(meta, g_refs, w_refs, g_all, w_all, sems, row_shard)
        token_ref[...] = jnp.zeros_like(token_ref)

    at_row = first_row + (start + step) * (POS_BLOCK // CLUSTER_ROWS)
    picks = pick_rows(order_ref, at_row, unit_len)
    d_mixture = dot(picks, g_all[...]).astype(BF16)
    low, high, lane_low = lane_masks()
    pairs = width // CLUSTER_ROWS
    units = [(part, pair) for part in range(POS_BLOCK // CLUSTER_ROWS) for pair in range(pairs)]
    for index in range(0, len(units), 2):
        values, d_rows = [], []
        for part, pair in units[index : index + 2]:
            rows_now = slice(part * CLUSTER_ROWS, (part + 1) * CLUSTER_ROWS)
            base = pair * CLUSTER_ROWS
            one_value = arranged_ref[rows_now, 2 * width + base : 2 * width + base + CLUSTER_ROWS]
            values.append(both_heads(one_value, low, high))
            d_rows.append(d_mixture[rows_now, base : base + CLUSTER_ROWS])
        both_probs = dot(jnp.concatenate(values, axis=1), corners(*d_rows), NT)
        for which, (part, pair) in enumerate(units[index : index + 2]):
            rows_now = slice(part * CLUSTER_ROWS, (part + 1) * CLUSTER_ROWS)
            base = pair * CLUSTER_ROWS
            q_lanes = slice(base, base + CLUSTER_ROWS)
            k_lanes = slice(width + base, width + base + CLUSTER_ROWS)
            v_lanes = slice(2 * width + base, 2 * width + base + CLUSTER_ROWS)
            queries = arranged_ref[rows_now, q_lanes] * SCALE
            keys = arranged_ref[rows_now, k_lanes] * SCALE
            at = (part * pairs + pair) * 2 * CLUSTER_ROWS
            probs = probs_ref[at : at + 2 * CLUSTER_ROWS, :]
            d_probs = both_probs[:, which * CLUSTER_ROWS : (which + 1) * CLUSTER_ROWS]
            pieces = []
            for head in range(2):
                rows = slice(head * CLUSTER_ROWS, (head + 1) * CLUSTER_ROWS)
                weight = probs[rows].astype(F32)
                d_one = d_probs[rows]
                inner = jnp.sum(weight * d_one, axis=0, keepdims=True)
                pieces.append(weight * (d_one - inner))
            d_scores = jnp.concatenate(pieces, axis=0).astype(BF16)
            d_query = dot(d_scores, both_heads(keys, low, high), TN)
            d_pair = dot(
                jnp.concatenate([probs, d_scores], axis=1), corners(d_rows[which], queries)
            )
            d_values, d_keys = d_pair[:, :CLUSTER_ROWS], d_pair[:, CLUSTER_ROWS:]
            grads_ref[rows_now, q_lanes] = d_query.astype(BF16)
            grads_ref[rows_now, k_lanes] = jnp.where(
                lane_low, d_keys[:CLUSTER_ROWS], d_keys[CLUSTER_ROWS:]
            ).astype(BF16)
            grads_ref[rows_now, v_lanes] = jnp.where(
                lane_low, d_values[:CLUSTER_ROWS], d_values[CLUSTER_ROWS:]
            ).astype(BF16)
    grads = grads_ref[...]
    d_x_ref[...] = dot(grads, w_all[...], NT).astype(BF16)


def attend_back(
    meta, order, arranged, probs, g_pieces, w_pieces, row_shard, first_row, needs, span, into
):
    members, shards = len(g_pieces), len(w_pieces)
    member_rows, width = g_pieces[0].shape
    unit_len = members * member_rows
    position_count, cols = arranged.shape
    model_width = row_shard * shards
    start, stop = span
    pair_rows = POS_BLOCK // CLUSTER_ROWS * 2 * width
    used = 4 + members + shards

    def block(shape):
        return pl.BlockSpec(shape, lambda i: (start + i, 0))

    return pl.pallas_call(
        gated(
            partial(attend_back_kernel, (members, shards, unit_len, row_shard, first_row, start)),
            used,
            list(into) + list(needs),
        ),
        grid=(stop - start,),
        in_specs=[
            IN_SMEM,
            whole(order.shape),
            block((POS_BLOCK, cols)),
            block((pair_rows, CLUSTER_ROWS)),
        ]
        + [ANYWHERE] * (members + shards + len(into) + len(needs)),
        out_specs=[block((POS_BLOCK, cols)), block((POS_BLOCK, model_width)), whole((8, 128))],
        out_shape=[
            jax.ShapeDtypeStruct((position_count, cols), BF16),
            jax.ShapeDtypeStruct((position_count, model_width), BF16),
            jax.ShapeDtypeStruct((8, 128), F32),
        ],
        input_output_aliases={used + index: index for index in range(len(into))},
        scratch_shapes=[
            pltpu.VMEM((unit_len, width), BF16),
            pltpu.VMEM((model_width, cols), BF16),
            pltpu.SemaphoreType.DMA((members + shards,)),
        ],
        name="attend_back",
        **params(
            60,
            12 * (stop - start) * POS_BLOCK * (unit_len * width + model_width * cols),
            20_000_000,
            1,
        ),
    )(meta, order, arranged, probs, *g_pieces, *w_pieces, *into, *needs)


def normalise(summed):
    average = jnp.mean(summed, axis=-1, keepdims=True)
    centred = summed - average
    spread = jnp.mean(centred * centred, axis=-1, keepdims=True)
    scale_inv = lax.rsqrt(spread + EPSILON)
    return centred * scale_inv, scale_inv


def normalise_back(grad_out, normed, scale_inv, gain_row):
    scaled = grad_out * gain_row
    return scale_inv * (
        scaled
        - jnp.mean(scaled, axis=-1, keepdims=True)
        - normed * jnp.mean(scaled * normed, axis=-1, keepdims=True)
    )


def column_sum(rows_now):
    return jnp.sum(rows_now, axis=0, keepdims=True)


def gelu_parts(value):
    below = 0.5 + 0.5 * lax.erf(value * 0.7071067811865476)
    bell = jnp.exp(value * value * -0.5) * 0.3989422804014327
    return value * below, below + value * bell


class Pack:
    def __init__(self, model_width, feed_width, shards, units, depth):
        self.model_width, self.feed_width, self.shards = model_width, feed_width, shards
        self.row_shard = model_width // shards
        self.feed_shard = feed_width // shards
        self.down_rows = self.feed_shard // CORES
        self.blocks = feed_width // CORES // model_width
        self.up_at = self.down_rows
        self.out_at = self.up_at + self.blocks * self.row_shard
        self.out_rows = self.row_shard // CORES
        self.used = self.out_at + self.out_rows
        unit = 16 * depth
        self.rows = -(-self.used // unit) * unit
        self.rest_rows = self.rows - self.down_rows
        self.units = units
        self.group = units * self.row_shard

    def out_start(self, shard, member):
        return (
            lax.bitwise_xor(jnp.int32(shard) // self.units, member) * self.group
            + (shard % self.units) * self.row_shard
        )


def feed_kernel(pack, att_count, meta, x_ref, cot_ref, vec_ref, up_bias_ref, *refs):
    shards = pack.shards
    att_refs, refs = refs[:att_count], refs[att_count:]
    own_out, own_up, own_down = refs[:3]
    refs = refs[3:]
    pieces, refs = refs[: 2 * (shards - 1)], refs[2 * (shards - 1) :]
    out_ref, first_turned_ref, d_branch_ref, d_ffn_turned_ref, hidden_ref, d_pre_ref = refs[:6]
    att_turned_ref = refs[6]
    refs = refs[7:]
    d_att_refs, refs = refs[:att_count], refs[att_count:]
    sums_ref, up_sums_ref, w_out, w_up, w_down, slope, sems = refs
    step = pl.program_id(0)
    here, core, member = meta[1], meta[2], meta[3]
    feed_width = pack.feed_width

    def loads(kind):
        copies = []

        def add(source, target):
            copies.append(pltpu.make_async_copy(source, target, sems.at[kind, len(copies)]))

        if kind == 0:
            start = pl.multiple_of(pack.out_start(here, member), 16)
            add(own_out, w_out.at[pl.ds(start, pack.row_shard), :])
        elif kind == 1:
            start = pl.multiple_of(here * pack.row_shard, 16)
            add(own_up, w_up.at[pl.ds(start, pack.row_shard), :])
        else:
            start = pl.multiple_of(here * pack.feed_shard, 16)
            add(own_down, w_down.at[pl.ds(start, pack.feed_shard), :])
        for index, ref in enumerate(pieces):
            peer = lax.bitwise_xor(here, meta[8 + index])
            half = core if index < shards - 1 else 1 - core
            if kind == 0:
                start = pack.out_start(peer, member) + half * pack.out_rows
                start = pl.multiple_of(start, 16)
                add(
                    ref.at[pl.ds(pack.out_at, pack.out_rows), :],
                    w_out.at[pl.ds(start, pack.out_rows), :],
                )
            elif kind == 1:
                start = pl.multiple_of(peer * pack.row_shard, 16)
                for block in range(pack.blocks):
                    lane = pl.multiple_of(
                        (half * pack.blocks + block) * pack.model_width, CLUSTER_ROWS
                    )
                    add(
                        ref.at[pl.ds(pack.up_at + block * pack.row_shard, pack.row_shard), :],
                        w_up.at[pl.ds(start, pack.row_shard), pl.ds(lane, pack.model_width)],
                    )
            else:
                start = pl.multiple_of(peer * pack.feed_shard + half * pack.down_rows, 16)
                add(
                    ref.at[pl.ds(0, pack.down_rows), :],
                    w_down.at[pl.ds(start, pack.down_rows), :],
                )
        return copies

    @pl.when(step == 0)
    def _():
        for kind in range(3):
            for copy in loads(kind):
                copy.start()
        sums_ref[...] = jnp.zeros_like(sums_ref)
        up_sums_ref[...] = jnp.zeros_like(up_sums_ref)
        for copy in loads(0):
            copy.wait()

    bias_out, gain_one, gain_two = vec_ref[0:1, :], vec_ref[1:2, :], vec_ref[2:3, :]
    shift_one, shift_two, bias_down = vec_ref[3:4, :], vec_ref[4:5, :], vec_ref[5:6, :]
    att_width = att_refs[0].shape[1]
    summed = x_ref[...].astype(F32) + bias_out
    for index, ref in enumerate(att_refs):
        summed += dot(ref[...], w_out[index * att_width : (index + 1) * att_width, :])
    normed_one, inv_one = normalise(summed)
    first = normed_one * gain_one + shift_one
    first_low = first.astype(BF16)
    first_turned_ref[...] = jnp.transpose(first_low)
    for index, ref in enumerate(att_refs):
        att_turned_ref[index * att_width : (index + 1) * att_width, :] = jnp.transpose(ref[...])

    @pl.when(step == 0)
    def _():
        for kind in (1, 2):
            for copy in loads(kind):
                copy.wait()

    second = first + bias_down
    starts = list(range(0, feed_width, FF_BLOCK))

    def raised(base):
        lanes = slice(base, base + FF_BLOCK)
        return dot(first_low, w_up[:, lanes]) + up_bias_ref[:, lanes]

    pre = raised(starts[0])
    for index, base in enumerate(starts):
        lanes = slice(base, base + FF_BLOCK)
        pre_next = raised(starts[index + 1]) if index + 1 < len(starts) else None
        hidden, slope_now = gelu_parts(pre)
        hidden = hidden.astype(BF16)
        hidden_ref[:, lanes] = hidden
        slope[:, lanes] = slope_now
        second += dot(hidden, w_down[lanes, :])
        pre = pre_next
    normed_two, inv_two = normalise(second)
    out_ref[...] = (normed_two * gain_two + shift_two).astype(BF16)
    top = cot_ref[...].astype(F32)
    d_second = normalise_back(top, normed_two, inv_two, gain_two)
    d_ffn = d_second.astype(BF16)
    d_ffn_turned_ref[...] = jnp.transpose(d_ffn)
    d_first = d_second
    d_hidden = dot(d_ffn, w_down[0:FF_BLOCK, :], NT)
    for index, base in enumerate(starts):
        lanes = slice(base, base + FF_BLOCK)
        if index + 1 < len(starts):
            d_next = dot(d_ffn, w_down[starts[index + 1] : starts[index + 1] + FF_BLOCK, :], NT)
        d_pre = (d_hidden * slope[:, lanes]).astype(BF16)
        d_pre_ref[:, lanes] = d_pre
        up_sums_ref[:, lanes] += column_sum(d_pre.astype(F32))
        d_first += dot(d_pre, w_up[:, lanes], NT)
        d_hidden = d_next
    d_lower = normalise_back(d_first, normed_one, inv_one, gain_one)
    d_branch = d_lower.astype(BF16)
    d_branch_ref[...] = d_branch
    for index, ref in enumerate(d_att_refs):
        back = dot(d_branch, w_out[index * att_width : (index + 1) * att_width, :], NT)
        ref[...] = (0.5 * back).astype(BF16)
    sums_ref[0:1, :] += column_sum(d_branch.astype(F32))
    sums_ref[1:2, :] += column_sum(d_first * normed_one)
    sums_ref[2:3, :] += column_sum(top * normed_two)
    sums_ref[3:4, :] += column_sum(d_first)
    sums_ref[4:5, :] += column_sum(top)
    sums_ref[5:6, :] += column_sum(d_ffn.astype(F32))


def feed(pack, meta, x_own, cot_own, vectors, up_bias, att, own, pieces):
    row_count, model_width = x_own.shape
    feed_width = pack.feed_width
    att_width = att[0].shape[1]
    one = rows_of((ROW_BLOCK, model_width))
    wide = rows_of((ROW_BLOCK, feed_width))
    narrow = rows_of((ROW_BLOCK, att_width))
    turned = pl.BlockSpec((model_width, ROW_BLOCK), lambda i: (0, i))
    turned_shape = jax.ShapeDtypeStruct((model_width, row_count), BF16)

    def like(width):
        return jax.ShapeDtypeStruct((row_count, width), BF16)

    return pl.pallas_call(
        partial(feed_kernel, pack, len(att)),
        grid=(row_count // ROW_BLOCK,),
        in_specs=[IN_SMEM, one, one, whole(vectors.shape), whole(up_bias.shape)]
        + [narrow] * len(att)
        + [ANYWHERE] * (3 + len(pieces)),
        out_specs=[one, turned, one, turned, wide, wide, turned]
        + [narrow] * len(att)
        + [whole((8, model_width)), whole((1, feed_width))],
        out_shape=[
            like(model_width),
            turned_shape,
            like(model_width),
            turned_shape,
            like(feed_width),
            like(feed_width),
            turned_shape,
        ]
        + [like(att_width)] * len(att)
        + [
            jax.ShapeDtypeStruct((8, model_width), F32),
            jax.ShapeDtypeStruct((1, feed_width), F32),
        ],
        scratch_shapes=[
            pltpu.VMEM((model_width, model_width), BF16),
            pltpu.VMEM((model_width, feed_width), BF16),
            pltpu.VMEM((feed_width, model_width), BF16),
            pltpu.VMEM((ROW_BLOCK, feed_width), F32),
            pltpu.SemaphoreType.DMA((3, 1 + pack.blocks * len(pieces))),
        ],
        name="feed",
        **params(
            60, 2 * row_count * model_width * (2 * model_width + 4 * feed_width), 40_000_000
        ),
    )(meta, x_own, cot_own, vectors, up_bias, *att, *own, *pieces)


def down_grads_kernel(pack, table, d_ffn_ref, hidden_ref, theirs_ref, mine_ref, made, sems):
    step = pl.program_id(0)
    core = table[0]

    def stores(shard):
        return [
            pltpu.make_async_copy(made.at[1 - core, shard], theirs_ref.at[shard], sems.at[0, shard]),
            pltpu.make_async_copy(made.at[core, shard], mine_ref.at[shard], sems.at[1, shard]),
        ]

    grad = dot(d_ffn_ref[...], hidden_ref[...]).astype(BF16)
    for half in range(CORES):
        for lane in range(0, pack.model_width, pack.feed_shard):
            begin = half * (pack.model_width // CORES) + lane // pack.feed_shard * pack.down_rows
            made[half, step, :, lane : lane + pack.feed_shard] = grad[
                begin : begin + pack.down_rows
            ]
    for copy in stores(step):
        copy.start()

    @pl.when(step == pack.shards - 1)
    def _():
        for shard in range(pack.shards):
            for copy in stores(shard):
                copy.wait()


def down_grads(pack, table, d_ffn, hidden):
    model_width, row_count = d_ffn.shape
    shape = (pack.shards, pack.down_rows, model_width)
    return pl.pallas_call(
        partial(down_grads_kernel, pack),
        grid_spec=pltpu.PrefetchScalarGridSpec(
            num_scalar_prefetch=1,
            grid=(pack.shards,),
            in_specs=[
                pl.BlockSpec(d_ffn.shape, lambda step, table: (0, 0)),
                pl.BlockSpec((row_count, pack.feed_shard), lambda step, table: (0, step)),
            ],
            out_specs=[ANYWHERE] * 2,
            scratch_shapes=[
                pltpu.VMEM((CORES,) + shape, BF16),
                pltpu.SemaphoreType.DMA((CORES, pack.shards)),
            ],
        ),
        out_shape=[jax.ShapeDtypeStruct(shape, BF16)] * 2,
        name="down_grads",
        **params(60, 2 * row_count * model_width * pack.feed_width, 10_000_000),
    )(table, d_ffn, hidden)


def rest_grads_kernel(
    pack, table, first_ref, d_pre_ref, att_ref, d_branch_ref, theirs_ref, mine_ref, *scratch
):
    att, d_branch, tile, made, in_sems, sems = scratch
    step = pl.program_id(0)
    core, member = table[0], table[1]
    shards, blocks = pack.shards, pack.blocks
    out_at = pack.out_at - pack.down_rows

    loads = [
        pltpu.make_async_copy(att_ref, att, in_sems.at[0]),
        pltpu.make_async_copy(d_branch_ref, d_branch, in_sems.at[1]),
    ]

    def store(half, start, rows, sem):
        there = (slice(None), pl.ds(start, rows), slice(None))

        def copy(target):
            return pltpu.make_async_copy(
                made.at[(half,) + there], target.at[there], sems.at[half, sem]
            )

        return copy

    def both(half, start, rows, sem, act):
        copy = store(half, start, rows, sem)

        @pl.when(core == half)
        def _():
            act(copy(mine_ref))

        @pl.when(core != half)
        def _():
            act(copy(theirs_ref))

    @pl.when(step == 0)
    def _():
        for copy in loads:
            copy.start()

    @pl.when(step < CORES * blocks)
    def _():
        grad = dot(first_ref[...], d_pre_ref[...]).astype(BF16)
        start = pl.multiple_of(step % blocks * pack.row_shard, 16)
        for shard in range(shards):
            made[step // blocks, shard, pl.ds(start, pack.row_shard), :] = grad[
                shard * pack.row_shard : (shard + 1) * pack.row_shard
            ]

    for half in range(CORES):

        @pl.when(step == (half + 1) * blocks - 1)
        def _(half=half):
            both(half, 0, out_at, 0, lambda copy: copy.start())

    @pl.when(step == CORES * blocks)
    def _():
        for copy in loads:
            copy.wait()
        tile[...] = dot(att[...], d_branch[...])
        spare = pack.rows - pack.used
        for half in range(CORES):
            for shard in range(shards):
                start = pack.out_start(shard, member) + half * pack.out_rows
                start = pl.multiple_of(start, 16)
                made[half, shard, out_at : out_at + pack.out_rows, :] = tile[
                    pl.ds(start, pack.out_rows), :
                ].astype(BF16)
                if spare:
                    made[half, shard, out_at + pack.out_rows :, :] = jnp.zeros(
                        (spare, pack.model_width), BF16
                    )
            both(half, out_at, pack.rest_rows - out_at, 1, lambda copy: copy.start())
        for half in range(CORES):
            both(half, 0, out_at, 0, lambda copy: copy.wait())
            both(half, out_at, pack.rest_rows - out_at, 1, lambda copy: copy.wait())


def rest_grads(pack, table, first_low, d_pre, att, d_branch, needs=()):
    model_width, row_count = first_low.shape
    shape = (pack.shards, pack.rest_rows, model_width)
    steps = CORES * pack.blocks
    return pl.pallas_call(
        gated(partial(rest_grads_kernel, pack), 5, needs),
        grid_spec=pltpu.PrefetchScalarGridSpec(
            num_scalar_prefetch=1,
            grid=(steps + 1,),
            in_specs=[
                pl.BlockSpec(first_low.shape, lambda step, table: (0, 0)),
                pl.BlockSpec(
                    (row_count, model_width),
                    lambda step, table: (0, jnp.minimum(step, steps - 1)),
                ),
            ]
            + [ANYWHERE] * (2 + len(needs)),
            out_specs=[ANYWHERE] * 2,
            scratch_shapes=[
                pltpu.VMEM((model_width, row_count), BF16),
                pltpu.VMEM((row_count, model_width), BF16),
                pltpu.VMEM((model_width, model_width), F32),
                pltpu.VMEM((CORES,) + shape, BF16),
                pltpu.SemaphoreType.DMA((2,)),
                pltpu.SemaphoreType.DMA((CORES, 2)),
            ],
        ),
        out_shape=[jax.ShapeDtypeStruct(shape, BF16)] * 2,
        name="rest_grads",
        **params(60, 2 * row_count * model_width * (pack.feed_width + model_width), 10_000_000),
    )(table, first_low, d_pre, att, d_branch, *needs)


def qkv_grads_kernel(rounds, x_refs_then, *refs):
    refs = (x_refs_then,) + refs
    x_refs, grad_refs = refs[:rounds], refs[rounds : 2 * rounds]
    small_ref, out_ref = refs[2 * rounds :]
    shards, rows, _ = out_ref.shape
    row_shard = rows - small_ref.shape[1]
    total, sums = None, None
    for x_ref, grad_ref in zip(x_refs, grad_refs):
        grads = grad_ref[...]
        term = dot(x_ref[...], grads)
        down = column_sum(grads.astype(F32))
        total = term if total is None else total + term
        sums = down if sums is None else sums + down
    total = total.astype(BF16)
    row = lax.broadcasted_iota(jnp.int32, small_ref.shape[1:], 0)
    for shard in range(shards):
        out_ref[shard, :row_shard, :] = total[shard * row_shard : (shard + 1) * row_shard]
        last = jnp.where(row == BIAS_ROW, sums, small_ref[shard])
        out_ref[shard, row_shard:, :] = last.astype(BF16)


def qkv_grads(x_turned, grads, small, row_shard, needs=()):
    rounds = len(grads)
    model_width, positions = x_turned[0].shape
    cols = grads[0].shape[1]
    shards, extra, _ = small.shape
    block = GRAD_LANES if cols % GRAD_LANES == 0 else cols
    return pl.pallas_call(
        gated(partial(qkv_grads_kernel, rounds), 2 * rounds + 1, needs),
        grid=(cols // block,),
        in_specs=[whole((model_width, positions))] * rounds
        + [pl.BlockSpec((positions, block), lambda i: (0, i))] * rounds
        + [pl.BlockSpec((shards, extra, block), lambda i: (0, 0, i))]
        + [ANYWHERE] * len(needs),
        out_specs=pl.BlockSpec((shards, row_shard + extra, block), lambda i: (0, 0, i)),
        out_shape=jax.ShapeDtypeStruct((shards, row_shard + extra, cols), BF16),
        name="qkv_grads",
        **params(60, 2 * rounds * positions * model_width * cols, 18_000_000),
    )(*x_turned, *grads, small, *needs)


def add_picked_kernel(count, first, table, *refs):
    in_refs, out_refs = refs[:count], refs[count:]
    if count == 2:
        total = in_refs[0][...] + in_refs[1][...]
    else:
        total = in_refs[0][...].astype(F32)
        for ref in in_refs[1:]:
            total = total + ref[...].astype(F32)
        total = total.astype(BF16)
    if len(out_refs) == 1:
        out_refs[0][...] = total
        return

    @pl.when(pl.program_id(0) < first)
    def _():
        out_refs[0][...] = total

    @pl.when(pl.program_id(0) >= first)
    def _():
        out_refs[1][...] = total


def add_picked(table, arrays, steps, first=None, needs=(), work=0):
    _, rows, cols = arrays[0].shape
    parts = 2 if rows % 32 == 0 and steps == 1 else 1
    block = (1, rows // parts, cols)
    spec = [
        pl.BlockSpec(block, lambda s, p, t, k=k: (t[k * steps + s], p, 0))
        for k in range(len(arrays))
    ]
    if first is None:
        out_specs = [pl.BlockSpec(block, lambda s, p, t: (s, p, 0))]
        counts = [steps]
    else:
        out_specs = [
            pl.BlockSpec(
                block,
                lambda s, p, t: (
                    jnp.minimum(s, first - 1),
                    jnp.where(s < first, p, parts - 1),
                    0,
                ),
            ),
            pl.BlockSpec(
                block,
                lambda s, p, t: (jnp.maximum(s - first, 0), jnp.where(s < first, 0, p), 0),
            ),
        ]
        counts = [first, steps - first]
    return pl.pallas_call(
        gated(partial(add_picked_kernel, len(arrays), first), 1 + len(arrays), needs),
        grid_spec=pltpu.PrefetchScalarGridSpec(
            num_scalar_prefetch=1,
            grid=(steps, parts),
            in_specs=spec + [ANYWHERE] * len(needs),
            out_specs=out_specs,
        ),
        out_shape=[jax.ShapeDtypeStruct((n, rows, cols), BF16) for n in counts],
        name="add_picked",
        compiler_params=pltpu.CompilerParams(
            dimension_semantics=("arbitrary", "arbitrary"),
            vmem_limit_bytes=(60 if steps > 1 else 12) * MIB,
        ),
        cost_estimate=pl.CostEstimate(flops=work, bytes_accessed=1_000_000, transcendentals=0),
    )(table, *arrays, *needs)


def join_kernel(count, down_kept, down_landed, rest_kept, rest_landed, *outs):
    rows = down_kept.shape[1]
    for index in range(count):
        target = outs[1 - index % 2] if count > 1 else outs[0]
        place_now = index // 2
        target[place_now, :rows, :] = down_kept[index] + down_landed[index]
        target[place_now, rows:, :] = rest_kept[index] + rest_landed[index]


def join(kept, landed, needs=()):
    count = kept[0].shape[0]
    rows = kept[0].shape[1] + kept[1].shape[1]
    shape = jax.ShapeDtypeStruct(((count + 1) // 2, rows, kept[0].shape[2]), BF16)
    vmem = pl.BlockSpec(memory_space=pltpu.VMEM)
    outs = pl.pallas_call(
        gated(partial(join_kernel, count), 4, needs),
        in_specs=[vmem] * 4 + [ANYWHERE] * len(needs),
        out_specs=[vmem] * min(count, 2),
        out_shape=[shape] * min(count, 2),
        name="join",
        compiler_params=pltpu.CompilerParams(vmem_limit_bytes=24 * MIB),
        cost_estimate=pl.CostEstimate(flops=0, bytes_accessed=200_000, transcendentals=0),
    )(kept[0], landed[0], kept[1], landed[1], *needs)
    return outs if count > 1 else (None, outs[0])


def stack_kernel(count, *refs):
    for index in range(count):
        refs[count][index] = refs[index][...]


def home_kernel(count, meta, own_ref, *refs):
    out_ref = refs[count]
    rows = refs[0].shape[0]
    for index in range(count):
        start = pl.multiple_of((meta[5] + index) % count * rows, 16)
        target = out_ref.at[pl.ds(start, rows), :]
        if index:
            target[...] = refs[index][...].astype(out_ref.dtype)
            continue

        @pl.when(meta[6] == 0)
        def _():
            target[...] = refs[0][...].astype(out_ref.dtype)

        @pl.when(meta[6] == 1)
        def _():
            target[...] = own_ref[...].astype(out_ref.dtype)


def home_rows(meta, own, landed, dtype, needs=()):
    rows, cols = own.shape
    vmem = pl.BlockSpec(memory_space=pltpu.VMEM)
    return pl.pallas_call(
        gated(partial(home_kernel, len(landed)), 2 + len(landed), needs),
        in_specs=[IN_SMEM, vmem] + [vmem] * len(landed) + [ANYWHERE] * len(needs),
        out_specs=vmem,
        out_shape=jax.ShapeDtypeStruct((len(landed) * rows, cols), dtype),
        name="home_rows",
        compiler_params=pltpu.CompilerParams(vmem_limit_bytes=60 * MIB),
        cost_estimate=pl.CostEstimate(flops=0, bytes_accessed=100_000, transcendentals=0),
    )(meta, own, *landed, *needs)


def split_kernel(in_ref, *out_refs):
    rows = out_refs[0].shape[0]
    for index, ref in enumerate(out_refs):
        ref[...] = in_ref[index * rows : (index + 1) * rows, :]


def split_rows(value, count, needs=()):
    rows = value.shape[0] // count
    vmem = pl.BlockSpec(memory_space=pltpu.VMEM)
    return pl.pallas_call(
        gated(split_kernel, 1, needs),
        in_specs=[vmem] + [ANYWHERE] * len(needs),
        out_specs=[vmem] * count,
        out_shape=[jax.ShapeDtypeStruct((rows, value.shape[1]), value.dtype)] * count,
        name="split_rows",
        compiler_params=pltpu.CompilerParams(vmem_limit_bytes=12 * MIB),
        cost_estimate=pl.CostEstimate(flops=0, bytes_accessed=100_000, transcendentals=0),
    )(value, *needs)


def stack_up(pieces, needs=()):
    vmem = pl.BlockSpec(memory_space=pltpu.VMEM)
    return pl.pallas_call(
        gated(partial(stack_kernel, len(pieces)), len(pieces), needs),
        in_specs=[vmem] * len(pieces) + [ANYWHERE] * len(needs),
        out_specs=vmem,
        out_shape=jax.ShapeDtypeStruct((len(pieces),) + pieces[0].shape, BF16),
        name="stack_up",
        compiler_params=pltpu.CompilerParams(vmem_limit_bytes=24 * MIB),
        cost_estimate=pl.CostEstimate(flops=0, bytes_accessed=100_000, transcendentals=0),
    )(*pieces, *needs)


def unpack_kernel(pack, depth, meta, mine_ref, other_ref, down_ref, up_ref, out_ref, ordered):
    core, level = meta[2], meta[4]
    rows = pack.rows // depth
    for mask in range(depth):
        start = pl.multiple_of(lax.bitwise_xor(level, mask) * rows, 16)
        ordered[core, pl.ds(start, rows), :] = mine_ref[mask]
        ordered[1 - core, pl.ds(start, rows), :] = other_ref[mask]
    turned = []
    for half in range(CORES):
        for lane in range(0, pack.model_width, pack.feed_shard):
            turned.append(ordered[half, : pack.down_rows, lane : lane + pack.feed_shard])
    down_ref[...] = jnp.transpose(jnp.concatenate(turned, axis=0)).astype(F32)
    for half in range(CORES):
        for block in range(pack.blocks):
            lane = (half * pack.blocks + block) * pack.model_width
            start = pack.up_at + block * pack.row_shard
            up_ref[:, lane : lane + pack.model_width] = ordered[
                half, start : start + pack.row_shard, :
            ].astype(F32)
        out_ref[half * pack.out_rows : (half + 1) * pack.out_rows, :] = ordered[
            half, pack.out_at : pack.out_at + pack.out_rows, :
        ].astype(F32)


def unpack(pack, depth, meta, mine, other):
    vmem = pl.BlockSpec(memory_space=pltpu.VMEM)
    return pl.pallas_call(
        partial(unpack_kernel, pack, depth),
        in_specs=[IN_SMEM, vmem, vmem],
        out_specs=[vmem] * 3,
        out_shape=[
            jax.ShapeDtypeStruct((pack.feed_shard, pack.model_width), F32),
            jax.ShapeDtypeStruct((pack.row_shard, pack.feed_width), F32),
            jax.ShapeDtypeStruct((pack.row_shard, pack.model_width), F32),
        ],
        scratch_shapes=[pltpu.VMEM((CORES, pack.rows, pack.model_width), BF16)],
        name="unpack",
        compiler_params=pltpu.CompilerParams(vmem_limit_bytes=60 * MIB),
        cost_estimate=pl.CostEstimate(flops=0, bytes_accessed=10_000_000, transcendentals=0),
    )(meta, mine, other)


def unpack_qkv_kernel(meta, mine_ref, other_ref, grad_ref, bias_ref, small_ref):
    member = meta[3]
    row_shard, width = grad_ref.shape[0], grad_ref.shape[1] // 3
    part = mine_ref.shape[1] // 3
    for ref, at in ((mine_ref, member), (other_ref, 1 - member)):
        for kind in range(3):
            lane = pl.multiple_of(kind * width + at * part, CLUSTER_ROWS)
            from_lanes = slice(kind * part, (kind + 1) * part)
            grad_ref[:, pl.ds(lane, part)] = ref[:row_shard, from_lanes].astype(F32)
            lane = pl.multiple_of(at * part, CLUSTER_ROWS)
            bias_ref[kind : kind + 1, pl.ds(lane, part)] = ref[row_shard:, from_lanes].astype(F32)[
                BIAS_ROW : BIAS_ROW + 1
            ]
    small_ref[...] = (mine_ref[row_shard:, :].astype(F32) + other_ref[row_shard:, :].astype(F32))[
        :BIAS_ROW
    ]


def unpack_qkv(meta, mine, other, row_shard, needs=()):
    cols = mine.shape[1]
    vmem = pl.BlockSpec(memory_space=pltpu.VMEM)
    return pl.pallas_call(
        gated(unpack_qkv_kernel, 3, needs),
        in_specs=[IN_SMEM, vmem, vmem] + [ANYWHERE] * len(needs),
        out_specs=[vmem] * 3,
        out_shape=[
            jax.ShapeDtypeStruct((row_shard, CORES * cols), F32),
            jax.ShapeDtypeStruct((3, CORES * cols // 3), F32),
            jax.ShapeDtypeStruct((BIAS_ROW, cols), F32),
        ],
        name="unpack_qkv",
        compiler_params=pltpu.CompilerParams(vmem_limit_bytes=60 * MIB),
        cost_estimate=pl.CostEstimate(flops=0, bytes_accessed=200_000, transcendentals=0),
    )(meta, mine, other, *needs)


def tie(*values):
    return lax.optimization_barrier(values)


def body(
    tokens,
    cotangent,
    perms,
    unit_kind,
    w_qkv,
    bias_qv,
    w_out,
    bias_out,
    ln_gain,
    ln_bias,
    w_up,
    bias_up,
    w_down,
    bias_down,
):
    shards = lax.axis_size("fsdp")
    groups = lax.axis_size("dp")
    here = lax.axis_index("fsdp")
    dp_index = lax.axis_index("dp")
    core = dp_index % CORES
    level = dp_index // CORES
    depth = groups // CORES
    units, rounds, unit_len = perms.shape
    per_device = unit_len // shards
    model_width = tokens.shape[1]
    feed_width = w_up.shape[1]
    row_shard = model_width // shards
    members = shards // units
    member_rows = unit_len // members
    head_cols = model_width // members
    padded = -(-head_cols // CLUSTER_ROWS) * CLUSTER_ROWS
    spot = here * CORES + core
    home_core = spot // shards
    unit = (spot // members) % units
    member = spot % members
    pack = Pack(model_width, feed_width, shards, units, depth)
    bits = [1 << k for k in range(shards.bit_length() - 1)]
    bit_orders = (bits, bits[::-1])

    def plane_pairs(target):
        pairs = []
        for z in range(depth):
            for f_index in range(shards):
                for c_index in range(CORES):
                    f_new, c_new = target(f_index, c_index)
                    pairs.append(
                        (
                            (z * CORES + c_index) * shards + f_index,
                            (z * CORES + c_new) * shards + f_new,
                        )
                    )
        return pairs

    def send(value, pairs):
        return lax.ppermute(value, ("dp", "fsdp"), pairs)

    def cross(value, mask):
        return send(value, plane_pairs(lambda f, c: divmod((f * CORES + c) ^ mask, CORES)))

    def trade(value, stage):
        return send(value, plane_pairs(lambda f, c: (f ^ bit_orders[c][stage], c)))

    def trade_mask(index, which):
        mask = 0
        for stage in range(len(bits)):
            if index >> stage & 1:
                mask ^= bit_orders[which][stage]
        return mask

    def climb(value, mask):
        plane = CORES * shards
        pairs = []
        for z in range(depth):
            for rest in range(plane):
                pairs.append((z * plane + rest, (z ^ mask) * plane + rest))
        return send(value, pairs)

    def place_of(f, c, step):
        return (c * units + (f % units + step) % units) * members + f // units

    def outward(step):
        return plane_pairs(lambda f, c: divmod(place_of(f, c, step), CORES))

    def homeward(step):
        return [(b, a) for a, b in outward(step)]

    stays = place_of(here, core, 0) == spot

    def send_apart(value, pairs):
        return send(value, [(a, b) for a, b in pairs if a != b])

    def bring_start(value):
        blocks = value.reshape(units, per_device, model_width)
        return [
            lax.dynamic_index_in_dim(blocks, (here % units + step) % units, axis=0, keepdims=False)
            for step in range(units)
        ]

    def bring(chosen):
        return [
            (send_apart if step == 0 else send)(value, outward(step))
            for step, value in enumerate(chosen)
        ]

    def brought(chosen, landed):
        kept_one = jnp.where(stays, chosen[0], landed[0])
        return jnp.concatenate([kept_one] + list(landed[1:]), axis=0)

    def send_home(blocks):
        return [
            (send_apart if step == 0 else send)(blocks[step], homeward(step))
            for step in range(units)
        ]

    x_chosen = bring_start(tokens)
    x_own = brought(x_chosen, bring(x_chosen))
    small = jnp.concatenate(
        [
            bias_qv.reshape(-1),
            bias_out,
            ln_gain.reshape(-1),
            ln_bias.reshape(-1),
            bias_up,
            bias_down,
        ]
    )
    small_rows = -(-small.shape[0] // (3 * padded))
    small_block = jnp.pad(
        jnp.pad(small, (0, small_rows * 3 * padded - small.shape[0])).reshape(
            small_rows, 3 * padded
        ),
        ((0, 16 - small_rows), (0, 0)),
    )
    def columns_for(offset):
        start = lax.bitwise_xor(member, offset) * head_cols
        blocks = [
            jnp.pad(
                lax.dynamic_slice(
                    w_qkv, (0, kind * model_width + start), (row_shard, head_cols)
                ),
                ((0, 0), (0, padded - head_cols)),
            )
            for kind in range(3)
        ]
        return jnp.concatenate([jnp.concatenate(blocks, axis=1), small_block], axis=0)

    offsets = [(CORES * m) % members for m in range(shards)]
    kinds = sorted(set(offsets))
    order_pack = jnp.concatenate(
        [perms.reshape(-1), jnp.broadcast_to(unit_kind[:, None], (units, 128)).reshape(-1)]
    )
    order_other = cross(order_pack, 1)
    *tied, order_other = tie(*[columns_for(offset) for offset in kinds], order_other)
    piece_kinds = dict(zip(kinds, tied))
    x_pieces = [x_own] + [cross(x_own, mask) for mask in range(1, members)]
    if members == CORES:
        qkv_pieces = {0: piece_kinds[0]}
        for stage in range(len(bits)):
            qkv_pieces[1 << stage] = trade(piece_kinds[0], stage)
        for stage in range(1, len(bits)):
            for index in range(1, 1 << stage):
                qkv_pieces[index | 1 << stage] = trade(qkv_pieces[index], stage)
        qkv_pieces = [qkv_pieces[index] for index in range(shards)]
        qkv_masks = [[trade_mask(index, which) for index in range(shards)] for which in (0, 1)]
    else:
        qkv_pieces = [piece_kinds[0]] + [
            cross(piece_kinds[offsets[m]], CORES * m) for m in range(1, shards)
        ]
        qkv_masks = [list(range(shards))] * 2
    order_pack = jnp.where(home_core == core, order_pack, order_other)
    order_count = units * rounds * unit_len
    unit_perm = lax.dynamic_index_in_dim(
        order_pack[:order_count].reshape(units, rounds * unit_len), unit, 0, keepdims=False
    )
    kind_now = lax.dynamic_index_in_dim(
        order_pack[order_count:].reshape(units, 128), unit, 0, keepdims=False
    )[0]
    owner = unit_perm // per_device
    order = (
        lax.bitwise_xor(owner // units, member) * units + (unit - owner % units) % units
    ) * per_device + unit_perm % per_device
    order = order.reshape(rounds, unit_len)
    order = jnp.where(core == 0, order, order[::-1])
    order_row = order.reshape(1, rounds * unit_len)
    order = order.reshape(-1, CLUSTER_ROWS)
    x_here = arrange(order, x_pieces, unit_len, 0)
    x_now = [x_here, cross(x_here, 1)]
    own_masks = [
        jnp.where(core == 0, trade_mask(i, 0), trade_mask(i, 1)) for i in range(1, shards)
    ]
    other_masks = [
        jnp.where(core == 0, trade_mask(i, 1), trade_mask(i, 0)) for i in range(1, shards)
    ]
    zero = jnp.int32(0)
    meta = jnp.stack(
        [kind_now, here, core, member, level, here % units, stays, zero]
        + own_masks
        + other_masks
        + [jnp.where(core == 0, first, second) for first, second in zip(*qkv_masks)]
    ).astype(jnp.int32)

    def half_of(value, axis, length, at):
        return lax.dynamic_slice_in_dim(value, at * length, length, axis=axis)

    packed = jnp.concatenate(
        [half_of(w_down, 0, pack.down_rows, core)]
        + [
            half_of(w_up, 1, model_width, core * pack.blocks + block)
            for block in range(pack.blocks)
        ]
        + [half_of(w_out, 0, pack.out_rows, core)],
        axis=0,
    )
    order_rows = unit_len // CLUSTER_ROWS
    arranged, probs, mixtures, x_turned = [], [], [], []
    *tied, packed, x_now[0] = tie(*qkv_pieces[1:], packed, x_now[0])
    qkv_pieces = qkv_pieces[:1] + tied
    smalls = jnp.stack(
        [
            piece[row_shard : row_shard + small_rows].reshape(-1)[: small.shape[0]]
            for piece in qkv_pieces
        ]
    )
    spots_of = [[masks.index(mask) for mask in range(shards)] for masks in qkv_masks]
    spots_of = jnp.where(core == 0, jnp.array(spots_of[0]), jnp.array(spots_of[1]))
    spots_of = jnp.take(spots_of, lax.bitwise_xor(here, jnp.arange(shards)))
    smalls = jnp.take(smalls, spots_of, axis=0).astype(F32)

    def vectors_at(start, count, length):
        part = smalls[:, start * row_shard : start * row_shard + count * length]
        return (
            part.reshape(shards, count, length).transpose(1, 0, 2).reshape(count, shards * length)
        )

    my_bias = lax.dynamic_index_in_dim(
        vectors_at(0, 2, row_shard).reshape(2, members, head_cols), member, 1, keepdims=False
    )
    my_bias = jnp.pad(my_bias, ((0, 0), (0, padded - head_cols)))
    my_bias = jnp.stack([my_bias[0], jnp.zeros_like(my_bias[0]), my_bias[1]]).reshape(1, -1)
    up_bias = vectors_at(7, 1, feed_width // shards)
    down_bias = smalls[:, small.shape[0] - row_shard :].reshape(1, model_width)
    vectors = jnp.concatenate(
        [vectors_at(2, 5, row_shard), down_bias, jnp.zeros((2, model_width), F32)], axis=0
    )

    weight_pieces = {0: packed}
    for stage in range(len(bits)):
        weight_pieces[1 << stage] = trade(packed, stage)
    for index in range(rounds):
        results = attend(meta, x_now[index], my_bias, qkv_pieces, row_shard, mixtures[-1:])
        for kept, result in zip((arranged, probs, mixtures, x_turned), results):
            kept.append(result)
    cot_now, mixtures[0] = tie(cotangent, mixtures[0])
    cot_chosen = bring_start(cot_now)
    cot_landed = bring(cot_chosen)
    cot_own = brought(cot_chosen, cot_landed)
    for stage in range(1, len(bits)):
        for index in range(1, 1 << stage):
            weight_pieces[index | 1 << stage] = trade(weight_pieces[index], stage)
    att_there, att_sent = [], []
    for mask in range(1, members):
        there = place(
            order_row, mixtures, mask * member_rows, member_rows, 0.5, needs=cot_landed
        )
        att_sent.append(there)
        att_there.append(cross(there[:, :head_cols], mask))
    att_here = place(order_row, mixtures, 0, member_rows, 0.5, needs=att_sent)

    direct = [weight_pieces[index] for index in range(1, shards)]
    swapped = [cross(piece, 1) for piece in direct[:-1]]
    last_piece, att_here = tie(direct[-1], att_here)
    swapped.append(cross(last_piece, 1))
    att_raw = [att_here[:, :head_cols]] + att_there
    if head_cols % CLUSTER_ROWS:
        att_raw = [jnp.concatenate(att_raw, axis=1)]
    block_out, first_low, d_branch, d_ffn, hidden, d_pre, att_turned, *rest = feed(
        pack,
        meta,
        x_own,
        cot_own,
        vectors,
        up_bias,
        att_raw,
        [w_out, w_up, w_down],
        direct + swapped,
    )
    d_att, (row_sums, up_sums) = rest[: len(att_raw)], rest[len(att_raw) :]
    if head_cols % CLUSTER_ROWS:
        d_att = [d_att[0][:, mask * head_cols : (mask + 1) * head_cols] for mask in range(members)]
    d_att = [d_att[0]] + [cross(d_att[mask], mask) for mask in range(1, members)]
    d_att = [jnp.pad(piece, ((0, 0), (0, padded - head_cols))) for piece in d_att]

    table = jnp.stack([core, member]).astype(jnp.int32)
    sending = [index for index in range(shards) if index & 1]
    keeping = [index for index in range(shards) if not index & 1]
    slots = jnp.stack(
        [
            lax.bitwise_xor(here, jnp.where(core == 0, trade_mask(i, 0), trade_mask(i, 1)))
            for i in sending + keeping
        ]
    )
    slots = jnp.concatenate([slots, slots]).astype(jnp.int32)

    def pair_sum(mine, theirs, needs):
        return add_picked(
            slots, [mine, cross(theirs, 1)], shards, len(sending), needs, 20_000_000_000
        )

    theirs_down, mine_down = down_grads(pack, table, d_ffn, hidden)
    theirs_rest, mine_rest = rest_grads(
        pack, table, first_low, d_pre, att_turned, d_branch, [theirs_down]
    )
    down_going, down_kept = pair_sum(mine_down, theirs_down, [theirs_rest])
    rest_going, rest_kept = pair_sum(mine_rest, theirs_rest, [down_going] + d_att[1:])

    def merge(kept, landed, *needs):
        count = kept.shape[0]
        if count == 1:
            table = jnp.zeros((2,), jnp.int32)
            return None, add_picked(table, [kept, landed], 1, None, needs)[0]
        order_now = [i for i in range(count) if i & 1] + [i for i in range(count) if not i & 1]
        table = jnp.array(order_now * 2, jnp.int32)
        return add_picked(table, [kept, landed], count, count // 2, needs)

    grads, d_x = [None] * rounds, [None] * rounds
    needs = [rest_going]
    blocks = unit_len // POS_BLOCK
    spans = [(index, (0, blocks)) for index in reversed(range(rounds))]
    for turn, (index, span) in enumerate(spans):
        grads[index], d_x[index], token = attend_back(
            meta,
            order,
            arranged[index],
            probs[index],
            d_att,
            qkv_pieces,
            row_shard,
            index * order_rows,
            needs,
            span,
            [],
        )
        if turn == 0:
            d_x_there = cross(d_x[index], 1)
            going, kept = join(
                [down_kept, rest_kept], [trade(down_going, 0), trade(rest_going, 0)], [token]
            )
            output_blocks = split_rows(block_out, units, [token])
            output_landed = send_home(output_blocks)
            needs = [kept]
    for stage in range(1, len(bits)):
        going, kept = merge(kept, trade(going, stage), token)

    def level_pieces(block):
        return block.reshape((depth, block.shape[0] // depth) + block.shape[1:])

    def level_scatter(cut):
        return [
            climb(
                lax.dynamic_index_in_dim(cut, lax.bitwise_xor(level, mask), 0, keepdims=False), mask
            )
            for mask in range(1, depth)
        ]

    def level_gather(piece):
        pieces = {0: piece}
        mask = depth // 2
        while mask:
            pieces[mask] = climb(piece, mask)
            mask //= 2
        return pieces

    def level_forward(pieces):
        for index in sorted(range(depth), key=lambda value: value.bit_count()):
            if index not in pieces:
                low = index & -index
                pieces[index] = climb(pieces[index ^ low], low)
        return [pieces[index] for index in range(depth)]

    def by_shard(value):
        count, length = value.shape
        return (
            value.reshape(count, shards, length // shards)
            .transpose(1, 0, 2)
            .reshape(shards, count * length // shards)
        )

    small_grad = jnp.concatenate(
        [by_shard(row_sums[:5]), by_shard(up_sums), by_shard(row_sums[5:6])], axis=1
    )
    small_length = small_grad.shape[1]
    small_lanes = 3 * head_cols
    small_grad = jnp.pad(small_grad, ((0, 0), (0, BIAS_ROW * small_lanes - small_length)))
    small_grad = jnp.pad(
        small_grad.reshape(shards, BIAS_ROW, small_lanes), ((0, 0), (0, 16 - BIAS_ROW), (0, 0))
    )
    extra_rows = 16
    if padded == head_cols:
        joined = qkv_grads(
            x_turned, grads, small_grad, row_shard, output_landed + [kept]
        )
    else:
        qkv_grad = dot(x_turned[0], grads[0]) + dot(x_turned[1], grads[1])
        qkv_grad = qkv_grad.reshape(shards, row_shard, 3, padded)[..., :head_cols]
        bias_sum = sum(jnp.sum(value.astype(F32), axis=0) for value in grads)
        bias_sum = bias_sum.reshape(3, padded)[:, :head_cols].reshape(small_lanes)
        small_grad = small_grad.at[:, BIAS_ROW].set(bias_sum[None])
        joined = jnp.concatenate(
            [qkv_grad.reshape(shards, row_shard, small_lanes), small_grad], axis=1
        ).astype(BF16)
    cut = level_pieces(kept[0])
    landed = level_scatter(cut)
    classes = max(1, members // CORES)
    d_x_parts = [d_x[0], d_x_there]
    order_mine = order_row[:, :unit_len]
    if classes == 1:
        slots_held = jnp.stack(
            [
                lax.bitwise_xor(here, jnp.where(core == 0, trade_mask(i, 0), trade_mask(i, 1)))
                for i in range(shards)
            ]
        )
        held = jnp.stack(
            [
                lax.dynamic_index_in_dim(joined, slots_held[i], 0, keepdims=False)
                for i in range(0, shards, 2)
            ]
        )
        leaving = jnp.stack(
            [
                lax.dynamic_index_in_dim(joined, slots_held[i], 0, keepdims=False)
                for i in range(1, shards, 2)
            ]
        )
        totals = None
    else:
        totals = [None] * classes
        for m in range(shards):
            offset = offsets[m] // CORES
            piece = lax.dynamic_index_in_dim(joined, lax.bitwise_xor(here, m), 0, keepdims=False)
            piece = (piece if m == 0 else cross(piece, CORES * m)).astype(F32)
            totals[offset] = piece if totals[offset] is None else totals[offset] + piece

    d_there = [
        place(
            order_mine,
            d_x_parts,
            mask * member_rows,
            member_rows,
            added=True,
            needs=[joined],
        )
        for mask in range(1, members)
    ]
    if depth > 1:
        picks = jnp.concatenate([level[None], jnp.zeros((depth - 1,), level.dtype)])
        (kept,) = add_picked(
            picks.astype(jnp.int32),
            [cut] + [piece[None] for piece in landed],
            1,
            None,
            d_there,
        )
    gathered = level_gather(kept[0]) if depth > 1 else {0: cut[0]}
    early = [kept] + d_there
    if totals is None:
        held = held + trade(leaving, 0)
        early.append(held)
    d_here = place(
        order_mine,
        d_x_parts,
        0,
        member_rows,
        1.0,
        F32,
        d_branch,
        added=True,
        needs=early,
    )
    d_inputs = d_here
    for mask, there in enumerate(d_there, 1):
        d_inputs = d_inputs + cross(there, mask).astype(F32)
    d_inputs = d_inputs.astype(BF16)
    home_blocks = d_inputs.reshape(units, per_device, model_width)
    home = send_home(home_blocks)
    last = d_inputs
    if totals is None:
        for stage in range(1, len(bits)):
            held = held[::2] + trade(held[1::2], stage)
        last = held
        totals = [held[0]]
    output = home_rows(meta, output_blocks[0], output_landed, BF16, [last])
    totals = jnp.concatenate(totals, axis=0).astype(BF16)
    rows_each = row_shard + extra_rows
    if depth > 1:
        halves = totals.reshape((2, totals.shape[0] // 2) + totals.shape[1:])
        side = level % 2
        mine = lax.dynamic_index_in_dim(halves, side, 0, keepdims=False)
        theirs = lax.dynamic_index_in_dim(halves, 1 - side, 0, keepdims=False)
        half = (mine.astype(F32) + climb(theirs, 1).astype(F32)).astype(BF16)
        masks = [mask for mask in gathered if mask]
        *tied, half = tie(*[gathered[mask] for mask in masks], half)
        gathered.update(zip(masks, tied))
        mask = 2
        while mask < depth:
            half = (half.astype(F32) + climb(half, mask).astype(F32)).astype(BF16)
            mask *= 2
        *home, output, half = tie(*home, output, half)
        other_half = climb(half, 1)
        d_inputs = home_rows(meta, home_blocks[0], home, F32)
        d_inputs, other_half = tie(d_inputs, other_half)
        totals = jnp.concatenate(
            [
                jnp.where(side == 0, half, other_half),
                jnp.where(side == 0, other_half, half),
            ],
            axis=0,
        )
    else:
        d_inputs = home_rows(meta, home_blocks[0], home, F32)
    stacked = stack_up(level_forward(gathered))
    grad_down, grad_up, grad_out = unpack(pack, depth, meta, stacked, cross(stacked, 1))
    if padded == head_cols and members == CORES:
        grad_qkv, bias_out_row, smalls_out = unpack_qkv(
            meta, totals, cross(totals, 1), row_shard, [grad_down]
        )
        smalls_out = smalls_out.reshape(-1)[:small_length]
        bias_out_row = lax.dynamic_slice(bias_out_row, (0, here * row_shard), (3, row_shard))
    else:
        landed = jnp.stack([totals, cross(totals, 1)], axis=0).reshape(
            CORES, classes, rows_each, 3 * head_cols
        )
        smalls_out = jnp.sum(
            landed[:, :, row_shard : row_shard + BIAS_ROW].astype(F32), axis=(0, 1)
        ).reshape(-1)[:small_length]
        landed = (
            landed.transpose(1, 0, 2, 3)
            .reshape(members, rows_each, 3, head_cols)[:, : row_shard + BIAS_ROW + 1]
        )
        if members == 2:
            swap = member == 1
            landed = jnp.stack(
                [
                    jnp.where(swap, landed[1], landed[0]),
                    jnp.where(swap, landed[0], landed[1]),
                ]
            )
        else:
            landed = jnp.take(landed, lax.bitwise_xor(member, jnp.arange(members)), axis=0)
        grad_qkv = landed[:, :row_shard].transpose(1, 2, 0, 3)
        grad_qkv = grad_qkv.reshape(row_shard, 3 * model_width).astype(F32)
        bias_out_row = landed[:, row_shard + BIAS_ROW].astype(F32).transpose(1, 0, 2)
        bias_out_row = lax.dynamic_slice(
            bias_out_row.reshape(3, model_width), (0, here * row_shard), (3, row_shard)
        )

    feed_shard = feed_width // shards
    spots = [0, row_shard, 3 * row_shard, 5 * row_shard]
    return (
        output,
        d_inputs,
        grad_qkv,
        bias_out_row[::2],
        grad_out,
        smalls_out[spots[0] : spots[1]],
        smalls_out[spots[1] : spots[2]].reshape(2, row_shard),
        smalls_out[spots[2] : spots[3]].reshape(2, row_shard),
        grad_up,
        smalls_out[spots[3] : spots[3] + feed_shard],
        grad_down,
        smalls_out[spots[3] + feed_shard :],
    )


def solution(mesh):
    placed = (
        P(("dp", "fsdp"), None),
        P(("dp", "fsdp"), None),
        P("dp", None, None),
        P("dp"),
        P("fsdp", None),
        P(None, "fsdp"),
        P("fsdp", None),
        P("fsdp"),
        P(None, "fsdp"),
        P(None, "fsdp"),
        P("fsdp", None),
        P("fsdp"),
        P("fsdp", None),
        P("fsdp"),
    )
    return jax.shard_map(
        body,
        mesh=mesh,
        in_specs=placed,
        out_specs=(
            P(("dp", "fsdp"), None),
            P(("dp", "fsdp"), None),
            P("fsdp", None),
            P(None, "fsdp"),
            P("fsdp", None),
            P("fsdp"),
            P(None, "fsdp"),
            P(None, "fsdp"),
            P("fsdp", None),
            P("fsdp"),
            P("fsdp", None),
            P("fsdp"),
        ),
        check_vma=False,
    )
```

```python
from functools import partial

import jax
import jax.numpy as jnp
from jax import lax
from jax.experimental import pallas as pl
from jax.experimental.pallas import tpu as pltpu
from jax.sharding import PartitionSpec as P

HEAD_DIM = 64
CORES = 2
NEG_FILL = -1000000000.0
EPSILON = 1e-05
SCALE = HEAD_DIM ** (-0.5)
BIAS_ROW = 2
GRAD_LANES = 384
CLUSTER_ROWS = 128
HALF_ROWS = 64
POS_BLOCK = 512
TOKEN_BLOCK = 512
ROW_BLOCK = 256
FF_BLOCK = 1024
MIB = 1024 * 1024
NT = (((1,), (1,)), ((), ()))
TN = (((0,), (0,)), ((), ()))
F32 = jnp.float32
BF16 = jnp.bfloat16
ANYWHERE = pl.BlockSpec(memory_space=pl.ANY)
IN_SMEM = pl.BlockSpec(memory_space=pltpu.SMEM)


def whole(shape):
    return pl.BlockSpec(shape, lambda i: (0,) * len(shape))


def rows_of(shape):
    return pl.BlockSpec(shape, lambda i: (i,) + (0,) * (len(shape) - 1))


def dot(a, b, dims=(((1,), (0,)), ((), ()))):
    return lax.dot_general(a, b, dims, preferred_element_type=F32)


def params(mib, flops=0, moved=0, share=16):
    return dict(
        compiler_params=pltpu.CompilerParams(
            dimension_semantics=("arbitrary",),
            vmem_limit_bytes=mib * MIB,
        ),
        cost_estimate=pl.CostEstimate(
            flops=flops // share, bytes_accessed=moved // share, transcendentals=0
        ),
    )


def gated(kernel, used, needs):
    if not needs:
        return kernel

    def run(*refs):
        return kernel(*refs[:used], *refs[used + len(needs) :])

    return run


def lane_masks():
    lane = lax.broadcasted_iota(jnp.int32, (CLUSTER_ROWS, CLUSTER_ROWS), 1)
    low = (lane < HEAD_DIM).astype(F32)
    return low.astype(BF16), (1.0 - low).astype(BF16), lane < HEAD_DIM


def corners(first, second):
    blank = jnp.zeros_like(first)
    return jnp.concatenate(
        [
            jnp.concatenate([first, blank], axis=1),
            jnp.concatenate([blank, second], axis=1),
        ],
        axis=0,
    )


def both_heads(rows_now, low, high):
    return jnp.concatenate([rows_now * low, rows_now * high], axis=0)


def equal_ones(left, right):
    return jnp.where(left == right, jnp.ones((), BF16), jnp.zeros((), BF16))


def pick_rows(order_ref, first_row, unit_len):
    parts = []
    lane = lax.broadcasted_iota(jnp.int16, (CLUSTER_ROWS, CLUSTER_ROWS), 1)
    for part in range(POS_BLOCK // CLUSTER_ROWS):
        row = order_ref[pl.ds(first_row + part, 1), :]
        column = jnp.transpose(jnp.broadcast_to(row, (CLUSTER_ROWS, CLUSTER_ROWS)))
        column = column.astype(jnp.int16)
        pieces = [
            equal_ones(column, lane + jnp.int16(base)) for base in range(0, unit_len, CLUSTER_ROWS)
        ]
        parts.append(jnp.concatenate(pieces, axis=1))
    return jnp.concatenate(parts, axis=0)


def load_pieces(meta, x_refs, w_refs, x_all, w_all, sems, row_shard):
    member_rows = x_all.shape[0] // max(1, len(x_refs))
    copies = []
    for index, ref in enumerate(x_refs):
        copies.append(
            pltpu.make_async_copy(
                ref, x_all.at[pl.ds(index * member_rows, member_rows), :], sems.at[index]
            )
        )
    for index, ref in enumerate(w_refs):
        mask = meta[meta.shape[0] - len(w_refs) + index]
        start = pl.multiple_of(lax.bitwise_xor(meta[1], mask) * row_shard, 16)
        copies.append(
            pltpu.make_async_copy(
                ref.at[pl.ds(0, row_shard), :],
                w_all.at[pl.ds(start, row_shard), :],
                sems.at[len(x_refs) + index],
            )
        )
    for copy in copies:
        copy.start()
    for copy in copies:
        copy.wait()


def arrange_kernel(unit_len, first_row, order_ref, *refs):
    x_refs, out_ref = refs[:-1], refs[-1]
    step = pl.program_id(0)
    picks = pick_rows(order_ref, first_row + step * (POS_BLOCK // CLUSTER_ROWS), unit_len)
    rows = x_refs[0].shape[0]
    total = None
    for index, ref in enumerate(x_refs):
        term = dot(picks[:, index * rows : (index + 1) * rows], ref[...])
        total = term if total is None else total + term
    out_ref[...] = total.astype(BF16)


def arrange(order, x_pieces, position_count, first_row):
    member_rows, width = x_pieces[0].shape
    unit_len = member_rows * len(x_pieces)
    return pl.pallas_call(
        partial(arrange_kernel, unit_len, first_row),
        grid=(position_count // POS_BLOCK,),
        in_specs=[whole(order.shape)] + [whole(piece.shape) for piece in x_pieces],
        out_specs=rows_of((POS_BLOCK, width)),
        out_shape=jax.ShapeDtypeStruct((position_count, width), BF16),
        name="arrange",
        **params(20, 2 * position_count * unit_len * width, 6_000_000),
    )(order, *x_pieces)


def attend_kernel(sizes, meta, x_now_ref, bias_ref, *refs):
    shards, row_shard = sizes
    w_refs, refs = refs[:shards], refs[shards:]
    arranged_ref, probs_ref, mixture_ref, turned_ref, w_all, sems = refs
    width = w_all.shape[1] // 3
    step = pl.program_id(0)

    @pl.when(step == 0)
    def _():
        load_pieces(meta, [], w_refs, w_all, w_all, sems, row_shard)

    x_now = x_now_ref[...]
    turned_ref[...] = jnp.transpose(x_now)
    arranged = (dot(x_now, w_all[...]) + bias_ref[...]).astype(BF16)
    arranged_ref[...] = arranged
    low, high, lane_low = lane_masks()
    position = lax.broadcasted_iota(jnp.int32, (CLUSTER_ROWS, CLUSTER_ROWS), 0)
    other = lax.broadcasted_iota(jnp.int32, (CLUSTER_ROWS, CLUSTER_ROWS), 1)
    same_half = (position < HALF_ROWS) == (other < HALF_ROWS)
    allowed = jnp.logical_or(same_half, meta[0] == 1)
    pairs = width // CLUSTER_ROWS
    units = [(part, pair) for part in range(POS_BLOCK // CLUSTER_ROWS) for pair in range(pairs)]
    for index in range(0, len(units), 2):
        queries, keys, values = [], [], []
        for part, pair in units[index : index + 2]:
            rows_now = slice(part * CLUSTER_ROWS, (part + 1) * CLUSTER_ROWS)
            base = pair * CLUSTER_ROWS
            queries.append(arranged[rows_now, base : base + CLUSTER_ROWS] * SCALE)
            one_key = arranged[rows_now, width + base : width + base + CLUSTER_ROWS]
            keys.append(both_heads(one_key, low, high))
            one_value = arranged[rows_now, 2 * width + base : 2 * width + base + CLUSTER_ROWS]
            values.append(both_heads(one_value, low, high))
        both_scores = dot(jnp.concatenate(keys, axis=1), corners(*queries), NT)
        for which, (part, pair) in enumerate(units[index : index + 2]):
            halves = []
            for head in range(2):
                one = both_scores[
                    head * CLUSTER_ROWS : (head + 1) * CLUSTER_ROWS,
                    which * CLUSTER_ROWS : (which + 1) * CLUSTER_ROWS,
                ]
                one = jnp.where(allowed, one, NEG_FILL)
                grown = jnp.exp(one - jnp.max(one, axis=0, keepdims=True))
                halves.append(grown * (1.0 / jnp.sum(grown, axis=0, keepdims=True)))
            probs = jnp.concatenate(halves, axis=0).astype(BF16)
            at = (part * pairs + pair) * 2 * CLUSTER_ROWS
            probs_ref[at : at + 2 * CLUSTER_ROWS, :] = probs
            mixture_ref[
                part * CLUSTER_ROWS : (part + 1) * CLUSTER_ROWS,
                pair * CLUSTER_ROWS : (pair + 1) * CLUSTER_ROWS,
            ] = dot(probs, values[which], TN).astype(BF16)


def attend(meta, x_now, bias, w_pieces, row_shard, needs=()):
    shards = len(w_pieces)
    position_count, model_width = x_now.shape
    cols = w_pieces[0].shape[1]
    width = cols // 3
    pair_rows = 2 * width
    return pl.pallas_call(
        gated(partial(attend_kernel, (shards, row_shard)), 3 + shards, needs),
        grid=(position_count // POS_BLOCK,),
        in_specs=[IN_SMEM, rows_of((POS_BLOCK, model_width)), whole(bias.shape)]
        + [ANYWHERE] * (shards + len(needs)),
        out_specs=[
            rows_of((POS_BLOCK, cols)),
            rows_of((POS_BLOCK // CLUSTER_ROWS * pair_rows, CLUSTER_ROWS)),
            rows_of((POS_BLOCK, width)),
            pl.BlockSpec((model_width, POS_BLOCK), lambda i: (0, i)),
        ],
        out_shape=[
            jax.ShapeDtypeStruct((position_count, cols), BF16),
            jax.ShapeDtypeStruct((position_count // CLUSTER_ROWS * pair_rows, CLUSTER_ROWS), BF16),
            jax.ShapeDtypeStruct((position_count, width), BF16),
            jax.ShapeDtypeStruct((model_width, position_count), BF16),
        ],
        scratch_shapes=[
            pltpu.VMEM((model_width, cols), BF16),
            pltpu.SemaphoreType.DMA((shards,)),
        ],
        name="attend",
        **params(
            60, 8 * position_count * (model_width * cols + 4 * CLUSTER_ROWS * width), 18_000_000, 1
        ),
    )(meta, x_now, bias, *w_pieces, *needs)


def place_kernel(sizes, scale, has_base, order_row_ref, *refs):
    unit_len, first_token, added = sizes
    base_ref = refs[0] if has_base else None
    refs = refs[1 if has_base else 0 :]
    if added:
        first_ref, second_ref, out_ref, held = refs

        @pl.when(pl.program_id(0) == 0)
        def _():
            held[...] = (first_ref[...].astype(F32) + second_ref[...].astype(F32)).astype(BF16)

        source_refs = [held]
    else:
        source_refs, out_ref = refs[:-1], refs[-1]
    block_rows = out_ref.shape[0]
    first = jnp.full((1, 1), first_token + pl.program_id(0) * block_rows, jnp.int32)
    token = lax.broadcasted_iota(jnp.int16, (block_rows, unit_len), 0)
    total = None
    for index, ref in enumerate(source_refs):
        row = order_row_ref[:, index * unit_len : (index + 1) * unit_len] - first
        row = jnp.broadcast_to(row, (16, unit_len)).astype(jnp.int16)
        row = jnp.concatenate([row] * (block_rows // 16), axis=0)
        term = dot(equal_ones(row, token), ref[...])
        total = term if total is None else total + term
    if scale != 1.0:
        total = total * scale
    if has_base:
        total = total + base_ref[...].astype(F32)
    out_ref[...] = total.astype(out_ref.dtype)


def place(
    order_row,
    sources,
    first_token,
    row_count,
    scale=1.0,
    dtype=BF16,
    base=None,
    added=False,
    needs=(),
):
    unit_len, width = sources[0].shape
    block_rows = min(TOKEN_BLOCK, row_count)
    extra = [] if base is None else [base]
    return pl.pallas_call(
        gated(
            partial(place_kernel, (unit_len, first_token, added), scale, base is not None),
            1 + len(extra) + len(sources),
            needs,
        ),
        grid=(row_count // block_rows,),
        in_specs=[whole(order_row.shape)]
        + [rows_of((block_rows, width))] * len(extra)
        + [whole(source.shape) for source in sources]
        + [ANYWHERE] * len(needs),
        out_specs=rows_of((block_rows, width)),
        out_shape=jax.ShapeDtypeStruct((row_count, width), dtype),
        scratch_shapes=[pltpu.VMEM((unit_len, width), BF16)] if added else [],
        name="place",
        **params(
            32 if added else 20,
            16 * row_count * unit_len * width,
            10_000_000,
            1,
        ),
    )(order_row, *extra, *sources, *needs)


def attend_back_kernel(sizes, meta, order_ref, arranged_ref, probs_ref, *refs):
    members, shards, unit_len, row_shard, first_row, start = sizes
    g_refs, refs = refs[:members], refs[members:]
    w_refs, refs = refs[:shards], refs[shards:]
    grads_ref, d_x_ref, token_ref, g_all, w_all, sems = refs
    width = w_all.shape[1] // 3
    step = pl.program_id(0)

    @pl.when(step == 0)
    def _():
        load_pieces(meta, g_refs, w_refs, g_all, w_all, sems, row_shard)
        token_ref[...] = jnp.zeros_like(token_ref)

    at_row = first_row + (start + step) * (POS_BLOCK // CLUSTER_ROWS)
    picks = pick_rows(order_ref, at_row, unit_len)
    d_mixture = dot(picks, g_all[...]).astype(BF16)
    low, high, lane_low = lane_masks()
    pairs = width // CLUSTER_ROWS
    units = [(part, pair) for part in range(POS_BLOCK // CLUSTER_ROWS) for pair in range(pairs)]
    for index in range(0, len(units), 2):
        values, d_rows = [], []
        for part, pair in units[index : index + 2]:
            rows_now = slice(part * CLUSTER_ROWS, (part + 1) * CLUSTER_ROWS)
            base = pair * CLUSTER_ROWS
            one_value = arranged_ref[rows_now, 2 * width + base : 2 * width + base + CLUSTER_ROWS]
            values.append(both_heads(one_value, low, high))
            d_rows.append(d_mixture[rows_now, base : base + CLUSTER_ROWS])
        both_probs = dot(jnp.concatenate(values, axis=1), corners(*d_rows), NT)
        for which, (part, pair) in enumerate(units[index : index + 2]):
            rows_now = slice(part * CLUSTER_ROWS, (part + 1) * CLUSTER_ROWS)
            base = pair * CLUSTER_ROWS
            q_lanes = slice(base, base + CLUSTER_ROWS)
            k_lanes = slice(width + base, width + base + CLUSTER_ROWS)
            v_lanes = slice(2 * width + base, 2 * width + base + CLUSTER_ROWS)
            queries = arranged_ref[rows_now, q_lanes] * SCALE
            keys = arranged_ref[rows_now, k_lanes] * SCALE
            at = (part * pairs + pair) * 2 * CLUSTER_ROWS
            probs = probs_ref[at : at + 2 * CLUSTER_ROWS, :]
            d_probs = both_probs[:, which * CLUSTER_ROWS : (which + 1) * CLUSTER_ROWS]
            pieces = []
            for head in range(2):
                rows = slice(head * CLUSTER_ROWS, (head + 1) * CLUSTER_ROWS)
                weight = probs[rows].astype(F32)
                d_one = d_probs[rows]
                inner = jnp.sum(weight * d_one, axis=0, keepdims=True)
                pieces.append(weight * (d_one - inner))
            d_scores = jnp.concatenate(pieces, axis=0).astype(BF16)
            d_query = dot(d_scores, both_heads(keys, low, high), TN)
            d_pair = dot(
                jnp.concatenate([probs, d_scores], axis=1), corners(d_rows[which], queries)
            )
            d_values, d_keys = d_pair[:, :CLUSTER_ROWS], d_pair[:, CLUSTER_ROWS:]
            grads_ref[rows_now, q_lanes] = d_query.astype(BF16)
            grads_ref[rows_now, k_lanes] = jnp.where(
                lane_low, d_keys[:CLUSTER_ROWS], d_keys[CLUSTER_ROWS:]
            ).astype(BF16)
            grads_ref[rows_now, v_lanes] = jnp.where(
                lane_low, d_values[:CLUSTER_ROWS], d_values[CLUSTER_ROWS:]
            ).astype(BF16)
    grads = grads_ref[...]
    d_x_ref[...] = dot(grads, w_all[...], NT).astype(BF16)


def attend_back(
    meta, order, arranged, probs, g_pieces, w_pieces, row_shard, first_row, needs, span, into
):
    members, shards = len(g_pieces), len(w_pieces)
    member_rows, width = g_pieces[0].shape
    unit_len = members * member_rows
    position_count, cols = arranged.shape
    model_width = row_shard * shards
    start, stop = span
    pair_rows = POS_BLOCK // CLUSTER_ROWS * 2 * width
    used = 4 + members + shards

    def block(shape):
        return pl.BlockSpec(shape, lambda i: (start + i, 0))

    return pl.pallas_call(
        gated(
            partial(attend_back_kernel, (members, shards, unit_len, row_shard, first_row, start)),
            used,
            list(into) + list(needs),
        ),
        grid=(stop - start,),
        in_specs=[
            IN_SMEM,
            whole(order.shape),
            block((POS_BLOCK, cols)),
            block((pair_rows, CLUSTER_ROWS)),
        ]
        + [ANYWHERE] * (members + shards + len(into) + len(needs)),
        out_specs=[block((POS_BLOCK, cols)), block((POS_BLOCK, model_width)), whole((8, 128))],
        out_shape=[
            jax.ShapeDtypeStruct((position_count, cols), BF16),
            jax.ShapeDtypeStruct((position_count, model_width), BF16),
            jax.ShapeDtypeStruct((8, 128), F32),
        ],
        input_output_aliases={used + index: index for index in range(len(into))},
        scratch_shapes=[
            pltpu.VMEM((unit_len, width), BF16),
            pltpu.VMEM((model_width, cols), BF16),
            pltpu.SemaphoreType.DMA((members + shards,)),
        ],
        name="attend_back",
        **params(
            60,
            12 * (stop - start) * POS_BLOCK * (unit_len * width + model_width * cols),
            20_000_000,
            1,
        ),
    )(meta, order, arranged, probs, *g_pieces, *w_pieces, *into, *needs)


def normalise(summed):
    average = jnp.mean(summed, axis=-1, keepdims=True)
    centred = summed - average
    spread = jnp.mean(centred * centred, axis=-1, keepdims=True)
    scale_inv = lax.rsqrt(spread + EPSILON)
    return centred * scale_inv, scale_inv


def normalise_back(grad_out, normed, scale_inv, gain_row):
    scaled = grad_out * gain_row
    return scale_inv * (
        scaled
        - jnp.mean(scaled, axis=-1, keepdims=True)
        - normed * jnp.mean(scaled * normed, axis=-1, keepdims=True)
    )


def column_sum(rows_now):
    return jnp.sum(rows_now, axis=0, keepdims=True)


def gelu_parts(value):
    below = 0.5 + 0.5 * lax.erf(value * 0.7071067811865476)
    bell = jnp.exp(value * value * -0.5) * 0.3989422804014327
    return value * below, below + value * bell


class Pack:
    def __init__(self, model_width, feed_width, shards, units, depth):
        self.model_width, self.feed_width, self.shards = model_width, feed_width, shards
        self.row_shard = model_width // shards
        self.feed_shard = feed_width // shards
        self.down_rows = self.feed_shard // CORES
        self.blocks = feed_width // CORES // model_width
        self.up_at = self.down_rows
        self.out_at = self.up_at + self.blocks * self.row_shard
        self.out_rows = self.row_shard // CORES
        self.used = self.out_at + self.out_rows
        unit = 16 * depth
        self.rows = -(-self.used // unit) * unit
        self.rest_rows = self.rows - self.down_rows
        self.units = units
        self.group = units * self.row_shard

    def out_start(self, shard, member):
        return (
            lax.bitwise_xor(jnp.int32(shard) // self.units, member) * self.group
            + (shard % self.units) * self.row_shard
        )


def feed_kernel(pack, att_count, meta, x_ref, cot_ref, vec_ref, up_bias_ref, *refs):
    shards = pack.shards
    att_refs, refs = refs[:att_count], refs[att_count:]
    own_out, own_up, own_down = refs[:3]
    refs = refs[3:]
    pieces, refs = refs[: 2 * (shards - 1)], refs[2 * (shards - 1) :]
    out_ref, first_turned_ref, d_branch_ref, d_ffn_turned_ref, hidden_ref, d_pre_ref = refs[:6]
    att_turned_ref = refs[6]
    refs = refs[7:]
    d_att_refs, refs = refs[:att_count], refs[att_count:]
    sums_ref, up_sums_ref, w_out, w_up, w_down, slope, total, sems = refs
    step = pl.program_id(0)
    here, core, member = meta[1], meta[2], meta[3]
    feed_width = pack.feed_width

    def loads(kind):
        copies = []

        def add(source, target):
            copies.append(pltpu.make_async_copy(source, target, sems.at[kind, len(copies)]))

        if kind == 0:
            start = pl.multiple_of(pack.out_start(here, member), 16)
            add(own_out, w_out.at[pl.ds(start, pack.row_shard), :])
        elif kind == 1:
            start = pl.multiple_of(here * pack.row_shard, 16)
            add(own_up, w_up.at[pl.ds(start, pack.row_shard), :])
        else:
            start = pl.multiple_of(here * pack.feed_shard, 16)
            add(own_down, w_down.at[pl.ds(start, pack.feed_shard), :])
        for index, ref in enumerate(pieces):
            peer = lax.bitwise_xor(here, meta[8 + index])
            half = core if index < shards - 1 else 1 - core
            if kind == 0:
                start = pack.out_start(peer, member) + half * pack.out_rows
                start = pl.multiple_of(start, 16)
                add(
                    ref.at[pl.ds(pack.out_at, pack.out_rows), :],
                    w_out.at[pl.ds(start, pack.out_rows), :],
                )
            elif kind == 1:
                start = pl.multiple_of(peer * pack.row_shard, 16)
                for block in range(pack.blocks):
                    lane = pl.multiple_of(
                        (half * pack.blocks + block) * pack.model_width, CLUSTER_ROWS
                    )
                    add(
                        ref.at[pl.ds(pack.up_at + block * pack.row_shard, pack.row_shard), :],
                        w_up.at[pl.ds(start, pack.row_shard), pl.ds(lane, pack.model_width)],
                    )
            else:
                start = pl.multiple_of(peer * pack.feed_shard + half * pack.down_rows, 16)
                add(
                    ref.at[pl.ds(0, pack.down_rows), :],
                    w_down.at[pl.ds(start, pack.down_rows), :],
                )
        return copies

    @pl.when(step == 0)
    def _():
        for kind in range(3):
            for copy in loads(kind):
                copy.start()
        sums_ref[...] = jnp.zeros_like(sums_ref)
        up_sums_ref[...] = jnp.zeros_like(up_sums_ref)
        for copy in loads(0):
            copy.wait()

    bias_out, gain_one, gain_two = vec_ref[0:1, :], vec_ref[1:2, :], vec_ref[2:3, :]
    shift_one, shift_two, bias_down = vec_ref[3:4, :], vec_ref[4:5, :], vec_ref[5:6, :]
    att_width = att_refs[0].shape[1]
    summed = x_ref[...].astype(F32) + bias_out
    for index, ref in enumerate(att_refs):
        summed += dot(ref[...], w_out[index * att_width : (index + 1) * att_width, :])
    normed_one, inv_one = normalise(summed)
    first = normed_one * gain_one + shift_one
    first_low = first.astype(BF16)
    first_turned_ref[...] = jnp.transpose(first_low)
    for index, ref in enumerate(att_refs):
        att_turned_ref[index * att_width : (index + 1) * att_width, :] = jnp.transpose(ref[...])

    @pl.when(step == 0)
    def _():
        for kind in (1, 2):
            for copy in loads(kind):
                copy.wait()

    total[...] = first + bias_down

    @pl.loop(0, feed_width // FF_BLOCK)
    def _(block):
        lanes = pl.ds(pl.multiple_of(block * FF_BLOCK, FF_BLOCK), FF_BLOCK)
        pre = dot(first_low, w_up[:, lanes]) + up_bias_ref[:, lanes]
        hidden, slope_now = gelu_parts(pre)
        hidden = hidden.astype(BF16)
        hidden_ref[:, lanes] = hidden
        slope[:, lanes] = slope_now
        total[...] += dot(hidden, w_down[lanes, :])

    second = total[...]
    normed_two, inv_two = normalise(second)
    out_ref[...] = (normed_two * gain_two + shift_two).astype(BF16)
    top = cot_ref[...].astype(F32)
    d_second = normalise_back(top, normed_two, inv_two, gain_two)
    d_ffn = d_second.astype(BF16)
    d_ffn_turned_ref[...] = jnp.transpose(d_ffn)
    total[...] = d_second

    @pl.loop(0, feed_width // FF_BLOCK)
    def _(block):
        lanes = pl.ds(pl.multiple_of(block * FF_BLOCK, FF_BLOCK), FF_BLOCK)
        d_pre = (dot(d_ffn, w_down[lanes, :], NT) * slope[:, lanes]).astype(BF16)
        d_pre_ref[:, lanes] = d_pre
        up_sums_ref[:, lanes] += column_sum(d_pre.astype(F32))
        total[...] += dot(d_pre, w_up[:, lanes], NT)

    d_first = total[...]
    d_lower = normalise_back(d_first, normed_one, inv_one, gain_one)
    d_branch = d_lower.astype(BF16)
    d_branch_ref[...] = d_branch
    for index, ref in enumerate(d_att_refs):
        back = dot(d_branch, w_out[index * att_width : (index + 1) * att_width, :], NT)
        ref[...] = (0.5 * back).astype(BF16)
    sums_ref[0:1, :] += column_sum(d_branch.astype(F32))
    sums_ref[1:2, :] += column_sum(d_first * normed_one)
    sums_ref[2:3, :] += column_sum(top * normed_two)
    sums_ref[3:4, :] += column_sum(d_first)
    sums_ref[4:5, :] += column_sum(top)
    sums_ref[5:6, :] += column_sum(d_ffn.astype(F32))


def feed(pack, meta, x_own, cot_own, vectors, up_bias, att, own, pieces):
    row_count, model_width = x_own.shape
    feed_width = pack.feed_width
    att_width = att[0].shape[1]
    one = rows_of((ROW_BLOCK, model_width))
    wide = rows_of((ROW_BLOCK, feed_width))
    narrow = rows_of((ROW_BLOCK, att_width))
    turned = pl.BlockSpec((model_width, ROW_BLOCK), lambda i: (0, i))
    turned_shape = jax.ShapeDtypeStruct((model_width, row_count), BF16)

    def like(width):
        return jax.ShapeDtypeStruct((row_count, width), BF16)

    return pl.pallas_call(
        partial(feed_kernel, pack, len(att)),
        grid=(row_count // ROW_BLOCK,),
        in_specs=[IN_SMEM, one, one, whole(vectors.shape), whole(up_bias.shape)]
        + [narrow] * len(att)
        + [ANYWHERE] * (3 + len(pieces)),
        out_specs=[one, turned, one, turned, wide, wide, turned]
        + [narrow] * len(att)
        + [whole((8, model_width)), whole((1, feed_width))],
        out_shape=[
            like(model_width),
            turned_shape,
            like(model_width),
            turned_shape,
            like(feed_width),
            like(feed_width),
            turned_shape,
        ]
        + [like(att_width)] * len(att)
        + [
            jax.ShapeDtypeStruct((8, model_width), F32),
            jax.ShapeDtypeStruct((1, feed_width), F32),
        ],
        scratch_shapes=[
            pltpu.VMEM((model_width, model_width), BF16),
            pltpu.VMEM((model_width, feed_width), BF16),
            pltpu.VMEM((feed_width, model_width), BF16),
            pltpu.VMEM((ROW_BLOCK, feed_width), F32),
            pltpu.VMEM((ROW_BLOCK, model_width), F32),
            pltpu.SemaphoreType.DMA((3, 1 + pack.blocks * len(pieces))),
        ],
        name="feed",
        **params(
            40, 2 * row_count * model_width * (2 * model_width + 4 * feed_width), 40_000_000
        ),
    )(meta, x_own, cot_own, vectors, up_bias, *att, *own, *pieces)


def down_grads_kernel(pack, table, d_ffn_ref, hidden_ref, theirs_ref, mine_ref, made, sems):
    step = pl.program_id(0)
    core = table[0]

    def stores(shard):
        return [
            pltpu.make_async_copy(made.at[1 - core, shard], theirs_ref.at[shard], sems.at[0, shard]),
            pltpu.make_async_copy(made.at[core, shard], mine_ref.at[shard], sems.at[1, shard]),
        ]

    grad = dot(d_ffn_ref[...], hidden_ref[...]).astype(BF16)
    for half in range(CORES):
        for lane in range(0, pack.model_width, pack.feed_shard):
            begin = half * (pack.model_width // CORES) + lane // pack.feed_shard * pack.down_rows
            made[half, step, :, lane : lane + pack.feed_shard] = grad[
                begin : begin + pack.down_rows
            ]
    for copy in stores(step):
        copy.start()

    @pl.when(step == pack.shards - 1)
    def _():
        for shard in range(pack.shards):
            for copy in stores(shard):
                copy.wait()


def down_grads(pack, table, d_ffn, hidden):
    model_width, row_count = d_ffn.shape
    shape = (pack.shards, pack.down_rows, model_width)
    return pl.pallas_call(
        partial(down_grads_kernel, pack),
        grid_spec=pltpu.PrefetchScalarGridSpec(
            num_scalar_prefetch=1,
            grid=(pack.shards,),
            in_specs=[
                pl.BlockSpec(d_ffn.shape, lambda step, table: (0, 0)),
                pl.BlockSpec((row_count, pack.feed_shard), lambda step, table: (0, step)),
            ],
            out_specs=[ANYWHERE] * 2,
            scratch_shapes=[
                pltpu.VMEM((CORES,) + shape, BF16),
                pltpu.SemaphoreType.DMA((CORES, pack.shards)),
            ],
        ),
        out_shape=[jax.ShapeDtypeStruct(shape, BF16)] * 2,
        name="down_grads",
        **params(60, 2 * row_count * model_width * pack.feed_width, 10_000_000),
    )(table, d_ffn, hidden)


def rest_grads_kernel(
    pack, table, first_ref, d_pre_ref, att_ref, d_branch_ref, theirs_ref, mine_ref, *scratch
):
    att, d_branch, tile, made, in_sems, sems = scratch
    step = pl.program_id(0)
    core, member = table[0], table[1]
    shards, blocks = pack.shards, pack.blocks
    out_at = pack.out_at - pack.down_rows

    loads = [
        pltpu.make_async_copy(att_ref, att, in_sems.at[0]),
        pltpu.make_async_copy(d_branch_ref, d_branch, in_sems.at[1]),
    ]

    def store(half, start, rows, sem):
        there = (slice(None), pl.ds(start, rows), slice(None))

        def copy(target):
            return pltpu.make_async_copy(
                made.at[(half,) + there], target.at[there], sems.at[half, sem]
            )

        return copy

    def both(half, start, rows, sem, act):
        copy = store(half, start, rows, sem)

        @pl.when(core == half)
        def _():
            act(copy(mine_ref))

        @pl.when(core != half)
        def _():
            act(copy(theirs_ref))

    @pl.when(step == 0)
    def _():
        for copy in loads:
            copy.start()

    @pl.when(step < CORES * blocks)
    def _():
        grad = dot(first_ref[...], d_pre_ref[...]).astype(BF16)
        start = pl.multiple_of(step % blocks * pack.row_shard, 16)
        for shard in range(shards):
            made[step // blocks, shard, pl.ds(start, pack.row_shard), :] = grad[
                shard * pack.row_shard : (shard + 1) * pack.row_shard
            ]

    for half in range(CORES):

        @pl.when(step == (half + 1) * blocks - 1)
        def _(half=half):
            both(half, 0, out_at, 0, lambda copy: copy.start())

    @pl.when(step == CORES * blocks)
    def _():
        for copy in loads:
            copy.wait()
        tile[...] = dot(att[...], d_branch[...])
        spare = pack.rows - pack.used
        for half in range(CORES):
            for shard in range(shards):
                start = pack.out_start(shard, member) + half * pack.out_rows
                start = pl.multiple_of(start, 16)
                made[half, shard, out_at : out_at + pack.out_rows, :] = tile[
                    pl.ds(start, pack.out_rows), :
                ].astype(BF16)
                if spare:
                    made[half, shard, out_at + pack.out_rows :, :] = jnp.zeros(
                        (spare, pack.model_width), BF16
                    )
            both(half, out_at, pack.rest_rows - out_at, 1, lambda copy: copy.start())
        for half in range(CORES):
            both(half, 0, out_at, 0, lambda copy: copy.wait())
            both(half, out_at, pack.rest_rows - out_at, 1, lambda copy: copy.wait())


def rest_grads(pack, table, first_low, d_pre, att, d_branch, needs=()):
    model_width, row_count = first_low.shape
    shape = (pack.shards, pack.rest_rows, model_width)
    steps = CORES * pack.blocks
    return pl.pallas_call(
        gated(partial(rest_grads_kernel, pack), 5, needs),
        grid_spec=pltpu.PrefetchScalarGridSpec(
            num_scalar_prefetch=1,
            grid=(steps + 1,),
            in_specs=[
                pl.BlockSpec(first_low.shape, lambda step, table: (0, 0)),
                pl.BlockSpec(
                    (row_count, model_width),
                    lambda step, table: (0, jnp.minimum(step, steps - 1)),
                ),
            ]
            + [ANYWHERE] * (2 + len(needs)),
            out_specs=[ANYWHERE] * 2,
            scratch_shapes=[
                pltpu.VMEM((model_width, row_count), BF16),
                pltpu.VMEM((row_count, model_width), BF16),
                pltpu.VMEM((model_width, model_width), F32),
                pltpu.VMEM((CORES,) + shape, BF16),
                pltpu.SemaphoreType.DMA((2,)),
                pltpu.SemaphoreType.DMA((CORES, 2)),
            ],
        ),
        out_shape=[jax.ShapeDtypeStruct(shape, BF16)] * 2,
        name="rest_grads",
        **params(60, 2 * row_count * model_width * (pack.feed_width + model_width), 10_000_000),
    )(table, first_low, d_pre, att, d_branch, *needs)


def qkv_grads_kernel(rounds, x_refs_then, *refs):
    refs = (x_refs_then,) + refs
    x_refs, grad_refs = refs[:rounds], refs[rounds : 2 * rounds]
    small_ref, out_ref = refs[2 * rounds :]
    shards, rows, _ = out_ref.shape
    row_shard = rows - small_ref.shape[1]
    total, sums = None, None
    for x_ref, grad_ref in zip(x_refs, grad_refs):
        grads = grad_ref[...]
        term = dot(x_ref[...], grads)
        down = column_sum(grads.astype(F32))
        total = term if total is None else total + term
        sums = down if sums is None else sums + down
    total = total.astype(BF16)
    row = lax.broadcasted_iota(jnp.int32, small_ref.shape[1:], 0)
    for shard in range(shards):
        out_ref[shard, :row_shard, :] = total[shard * row_shard : (shard + 1) * row_shard]
        last = jnp.where(row == BIAS_ROW, sums, small_ref[shard])
        out_ref[shard, row_shard:, :] = last.astype(BF16)


def qkv_grads(x_turned, grads, small, row_shard, needs=()):
    rounds = len(grads)
    model_width, positions = x_turned[0].shape
    cols = grads[0].shape[1]
    shards, extra, _ = small.shape
    block = GRAD_LANES if cols % GRAD_LANES == 0 else cols
    return pl.pallas_call(
        gated(partial(qkv_grads_kernel, rounds), 2 * rounds + 1, needs),
        grid=(cols // block,),
        in_specs=[whole((model_width, positions))] * rounds
        + [pl.BlockSpec((positions, block), lambda i: (0, i))] * rounds
        + [pl.BlockSpec((shards, extra, block), lambda i: (0, 0, i))]
        + [ANYWHERE] * len(needs),
        out_specs=pl.BlockSpec((shards, row_shard + extra, block), lambda i: (0, 0, i)),
        out_shape=jax.ShapeDtypeStruct((shards, row_shard + extra, cols), BF16),
        name="qkv_grads",
        **params(60, 2 * rounds * positions * model_width * cols, 18_000_000),
    )(*x_turned, *grads, small, *needs)


def add_picked_kernel(count, first, table, *refs):
    in_refs, out_refs = refs[:count], refs[count:]
    if count == 2:
        total = in_refs[0][...] + in_refs[1][...]
    else:
        total = in_refs[0][...].astype(F32)
        for ref in in_refs[1:]:
            total = total + ref[...].astype(F32)
        total = total.astype(BF16)
    if len(out_refs) == 1:
        out_refs[0][...] = total
        return

    @pl.when(pl.program_id(0) < first)
    def _():
        out_refs[0][...] = total

    @pl.when(pl.program_id(0) >= first)
    def _():
        out_refs[1][...] = total


def add_picked(table, arrays, steps, first=None, needs=(), work=0):
    _, rows, cols = arrays[0].shape
    parts = 2 if rows % 32 == 0 and steps == 1 else 1
    block = (1, rows // parts, cols)
    spec = [
        pl.BlockSpec(block, lambda s, p, t, k=k: (t[k * steps + s], p, 0))
        for k in range(len(arrays))
    ]
    if first is None:
        out_specs = [pl.BlockSpec(block, lambda s, p, t: (s, p, 0))]
        counts = [steps]
    else:
        out_specs = [
            pl.BlockSpec(
                block,
                lambda s, p, t: (
                    jnp.minimum(s, first - 1),
                    jnp.where(s < first, p, parts - 1),
                    0,
                ),
            ),
            pl.BlockSpec(
                block,
                lambda s, p, t: (jnp.maximum(s - first, 0), jnp.where(s < first, 0, p), 0),
            ),
        ]
        counts = [first, steps - first]
    return pl.pallas_call(
        gated(partial(add_picked_kernel, len(arrays), first), 1 + len(arrays), needs),
        grid_spec=pltpu.PrefetchScalarGridSpec(
            num_scalar_prefetch=1,
            grid=(steps, parts),
            in_specs=spec + [ANYWHERE] * len(needs),
            out_specs=out_specs,
        ),
        out_shape=[jax.ShapeDtypeStruct((n, rows, cols), BF16) for n in counts],
        name="add_picked",
        compiler_params=pltpu.CompilerParams(
            dimension_semantics=("arbitrary", "arbitrary"),
            vmem_limit_bytes=(60 if steps > 1 else 12) * MIB,
        ),
        cost_estimate=pl.CostEstimate(flops=work, bytes_accessed=1_000_000, transcendentals=0),
    )(table, *arrays, *needs)


def join_kernel(count, down_kept, down_landed, rest_kept, rest_landed, *outs):
    rows = down_kept.shape[1]
    for index in range(count):
        target = outs[1 - index % 2] if count > 1 else outs[0]
        place_now = index // 2
        target[place_now, :rows, :] = down_kept[index] + down_landed[index]
        target[place_now, rows:, :] = rest_kept[index] + rest_landed[index]


def join(kept, landed, needs=()):
    count = kept[0].shape[0]
    rows = kept[0].shape[1] + kept[1].shape[1]
    shape = jax.ShapeDtypeStruct(((count + 1) // 2, rows, kept[0].shape[2]), BF16)
    vmem = pl.BlockSpec(memory_space=pltpu.VMEM)
    outs = pl.pallas_call(
        gated(partial(join_kernel, count), 4, needs),
        in_specs=[vmem] * 4 + [ANYWHERE] * len(needs),
        out_specs=[vmem] * min(count, 2),
        out_shape=[shape] * min(count, 2),
        name="join",
        compiler_params=pltpu.CompilerParams(vmem_limit_bytes=24 * MIB),
        cost_estimate=pl.CostEstimate(flops=0, bytes_accessed=200_000, transcendentals=0),
    )(kept[0], landed[0], kept[1], landed[1], *needs)
    return outs if count > 1 else (None, outs[0])


def stack_kernel(count, *refs):
    for index in range(count):
        refs[count][index] = refs[index][...]


def home_kernel(count, meta, own_ref, *refs):
    out_ref = refs[count]
    rows = refs[0].shape[0]
    for index in range(count):
        start = pl.multiple_of((meta[5] + index) % count * rows, 16)
        target = out_ref.at[pl.ds(start, rows), :]
        if index:
            target[...] = refs[index][...].astype(out_ref.dtype)
            continue

        @pl.when(meta[6] == 0)
        def _():
            target[...] = refs[0][...].astype(out_ref.dtype)

        @pl.when(meta[6] == 1)
        def _():
            target[...] = own_ref[...].astype(out_ref.dtype)


def home_rows(meta, own, landed, dtype, needs=()):
    rows, cols = own.shape
    vmem = pl.BlockSpec(memory_space=pltpu.VMEM)
    return pl.pallas_call(
        gated(partial(home_kernel, len(landed)), 2 + len(landed), needs),
        in_specs=[IN_SMEM, vmem] + [vmem] * len(landed) + [ANYWHERE] * len(needs),
        out_specs=vmem,
        out_shape=jax.ShapeDtypeStruct((len(landed) * rows, cols), dtype),
        name="home_rows",
        compiler_params=pltpu.CompilerParams(vmem_limit_bytes=60 * MIB),
        cost_estimate=pl.CostEstimate(flops=0, bytes_accessed=100_000, transcendentals=0),
    )(meta, own, *landed, *needs)


def split_kernel(in_ref, *out_refs):
    rows = out_refs[0].shape[0]
    for index, ref in enumerate(out_refs):
        ref[...] = in_ref[index * rows : (index + 1) * rows, :]


def split_rows(value, count, needs=()):
    rows = value.shape[0] // count
    vmem = pl.BlockSpec(memory_space=pltpu.VMEM)
    return pl.pallas_call(
        gated(split_kernel, 1, needs),
        in_specs=[vmem] + [ANYWHERE] * len(needs),
        out_specs=[vmem] * count,
        out_shape=[jax.ShapeDtypeStruct((rows, value.shape[1]), value.dtype)] * count,
        name="split_rows",
        compiler_params=pltpu.CompilerParams(vmem_limit_bytes=12 * MIB),
        cost_estimate=pl.CostEstimate(flops=0, bytes_accessed=100_000, transcendentals=0),
    )(value, *needs)


def stack_up(pieces, needs=()):
    vmem = pl.BlockSpec(memory_space=pltpu.VMEM)
    return pl.pallas_call(
        gated(partial(stack_kernel, len(pieces)), len(pieces), needs),
        in_specs=[vmem] * len(pieces) + [ANYWHERE] * len(needs),
        out_specs=vmem,
        out_shape=jax.ShapeDtypeStruct((len(pieces),) + pieces[0].shape, BF16),
        name="stack_up",
        compiler_params=pltpu.CompilerParams(vmem_limit_bytes=24 * MIB),
        cost_estimate=pl.CostEstimate(flops=0, bytes_accessed=100_000, transcendentals=0),
    )(*pieces, *needs)


def unpack_kernel(pack, depth, meta, mine_ref, other_ref, down_ref, up_ref, out_ref, ordered):
    core, level = meta[2], meta[4]
    rows = pack.rows // depth
    for mask in range(depth):
        start = pl.multiple_of(lax.bitwise_xor(level, mask) * rows, 16)
        ordered[core, pl.ds(start, rows), :] = mine_ref[mask]
        ordered[1 - core, pl.ds(start, rows), :] = other_ref[mask]
    turned = []
    for half in range(CORES):
        for lane in range(0, pack.model_width, pack.feed_shard):
            turned.append(ordered[half, : pack.down_rows, lane : lane + pack.feed_shard])
    down_ref[...] = jnp.transpose(jnp.concatenate(turned, axis=0)).astype(F32)
    for half in range(CORES):
        for block in range(pack.blocks):
            lane = (half * pack.blocks + block) * pack.model_width
            start = pack.up_at + block * pack.row_shard
            up_ref[:, lane : lane + pack.model_width] = ordered[
                half, start : start + pack.row_shard, :
            ].astype(F32)
        out_ref[half * pack.out_rows : (half + 1) * pack.out_rows, :] = ordered[
            half, pack.out_at : pack.out_at + pack.out_rows, :
        ].astype(F32)


def unpack(pack, depth, meta, mine, other):
    vmem = pl.BlockSpec(memory_space=pltpu.VMEM)
    return pl.pallas_call(
        partial(unpack_kernel, pack, depth),
        in_specs=[IN_SMEM, vmem, vmem],
        out_specs=[vmem] * 3,
        out_shape=[
            jax.ShapeDtypeStruct((pack.feed_shard, pack.model_width), F32),
            jax.ShapeDtypeStruct((pack.row_shard, pack.feed_width), F32),
            jax.ShapeDtypeStruct((pack.row_shard, pack.model_width), F32),
        ],
        scratch_shapes=[pltpu.VMEM((CORES, pack.rows, pack.model_width), BF16)],
        name="unpack",
        compiler_params=pltpu.CompilerParams(vmem_limit_bytes=60 * MIB),
        cost_estimate=pl.CostEstimate(flops=0, bytes_accessed=10_000_000, transcendentals=0),
    )(meta, mine, other)


def unpack_qkv_kernel(meta, mine_ref, other_ref, grad_ref, bias_ref, small_ref):
    member = meta[3]
    row_shard, width = grad_ref.shape[0], grad_ref.shape[1] // 3
    part = mine_ref.shape[1] // 3
    for ref, at in ((mine_ref, member), (other_ref, 1 - member)):
        for kind in range(3):
            lane = pl.multiple_of(kind * width + at * part, CLUSTER_ROWS)
            from_lanes = slice(kind * part, (kind + 1) * part)
            grad_ref[:, pl.ds(lane, part)] = ref[:row_shard, from_lanes].astype(F32)
            lane = pl.multiple_of(at * part, CLUSTER_ROWS)
            bias_ref[kind : kind + 1, pl.ds(lane, part)] = ref[row_shard:, from_lanes].astype(F32)[
                BIAS_ROW : BIAS_ROW + 1
            ]
    small_ref[...] = (mine_ref[row_shard:, :].astype(F32) + other_ref[row_shard:, :].astype(F32))[
        :BIAS_ROW
    ]


def unpack_qkv(meta, mine, other, row_shard, needs=()):
    cols = mine.shape[1]
    vmem = pl.BlockSpec(memory_space=pltpu.VMEM)
    return pl.pallas_call(
        gated(unpack_qkv_kernel, 3, needs),
        in_specs=[IN_SMEM, vmem, vmem] + [ANYWHERE] * len(needs),
        out_specs=[vmem] * 3,
        out_shape=[
            jax.ShapeDtypeStruct((row_shard, CORES * cols), F32),
            jax.ShapeDtypeStruct((3, CORES * cols // 3), F32),
            jax.ShapeDtypeStruct((BIAS_ROW, cols), F32),
        ],
        name="unpack_qkv",
        compiler_params=pltpu.CompilerParams(vmem_limit_bytes=60 * MIB),
        cost_estimate=pl.CostEstimate(flops=0, bytes_accessed=200_000, transcendentals=0),
    )(meta, mine, other, *needs)


def tie(*values):
    return lax.optimization_barrier(values)


def body(
    tokens,
    cotangent,
    perms,
    unit_kind,
    w_qkv,
    bias_qv,
    w_out,
    bias_out,
    ln_gain,
    ln_bias,
    w_up,
    bias_up,
    w_down,
    bias_down,
):
    shards = lax.axis_size("fsdp")
    groups = lax.axis_size("dp")
    here = lax.axis_index("fsdp")
    dp_index = lax.axis_index("dp")
    core = dp_index % CORES
    level = dp_index // CORES
    depth = groups // CORES
    units, rounds, unit_len = perms.shape
    per_device = unit_len // shards
    model_width = tokens.shape[1]
    feed_width = w_up.shape[1]
    row_shard = model_width // shards
    members = shards // units
    member_rows = unit_len // members
    head_cols = model_width // members
    padded = -(-head_cols // CLUSTER_ROWS) * CLUSTER_ROWS
    spot = here * CORES + core
    home_core = spot // shards
    unit = (spot // members) % units
    member = spot % members
    pack = Pack(model_width, feed_width, shards, units, depth)
    bits = [1 << k for k in range(shards.bit_length() - 1)]
    bit_orders = (bits, bits[::-1])

    def plane_pairs(target):
        pairs = []
        for z in range(depth):
            for f_index in range(shards):
                for c_index in range(CORES):
                    f_new, c_new = target(f_index, c_index)
                    pairs.append(
                        (
                            (z * CORES + c_index) * shards + f_index,
                            (z * CORES + c_new) * shards + f_new,
                        )
                    )
        return pairs

    def send(value, pairs):
        return lax.ppermute(value, ("dp", "fsdp"), pairs)

    def cross(value, mask):
        return send(value, plane_pairs(lambda f, c: divmod((f * CORES + c) ^ mask, CORES)))

    def trade(value, stage):
        return send(value, plane_pairs(lambda f, c: (f ^ bit_orders[c][stage], c)))

    def trade_mask(index, which):
        mask = 0
        for stage in range(len(bits)):
            if index >> stage & 1:
                mask ^= bit_orders[which][stage]
        return mask

    def climb(value, mask):
        plane = CORES * shards
        pairs = []
        for z in range(depth):
            for rest in range(plane):
                pairs.append((z * plane + rest, (z ^ mask) * plane + rest))
        return send(value, pairs)

    def place_of(f, c, step):
        return (c * units + (f % units + step) % units) * members + f // units

    def outward(step):
        return plane_pairs(lambda f, c: divmod(place_of(f, c, step), CORES))

    def homeward(step):
        return [(b, a) for a, b in outward(step)]

    stays = place_of(here, core, 0) == spot

    def send_apart(value, pairs):
        return send(value, [(a, b) for a, b in pairs if a != b])

    def bring_start(value):
        blocks = value.reshape(units, per_device, model_width)
        return [
            lax.dynamic_index_in_dim(blocks, (here % units + step) % units, axis=0, keepdims=False)
            for step in range(units)
        ]

    def bring(chosen):
        return [
            (send_apart if step == 0 else send)(value, outward(step))
            for step, value in enumerate(chosen)
        ]

    def brought(chosen, landed):
        kept_one = jnp.where(stays, chosen[0], landed[0])
        return jnp.concatenate([kept_one] + list(landed[1:]), axis=0)

    def send_home(blocks):
        return [
            (send_apart if step == 0 else send)(blocks[step], homeward(step))
            for step in range(units)
        ]

    x_chosen = bring_start(tokens)
    x_own = brought(x_chosen, bring(x_chosen))
    small = jnp.concatenate(
        [
            bias_qv.reshape(-1),
            bias_out,
            ln_gain.reshape(-1),
            ln_bias.reshape(-1),
            bias_up,
            bias_down,
        ]
    )
    small_rows = -(-small.shape[0] // (3 * padded))
    small_block = jnp.pad(
        jnp.pad(small, (0, small_rows * 3 * padded - small.shape[0])).reshape(
            small_rows, 3 * padded
        ),
        ((0, 16 - small_rows), (0, 0)),
    )
    def columns_for(offset):
        start = lax.bitwise_xor(member, offset) * head_cols
        blocks = [
            jnp.pad(
                lax.dynamic_slice(
                    w_qkv, (0, kind * model_width + start), (row_shard, head_cols)
                ),
                ((0, 0), (0, padded - head_cols)),
            )
            for kind in range(3)
        ]
        return jnp.concatenate([jnp.concatenate(blocks, axis=1), small_block], axis=0)

    offsets = [(CORES * m) % members for m in range(shards)]
    kinds = sorted(set(offsets))
    order_pack = jnp.concatenate(
        [perms.reshape(-1), jnp.broadcast_to(unit_kind[:, None], (units, 128)).reshape(-1)]
    )
    order_other = cross(order_pack, 1)
    *tied, order_other = tie(*[columns_for(offset) for offset in kinds], order_other)
    piece_kinds = dict(zip(kinds, tied))
    x_pieces = [x_own] + [cross(x_own, mask) for mask in range(1, members)]
    if members == CORES:
        qkv_pieces = {0: piece_kinds[0]}
        for stage in range(len(bits)):
            qkv_pieces[1 << stage] = trade(piece_kinds[0], stage)
        for stage in range(1, len(bits)):
            for index in range(1, 1 << stage):
                qkv_pieces[index | 1 << stage] = trade(qkv_pieces[index], stage)
        qkv_pieces = [qkv_pieces[index] for index in range(shards)]
        qkv_masks = [[trade_mask(index, which) for index in range(shards)] for which in (0, 1)]
    else:
        qkv_pieces = [piece_kinds[0]] + [
            cross(piece_kinds[offsets[m]], CORES * m) for m in range(1, shards)
        ]
        qkv_masks = [list(range(shards))] * 2
    order_pack = jnp.where(home_core == core, order_pack, order_other)
    order_count = units * rounds * unit_len
    unit_perm = lax.dynamic_index_in_dim(
        order_pack[:order_count].reshape(units, rounds * unit_len), unit, 0, keepdims=False
    )
    kind_now = lax.dynamic_index_in_dim(
        order_pack[order_count:].reshape(units, 128), unit, 0, keepdims=False
    )[0]
    owner = unit_perm // per_device
    order = (
        lax.bitwise_xor(owner // units, member) * units + (unit - owner % units) % units
    ) * per_device + unit_perm % per_device
    order = order.reshape(rounds, unit_len)
    order = jnp.where(core == 0, order, order[::-1])
    order_row = order.reshape(1, rounds * unit_len)
    order = order.reshape(-1, CLUSTER_ROWS)
    x_here = arrange(order, x_pieces, unit_len, 0)
    x_now = [x_here, cross(x_here, 1)]
    own_masks = [
        jnp.where(core == 0, trade_mask(i, 0), trade_mask(i, 1)) for i in range(1, shards)
    ]
    other_masks = [
        jnp.where(core == 0, trade_mask(i, 1), trade_mask(i, 0)) for i in range(1, shards)
    ]
    zero = jnp.int32(0)
    meta = jnp.stack(
        [kind_now, here, core, member, level, here % units, stays, zero]
        + own_masks
        + other_masks
        + [jnp.where(core == 0, first, second) for first, second in zip(*qkv_masks)]
    ).astype(jnp.int32)

    def half_of(value, axis, length, at):
        return lax.dynamic_slice_in_dim(value, at * length, length, axis=axis)

    packed = jnp.concatenate(
        [half_of(w_down, 0, pack.down_rows, core)]
        + [
            half_of(w_up, 1, model_width, core * pack.blocks + block)
            for block in range(pack.blocks)
        ]
        + [half_of(w_out, 0, pack.out_rows, core)],
        axis=0,
    )
    order_rows = unit_len // CLUSTER_ROWS
    arranged, probs, mixtures, x_turned = [], [], [], []
    *tied, packed, x_now[0] = tie(*qkv_pieces[1:], packed, x_now[0])
    qkv_pieces = qkv_pieces[:1] + tied
    smalls = jnp.stack(
        [
            piece[row_shard : row_shard + small_rows].reshape(-1)[: small.shape[0]]
            for piece in qkv_pieces
        ]
    )
    spots_of = [[masks.index(mask) for mask in range(shards)] for masks in qkv_masks]
    spots_of = jnp.where(core == 0, jnp.array(spots_of[0]), jnp.array(spots_of[1]))
    spots_of = jnp.take(spots_of, lax.bitwise_xor(here, jnp.arange(shards)))
    smalls = jnp.take(smalls, spots_of, axis=0).astype(F32)

    def vectors_at(start, count, length):
        part = smalls[:, start * row_shard : start * row_shard + count * length]
        return (
            part.reshape(shards, count, length).transpose(1, 0, 2).reshape(count, shards * length)
        )

    my_bias = lax.dynamic_index_in_dim(
        vectors_at(0, 2, row_shard).reshape(2, members, head_cols), member, 1, keepdims=False
    )
    my_bias = jnp.pad(my_bias, ((0, 0), (0, padded - head_cols)))
    my_bias = jnp.stack([my_bias[0], jnp.zeros_like(my_bias[0]), my_bias[1]]).reshape(1, -1)
    up_bias = vectors_at(7, 1, feed_width // shards)
    down_bias = smalls[:, small.shape[0] - row_shard :].reshape(1, model_width)
    vectors = jnp.concatenate(
        [vectors_at(2, 5, row_shard), down_bias, jnp.zeros((2, model_width), F32)], axis=0
    )

    weight_pieces = {0: packed}
    for stage in range(len(bits)):
        weight_pieces[1 << stage] = trade(packed, stage)
    for index in range(rounds):
        results = attend(meta, x_now[index], my_bias, qkv_pieces, row_shard, mixtures[-1:])
        for kept, result in zip((arranged, probs, mixtures, x_turned), results):
            kept.append(result)
    cot_now, mixtures[0] = tie(cotangent, mixtures[0])
    cot_chosen = bring_start(cot_now)
    cot_landed = bring(cot_chosen)
    cot_own = brought(cot_chosen, cot_landed)
    for stage in range(1, len(bits)):
        for index in range(1, 1 << stage):
            weight_pieces[index | 1 << stage] = trade(weight_pieces[index], stage)
    att_there, att_sent = [], []
    for mask in range(1, members):
        there = place(
            order_row, mixtures, mask * member_rows, member_rows, 0.5, needs=cot_landed
        )
        att_sent.append(there)
        att_there.append(cross(there[:, :head_cols], mask))
    att_here = place(order_row, mixtures, 0, member_rows, 0.5, needs=att_sent)

    direct = [weight_pieces[index] for index in range(1, shards)]
    swapped = [cross(piece, 1) for piece in direct[:-1]]
    last_piece, att_here = tie(direct[-1], att_here)
    swapped.append(cross(last_piece, 1))
    att_raw = [att_here[:, :head_cols]] + att_there
    if head_cols % CLUSTER_ROWS:
        att_raw = [jnp.concatenate(att_raw, axis=1)]
    block_out, first_low, d_branch, d_ffn, hidden, d_pre, att_turned, *rest = feed(
        pack,
        meta,
        x_own,
        cot_own,
        vectors,
        up_bias,
        att_raw,
        [w_out, w_up, w_down],
        direct + swapped,
    )
    d_att, (row_sums, up_sums) = rest[: len(att_raw)], rest[len(att_raw) :]
    if head_cols % CLUSTER_ROWS:
        d_att = [d_att[0][:, mask * head_cols : (mask + 1) * head_cols] for mask in range(members)]
    d_att = [d_att[0]] + [cross(d_att[mask], mask) for mask in range(1, members)]
    d_att = [jnp.pad(piece, ((0, 0), (0, padded - head_cols))) for piece in d_att]

    table = jnp.stack([core, member]).astype(jnp.int32)
    sending = [index for index in range(shards) if index & 1]
    keeping = [index for index in range(shards) if not index & 1]
    slots = jnp.stack(
        [
            lax.bitwise_xor(here, jnp.where(core == 0, trade_mask(i, 0), trade_mask(i, 1)))
            for i in sending + keeping
        ]
    )
    slots = jnp.concatenate([slots, slots]).astype(jnp.int32)

    def pair_sum(mine, theirs, needs):
        return add_picked(
            slots, [mine, cross(theirs, 1)], shards, len(sending), needs, 20_000_000_000
        )

    theirs_down, mine_down = down_grads(pack, table, d_ffn, hidden)
    theirs_rest, mine_rest = rest_grads(
        pack, table, first_low, d_pre, att_turned, d_branch, [theirs_down]
    )
    down_going, down_kept = pair_sum(mine_down, theirs_down, [theirs_rest])
    rest_going, rest_kept = pair_sum(mine_rest, theirs_rest, [down_going] + d_att[1:])

    def merge(kept, landed, *needs):
        count = kept.shape[0]
        if count == 1:
            table = jnp.zeros((2,), jnp.int32)
            return None, add_picked(table, [kept, landed], 1, None, needs)[0]
        order_now = [i for i in range(count) if i & 1] + [i for i in range(count) if not i & 1]
        table = jnp.array(order_now * 2, jnp.int32)
        return add_picked(table, [kept, landed], count, count // 2, needs)

    grads, d_x = [None] * rounds, [None] * rounds
    needs = [rest_going]
    blocks = unit_len // POS_BLOCK
    spans = [(index, (0, blocks)) for index in reversed(range(rounds))]
    for turn, (index, span) in enumerate(spans):
        grads[index], d_x[index], token = attend_back(
            meta,
            order,
            arranged[index],
            probs[index],
            d_att,
            qkv_pieces,
            row_shard,
            index * order_rows,
            needs,
            span,
            [],
        )
        if turn == 0:
            d_x_there = cross(d_x[index], 1)
            going, kept = join(
                [down_kept, rest_kept], [trade(down_going, 0), trade(rest_going, 0)], [token]
            )
            output_blocks = split_rows(block_out, units, [token])
            output_landed = send_home(output_blocks)
            needs = [kept]
    for stage in range(1, len(bits)):
        going, kept = merge(kept, trade(going, stage), token)

    def level_pieces(block):
        return block.reshape((depth, block.shape[0] // depth) + block.shape[1:])

    def level_scatter(cut):
        return [
            climb(
                lax.dynamic_index_in_dim(cut, lax.bitwise_xor(level, mask), 0, keepdims=False), mask
            )
            for mask in range(1, depth)
        ]

    def level_gather(piece):
        pieces = {0: piece}
        mask = depth // 2
        while mask:
            pieces[mask] = climb(piece, mask)
            mask //= 2
        return pieces

    def level_forward(pieces):
        for index in sorted(range(depth), key=lambda value: value.bit_count()):
            if index not in pieces:
                low = index & -index
                pieces[index] = climb(pieces[index ^ low], low)
        return [pieces[index] for index in range(depth)]

    def by_shard(value):
        count, length = value.shape
        return (
            value.reshape(count, shards, length // shards)
            .transpose(1, 0, 2)
            .reshape(shards, count * length // shards)
        )

    small_grad = jnp.concatenate(
        [by_shard(row_sums[:5]), by_shard(up_sums), by_shard(row_sums[5:6])], axis=1
    )
    small_length = small_grad.shape[1]
    small_lanes = 3 * head_cols
    small_grad = jnp.pad(small_grad, ((0, 0), (0, BIAS_ROW * small_lanes - small_length)))
    small_grad = jnp.pad(
        small_grad.reshape(shards, BIAS_ROW, small_lanes), ((0, 0), (0, 16 - BIAS_ROW), (0, 0))
    )
    extra_rows = 16
    if padded == head_cols:
        joined = qkv_grads(
            x_turned, grads, small_grad, row_shard, output_landed + [kept]
        )
    else:
        qkv_grad = dot(x_turned[0], grads[0]) + dot(x_turned[1], grads[1])
        qkv_grad = qkv_grad.reshape(shards, row_shard, 3, padded)[..., :head_cols]
        bias_sum = sum(jnp.sum(value.astype(F32), axis=0) for value in grads)
        bias_sum = bias_sum.reshape(3, padded)[:, :head_cols].reshape(small_lanes)
        small_grad = small_grad.at[:, BIAS_ROW].set(bias_sum[None])
        joined = jnp.concatenate(
            [qkv_grad.reshape(shards, row_shard, small_lanes), small_grad], axis=1
        ).astype(BF16)
    cut = level_pieces(kept[0])
    landed = level_scatter(cut)
    classes = max(1, members // CORES)
    d_x_parts = [d_x[0], d_x_there]
    order_mine = order_row[:, :unit_len]
    if classes == 1:
        slots_held = jnp.stack(
            [
                lax.bitwise_xor(here, jnp.where(core == 0, trade_mask(i, 0), trade_mask(i, 1)))
                for i in range(shards)
            ]
        )
        held = jnp.stack(
            [
                lax.dynamic_index_in_dim(joined, slots_held[i], 0, keepdims=False)
                for i in range(0, shards, 2)
            ]
        )
        leaving = jnp.stack(
            [
                lax.dynamic_index_in_dim(joined, slots_held[i], 0, keepdims=False)
                for i in range(1, shards, 2)
            ]
        )
        totals = None
    else:
        totals = [None] * classes
        for m in range(shards):
            offset = offsets[m] // CORES
            piece = lax.dynamic_index_in_dim(joined, lax.bitwise_xor(here, m), 0, keepdims=False)
            piece = (piece if m == 0 else cross(piece, CORES * m)).astype(F32)
            totals[offset] = piece if totals[offset] is None else totals[offset] + piece

    d_there = [
        place(
            order_mine,
            d_x_parts,
            mask * member_rows,
            member_rows,
            added=True,
            needs=[joined],
        )
        for mask in range(1, members)
    ]
    if depth > 1:
        picks = jnp.concatenate([level[None], jnp.zeros((depth - 1,), level.dtype)])
        (kept,) = add_picked(
            picks.astype(jnp.int32),
            [cut] + [piece[None] for piece in landed],
            1,
            None,
            d_there,
        )
    gathered = level_gather(kept[0]) if depth > 1 else {0: cut[0]}
    early = [kept] + d_there
    if totals is None:
        held = held + trade(leaving, 0)
        early.append(held)
    d_here = place(
        order_mine,
        d_x_parts,
        0,
        member_rows,
        1.0,
        F32,
        d_branch,
        added=True,
        needs=early,
    )
    d_inputs = d_here
    for mask, there in enumerate(d_there, 1):
        d_inputs = d_inputs + cross(there, mask).astype(F32)
    d_inputs = d_inputs.astype(BF16)
    home_blocks = d_inputs.reshape(units, per_device, model_width)
    home = send_home(home_blocks)
    last = d_inputs
    if totals is None:
        for stage in range(1, len(bits)):
            held = held[::2] + trade(held[1::2], stage)
        last = held
        totals = [held[0]]
    output = home_rows(meta, output_blocks[0], output_landed, BF16, [last])
    totals = jnp.concatenate(totals, axis=0).astype(BF16)
    rows_each = row_shard + extra_rows
    if depth > 1:
        halves = totals.reshape((2, totals.shape[0] // 2) + totals.shape[1:])
        side = level % 2
        mine = lax.dynamic_index_in_dim(halves, side, 0, keepdims=False)
        theirs = lax.dynamic_index_in_dim(halves, 1 - side, 0, keepdims=False)
        half = (mine.astype(F32) + climb(theirs, 1).astype(F32)).astype(BF16)
        masks = [mask for mask in gathered if mask]
        *tied, half = tie(*[gathered[mask] for mask in masks], half)
        gathered.update(zip(masks, tied))
        mask = 2
        while mask < depth:
            half = (half.astype(F32) + climb(half, mask).astype(F32)).astype(BF16)
            mask *= 2
        *home, output, half = tie(*home, output, half)
        other_half = climb(half, 1)
        d_inputs = home_rows(meta, home_blocks[0], home, F32)
        d_inputs, other_half = tie(d_inputs, other_half)
        totals = jnp.concatenate(
            [
                jnp.where(side == 0, half, other_half),
                jnp.where(side == 0, other_half, half),
            ],
            axis=0,
        )
    else:
        d_inputs = home_rows(meta, home_blocks[0], home, F32)
    stacked = stack_up(level_forward(gathered))
    grad_down, grad_up, grad_out = unpack(pack, depth, meta, stacked, cross(stacked, 1))
    if padded == head_cols and members == CORES:
        grad_qkv, bias_out_row, smalls_out = unpack_qkv(
            meta, totals, cross(totals, 1), row_shard, [grad_down]
        )
        smalls_out = smalls_out.reshape(-1)[:small_length]
        bias_out_row = lax.dynamic_slice(bias_out_row, (0, here * row_shard), (3, row_shard))
    else:
        landed = jnp.stack([totals, cross(totals, 1)], axis=0).reshape(
            CORES, classes, rows_each, 3 * head_cols
        )
        smalls_out = jnp.sum(
            landed[:, :, row_shard : row_shard + BIAS_ROW].astype(F32), axis=(0, 1)
        ).reshape(-1)[:small_length]
        landed = (
            landed.transpose(1, 0, 2, 3)
            .reshape(members, rows_each, 3, head_cols)[:, : row_shard + BIAS_ROW + 1]
        )
        if members == 2:
            swap = member == 1
            landed = jnp.stack(
                [
                    jnp.where(swap, landed[1], landed[0]),
                    jnp.where(swap, landed[0], landed[1]),
                ]
            )
        else:
            landed = jnp.take(landed, lax.bitwise_xor(member, jnp.arange(members)), axis=0)
        grad_qkv = landed[:, :row_shard].transpose(1, 2, 0, 3)
        grad_qkv = grad_qkv.reshape(row_shard, 3 * model_width).astype(F32)
        bias_out_row = landed[:, row_shard + BIAS_ROW].astype(F32).transpose(1, 0, 2)
        bias_out_row = lax.dynamic_slice(
            bias_out_row.reshape(3, model_width), (0, here * row_shard), (3, row_shard)
        )

    feed_shard = feed_width // shards
    spots = [0, row_shard, 3 * row_shard, 5 * row_shard]
    return (
        output,
        d_inputs,
        grad_qkv,
        bias_out_row[::2],
        grad_out,
        smalls_out[spots[0] : spots[1]],
        smalls_out[spots[1] : spots[2]].reshape(2, row_shard),
        smalls_out[spots[2] : spots[3]].reshape(2, row_shard),
        grad_up,
        smalls_out[spots[3] : spots[3] + feed_shard],
        grad_down,
        smalls_out[spots[3] + feed_shard :],
    )


def solution(mesh):
    placed = (
        P(("dp", "fsdp"), None),
        P(("dp", "fsdp"), None),
        P("dp", None, None),
        P("dp"),
        P("fsdp", None),
        P(None, "fsdp"),
        P("fsdp", None),
        P("fsdp"),
        P(None, "fsdp"),
        P(None, "fsdp"),
        P("fsdp", None),
        P("fsdp"),
        P("fsdp", None),
        P("fsdp"),
    )
    return jax.shard_map(
        body,
        mesh=mesh,
        in_specs=placed,
        out_specs=(
            P(("dp", "fsdp"), None),
            P(("dp", "fsdp"), None),
            P("fsdp", None),
            P(None, "fsdp"),
            P("fsdp", None),
            P("fsdp"),
            P(None, "fsdp"),
            P(None, "fsdp"),
            P("fsdp", None),
            P("fsdp"),
            P("fsdp", None),
            P("fsdp"),
        ),
        check_vma=False,
    )
```

```python
from functools import partial

import jax
import jax.numpy as jnp
from jax import lax
from jax.experimental import pallas as pl
from jax.experimental.pallas import tpu as pltpu
from jax.sharding import PartitionSpec as P

HEAD_DIM = 64
CORES = 2
NEG_FILL = -1000000000.0
EPSILON = 1e-05
SCALE = HEAD_DIM ** (-0.5)
BIAS_ROW = 2
GRAD_LANES = 384
CLUSTER_ROWS = 128
HALF_ROWS = 64
POS_BLOCK = 512
TOKEN_BLOCK = 512
ROW_BLOCK = 256
FF_BLOCK = 512
MIB = 1024 * 1024
NT = (((1,), (1,)), ((), ()))
TN = (((0,), (0,)), ((), ()))
F32 = jnp.float32
BF16 = jnp.bfloat16
ANYWHERE = pl.BlockSpec(memory_space=pl.ANY)
IN_SMEM = pl.BlockSpec(memory_space=pltpu.SMEM)


def whole(shape):
    return pl.BlockSpec(shape, lambda i: (0,) * len(shape))


def rows_of(shape):
    return pl.BlockSpec(shape, lambda i: (i,) + (0,) * (len(shape) - 1))


def dot(a, b, dims=(((1,), (0,)), ((), ()))):
    return lax.dot_general(a, b, dims, preferred_element_type=F32)


def params(mib, flops=0, moved=0, share=16):
    return dict(
        compiler_params=pltpu.CompilerParams(
            dimension_semantics=("arbitrary",),
            vmem_limit_bytes=mib * MIB,
        ),
        cost_estimate=pl.CostEstimate(
            flops=flops // share, bytes_accessed=moved // share, transcendentals=0
        ),
    )


def gated(kernel, used, needs):
    if not needs:
        return kernel

    def run(*refs):
        return kernel(*refs[:used], *refs[used + len(needs) :])

    return run


def lane_masks():
    lane = lax.broadcasted_iota(jnp.int32, (CLUSTER_ROWS, CLUSTER_ROWS), 1)
    low = (lane < HEAD_DIM).astype(F32)
    return low.astype(BF16), (1.0 - low).astype(BF16), lane < HEAD_DIM


def corners(first, second):
    blank = jnp.zeros_like(first)
    return jnp.concatenate(
        [
            jnp.concatenate([first, blank], axis=1),
            jnp.concatenate([blank, second], axis=1),
        ],
        axis=0,
    )


def both_heads(rows_now, low, high):
    return jnp.concatenate([rows_now * low, rows_now * high], axis=0)


def equal_ones(left, right):
    return jnp.where(left == right, jnp.ones((), BF16), jnp.zeros((), BF16))


def pick_rows(order_ref, first_row, unit_len):
    parts = []
    lane = lax.broadcasted_iota(jnp.int16, (CLUSTER_ROWS, CLUSTER_ROWS), 1)
    for part in range(POS_BLOCK // CLUSTER_ROWS):
        row = order_ref[pl.ds(first_row + part, 1), :]
        column = jnp.transpose(jnp.broadcast_to(row, (CLUSTER_ROWS, CLUSTER_ROWS)))
        column = column.astype(jnp.int16)
        pieces = [
            equal_ones(column, lane + jnp.int16(base)) for base in range(0, unit_len, CLUSTER_ROWS)
        ]
        parts.append(jnp.concatenate(pieces, axis=1))
    return jnp.concatenate(parts, axis=0)


def load_pieces(meta, x_refs, w_refs, x_all, w_all, sems, row_shard):
    member_rows = x_all.shape[0] // max(1, len(x_refs))
    copies = []
    for index, ref in enumerate(x_refs):
        copies.append(
            pltpu.make_async_copy(
                ref, x_all.at[pl.ds(index * member_rows, member_rows), :], sems.at[index]
            )
        )
    for index, ref in enumerate(w_refs):
        mask = meta[meta.shape[0] - len(w_refs) + index]
        start = pl.multiple_of(lax.bitwise_xor(meta[1], mask) * row_shard, 16)
        copies.append(
            pltpu.make_async_copy(
                ref.at[pl.ds(0, row_shard), :],
                w_all.at[pl.ds(start, row_shard), :],
                sems.at[len(x_refs) + index],
            )
        )
    for copy in copies:
        copy.start()
    for copy in copies:
        copy.wait()


def arrange_kernel(unit_len, first_row, order_ref, *refs):
    x_refs, out_ref = refs[:-1], refs[-1]
    step = pl.program_id(0)
    picks = pick_rows(order_ref, first_row + step * (POS_BLOCK // CLUSTER_ROWS), unit_len)
    rows = x_refs[0].shape[0]
    total = None
    for index, ref in enumerate(x_refs):
        term = dot(picks[:, index * rows : (index + 1) * rows], ref[...])
        total = term if total is None else total + term
    out_ref[...] = total.astype(BF16)


def arrange(order, x_pieces, position_count, first_row):
    member_rows, width = x_pieces[0].shape
    unit_len = member_rows * len(x_pieces)
    return pl.pallas_call(
        partial(arrange_kernel, unit_len, first_row),
        grid=(position_count // POS_BLOCK,),
        in_specs=[whole(order.shape)] + [whole(piece.shape) for piece in x_pieces],
        out_specs=rows_of((POS_BLOCK, width)),
        out_shape=jax.ShapeDtypeStruct((position_count, width), BF16),
        name="arrange",
        **params(20, 2 * position_count * unit_len * width, 6_000_000),
    )(order, *x_pieces)


def attend_kernel(sizes, meta, x_now_ref, bias_ref, *refs):
    shards, row_shard = sizes
    w_refs, refs = refs[:shards], refs[shards:]
    arranged_ref, probs_ref, mixture_ref, turned_ref, w_all, sems = refs
    width = w_all.shape[1] // 3
    step = pl.program_id(0)

    @pl.when(step == 0)
    def _():
        load_pieces(meta, [], w_refs, w_all, w_all, sems, row_shard)

    x_now = x_now_ref[...]
    turned_ref[...] = jnp.transpose(x_now)
    arranged = (dot(x_now, w_all[...]) + bias_ref[...]).astype(BF16)
    arranged_ref[...] = arranged
    low, high, lane_low = lane_masks()
    position = lax.broadcasted_iota(jnp.int32, (CLUSTER_ROWS, CLUSTER_ROWS), 0)
    other = lax.broadcasted_iota(jnp.int32, (CLUSTER_ROWS, CLUSTER_ROWS), 1)
    same_half = (position < HALF_ROWS) == (other < HALF_ROWS)
    allowed = jnp.logical_or(same_half, meta[0] == 1)
    pairs = width // CLUSTER_ROWS
    units = [(part, pair) for part in range(POS_BLOCK // CLUSTER_ROWS) for pair in range(pairs)]
    for index in range(0, len(units), 2):
        queries, keys, values = [], [], []
        for part, pair in units[index : index + 2]:
            rows_now = slice(part * CLUSTER_ROWS, (part + 1) * CLUSTER_ROWS)
            base = pair * CLUSTER_ROWS
            queries.append(arranged[rows_now, base : base + CLUSTER_ROWS] * SCALE)
            one_key = arranged[rows_now, width + base : width + base + CLUSTER_ROWS]
            keys.append(both_heads(one_key, low, high))
            one_value = arranged[rows_now, 2 * width + base : 2 * width + base + CLUSTER_ROWS]
            values.append(both_heads(one_value, low, high))
        both_scores = dot(jnp.concatenate(keys, axis=1), corners(*queries), NT)
        for which, (part, pair) in enumerate(units[index : index + 2]):
            halves = []
            for head in range(2):
                one = both_scores[
                    head * CLUSTER_ROWS : (head + 1) * CLUSTER_ROWS,
                    which * CLUSTER_ROWS : (which + 1) * CLUSTER_ROWS,
                ]
                one = jnp.where(allowed, one, NEG_FILL)
                grown = jnp.exp(one - jnp.max(one, axis=0, keepdims=True))
                halves.append(grown * (1.0 / jnp.sum(grown, axis=0, keepdims=True)))
            probs = jnp.concatenate(halves, axis=0).astype(BF16)
            at = (part * pairs + pair) * 2 * CLUSTER_ROWS
            probs_ref[at : at + 2 * CLUSTER_ROWS, :] = probs
            mixture_ref[
                part * CLUSTER_ROWS : (part + 1) * CLUSTER_ROWS,
                pair * CLUSTER_ROWS : (pair + 1) * CLUSTER_ROWS,
            ] = dot(probs, values[which], TN).astype(BF16)


def attend(meta, x_now, bias, w_pieces, row_shard, needs=()):
    shards = len(w_pieces)
    position_count, model_width = x_now.shape
    cols = w_pieces[0].shape[1]
    width = cols // 3
    pair_rows = 2 * width
    return pl.pallas_call(
        gated(partial(attend_kernel, (shards, row_shard)), 3 + shards, needs),
        grid=(position_count // POS_BLOCK,),
        in_specs=[IN_SMEM, rows_of((POS_BLOCK, model_width)), whole(bias.shape)]
        + [ANYWHERE] * (shards + len(needs)),
        out_specs=[
            rows_of((POS_BLOCK, cols)),
            rows_of((POS_BLOCK // CLUSTER_ROWS * pair_rows, CLUSTER_ROWS)),
            rows_of((POS_BLOCK, width)),
            pl.BlockSpec((model_width, POS_BLOCK), lambda i: (0, i)),
        ],
        out_shape=[
            jax.ShapeDtypeStruct((position_count, cols), BF16),
            jax.ShapeDtypeStruct((position_count // CLUSTER_ROWS * pair_rows, CLUSTER_ROWS), BF16),
            jax.ShapeDtypeStruct((position_count, width), BF16),
            jax.ShapeDtypeStruct((model_width, position_count), BF16),
        ],
        scratch_shapes=[
            pltpu.VMEM((model_width, cols), BF16),
            pltpu.SemaphoreType.DMA((shards,)),
        ],
        name="attend",
        **params(
            60, 8 * position_count * (model_width * cols + 4 * CLUSTER_ROWS * width), 18_000_000, 1
        ),
    )(meta, x_now, bias, *w_pieces, *needs)


def place_kernel(sizes, scale, has_base, order_row_ref, *refs):
    unit_len, first_token, added = sizes
    base_ref = refs[0] if has_base else None
    refs = refs[1 if has_base else 0 :]
    if added:
        first_ref, second_ref, out_ref, held = refs

        @pl.when(pl.program_id(0) == 0)
        def _():
            held[...] = (first_ref[...].astype(F32) + second_ref[...].astype(F32)).astype(BF16)

        source_refs = [held]
    else:
        source_refs, out_ref = refs[:-1], refs[-1]
    block_rows = out_ref.shape[0]
    first = jnp.full((1, 1), first_token + pl.program_id(0) * block_rows, jnp.int32)
    token = lax.broadcasted_iota(jnp.int16, (block_rows, unit_len), 0)
    total = None
    for index, ref in enumerate(source_refs):
        row = order_row_ref[:, index * unit_len : (index + 1) * unit_len] - first
        row = jnp.broadcast_to(row, (16, unit_len)).astype(jnp.int16)
        row = jnp.concatenate([row] * (block_rows // 16), axis=0)
        term = dot(equal_ones(row, token), ref[...])
        total = term if total is None else total + term
    if scale != 1.0:
        total = total * scale
    if has_base:
        total = total + base_ref[...].astype(F32)
    out_ref[...] = total.astype(out_ref.dtype)


def place(
    order_row,
    sources,
    first_token,
    row_count,
    scale=1.0,
    dtype=BF16,
    base=None,
    added=False,
    needs=(),
):
    unit_len, width = sources[0].shape
    block_rows = min(TOKEN_BLOCK, row_count)
    extra = [] if base is None else [base]
    return pl.pallas_call(
        gated(
            partial(place_kernel, (unit_len, first_token, added), scale, base is not None),
            1 + len(extra) + len(sources),
            needs,
        ),
        grid=(row_count // block_rows,),
        in_specs=[whole(order_row.shape)]
        + [rows_of((block_rows, width))] * len(extra)
        + [whole(source.shape) for source in sources]
        + [ANYWHERE] * len(needs),
        out_specs=rows_of((block_rows, width)),
        out_shape=jax.ShapeDtypeStruct((row_count, width), dtype),
        scratch_shapes=[pltpu.VMEM((unit_len, width), BF16)] if added else [],
        name="place",
        **params(
            32 if added else 20,
            16 * row_count * unit_len * width,
            10_000_000,
            1,
        ),
    )(order_row, *extra, *sources, *needs)


def attend_back_kernel(sizes, meta, order_ref, arranged_ref, probs_ref, *refs):
    members, shards, unit_len, row_shard, first_row, start = sizes
    g_refs, refs = refs[:members], refs[members:]
    w_refs, refs = refs[:shards], refs[shards:]
    grads_ref, d_x_ref, token_ref, g_all, w_all, sems = refs
    width = w_all.shape[1] // 3
    step = pl.program_id(0)

    @pl.when(step == 0)
    def _():
        load_pieces(meta, g_refs, w_refs, g_all, w_all, sems, row_shard)
        token_ref[...] = jnp.zeros_like(token_ref)

    at_row = first_row + (start + step) * (POS_BLOCK // CLUSTER_ROWS)
    picks = pick_rows(order_ref, at_row, unit_len)
    d_mixture = dot(picks, g_all[...]).astype(BF16)
    low, high, lane_low = lane_masks()
    pairs = width // CLUSTER_ROWS
    units = [(part, pair) for part in range(POS_BLOCK // CLUSTER_ROWS) for pair in range(pairs)]
    for index in range(0, len(units), 2):
        values, d_rows = [], []
        for part, pair in units[index : index + 2]:
            rows_now = slice(part * CLUSTER_ROWS, (part + 1) * CLUSTER_ROWS)
            base = pair * CLUSTER_ROWS
            one_value = arranged_ref[rows_now, 2 * width + base : 2 * width + base + CLUSTER_ROWS]
            values.append(both_heads(one_value, low, high))
            d_rows.append(d_mixture[rows_now, base : base + CLUSTER_ROWS])
        both_probs = dot(jnp.concatenate(values, axis=1), corners(*d_rows), NT)
        for which, (part, pair) in enumerate(units[index : index + 2]):
            rows_now = slice(part * CLUSTER_ROWS, (part + 1) * CLUSTER_ROWS)
            base = pair * CLUSTER_ROWS
            q_lanes = slice(base, base + CLUSTER_ROWS)
            k_lanes = slice(width + base, width + base + CLUSTER_ROWS)
            v_lanes = slice(2 * width + base, 2 * width + base + CLUSTER_ROWS)
            queries = arranged_ref[rows_now, q_lanes] * SCALE
            keys = arranged_ref[rows_now, k_lanes] * SCALE
            at = (part * pairs + pair) * 2 * CLUSTER_ROWS
            probs = probs_ref[at : at + 2 * CLUSTER_ROWS, :]
            d_probs = both_probs[:, which * CLUSTER_ROWS : (which + 1) * CLUSTER_ROWS]
            pieces = []
            for head in range(2):
                rows = slice(head * CLUSTER_ROWS, (head + 1) * CLUSTER_ROWS)
                weight = probs[rows].astype(F32)
                d_one = d_probs[rows]
                inner = jnp.sum(weight * d_one, axis=0, keepdims=True)
                pieces.append(weight * (d_one - inner))
            d_scores = jnp.concatenate(pieces, axis=0).astype(BF16)
            d_query = dot(d_scores, both_heads(keys, low, high), TN)
            d_pair = dot(
                jnp.concatenate([probs, d_scores], axis=1), corners(d_rows[which], queries)
            )
            d_values, d_keys = d_pair[:, :CLUSTER_ROWS], d_pair[:, CLUSTER_ROWS:]
            grads_ref[rows_now, q_lanes] = d_query.astype(BF16)
            grads_ref[rows_now, k_lanes] = jnp.where(
                lane_low, d_keys[:CLUSTER_ROWS], d_keys[CLUSTER_ROWS:]
            ).astype(BF16)
            grads_ref[rows_now, v_lanes] = jnp.where(
                lane_low, d_values[:CLUSTER_ROWS], d_values[CLUSTER_ROWS:]
            ).astype(BF16)
    grads = grads_ref[...]
    d_x_ref[...] = dot(grads, w_all[...], NT).astype(BF16)


def attend_back(
    meta, order, arranged, probs, g_pieces, w_pieces, row_shard, first_row, needs, span, into
):
    members, shards = len(g_pieces), len(w_pieces)
    member_rows, width = g_pieces[0].shape
    unit_len = members * member_rows
    position_count, cols = arranged.shape
    model_width = row_shard * shards
    start, stop = span
    pair_rows = POS_BLOCK // CLUSTER_ROWS * 2 * width
    used = 4 + members + shards

    def block(shape):
        return pl.BlockSpec(shape, lambda i: (start + i, 0))

    return pl.pallas_call(
        gated(
            partial(attend_back_kernel, (members, shards, unit_len, row_shard, first_row, start)),
            used,
            list(into) + list(needs),
        ),
        grid=(stop - start,),
        in_specs=[
            IN_SMEM,
            whole(order.shape),
            block((POS_BLOCK, cols)),
            block((pair_rows, CLUSTER_ROWS)),
        ]
        + [ANYWHERE] * (members + shards + len(into) + len(needs)),
        out_specs=[block((POS_BLOCK, cols)), block((POS_BLOCK, model_width)), whole((8, 128))],
        out_shape=[
            jax.ShapeDtypeStruct((position_count, cols), BF16),
            jax.ShapeDtypeStruct((position_count, model_width), BF16),
            jax.ShapeDtypeStruct((8, 128), F32),
        ],
        input_output_aliases={used + index: index for index in range(len(into))},
        scratch_shapes=[
            pltpu.VMEM((unit_len, width), BF16),
            pltpu.VMEM((model_width, cols), BF16),
            pltpu.SemaphoreType.DMA((members + shards,)),
        ],
        name="attend_back",
        **params(
            60,
            12 * (stop - start) * POS_BLOCK * (unit_len * width + model_width * cols),
            20_000_000,
            1,
        ),
    )(meta, order, arranged, probs, *g_pieces, *w_pieces, *into, *needs)


def normalise(summed):
    average = jnp.mean(summed, axis=-1, keepdims=True)
    centred = summed - average
    spread = jnp.mean(centred * centred, axis=-1, keepdims=True)
    scale_inv = lax.rsqrt(spread + EPSILON)
    return centred * scale_inv, scale_inv


def normalise_back(grad_out, normed, scale_inv, gain_row):
    scaled = grad_out * gain_row
    return scale_inv * (
        scaled
        - jnp.mean(scaled, axis=-1, keepdims=True)
        - normed * jnp.mean(scaled * normed, axis=-1, keepdims=True)
    )


def column_sum(rows_now):
    return jnp.sum(rows_now, axis=0, keepdims=True)


def gelu_parts(value):
    below = 0.5 + 0.5 * lax.erf(value * 0.7071067811865476)
    bell = jnp.exp(value * value * -0.5) * 0.3989422804014327
    return value * below, below + value * bell


class Pack:
    def __init__(self, model_width, feed_width, shards, units, depth):
        self.model_width, self.feed_width, self.shards = model_width, feed_width, shards
        self.row_shard = model_width // shards
        self.feed_shard = feed_width // shards
        self.down_rows = self.feed_shard // CORES
        self.blocks = feed_width // CORES // model_width
        self.up_at = self.down_rows
        self.out_at = self.up_at + self.blocks * self.row_shard
        self.out_rows = self.row_shard // CORES
        self.used = self.out_at + self.out_rows
        unit = 16 * depth
        self.rows = -(-self.used // unit) * unit
        self.rest_rows = self.rows - self.down_rows
        self.units = units
        self.group = units * self.row_shard

    def out_start(self, shard, member):
        return (
            lax.bitwise_xor(jnp.int32(shard) // self.units, member) * self.group
            + (shard % self.units) * self.row_shard
        )


def feed_kernel(pack, att_count, meta, x_ref, cot_ref, vec_ref, up_bias_ref, *refs):
    shards = pack.shards
    att_refs, refs = refs[:att_count], refs[att_count:]
    own_out, own_up, own_down = refs[:3]
    refs = refs[3:]
    pieces, refs = refs[: 2 * (shards - 1)], refs[2 * (shards - 1) :]
    out_ref, first_turned_ref, d_branch_ref, d_ffn_turned_ref, hidden_ref, d_pre_ref = refs[:6]
    att_turned_ref = refs[6]
    refs = refs[7:]
    d_att_refs, refs = refs[:att_count], refs[att_count:]
    sums_ref, up_sums_ref, w_out, w_up, w_down, slope, sems = refs
    step = pl.program_id(0)
    here, core, member = meta[1], meta[2], meta[3]
    feed_width = pack.feed_width

    def loads(kind):
        copies = []

        def add(source, target):
            copies.append(pltpu.make_async_copy(source, target, sems.at[kind, len(copies)]))

        if kind == 0:
            start = pl.multiple_of(pack.out_start(here, member), 16)
            add(own_out, w_out.at[pl.ds(start, pack.row_shard), :])
        elif kind == 1:
            start = pl.multiple_of(here * pack.row_shard, 16)
            add(own_up, w_up.at[pl.ds(start, pack.row_shard), :])
        else:
            start = pl.multiple_of(here * pack.feed_shard, 16)
            add(own_down, w_down.at[pl.ds(start, pack.feed_shard), :])
        for index, ref in enumerate(pieces):
            peer = lax.bitwise_xor(here, meta[8 + index])
            half = core if index < shards - 1 else 1 - core
            if kind == 0:
                start = pack.out_start(peer, member) + half * pack.out_rows
                start = pl.multiple_of(start, 16)
                add(
                    ref.at[pl.ds(pack.out_at, pack.out_rows), :],
                    w_out.at[pl.ds(start, pack.out_rows), :],
                )
            elif kind == 1:
                start = pl.multiple_of(peer * pack.row_shard, 16)
                for block in range(pack.blocks):
                    lane = pl.multiple_of(
                        (half * pack.blocks + block) * pack.model_width, CLUSTER_ROWS
                    )
                    add(
                        ref.at[pl.ds(pack.up_at + block * pack.row_shard, pack.row_shard), :],
                        w_up.at[pl.ds(start, pack.row_shard), pl.ds(lane, pack.model_width)],
                    )
            else:
                start = pl.multiple_of(peer * pack.feed_shard + half * pack.down_rows, 16)
                add(
                    ref.at[pl.ds(0, pack.down_rows), :],
                    w_down.at[pl.ds(start, pack.down_rows), :],
                )
        return copies

    @pl.when(step == 0)
    def _():
        for kind in range(3):
            for copy in loads(kind):
                copy.start()
        sums_ref[...] = jnp.zeros_like(sums_ref)
        up_sums_ref[...] = jnp.zeros_like(up_sums_ref)
        for copy in loads(0):
            copy.wait()

    bias_out, gain_one, gain_two = vec_ref[0:1, :], vec_ref[1:2, :], vec_ref[2:3, :]
    shift_one, shift_two, bias_down = vec_ref[3:4, :], vec_ref[4:5, :], vec_ref[5:6, :]
    att_width = att_refs[0].shape[1]
    summed = x_ref[...].astype(F32) + bias_out
    for index, ref in enumerate(att_refs):
        summed += dot(ref[...], w_out[index * att_width : (index + 1) * att_width, :])
    normed_one, inv_one = normalise(summed)
    first = normed_one * gain_one + shift_one
    first_low = first.astype(BF16)
    first_turned_ref[...] = jnp.transpose(first_low)
    for index, ref in enumerate(att_refs):
        att_turned_ref[index * att_width : (index + 1) * att_width, :] = jnp.transpose(ref[...])

    @pl.when(step == 0)
    def _():
        for kind in (1, 2):
            for copy in loads(kind):
                copy.wait()

    second = first + bias_down
    starts = list(range(0, feed_width, FF_BLOCK))

    def raised(base):
        lanes = slice(base, base + FF_BLOCK)
        return dot(first_low, w_up[:, lanes]) + up_bias_ref[:, lanes]

    pre = raised(starts[0])
    for index, base in enumerate(starts):
        lanes = slice(base, base + FF_BLOCK)
        pre_next = raised(starts[index + 1]) if index + 1 < len(starts) else None
        hidden, slope_now = gelu_parts(pre)
        hidden = hidden.astype(BF16)
        hidden_ref[:, lanes] = hidden
        slope[:, lanes] = slope_now
        second += dot(hidden, w_down[lanes, :])
        pre = pre_next
    normed_two, inv_two = normalise(second)
    out_ref[...] = (normed_two * gain_two + shift_two).astype(BF16)
    top = cot_ref[...].astype(F32)
    d_second = normalise_back(top, normed_two, inv_two, gain_two)
    d_ffn = d_second.astype(BF16)
    d_ffn_turned_ref[...] = jnp.transpose(d_ffn)
    d_first = d_second
    d_hidden = dot(d_ffn, w_down[0:FF_BLOCK, :], NT)
    for index, base in enumerate(starts):
        lanes = slice(base, base + FF_BLOCK)
        if index + 1 < len(starts):
            d_next = dot(d_ffn, w_down[starts[index + 1] : starts[index + 1] + FF_BLOCK, :], NT)
        d_pre = (d_hidden * slope[:, lanes]).astype(BF16)
        d_pre_ref[:, lanes] = d_pre
        up_sums_ref[:, lanes] += column_sum(d_pre.astype(F32))
        d_first += dot(d_pre, w_up[:, lanes], NT)
        d_hidden = d_next
    d_lower = normalise_back(d_first, normed_one, inv_one, gain_one)
    d_branch = d_lower.astype(BF16)
    d_branch_ref[...] = d_branch
    for index, ref in enumerate(d_att_refs):
        back = dot(d_branch, w_out[index * att_width : (index + 1) * att_width, :], NT)
        ref[...] = (0.5 * back).astype(BF16)
    sums_ref[0:1, :] += column_sum(d_branch.astype(F32))
    sums_ref[1:2, :] += column_sum(d_first * normed_one)
    sums_ref[2:3, :] += column_sum(top * normed_two)
    sums_ref[3:4, :] += column_sum(d_first)
    sums_ref[4:5, :] += column_sum(top)
    sums_ref[5:6, :] += column_sum(d_ffn.astype(F32))


def feed(pack, meta, x_own, cot_own, vectors, up_bias, att, own, pieces):
    row_count, model_width = x_own.shape
    feed_width = pack.feed_width
    att_width = att[0].shape[1]
    one = rows_of((ROW_BLOCK, model_width))
    wide = rows_of((ROW_BLOCK, feed_width))
    narrow = rows_of((ROW_BLOCK, att_width))
    turned = pl.BlockSpec((model_width, ROW_BLOCK), lambda i: (0, i))
    turned_shape = jax.ShapeDtypeStruct((model_width, row_count), BF16)

    def like(width):
        return jax.ShapeDtypeStruct((row_count, width), BF16)

    return pl.pallas_call(
        partial(feed_kernel, pack, len(att)),
        grid=(row_count // ROW_BLOCK,),
        in_specs=[IN_SMEM, one, one, whole(vectors.shape), whole(up_bias.shape)]
        + [narrow] * len(att)
        + [ANYWHERE] * (3 + len(pieces)),
        out_specs=[one, turned, one, turned, wide, wide, turned]
        + [narrow] * len(att)
        + [whole((8, model_width)), whole((1, feed_width))],
        out_shape=[
            like(model_width),
            turned_shape,
            like(model_width),
            turned_shape,
            like(feed_width),
            like(feed_width),
            turned_shape,
        ]
        + [like(att_width)] * len(att)
        + [
            jax.ShapeDtypeStruct((8, model_width), F32),
            jax.ShapeDtypeStruct((1, feed_width), F32),
        ],
        scratch_shapes=[
            pltpu.VMEM((model_width, model_width), BF16),
            pltpu.VMEM((model_width, feed_width), BF16),
            pltpu.VMEM((feed_width, model_width), BF16),
            pltpu.VMEM((ROW_BLOCK, feed_width), F32),
            pltpu.SemaphoreType.DMA((3, 1 + pack.blocks * len(pieces))),
        ],
        name="feed",
        **params(
            40, 2 * row_count * model_width * (2 * model_width + 4 * feed_width), 40_000_000
        ),
    )(meta, x_own, cot_own, vectors, up_bias, *att, *own, *pieces)


def down_grads_kernel(pack, table, d_ffn_ref, hidden_ref, theirs_ref, mine_ref, made, sems):
    step = pl.program_id(0)
    core = table[0]

    def stores(shard):
        return [
            pltpu.make_async_copy(made.at[1 - core, shard], theirs_ref.at[shard], sems.at[0, shard]),
            pltpu.make_async_copy(made.at[core, shard], mine_ref.at[shard], sems.at[1, shard]),
        ]

    grad = dot(d_ffn_ref[...], hidden_ref[...]).astype(BF16)
    for half in range(CORES):
        for lane in range(0, pack.model_width, pack.feed_shard):
            begin = half * (pack.model_width // CORES) + lane // pack.feed_shard * pack.down_rows
            made[half, step, :, lane : lane + pack.feed_shard] = grad[
                begin : begin + pack.down_rows
            ]
    for copy in stores(step):
        copy.start()

    @pl.when(step == pack.shards - 1)
    def _():
        for shard in range(pack.shards):
            for copy in stores(shard):
                copy.wait()


def down_grads(pack, table, d_ffn, hidden):
    model_width, row_count = d_ffn.shape
    shape = (pack.shards, pack.down_rows, model_width)
    return pl.pallas_call(
        partial(down_grads_kernel, pack),
        grid_spec=pltpu.PrefetchScalarGridSpec(
            num_scalar_prefetch=1,
            grid=(pack.shards,),
            in_specs=[
                pl.BlockSpec(d_ffn.shape, lambda step, table: (0, 0)),
                pl.BlockSpec((row_count, pack.feed_shard), lambda step, table: (0, step)),
            ],
            out_specs=[ANYWHERE] * 2,
            scratch_shapes=[
                pltpu.VMEM((CORES,) + shape, BF16),
                pltpu.SemaphoreType.DMA((CORES, pack.shards)),
            ],
        ),
        out_shape=[jax.ShapeDtypeStruct(shape, BF16)] * 2,
        name="down_grads",
        **params(60, 2 * row_count * model_width * pack.feed_width, 10_000_000),
    )(table, d_ffn, hidden)


def rest_grads_kernel(
    pack, table, first_ref, d_pre_ref, att_ref, d_branch_ref, theirs_ref, mine_ref, *scratch
):
    att, d_branch, tile, made, in_sems, sems = scratch
    step = pl.program_id(0)
    core, member = table[0], table[1]
    shards, blocks = pack.shards, pack.blocks
    out_at = pack.out_at - pack.down_rows

    loads = [
        pltpu.make_async_copy(att_ref, att, in_sems.at[0]),
        pltpu.make_async_copy(d_branch_ref, d_branch, in_sems.at[1]),
    ]

    def store(half, start, rows, sem):
        there = (slice(None), pl.ds(start, rows), slice(None))

        def copy(target):
            return pltpu.make_async_copy(
                made.at[(half,) + there], target.at[there], sems.at[half, sem]
            )

        return copy

    def both(half, start, rows, sem, act):
        copy = store(half, start, rows, sem)

        @pl.when(core == half)
        def _():
            act(copy(mine_ref))

        @pl.when(core != half)
        def _():
            act(copy(theirs_ref))

    @pl.when(step == 0)
    def _():
        for copy in loads:
            copy.start()

    @pl.when(step < CORES * blocks)
    def _():
        grad = dot(first_ref[...], d_pre_ref[...]).astype(BF16)
        start = pl.multiple_of(step % blocks * pack.row_shard, 16)
        for shard in range(shards):
            made[step // blocks, shard, pl.ds(start, pack.row_shard), :] = grad[
                shard * pack.row_shard : (shard + 1) * pack.row_shard
            ]

    for half in range(CORES):

        @pl.when(step == (half + 1) * blocks - 1)
        def _(half=half):
            both(half, 0, out_at, 0, lambda copy: copy.start())

    @pl.when(step == CORES * blocks)
    def _():
        for copy in loads:
            copy.wait()
        tile[...] = dot(att[...], d_branch[...])
        spare = pack.rows - pack.used
        for half in range(CORES):
            for shard in range(shards):
                start = pack.out_start(shard, member) + half * pack.out_rows
                start = pl.multiple_of(start, 16)
                made[half, shard, out_at : out_at + pack.out_rows, :] = tile[
                    pl.ds(start, pack.out_rows), :
                ].astype(BF16)
                if spare:
                    made[half, shard, out_at + pack.out_rows :, :] = jnp.zeros(
                        (spare, pack.model_width), BF16
                    )
            both(half, out_at, pack.rest_rows - out_at, 1, lambda copy: copy.start())
        for half in range(CORES):
            both(half, 0, out_at, 0, lambda copy: copy.wait())
            both(half, out_at, pack.rest_rows - out_at, 1, lambda copy: copy.wait())


def rest_grads(pack, table, first_low, d_pre, att, d_branch, needs=()):
    model_width, row_count = first_low.shape
    shape = (pack.shards, pack.rest_rows, model_width)
    steps = CORES * pack.blocks
    return pl.pallas_call(
        gated(partial(rest_grads_kernel, pack), 5, needs),
        grid_spec=pltpu.PrefetchScalarGridSpec(
            num_scalar_prefetch=1,
            grid=(steps + 1,),
            in_specs=[
                pl.BlockSpec(first_low.shape, lambda step, table: (0, 0)),
                pl.BlockSpec(
                    (row_count, model_width),
                    lambda step, table: (0, jnp.minimum(step, steps - 1)),
                ),
            ]
            + [ANYWHERE] * (2 + len(needs)),
            out_specs=[ANYWHERE] * 2,
            scratch_shapes=[
                pltpu.VMEM((model_width, row_count), BF16),
                pltpu.VMEM((row_count, model_width), BF16),
                pltpu.VMEM((model_width, model_width), F32),
                pltpu.VMEM((CORES,) + shape, BF16),
                pltpu.SemaphoreType.DMA((2,)),
                pltpu.SemaphoreType.DMA((CORES, 2)),
            ],
        ),
        out_shape=[jax.ShapeDtypeStruct(shape, BF16)] * 2,
        name="rest_grads",
        **params(60, 2 * row_count * model_width * (pack.feed_width + model_width), 10_000_000),
    )(table, first_low, d_pre, att, d_branch, *needs)


def qkv_grads_kernel(rounds, x_refs_then, *refs):
    refs = (x_refs_then,) + refs
    x_refs, grad_refs = refs[:rounds], refs[rounds : 2 * rounds]
    small_ref, out_ref = refs[2 * rounds :]
    shards, rows, _ = out_ref.shape
    row_shard = rows - small_ref.shape[1]
    total, sums = None, None
    for x_ref, grad_ref in zip(x_refs, grad_refs):
        grads = grad_ref[...]
        term = dot(x_ref[...], grads)
        down = column_sum(grads.astype(F32))
        total = term if total is None else total + term
        sums = down if sums is None else sums + down
    total = total.astype(BF16)
    row = lax.broadcasted_iota(jnp.int32, small_ref.shape[1:], 0)
    for shard in range(shards):
        out_ref[shard, :row_shard, :] = total[shard * row_shard : (shard + 1) * row_shard]
        last = jnp.where(row == BIAS_ROW, sums, small_ref[shard])
        out_ref[shard, row_shard:, :] = last.astype(BF16)


def qkv_grads(x_turned, grads, small, row_shard, needs=()):
    rounds = len(grads)
    model_width, positions = x_turned[0].shape
    cols = grads[0].shape[1]
    shards, extra, _ = small.shape
    block = GRAD_LANES if cols % GRAD_LANES == 0 else cols
    return pl.pallas_call(
        gated(partial(qkv_grads_kernel, rounds), 2 * rounds + 1, needs),
        grid=(cols // block,),
        in_specs=[whole((model_width, positions))] * rounds
        + [pl.BlockSpec((positions, block), lambda i: (0, i))] * rounds
        + [pl.BlockSpec((shards, extra, block), lambda i: (0, 0, i))]
        + [ANYWHERE] * len(needs),
        out_specs=pl.BlockSpec((shards, row_shard + extra, block), lambda i: (0, 0, i)),
        out_shape=jax.ShapeDtypeStruct((shards, row_shard + extra, cols), BF16),
        name="qkv_grads",
        **params(60, 2 * rounds * positions * model_width * cols, 18_000_000),
    )(*x_turned, *grads, small, *needs)


def add_picked_kernel(count, first, table, *refs):
    in_refs, out_refs = refs[:count], refs[count:]
    if count == 2:
        total = in_refs[0][...] + in_refs[1][...]
    else:
        total = in_refs[0][...].astype(F32)
        for ref in in_refs[1:]:
            total = total + ref[...].astype(F32)
        total = total.astype(BF16)
    if len(out_refs) == 1:
        out_refs[0][...] = total
        return

    @pl.when(pl.program_id(0) < first)
    def _():
        out_refs[0][...] = total

    @pl.when(pl.program_id(0) >= first)
    def _():
        out_refs[1][...] = total


def add_picked(table, arrays, steps, first=None, needs=(), work=0):
    _, rows, cols = arrays[0].shape
    parts = 2 if rows % 32 == 0 and steps == 1 else 1
    block = (1, rows // parts, cols)
    spec = [
        pl.BlockSpec(block, lambda s, p, t, k=k: (t[k * steps + s], p, 0))
        for k in range(len(arrays))
    ]
    if first is None:
        out_specs = [pl.BlockSpec(block, lambda s, p, t: (s, p, 0))]
        counts = [steps]
    else:
        out_specs = [
            pl.BlockSpec(
                block,
                lambda s, p, t: (
                    jnp.minimum(s, first - 1),
                    jnp.where(s < first, p, parts - 1),
                    0,
                ),
            ),
            pl.BlockSpec(
                block,
                lambda s, p, t: (jnp.maximum(s - first, 0), jnp.where(s < first, 0, p), 0),
            ),
        ]
        counts = [first, steps - first]
    return pl.pallas_call(
        gated(partial(add_picked_kernel, len(arrays), first), 1 + len(arrays), needs),
        grid_spec=pltpu.PrefetchScalarGridSpec(
            num_scalar_prefetch=1,
            grid=(steps, parts),
            in_specs=spec + [ANYWHERE] * len(needs),
            out_specs=out_specs,
        ),
        out_shape=[jax.ShapeDtypeStruct((n, rows, cols), BF16) for n in counts],
        name="add_picked",
        compiler_params=pltpu.CompilerParams(
            dimension_semantics=("arbitrary", "arbitrary"),
            vmem_limit_bytes=(60 if steps > 1 else 12) * MIB,
        ),
        cost_estimate=pl.CostEstimate(flops=work, bytes_accessed=1_000_000, transcendentals=0),
    )(table, *arrays, *needs)


def join_kernel(count, down_kept, down_landed, rest_kept, rest_landed, *outs):
    rows = down_kept.shape[1]
    for index in range(count):
        target = outs[1 - index % 2] if count > 1 else outs[0]
        place_now = index // 2
        target[place_now, :rows, :] = down_kept[index] + down_landed[index]
        target[place_now, rows:, :] = rest_kept[index] + rest_landed[index]


def join(kept, landed, needs=()):
    count = kept[0].shape[0]
    rows = kept[0].shape[1] + kept[1].shape[1]
    shape = jax.ShapeDtypeStruct(((count + 1) // 2, rows, kept[0].shape[2]), BF16)
    vmem = pl.BlockSpec(memory_space=pltpu.VMEM)
    outs = pl.pallas_call(
        gated(partial(join_kernel, count), 4, needs),
        in_specs=[vmem] * 4 + [ANYWHERE] * len(needs),
        out_specs=[vmem] * min(count, 2),
        out_shape=[shape] * min(count, 2),
        name="join",
        compiler_params=pltpu.CompilerParams(vmem_limit_bytes=24 * MIB),
        cost_estimate=pl.CostEstimate(flops=0, bytes_accessed=200_000, transcendentals=0),
    )(kept[0], landed[0], kept[1], landed[1], *needs)
    return outs if count > 1 else (None, outs[0])


def stack_kernel(count, *refs):
    for index in range(count):
        refs[count][index] = refs[index][...]


def home_kernel(count, meta, own_ref, *refs):
    out_ref = refs[count]
    rows = refs[0].shape[0]
    for index in range(count):
        start = pl.multiple_of((meta[5] + index) % count * rows, 16)
        target = out_ref.at[pl.ds(start, rows), :]
        if index:
            target[...] = refs[index][...].astype(out_ref.dtype)
            continue

        @pl.when(meta[6] == 0)
        def _():
            target[...] = refs[0][...].astype(out_ref.dtype)

        @pl.when(meta[6] == 1)
        def _():
            target[...] = own_ref[...].astype(out_ref.dtype)


def home_rows(meta, own, landed, dtype, needs=()):
    rows, cols = own.shape
    vmem = pl.BlockSpec(memory_space=pltpu.VMEM)
    return pl.pallas_call(
        gated(partial(home_kernel, len(landed)), 2 + len(landed), needs),
        in_specs=[IN_SMEM, vmem] + [vmem] * len(landed) + [ANYWHERE] * len(needs),
        out_specs=vmem,
        out_shape=jax.ShapeDtypeStruct((len(landed) * rows, cols), dtype),
        name="home_rows",
        compiler_params=pltpu.CompilerParams(vmem_limit_bytes=60 * MIB),
        cost_estimate=pl.CostEstimate(flops=0, bytes_accessed=100_000, transcendentals=0),
    )(meta, own, *landed, *needs)


def split_kernel(in_ref, *out_refs):
    rows = out_refs[0].shape[0]
    for index, ref in enumerate(out_refs):
        ref[...] = in_ref[index * rows : (index + 1) * rows, :]


def split_rows(value, count, needs=()):
    rows = value.shape[0] // count
    vmem = pl.BlockSpec(memory_space=pltpu.VMEM)
    return pl.pallas_call(
        gated(split_kernel, 1, needs),
        in_specs=[vmem] + [ANYWHERE] * len(needs),
        out_specs=[vmem] * count,
        out_shape=[jax.ShapeDtypeStruct((rows, value.shape[1]), value.dtype)] * count,
        name="split_rows",
        compiler_params=pltpu.CompilerParams(vmem_limit_bytes=12 * MIB),
        cost_estimate=pl.CostEstimate(flops=0, bytes_accessed=100_000, transcendentals=0),
    )(value, *needs)


def stack_up(pieces, needs=()):
    vmem = pl.BlockSpec(memory_space=pltpu.VMEM)
    return pl.pallas_call(
        gated(partial(stack_kernel, len(pieces)), len(pieces), needs),
        in_specs=[vmem] * len(pieces) + [ANYWHERE] * len(needs),
        out_specs=vmem,
        out_shape=jax.ShapeDtypeStruct((len(pieces),) + pieces[0].shape, BF16),
        name="stack_up",
        compiler_params=pltpu.CompilerParams(vmem_limit_bytes=24 * MIB),
        cost_estimate=pl.CostEstimate(flops=0, bytes_accessed=100_000, transcendentals=0),
    )(*pieces, *needs)


def unpack_kernel(pack, depth, meta, mine_ref, other_ref, down_ref, up_ref, out_ref, ordered):
    core, level = meta[2], meta[4]
    rows = pack.rows // depth
    for mask in range(depth):
        start = pl.multiple_of(lax.bitwise_xor(level, mask) * rows, 16)
        ordered[core, pl.ds(start, rows), :] = mine_ref[mask]
        ordered[1 - core, pl.ds(start, rows), :] = other_ref[mask]
    turned = []
    for half in range(CORES):
        for lane in range(0, pack.model_width, pack.feed_shard):
            turned.append(ordered[half, : pack.down_rows, lane : lane + pack.feed_shard])
    down_ref[...] = jnp.transpose(jnp.concatenate(turned, axis=0)).astype(F32)
    for half in range(CORES):
        for block in range(pack.blocks):
            lane = (half * pack.blocks + block) * pack.model_width
            start = pack.up_at + block * pack.row_shard
            up_ref[:, lane : lane + pack.model_width] = ordered[
                half, start : start + pack.row_shard, :
            ].astype(F32)
        out_ref[half * pack.out_rows : (half + 1) * pack.out_rows, :] = ordered[
            half, pack.out_at : pack.out_at + pack.out_rows, :
        ].astype(F32)


def unpack(pack, depth, meta, mine, other):
    vmem = pl.BlockSpec(memory_space=pltpu.VMEM)
    return pl.pallas_call(
        partial(unpack_kernel, pack, depth),
        in_specs=[IN_SMEM, vmem, vmem],
        out_specs=[vmem] * 3,
        out_shape=[
            jax.ShapeDtypeStruct((pack.feed_shard, pack.model_width), F32),
            jax.ShapeDtypeStruct((pack.row_shard, pack.feed_width), F32),
            jax.ShapeDtypeStruct((pack.row_shard, pack.model_width), F32),
        ],
        scratch_shapes=[pltpu.VMEM((CORES, pack.rows, pack.model_width), BF16)],
        name="unpack",
        compiler_params=pltpu.CompilerParams(vmem_limit_bytes=60 * MIB),
        cost_estimate=pl.CostEstimate(flops=0, bytes_accessed=10_000_000, transcendentals=0),
    )(meta, mine, other)


def unpack_qkv_kernel(meta, mine_ref, other_ref, grad_ref, bias_ref, small_ref):
    member = meta[3]
    row_shard, width = grad_ref.shape[0], grad_ref.shape[1] // 3
    part = mine_ref.shape[1] // 3
    for ref, at in ((mine_ref, member), (other_ref, 1 - member)):
        for kind in range(3):
            lane = pl.multiple_of(kind * width + at * part, CLUSTER_ROWS)
            from_lanes = slice(kind * part, (kind + 1) * part)
            grad_ref[:, pl.ds(lane, part)] = ref[:row_shard, from_lanes].astype(F32)
            lane = pl.multiple_of(at * part, CLUSTER_ROWS)
            bias_ref[kind : kind + 1, pl.ds(lane, part)] = ref[row_shard:, from_lanes].astype(F32)[
                BIAS_ROW : BIAS_ROW + 1
            ]
    small_ref[...] = (mine_ref[row_shard:, :].astype(F32) + other_ref[row_shard:, :].astype(F32))[
        :BIAS_ROW
    ]


def unpack_qkv(meta, mine, other, row_shard, needs=()):
    cols = mine.shape[1]
    vmem = pl.BlockSpec(memory_space=pltpu.VMEM)
    return pl.pallas_call(
        gated(unpack_qkv_kernel, 3, needs),
        in_specs=[IN_SMEM, vmem, vmem] + [ANYWHERE] * len(needs),
        out_specs=[vmem] * 3,
        out_shape=[
            jax.ShapeDtypeStruct((row_shard, CORES * cols), F32),
            jax.ShapeDtypeStruct((3, CORES * cols // 3), F32),
            jax.ShapeDtypeStruct((BIAS_ROW, cols), F32),
        ],
        name="unpack_qkv",
        compiler_params=pltpu.CompilerParams(vmem_limit_bytes=60 * MIB),
        cost_estimate=pl.CostEstimate(flops=0, bytes_accessed=200_000, transcendentals=0),
    )(meta, mine, other, *needs)


def tie(*values):
    return lax.optimization_barrier(values)


def body(
    tokens,
    cotangent,
    perms,
    unit_kind,
    w_qkv,
    bias_qv,
    w_out,
    bias_out,
    ln_gain,
    ln_bias,
    w_up,
    bias_up,
    w_down,
    bias_down,
):
    shards = lax.axis_size("fsdp")
    groups = lax.axis_size("dp")
    here = lax.axis_index("fsdp")
    dp_index = lax.axis_index("dp")
    core = dp_index % CORES
    level = dp_index // CORES
    depth = groups // CORES
    units, rounds, unit_len = perms.shape
    per_device = unit_len // shards
    model_width = tokens.shape[1]
    feed_width = w_up.shape[1]
    row_shard = model_width // shards
    members = shards // units
    member_rows = unit_len // members
    head_cols = model_width // members
    padded = -(-head_cols // CLUSTER_ROWS) * CLUSTER_ROWS
    spot = here * CORES + core
    home_core = spot // shards
    unit = (spot // members) % units
    member = spot % members
    pack = Pack(model_width, feed_width, shards, units, depth)
    bits = [1 << k for k in range(shards.bit_length() - 1)]
    bit_orders = (bits, bits[::-1])

    def plane_pairs(target):
        pairs = []
        for z in range(depth):
            for f_index in range(shards):
                for c_index in range(CORES):
                    f_new, c_new = target(f_index, c_index)
                    pairs.append(
                        (
                            (z * CORES + c_index) * shards + f_index,
                            (z * CORES + c_new) * shards + f_new,
                        )
                    )
        return pairs

    def send(value, pairs):
        return lax.ppermute(value, ("dp", "fsdp"), pairs)

    def cross(value, mask):
        return send(value, plane_pairs(lambda f, c: divmod((f * CORES + c) ^ mask, CORES)))

    def trade(value, stage):
        return send(value, plane_pairs(lambda f, c: (f ^ bit_orders[c][stage], c)))

    def trade_mask(index, which):
        mask = 0
        for stage in range(len(bits)):
            if index >> stage & 1:
                mask ^= bit_orders[which][stage]
        return mask

    def climb(value, mask):
        plane = CORES * shards
        pairs = []
        for z in range(depth):
            for rest in range(plane):
                pairs.append((z * plane + rest, (z ^ mask) * plane + rest))
        return send(value, pairs)

    def place_of(f, c, step):
        return (c * units + (f % units + step) % units) * members + f // units

    def outward(step):
        return plane_pairs(lambda f, c: divmod(place_of(f, c, step), CORES))

    def homeward(step):
        return [(b, a) for a, b in outward(step)]

    stays = place_of(here, core, 0) == spot

    def send_apart(value, pairs):
        return send(value, [(a, b) for a, b in pairs if a != b])

    def bring_start(value):
        blocks = value.reshape(units, per_device, model_width)
        return [
            lax.dynamic_index_in_dim(blocks, (here % units + step) % units, axis=0, keepdims=False)
            for step in range(units)
        ]

    def bring(chosen):
        return [
            (send_apart if step == 0 else send)(value, outward(step))
            for step, value in enumerate(chosen)
        ]

    def brought(chosen, landed):
        kept_one = jnp.where(stays, chosen[0], landed[0])
        return jnp.concatenate([kept_one] + list(landed[1:]), axis=0)

    def send_home(blocks):
        return [
            (send_apart if step == 0 else send)(blocks[step], homeward(step))
            for step in range(units)
        ]

    x_chosen = bring_start(tokens)
    x_own = brought(x_chosen, bring(x_chosen))
    small = jnp.concatenate(
        [
            bias_qv.reshape(-1),
            bias_out,
            ln_gain.reshape(-1),
            ln_bias.reshape(-1),
            bias_up,
            bias_down,
        ]
    )
    small_rows = -(-small.shape[0] // (3 * padded))
    small_block = jnp.pad(
        jnp.pad(small, (0, small_rows * 3 * padded - small.shape[0])).reshape(
            small_rows, 3 * padded
        ),
        ((0, 16 - small_rows), (0, 0)),
    )
    def columns_for(offset):
        start = lax.bitwise_xor(member, offset) * head_cols
        blocks = [
            jnp.pad(
                lax.dynamic_slice(
                    w_qkv, (0, kind * model_width + start), (row_shard, head_cols)
                ),
                ((0, 0), (0, padded - head_cols)),
            )
            for kind in range(3)
        ]
        return jnp.concatenate([jnp.concatenate(blocks, axis=1), small_block], axis=0)

    offsets = [(CORES * m) % members for m in range(shards)]
    kinds = sorted(set(offsets))
    order_pack = jnp.concatenate(
        [perms.reshape(-1), jnp.broadcast_to(unit_kind[:, None], (units, 128)).reshape(-1)]
    )
    order_other = cross(order_pack, 1)
    *tied, order_other = tie(*[columns_for(offset) for offset in kinds], order_other)
    piece_kinds = dict(zip(kinds, tied))
    x_pieces = [x_own] + [cross(x_own, mask) for mask in range(1, members)]
    if members == CORES:
        qkv_pieces = {0: piece_kinds[0]}
        for stage in range(len(bits)):
            qkv_pieces[1 << stage] = trade(piece_kinds[0], stage)
        for stage in range(1, len(bits)):
            for index in range(1, 1 << stage):
                qkv_pieces[index | 1 << stage] = trade(qkv_pieces[index], stage)
        qkv_pieces = [qkv_pieces[index] for index in range(shards)]
        qkv_masks = [[trade_mask(index, which) for index in range(shards)] for which in (0, 1)]
    else:
        qkv_pieces = [piece_kinds[0]] + [
            cross(piece_kinds[offsets[m]], CORES * m) for m in range(1, shards)
        ]
        qkv_masks = [list(range(shards))] * 2
    order_pack = jnp.where(home_core == core, order_pack, order_other)
    order_count = units * rounds * unit_len
    unit_perm = lax.dynamic_index_in_dim(
        order_pack[:order_count].reshape(units, rounds * unit_len), unit, 0, keepdims=False
    )
    kind_now = lax.dynamic_index_in_dim(
        order_pack[order_count:].reshape(units, 128), unit, 0, keepdims=False
    )[0]
    owner = unit_perm // per_device
    order = (
        lax.bitwise_xor(owner // units, member) * units + (unit - owner % units) % units
    ) * per_device + unit_perm % per_device
    order = order.reshape(rounds, unit_len)
    order = jnp.where(core == 0, order, order[::-1])
    order_row = order.reshape(1, rounds * unit_len)
    order = order.reshape(-1, CLUSTER_ROWS)
    x_here = arrange(order, x_pieces, unit_len, 0)
    x_now = [x_here, cross(x_here, 1)]
    own_masks = [
        jnp.where(core == 0, trade_mask(i, 0), trade_mask(i, 1)) for i in range(1, shards)
    ]
    other_masks = [
        jnp.where(core == 0, trade_mask(i, 1), trade_mask(i, 0)) for i in range(1, shards)
    ]
    zero = jnp.int32(0)
    meta = jnp.stack(
        [kind_now, here, core, member, level, here % units, stays, zero]
        + own_masks
        + other_masks
        + [jnp.where(core == 0, first, second) for first, second in zip(*qkv_masks)]
    ).astype(jnp.int32)

    def half_of(value, axis, length, at):
        return lax.dynamic_slice_in_dim(value, at * length, length, axis=axis)

    packed = jnp.concatenate(
        [half_of(w_down, 0, pack.down_rows, core)]
        + [
            half_of(w_up, 1, model_width, core * pack.blocks + block)
            for block in range(pack.blocks)
        ]
        + [half_of(w_out, 0, pack.out_rows, core)],
        axis=0,
    )
    order_rows = unit_len // CLUSTER_ROWS
    arranged, probs, mixtures, x_turned = [], [], [], []
    *tied, packed, x_now[0] = tie(*qkv_pieces[1:], packed, x_now[0])
    qkv_pieces = qkv_pieces[:1] + tied
    smalls = jnp.stack(
        [
            piece[row_shard : row_shard + small_rows].reshape(-1)[: small.shape[0]]
            for piece in qkv_pieces
        ]
    )
    spots_of = [[masks.index(mask) for mask in range(shards)] for masks in qkv_masks]
    spots_of = jnp.where(core == 0, jnp.array(spots_of[0]), jnp.array(spots_of[1]))
    spots_of = jnp.take(spots_of, lax.bitwise_xor(here, jnp.arange(shards)))
    smalls = jnp.take(smalls, spots_of, axis=0).astype(F32)

    def vectors_at(start, count, length):
        part = smalls[:, start * row_shard : start * row_shard + count * length]
        return (
            part.reshape(shards, count, length).transpose(1, 0, 2).reshape(count, shards * length)
        )

    my_bias = lax.dynamic_index_in_dim(
        vectors_at(0, 2, row_shard).reshape(2, members, head_cols), member, 1, keepdims=False
    )
    my_bias = jnp.pad(my_bias, ((0, 0), (0, padded - head_cols)))
    my_bias = jnp.stack([my_bias[0], jnp.zeros_like(my_bias[0]), my_bias[1]]).reshape(1, -1)
    up_bias = vectors_at(7, 1, feed_width // shards)
    down_bias = smalls[:, small.shape[0] - row_shard :].reshape(1, model_width)
    vectors = jnp.concatenate(
        [vectors_at(2, 5, row_shard), down_bias, jnp.zeros((2, model_width), F32)], axis=0
    )

    weight_pieces = {0: packed}
    for stage in range(len(bits)):
        weight_pieces[1 << stage] = trade(packed, stage)
    for index in range(rounds):
        results = attend(meta, x_now[index], my_bias, qkv_pieces, row_shard, mixtures[-1:])
        for kept, result in zip((arranged, probs, mixtures, x_turned), results):
            kept.append(result)
    cot_now, mixtures[0] = tie(cotangent, mixtures[0])
    cot_chosen = bring_start(cot_now)
    cot_landed = bring(cot_chosen)
    cot_own = brought(cot_chosen, cot_landed)
    for stage in range(1, len(bits)):
        for index in range(1, 1 << stage):
            weight_pieces[index | 1 << stage] = trade(weight_pieces[index], stage)
    att_there, att_sent = [], []
    for mask in range(1, members):
        there = place(
            order_row, mixtures, mask * member_rows, member_rows, 0.5, needs=cot_landed
        )
        att_sent.append(there)
        att_there.append(cross(there[:, :head_cols], mask))
    att_here = place(order_row, mixtures, 0, member_rows, 0.5, needs=att_sent)

    direct = [weight_pieces[index] for index in range(1, shards)]
    swapped = [cross(piece, 1) for piece in direct[:-1]]
    last_piece, att_here = tie(direct[-1], att_here)
    swapped.append(cross(last_piece, 1))
    att_raw = [att_here[:, :head_cols]] + att_there
    if head_cols % CLUSTER_ROWS:
        att_raw = [jnp.concatenate(att_raw, axis=1)]
    block_out, first_low, d_branch, d_ffn, hidden, d_pre, att_turned, *rest = feed(
        pack,
        meta,
        x_own,
        cot_own,
        vectors,
        up_bias,
        att_raw,
        [w_out, w_up, w_down],
        direct + swapped,
    )
    d_att, (row_sums, up_sums) = rest[: len(att_raw)], rest[len(att_raw) :]
    if head_cols % CLUSTER_ROWS:
        d_att = [d_att[0][:, mask * head_cols : (mask + 1) * head_cols] for mask in range(members)]
    d_att = [d_att[0]] + [cross(d_att[mask], mask) for mask in range(1, members)]
    d_att = [jnp.pad(piece, ((0, 0), (0, padded - head_cols))) for piece in d_att]

    table = jnp.stack([core, member]).astype(jnp.int32)
    sending = [index for index in range(shards) if index & 1]
    keeping = [index for index in range(shards) if not index & 1]
    slots = jnp.stack(
        [
            lax.bitwise_xor(here, jnp.where(core == 0, trade_mask(i, 0), trade_mask(i, 1)))
            for i in sending + keeping
        ]
    )
    slots = jnp.concatenate([slots, slots]).astype(jnp.int32)

    def pair_sum(mine, theirs, needs):
        return add_picked(
            slots, [mine, cross(theirs, 1)], shards, len(sending), needs, 20_000_000_000
        )

    theirs_down, mine_down = down_grads(pack, table, d_ffn, hidden)
    theirs_rest, mine_rest = rest_grads(
        pack, table, first_low, d_pre, att_turned, d_branch, [theirs_down]
    )
    down_going, down_kept = pair_sum(mine_down, theirs_down, [theirs_rest])
    rest_going, rest_kept = pair_sum(mine_rest, theirs_rest, [down_going] + d_att[1:])

    def merge(kept, landed, *needs):
        count = kept.shape[0]
        if count == 1:
            table = jnp.zeros((2,), jnp.int32)
            return None, add_picked(table, [kept, landed], 1, None, needs)[0]
        order_now = [i for i in range(count) if i & 1] + [i for i in range(count) if not i & 1]
        table = jnp.array(order_now * 2, jnp.int32)
        return add_picked(table, [kept, landed], count, count // 2, needs)

    grads, d_x = [None] * rounds, [None] * rounds
    needs = [rest_going]
    blocks = unit_len // POS_BLOCK
    spans = [(index, (0, blocks)) for index in reversed(range(rounds))]
    for turn, (index, span) in enumerate(spans):
        grads[index], d_x[index], token = attend_back(
            meta,
            order,
            arranged[index],
            probs[index],
            d_att,
            qkv_pieces,
            row_shard,
            index * order_rows,
            needs,
            span,
            [],
        )
        if turn == 0:
            d_x_there = cross(d_x[index], 1)
            going, kept = join(
                [down_kept, rest_kept], [trade(down_going, 0), trade(rest_going, 0)], [token]
            )
            output_blocks = split_rows(block_out, units, [token])
            output_landed = send_home(output_blocks)
            needs = [kept]
    for stage in range(1, len(bits)):
        going, kept = merge(kept, trade(going, stage), token)

    def level_pieces(block):
        return block.reshape((depth, block.shape[0] // depth) + block.shape[1:])

    def level_scatter(cut):
        return [
            climb(
                lax.dynamic_index_in_dim(cut, lax.bitwise_xor(level, mask), 0, keepdims=False), mask
            )
            for mask in range(1, depth)
        ]

    def level_gather(piece):
        pieces = {0: piece}
        mask = depth // 2
        while mask:
            pieces[mask] = climb(piece, mask)
            mask //= 2
        return pieces

    def level_forward(pieces):
        for index in sorted(range(depth), key=lambda value: value.bit_count()):
            if index not in pieces:
                low = index & -index
                pieces[index] = climb(pieces[index ^ low], low)
        return [pieces[index] for index in range(depth)]

    def by_shard(value):
        count, length = value.shape
        return (
            value.reshape(count, shards, length // shards)
            .transpose(1, 0, 2)
            .reshape(shards, count * length // shards)
        )

    small_grad = jnp.concatenate(
        [by_shard(row_sums[:5]), by_shard(up_sums), by_shard(row_sums[5:6])], axis=1
    )
    small_length = small_grad.shape[1]
    small_lanes = 3 * head_cols
    small_grad = jnp.pad(small_grad, ((0, 0), (0, BIAS_ROW * small_lanes - small_length)))
    small_grad = jnp.pad(
        small_grad.reshape(shards, BIAS_ROW, small_lanes), ((0, 0), (0, 16 - BIAS_ROW), (0, 0))
    )
    extra_rows = 16
    if padded == head_cols:
        joined = qkv_grads(
            x_turned, grads, small_grad, row_shard, output_landed + [kept]
        )
    else:
        qkv_grad = dot(x_turned[0], grads[0]) + dot(x_turned[1], grads[1])
        qkv_grad = qkv_grad.reshape(shards, row_shard, 3, padded)[..., :head_cols]
        bias_sum = sum(jnp.sum(value.astype(F32), axis=0) for value in grads)
        bias_sum = bias_sum.reshape(3, padded)[:, :head_cols].reshape(small_lanes)
        small_grad = small_grad.at[:, BIAS_ROW].set(bias_sum[None])
        joined = jnp.concatenate(
            [qkv_grad.reshape(shards, row_shard, small_lanes), small_grad], axis=1
        ).astype(BF16)
    cut = level_pieces(kept[0])
    landed = level_scatter(cut)
    classes = max(1, members // CORES)
    d_x_parts = [d_x[0], d_x_there]
    order_mine = order_row[:, :unit_len]
    if classes == 1:
        slots_held = jnp.stack(
            [
                lax.bitwise_xor(here, jnp.where(core == 0, trade_mask(i, 0), trade_mask(i, 1)))
                for i in range(shards)
            ]
        )
        held = jnp.stack(
            [
                lax.dynamic_index_in_dim(joined, slots_held[i], 0, keepdims=False)
                for i in range(0, shards, 2)
            ]
        )
        leaving = jnp.stack(
            [
                lax.dynamic_index_in_dim(joined, slots_held[i], 0, keepdims=False)
                for i in range(1, shards, 2)
            ]
        )
        totals = None
    else:
        totals = [None] * classes
        for m in range(shards):
            offset = offsets[m] // CORES
            piece = lax.dynamic_index_in_dim(joined, lax.bitwise_xor(here, m), 0, keepdims=False)
            piece = (piece if m == 0 else cross(piece, CORES * m)).astype(F32)
            totals[offset] = piece if totals[offset] is None else totals[offset] + piece

    d_there = [
        place(
            order_mine,
            d_x_parts,
            mask * member_rows,
            member_rows,
            added=True,
            needs=[joined],
        )
        for mask in range(1, members)
    ]
    if depth > 1:
        picks = jnp.concatenate([level[None], jnp.zeros((depth - 1,), level.dtype)])
        (kept,) = add_picked(
            picks.astype(jnp.int32),
            [cut] + [piece[None] for piece in landed],
            1,
            None,
            d_there,
        )
    gathered = level_gather(kept[0]) if depth > 1 else {0: cut[0]}
    early = [kept] + d_there
    if totals is None:
        held = held + trade(leaving, 0)
        early.append(held)
    d_here = place(
        order_mine,
        d_x_parts,
        0,
        member_rows,
        1.0,
        F32,
        d_branch,
        added=True,
        needs=early,
    )
    d_inputs = d_here
    for mask, there in enumerate(d_there, 1):
        d_inputs = d_inputs + cross(there, mask).astype(F32)
    d_inputs = d_inputs.astype(BF16)
    home_blocks = d_inputs.reshape(units, per_device, model_width)
    home = send_home(home_blocks)
    last = d_inputs
    if totals is None:
        for stage in range(1, len(bits)):
            held = held[::2] + trade(held[1::2], stage)
        last = held
        totals = [held[0]]
    output = home_rows(meta, output_blocks[0], output_landed, BF16, [last])
    totals = jnp.concatenate(totals, axis=0).astype(BF16)
    rows_each = row_shard + extra_rows
    if depth > 1:
        halves = totals.reshape((2, totals.shape[0] // 2) + totals.shape[1:])
        side = level % 2
        mine = lax.dynamic_index_in_dim(halves, side, 0, keepdims=False)
        theirs = lax.dynamic_index_in_dim(halves, 1 - side, 0, keepdims=False)
        half = (mine.astype(F32) + climb(theirs, 1).astype(F32)).astype(BF16)
        masks = [mask for mask in gathered if mask]
        *tied, half = tie(*[gathered[mask] for mask in masks], half)
        gathered.update(zip(masks, tied))
        mask = 2
        while mask < depth:
            half = (half.astype(F32) + climb(half, mask).astype(F32)).astype(BF16)
            mask *= 2
        *home, output, half = tie(*home, output, half)
        other_half = climb(half, 1)
        d_inputs = home_rows(meta, home_blocks[0], home, F32)
        d_inputs, other_half = tie(d_inputs, other_half)
        totals = jnp.concatenate(
            [
                jnp.where(side == 0, half, other_half),
                jnp.where(side == 0, other_half, half),
            ],
            axis=0,
        )
    else:
        d_inputs = home_rows(meta, home_blocks[0], home, F32)
    stacked = stack_up(level_forward(gathered))
    grad_down, grad_up, grad_out = unpack(pack, depth, meta, stacked, cross(stacked, 1))
    if padded == head_cols and members == CORES:
        grad_qkv, bias_out_row, smalls_out = unpack_qkv(
            meta, totals, cross(totals, 1), row_shard, [grad_down]
        )
        smalls_out = smalls_out.reshape(-1)[:small_length]
        bias_out_row = lax.dynamic_slice(bias_out_row, (0, here * row_shard), (3, row_shard))
    else:
        landed = jnp.stack([totals, cross(totals, 1)], axis=0).reshape(
            CORES, classes, rows_each, 3 * head_cols
        )
        smalls_out = jnp.sum(
            landed[:, :, row_shard : row_shard + BIAS_ROW].astype(F32), axis=(0, 1)
        ).reshape(-1)[:small_length]
        landed = (
            landed.transpose(1, 0, 2, 3)
            .reshape(members, rows_each, 3, head_cols)[:, : row_shard + BIAS_ROW + 1]
        )
        if members == 2:
            swap = member == 1
            landed = jnp.stack(
                [
                    jnp.where(swap, landed[1], landed[0]),
                    jnp.where(swap, landed[0], landed[1]),
                ]
            )
        else:
            landed = jnp.take(landed, lax.bitwise_xor(member, jnp.arange(members)), axis=0)
        grad_qkv = landed[:, :row_shard].transpose(1, 2, 0, 3)
        grad_qkv = grad_qkv.reshape(row_shard, 3 * model_width).astype(F32)
        bias_out_row = landed[:, row_shard + BIAS_ROW].astype(F32).transpose(1, 0, 2)
        bias_out_row = lax.dynamic_slice(
            bias_out_row.reshape(3, model_width), (0, here * row_shard), (3, row_shard)
        )

    feed_shard = feed_width // shards
    spots = [0, row_shard, 3 * row_shard, 5 * row_shard]
    return (
        output,
        d_inputs,
        grad_qkv,
        bias_out_row[::2],
        grad_out,
        smalls_out[spots[0] : spots[1]],
        smalls_out[spots[1] : spots[2]].reshape(2, row_shard),
        smalls_out[spots[2] : spots[3]].reshape(2, row_shard),
        grad_up,
        smalls_out[spots[3] : spots[3] + feed_shard],
        grad_down,
        smalls_out[spots[3] + feed_shard :],
    )


def solution(mesh):
    placed = (
        P(("dp", "fsdp"), None),
        P(("dp", "fsdp"), None),
        P("dp", None, None),
        P("dp"),
        P("fsdp", None),
        P(None, "fsdp"),
        P("fsdp", None),
        P("fsdp"),
        P(None, "fsdp"),
        P(None, "fsdp"),
        P("fsdp", None),
        P("fsdp"),
        P("fsdp", None),
        P("fsdp"),
    )
    return jax.shard_map(
        body,
        mesh=mesh,
        in_specs=placed,
        out_specs=(
            P(("dp", "fsdp"), None),
            P(("dp", "fsdp"), None),
            P("fsdp", None),
            P(None, "fsdp"),
            P("fsdp", None),
            P("fsdp"),
            P(None, "fsdp"),
            P(None, "fsdp"),
            P("fsdp", None),
            P("fsdp"),
            P("fsdp", None),
            P("fsdp"),
        ),
        check_vma=False,
    )
```
